32 devices in a mesh: dp: 4 (over z), seq: 8 (over y, x, core).
Axes of the slice: x: 2, y: 2, z: 4, core: 2. Of those that a mesh axis runs over, the one named last changes fastest.
Arguments:
- tokens: bfloat16 [4, 2, 1024, 2048], P('dp', None, 'seq'), may hold values from -6 to 6
- doc_lengths: int32 [4, 2, 8], P('dp'), may hold values from 1 to 1017, as said below
- w_query: bfloat16 [2048, 256], P('dp'), may hold values from -0.125 to 0.125
- w_key: bfloat16 [2048, 256], P('dp'), may hold values from -0.125 to 0.125
- w_value: bfloat16 [2048, 2048], P('dp'), may hold values from -0.125 to 0.125
- w_out: bfloat16 [2048, 2048], P('dp'), may hold values from -1 to 1
- w_gate: bfloat16 [2048, 5632], P('dp'), may hold values from -0.125 to 0.125
- w_up: bfloat16 [2048, 5632], P('dp'), may hold values from -0.125 to 0.125
- w_down: bfloat16 [5632, 2048], P('dp'), may hold values from -0.078125 to 0.078125
- gain_attn: bfloat16 [2048], P('dp'), may hold values from 0.5 to 1.5
- gain_mlp: bfloat16 [2048], P('dp'), may hold values from 0.5 to 1.5
- cotangent: bfloat16 [4, 2, 1024, 2048], P('dp', None, 'seq'), may hold values from -6 to 6
Outputs:
- output: bfloat16 [4, 2, 1024, 2048], P('dp', None, 'seq')
- input_grad: float32 [4, 2, 1024, 2048], P('dp', None, 'seq')
- grad_query: float32 [2048, 256], P(('dp', 'seq'))
- grad_key: float32 [2048, 256], P(('dp', 'seq'))
- grad_value: float32 [2048, 2048], P(('dp', 'seq'))
- grad_out: float32 [2048, 2048], P(('dp', 'seq'))
- grad_gate: float32 [2048, 5632], P(('dp', 'seq'))
- grad_up: float32 [2048, 5632], P(('dp', 'seq'))
- grad_down: float32 [5632, 2048], P(('dp', 'seq'))
- grad_gain_attn: float32 [2048], P(('dp', 'seq'))
- grad_gain_mlp: float32 [2048], P(('dp', 'seq'))
The draws below stay inside these ranges and needn't reach their ends.
Inputs may be any that keep to these rules, and one draw needn't show every extreme that they name: `doc_lengths`: in every stream the 8 lengths add up to 1024; one document of each stream, at a place drawn from the seed, holds all tokens but fewer than 128 before it and fewer than 128 after it; in one stream, drawn from the seed, every other document has one token.
All inputs are finite; a program needn't handle non-finite values.
Results may differ from the reference program's by a relative error of at most 0.02.
Values may be sent and summed in bfloat16 or wider, within the bound.
A program may use at most 640 MiB of HBM per device.

```python
import math
import jax
import jax.numpy as jnp
from jax import lax

D = 2048
HEADS = 16
QK_DIM = 16
FF = 5632
SPAN = 128
MICRO = 2
BLOCK = 128
DOCS = 8
FEAT = 273
HEAD_V = 128
GROUPS = 4
STREAM = 1024


def draw_doc_lengths(key, part):
    key = jax.random.fold_in(key, 11)
    long_key, short_key, stream_key = jax.random.split(key, 3)
    place = jax.random.randint(long_key, (GROUPS, MICRO, 1), 0, DOCS)
    shorts = jax.random.randint(short_key, (GROUPS, MICRO, DOCS), 1, SPAN // DOCS + 1)
    chosen = jax.random.randint(stream_key, (), 0, GROUPS * MICRO)
    stream_number = jnp.arange(GROUPS * MICRO, dtype=jnp.int32).reshape(GROUPS, MICRO, 1)
    shorts = jnp.where(stream_number == chosen, 1, shorts)
    slot = jnp.arange(DOCS)[None, None, :]
    others = jnp.sum(jnp.where(slot == place, 0, shorts), axis=-1, keepdims=True)
    return jnp.where(slot == place, STREAM - others, shorts).astype(jnp.int32)


def block_levels(key, extent, pieces, least, high):
    loudness = 1.0
    for dim, blocks in pieces:
        draws = jax.random.uniform(jax.random.fold_in(jax.random.fold_in(key, 6), dim), (blocks,), jnp.float32, least / len(pieces), high / len(pieces))
        loudness = loudness * jnp.repeat(jnp.exp(draws), extent[dim] // blocks).reshape((-1,) + (1,) * (len(extent) - 1 - dim))
    return loudness


def normal_values(key, dims, deviation, bound, shards=(), held_as=jnp.bfloat16):
    values = deviation * jax.random.normal(key, dims, jnp.float32)
    if shards:
        values = values * block_levels(key, dims, shards, -0.22, 0.18)
    return jnp.clip(values, -bound, bound).astype(held_as)


def setup_inputs(seed: int = 0) -> dict:
    keys = jax.random.split(jax.random.key(seed), 13)
    tokens = normal_values(keys[0], (GROUPS, MICRO, STREAM, D), 1.0, 6.0, ((0, 4), (2, 8)))
    doc_lengths = draw_doc_lengths(jax.random.fold_in(keys[12], 71), 0)
    w_query = normal_values(keys[2], (D, HEADS * QK_DIM), D ** -0.5, 0.125, ((0, 4),))
    w_key = normal_values(keys[3], (D, HEADS * QK_DIM), D ** -0.5, 0.125, ((0, 4),))
    w_value = normal_values(keys[4], (D, D), D ** -0.5, 0.125, ((0, 4),))
    w_out = normal_values(keys[5], (D, D), (D // 64) ** -0.5, 1.0, ((0, 4),))
    w_gate = normal_values(keys[6], (D, FF), D ** -0.5, 0.125, ((0, 4),))
    w_up = normal_values(keys[7], (D, FF), D ** -0.5, 0.125, ((0, 4),))
    w_down = normal_values(keys[8], (FF, D), FF ** -0.5, 0.078125, ((0, 4),))
    gain_attn = jnp.clip(1.0 + 0.1 * jax.random.normal(keys[9], (D,), jnp.float32), 0.5, 1.5).astype(jnp.bfloat16)
    gain_mlp = jnp.clip(1.0 + 0.1 * jax.random.normal(keys[10], (D,), jnp.float32), 0.5, 1.5).astype(jnp.bfloat16)
    cotangent = normal_values(keys[11], (GROUPS, MICRO, STREAM, D), 1.0, 6.0, ((0, 4), (2, 8)))
    return {"tokens": tokens, "doc_lengths": doc_lengths, "w_query": w_query, "w_key": w_key, "w_value": w_value, "w_out": w_out, "w_gate": w_gate, "w_up": w_up, "w_down": w_down, "gain_attn": gain_attn, "gain_mlp": gain_mlp, "cotangent": cotangent}


@jax.custom_vjp
def low(v):
    return lax.optimization_barrier(v.astype(jnp.bfloat16)).astype(jnp.float32)

@jax.custom_vjp
def low_back(v):
    return v

def low_keep(v):
    return (low(v), None)

def low_pass(kept, grad):
    return (grad,)

def back_keep(v):
    return (v, None)

def back_low(kept, grad):
    return (low(grad),)
low.defvjp(low_keep, low_pass)
low_back.defvjp(back_keep, back_low)
epsilon = 1e-06
highest = lax.Precision.HIGHEST

def rms_norm(rows, gain):
    return rows * lax.rsqrt(lax.optimization_barrier(jnp.mean(rows * rows, axis=-1, keepdims=True)) + epsilon) * gain

def matmul(left, right):
    return jnp.dot(left, right, precision=highest, preferred_element_type=jnp.float32)

def taylor_map(vectors):
    width = vectors.shape[-1]
    outer = (vectors[..., :, None] * vectors[..., None, :]).reshape(vectors.shape[:-1] + (width * width,))
    ones = jnp.ones(vectors.shape[:-1] + (1,), jnp.float32)
    return jnp.concatenate([ones, vectors / math.sqrt(math.sqrt(width)), outer / math.sqrt(2.0 * width)], axis=-1)

def block_step(carry, block):
    state, norm_state, last_doc = carry
    query, key, value, doc = block
    width = query.shape[-1]
    scores = jnp.einsum('ihf,jhf->hij', query, key, precision=highest)
    poly = 1.0 + scores / math.sqrt(width) + scores * scores / (2.0 * width)
    count = doc.shape[0]
    causal = jnp.arange(count)[:, None] >= jnp.arange(count)[None, :]
    mask = causal & (doc[:, None] == doc[None, :])
    weight = jnp.where(mask[None], poly, 0.0)
    numer = jnp.einsum('hij,jhe->ihe', weight, value, precision=highest)
    denom = jnp.transpose(lax.optimization_barrier(jnp.sum(weight, axis=-1)))
    q_feat = taylor_map(query)
    k_feat = taylor_map(key)
    carry_mask = (doc == last_doc).astype(jnp.float32)
    numer = numer + carry_mask[:, None, None] * jnp.einsum('ihf,hfe->ihe', q_feat, state, precision=highest)
    denom = denom + carry_mask[:, None] * jnp.einsum('ihf,hf->ih', q_feat, norm_state, precision=highest)
    attended = numer / denom[:, :, None]
    keep = (doc[-1] == last_doc).astype(jnp.float32)
    tail = (doc == doc[-1]).astype(jnp.float32)
    new_state = keep * state + jnp.einsum('j,jhf,jhe->hfe', tail, k_feat, value, precision=highest)
    new_norm = keep * norm_state + jnp.einsum('j,jhf->hf', tail, k_feat, precision=highest)
    return ((new_state, new_norm, doc[-1]), attended)

def stream_attention(query, key, value, doc):
    count = query.shape[0] // BLOCK
    blocks = (query.reshape(count, BLOCK, HEADS, QK_DIM), key.reshape(count, BLOCK, HEADS, QK_DIM), value.reshape(count, BLOCK, HEADS, HEAD_V), doc.reshape(count, BLOCK))
    init = (jnp.zeros((HEADS, FEAT, HEAD_V), jnp.float32), jnp.zeros((HEADS, FEAT), jnp.float32), jnp.array(-1, jnp.int32))
    unused, attended = lax.scan(jax.checkpoint(block_step), init, blocks)
    return attended.reshape(query.shape[0], HEADS * HEAD_V)

def layer(rows, w_query, w_key, w_value, w_out, w_gate, w_up, w_down, gain_attn, gain_mlp, docs):
    streams = docs.shape[0]
    h1 = low(rms_norm(rows, gain_attn))
    query = low_back(low(matmul(h1, w_query)))
    key = low_back(low(matmul(h1, w_key)))
    value = low_back(low(matmul(h1, w_value)))
    attended = jax.vmap(stream_attention)(query.reshape(streams, STREAM, HEADS, QK_DIM), key.reshape(streams, STREAM, HEADS, QK_DIM), value.reshape(streams, STREAM, HEADS, HEAD_V), docs)
    attended = low(attended.reshape(rows.shape[0], D))
    mid = rows + low_back(matmul(attended, w_out))
    h2 = low(rms_norm(mid, gain_mlp))
    gate = low_back(matmul(h2, w_gate))
    up = low_back(matmul(h2, w_up))
    act = low(jax.nn.silu(gate) * up)
    return mid + low_back(matmul(act, w_down))

def reference(tokens, doc_lengths, w_query, w_key, w_value, w_out, w_gate, w_up, w_down, gain_attn, gain_mlp, cotangent):
    starts = jnp.cumsum(doc_lengths, axis=-1).astype(jnp.int32) - doc_lengths
    position = jnp.arange(STREAM, dtype=jnp.int32)
    docs = lax.optimization_barrier(jnp.sum((starts[:, :, None, :] <= position[None, None, :, None]).astype(jnp.int32), axis=-1)) - 1
    docs = docs.reshape(GROUPS * MICRO, STREAM).astype(jnp.int32)
    rows = tokens.astype(jnp.float32).reshape(GROUPS * MICRO * STREAM, D)
    params = [w.astype(jnp.float32) for w in (w_query, w_key, w_value, w_out, w_gate, w_up, w_down, gain_attn, gain_mlp)]

    def forward(rows_in, *weights):
        return layer(rows_in, *weights, docs)
    result, pull = jax.vjp(forward, rows, *params)
    grads = pull(cotangent.astype(jnp.float32).reshape(rows.shape))
    output = result.reshape(tokens.shape).astype(jnp.bfloat16)
    input_grad = grads[0].reshape(tokens.shape)
    return (output, input_grad, grads[1], grads[2], grads[3], grads[4], grads[5], grads[6], grads[7], grads[8], grads[9])
```

```python
import functools
import math

import jax
import jax.numpy as jnp
from jax import lax
from jax.experimental import pallas as pl
from jax.experimental.pallas import tpu as pltpu
from jax.sharding import PartitionSpec as P

D = 2048
HEADS = 16
QK_DIM = 16
FF = 5632
HEAD_V = 128
epsilon = 1e-06
MIB = 1024 * 1024


def dot(left, right):
    return jnp.dot(left, right, preferred_element_type=jnp.float32)


def contract(left, right, left_dim, right_dim):
    return lax.dot_general(
        left, right, (((left_dim,), (right_dim,)), ((), ())), preferred_element_type=jnp.float32
    )


def head_lanes(rows, head):
    lane = lax.broadcasted_iota(jnp.int32, rows.shape, 1)
    inside = (lane >= head * QK_DIM) & (lane < (head + 1) * QK_DIM)
    return jnp.where(inside, rows, jnp.zeros_like(rows))


def weights_of(query, key, head, first, base):
    scores = contract(head_lanes(query, head), key, 1, 1)
    row = base + lax.broadcasted_iota(jnp.int32, scores.shape, 0)
    column = lax.broadcasted_iota(jnp.int32, scores.shape, 1)
    mask = (column <= row) & (column >= first)
    poly = 1.0 + scores * (1.0 / math.sqrt(QK_DIM)) + scores * scores * (0.5 / QK_DIM)
    return scores, mask, jnp.where(mask, poly, 0.0)


def attend_kernel(heads, q_ref, k_ref, v_ref, first_ref, out_ref):
    rows = q_ref.shape[1]
    base = pl.program_id(1) * rows
    for head in range(heads):
        columns = slice(head * HEAD_V, (head + 1) * HEAD_V)
        unused, unused_mask, weight = weights_of(
            q_ref[0], k_ref[0], head, first_ref[0], base
        )
        denom = jnp.sum(weight, axis=1, keepdims=True)
        numer = dot(weight.astype(jnp.bfloat16), v_ref[0, :, columns])
        out_ref[0, :, columns] = (numer / denom).astype(jnp.bfloat16)


def attend(query, key, value, first, heads):
    streams, length, width = query.shape
    rows = min(256, length)
    return pl.pallas_call(
        functools.partial(attend_kernel, heads),
        grid=(streams, length // rows),
        in_specs=[
            pl.BlockSpec((1, rows, width), lambda m, i: (m, i, 0)),
            pl.BlockSpec((1, length, width), lambda m, i: (m, 0, 0)),
            pl.BlockSpec((1, length, heads * HEAD_V), lambda m, i: (m, 0, 0)),
            pl.BlockSpec((1, rows, 1), lambda m, i: (m, i, 0)),
        ],
        out_specs=pl.BlockSpec((1, rows, heads * HEAD_V), lambda m, i: (m, i, 0)),
        out_shape=jax.ShapeDtypeStruct(value.shape, jnp.bfloat16),
        compiler_params=pltpu.CompilerParams(vmem_limit_bytes=48 * MIB),
        name="attend",
    )(query, key, value, first)


def attend_back_kernel(
    heads, q_ref, k_ref, v_ref, first_ref, att_ref, g_ref, gq_ref, gk_ref, gv_ref, gk_sum, gv_sum
):
    rows = q_ref.shape[1]
    step = pl.program_id(1)
    base = step * rows

    @pl.when(step == 0)
    def _():
        gk_sum[...] = jnp.zeros_like(gk_sum)
        gv_sum[...] = jnp.zeros_like(gv_sum)

    query, key = q_ref[0], k_ref[0]
    g_query = jnp.zeros(query.shape, jnp.float32)
    for head in range(heads):
        columns = slice(head * HEAD_V, (head + 1) * HEAD_V)
        scores, mask, weight = weights_of(query, key, head, first_ref[0], base)
        denom = jnp.sum(weight, axis=1, keepdims=True)
        a = (g_ref[0, :, columns].astype(jnp.float32) / denom).astype(jnp.bfloat16)
        b = -jnp.sum(
            a.astype(jnp.float32) * att_ref[0, :, columns].astype(jnp.float32),
            axis=1,
            keepdims=True,
        )
        g_weight = contract(a, v_ref[0, :, columns], 1, 1) + b
        slope = 1.0 / math.sqrt(QK_DIM) + scores * (1.0 / QK_DIM)
        g_scores = jnp.where(mask, g_weight * slope, 0.0).astype(jnp.bfloat16)
        g_query += head_lanes(dot(g_scores, key), head)
        gk_sum[...] += contract(g_scores, head_lanes(query, head), 0, 0)
        gv_sum[:, columns] += contract(weight.astype(jnp.bfloat16), a, 0, 0)
    gq_ref[0] = g_query.astype(jnp.bfloat16)

    @pl.when(step == pl.num_programs(1) - 1)
    def _():
        gk_ref[0] = gk_sum[...].astype(jnp.bfloat16)
        gv_ref[0] = gv_sum[...].astype(jnp.bfloat16)


def attend_back(query, key, value, first, attended, grad, heads):
    streams, length, width = query.shape
    rows = min(256, length)
    some = pl.BlockSpec((1, rows, width), lambda m, i: (m, i, 0))
    all_narrow = pl.BlockSpec((1, length, width), lambda m, i: (m, 0, 0))
    all_wide = pl.BlockSpec((1, length, heads * HEAD_V), lambda m, i: (m, 0, 0))
    some_wide = pl.BlockSpec((1, rows, heads * HEAD_V), lambda m, i: (m, i, 0))
    return pl.pallas_call(
        functools.partial(attend_back_kernel, heads),
        grid=(streams, length // rows),
        in_specs=[
            some,
            all_narrow,
            all_wide,
            pl.BlockSpec((1, rows, 1), lambda m, i: (m, i, 0)),
            some_wide,
            some_wide,
        ],
        out_specs=[some, all_narrow, all_wide],
        out_shape=[
            jax.ShapeDtypeStruct(query.shape, jnp.bfloat16),
            jax.ShapeDtypeStruct(key.shape, jnp.bfloat16),
            jax.ShapeDtypeStruct(value.shape, jnp.bfloat16),
        ],
        scratch_shapes=[
            pltpu.VMEM((length, width), jnp.float32),
            pltpu.VMEM((length, heads * HEAD_V), jnp.float32),
        ],
        compiler_params=pltpu.CompilerParams(vmem_limit_bytes=56 * MIB),
        name="attend_back",
    )(query, key, value, first, attended, grad)


def norm_scale(rows):
    return lax.rsqrt(jnp.mean(rows * rows, axis=-1, keepdims=True) + epsilon)


def norm_backward(grad, normed, inverse, gain):
    scaled = grad * gain
    return inverse * (scaled - normed * jnp.mean(scaled * normed, axis=-1, keepdims=True))


def local(
    tokens,
    doc_lengths,
    w_query,
    w_key,
    w_value,
    w_out,
    w_gate,
    w_up,
    w_down,
    gain_attn,
    gain_mlp,
    cotangent,
):
    micro, span = tokens.shape[1:3]
    pieces, groups = lax.axis_size("seq"), lax.axis_size("dp")
    place = lax.axis_index("seq")
    length = pieces * span
    heads = max(1, HEADS // pieces)
    sharers = max(1, pieces // HEADS)
    streams = micro // sharers
    first_head = place // sharers * heads
    first_stream = place % sharers * streams
    qk, wide = heads * QK_DIM, heads * HEAD_V
    hidden = FF // pieces
    low = jnp.bfloat16

    attn_slice = jnp.concatenate(
        [
            lax.dynamic_slice_in_dim(w_value, first_head * HEAD_V, wide, 1),
            lax.dynamic_slice_in_dim(w_query, first_head * QK_DIM, qk, 1),
            lax.dynamic_slice_in_dim(w_key, first_head * QK_DIM, qk, 1),
        ],
        axis=1,
    )
    rows_dp = w_gate.shape[0]
    share = hidden // groups

    def hidden_columns(w):
        return lax.dynamic_slice_in_dim(
            w.reshape(rows_dp, groups, pieces, share), place, 1, 2
        ).reshape(rows_dp, hidden)

    ffn_slice = jnp.concatenate([hidden_columns(w_gate), hidden_columns(w_up)], axis=1)
    down_slice = lax.dynamic_slice_in_dim(w_down, place * share, share, 0)
    out_width = D // pieces
    out_slice = lax.dynamic_slice_in_dim(w_out, place * out_width, out_width, 1)

    def gather_dp(w):
        return lax.all_gather(w, "dp", axis=0, tiled=True)

    gains = gather_dp(jnp.stack([gain_attn, gain_mlp], axis=1)).astype(jnp.float32)
    gain_one, gain_two = gains[:, 0], gains[:, 1]
    attn_full = gather_dp(attn_slice)
    out_full = lax.all_gather(gather_dp(out_slice), "seq", axis=1, tiled=True)
    ffn_full = gather_dp(ffn_slice)
    down_full = gather_dp(down_slice)
    gate_full, up_full = ffn_full[:, :hidden], ffn_full[:, hidden:]

    lengths = lax.dynamic_slice_in_dim(doc_lengths[0], first_stream, streams, 0)
    starts = jnp.cumsum(lengths, axis=1) - lengths
    position = jnp.arange(length, dtype=jnp.int32)
    begun = starts[:, None, :] <= position[None, :, None]
    first = jnp.max(jnp.where(begun, starts[:, None, :], 0), axis=2)[..., None]

    rows = tokens[0].astype(jnp.float32)
    inverse_one = norm_scale(rows)
    plain_one = rows * inverse_one
    h_one = (plain_one * gain_one).astype(low)
    if sharers == 1:
        h_all = jnp.stack(
            [lax.all_gather(h_one[m], "seq", axis=0, tiled=True) for m in range(micro)]
        )
    else:
        h_all = lax.all_gather(h_one, "seq", axis=1, tiled=True)
        h_all = lax.dynamic_slice_in_dim(h_all, first_stream, streams, 0)
    h_flat = h_all.reshape(streams * length, D)
    projected = dot(h_flat, attn_full).astype(low)
    value = projected[:, :wide].reshape(streams, length, wide)
    query = projected[:, wide : wide + qk].reshape(streams, length, qk)
    key = projected[:, wide + qk :].reshape(streams, length, qk)
    att_heads = attend(query, key, value, first, heads)

    def to_tokens(by_head):
        sent = by_head.reshape(streams, pieces, span, wide)
        got = lax.all_to_all(sent, "seq", 1, 0, tiled=False)
        got = got.reshape(pieces // sharers, micro, span, wide)
        return got.transpose(1, 2, 0, 3).reshape(micro * span, HEADS * HEAD_V)

    def to_heads(by_token):
        sent = by_token.reshape(micro, span, pieces // sharers, wide).transpose(2, 0, 1, 3)
        sent = sent.reshape(pieces, streams, span, wide)
        got = lax.all_to_all(sent, "seq", 0, 1, tiled=False)
        return got.reshape(streams, length, wide)

    attended = to_tokens(att_heads)
    flat = rows.reshape(micro * span, D)
    mid = flat + dot(attended, out_full)
    inverse_two = norm_scale(mid)
    plain_two = mid * inverse_two
    h_two = (plain_two * gain_two).astype(low)
    cot = cotangent[0].reshape(micro * span, D)

    h_two_all = lax.all_gather(h_two, "seq", axis=0, tiled=True)
    cot_all = lax.all_gather(cot, "seq", axis=0, tiled=True)
    gate = dot(h_two_all, gate_full)
    up = dot(h_two_all, up_full)
    g_act = contract(cot_all, down_full, 1, 1)
    sigmoid = jax.nn.sigmoid(gate)
    silu = gate * sigmoid
    act = (silu * up).astype(low)
    g_gate = (g_act * up * sigmoid * (1.0 + gate * (1.0 - sigmoid))).astype(low)
    g_up = (g_act * silu).astype(low)
    g_h_two_part = (contract(g_gate, gate_full, 1, 1) + contract(g_up, up_full, 1, 1)).astype(low)
    out_part = dot(act, down_full).astype(low)

    def scatter(part):
        return lax.psum_scatter(part, "seq", scatter_dimension=0, tiled=True).astype(jnp.float32)

    g_h_two = scatter(g_h_two_part)
    output = (mid + scatter(out_part)).astype(low)
    grad_down = lax.psum_scatter(
        contract(act, cot_all, 0, 0).astype(low), "dp", scatter_dimension=0, tiled=True
    ).astype(jnp.float32)
    grad_ffn = lax.psum_scatter(
        jnp.concatenate(
            [contract(h_two_all, g_gate, 0, 0).astype(low), contract(h_two_all, g_up, 0, 0).astype(low)],
            axis=1,
        ),
        "dp",
        scatter_dimension=0,
        tiled=True,
    )

    g_mid = cot.astype(jnp.float32) + norm_backward(g_h_two, plain_two, inverse_two, gain_two)
    g_mid_low = g_mid.astype(low)
    g_att = to_heads(contract(g_mid_low, out_full, 1, 1).astype(low))
    g_query, g_key, g_value = attend_back(query, key, value, first, att_heads, g_att, heads)
    g_all = jnp.concatenate([g_value, g_query, g_key], axis=2).reshape(streams * length, -1)
    g_h_one_part = contract(g_all, attn_full, 1, 1).astype(low).reshape(streams, length, D)
    if sharers == 1:
        g_h_one = jnp.stack([scatter(g_h_one_part[m]) for m in range(micro)])
    else:
        padded = jnp.zeros((micro, length, D), low)
        padded = lax.dynamic_update_slice_in_dim(padded, g_h_one_part, first_stream, 0)
        g_h_one = lax.psum_scatter(padded, "seq", scatter_dimension=1, tiled=True)
        g_h_one = g_h_one.astype(jnp.float32)
    input_grad = g_mid.reshape(micro, span, D) + norm_backward(
        g_h_one, plain_one, inverse_one, gain_one
    )

    grad_attn = lax.psum_scatter(
        contract(h_flat, g_all, 0, 0).astype(low), "dp", scatter_dimension=0, tiled=True
    )
    own = rows_dp // pieces
    exchanged = lax.all_to_all(
        jnp.concatenate([grad_attn, grad_ffn], axis=1).reshape(pieces, own, -1), "seq", 0, 0
    ).astype(jnp.float32)
    attn_got = exchanged[:, :, : wide + 2 * qk]
    attn_got = jnp.sum(attn_got.reshape(pieces // sharers, sharers, own, -1), axis=1)

    def by_rows(block):
        return block.transpose(1, 0, 2).reshape(own, -1)

    grad_value = by_rows(attn_got[:, :, :wide])
    grad_query = by_rows(attn_got[:, :, wide : wide + qk])
    grad_key = by_rows(attn_got[:, :, wide + qk :])

    def by_hidden(block):
        return block.reshape(pieces, own, groups, share).transpose(1, 2, 0, 3).reshape(own, FF)

    ffn_got = exchanged[:, :, wide + 2 * qk :]
    grad_gate = by_hidden(ffn_got[:, :, :hidden])
    grad_up = by_hidden(ffn_got[:, :, hidden:])
    gain_part = jnp.stack(
        [
            jnp.sum(g_h_one * plain_one, axis=(0, 1)),
            jnp.sum(g_h_two * plain_two, axis=0),
        ],
        axis=1,
    )
    out_part = jnp.concatenate([contract(attended, g_mid_low, 0, 0), gain_part], axis=1)
    out_part = out_part.astype(low).reshape(groups, pieces, own, -1).transpose(1, 0, 2, 3)
    out_group = lax.psum_scatter(out_part, "seq", scatter_dimension=0, tiled=False)
    out_sum = lax.psum_scatter(out_group, "dp", scatter_dimension=0, tiled=False)
    out_sum = out_sum.astype(jnp.float32)
    return (
        output.reshape(tokens.shape),
        input_grad[None],
        grad_query,
        grad_key,
        grad_value,
        out_sum[:, :D],
        grad_gate,
        grad_up,
        grad_down,
        out_sum[:, D],
        out_sum[:, D + 1],
    )


def solution(mesh):
    by_token, by_row = P("dp", None, "seq", None), P("dp", None)
    grad_rows, grad_entries = P(("dp", "seq"), None), P(("dp", "seq"))
    return jax.shard_map(
        local,
        mesh=mesh,
        in_specs=(by_token, P("dp", None, None)) + (by_row,) * 7 + (P("dp"), P("dp"), by_token),
        out_specs=(by_token, by_token) + (grad_rows,) * 7 + (grad_entries,) * 2,
        check_vma=False,
    )
```

```python
import functools
import math

import jax
import jax.numpy as jnp
from jax import lax
from jax.experimental import pallas as pl
from jax.experimental.pallas import tpu as pltpu
from jax.sharding import PartitionSpec as P

D = 2048
HEADS = 16
QK_DIM = 16
FF = 5632
HEAD_V = 128
epsilon = 1e-06
MIB = 1024 * 1024


def dot(left, right):
    return jnp.dot(left, right, preferred_element_type=jnp.float32)


def contract(left, right, left_dim, right_dim):
    return lax.dot_general(
        left, right, (((left_dim,), (right_dim,)), ((), ())), preferred_element_type=jnp.float32
    )


def head_lanes(rows, head):
    lane = lax.broadcasted_iota(jnp.int32, rows.shape, 1)
    inside = (lane >= head * QK_DIM) & (lane < (head + 1) * QK_DIM)
    return jnp.where(inside, rows, jnp.zeros_like(rows))


def weights_of(query, key, head, first, base):
    scores = contract(head_lanes(query, head), key, 1, 1)
    row = base + lax.broadcasted_iota(jnp.int32, scores.shape, 0)
    column = lax.broadcasted_iota(jnp.int32, scores.shape, 1)
    mask = (column <= row) & (column >= first)
    poly = 1.0 + scores * (1.0 / math.sqrt(QK_DIM)) + scores * scores * (0.5 / QK_DIM)
    return scores, mask, jnp.where(mask, poly, 0.0)


def attend_kernel(heads, q_ref, k_ref, v_ref, first_ref, out_ref):
    rows = q_ref.shape[1]
    base = pl.program_id(1) * rows
    for head in range(heads):
        columns = slice(head * HEAD_V, (head + 1) * HEAD_V)
        unused, unused_mask, weight = weights_of(
            q_ref[0], k_ref[0], head, first_ref[0], base
        )
        denom = jnp.sum(weight, axis=1, keepdims=True)
        numer = dot(weight.astype(jnp.bfloat16), v_ref[0, :, columns])
        out_ref[0, :, columns] = (numer / denom).astype(jnp.bfloat16)


def attend(query, key, value, first, heads):
    streams, length, width = query.shape
    rows = min(256, length)
    return pl.pallas_call(
        functools.partial(attend_kernel, heads),
        grid=(streams, length // rows),
        in_specs=[
            pl.BlockSpec((1, rows, width), lambda m, i: (m, i, 0)),
            pl.BlockSpec((1, length, width), lambda m, i: (m, 0, 0)),
            pl.BlockSpec((1, length, heads * HEAD_V), lambda m, i: (m, 0, 0)),
            pl.BlockSpec((1, rows, 1), lambda m, i: (m, i, 0)),
        ],
        out_specs=pl.BlockSpec((1, rows, heads * HEAD_V), lambda m, i: (m, i, 0)),
        out_shape=jax.ShapeDtypeStruct(value.shape, jnp.bfloat16),
        compiler_params=pltpu.CompilerParams(vmem_limit_bytes=48 * MIB),
        name="attend",
    )(query, key, value, first)


def attend_back_kernel(
    heads, q_ref, k_ref, v_ref, first_ref, att_ref, g_ref, gq_ref, gk_ref, gv_ref, gk_sum, gv_sum
):
    rows = q_ref.shape[1]
    step = pl.program_id(1)
    base = step * rows

    @pl.when(step == 0)
    def _():
        gk_sum[...] = jnp.zeros_like(gk_sum)
        gv_sum[...] = jnp.zeros_like(gv_sum)

    query, key = q_ref[0], k_ref[0]
    g_query = jnp.zeros(query.shape, jnp.float32)
    for head in range(heads):
        columns = slice(head * HEAD_V, (head + 1) * HEAD_V)
        scores, mask, weight = weights_of(query, key, head, first_ref[0], base)
        denom = jnp.sum(weight, axis=1, keepdims=True)
        a = (g_ref[0, :, columns].astype(jnp.float32) / denom).astype(jnp.bfloat16)
        b = -jnp.sum(
            a.astype(jnp.float32) * att_ref[0, :, columns].astype(jnp.float32),
            axis=1,
            keepdims=True,
        )
        g_weight = contract(a, v_ref[0, :, columns], 1, 1) + b
        slope = 1.0 / math.sqrt(QK_DIM) + scores * (1.0 / QK_DIM)
        g_scores = jnp.where(mask, g_weight * slope, 0.0).astype(jnp.bfloat16)
        g_query += head_lanes(dot(g_scores, key), head)
        gk_sum[...] += contract(g_scores, head_lanes(query, head), 0, 0)
        gv_sum[:, columns] += contract(weight.astype(jnp.bfloat16), a, 0, 0)
    gq_ref[0] = g_query.astype(jnp.bfloat16)

    @pl.when(step == pl.num_programs(1) - 1)
    def _():
        gk_ref[0] = gk_sum[...].astype(jnp.bfloat16)
        gv_ref[0] = gv_sum[...].astype(jnp.bfloat16)


def attend_back(query, key, value, first, attended, grad, heads):
    streams, length, width = query.shape
    rows = min(256, length)
    some = pl.BlockSpec((1, rows, width), lambda m, i: (m, i, 0))
    all_narrow = pl.BlockSpec((1, length, width), lambda m, i: (m, 0, 0))
    all_wide = pl.BlockSpec((1, length, heads * HEAD_V), lambda m, i: (m, 0, 0))
    some_wide = pl.BlockSpec((1, rows, heads * HEAD_V), lambda m, i: (m, i, 0))
    return pl.pallas_call(
        functools.partial(attend_back_kernel, heads),
        grid=(streams, length // rows),
        in_specs=[
            some,
            all_narrow,
            all_wide,
            pl.BlockSpec((1, rows, 1), lambda m, i: (m, i, 0)),
            some_wide,
            some_wide,
        ],
        out_specs=[some, all_narrow, all_wide],
        out_shape=[
            jax.ShapeDtypeStruct(query.shape, jnp.bfloat16),
            jax.ShapeDtypeStruct(key.shape, jnp.bfloat16),
            jax.ShapeDtypeStruct(value.shape, jnp.bfloat16),
        ],
        scratch_shapes=[
            pltpu.VMEM((length, width), jnp.float32),
            pltpu.VMEM((length, heads * HEAD_V), jnp.float32),
        ],
        compiler_params=pltpu.CompilerParams(vmem_limit_bytes=56 * MIB),
        name="attend_back",
    )(query, key, value, first, attended, grad)

MESH = pl.DeviceIdType.MESH
LOW = jnp.bfloat16


def partners():
    me = lax.axis_index("seq")
    core, x, y = me % 2, me // 2 % 2, me // 4
    return me, me + 1 - 2 * core, me + 2 - 4 * x, me + 4 - 8 * y


def greet(others):
    barrier = pltpu.get_barrier_semaphore()
    for other in others:
        pl.semaphore_signal(barrier, inc=1, device_id={"seq": other}, device_id_type=MESH)
    pl.semaphore_wait(barrier, len(others))


def remote(send, recv, k, src, dst, to):
    return pltpu.make_async_remote_copy(
        src_ref=src,
        dst_ref=dst,
        send_sem=send.at[k],
        recv_sem=recv.at[k],
        device_id={"seq": to},
        device_id_type=MESH,
    )


def gather_kernel(x_ref, o_ref, send, recv, own_sem):
    me, sib, xn, yn = partners()
    diag = xn + yn - me
    half = x_ref.shape[0] // 2
    copy = functools.partial(remote, send, recv)
    upper, lower = pl.ds(0, half), pl.ds(half, half)
    greet((sib, xn, yn))
    own = pltpu.make_async_copy(x_ref, o_ref.at[me], own_sem)
    own.start()
    xa = copy(0, x_ref.at[upper], o_ref.at[me, upper], xn)
    yb = copy(1, x_ref.at[lower], o_ref.at[me, lower], yn)
    xb = copy(2, x_ref.at[lower], o_ref.at[me, lower], xn)
    ya = copy(3, x_ref.at[upper], o_ref.at[me, upper], yn)
    beside = [copy(4, x_ref, o_ref.at[me], sib)]
    started = [xa, yb, xb, ya, beside[0]]
    for c in started:
        c.start()

    def pass_on(k, origin, part, to):
        block = o_ref.at[origin, part]
        c = copy(k, block, block, to)
        c.start()
        started.append(c)
        return c

    xa.wait_recv()
    fy = pass_on(5, xn, upper, yn)
    beside.append(pass_on(6, xn, upper, sib))
    yb.wait_recv()
    fx = pass_on(7, yn, lower, xn)
    beside.append(pass_on(8, yn, lower, sib))
    xb.wait_recv()
    beside.append(pass_on(9, xn, lower, sib))
    ya.wait_recv()
    beside.append(pass_on(10, yn, upper, sib))
    fy.wait_recv()
    beside.append(pass_on(11, diag, upper, sib))
    fx.wait_recv()
    beside.append(pass_on(12, diag, lower, sib))
    own.wait()
    for c in beside:
        c.wait_recv()
    for c in started:
        c.wait_send()


def moved(nbytes):
    return pl.CostEstimate(flops=0, bytes_accessed=nbytes * 10, transcendentals=0)


def gather_plane(x, number):
    pieces = lax.axis_size("seq")
    if pieces != 8:
        return lax.all_gather(x, "seq", axis=0)
    return pl.pallas_call(
        gather_kernel,
        out_shape=jax.ShapeDtypeStruct((8,) + x.shape, x.dtype),
        in_specs=[pl.BlockSpec(memory_space=pl.ANY)],
        out_specs=pl.BlockSpec(memory_space=pl.ANY),
        scratch_shapes=[
            pltpu.SemaphoreType.DMA((13,)),
            pltpu.SemaphoreType.DMA((13,)),
            pltpu.SemaphoreType.DMA,
        ],
        compiler_params=pltpu.CompilerParams(collective_id=number, has_side_effects=True),
        cost_estimate=moved(16 * x.size),
        name="gather",
    )(x)


def scatter_kernel(p_ref, o_ref, held, got, one, two, send, recv, own_sem):
    me, sib, xn, yn = partners()
    diag = xn + yn - me
    half = p_ref.shape[1] // 2
    copy = functools.partial(remote, send, recv)
    upper, lower = pl.ds(0, half), pl.ds(half, half)
    greet((sib, xn, yn))
    beside, loads = [], []
    for i, owner in enumerate((diag, xn, yn, me)):
        beside.append(copy(i, p_ref.at[owner + sib - me], got.at[i], sib))
        loads.append(pltpu.make_async_copy(p_ref.at[owner], held.at[i], own_sem.at[i]))
        beside[i].start()
        loads[i].start()

    def pair_sum(i):
        beside[i].wait_recv()
        loads[i].wait()
        held[i] = held[i] + got[i]

    pair_sum(0)
    x0 = copy(4, held.at[0, upper], one.at[0], xn)
    x0.start()
    y0 = copy(5, held.at[0, lower], one.at[1], yn)
    y0.start()
    pair_sum(1)
    x1 = copy(6, held.at[1, upper], one.at[2], xn)
    x1.start()
    pair_sum(2)
    y1 = copy(7, held.at[2, lower], one.at[3], yn)
    y1.start()
    pair_sum(3)
    x0.wait_recv()
    held[2, :half] = held[2, :half] + one[0]
    y2 = copy(8, held.at[2, upper], two.at[0], yn)
    y2.start()
    y0.wait_recv()
    held[1, half:] = held[1, half:] + one[1]
    x2 = copy(9, held.at[1, lower], two.at[1], xn)
    x2.start()
    x1.wait_recv()
    y1.wait_recv()
    y2.wait_recv()
    wide = jnp.float32
    o_ref[:half] = held[3, :half].astype(wide) + one[2].astype(wide) + two[0].astype(wide)
    x2.wait_recv()
    o_ref[half:] = held[3, half:].astype(wide) + one[3].astype(wide) + two[1].astype(wide)
    for c in (*beside, x0, y0, x1, y1, y2, x2):
        c.wait_send()


def scatter_plane(part, number):
    pieces, rows, columns = part.shape
    if pieces != 8:
        return lax.psum_scatter(part, "seq", scatter_dimension=0).astype(jnp.float32)
    return pl.pallas_call(
        scatter_kernel,
        out_shape=jax.ShapeDtypeStruct((rows, columns), jnp.float32),
        in_specs=[pl.BlockSpec(memory_space=pl.ANY)],
        out_specs=pl.BlockSpec(memory_space=pltpu.VMEM),
        scratch_shapes=[
            pltpu.VMEM((4, rows, columns), LOW),
            pltpu.VMEM((4, rows, columns), LOW),
            pltpu.VMEM((4, rows // 2, columns), LOW),
            pltpu.VMEM((2, rows // 2, columns), LOW),
            pltpu.SemaphoreType.DMA((10,)),
            pltpu.SemaphoreType.DMA((10,)),
            pltpu.SemaphoreType.DMA((4,)),
        ],
        compiler_params=pltpu.CompilerParams(
            collective_id=number, has_side_effects=True, vmem_limit_bytes=40 * MIB
        ),
        cost_estimate=moved(2 * part.size),
        name="scatter",
    )(part)


def exchange_kernel(x_ref, o_ref, send, recv, own_sem):
    me = lax.axis_index("seq")
    others = [lax.rem(me + i, 8) for i in range(1, 8)]
    greet(others)
    own = pltpu.make_async_copy(x_ref.at[me], o_ref.at[me], own_sem)
    own.start()
    copies = [
        remote(send, recv, i, x_ref.at[other], o_ref.at[me], other)
        for i, other in enumerate(others)
    ]
    for c in copies:
        c.start()
    own.wait()
    for c in copies:
        c.wait()


def exchange_plane(x, number):
    if lax.axis_size("seq") != 8:
        return lax.all_to_all(x, "seq", 0, 0)
    return pl.pallas_call(
        exchange_kernel,
        out_shape=jax.ShapeDtypeStruct(x.shape, x.dtype),
        in_specs=[pl.BlockSpec(memory_space=pl.ANY)],
        out_specs=pl.BlockSpec(memory_space=pl.ANY),
        scratch_shapes=[
            pltpu.SemaphoreType.DMA((7,)),
            pltpu.SemaphoreType.DMA((7,)),
            pltpu.SemaphoreType.DMA,
        ],
        compiler_params=pltpu.CompilerParams(collective_id=number, has_side_effects=True),
        cost_estimate=moved(4 * x.size),
        name="exchange",
    )(x)


def norm_scale(rows):
    return lax.rsqrt(jnp.mean(rows * rows, axis=-1, keepdims=True) + epsilon)


def norm_backward(grad, normed, inverse, gain):
    scaled = grad * gain
    return inverse * (scaled - normed * jnp.mean(scaled * normed, axis=-1, keepdims=True))


def local(
    tokens,
    doc_lengths,
    w_query,
    w_key,
    w_value,
    w_out,
    w_gate,
    w_up,
    w_down,
    gain_attn,
    gain_mlp,
    cotangent,
):
    micro, span = tokens.shape[1:3]
    pieces, groups = lax.axis_size("seq"), lax.axis_size("dp")
    place = lax.axis_index("seq")
    length = pieces * span
    heads = max(1, HEADS // pieces)
    sharers = max(1, pieces // HEADS)
    streams = micro // sharers
    first_head = place // sharers * heads
    first_stream = place % sharers * streams
    qk, wide = heads * QK_DIM, heads * HEAD_V
    hidden = FF // pieces

    out_width = D // pieces
    attn_slice = jnp.concatenate(
        [
            lax.dynamic_slice_in_dim(w_value, first_head * HEAD_V, wide, 1),
            lax.dynamic_slice_in_dim(w_out, place * out_width, out_width, 1),
            lax.dynamic_slice_in_dim(w_query, first_head * QK_DIM, qk, 1),
            lax.dynamic_slice_in_dim(w_key, first_head * QK_DIM, qk, 1),
            gain_attn[:, None],
            gain_mlp[:, None],
        ],
        axis=1,
    )
    rows_dp = w_gate.shape[0]
    share = hidden // groups
    block = FF // groups

    def hidden_columns(w):
        return [
            lax.dynamic_slice_in_dim(w, z * block + place * share, share, 1) for z in range(groups)
        ]

    ffn_slice = jnp.concatenate(hidden_columns(w_gate) + hidden_columns(w_up), axis=1)
    down_slice = lax.dynamic_slice_in_dim(w_down, place * share, share, 0)

    def gather_dp(w):
        return lax.all_gather(w, "dp", axis=0, tiled=True)

    attn_got = gather_dp(attn_slice)
    ffn_full = gather_dp(ffn_slice)
    down_full = gather_dp(down_slice)
    value_full = attn_got[:, :wide]
    query_full = attn_got[:, wide + out_width : wide + out_width + qk]
    key_full = attn_got[:, wide + out_width + qk : wide + out_width + 2 * qk]
    gains = attn_got[:, wide + out_width + 2 * qk :].astype(jnp.float32)
    gain_one, gain_two = gains[:, 0], gains[:, 1]
    gate_full, up_full = ffn_full[:, :hidden], ffn_full[:, hidden:]

    lengths = lax.dynamic_slice_in_dim(doc_lengths[0], first_stream, streams, 0)
    starts = jnp.cumsum(lengths, axis=1) - lengths
    position = jnp.arange(length, dtype=jnp.int32)
    begun = starts[:, None, :] <= position[None, :, None]
    first = jnp.max(jnp.where(begun, starts[:, None, :], 0), axis=2)[..., None]

    mine = micro * span
    cot = cotangent[0].reshape(mine, D)
    x_all = gather_plane(tokens[0].reshape(mine, D), 1)
    out_full = gather_plane(attn_got[:, wide : wide + out_width], 2)
    x_all = x_all.reshape(pieces, micro, span, D).transpose(1, 0, 2, 3)
    x_all = lax.dynamic_slice_in_dim(x_all, first_stream, streams, 0)
    x_all = x_all.astype(jnp.float32)
    h_flat = (x_all * norm_scale(x_all) * gain_one).astype(LOW).reshape(streams * length, D)
    value = dot(h_flat, value_full).astype(LOW).reshape(streams, length, wide)
    query = dot(h_flat, query_full).astype(LOW).reshape(streams, length, qk)
    key = dot(h_flat, key_full).astype(LOW).reshape(streams, length, qk)
    att_heads = attend(query, key, value, first, heads)

    def to_tokens(by_head):
        sent = by_head.reshape(streams, pieces, span, wide).transpose(1, 0, 2, 3)
        got = exchange_plane(sent, 3).reshape(pieces // sharers, micro, span, wide)
        return got.transpose(1, 2, 0, 3).reshape(mine, HEADS * HEAD_V)

    def to_heads(by_token):
        sent = by_token.reshape(micro, span, pieces // sharers, wide).transpose(2, 0, 1, 3)
        got = exchange_plane(sent.reshape(pieces, streams, span, wide), 4)
        return got.transpose(1, 0, 2, 3).reshape(streams, length, wide)

    attended = to_tokens(att_heads)
    flat = tokens[0].reshape(mine, D).astype(jnp.float32)
    mid = flat + jnp.einsum(
        "tk,skn->tsn", attended, out_full, preferred_element_type=jnp.float32
    ).reshape(mine, D)
    inverse_two = norm_scale(mid)
    plain_two = mid * inverse_two
    h_two = (plain_two * gain_two).astype(LOW)

    h_two_all = gather_plane(h_two, 5).reshape(-1, D)
    cot_all = gather_plane(cot, 6).reshape(-1, D)
    gate = dot(h_two_all, gate_full)
    up = dot(h_two_all, up_full)
    g_act = contract(cot_all, down_full, 1, 1)
    sigmoid = jax.nn.sigmoid(gate)
    silu = gate * sigmoid
    act = (silu * up).astype(LOW)
    g_gate = (g_act * up * sigmoid * (1.0 + gate * (1.0 - sigmoid))).astype(LOW)
    g_up = (g_act * silu).astype(LOW)
    g_h_two_part = (contract(g_gate, gate_full, 1, 1) + contract(g_up, up_full, 1, 1)).astype(LOW)
    g_h_two = scatter_plane(g_h_two_part.reshape(pieces, mine, D), 7)
    grad_down = lax.psum_scatter(
        contract(act, cot_all, 0, 0).astype(LOW), "dp", scatter_dimension=0, tiled=True
    ).astype(jnp.float32)
    grad_ffn = lax.psum_scatter(
        jnp.concatenate(
            [contract(h_two_all, g_gate, 0, 0).astype(LOW), contract(h_two_all, g_up, 0, 0).astype(LOW)],
            axis=1,
        ),
        "dp",
        scatter_dimension=0,
        tiled=True,
    )
    out_part = dot(act, down_full).astype(LOW)
    output = (mid + scatter_plane(out_part.reshape(pieces, mine, D), 8)).astype(LOW)

    g_mid = cot.astype(jnp.float32) + norm_backward(g_h_two, plain_two, inverse_two, gain_two)
    g_mid_low = g_mid.astype(LOW)
    g_att = jnp.einsum(
        "tsn,skn->tk",
        g_mid_low.reshape(mine, pieces, out_width),
        out_full,
        preferred_element_type=jnp.float32,
    )
    g_att = to_heads(g_att.astype(LOW))
    g_query, g_key, g_value = attend_back(query, key, value, first, att_heads, g_att, heads)
    g_value = g_value.reshape(streams * length, wide)
    g_query = g_query.reshape(streams * length, qk)
    g_key = g_key.reshape(streams * length, qk)
    g_h_one_part = (
        contract(g_value, value_full, 1, 1)
        + contract(g_query, query_full, 1, 1)
        + contract(g_key, key_full, 1, 1)
    ).astype(LOW)
    g_h_one_part = g_h_one_part.reshape(streams, pieces, span, D).transpose(1, 0, 2, 3)
    if sharers > 1:
        padded = jnp.zeros((pieces, micro, span, D), LOW)
        g_h_one_part = lax.dynamic_update_slice_in_dim(padded, g_h_one_part, first_stream, 1)
    g_h_one = scatter_plane(g_h_one_part.reshape(pieces, mine, D), 9)
    inverse_one = norm_scale(flat)
    plain_one = flat * inverse_one
    input_grad = g_mid + norm_backward(g_h_one, plain_one, inverse_one, gain_one)

    own = rows_dp // pieces
    grad_out = contract(attended, g_mid_low, 0, 0).astype(LOW)
    grad_out = grad_out.reshape(groups, pieces, own, D).transpose(1, 0, 2, 3)
    grad_out = scatter_plane(grad_out.reshape(pieces, groups * own, D), 10).astype(LOW)
    grad_out = lax.psum_scatter(grad_out, "dp", scatter_dimension=0, tiled=True)
    grad_attn = jnp.concatenate(
        [
            contract(h_flat, g_value, 0, 0).astype(LOW),
            contract(h_flat, g_query, 0, 0).astype(LOW),
            contract(h_flat, g_key, 0, 0).astype(LOW),
            jnp.sum(g_h_one * plain_one, axis=0).astype(LOW)[:, None],
            jnp.sum(g_h_two * plain_two, axis=0).astype(LOW)[:, None],
        ],
        axis=1,
    )
    grad_attn = lax.psum_scatter(grad_attn, "dp", scatter_dimension=0, tiled=True)
    ffn_got = exchange_plane(grad_ffn.reshape(pieces, own, 2 * hidden), 11).astype(jnp.float32)
    attn_got = exchange_plane(grad_attn.reshape(pieces, own, -1), 12).astype(jnp.float32)
    grad_gains = jnp.sum(attn_got[:, :, wide + 2 * qk :], axis=0)
    attn_got = jnp.sum(attn_got.reshape(pieces // sharers, sharers, own, -1), axis=1)

    def by_rows(block):
        return block.transpose(1, 0, 2).reshape(own, -1)

    def by_hidden(block):
        return block.reshape(pieces, own, groups, share).transpose(1, 2, 0, 3).reshape(own, FF)

    return (
        output.reshape(tokens.shape),
        input_grad.reshape(tokens.shape),
        by_rows(attn_got[:, :, wide : wide + qk]),
        by_rows(attn_got[:, :, wide + qk : wide + 2 * qk]),
        by_rows(attn_got[:, :, :wide]),
        grad_out.astype(jnp.float32),
        by_hidden(ffn_got[:, :, :hidden]),
        by_hidden(ffn_got[:, :, hidden:]),
        grad_down,
        grad_gains[:, 0],
        grad_gains[:, 1],
    )


def solution(mesh):
    by_token, by_row = P("dp", None, "seq", None), P("dp", None)
    grad_rows, grad_entries = P(("dp", "seq"), None), P(("dp", "seq"))
    return jax.shard_map(
        local,
        mesh=mesh,
        in_specs=(by_token, P("dp", None, None)) + (by_row,) * 7 + (P("dp"), P("dp"), by_token),
        out_specs=(by_token, by_token) + (grad_rows,) * 7 + (grad_entries,) * 2,
        check_vma=False,
    )
```

```python
import functools
import math

import jax
import jax.numpy as jnp
from jax import lax
from jax.experimental import pallas as pl
from jax.experimental.pallas import tpu as pltpu
from jax.sharding import PartitionSpec as P

D = 2048
HEADS = 16
QK_DIM = 16
FF = 5632
HEAD_V = 128
epsilon = 1e-06
MIB = 1024 * 1024


def dot(left, right):
    return jnp.dot(left, right, preferred_element_type=jnp.float32)


def contract(left, right, left_dim, right_dim):
    return lax.dot_general(
        left, right, (((left_dim,), (right_dim,)), ((), ())), preferred_element_type=jnp.float32
    )


def head_lanes(rows, head):
    lane = lax.broadcasted_iota(jnp.int32, rows.shape, 1)
    inside = (lane >= head * QK_DIM) & (lane < (head + 1) * QK_DIM)
    return jnp.where(inside, rows, jnp.zeros_like(rows))


def weights_of(query, key, head, first, base):
    scores = contract(head_lanes(query, head), key, 1, 1)
    row = base + lax.broadcasted_iota(jnp.int32, scores.shape, 0)
    column = lax.broadcasted_iota(jnp.int32, scores.shape, 1)
    mask = (column <= row) & (column >= first)
    poly = 1.0 + scores * (1.0 / math.sqrt(QK_DIM)) + scores * scores * (0.5 / QK_DIM)
    return scores, mask, jnp.where(mask, poly, 0.0)


def attend_kernel(heads, q_ref, k_ref, v_ref, first_ref, out_ref):
    rows = q_ref.shape[1]
    base = pl.program_id(1) * rows
    for head in range(heads):
        columns = slice(head * HEAD_V, (head + 1) * HEAD_V)
        unused, unused_mask, weight = weights_of(
            q_ref[0], k_ref[0], head, first_ref[0], base
        )
        denom = jnp.sum(weight, axis=1, keepdims=True)
        numer = dot(weight.astype(jnp.bfloat16), v_ref[0, :, columns])
        out_ref[0, :, columns] = (numer / denom).astype(jnp.bfloat16)


def attend(query, key, value, first, heads):
    streams, length, width = query.shape
    rows = min(256, length)
    return pl.pallas_call(
        functools.partial(attend_kernel, heads),
        grid=(streams, length // rows),
        in_specs=[
            pl.BlockSpec((1, rows, width), lambda m, i: (m, i, 0)),
            pl.BlockSpec((1, length, width), lambda m, i: (m, 0, 0)),
            pl.BlockSpec((1, length, heads * HEAD_V), lambda m, i: (m, 0, 0)),
            pl.BlockSpec((1, rows, 1), lambda m, i: (m, i, 0)),
        ],
        out_specs=pl.BlockSpec((1, rows, heads * HEAD_V), lambda m, i: (m, i, 0)),
        out_shape=jax.ShapeDtypeStruct(value.shape, jnp.bfloat16),
        compiler_params=pltpu.CompilerParams(vmem_limit_bytes=48 * MIB),
        name="attend",
    )(query, key, value, first)


def attend_back_kernel(
    heads, q_ref, k_ref, v_ref, first_ref, att_ref, g_ref, gq_ref, gk_ref, gv_ref, gk_sum, gv_sum
):
    rows = q_ref.shape[1]
    step = pl.program_id(1)
    base = step * rows

    @pl.when(step == 0)
    def _():
        gk_sum[...] = jnp.zeros_like(gk_sum)
        gv_sum[...] = jnp.zeros_like(gv_sum)

    query, key = q_ref[0], k_ref[0]
    g_query = jnp.zeros(query.shape, jnp.float32)
    for head in range(heads):
        columns = slice(head * HEAD_V, (head + 1) * HEAD_V)
        scores, mask, weight = weights_of(query, key, head, first_ref[0], base)
        denom = jnp.sum(weight, axis=1, keepdims=True)
        a = (g_ref[0, :, columns].astype(jnp.float32) / denom).astype(jnp.bfloat16)
        b = -jnp.sum(
            a.astype(jnp.float32) * att_ref[0, :, columns].astype(jnp.float32),
            axis=1,
            keepdims=True,
        )
        g_weight = contract(a, v_ref[0, :, columns], 1, 1) + b
        slope = 1.0 / math.sqrt(QK_DIM) + scores * (1.0 / QK_DIM)
        g_scores = jnp.where(mask, g_weight * slope, 0.0).astype(jnp.bfloat16)
        g_query += head_lanes(dot(g_scores, key), head)
        gk_sum[...] += contract(g_scores, head_lanes(query, head), 0, 0)
        gv_sum[:, columns] += contract(weight.astype(jnp.bfloat16), a, 0, 0)
    gq_ref[0] = g_query.astype(jnp.bfloat16)

    @pl.when(step == pl.num_programs(1) - 1)
    def _():
        gk_ref[0] = gk_sum[...].astype(jnp.bfloat16)
        gv_ref[0] = gv_sum[...].astype(jnp.bfloat16)


def attend_back(query, key, value, first, attended, grad, heads):
    streams, length, width = query.shape
    rows = min(256, length)
    some = pl.BlockSpec((1, rows, width), lambda m, i: (m, i, 0))
    all_narrow = pl.BlockSpec((1, length, width), lambda m, i: (m, 0, 0))
    all_wide = pl.BlockSpec((1, length, heads * HEAD_V), lambda m, i: (m, 0, 0))
    some_wide = pl.BlockSpec((1, rows, heads * HEAD_V), lambda m, i: (m, i, 0))
    return pl.pallas_call(
        functools.partial(attend_back_kernel, heads),
        grid=(streams, length // rows),
        in_specs=[
            some,
            all_narrow,
            all_wide,
            pl.BlockSpec((1, rows, 1), lambda m, i: (m, i, 0)),
            some_wide,
            some_wide,
        ],
        out_specs=[some, all_narrow, all_wide],
        out_shape=[
            jax.ShapeDtypeStruct(query.shape, jnp.bfloat16),
            jax.ShapeDtypeStruct(key.shape, jnp.bfloat16),
            jax.ShapeDtypeStruct(value.shape, jnp.bfloat16),
        ],
        scratch_shapes=[
            pltpu.VMEM((length, width), jnp.float32),
            pltpu.VMEM((length, heads * HEAD_V), jnp.float32),
        ],
        compiler_params=pltpu.CompilerParams(vmem_limit_bytes=56 * MIB),
        name="attend_back",
    )(query, key, value, first, attended, grad)

MESH = pl.DeviceIdType.MESH
LOW = jnp.bfloat16


def partners():
    me = lax.axis_index("seq")
    core, x, y = me % 2, me // 2 % 2, me // 4
    return me, me + 1 - 2 * core, me + 2 - 4 * x, me + 4 - 8 * y


def greet(others):
    barrier = pltpu.get_barrier_semaphore()
    for other in others:
        pl.semaphore_signal(barrier, inc=1, device_id={"seq": other}, device_id_type=MESH)
    pl.semaphore_wait(barrier, len(others))


def remote(send, recv, k, src, dst, to):
    return pltpu.make_async_remote_copy(
        src_ref=src,
        dst_ref=dst,
        send_sem=send.at[k],
        recv_sem=recv.at[k],
        device_id={"seq": to},
        device_id_type=MESH,
    )


def gather_kernel(x_ref, o_ref, send, recv, own_sem):
    me, sib, xn, yn = partners()
    diag = xn + yn - me
    half = x_ref.shape[0] // 2
    copy = functools.partial(remote, send, recv)
    upper, lower = pl.ds(0, half), pl.ds(half, half)
    greet((sib, xn, yn))
    own = pltpu.make_async_copy(x_ref, o_ref.at[me], own_sem)
    own.start()
    xa = copy(0, x_ref.at[upper], o_ref.at[me, upper], xn)
    yb = copy(1, x_ref.at[lower], o_ref.at[me, lower], yn)
    xb = copy(2, x_ref.at[lower], o_ref.at[me, lower], xn)
    ya = copy(3, x_ref.at[upper], o_ref.at[me, upper], yn)
    beside = [copy(4, x_ref, o_ref.at[me], sib)]
    started = [xa, yb, xb, ya, beside[0]]
    for c in started:
        c.start()

    def pass_on(k, origin, part, to):
        block = o_ref.at[origin, part]
        c = copy(k, block, block, to)
        c.start()
        started.append(c)
        return c

    xa.wait_recv()
    fy = pass_on(5, xn, upper, yn)
    beside.append(pass_on(6, xn, upper, sib))
    yb.wait_recv()
    fx = pass_on(7, yn, lower, xn)
    beside.append(pass_on(8, yn, lower, sib))
    xb.wait_recv()
    beside.append(pass_on(9, xn, lower, sib))
    ya.wait_recv()
    beside.append(pass_on(10, yn, upper, sib))
    fy.wait_recv()
    beside.append(pass_on(11, diag, upper, sib))
    fx.wait_recv()
    beside.append(pass_on(12, diag, lower, sib))
    own.wait()
    for c in beside:
        c.wait_recv()
    for c in started:
        c.wait_send()


def moved(nbytes):
    return pl.CostEstimate(flops=0, bytes_accessed=nbytes * 10, transcendentals=0)


def gather_plane(x, number):
    pieces = lax.axis_size("seq")
    if pieces != 8:
        return lax.all_gather(x, "seq", axis=0)
    return pl.pallas_call(
        gather_kernel,
        out_shape=jax.ShapeDtypeStruct((8,) + x.shape, x.dtype),
        in_specs=[pl.BlockSpec(memory_space=pl.ANY)],
        out_specs=pl.BlockSpec(memory_space=pl.ANY),
        scratch_shapes=[
            pltpu.SemaphoreType.DMA((13,)),
            pltpu.SemaphoreType.DMA((13,)),
            pltpu.SemaphoreType.DMA,
        ],
        compiler_params=pltpu.CompilerParams(collective_id=number, has_side_effects=True),
        cost_estimate=moved(16 * x.size),
        name="gather",
    )(x)


def scatter_kernel(p_ref, o_ref, held, got, one, two, send, recv, own_sem):
    me, sib, xn, yn = partners()
    diag = xn + yn - me
    half = p_ref.shape[1] // 2
    copy = functools.partial(remote, send, recv)
    upper, lower = pl.ds(0, half), pl.ds(half, half)
    greet((sib, xn, yn))
    beside, loads = [], []
    for i, owner in enumerate((diag, xn, yn, me)):
        beside.append(copy(i, p_ref.at[owner + sib - me], got.at[i], sib))
        loads.append(pltpu.make_async_copy(p_ref.at[owner], held.at[i], own_sem.at[i]))
        beside[i].start()
        loads[i].start()

    def pair_sum(i):
        beside[i].wait_recv()
        loads[i].wait()
        held[i] = held[i] + got[i]

    pair_sum(0)
    x0 = copy(4, held.at[0, upper], one.at[0], xn)
    x0.start()
    y0 = copy(5, held.at[0, lower], one.at[1], yn)
    y0.start()
    pair_sum(1)
    x1 = copy(6, held.at[1, upper], one.at[2], xn)
    x1.start()
    pair_sum(2)
    y1 = copy(7, held.at[2, lower], one.at[3], yn)
    y1.start()
    pair_sum(3)
    x0.wait_recv()
    held[2, :half] = held[2, :half] + one[0]
    y2 = copy(8, held.at[2, upper], two.at[0], yn)
    y2.start()
    y0.wait_recv()
    held[1, half:] = held[1, half:] + one[1]
    x2 = copy(9, held.at[1, lower], two.at[1], xn)
    x2.start()
    x1.wait_recv()
    y1.wait_recv()
    y2.wait_recv()
    wide = jnp.float32
    o_ref[:half] = held[3, :half].astype(wide) + one[2].astype(wide) + two[0].astype(wide)
    x2.wait_recv()
    o_ref[half:] = held[3, half:].astype(wide) + one[3].astype(wide) + two[1].astype(wide)
    for c in (*beside, x0, y0, x1, y1, y2, x2):
        c.wait_send()


def scatter_plane(part, number):
    pieces, rows, columns = part.shape
    if pieces != 8:
        return lax.psum_scatter(part, "seq", scatter_dimension=0).astype(jnp.float32)
    return pl.pallas_call(
        scatter_kernel,
        out_shape=jax.ShapeDtypeStruct((rows, columns), jnp.float32),
        in_specs=[pl.BlockSpec(memory_space=pl.ANY)],
        out_specs=pl.BlockSpec(memory_space=pltpu.VMEM),
        scratch_shapes=[
            pltpu.VMEM((4, rows, columns), LOW),
            pltpu.VMEM((4, rows, columns), LOW),
            pltpu.VMEM((4, rows // 2, columns), LOW),
            pltpu.VMEM((2, rows // 2, columns), LOW),
            pltpu.SemaphoreType.DMA((10,)),
            pltpu.SemaphoreType.DMA((10,)),
            pltpu.SemaphoreType.DMA((4,)),
        ],
        compiler_params=pltpu.CompilerParams(
            collective_id=number, has_side_effects=True, vmem_limit_bytes=40 * MIB
        ),
        cost_estimate=moved(2 * part.size),
        name="scatter",
    )(part)


def exchange_kernel(x_ref, o_ref, send, recv, own_sem):
    me = lax.axis_index("seq")
    others = [lax.rem(me + i, 8) for i in range(1, 8)]
    greet(others)
    own = pltpu.make_async_copy(x_ref.at[me], o_ref.at[me], own_sem)
    own.start()
    copies = [
        remote(send, recv, i, x_ref.at[other], o_ref.at[me], other)
        for i, other in enumerate(others)
    ]
    for c in copies:
        c.start()
    own.wait()
    for c in copies:
        c.wait()


def exchange_plane(x, number):
    if lax.axis_size("seq") != 8:
        return lax.all_to_all(x, "seq", 0, 0)
    return pl.pallas_call(
        exchange_kernel,
        out_shape=jax.ShapeDtypeStruct(x.shape, x.dtype),
        in_specs=[pl.BlockSpec(memory_space=pl.ANY)],
        out_specs=pl.BlockSpec(memory_space=pl.ANY),
        scratch_shapes=[
            pltpu.SemaphoreType.DMA((7,)),
            pltpu.SemaphoreType.DMA((7,)),
            pltpu.SemaphoreType.DMA,
        ],
        compiler_params=pltpu.CompilerParams(collective_id=number, has_side_effects=True),
        cost_estimate=moved(4 * x.size),
        name="exchange",
    )(x)


def ffn_kernel(
    h_ref,
    c_ref,
    wg_ref,
    wu_ref,
    wd_ref,
    h_all,
    out_part,
    gh_ref,
    dg_ref,
    du_ref,
    dd_ref,
    h_buf,
    c_buf,
    o_buf,
    beside,
    held,
    got,
    one,
    two,
    sum_g,
    sum_u,
    sum_d,
    emit,
    send,
    recv,
    load_sem,
    out_sem,
    emit_sem,
):
    me, sib, xn, yn = partners()
    diag = xn + yn - me
    flip = sib - me
    rows = h_ref.shape[0]
    half = rows // 2
    upper, lower = pl.ds(0, half), pl.ds(half, half)
    copy = functools.partial(remote, send, recv)

    xa = copy(0, h_ref.at[upper], h_all.at[me, upper], xn)
    yb = copy(1, h_ref.at[lower], h_all.at[me, lower], yn)
    xb = copy(2, h_ref.at[lower], h_all.at[me, lower], xn)
    ya = copy(3, h_ref.at[upper], h_all.at[me, upper], yn)
    s0 = copy(4, h_ref, h_all.at[me], sib)

    def pass_on(k, origin, part, to):
        return copy(k, h_all.at[origin, part], h_all.at[origin, part], to)

    fy = pass_on(5, xn, upper, yn)
    fx = pass_on(6, yn, lower, xn)
    s1 = pass_on(7, xn, upper, sib)
    s2 = pass_on(8, yn, lower, sib)
    s3 = pass_on(9, xn, lower, sib)
    s4 = pass_on(10, yn, upper, sib)
    s5 = pass_on(11, diag, upper, sib)
    s6 = pass_on(12, diag, lower, sib)
    b0 = copy(13, beside.at[0], got.at[0], sib)
    b1 = copy(14, beside.at[1], got.at[1], sib)
    b2 = copy(15, beside.at[0], got.at[2], sib)
    b3 = copy(16, beside.at[1], got.at[3], sib)
    x0 = copy(17, held.at[2, upper], one.at[0], xn)
    y0 = copy(18, held.at[2, lower], one.at[1], yn)
    x1 = copy(19, held.at[1, upper], one.at[2], xn)
    y1 = copy(20, held.at[3, lower], one.at[3], yn)
    y2 = copy(21, held.at[3, upper], two.at[0], yn)
    x2 = copy(22, held.at[1, lower], two.at[1], xn)

    def owner_of(step):
        chip = jnp.where(step < 4, xn, jnp.where(step < 6, diag, yn))
        later = chip + jnp.where(lax.rem(step, 2) == 0, flip, 0)
        return jnp.where(step == 0, me, jnp.where(step == 1, sib, later))

    def loads(step):
        slot = lax.rem(step, 2)
        owner = owner_of(step)
        return (
            pltpu.make_async_copy(h_all.at[owner], h_buf.at[slot], load_sem.at[0, slot]),
            pltpu.make_async_copy(c_ref.at[owner], c_buf.at[slot], load_sem.at[1, slot]),
        )

    def out_copy(step):
        slot = lax.rem(step, 2)
        return pltpu.make_async_copy(o_buf.at[slot], out_part.at[owner_of(step)], out_sem.at[slot])

    greet((sib, xn, yn))
    for c in (xa, yb, xb, ya, s0):
        c.start()
    first = (
        pltpu.make_async_copy(h_ref, h_buf.at[0], load_sem.at[0, 0]),
        pltpu.make_async_copy(c_ref.at[me], c_buf.at[0], load_sem.at[1, 0]),
    )
    for c in first:
        c.start()
    for total in (sum_g, sum_u, sum_d):
        total[...] = jnp.zeros_like(total)

    def arrive(step):
        @pl.when(step == 1)
        def _():
            s0.wait_recv()

        @pl.when(step == 2)
        def _():
            xa.wait_recv()
            yb.wait_recv()
            for c in (fy, fx, s1, s2):
                c.start()
            xb.wait_recv()
            ya.wait_recv()
            s3.start()
            s4.start()
            s1.wait_recv()
            s3.wait_recv()

        @pl.when(step == 4)
        def _():
            fy.wait_recv()
            fx.wait_recv()
            s5.start()
            s6.start()
            s5.wait_recv()
            s6.wait_recv()

        @pl.when(step == 6)
        def _():
            s2.wait_recv()
            s4.wait_recv()

        @pl.when(step == 7)
        def _():
            y0.wait_recv()
            held[1, half:] = held[1, half:] + one[1]
            x2.start()

    def body(step, carry):
        slot = lax.rem(step, 2)
        for c in loads(step):
            c.wait()
        h, c = h_buf[slot], c_buf[slot]
        gate = dot(h, wg_ref[...])
        up = dot(h, wu_ref[...])
        g_act = contract(c, wd_ref[...], 1, 1)
        sigmoid = jax.nn.sigmoid(gate)
        silu = gate * sigmoid
        act = (silu * up).astype(LOW)
        g_gate = (g_act * up * sigmoid * (1.0 + gate * (1.0 - sigmoid))).astype(LOW)
        g_up = (g_act * silu).astype(LOW)
        part = (contract(g_gate, wg_ref[...], 1, 1) + contract(g_up, wu_ref[...], 1, 1)).astype(LOW)

        for k, place, sent in ((1, 0, b0), (2, 1, b1), (4, 0, b2), (6, 1, b3)):

            @pl.when(step == k)
            def _(k=k, place=place, sent=sent):
                if k == 4:
                    b0.wait_send()
                if k == 6:
                    b1.wait_send()
                beside[place] = part
                sent.start()

        for k, place, arrived in ((0, 0, None), (3, 1, b1), (5, 2, b2), (7, 3, b3)):

            @pl.when(step == k)
            def _(k=k, place=place, arrived=arrived):
                if arrived is None:
                    held[place] = part
                else:
                    arrived.wait_recv()
                    held[place] = part + got[place]
                if k == 3:
                    x1.start()
                if k == 5:
                    x0.start()
                    y0.start()
                if k == 7:
                    y1.start()
                    x0.wait_recv()
                    held[3, :half] = held[3, :half] + one[0]
                    y2.start()

        @pl.when(step >= 2)
        def _():
            out_copy(step - 2).wait()

        o_buf[slot] = dot(act, wd_ref[...]).astype(LOW)
        out_copy(step).start()
        arrive(step + 1)

        @pl.when(step < 7)
        def _():
            for c in loads(step + 1):
                c.start()

        sum_g[...] += contract(h, g_gate, 0, 0)
        sum_u[...] += contract(h, g_up, 0, 0)
        sum_d[...] += contract(act, c, 0, 0)
        return carry

    lax.fori_loop(0, 8, body, 0)
    out_copy(6).wait()
    out_copy(7).wait()

    pending = [None, None]
    count = 0
    for total, target in ((sum_g, dg_ref), (sum_u, du_ref)):
        block = emit.shape[1]
        for start in range(0, total.shape[0], block):
            slot = count % 2
            if pending[slot] is not None:
                pending[slot].wait()
            emit[slot] = total[start : start + block].astype(LOW)
            pending[slot] = pltpu.make_async_copy(
                emit.at[slot], target.at[pl.ds(start, block)], emit_sem.at[slot]
            )
            pending[slot].start()
            count += 1
    hidden = sum_d.shape[0]
    downs = []
    for slot, start in enumerate(range(0, hidden, rows)):
        size = min(rows, hidden - start)
        if slot >= 2:
            downs[slot - 2].wait()
        o_buf[slot % 2, :size] = sum_d[start : start + size].astype(LOW)
        downs.append(
            pltpu.make_async_copy(
                o_buf.at[slot % 2, pl.ds(0, size)],
                dd_ref.at[pl.ds(start, size)],
                out_sem.at[slot % 2],
            )
        )
        downs[-1].start()

    b0.wait_recv()
    wide = jnp.float32
    x1.wait_recv()
    y1.wait_recv()
    y2.wait_recv()
    own = held[0, :half].astype(wide) + got[0, :half].astype(wide)
    gh_ref[:half] = own + one[2].astype(wide) + two[0].astype(wide)
    x2.wait_recv()
    own = held[0, half:].astype(wide) + got[0, half:].astype(wide)
    gh_ref[half:] = own + one[3].astype(wide) + two[1].astype(wide)
    for c in downs[-2:]:
        c.wait()
    for c in pending:
        c.wait()
    for c in (xa, yb, xb, ya, s0, fy, fx, s1, s2, s3, s4, s5, s6, b2, b3, x0, y0, x1, y1, y2, x2):
        c.wait_send()


def ffn_plane(h_two, cot_all, gate_full, up_full, down_full):
    rows, width = h_two.shape
    hidden = gate_full.shape[1]
    anywhere = pl.BlockSpec(memory_space=pl.ANY)
    in_vmem = pl.BlockSpec(memory_space=pltpu.VMEM)
    emit_rows = 256
    shape = jax.ShapeDtypeStruct
    unused, out_part, g_h_two, d_gate, d_up, d_down = pl.pallas_call(
        ffn_kernel,
        out_shape=[
            shape((8, rows, width), LOW),
            shape((8, rows, width), LOW),
            shape((rows, width), jnp.float32),
            shape((width, hidden), LOW),
            shape((width, hidden), LOW),
            shape((hidden, width), LOW),
        ],
        in_specs=[anywhere, anywhere, in_vmem, in_vmem, in_vmem],
        out_specs=[anywhere, anywhere, in_vmem, anywhere, anywhere, anywhere],
        scratch_shapes=[
            pltpu.VMEM((2, rows, width), LOW),
            pltpu.VMEM((2, rows, width), LOW),
            pltpu.VMEM((2, rows, width), LOW),
            pltpu.VMEM((2, rows, width), LOW),
            pltpu.VMEM((4, rows, width), LOW),
            pltpu.VMEM((4, rows, width), LOW),
            pltpu.VMEM((4, rows // 2, width), LOW),
            pltpu.VMEM((2, rows // 2, width), LOW),
            pltpu.VMEM((width, hidden), jnp.float32),
            pltpu.VMEM((width, hidden), jnp.float32),
            pltpu.VMEM((hidden, width), jnp.float32),
            pltpu.VMEM((2, emit_rows, hidden), LOW),
            pltpu.SemaphoreType.DMA((23,)),
            pltpu.SemaphoreType.DMA((23,)),
            pltpu.SemaphoreType.DMA((2, 2)),
            pltpu.SemaphoreType.DMA((2,)),
            pltpu.SemaphoreType.DMA((2,)),
        ],
        compiler_params=pltpu.CompilerParams(
            collective_id=20, has_side_effects=True, vmem_limit_bytes=63 * MIB
        ),
        cost_estimate=pl.CostEstimate(
            flops=6 * 3 * 8 * rows * width * hidden,
            bytes_accessed=64 * rows * width,
            transcendentals=0,
        ),
        name="ffn",
    )(h_two, cot_all, gate_full, up_full, down_full)
    return out_part, g_h_two, d_gate, d_up, d_down


def ffn_lax(h_two, cot_all, gate_full, up_full, down_full):
    pieces, rows, width = cot_all.shape
    h_two_all = gather_plane(h_two, 5).reshape(-1, width)
    cot_all = cot_all.reshape(-1, width)
    gate = dot(h_two_all, gate_full)
    up = dot(h_two_all, up_full)
    g_act = contract(cot_all, down_full, 1, 1)
    sigmoid = jax.nn.sigmoid(gate)
    silu = gate * sigmoid
    act = (silu * up).astype(LOW)
    g_gate = (g_act * up * sigmoid * (1.0 + gate * (1.0 - sigmoid))).astype(LOW)
    g_up = (g_act * silu).astype(LOW)
    part = (contract(g_gate, gate_full, 1, 1) + contract(g_up, up_full, 1, 1)).astype(LOW)
    return (
        dot(act, down_full).astype(LOW).reshape(pieces, rows, width),
        scatter_plane(part.reshape(pieces, rows, width), 7),
        contract(h_two_all, g_gate, 0, 0).astype(LOW),
        contract(h_two_all, g_up, 0, 0).astype(LOW),
        contract(act, cot_all, 0, 0).astype(LOW),
    )


def norm_scale(rows):
    return lax.rsqrt(jnp.mean(rows * rows, axis=-1, keepdims=True) + epsilon)


def norm_backward(grad, normed, inverse, gain):
    scaled = grad * gain
    return inverse * (scaled - normed * jnp.mean(scaled * normed, axis=-1, keepdims=True))


def local(
    tokens,
    doc_lengths,
    w_query,
    w_key,
    w_value,
    w_out,
    w_gate,
    w_up,
    w_down,
    gain_attn,
    gain_mlp,
    cotangent,
):
    micro, span = tokens.shape[1:3]
    pieces, groups = lax.axis_size("seq"), lax.axis_size("dp")
    place = lax.axis_index("seq")
    length = pieces * span
    heads = max(1, HEADS // pieces)
    sharers = max(1, pieces // HEADS)
    streams = micro // sharers
    first_head = place // sharers * heads
    first_stream = place % sharers * streams
    qk, wide = heads * QK_DIM, heads * HEAD_V
    hidden = FF // pieces

    out_width = D // pieces
    attn_slice = jnp.concatenate(
        [
            lax.dynamic_slice_in_dim(w_value, first_head * HEAD_V, wide, 1),
            lax.dynamic_slice_in_dim(w_out, place * out_width, out_width, 1),
            lax.dynamic_slice_in_dim(w_query, first_head * QK_DIM, qk, 1),
            lax.dynamic_slice_in_dim(w_key, first_head * QK_DIM, qk, 1),
            gain_attn[:, None],
            gain_mlp[:, None],
        ],
        axis=1,
    )
    rows_dp = w_gate.shape[0]
    share = hidden // groups
    block = FF // groups

    def hidden_columns(w):
        return [
            lax.dynamic_slice_in_dim(w, z * block + place * share, share, 1) for z in range(groups)
        ]

    ffn_slice = jnp.concatenate(hidden_columns(w_gate) + hidden_columns(w_up), axis=1)
    down_slice = lax.dynamic_slice_in_dim(w_down, place * share, share, 0)

    def gather_dp(w):
        return lax.all_gather(w, "dp", axis=0, tiled=True)

    attn_got = gather_dp(attn_slice)
    ffn_full = gather_dp(ffn_slice)
    down_full = gather_dp(down_slice)
    value_full = attn_got[:, :wide]
    query_full = attn_got[:, wide + out_width : wide + out_width + qk]
    key_full = attn_got[:, wide + out_width + qk : wide + out_width + 2 * qk]
    gains = attn_got[:, wide + out_width + 2 * qk :].astype(jnp.float32)
    gain_one, gain_two = gains[:, 0], gains[:, 1]
    gate_full, up_full = ffn_full[:, :hidden], ffn_full[:, hidden:]

    lengths = lax.dynamic_slice_in_dim(doc_lengths[0], first_stream, streams, 0)
    starts = jnp.cumsum(lengths, axis=1) - lengths
    position = jnp.arange(length, dtype=jnp.int32)
    begun = starts[:, None, :] <= position[None, :, None]
    first = jnp.max(jnp.where(begun, starts[:, None, :], 0), axis=2)[..., None]

    mine = micro * span
    cot = cotangent[0].reshape(mine, D)
    x_all = gather_plane(tokens[0].reshape(mine, D), 1)
    out_full = gather_plane(attn_got[:, wide : wide + out_width], 2)
    x_all = x_all.reshape(pieces, micro, span, D).transpose(1, 0, 2, 3)
    x_all = lax.dynamic_slice_in_dim(x_all, first_stream, streams, 0)
    x_all = x_all.astype(jnp.float32)
    h_flat = (x_all * norm_scale(x_all) * gain_one).astype(LOW).reshape(streams * length, D)
    value = dot(h_flat, value_full).astype(LOW).reshape(streams, length, wide)
    query = dot(h_flat, query_full).astype(LOW).reshape(streams, length, qk)
    key = dot(h_flat, key_full).astype(LOW).reshape(streams, length, qk)
    att_heads = attend(query, key, value, first, heads)

    def to_tokens(by_head):
        sent = by_head.reshape(streams, pieces, span, wide).transpose(1, 0, 2, 3)
        got = exchange_plane(sent, 3).reshape(pieces // sharers, micro, span, wide)
        return got.transpose(1, 2, 0, 3).reshape(mine, HEADS * HEAD_V)

    def to_heads(by_token):
        sent = by_token.reshape(micro, span, pieces // sharers, wide).transpose(2, 0, 1, 3)
        got = exchange_plane(sent.reshape(pieces, streams, span, wide), 4)
        return got.transpose(1, 0, 2, 3).reshape(streams, length, wide)

    attended = to_tokens(att_heads)
    flat = tokens[0].reshape(mine, D).astype(jnp.float32)
    mid = flat + jnp.einsum(
        "tk,skn->tsn", attended, out_full, preferred_element_type=jnp.float32
    ).reshape(mine, D)
    inverse_two = norm_scale(mid)
    plain_two = mid * inverse_two
    h_two = (plain_two * gain_two).astype(LOW)

    cot_all = gather_plane(cot, 6)
    feed_forward = ffn_plane if pieces == 8 else ffn_lax
    out_part, g_h_two, d_gate, d_up, d_down = feed_forward(
        h_two, cot_all, gate_full, up_full, down_full
    )

    def scatter_dp(part):
        return lax.psum_scatter(part, "dp", scatter_dimension=0, tiled=True)

    grad_ffn = scatter_dp(jnp.concatenate([d_gate, d_up], axis=1))
    grad_down = scatter_dp(d_down).astype(jnp.float32)
    output = (mid + scatter_plane(out_part, 8)).astype(LOW)

    g_mid = cot.astype(jnp.float32) + norm_backward(g_h_two, plain_two, inverse_two, gain_two)
    g_mid_low = g_mid.astype(LOW)
    g_att = jnp.einsum(
        "tsn,skn->tk",
        g_mid_low.reshape(mine, pieces, out_width),
        out_full,
        preferred_element_type=jnp.float32,
    )
    g_att = to_heads(g_att.astype(LOW))
    g_query, g_key, g_value = attend_back(query, key, value, first, att_heads, g_att, heads)
    g_value = g_value.reshape(streams * length, wide)
    g_query = g_query.reshape(streams * length, qk)
    g_key = g_key.reshape(streams * length, qk)
    g_h_one_part = (
        contract(g_value, value_full, 1, 1)
        + contract(g_query, query_full, 1, 1)
        + contract(g_key, key_full, 1, 1)
    ).astype(LOW)
    g_h_one_part = g_h_one_part.reshape(streams, pieces, span, D).transpose(1, 0, 2, 3)
    if sharers > 1:
        padded = jnp.zeros((pieces, micro, span, D), LOW)
        g_h_one_part = lax.dynamic_update_slice_in_dim(padded, g_h_one_part, first_stream, 1)
    g_h_one = scatter_plane(g_h_one_part.reshape(pieces, mine, D), 9)
    inverse_one = norm_scale(flat)
    plain_one = flat * inverse_one
    input_grad = g_mid + norm_backward(g_h_one, plain_one, inverse_one, gain_one)

    own = rows_dp // pieces
    grad_out = contract(attended, g_mid_low, 0, 0).astype(LOW)
    grad_out = grad_out.reshape(groups, pieces, own, D).transpose(1, 0, 2, 3)
    grad_out = scatter_plane(grad_out.reshape(pieces, groups * own, D), 10).astype(LOW)
    grad_out = scatter_dp(grad_out)
    grad_attn = jnp.concatenate(
        [
            contract(h_flat, g_value, 0, 0).astype(LOW),
            contract(h_flat, g_query, 0, 0).astype(LOW),
            contract(h_flat, g_key, 0, 0).astype(LOW),
            jnp.sum(g_h_one * plain_one, axis=0).astype(LOW)[:, None],
            jnp.sum(g_h_two * plain_two, axis=0).astype(LOW)[:, None],
        ],
        axis=1,
    )
    grad_attn = scatter_dp(grad_attn)
    ffn_got = exchange_plane(grad_ffn.reshape(pieces, own, 2 * hidden), 11).astype(jnp.float32)
    attn_got = exchange_plane(grad_attn.reshape(pieces, own, -1), 12).astype(jnp.float32)
    grad_gains = jnp.sum(attn_got[:, :, wide + 2 * qk :], axis=0)
    attn_got = jnp.sum(attn_got.reshape(pieces // sharers, sharers, own, -1), axis=1)

    def by_rows(block):
        return block.transpose(1, 0, 2).reshape(own, -1)

    def by_hidden(block):
        return block.reshape(pieces, own, groups, share).transpose(1, 2, 0, 3).reshape(own, FF)

    return (
        output.reshape(tokens.shape),
        input_grad.reshape(tokens.shape),
        by_rows(attn_got[:, :, wide : wide + qk]),
        by_rows(attn_got[:, :, wide + qk : wide + 2 * qk]),
        by_rows(attn_got[:, :, :wide]),
        grad_out.astype(jnp.float32),
        by_hidden(ffn_got[:, :, :hidden]),
        by_hidden(ffn_got[:, :, hidden:]),
        grad_down,
        grad_gains[:, 0],
        grad_gains[:, 1],
    )


def solution(mesh):
    by_token, by_row = P("dp", None, "seq", None), P("dp", None)
    grad_rows, grad_entries = P(("dp", "seq"), None), P(("dp", "seq"))
    return jax.shard_map(
        local,
        mesh=mesh,
        in_specs=(by_token, P("dp", None, None)) + (by_row,) * 7 + (P("dp"), P("dp"), by_token),
        out_specs=(by_token, by_token) + (grad_rows,) * 7 + (grad_entries,) * 2,
        check_vma=False,
    )
```

```python
import functools
import math

import jax
import jax.numpy as jnp
from jax import lax
from jax.experimental import pallas as pl
from jax.experimental.pallas import tpu as pltpu
from jax.sharding import PartitionSpec as P

D = 2048
HEADS = 16
QK_DIM = 16
FF = 5632
HEAD_V = 128
epsilon = 1e-06
MIB = 1024 * 1024


def dot(left, right):
    return jnp.dot(left, right, preferred_element_type=jnp.float32)


def contract(left, right, left_dim, right_dim):
    return lax.dot_general(
        left, right, (((left_dim,), (right_dim,)), ((), ())), preferred_element_type=jnp.float32
    )


def head_lanes(rows, head):
    lane = lax.broadcasted_iota(jnp.int32, rows.shape, 1)
    inside = (lane >= head * QK_DIM) & (lane < (head + 1) * QK_DIM)
    return jnp.where(inside, rows, jnp.zeros_like(rows))


def weights_of(query, key, head, first, base):
    scores = contract(head_lanes(query, head), key, 1, 1)
    row = base + lax.broadcasted_iota(jnp.int32, scores.shape, 0)
    column = lax.broadcasted_iota(jnp.int32, scores.shape, 1)
    mask = (column <= row) & (column >= first)
    poly = 1.0 + scores * (1.0 / math.sqrt(QK_DIM)) + scores * scores * (0.5 / QK_DIM)
    return scores, mask, jnp.where(mask, poly, 0.0)


def attend_kernel(heads, q_ref, k_ref, v_ref, first_ref, out_ref):
    rows = q_ref.shape[1]
    base = pl.program_id(1) * rows
    for head in range(heads):
        columns = slice(head * HEAD_V, (head + 1) * HEAD_V)
        unused, unused_mask, weight = weights_of(
            q_ref[0], k_ref[0], head, first_ref[0], base
        )
        denom = jnp.sum(weight, axis=1, keepdims=True)
        numer = dot(weight.astype(jnp.bfloat16), v_ref[0, :, columns])
        out_ref[0, :, columns] = (numer / denom).astype(jnp.bfloat16)


def attend(query, key, value, first, heads):
    streams, length, width = query.shape
    rows = min(256, length)
    return pl.pallas_call(
        functools.partial(attend_kernel, heads),
        grid=(streams, length // rows),
        in_specs=[
            pl.BlockSpec((1, rows, width), lambda m, i: (m, i, 0)),
            pl.BlockSpec((1, length, width), lambda m, i: (m, 0, 0)),
            pl.BlockSpec((1, length, heads * HEAD_V), lambda m, i: (m, 0, 0)),
            pl.BlockSpec((1, rows, 1), lambda m, i: (m, i, 0)),
        ],
        out_specs=pl.BlockSpec((1, rows, heads * HEAD_V), lambda m, i: (m, i, 0)),
        out_shape=jax.ShapeDtypeStruct(value.shape, jnp.bfloat16),
        compiler_params=pltpu.CompilerParams(vmem_limit_bytes=48 * MIB),
        name="attend",
    )(query, key, value, first)


def attend_back_kernel(
    heads, q_ref, k_ref, v_ref, first_ref, att_ref, g_ref, gq_ref, gk_ref, gv_ref, gk_sum, gv_sum
):
    rows = q_ref.shape[1]
    step = pl.program_id(1)
    base = step * rows

    @pl.when(step == 0)
    def _():
        gk_sum[...] = jnp.zeros_like(gk_sum)
        gv_sum[...] = jnp.zeros_like(gv_sum)

    query, key = q_ref[0], k_ref[0]
    g_query = jnp.zeros(query.shape, jnp.float32)
    for head in range(heads):
        columns = slice(head * HEAD_V, (head + 1) * HEAD_V)
        scores, mask, weight = weights_of(query, key, head, first_ref[0], base)
        denom = jnp.sum(weight, axis=1, keepdims=True)
        a = (g_ref[0, :, columns].astype(jnp.float32) / denom).astype(jnp.bfloat16)
        b = -jnp.sum(
            a.astype(jnp.float32) * att_ref[0, :, columns].astype(jnp.float32),
            axis=1,
            keepdims=True,
        )
        g_weight = contract(a, v_ref[0, :, columns], 1, 1) + b
        slope = 1.0 / math.sqrt(QK_DIM) + scores * (1.0 / QK_DIM)
        g_scores = jnp.where(mask, g_weight * slope, 0.0).astype(jnp.bfloat16)
        g_query += head_lanes(dot(g_scores, key), head)
        gk_sum[...] += contract(g_scores, head_lanes(query, head), 0, 0)
        gv_sum[:, columns] += contract(weight.astype(jnp.bfloat16), a, 0, 0)
    gq_ref[0] = g_query.astype(jnp.bfloat16)

    @pl.when(step == pl.num_programs(1) - 1)
    def _():
        gk_ref[0] = gk_sum[...].astype(jnp.bfloat16)
        gv_ref[0] = gv_sum[...].astype(jnp.bfloat16)


def attend_back(query, key, value, first, attended, grad, heads):
    streams, length, width = query.shape
    rows = min(256, length)
    some = pl.BlockSpec((1, rows, width), lambda m, i: (m, i, 0))
    all_narrow = pl.BlockSpec((1, length, width), lambda m, i: (m, 0, 0))
    all_wide = pl.BlockSpec((1, length, heads * HEAD_V), lambda m, i: (m, 0, 0))
    some_wide = pl.BlockSpec((1, rows, heads * HEAD_V), lambda m, i: (m, i, 0))
    return pl.pallas_call(
        functools.partial(attend_back_kernel, heads),
        grid=(streams, length // rows),
        in_specs=[
            some,
            all_narrow,
            all_wide,
            pl.BlockSpec((1, rows, 1), lambda m, i: (m, i, 0)),
            some_wide,
            some_wide,
        ],
        out_specs=[some, all_narrow, all_wide],
        out_shape=[
            jax.ShapeDtypeStruct(query.shape, jnp.bfloat16),
            jax.ShapeDtypeStruct(key.shape, jnp.bfloat16),
            jax.ShapeDtypeStruct(value.shape, jnp.bfloat16),
        ],
        scratch_shapes=[
            pltpu.VMEM((length, width), jnp.float32),
            pltpu.VMEM((length, heads * HEAD_V), jnp.float32),
        ],
        compiler_params=pltpu.CompilerParams(vmem_limit_bytes=56 * MIB),
        name="attend_back",
    )(query, key, value, first, attended, grad)

MESH = pl.DeviceIdType.MESH
LOW = jnp.bfloat16


def partners():
    me = lax.axis_index("seq")
    core, x, y = me % 2, me // 2 % 2, me // 4
    return me, me + 1 - 2 * core, me + 2 - 4 * x, me + 4 - 8 * y


def greet(others):
    barrier = pltpu.get_barrier_semaphore()
    for other in others:
        pl.semaphore_signal(barrier, inc=1, device_id={"seq": other}, device_id_type=MESH)
    pl.semaphore_wait(barrier, len(others))


def remote(send, recv, k, src, dst, to):
    return pltpu.make_async_remote_copy(
        src_ref=src,
        dst_ref=dst,
        send_sem=send.at[k],
        recv_sem=recv.at[k],
        device_id={"seq": to},
        device_id_type=MESH,
    )


def gather_kernel(x_ref, o_ref, send, recv, own_sem):
    me, sib, xn, yn = partners()
    diag = xn + yn - me
    half = x_ref.shape[0] // 2
    copy = functools.partial(remote, send, recv)
    upper, lower = pl.ds(0, half), pl.ds(half, half)
    greet((sib, xn, yn))
    own = pltpu.make_async_copy(x_ref, o_ref.at[me], own_sem)
    own.start()
    xa = copy(0, x_ref.at[upper], o_ref.at[me, upper], xn)
    yb = copy(1, x_ref.at[lower], o_ref.at[me, lower], yn)
    xb = copy(2, x_ref.at[lower], o_ref.at[me, lower], xn)
    ya = copy(3, x_ref.at[upper], o_ref.at[me, upper], yn)
    beside = [copy(4, x_ref, o_ref.at[me], sib)]
    started = [xa, yb, xb, ya, beside[0]]
    for c in started:
        c.start()

    def pass_on(k, origin, part, to):
        block = o_ref.at[origin, part]
        c = copy(k, block, block, to)
        c.start()
        started.append(c)
        return c

    xa.wait_recv()
    fy = pass_on(5, xn, upper, yn)
    beside.append(pass_on(6, xn, upper, sib))
    yb.wait_recv()
    fx = pass_on(7, yn, lower, xn)
    beside.append(pass_on(8, yn, lower, sib))
    xb.wait_recv()
    beside.append(pass_on(9, xn, lower, sib))
    ya.wait_recv()
    beside.append(pass_on(10, yn, upper, sib))
    fy.wait_recv()
    beside.append(pass_on(11, diag, upper, sib))
    fx.wait_recv()
    beside.append(pass_on(12, diag, lower, sib))
    own.wait()
    for c in beside:
        c.wait_recv()
    for c in started:
        c.wait_send()


def moved(nbytes):
    return pl.CostEstimate(flops=0, bytes_accessed=nbytes * 10, transcendentals=0)


def gather_plane(x, number):
    pieces = lax.axis_size("seq")
    if pieces != 8:
        return lax.all_gather(x, "seq", axis=0)
    return pl.pallas_call(
        gather_kernel,
        out_shape=jax.ShapeDtypeStruct((8,) + x.shape, x.dtype),
        in_specs=[pl.BlockSpec(memory_space=pl.ANY)],
        out_specs=pl.BlockSpec(memory_space=pl.ANY),
        scratch_shapes=[
            pltpu.SemaphoreType.DMA((13,)),
            pltpu.SemaphoreType.DMA((13,)),
            pltpu.SemaphoreType.DMA,
        ],
        compiler_params=pltpu.CompilerParams(collective_id=number, has_side_effects=True),
        cost_estimate=moved(16 * x.size),
        name="gather",
    )(x)


def scatter_kernel(p_ref, o_ref, held, got, one, two, send, recv, own_sem):
    me, sib, xn, yn = partners()
    diag = xn + yn - me
    half = p_ref.shape[1] // 2
    copy = functools.partial(remote, send, recv)
    upper, lower = pl.ds(0, half), pl.ds(half, half)
    greet((sib, xn, yn))
    beside, loads = [], []
    for i, owner in enumerate((diag, xn, yn, me)):
        beside.append(copy(i, p_ref.at[owner + sib - me], got.at[i], sib))
        loads.append(pltpu.make_async_copy(p_ref.at[owner], held.at[i], own_sem.at[i]))
        beside[i].start()
        loads[i].start()

    def pair_sum(i):
        beside[i].wait_recv()
        loads[i].wait()
        held[i] = held[i] + got[i]

    pair_sum(0)
    x0 = copy(4, held.at[0, upper], one.at[0], xn)
    x0.start()
    y0 = copy(5, held.at[0, lower], one.at[1], yn)
    y0.start()
    pair_sum(1)
    x1 = copy(6, held.at[1, upper], one.at[2], xn)
    x1.start()
    pair_sum(2)
    y1 = copy(7, held.at[2, lower], one.at[3], yn)
    y1.start()
    pair_sum(3)
    x0.wait_recv()
    held[2, :half] = held[2, :half] + one[0]
    y2 = copy(8, held.at[2, upper], two.at[0], yn)
    y2.start()
    y0.wait_recv()
    held[1, half:] = held[1, half:] + one[1]
    x2 = copy(9, held.at[1, lower], two.at[1], xn)
    x2.start()
    x1.wait_recv()
    y1.wait_recv()
    y2.wait_recv()
    wide = jnp.float32
    o_ref[:half] = held[3, :half].astype(wide) + one[2].astype(wide) + two[0].astype(wide)
    x2.wait_recv()
    o_ref[half:] = held[3, half:].astype(wide) + one[3].astype(wide) + two[1].astype(wide)
    for c in (*beside, x0, y0, x1, y1, y2, x2):
        c.wait_send()


def scatter_plane(part, number):
    pieces, rows, columns = part.shape
    if pieces != 8:
        return lax.psum_scatter(part, "seq", scatter_dimension=0).astype(jnp.float32)
    return pl.pallas_call(
        scatter_kernel,
        out_shape=jax.ShapeDtypeStruct((rows, columns), jnp.float32),
        in_specs=[pl.BlockSpec(memory_space=pl.ANY)],
        out_specs=pl.BlockSpec(memory_space=pltpu.VMEM),
        scratch_shapes=[
            pltpu.VMEM((4, rows, columns), LOW),
            pltpu.VMEM((4, rows, columns), LOW),
            pltpu.VMEM((4, rows // 2, columns), LOW),
            pltpu.VMEM((2, rows // 2, columns), LOW),
            pltpu.SemaphoreType.DMA((10,)),
            pltpu.SemaphoreType.DMA((10,)),
            pltpu.SemaphoreType.DMA((4,)),
        ],
        compiler_params=pltpu.CompilerParams(
            collective_id=number, has_side_effects=True, vmem_limit_bytes=40 * MIB
        ),
        cost_estimate=moved(2 * part.size),
        name="scatter",
    )(part)


def exchange_kernel(x_ref, o_ref, send, recv, own_sem):
    me = lax.axis_index("seq")
    others = [lax.rem(me + i, 8) for i in range(1, 8)]
    greet(others)
    own = pltpu.make_async_copy(x_ref.at[me], o_ref.at[me], own_sem)
    own.start()
    copies = [
        remote(send, recv, i, x_ref.at[other], o_ref.at[me], other)
        for i, other in enumerate(others)
    ]
    for c in copies:
        c.start()
    own.wait()
    for c in copies:
        c.wait()


def exchange_plane(x, number):
    if lax.axis_size("seq") != 8:
        return lax.all_to_all(x, "seq", 0, 0)
    return pl.pallas_call(
        exchange_kernel,
        out_shape=jax.ShapeDtypeStruct(x.shape, x.dtype),
        in_specs=[pl.BlockSpec(memory_space=pl.ANY)],
        out_specs=pl.BlockSpec(memory_space=pl.ANY),
        scratch_shapes=[
            pltpu.SemaphoreType.DMA((7,)),
            pltpu.SemaphoreType.DMA((7,)),
            pltpu.SemaphoreType.DMA,
        ],
        compiler_params=pltpu.CompilerParams(collective_id=number, has_side_effects=True),
        cost_estimate=moved(4 * x.size),
        name="exchange",
    )(x)


def ffn_kernel(
    h_ref,
    c_ref,
    wg_ref,
    wu_ref,
    wd_ref,
    h_all,
    out_part,
    gh_ref,
    dg_ref,
    du_ref,
    dd_ref,
    h_buf,
    c_buf,
    o_buf,
    beside,
    held,
    got,
    one,
    two,
    sum_g,
    sum_u,
    sum_d,
    emit,
    send,
    recv,
    load_sem,
    out_sem,
    emit_sem,
):
    me, sib, xn, yn = partners()
    diag = xn + yn - me
    flip = sib - me
    rows = h_ref.shape[0]
    half = rows // 2
    upper, lower = pl.ds(0, half), pl.ds(half, half)
    copy = functools.partial(remote, send, recv)

    xa = copy(0, h_ref.at[upper], h_all.at[me, upper], xn)
    yb = copy(1, h_ref.at[lower], h_all.at[me, lower], yn)
    xb = copy(2, h_ref.at[lower], h_all.at[me, lower], xn)
    ya = copy(3, h_ref.at[upper], h_all.at[me, upper], yn)
    s0 = copy(4, h_ref, h_all.at[me], sib)

    def pass_on(k, origin, part, to):
        return copy(k, h_all.at[origin, part], h_all.at[origin, part], to)

    fy = pass_on(5, xn, upper, yn)
    fx = pass_on(6, yn, lower, xn)
    s1 = pass_on(7, xn, upper, sib)
    s2 = pass_on(8, yn, lower, sib)
    s3 = pass_on(9, xn, lower, sib)
    s4 = pass_on(10, yn, upper, sib)
    s5 = pass_on(11, diag, upper, sib)
    s6 = pass_on(12, diag, lower, sib)
    b0 = copy(13, beside.at[0], got.at[0], sib)
    b1 = copy(14, beside.at[1], got.at[1], sib)
    b2 = copy(15, beside.at[0], got.at[2], sib)
    b3 = copy(16, beside.at[1], got.at[3], sib)
    x0 = copy(17, held.at[2, upper], one.at[0], xn)
    y0 = copy(18, held.at[2, lower], one.at[1], yn)
    x1 = copy(19, held.at[1, upper], one.at[2], xn)
    y1 = copy(20, held.at[3, lower], one.at[3], yn)
    y2 = copy(21, held.at[3, upper], two.at[0], yn)
    x2 = copy(22, held.at[1, lower], two.at[1], xn)

    def owner_of(step):
        chip = jnp.where(step < 4, xn, jnp.where(step < 6, diag, yn))
        later = chip + jnp.where(lax.rem(step, 2) == 0, flip, 0)
        return jnp.where(step == 0, me, jnp.where(step == 1, sib, later))

    def loads(step):
        slot = lax.rem(step, 2)
        owner = owner_of(step)
        return (
            pltpu.make_async_copy(h_all.at[owner], h_buf.at[slot], load_sem.at[0, slot]),
            pltpu.make_async_copy(c_ref.at[owner], c_buf.at[slot], load_sem.at[1, slot]),
        )

    def out_copy(step):
        slot = lax.rem(step, 2)
        return pltpu.make_async_copy(o_buf.at[slot], out_part.at[owner_of(step)], out_sem.at[slot])

    greet((sib, xn, yn))
    for c in (xa, yb, xb, ya, s0):
        c.start()
    first = (
        pltpu.make_async_copy(h_ref, h_buf.at[0], load_sem.at[0, 0]),
        pltpu.make_async_copy(c_ref.at[me], c_buf.at[0], load_sem.at[1, 0]),
    )
    for c in first:
        c.start()
    for total in (sum_g, sum_u, sum_d):
        total[...] = jnp.zeros_like(total)

    def arrive(step):
        @pl.when(step == 1)
        def _():
            s0.wait_recv()

        @pl.when(step == 2)
        def _():
            xa.wait_recv()
            yb.wait_recv()
            for c in (fy, fx, s1, s2):
                c.start()
            xb.wait_recv()
            ya.wait_recv()
            s3.start()
            s4.start()
            s1.wait_recv()
            s3.wait_recv()

        @pl.when(step == 4)
        def _():
            fy.wait_recv()
            fx.wait_recv()
            s5.start()
            s6.start()
            s5.wait_recv()
            s6.wait_recv()

        @pl.when(step == 6)
        def _():
            s2.wait_recv()
            s4.wait_recv()

        @pl.when(step == 7)
        def _():
            y0.wait_recv()
            held[1, half:] = held[1, half:] + one[1]
            x2.start()

    def body(step, carry):
        slot = lax.rem(step, 2)
        for c in loads(step):
            c.wait()
        h, c = h_buf[slot], c_buf[slot]
        gate = dot(h, wg_ref[...])
        up = dot(h, wu_ref[...])
        g_act = contract(c, wd_ref[...], 1, 1)
        sigmoid = jax.nn.sigmoid(gate)
        silu = gate * sigmoid
        act = (silu * up).astype(LOW)
        g_gate = (g_act * up * sigmoid * (1.0 + gate * (1.0 - sigmoid))).astype(LOW)
        g_up = (g_act * silu).astype(LOW)
        part = (contract(g_gate, wg_ref[...], 1, 1) + contract(g_up, wu_ref[...], 1, 1)).astype(LOW)

        for k, place, sent in ((1, 0, b0), (2, 1, b1), (4, 0, b2), (6, 1, b3)):

            @pl.when(step == k)
            def _(k=k, place=place, sent=sent):
                if k == 4:
                    b0.wait_send()
                if k == 6:
                    b1.wait_send()
                beside[place] = part
                sent.start()

        for k, place, arrived in ((0, 0, None), (3, 1, b1), (5, 2, b2), (7, 3, b3)):

            @pl.when(step == k)
            def _(k=k, place=place, arrived=arrived):
                if arrived is None:
                    held[place] = part
                else:
                    arrived.wait_recv()
                    held[place] = part + got[place]
                if k == 3:
                    x1.start()
                if k == 5:
                    x0.start()
                    y0.start()
                if k == 7:
                    y1.start()
                    x0.wait_recv()
                    held[3, :half] = held[3, :half] + one[0]
                    y2.start()

        @pl.when(step >= 2)
        def _():
            out_copy(step - 2).wait()

        o_buf[slot] = dot(act, wd_ref[...]).astype(LOW)
        out_copy(step).start()
        arrive(step + 1)

        @pl.when(step < 7)
        def _():
            for c in loads(step + 1):
                c.start()

        sum_g[...] += contract(h, g_gate, 0, 0)
        sum_u[...] += contract(h, g_up, 0, 0)
        sum_d[...] += contract(act, c, 0, 0)
        return carry

    lax.fori_loop(0, 8, body, 0)
    out_copy(6).wait()
    out_copy(7).wait()

    pending = [None, None]
    count = 0
    for total, target in ((sum_g, dg_ref), (sum_u, du_ref)):
        block = emit.shape[1]
        for start in range(0, total.shape[0], block):
            slot = count % 2
            if pending[slot] is not None:
                pending[slot].wait()
            emit[slot] = total[start : start + block].astype(LOW)
            pending[slot] = pltpu.make_async_copy(
                emit.at[slot], target.at[pl.ds(start, block)], emit_sem.at[slot]
            )
            pending[slot].start()
            count += 1
    hidden = sum_d.shape[0]
    downs = []
    for slot, start in enumerate(range(0, hidden, rows)):
        size = min(rows, hidden - start)
        if slot >= 2:
            downs[slot - 2].wait()
        o_buf[slot % 2, :size] = sum_d[start : start + size].astype(LOW)
        downs.append(
            pltpu.make_async_copy(
                o_buf.at[slot % 2, pl.ds(0, size)],
                dd_ref.at[pl.ds(start, size)],
                out_sem.at[slot % 2],
            )
        )
        downs[-1].start()

    b0.wait_recv()
    wide = jnp.float32
    x1.wait_recv()
    y1.wait_recv()
    y2.wait_recv()
    own = held[0, :half].astype(wide) + got[0, :half].astype(wide)
    gh_ref[:half] = own + one[2].astype(wide) + two[0].astype(wide)
    x2.wait_recv()
    own = held[0, half:].astype(wide) + got[0, half:].astype(wide)
    gh_ref[half:] = own + one[3].astype(wide) + two[1].astype(wide)
    for c in downs[-2:]:
        c.wait()
    for c in pending:
        c.wait()
    for c in (xa, yb, xb, ya, s0, fy, fx, s1, s2, s3, s4, s5, s6, b2, b3, x0, y0, x1, y1, y2, x2):
        c.wait_send()


def ffn_plane(h_two, cot_all, gate_full, up_full, down_full):
    rows, width = h_two.shape
    hidden = gate_full.shape[1]
    anywhere = pl.BlockSpec(memory_space=pl.ANY)
    in_vmem = pl.BlockSpec(memory_space=pltpu.VMEM)
    emit_rows = 256
    shape = jax.ShapeDtypeStruct
    unused, out_part, g_h_two, d_gate, d_up, d_down = pl.pallas_call(
        ffn_kernel,
        out_shape=[
            shape((8, rows, width), LOW),
            shape((8, rows, width), LOW),
            shape((rows, width), jnp.float32),
            shape((width, hidden), LOW),
            shape((width, hidden), LOW),
            shape((hidden, width), LOW),
        ],
        in_specs=[anywhere, anywhere, in_vmem, in_vmem, in_vmem],
        out_specs=[anywhere, anywhere, in_vmem, anywhere, anywhere, anywhere],
        scratch_shapes=[
            pltpu.VMEM((2, rows, width), LOW),
            pltpu.VMEM((2, rows, width), LOW),
            pltpu.VMEM((2, rows, width), LOW),
            pltpu.VMEM((2, rows, width), LOW),
            pltpu.VMEM((4, rows, width), LOW),
            pltpu.VMEM((4, rows, width), LOW),
            pltpu.VMEM((4, rows // 2, width), LOW),
            pltpu.VMEM((2, rows // 2, width), LOW),
            pltpu.VMEM((width, hidden), jnp.float32),
            pltpu.VMEM((width, hidden), jnp.float32),
            pltpu.VMEM((hidden, width), jnp.float32),
            pltpu.VMEM((2, emit_rows, hidden), LOW),
            pltpu.SemaphoreType.DMA((23,)),
            pltpu.SemaphoreType.DMA((23,)),
            pltpu.SemaphoreType.DMA((2, 2)),
            pltpu.SemaphoreType.DMA((2,)),
            pltpu.SemaphoreType.DMA((2,)),
        ],
        compiler_params=pltpu.CompilerParams(
            collective_id=20, has_side_effects=True, vmem_limit_bytes=63 * MIB
        ),
        cost_estimate=pl.CostEstimate(
            flops=6 * 3 * 8 * rows * width * hidden,
            bytes_accessed=64 * rows * width,
            transcendentals=0,
        ),
        name="ffn",
    )(h_two, cot_all, gate_full, up_full, down_full)
    return out_part, g_h_two, d_gate, d_up, d_down


def ffn_lax(h_two, cot_all, gate_full, up_full, down_full):
    pieces, rows, width = cot_all.shape
    h_two_all = gather_plane(h_two, 5).reshape(-1, width)
    cot_all = cot_all.reshape(-1, width)
    gate = dot(h_two_all, gate_full)
    up = dot(h_two_all, up_full)
    g_act = contract(cot_all, down_full, 1, 1)
    sigmoid = jax.nn.sigmoid(gate)
    silu = gate * sigmoid
    act = (silu * up).astype(LOW)
    g_gate = (g_act * up * sigmoid * (1.0 + gate * (1.0 - sigmoid))).astype(LOW)
    g_up = (g_act * silu).astype(LOW)
    part = (contract(g_gate, gate_full, 1, 1) + contract(g_up, up_full, 1, 1)).astype(LOW)
    return (
        dot(act, down_full).astype(LOW).reshape(pieces, rows, width),
        scatter_plane(part.reshape(pieces, rows, width), 7),
        contract(h_two_all, g_gate, 0, 0).astype(LOW),
        contract(h_two_all, g_up, 0, 0).astype(LOW),
        contract(act, cot_all, 0, 0).astype(LOW),
    )


def norm_scale(rows):
    return lax.rsqrt(jnp.mean(rows * rows, axis=-1, keepdims=True) + epsilon)


def norm_backward(grad, normed, inverse, gain):
    scaled = grad * gain
    return inverse * (scaled - normed * jnp.mean(scaled * normed, axis=-1, keepdims=True))


def local(
    tokens,
    doc_lengths,
    w_query,
    w_key,
    w_value,
    w_out,
    w_gate,
    w_up,
    w_down,
    gain_attn,
    gain_mlp,
    cotangent,
):
    micro, span = tokens.shape[1:3]
    pieces, groups = lax.axis_size("seq"), lax.axis_size("dp")
    place = lax.axis_index("seq")
    length = pieces * span
    heads = max(1, HEADS // pieces)
    sharers = max(1, pieces // HEADS)
    streams = micro // sharers
    first_head = place // sharers * heads
    first_stream = place % sharers * streams
    qk, wide = heads * QK_DIM, heads * HEAD_V
    hidden = FF // pieces

    out_width = D // pieces
    attn_slice = jnp.concatenate(
        [
            lax.dynamic_slice_in_dim(w_value, first_head * HEAD_V, wide, 1),
            lax.dynamic_slice_in_dim(w_out, place * out_width, out_width, 1),
            lax.dynamic_slice_in_dim(w_query, first_head * QK_DIM, qk, 1),
            lax.dynamic_slice_in_dim(w_key, first_head * QK_DIM, qk, 1),
            gain_attn[:, None],
            gain_mlp[:, None],
        ],
        axis=1,
    )
    rows_dp = w_gate.shape[0]
    share = hidden // groups
    block = FF // groups

    def hidden_columns(w):
        return [
            lax.dynamic_slice_in_dim(w, z * block + place * share, share, 1) for z in range(groups)
        ]

    ffn_slice = jnp.concatenate(hidden_columns(w_gate) + hidden_columns(w_up), axis=1)
    down_slice = lax.dynamic_slice_in_dim(w_down, place * share, share, 0)

    def gather_dp(w):
        return lax.all_gather(w, "dp", axis=0, tiled=True)

    attn_got = gather_dp(attn_slice)
    ffn_full = gather_dp(ffn_slice)
    down_full = gather_dp(down_slice)
    value_full = attn_got[:, :wide]
    query_full = attn_got[:, wide + out_width : wide + out_width + qk]
    key_full = attn_got[:, wide + out_width + qk : wide + out_width + 2 * qk]
    gains = attn_got[:, wide + out_width + 2 * qk :].astype(jnp.float32)
    gain_one, gain_two = gains[:, 0], gains[:, 1]
    gate_full, up_full = ffn_full[:, :hidden], ffn_full[:, hidden:]

    lengths = lax.dynamic_slice_in_dim(doc_lengths[0], first_stream, streams, 0)
    starts = jnp.cumsum(lengths, axis=1) - lengths
    position = jnp.arange(length, dtype=jnp.int32)
    begun = starts[:, None, :] <= position[None, :, None]
    first = jnp.max(jnp.where(begun, starts[:, None, :], 0), axis=2)[..., None]

    mine = micro * span
    cot = cotangent[0].reshape(mine, D)
    x_all = gather_plane(tokens[0].reshape(mine, D), 1)
    out_full = gather_plane(attn_got[:, wide : wide + out_width], 2)
    x_all = x_all.reshape(pieces, micro, span, D).transpose(1, 0, 2, 3)
    x_all = lax.dynamic_slice_in_dim(x_all, first_stream, streams, 0)
    x_all = x_all.astype(jnp.float32)
    h_flat = (x_all * norm_scale(x_all) * gain_one).astype(LOW).reshape(streams * length, D)
    value = dot(h_flat, value_full).astype(LOW).reshape(streams, length, wide)
    query = dot(h_flat, query_full).astype(LOW).reshape(streams, length, qk)
    key = dot(h_flat, key_full).astype(LOW).reshape(streams, length, qk)
    att_heads = attend(query, key, value, first, heads)

    def to_tokens(by_head):
        sent = by_head.reshape(streams, pieces, span, wide).transpose(1, 0, 2, 3)
        got = exchange_plane(sent, 3).reshape(pieces // sharers, micro, span, wide)
        return got.transpose(1, 2, 0, 3).reshape(mine, HEADS * HEAD_V)

    def to_heads(by_token):
        sent = by_token.reshape(micro, span, pieces // sharers, wide).transpose(2, 0, 1, 3)
        got = exchange_plane(sent.reshape(pieces, streams, span, wide), 4)
        return got.transpose(1, 0, 2, 3).reshape(streams, length, wide)

    attended = to_tokens(att_heads)
    flat = tokens[0].reshape(mine, D).astype(jnp.float32)
    mid = flat + jnp.einsum(
        "tk,skn->tsn", attended, out_full, preferred_element_type=jnp.float32
    ).reshape(mine, D)
    inverse_two = norm_scale(mid)
    plain_two = mid * inverse_two
    h_two = (plain_two * gain_two).astype(LOW)

    cot_all = gather_plane(cot, 6)
    feed_forward = ffn_plane if pieces == 8 else ffn_lax
    out_part, g_h_two, d_gate, d_up, d_down = feed_forward(
        h_two, cot_all, gate_full, up_full, down_full
    )

    def scatter_dp(part):
        return lax.psum_scatter(part, "dp", scatter_dimension=0, tiled=True)

    sum_gate, sum_up, sum_down = scatter_dp(d_gate), scatter_dp(d_up), scatter_dp(d_down)
    output = (mid + scatter_plane(out_part, 8)).astype(LOW)

    g_mid = cot.astype(jnp.float32) + norm_backward(g_h_two, plain_two, inverse_two, gain_two)
    g_mid_low = g_mid.astype(LOW)
    g_att = jnp.einsum(
        "tsn,skn->tk",
        g_mid_low.reshape(mine, pieces, out_width),
        out_full,
        preferred_element_type=jnp.float32,
    )
    g_att = to_heads(g_att.astype(LOW))
    g_query, g_key, g_value = attend_back(query, key, value, first, att_heads, g_att, heads)
    g_value = g_value.reshape(streams * length, wide)
    g_query = g_query.reshape(streams * length, qk)
    g_key = g_key.reshape(streams * length, qk)
    g_h_one_part = (
        contract(g_value, value_full, 1, 1)
        + contract(g_query, query_full, 1, 1)
        + contract(g_key, key_full, 1, 1)
    ).astype(LOW)
    g_h_one_part = g_h_one_part.reshape(streams, pieces, span, D).transpose(1, 0, 2, 3)
    if sharers > 1:
        padded = jnp.zeros((pieces, micro, span, D), LOW)
        g_h_one_part = lax.dynamic_update_slice_in_dim(padded, g_h_one_part, first_stream, 1)
    g_h_one = scatter_plane(g_h_one_part.reshape(pieces, mine, D), 9)
    inverse_one = norm_scale(flat)
    plain_one = flat * inverse_one
    input_grad = g_mid + norm_backward(g_h_one, plain_one, inverse_one, gain_one)

    own = rows_dp // pieces
    grad_out = contract(attended, g_mid_low, 0, 0).astype(LOW)
    grad_out = grad_out.reshape(groups, pieces, own, D).transpose(1, 0, 2, 3)
    grad_out = scatter_plane(grad_out.reshape(pieces, groups * own, D), 10).astype(LOW)
    grad_out, sum_gate, sum_up, sum_down = lax.optimization_barrier(
        (grad_out, sum_gate, sum_up, sum_down)
    )
    grad_out = scatter_dp(grad_out)
    grad_attn = jnp.concatenate(
        [
            contract(h_flat, g_value, 0, 0).astype(LOW),
            contract(h_flat, g_query, 0, 0).astype(LOW),
            contract(h_flat, g_key, 0, 0).astype(LOW),
            jnp.sum(g_h_one * plain_one, axis=0).astype(LOW)[:, None],
            jnp.sum(g_h_two * plain_two, axis=0).astype(LOW)[:, None],
        ],
        axis=1,
    )
    grad_attn, grad_out = lax.optimization_barrier((grad_attn, grad_out))
    grad_attn = scatter_dp(grad_attn)
    gate_got = exchange_plane(sum_gate.reshape(pieces, own, hidden), 11)
    up_got = exchange_plane(sum_up.reshape(pieces, own, hidden), 13)
    attn_got = exchange_plane(grad_attn.reshape(pieces, own, -1), 12).astype(jnp.float32)
    grad_gains = jnp.sum(attn_got[:, :, wide + 2 * qk :], axis=0)
    attn_got = jnp.sum(attn_got.reshape(pieces // sharers, sharers, own, -1), axis=1)

    def by_rows(block):
        return block.transpose(1, 0, 2).reshape(own, -1)

    def by_hidden(block):
        block = block.astype(jnp.float32).reshape(pieces, own, groups, share)
        return block.transpose(1, 2, 0, 3).reshape(own, FF)

    return (
        output.reshape(tokens.shape),
        input_grad.reshape(tokens.shape),
        by_rows(attn_got[:, :, wide : wide + qk]),
        by_rows(attn_got[:, :, wide + qk : wide + 2 * qk]),
        by_rows(attn_got[:, :, :wide]),
        grad_out.astype(jnp.float32),
        by_hidden(gate_got),
        by_hidden(up_got),
        sum_down.astype(jnp.float32),
        grad_gains[:, 0],
        grad_gains[:, 1],
    )


def solution(mesh):
    by_token, by_row = P("dp", None, "seq", None), P("dp", None)
    grad_rows, grad_entries = P(("dp", "seq"), None), P(("dp", "seq"))
    return jax.shard_map(
        local,
        mesh=mesh,
        in_specs=(by_token, P("dp", None, None)) + (by_row,) * 7 + (P("dp"), P("dp"), by_token),
        out_specs=(by_token, by_token) + (grad_rows,) * 7 + (grad_entries,) * 2,
        check_vma=False,
    )
```

```python
import functools
import math

import jax
import jax.numpy as jnp
from jax import lax
from jax.experimental import pallas as pl
from jax.experimental.pallas import tpu as pltpu
from jax.sharding import PartitionSpec as P

D = 2048
HEADS = 16
QK_DIM = 16
FF = 5632
HEAD_V = 128
epsilon = 1e-06
MIB = 1024 * 1024


def dot(left, right):
    return jnp.dot(left, right, preferred_element_type=jnp.float32)


def contract(left, right, left_dim, right_dim):
    return lax.dot_general(
        left, right, (((left_dim,), (right_dim,)), ((), ())), preferred_element_type=jnp.float32
    )


def head_lanes(rows, head):
    lane = lax.broadcasted_iota(jnp.int32, rows.shape, 1)
    inside = (lane >= head * QK_DIM) & (lane < (head + 1) * QK_DIM)
    return jnp.where(inside, rows, jnp.zeros_like(rows))


def weights_of(query, key, head, first, base):
    scores = contract(head_lanes(query, head), key, 1, 1)
    row = base + lax.broadcasted_iota(jnp.int32, scores.shape, 0)
    column = lax.broadcasted_iota(jnp.int32, scores.shape, 1)
    mask = (column <= row) & (column >= first)
    poly = 1.0 + scores * (1.0 / math.sqrt(QK_DIM)) + scores * scores * (0.5 / QK_DIM)
    return scores, mask, jnp.where(mask, poly, 0.0)


def attend_kernel(heads, q_ref, k_ref, v_ref, first_ref, out_ref):
    rows = q_ref.shape[1]
    base = pl.program_id(1) * rows
    for head in range(heads):
        columns = slice(head * HEAD_V, (head + 1) * HEAD_V)
        unused, unused_mask, weight = weights_of(
            q_ref[0], k_ref[0], head, first_ref[0], base
        )
        denom = jnp.sum(weight, axis=1, keepdims=True)
        numer = dot(weight.astype(jnp.bfloat16), v_ref[0, :, columns])
        out_ref[0, :, columns] = (numer / denom).astype(jnp.bfloat16)


def attend(query, key, value, first, heads):
    streams, length, width = query.shape
    rows = min(256, length)
    return pl.pallas_call(
        functools.partial(attend_kernel, heads),
        grid=(streams, length // rows),
        in_specs=[
            pl.BlockSpec((1, rows, width), lambda m, i: (m, i, 0)),
            pl.BlockSpec((1, length, width), lambda m, i: (m, 0, 0)),
            pl.BlockSpec((1, length, heads * HEAD_V), lambda m, i: (m, 0, 0)),
            pl.BlockSpec((1, rows, 1), lambda m, i: (m, i, 0)),
        ],
        out_specs=pl.BlockSpec((1, rows, heads * HEAD_V), lambda m, i: (m, i, 0)),
        out_shape=jax.ShapeDtypeStruct(value.shape, jnp.bfloat16),
        compiler_params=pltpu.CompilerParams(vmem_limit_bytes=48 * MIB),
        name="attend",
    )(query, key, value, first)


def attend_back_kernel(
    heads, q_ref, k_ref, v_ref, first_ref, att_ref, g_ref, gq_ref, gk_ref, gv_ref, gk_sum, gv_sum
):
    rows = q_ref.shape[1]
    step = pl.program_id(1)
    base = step * rows

    @pl.when(step == 0)
    def _():
        gk_sum[...] = jnp.zeros_like(gk_sum)
        gv_sum[...] = jnp.zeros_like(gv_sum)

    query, key = q_ref[0], k_ref[0]
    g_query = jnp.zeros(query.shape, jnp.float32)
    for head in range(heads):
        columns = slice(head * HEAD_V, (head + 1) * HEAD_V)
        scores, mask, weight = weights_of(query, key, head, first_ref[0], base)
        denom = jnp.sum(weight, axis=1, keepdims=True)
        a = (g_ref[0, :, columns].astype(jnp.float32) / denom).astype(jnp.bfloat16)
        b = -jnp.sum(
            a.astype(jnp.float32) * att_ref[0, :, columns].astype(jnp.float32),
            axis=1,
            keepdims=True,
        )
        g_weight = contract(a, v_ref[0, :, columns], 1, 1) + b
        slope = 1.0 / math.sqrt(QK_DIM) + scores * (1.0 / QK_DIM)
        g_scores = jnp.where(mask, g_weight * slope, 0.0).astype(jnp.bfloat16)
        g_query += head_lanes(dot(g_scores, key), head)
        gk_sum[...] += contract(g_scores, head_lanes(query, head), 0, 0)
        gv_sum[:, columns] += contract(weight.astype(jnp.bfloat16), a, 0, 0)
    gq_ref[0] = g_query.astype(jnp.bfloat16)

    @pl.when(step == pl.num_programs(1) - 1)
    def _():
        gk_ref[0] = gk_sum[...].astype(jnp.bfloat16)
        gv_ref[0] = gv_sum[...].astype(jnp.bfloat16)


def attend_back(query, key, value, first, attended, grad, heads):
    streams, length, width = query.shape
    rows = min(256, length)
    some = pl.BlockSpec((1, rows, width), lambda m, i: (m, i, 0))
    all_narrow = pl.BlockSpec((1, length, width), lambda m, i: (m, 0, 0))
    all_wide = pl.BlockSpec((1, length, heads * HEAD_V), lambda m, i: (m, 0, 0))
    some_wide = pl.BlockSpec((1, rows, heads * HEAD_V), lambda m, i: (m, i, 0))
    return pl.pallas_call(
        functools.partial(attend_back_kernel, heads),
        grid=(streams, length // rows),
        in_specs=[
            some,
            all_narrow,
            all_wide,
            pl.BlockSpec((1, rows, 1), lambda m, i: (m, i, 0)),
            some_wide,
            some_wide,
        ],
        out_specs=[some, all_narrow, all_wide],
        out_shape=[
            jax.ShapeDtypeStruct(query.shape, jnp.bfloat16),
            jax.ShapeDtypeStruct(key.shape, jnp.bfloat16),
            jax.ShapeDtypeStruct(value.shape, jnp.bfloat16),
        ],
        scratch_shapes=[
            pltpu.VMEM((length, width), jnp.float32),
            pltpu.VMEM((length, heads * HEAD_V), jnp.float32),
        ],
        compiler_params=pltpu.CompilerParams(vmem_limit_bytes=56 * MIB),
        name="attend_back",
    )(query, key, value, first, attended, grad)

MESH = pl.DeviceIdType.MESH
LOW = jnp.bfloat16


def partners():
    me = lax.axis_index("seq")
    core, x, y = me % 2, me // 2 % 2, me // 4
    return me, me + 1 - 2 * core, me + 2 - 4 * x, me + 4 - 8 * y


def greet(others):
    barrier = pltpu.get_barrier_semaphore()
    for other in others:
        pl.semaphore_signal(barrier, inc=1, device_id={"seq": other}, device_id_type=MESH)
    pl.semaphore_wait(barrier, len(others))


def remote(send, recv, k, src, dst, to):
    return pltpu.make_async_remote_copy(
        src_ref=src,
        dst_ref=dst,
        send_sem=send.at[k],
        recv_sem=recv.at[k],
        device_id={"seq": to},
        device_id_type=MESH,
    )


def gather_kernel(x_ref, o_ref, send, recv, own_sem):
    me, sib, xn, yn = partners()
    diag = xn + yn - me
    half = x_ref.shape[0] // 2
    copy = functools.partial(remote, send, recv)
    upper, lower = pl.ds(0, half), pl.ds(half, half)
    greet((sib, xn, yn))
    own = pltpu.make_async_copy(x_ref, o_ref.at[me], own_sem)
    own.start()
    xa = copy(0, x_ref.at[upper], o_ref.at[me, upper], xn)
    yb = copy(1, x_ref.at[lower], o_ref.at[me, lower], yn)
    xb = copy(2, x_ref.at[lower], o_ref.at[me, lower], xn)
    ya = copy(3, x_ref.at[upper], o_ref.at[me, upper], yn)
    beside = [copy(4, x_ref, o_ref.at[me], sib)]
    started = [xa, yb, xb, ya, beside[0]]
    for c in started:
        c.start()

    def pass_on(k, origin, part, to):
        block = o_ref.at[origin, part]
        c = copy(k, block, block, to)
        c.start()
        started.append(c)
        return c

    xa.wait_recv()
    fy = pass_on(5, xn, upper, yn)
    beside.append(pass_on(6, xn, upper, sib))
    yb.wait_recv()
    fx = pass_on(7, yn, lower, xn)
    beside.append(pass_on(8, yn, lower, sib))
    xb.wait_recv()
    beside.append(pass_on(9, xn, lower, sib))
    ya.wait_recv()
    beside.append(pass_on(10, yn, upper, sib))
    fy.wait_recv()
    beside.append(pass_on(11, diag, upper, sib))
    fx.wait_recv()
    beside.append(pass_on(12, diag, lower, sib))
    own.wait()
    for c in beside:
        c.wait_recv()
    for c in started:
        c.wait_send()


def moved(nbytes):
    return pl.CostEstimate(flops=0, bytes_accessed=nbytes * 10, transcendentals=0)


def gather_plane(x, number):
    pieces = lax.axis_size("seq")
    if pieces != 8:
        return lax.all_gather(x, "seq", axis=0)
    return pl.pallas_call(
        gather_kernel,
        out_shape=jax.ShapeDtypeStruct((8,) + x.shape, x.dtype),
        in_specs=[pl.BlockSpec(memory_space=pl.ANY)],
        out_specs=pl.BlockSpec(memory_space=pl.ANY),
        scratch_shapes=[
            pltpu.SemaphoreType.DMA((13,)),
            pltpu.SemaphoreType.DMA((13,)),
            pltpu.SemaphoreType.DMA,
        ],
        compiler_params=pltpu.CompilerParams(collective_id=number, has_side_effects=True),
        cost_estimate=moved(16 * x.size),
        name="gather",
    )(x)


def scatter_kernel(p_ref, o_ref, held, got, one, two, send, recv, own_sem):
    me, sib, xn, yn = partners()
    diag = xn + yn - me
    half = p_ref.shape[1] // 2
    copy = functools.partial(remote, send, recv)
    upper, lower = pl.ds(0, half), pl.ds(half, half)
    greet((sib, xn, yn))
    beside, loads = [], []
    for i, owner in enumerate((diag, xn, yn, me)):
        beside.append(copy(i, p_ref.at[owner + sib - me], got.at[i], sib))
        loads.append(pltpu.make_async_copy(p_ref.at[owner], held.at[i], own_sem.at[i]))
        beside[i].start()
        loads[i].start()

    def pair_sum(i):
        beside[i].wait_recv()
        loads[i].wait()
        held[i] = held[i] + got[i]

    pair_sum(0)
    x0 = copy(4, held.at[0, upper], one.at[0], xn)
    x0.start()
    y0 = copy(5, held.at[0, lower], one.at[1], yn)
    y0.start()
    pair_sum(1)
    x1 = copy(6, held.at[1, upper], one.at[2], xn)
    x1.start()
    pair_sum(2)
    y1 = copy(7, held.at[2, lower], one.at[3], yn)
    y1.start()
    pair_sum(3)
    x0.wait_recv()
    held[2, :half] = held[2, :half] + one[0]
    y2 = copy(8, held.at[2, upper], two.at[0], yn)
    y2.start()
    y0.wait_recv()
    held[1, half:] = held[1, half:] + one[1]
    x2 = copy(9, held.at[1, lower], two.at[1], xn)
    x2.start()
    x1.wait_recv()
    y1.wait_recv()
    y2.wait_recv()
    wide = jnp.float32
    o_ref[:half] = held[3, :half].astype(wide) + one[2].astype(wide) + two[0].astype(wide)
    x2.wait_recv()
    o_ref[half:] = held[3, half:].astype(wide) + one[3].astype(wide) + two[1].astype(wide)
    for c in (*beside, x0, y0, x1, y1, y2, x2):
        c.wait_send()


def scatter_plane(part, number):
    pieces, rows, columns = part.shape
    if pieces != 8:
        return lax.psum_scatter(part, "seq", scatter_dimension=0).astype(jnp.float32)
    return pl.pallas_call(
        scatter_kernel,
        out_shape=jax.ShapeDtypeStruct((rows, columns), jnp.float32),
        in_specs=[pl.BlockSpec(memory_space=pl.ANY)],
        out_specs=pl.BlockSpec(memory_space=pltpu.VMEM),
        scratch_shapes=[
            pltpu.VMEM((4, rows, columns), LOW),
            pltpu.VMEM((4, rows, columns), LOW),
            pltpu.VMEM((4, rows // 2, columns), LOW),
            pltpu.VMEM((2, rows // 2, columns), LOW),
            pltpu.SemaphoreType.DMA((10,)),
            pltpu.SemaphoreType.DMA((10,)),
            pltpu.SemaphoreType.DMA((4,)),
        ],
        compiler_params=pltpu.CompilerParams(
            collective_id=number, has_side_effects=True, vmem_limit_bytes=40 * MIB
        ),
        cost_estimate=moved(2 * part.size),
        name="scatter",
    )(part)


def exchange_kernel(x_ref, o_ref, send, recv, own_sem):
    me = lax.axis_index("seq")
    others = [lax.rem(me + i, 8) for i in range(1, 8)]
    greet(others)
    own = pltpu.make_async_copy(x_ref.at[me], o_ref.at[me], own_sem)
    own.start()
    copies = [
        remote(send, recv, i, x_ref.at[other], o_ref.at[me], other)
        for i, other in enumerate(others)
    ]
    for c in copies:
        c.start()
    own.wait()
    for c in copies:
        c.wait()


def exchange_plane(x, number):
    if lax.axis_size("seq") != 8:
        return lax.all_to_all(x, "seq", 0, 0)
    return pl.pallas_call(
        exchange_kernel,
        out_shape=jax.ShapeDtypeStruct(x.shape, x.dtype),
        in_specs=[pl.BlockSpec(memory_space=pl.ANY)],
        out_specs=pl.BlockSpec(memory_space=pl.ANY),
        scratch_shapes=[
            pltpu.SemaphoreType.DMA((7,)),
            pltpu.SemaphoreType.DMA((7,)),
            pltpu.SemaphoreType.DMA,
        ],
        compiler_params=pltpu.CompilerParams(collective_id=number, has_side_effects=True),
        cost_estimate=moved(4 * x.size),
        name="exchange",
    )(x)


CHUNKS = (64, 64, 48)


class PlaneGather:
    def __init__(self, source, target, send, recv):
        me, sib, xn, yn = partners()
        diag = xn + yn - me
        half = target.shape[1] // 2
        upper, lower = pl.ds(0, half), pl.ds(half, half)
        copy = functools.partial(remote, send, recv)

        def direct(k, part, to):
            return copy(k, source.at[part], target.at[me, part], to)

        def pass_on(k, origin, part, to):
            return copy(k, target.at[origin, part], target.at[origin, part], to)

        self.xa, self.yb = direct(0, upper, xn), direct(1, lower, yn)
        self.xb, self.ya = direct(2, lower, xn), direct(3, upper, yn)
        self.s0 = copy(4, source, target.at[me], sib)
        self.fy, self.fx = pass_on(5, xn, upper, yn), pass_on(6, yn, lower, xn)
        self.s1, self.s2 = pass_on(7, xn, upper, sib), pass_on(8, yn, lower, sib)
        self.s3, self.s4 = pass_on(9, xn, lower, sib), pass_on(10, yn, upper, sib)
        self.s5, self.s6 = pass_on(11, diag, upper, sib), pass_on(12, diag, lower, sib)

    def start(self):
        for c in (self.xa, self.yb, self.xb, self.ya, self.s0):
            c.start()

    def forward_first(self):
        self.xa.wait_recv()
        self.yb.wait_recv()
        for c in (self.fy, self.fx, self.s1, self.s2):
            c.start()

    def forward_second(self):
        self.xb.wait_recv()
        self.ya.wait_recv()
        self.s3.start()
        self.s4.start()

    def forward_third(self):
        self.fy.wait_recv()
        self.fx.wait_recv()
        self.s5.start()
        self.s6.start()

    def from_sibling(self, chip):
        for c in {"own": (self.s0,), "x": (self.s1, self.s3), "y": (self.s2, self.s4), "diag": (self.s5, self.s6)}[chip]:
            c.wait_recv()

    def sent(self):
        for c in (self.xa, self.yb, self.xb, self.ya, self.s0, self.fy, self.fx):
            c.wait_send()
        for c in (self.s1, self.s2, self.s3, self.s4, self.s5, self.s6):
            c.wait_send()

    def arrive(self, step):
        @pl.when(step == 1)
        def _():
            self.from_sibling("own")

        @pl.when(step == 2)
        def _():
            self.forward_first()
            self.forward_second()
            self.from_sibling("x")

        @pl.when(step == 4)
        def _():
            self.from_sibling("y")

        @pl.when(step == 6)
        def _():
            self.forward_third()
            self.from_sibling("diag")


class LineGather:
    def __init__(self, item, source, block, send, recv, local):
        z = lax.axis_index("dp")
        self.z = z

        def copy(k, src, owner, to):
            return pltpu.make_async_remote_copy(
                src_ref=src,
                dst_ref=block(owner),
                send_sem=send.at[item, k],
                recv_sem=recv.at[item, owner],
                device_id={"dp": to},
                device_id_type=MESH,
            )

        self.sends = []
        for k, d in enumerate((2, -2, 1, -1)):
            to = z + d
            valid = (to >= 0) & (to < 4)
            self.sends.append((valid, copy(k, source, z, jnp.clip(to, 0, 3))))
        inner = (z == 1) | (z == 2)
        far = jnp.where(z == 1, 3, 0)
        self.stop = (inner, copy(4, block(far), far, jnp.where(z == 1, 0, 3)))
        others = [lax.rem(z + o, 4) for o in (1, 2, 3)]
        self.blocks = [copy(0, source, other, other) for other in others]
        self.own = pltpu.make_async_copy(source, block(z), local.at[item])

    def start(self):
        self.own.start()
        for valid, c in self.sends:

            @pl.when(valid)
            def _(c=c):
                c.start()

    def forward(self):
        inner, c = self.stop

        @pl.when(inner)
        def _():
            self.blocks[1].wait_recv()
            c.start()

    def wait(self):
        inner, unused = self.stop
        self.blocks[0].wait_recv()
        self.blocks[2].wait_recv()

        @pl.when(jnp.logical_not(inner))
        def _():
            self.blocks[1].wait_recv()

        self.own.wait()

    def sent(self):
        for valid, c in (*self.sends, self.stop):

            @pl.when(valid)
            def _(c=c):
                c.wait_send()


def nearest_first(step):
    me, sib, xn, yn = partners()
    chip = jnp.where(step < 4, xn, jnp.where(step < 6, yn, xn + yn - me))
    later = chip + jnp.where(lax.rem(step, 2) == 0, sib - me, 0)
    return jnp.where(step == 0, me, jnp.where(step == 1, sib, later))


def farthest_first(step):
    me, sib, xn, yn = partners()
    chip = jnp.where(step < 4, xn, yn)
    chip = jnp.where(step < 2, xn + yn - me, jnp.where(step < 6, chip, me))
    return chip + jnp.where(lax.rem(step, 2) == 0, sib - me, 0)


def layer_kernel(
    x_ref,
    c_ref,
    wa_ref,
    wo_ref,
    wgu_ref,
    wd_ref,
    gain_ref,
    first_ref,
    x_all,
    c_all,
    h2_all,
    wo_all,
    h1_out,
    q_out,
    k_out,
    v_out,
    att_out,
    tok_out,
    mid_out,
    wa_out,
    gain_out,
    out_part,
    gh_ref,
    dgu_out,
    dd_out,
    wa,
    wgu,
    wd,
    gains,
    q_s,
    k_s,
    v_s,
    att_s,
    tok,
    mid,
    act_s,
    ggu_s,
    sum_gu,
    sum_d,
    x_buf,
    c_buf,
    o_buf,
    w_buf,
    beside,
    held,
    got,
    one,
    two,
    gsend,
    grecv,
    zsend,
    zrecv,
    zlocal,
    esend,
    erecv,
    rsend,
    rrecv,
    load_sem,
    out_sem,
    h1_sem,
    w_sem,
    done_sem,
    self_sem,
):
    me, sib, xn, yn = partners()
    z = lax.axis_index("dp")
    rows, width = x_ref.shape
    span = rows // 2
    wide, qk = v_s.shape[2], q_s.shape[2]
    share = CHUNKS[0] + CHUNKS[1] + CHUNKS[2]
    half = rows // 2
    upper, lower = pl.ds(0, half), pl.ds(half, half)

    barrier = pltpu.get_barrier_semaphore()
    for i in range(1, 8):
        pl.semaphore_signal(
            barrier, inc=1, device_id={"seq": lax.rem(me + i, 8)}, device_id_type=MESH
        )
    for i in range(1, 4):
        pl.semaphore_signal(
            barrier, inc=1, device_id={"dp": lax.rem(z + i, 4)}, device_id_type=MESH
        )
    pl.semaphore_wait(barrier, 10)

    tokens = PlaneGather(x_ref, x_all, gsend.at[0], grecv.at[0])
    out_w = PlaneGather(wo_all.at[me], wo_all, gsend.at[1], grecv.at[1])
    cots = PlaneGather(c_ref, c_all, gsend.at[2], grecv.at[2])
    hidden_in = PlaneGather(held.at[0], h2_all, gsend.at[3], grecv.at[3])

    def line(item, source, block):
        return LineGather(item, source, block, zsend, zrecv, zlocal)

    depth = wa_ref.shape[0]

    def rows_of(ref, count, columns=None):
        def block(owner):
            if columns is None:
                return ref.at[pl.ds(owner * count, count)]
            return ref.at[pl.ds(owner * count, count), columns]

        return block

    z_gain = line(
        0, gain_ref, lambda owner: gains.at[:, pl.ds(pl.multiple_of(owner * depth, 128), depth)]
    )
    z_attn = line(1, wa_ref, rows_of(wa, depth))
    z_out = line(
        2,
        wo_ref.at[:, pl.ds(pl.multiple_of(me * wide, 128), wide)],
        lambda owner: wo_all.at[me, pl.ds(owner * depth, depth)],
    )
    z_up, z_down = [], []
    column, before = 0, 0
    columns, hiddens = [], []
    for k, count in enumerate(CHUNKS):
        part = pl.ds(column, 8 * count)
        z_up.append(line(3 + k, wgu_ref.at[:, part], rows_of(wgu, depth, part)))
        z_down.append(
            line(
                6 + k,
                wd_ref.at[pl.ds(me * share + before, count)],
                lambda owner, base=4 * before, count=count: wd.at[
                    pl.ds(base + owner * count, count)
                ],
            )
        )
        columns.append(column)
        hiddens.append(4 * before)
        column += 8 * count
        before += count

    tokens.start()
    for g in (z_gain, z_attn, z_out):
        g.start()

    def loads(order, step, sources):
        slot = lax.rem(step, 2)
        owner = order(step)
        return [
            pltpu.make_async_copy(source.at[owner], buf.at[slot], load_sem.at[i, slot])
            for i, (source, buf) in enumerate(sources)
        ]

    first_load = pltpu.make_async_copy(x_ref, x_buf.at[0], load_sem.at[0, 0])
    first_load.start()
    tokens.forward_first()
    z_gain.forward()
    z_attn.forward()
    tokens.forward_second()
    z_gain.wait()
    z_attn.wait()
    for g in (z_up[0], z_down[0]):
        g.start()

    def h1_copies(step):
        slot = lax.rem(step, 2)
        owner = nearest_first(step)
        return [
            pltpu.make_async_copy(
                o_buf.at[slot, pl.ds(m * span, span)],
                h1_out.at[m, pl.ds(owner * span, span)],
                h1_sem.at[m, slot],
            )
            for m in range(2)
        ]

    def arrive_tokens(step):
        @pl.when(step == 1)
        def _():
            tokens.from_sibling("own")

        @pl.when(step == 2)
        def _():
            tokens.from_sibling("x")

        @pl.when(step == 4)
        def _():
            tokens.forward_third()
            tokens.from_sibling("y")

        @pl.when(step == 5)
        def _():
            z_out.forward()

        @pl.when(step == 6)
        def _():
            tokens.from_sibling("diag")

    token_source = [(x_all, x_buf)]

    def project(step, carry):
        slot = lax.rem(step, 2)
        owner = nearest_first(step)
        for c in loads(nearest_first, step, token_source):
            c.wait()

        @pl.when(step >= 2)
        def _():
            for c in h1_copies(step - 2):
                c.wait()

        x = x_buf[slot].astype(jnp.float32)
        gain = gains[0:1, :].astype(jnp.float32)
        h_one = (x * norm_scale(x) * gain).astype(LOW)
        o_buf[slot] = h_one
        for c in h1_copies(step):
            c.start()
        arrive_tokens(step + 1)

        @pl.when(step < 7)
        def _():
            for c in loads(nearest_first, step + 1, token_source):
                c.start()

        projected = dot(h_one, wa[...]).astype(LOW)
        for m in range(2):
            there = pl.ds(owner * span, span)
            mine = projected[m * span : (m + 1) * span]
            v_s[m, there, :] = mine[:, :wide]
            q_s[m, there, :] = mine[:, wide : wide + qk]
            k_s[m, there, :] = mine[:, wide + qk : wide + 2 * qk]
        return carry

    lax.fori_loop(0, 8, project, 0)
    for step in (6, 7):
        for c in h1_copies(step):
            c.wait()
    z_out.wait()
    out_w.start()
    for g in (z_up[1], z_down[1]):
        g.start()

    finals = [
        pltpu.make_async_copy(source, target, done_sem.at[i])
        for i, (source, target) in enumerate(
            (
                (q_s, q_out),
                (k_s, k_out),
                (v_s, v_out),
                (wa, wa_out),
                (gains, gain_out),
                (att_s, att_out),
                (tok, tok_out),
                (mid, mid_out),
            )
        )
    ]
    for c in finals[:5]:
        c.start()

    length = v_s.shape[1]
    block = 256

    def attend_stream(m, carry):
        for i in range(length // block):
            rows_i = slice(i * block, (i + 1) * block)
            seen = (i + 1) * block
            for head in range(wide // HEAD_V):
                lanes = slice(head * HEAD_V, (head + 1) * HEAD_V)
                unused, unused_mask, weight = weights_of(
                    q_s[m, rows_i, :], k_s[m, :seen, :], head, first_ref[m, rows_i, :], i * block
                )
                denom = jnp.sum(weight, axis=1, keepdims=True)
                numer = dot(weight.astype(LOW), v_s[m, :seen, lanes])
                att_s[m, rows_i, lanes] = (numer / denom).astype(LOW)
        return carry

    lax.fori_loop(0, 2, attend_stream, 0)
    out_w.forward_first()
    cots.start()
    finals[5].start()

    to_mine = pl.ds(pl.multiple_of(me * wide, 128), wide)
    swaps = []
    for i in range(1, 8):
        other = lax.rem(me + i, 8)
        for m in range(2):
            swaps.append(
                remote(
                    esend,
                    erecv,
                    2 * (i - 1) + m,
                    att_s.at[m, pl.ds(other * span, span)],
                    tok.at[pl.ds(m * span, span), to_mine],
                    other,
                )
            )
            swaps[-1].start()
    kept = [
        pltpu.make_async_copy(
            att_s.at[m, pl.ds(me * span, span)],
            tok.at[pl.ds(m * span, span), to_mine],
            self_sem.at[m],
        )
        for m in range(2)
    ]
    for c in kept:
        c.start()
    x_load = pltpu.make_async_copy(x_ref, x_buf.at[0], load_sem.at[0, 0])
    x_load.start()

    def w_load(step):
        slot = lax.rem(step, 2)
        return pltpu.make_async_copy(wo_all.at[nearest_first(step)], w_buf.at[slot], w_sem.at[slot])

    w_load(0).start()
    out_w.forward_second()
    z_up[0].forward()
    z_down[0].forward()
    for c in kept:
        c.wait()
    for c in swaps:
        c.wait_recv()
    finals[6].start()
    x_load.wait()

    def arrive_out(step):
        @pl.when(step == 1)
        def _():
            out_w.from_sibling("own")

        @pl.when(step == 2)
        def _():
            out_w.from_sibling("x")

        @pl.when(step == 4)
        def _():
            out_w.forward_third()
            out_w.from_sibling("y")

        @pl.when(step == 6)
        def _():
            out_w.from_sibling("diag")

    def project_out(step, carry):
        slot = lax.rem(step, 2)
        owner = nearest_first(step)
        w_load(step).wait()
        arrive_out(step + 1)

        @pl.when(step < 7)
        def _():
            w_load(step + 1).start()

        there = pl.ds(pl.multiple_of(owner * wide, 128), wide)
        mid[:, there] = dot(tok[...], w_buf[slot])
        return carry

    lax.fori_loop(0, 8, project_out, 0)
    mid_value = x_buf[0].astype(jnp.float32) + mid[...]
    mid[...] = mid_value
    held[0] = (mid_value * norm_scale(mid_value) * gains[1:2, :].astype(jnp.float32)).astype(LOW)
    finals[7].start()
    hidden_in.start()
    own_h2 = pltpu.make_async_copy(held.at[0], h2_all.at[me], self_sem.at[2])
    own_c = pltpu.make_async_copy(c_ref, c_all.at[me], self_sem.at[3])
    own_h2.start()
    own_c.start()
    cots.forward_first()
    cots.forward_second()
    for g in (z_up[2], z_down[2]):
        g.start()
    own_h2.wait()
    own_c.wait()
    z_up[0].wait()
    z_down[0].wait()

    sources = [(h2_all, x_buf), (c_all, c_buf)]

    def out_copy(order, step):
        slot = lax.rem(step, 2)
        return pltpu.make_async_copy(o_buf.at[slot], out_part.at[order(step)], out_sem.at[slot])

    def hidden_chunk(k, owner, h, c):
        count = 4 * CHUNKS[k]
        pair = pl.ds(columns[k], 2 * count)
        here = pl.ds(hiddens[k], count)
        both = dot(h, wgu[:, pair])
        gate, up = both[:, :count], both[:, count:]
        g_act = contract(c, wd[here, :], 1, 1)
        sigmoid = jax.nn.sigmoid(gate)
        silu = gate * sigmoid
        act = (silu * up).astype(LOW)
        g_gate = (g_act * up * sigmoid * (1.0 + gate * (1.0 - sigmoid))).astype(LOW)
        g_up = (g_act * silu).astype(LOW)
        there = pl.ds(owner * rows, rows)
        act_s[there, here] = act
        g_both = jnp.concatenate([g_gate, g_up], axis=1)
        ggu_s[there, pair] = g_both
        return act, g_both

    def add_grads(k, step, h, c, act, g_both):
        count = 4 * CHUNKS[k]

        @pl.when(step == 0)
        def _():
            sum_gu[...] = jnp.zeros_like(sum_gu)
            sum_d[...] = jnp.zeros_like(sum_d)

        sum_gu[:, : 2 * count] += contract(h, g_both, 0, 0)
        sum_d[:count, :] += contract(act, c, 0, 0)

    def emit(k):
        count = 4 * CHUNKS[k]
        pending = [None, None]
        for i in range(width // rows):
            slot = i % 2
            if pending[slot] is not None:
                pending[slot].wait()
            o_buf[slot, :, : 2 * count] = sum_gu[i * rows : (i + 1) * rows, : 2 * count].astype(LOW)
            pending[slot] = pltpu.make_async_copy(
                o_buf.at[slot, :, pl.ds(0, 2 * count)],
                dgu_out.at[pl.ds(i * rows, rows), pl.ds(columns[k], 2 * count)],
                out_sem.at[slot],
            )
            pending[slot].start()
        for c in pending:
            c.wait()
        o_buf[0, :count, :] = sum_d[:count, :].astype(LOW)
        downs = []
        for owner in range(4):
            downs.append(
                pltpu.make_async_copy(
                    o_buf.at[0, pl.ds(owner * CHUNKS[k], CHUNKS[k])],
                    dd_out.at[pl.ds(owner * share + hiddens[k] // 4, CHUNKS[k])],
                    h1_sem.at[owner // 2, owner % 2],
                )
            )
            downs[-1].start()
        for c in downs:
            c.wait()

    def forward_pass(k, arrive, step, carry):
        slot = lax.rem(step, 2)
        for c in loads(nearest_first, step, sources):
            c.wait()
        h, c = x_buf[slot], c_buf[slot]
        act, g_both = hidden_chunk(k, nearest_first(step), h, c)
        if arrive is not None:
            arrive(step + 1)

        @pl.when(step < 7)
        def _():
            for c in loads(nearest_first, step + 1, sources):
                c.start()

        add_grads(k, step, h, c, act, g_both)
        return carry

    def arrive_both(step):
        hidden_in.arrive(step)

        @pl.when(step == 1)
        def _():
            cots.from_sibling("own")

        @pl.when(step == 2)
        def _():
            cots.from_sibling("x")

        @pl.when(step == 4)
        def _():
            cots.forward_third()
            cots.from_sibling("y")

        @pl.when(step == 5)
        def _():
            z_up[1].forward()
            z_down[1].forward()

        @pl.when(step == 6)
        def _():
            cots.from_sibling("diag")

    for c in loads(nearest_first, 0, sources):
        c.start()
    lax.fori_loop(0, 8, functools.partial(forward_pass, 0, arrive_both), 0)
    hidden_in.sent()
    z_up[1].wait()
    z_down[1].wait()
    for c in loads(nearest_first, 0, sources):
        c.start()
    emit(0)

    def arrive_last(step):
        @pl.when(step == 4)
        def _():
            z_up[2].forward()
            z_down[2].forward()

    lax.fori_loop(0, 8, functools.partial(forward_pass, 1, arrive_last), 0)
    z_up[2].wait()
    z_down[2].wait()
    for c in loads(farthest_first, 0, sources):
        c.start()
    emit(1)

    copy = functools.partial(remote, rsend, rrecv)
    b_diag = copy(0, beside.at[0], got.at[2], sib)
    b_x = copy(1, beside.at[1], got.at[1], sib)
    b_y = copy(2, beside.at[0], got.at[3], sib)
    b_own = copy(3, beside.at[1], got.at[0], sib)
    x0 = copy(4, held.at[2, upper], one.at[0], xn)
    y0 = copy(5, held.at[2, lower], one.at[1], yn)
    x1 = copy(6, held.at[1, upper], one.at[2], xn)
    y1 = copy(7, held.at[3, lower], one.at[3], yn)
    y2 = copy(8, held.at[3, upper], two.at[0], yn)
    x2 = copy(9, held.at[1, lower], two.at[1], xn)

    def last_pass(step, carry):
        slot = lax.rem(step, 2)
        owner = farthest_first(step)
        there = pl.ds(owner * rows, rows)
        for c in loads(farthest_first, step, sources):
            c.wait()
        h, c = x_buf[slot], c_buf[slot]
        act, g_both = hidden_chunk(2, owner, h, c)
        part = contract(ggu_s[there, :], wgu[...], 1, 1).astype(LOW)

        for k, place, sent in ((0, 0, b_diag), (2, 1, b_x), (4, 0, b_y), (6, 1, b_own)):

            @pl.when(step == k)
            def _(k=k, place=place, sent=sent):
                if k == 4:
                    b_diag.wait_send()
                if k == 6:
                    b_x.wait_send()
                beside[place] = part
                sent.start()

        for k, place, arrived in ((1, 2, b_diag), (3, 1, b_x), (5, 3, b_y), (7, 0, b_own)):

            @pl.when(step == k)
            def _(k=k, place=place, arrived=arrived):
                arrived.wait_recv()
                held[place] = part + got[place]
                if k == 1:
                    x0.start()
                    y0.start()
                if k == 3:
                    x1.start()
                if k == 5:
                    y1.start()
                    y0.wait_recv()
                    held[1, half:] = held[1, half:] + one[1]
                    x2.start()
                    x0.wait_recv()
                    held[3, :half] = held[3, :half] + one[0]
                    y2.start()

        @pl.when(step >= 2)
        def _():
            out_copy(farthest_first, step - 2).wait()

        o_buf[slot] = dot(act_s[there, :], wd[...]).astype(LOW)
        out_copy(farthest_first, step).start()

        @pl.when(step < 7)
        def _():
            for c in loads(farthest_first, step + 1, sources):
                c.start()

        add_grads(2, step, h, c, act, g_both)
        return carry

    lax.fori_loop(0, 8, last_pass, 0)
    out_copy(farthest_first, 6).wait()
    out_copy(farthest_first, 7).wait()
    emit(2)
    f32 = jnp.float32
    x1.wait_recv()
    y2.wait_recv()
    gh_ref[:half] = held[0, :half].astype(f32) + one[2].astype(f32) + two[0].astype(f32)
    y1.wait_recv()
    x2.wait_recv()
    gh_ref[half:] = held[0, half:].astype(f32) + one[3].astype(f32) + two[1].astype(f32)
    for c in finals:
        c.wait()
    for c in (b_y, b_own, x0, y0, x1, y1, y2, x2, *swaps):
        c.wait_send()
    for g in (tokens, out_w, cots, z_gain, z_attn, z_out, *z_up, *z_down):
        g.sent()


def layer_front(tokens, cot, attn_slice, w_out, ffn_slice, w_down, gain_rows, first, wide, qk):
    rows, width = tokens.shape
    streams, length, unused = first.shape
    hidden = 4 * sum(CHUNKS)
    largest = 4 * max(CHUNKS)
    shape = jax.ShapeDtypeStruct
    f32 = jnp.float32
    anywhere = pl.BlockSpec(memory_space=pl.ANY)
    in_vmem = pl.BlockSpec(memory_space=pltpu.VMEM)
    plane = shape((8, rows, width), LOW)
    narrow = shape((streams, length, qk), LOW)
    broad = shape((streams, length, wide), LOW)
    attn_shape = (width, attn_slice.shape[1])
    out_shape = [
        plane,
        plane,
        plane,
        shape((8, width, width // 8), LOW),
        shape((streams, length, width), LOW),
        narrow,
        narrow,
        broad,
        broad,
        shape((rows, width), LOW),
        shape((rows, width), f32),
        shape(attn_shape, LOW),
        shape((gain_rows.shape[0], width), LOW),
        plane,
        shape((rows, width), f32),
        shape((width, 2 * hidden), LOW),
        shape((hidden, width), LOW),
    ]
    dma = pltpu.SemaphoreType.DMA
    vmem = pltpu.VMEM
    return pl.pallas_call(
        layer_kernel,
        out_shape=out_shape,
        in_specs=[anywhere] * 7 + [in_vmem],
        out_specs=[anywhere] * 14 + [in_vmem] + [anywhere] * 2,
        scratch_shapes=[
            vmem(attn_shape, LOW),
            vmem((width, 2 * hidden), LOW),
            vmem((hidden, width), LOW),
            vmem((gain_rows.shape[0], width), LOW),
            vmem(narrow.shape, LOW),
            vmem(narrow.shape, LOW),
            vmem(broad.shape, LOW),
            vmem(broad.shape, LOW),
            vmem((rows, width), LOW),
            vmem((rows, width), f32),
            vmem((8 * rows, hidden), LOW),
            vmem((8 * rows, 2 * hidden), LOW),
            vmem((width, 2 * largest), f32),
            vmem((largest, width), f32),
            vmem((2, rows, width), LOW),
            vmem((2, rows, width), LOW),
            vmem((2, rows, width), LOW),
            vmem((2, width, width // 8), LOW),
            vmem((2, rows, width), LOW),
            vmem((4, rows, width), LOW),
            vmem((4, rows, width), LOW),
            vmem((4, rows // 2, width), LOW),
            vmem((2, rows // 2, width), LOW),
            dma((4, 13)),
            dma((4, 13)),
            dma((9, 5)),
            dma((9, 4)),
            dma((9,)),
            dma((14,)),
            dma((14,)),
            dma((10,)),
            dma((10,)),
            dma((2, 2)),
            dma((2,)),
            dma((2, 2)),
            dma((2,)),
            dma((8,)),
            dma((4,)),
        ],
        compiler_params=pltpu.CompilerParams(
            collective_id=21, has_side_effects=True, vmem_limit_bytes=63 * MIB
        ),
        cost_estimate=pl.CostEstimate(
            flops=6 * 3 * 8 * rows * width * hidden,
            bytes_accessed=400 * rows * width,
            transcendentals=0,
        ),
        name="layer",
    )(tokens, cot, attn_slice, w_out, ffn_slice, w_down, gain_rows, first)


def ffn_lax(h_two, cot_all, gate_full, up_full, down_full):
    pieces, rows, width = cot_all.shape
    h_two_all = gather_plane(h_two, 5).reshape(-1, width)
    cot_all = cot_all.reshape(-1, width)
    gate = dot(h_two_all, gate_full)
    up = dot(h_two_all, up_full)
    g_act = contract(cot_all, down_full, 1, 1)
    sigmoid = jax.nn.sigmoid(gate)
    silu = gate * sigmoid
    act = (silu * up).astype(LOW)
    g_gate = (g_act * up * sigmoid * (1.0 + gate * (1.0 - sigmoid))).astype(LOW)
    g_up = (g_act * silu).astype(LOW)
    part = (contract(g_gate, gate_full, 1, 1) + contract(g_up, up_full, 1, 1)).astype(LOW)
    return (
        dot(act, down_full).astype(LOW).reshape(pieces, rows, width),
        scatter_plane(part.reshape(pieces, rows, width), 7),
        contract(h_two_all, g_gate, 0, 0).astype(LOW),
        contract(h_two_all, g_up, 0, 0).astype(LOW),
        contract(act, cot_all, 0, 0).astype(LOW),
    )


def norm_scale(rows):
    return lax.rsqrt(jnp.mean(rows * rows, axis=-1, keepdims=True) + epsilon)


def norm_backward(grad, normed, inverse, gain):
    scaled = grad * gain
    return inverse * (scaled - normed * jnp.mean(scaled * normed, axis=-1, keepdims=True))


def local(
    tokens,
    doc_lengths,
    w_query,
    w_key,
    w_value,
    w_out,
    w_gate,
    w_up,
    w_down,
    gain_attn,
    gain_mlp,
    cotangent,
):
    micro, span = tokens.shape[1:3]
    pieces, groups = lax.axis_size("seq"), lax.axis_size("dp")
    place = lax.axis_index("seq")
    length = pieces * span
    heads = max(1, HEADS // pieces)
    sharers = max(1, pieces // HEADS)
    streams = micro // sharers
    first_head = place // sharers * heads
    first_stream = place % sharers * streams
    qk, wide = heads * QK_DIM, heads * HEAD_V
    hidden = FF // pieces

    out_width = D // pieces
    rows_dp = w_gate.shape[0]
    share = hidden // groups
    block = FF // groups
    mine = micro * span
    fused = pieces == 8 and groups == 4 and micro == 2 and span == 128
    chunks = CHUNKS if fused else (share,)

    def hidden_columns(w):
        parts = [
            lax.dynamic_slice_in_dim(w, z * block + place * share, share, 1) for z in range(groups)
        ]
        edges = [sum(chunks[:k]) for k in range(len(chunks) + 1)]
        return [
            [part[:, edges[k] : edges[k + 1]] for part in parts] for k in range(len(chunks))
        ]

    gate_parts, up_parts = hidden_columns(w_gate), hidden_columns(w_up)
    ffn_slice = jnp.concatenate(
        [part for k in range(len(chunks)) for part in gate_parts[k] + up_parts[k]], axis=1
    )
    attn_parts = [
        lax.dynamic_slice_in_dim(w_value, first_head * HEAD_V, wide, 1),
        lax.dynamic_slice_in_dim(w_query, first_head * QK_DIM, qk, 1),
        lax.dynamic_slice_in_dim(w_key, first_head * QK_DIM, qk, 1),
    ]

    lengths = lax.dynamic_slice_in_dim(doc_lengths[0], first_stream, streams, 0)
    starts = jnp.cumsum(lengths, axis=1) - lengths
    position = jnp.arange(length, dtype=jnp.int32)
    begun = starts[:, None, :] <= position[None, :, None]
    first = jnp.max(jnp.where(begun, starts[:, None, :], 0), axis=2)[..., None]

    x_own = tokens[0].reshape(mine, D)
    flat = x_own.astype(jnp.float32)
    cot = cotangent[0].reshape(mine, D)

    def to_tokens(by_head):
        sent = by_head.reshape(streams, pieces, span, wide).transpose(1, 0, 2, 3)
        got = exchange_plane(sent, 3).reshape(pieces // sharers, micro, span, wide)
        return got.transpose(1, 2, 0, 3).reshape(mine, HEADS * HEAD_V)

    def to_heads(by_token):
        sent = by_token.reshape(micro, span, pieces // sharers, wide).transpose(2, 0, 1, 3)
        got = exchange_plane(sent.reshape(pieces, streams, span, wide), 4)
        return got.transpose(1, 0, 2, 3).reshape(streams, length, wide)

    if fused:
        attn_slice = jnp.concatenate(
            attn_parts + [jnp.zeros((rows_dp, 128 - 2 * qk), LOW)], axis=1
        )
        gain_rows = jnp.concatenate(
            [gain_attn[None], gain_mlp[None], jnp.zeros((14, rows_dp), LOW)], axis=0
        )
        front = layer_front(
            x_own, cot, attn_slice, w_out, ffn_slice, w_down, gain_rows, first, wide, qk
        )
        out_full, h_all, query, key, value, att_heads, attended, mid = front[3:11]
        attn_full, gains, out_part, g_h_two, d_ffn, d_down = front[11:]
        h_flat = h_all.reshape(streams * length, D)
        value_full = attn_full[:, :wide]
        query_full = attn_full[:, wide : wide + qk]
        key_full = attn_full[:, wide + qk : wide + 2 * qk]
        gains = gains.astype(jnp.float32)
        gain_one, gain_two = gains[0], gains[1]
    else:

        def gather_dp(w):
            return lax.all_gather(w, "dp", axis=0, tiled=True)

        attn_got = gather_dp(
            jnp.concatenate(
                attn_parts
                + [
                    lax.dynamic_slice_in_dim(w_out, place * out_width, out_width, 1),
                    gain_attn[:, None],
                    gain_mlp[:, None],
                ],
                axis=1,
            )
        )
        ffn_full = gather_dp(ffn_slice)
        down_full = gather_dp(lax.dynamic_slice_in_dim(w_down, place * share, share, 0))
        value_full = attn_got[:, :wide]
        query_full = attn_got[:, wide : wide + qk]
        key_full = attn_got[:, wide + qk : wide + 2 * qk]
        out_full = gather_plane(attn_got[:, wide + 2 * qk : wide + 2 * qk + out_width], 2)
        gains = attn_got[:, wide + 2 * qk + out_width :].astype(jnp.float32)
        gain_one, gain_two = gains[:, 0], gains[:, 1]
        x_all = gather_plane(x_own, 1).reshape(pieces, micro, span, D).transpose(1, 0, 2, 3)
        x_all = lax.dynamic_slice_in_dim(x_all, first_stream, streams, 0).astype(jnp.float32)
        h_flat = (x_all * norm_scale(x_all) * gain_one).astype(LOW).reshape(streams * length, D)
        value = dot(h_flat, value_full).astype(LOW).reshape(streams, length, wide)
        query = dot(h_flat, query_full).astype(LOW).reshape(streams, length, qk)
        key = dot(h_flat, key_full).astype(LOW).reshape(streams, length, qk)
        att_heads = attend(query, key, value, first, heads)
        attended = to_tokens(att_heads)
        mid = flat + jnp.einsum(
            "tk,skn->tsn", attended, out_full, preferred_element_type=jnp.float32
        ).reshape(mine, D)
        h_two = (mid * norm_scale(mid) * gain_two).astype(LOW)
        out_part, g_h_two, d_gate, d_up, d_down = ffn_lax(
            h_two, gather_plane(cot, 6), ffn_full[:, :hidden], ffn_full[:, hidden:], down_full
        )
        d_ffn = jnp.concatenate([d_gate, d_up], axis=1)

    inverse_two = norm_scale(mid)
    plain_two = mid * inverse_two

    def scatter_dp(part):
        return lax.psum_scatter(part, "dp", scatter_dimension=0, tiled=True)

    sum_ffn, sum_down = scatter_dp(d_ffn), scatter_dp(d_down)
    output = (mid + scatter_plane(out_part, 8)).astype(LOW)

    g_mid = cot.astype(jnp.float32) + norm_backward(g_h_two, plain_two, inverse_two, gain_two)
    g_mid_low = g_mid.astype(LOW)
    g_att = jnp.einsum(
        "tsn,skn->tk",
        g_mid_low.reshape(mine, pieces, out_width),
        out_full,
        preferred_element_type=jnp.float32,
    )
    g_att = to_heads(g_att.astype(LOW))
    g_query, g_key, g_value = attend_back(query, key, value, first, att_heads, g_att, heads)
    g_value = g_value.reshape(streams * length, wide)
    g_query = g_query.reshape(streams * length, qk)
    g_key = g_key.reshape(streams * length, qk)
    g_h_one_part = (
        contract(g_value, value_full, 1, 1)
        + contract(g_query, query_full, 1, 1)
        + contract(g_key, key_full, 1, 1)
    ).astype(LOW)
    g_h_one_part = g_h_one_part.reshape(streams, pieces, span, D).transpose(1, 0, 2, 3)
    if sharers > 1:
        padded = jnp.zeros((pieces, micro, span, D), LOW)
        g_h_one_part = lax.dynamic_update_slice_in_dim(padded, g_h_one_part, first_stream, 1)
    g_h_one = scatter_plane(g_h_one_part.reshape(pieces, mine, D), 9)
    inverse_one = norm_scale(flat)
    plain_one = flat * inverse_one
    input_grad = g_mid + norm_backward(g_h_one, plain_one, inverse_one, gain_one)

    own = rows_dp // pieces
    grad_out = contract(attended, g_mid_low, 0, 0).astype(LOW)
    grad_out = grad_out.reshape(groups, pieces, own, D).transpose(1, 0, 2, 3)
    grad_out = scatter_plane(grad_out.reshape(pieces, groups * own, D), 10).astype(LOW)
    grad_out, sum_ffn, sum_down = lax.optimization_barrier((grad_out, sum_ffn, sum_down))
    grad_out = scatter_dp(grad_out)
    grad_attn = jnp.concatenate(
        [
            contract(h_flat, g_value, 0, 0).astype(LOW),
            contract(h_flat, g_query, 0, 0).astype(LOW),
            contract(h_flat, g_key, 0, 0).astype(LOW),
            jnp.sum(g_h_one * plain_one, axis=0).astype(LOW)[:, None],
            jnp.sum(g_h_two * plain_two, axis=0).astype(LOW)[:, None],
        ],
        axis=1,
    )
    grad_attn, grad_out = lax.optimization_barrier((grad_attn, grad_out))
    grad_attn = scatter_dp(grad_attn)
    ffn_got = exchange_plane(sum_ffn.reshape(pieces, own, 2 * hidden), 11).astype(jnp.float32)
    attn_got = exchange_plane(grad_attn.reshape(pieces, own, -1), 12).astype(jnp.float32)
    grad_gains = jnp.sum(attn_got[:, :, wide + 2 * qk :], axis=0)
    attn_got = jnp.sum(attn_got.reshape(pieces // sharers, sharers, own, -1), axis=1)

    def by_rows(block):
        return block.transpose(1, 0, 2).reshape(own, -1)

    def by_hidden(second):
        parts, start = [], 0
        for count in chunks:
            begin = start + second * groups * count
            part = ffn_got[:, :, begin : begin + groups * count]
            parts.append(part.reshape(pieces, own, groups, count))
            start += 2 * groups * count
        whole = jnp.concatenate(parts, axis=3)
        return whole.transpose(1, 2, 0, 3).reshape(own, FF)

    return (
        output.reshape(tokens.shape),
        input_grad.reshape(tokens.shape),
        by_rows(attn_got[:, :, wide : wide + qk]),
        by_rows(attn_got[:, :, wide + qk : wide + 2 * qk]),
        by_rows(attn_got[:, :, :wide]),
        grad_out.astype(jnp.float32),
        by_hidden(0),
        by_hidden(1),
        sum_down.astype(jnp.float32),
        grad_gains[:, 0],
        grad_gains[:, 1],
    )


def solution(mesh):
    by_token, by_row = P("dp", None, "seq", None), P("dp", None)
    grad_rows, grad_entries = P(("dp", "seq"), None), P(("dp", "seq"))
    return jax.shard_map(
        local,
        mesh=mesh,
        in_specs=(by_token, P("dp", None, None)) + (by_row,) * 7 + (P("dp"), P("dp"), by_token),
        out_specs=(by_token, by_token) + (grad_rows,) * 7 + (grad_entries,) * 2,
        check_vma=False,
    )
```

```python
import functools
import math

import jax
import jax.numpy as jnp
from jax import lax
from jax.experimental import pallas as pl
from jax.experimental.pallas import tpu as pltpu
from jax.sharding import PartitionSpec as P

D = 2048
HEADS = 16
QK_DIM = 16
FF = 5632
HEAD_V = 128
epsilon = 1e-06
MIB = 1024 * 1024


def dot(left, right):
    return jnp.dot(left, right, preferred_element_type=jnp.float32)


def contract(left, right, left_dim, right_dim):
    return lax.dot_general(
        left, right, (((left_dim,), (right_dim,)), ((), ())), preferred_element_type=jnp.float32
    )


def head_lanes(rows, head):
    lane = lax.broadcasted_iota(jnp.int32, rows.shape, 1)
    inside = (lane >= head * QK_DIM) & (lane < (head + 1) * QK_DIM)
    return jnp.where(inside, rows, jnp.zeros_like(rows))


def weights_of(query, key, head, first, base):
    scores = contract(head_lanes(query, head), key, 1, 1)
    row = base + lax.broadcasted_iota(jnp.int32, scores.shape, 0)
    column = lax.broadcasted_iota(jnp.int32, scores.shape, 1)
    mask = (column <= row) & (column >= first)
    poly = 1.0 + scores * (1.0 / math.sqrt(QK_DIM)) + scores * scores * (0.5 / QK_DIM)
    return scores, mask, jnp.where(mask, poly, 0.0)


def attend_kernel(heads, q_ref, k_ref, v_ref, first_ref, out_ref):
    rows = q_ref.shape[1]
    base = pl.program_id(1) * rows
    for head in range(heads):
        columns = slice(head * HEAD_V, (head + 1) * HEAD_V)
        unused, unused_mask, weight = weights_of(
            q_ref[0], k_ref[0], head, first_ref[0], base
        )
        denom = jnp.sum(weight, axis=1, keepdims=True)
        numer = dot(weight.astype(jnp.bfloat16), v_ref[0, :, columns])
        out_ref[0, :, columns] = (numer / denom).astype(jnp.bfloat16)


def attend(query, key, value, first, heads):
    streams, length, width = query.shape
    rows = min(256, length)
    return pl.pallas_call(
        functools.partial(attend_kernel, heads),
        grid=(streams, length // rows),
        in_specs=[
            pl.BlockSpec((1, rows, width), lambda m, i: (m, i, 0)),
            pl.BlockSpec((1, length, width), lambda m, i: (m, 0, 0)),
            pl.BlockSpec((1, length, heads * HEAD_V), lambda m, i: (m, 0, 0)),
            pl.BlockSpec((1, rows, 1), lambda m, i: (m, i, 0)),
        ],
        out_specs=pl.BlockSpec((1, rows, heads * HEAD_V), lambda m, i: (m, i, 0)),
        out_shape=jax.ShapeDtypeStruct(value.shape, jnp.bfloat16),
        compiler_params=pltpu.CompilerParams(vmem_limit_bytes=48 * MIB),
        name="attend",
    )(query, key, value, first)


def attend_back_kernel(
    heads, q_ref, k_ref, v_ref, first_ref, att_ref, g_ref, gq_ref, gk_ref, gv_ref, gk_sum, gv_sum
):
    rows = q_ref.shape[1]
    step = pl.program_id(1)
    base = step * rows

    @pl.when(step == 0)
    def _():
        gk_sum[...] = jnp.zeros_like(gk_sum)
        gv_sum[...] = jnp.zeros_like(gv_sum)

    query, key = q_ref[0], k_ref[0]
    g_query = jnp.zeros(query.shape, jnp.float32)
    for head in range(heads):
        columns = slice(head * HEAD_V, (head + 1) * HEAD_V)
        scores, mask, weight = weights_of(query, key, head, first_ref[0], base)
        denom = jnp.sum(weight, axis=1, keepdims=True)
        a = (g_ref[0, :, columns].astype(jnp.float32) / denom).astype(jnp.bfloat16)
        b = -jnp.sum(
            a.astype(jnp.float32) * att_ref[0, :, columns].astype(jnp.float32),
            axis=1,
            keepdims=True,
        )
        g_weight = contract(a, v_ref[0, :, columns], 1, 1) + b
        slope = 1.0 / math.sqrt(QK_DIM) + scores * (1.0 / QK_DIM)
        g_scores = jnp.where(mask, g_weight * slope, 0.0).astype(jnp.bfloat16)
        g_query += head_lanes(dot(g_scores, key), head)
        gk_sum[...] += contract(g_scores, head_lanes(query, head), 0, 0)
        gv_sum[:, columns] += contract(weight.astype(jnp.bfloat16), a, 0, 0)
    gq_ref[0] = g_query.astype(jnp.bfloat16)

    @pl.when(step == pl.num_programs(1) - 1)
    def _():
        gk_ref[0] = gk_sum[...].astype(jnp.bfloat16)
        gv_ref[0] = gv_sum[...].astype(jnp.bfloat16)


def attend_back(query, key, value, first, attended, grad, heads):
    streams, length, width = query.shape
    rows = min(256, length)
    some = pl.BlockSpec((1, rows, width), lambda m, i: (m, i, 0))
    all_narrow = pl.BlockSpec((1, length, width), lambda m, i: (m, 0, 0))
    all_wide = pl.BlockSpec((1, length, heads * HEAD_V), lambda m, i: (m, 0, 0))
    some_wide = pl.BlockSpec((1, rows, heads * HEAD_V), lambda m, i: (m, i, 0))
    return pl.pallas_call(
        functools.partial(attend_back_kernel, heads),
        grid=(streams, length // rows),
        in_specs=[
            some,
            all_narrow,
            all_wide,
            pl.BlockSpec((1, rows, 1), lambda m, i: (m, i, 0)),
            some_wide,
            some_wide,
        ],
        out_specs=[some, all_narrow, all_wide],
        out_shape=[
            jax.ShapeDtypeStruct(query.shape, jnp.bfloat16),
            jax.ShapeDtypeStruct(key.shape, jnp.bfloat16),
            jax.ShapeDtypeStruct(value.shape, jnp.bfloat16),
        ],
        scratch_shapes=[
            pltpu.VMEM((length, width), jnp.float32),
            pltpu.VMEM((length, heads * HEAD_V), jnp.float32),
        ],
        compiler_params=pltpu.CompilerParams(vmem_limit_bytes=56 * MIB),
        name="attend_back",
    )(query, key, value, first, attended, grad)

MESH = pl.DeviceIdType.MESH
LOW = jnp.bfloat16


def partners():
    me = lax.axis_index("seq")
    core, x, y = me % 2, me // 2 % 2, me // 4
    return me, me + 1 - 2 * core, me + 2 - 4 * x, me + 4 - 8 * y


def greet(others):
    barrier = pltpu.get_barrier_semaphore()
    for other in others:
        pl.semaphore_signal(barrier, inc=1, device_id={"seq": other}, device_id_type=MESH)
    pl.semaphore_wait(barrier, len(others))


def remote(send, recv, k, src, dst, to):
    return pltpu.make_async_remote_copy(
        src_ref=src,
        dst_ref=dst,
        send_sem=send.at[k],
        recv_sem=recv.at[k],
        device_id={"seq": to},
        device_id_type=MESH,
    )


def gather_kernel(x_ref, o_ref, send, recv, own_sem):
    me, sib, xn, yn = partners()
    diag = xn + yn - me
    half = x_ref.shape[0] // 2
    copy = functools.partial(remote, send, recv)
    upper, lower = pl.ds(0, half), pl.ds(half, half)
    greet((sib, xn, yn))
    own = pltpu.make_async_copy(x_ref, o_ref.at[me], own_sem)
    own.start()
    xa = copy(0, x_ref.at[upper], o_ref.at[me, upper], xn)
    yb = copy(1, x_ref.at[lower], o_ref.at[me, lower], yn)
    xb = copy(2, x_ref.at[lower], o_ref.at[me, lower], xn)
    ya = copy(3, x_ref.at[upper], o_ref.at[me, upper], yn)
    beside = [copy(4, x_ref, o_ref.at[me], sib)]
    started = [xa, yb, xb, ya, beside[0]]
    for c in started:
        c.start()

    def pass_on(k, origin, part, to):
        block = o_ref.at[origin, part]
        c = copy(k, block, block, to)
        c.start()
        started.append(c)
        return c

    xa.wait_recv()
    fy = pass_on(5, xn, upper, yn)
    beside.append(pass_on(6, xn, upper, sib))
    yb.wait_recv()
    fx = pass_on(7, yn, lower, xn)
    beside.append(pass_on(8, yn, lower, sib))
    xb.wait_recv()
    beside.append(pass_on(9, xn, lower, sib))
    ya.wait_recv()
    beside.append(pass_on(10, yn, upper, sib))
    fy.wait_recv()
    beside.append(pass_on(11, diag, upper, sib))
    fx.wait_recv()
    beside.append(pass_on(12, diag, lower, sib))
    own.wait()
    for c in beside:
        c.wait_recv()
    for c in started:
        c.wait_send()


def moved(nbytes):
    return pl.CostEstimate(flops=0, bytes_accessed=nbytes * 10, transcendentals=0)


def gather_plane(x, number):
    pieces = lax.axis_size("seq")
    if pieces != 8:
        return lax.all_gather(x, "seq", axis=0)
    return pl.pallas_call(
        gather_kernel,
        out_shape=jax.ShapeDtypeStruct((8,) + x.shape, x.dtype),
        in_specs=[pl.BlockSpec(memory_space=pl.ANY)],
        out_specs=pl.BlockSpec(memory_space=pl.ANY),
        scratch_shapes=[
            pltpu.SemaphoreType.DMA((13,)),
            pltpu.SemaphoreType.DMA((13,)),
            pltpu.SemaphoreType.DMA,
        ],
        compiler_params=pltpu.CompilerParams(collective_id=number, has_side_effects=True),
        cost_estimate=moved(16 * x.size),
        name="gather",
    )(x)


def scatter_kernel(p_ref, o_ref, held, got, one, two, send, recv, own_sem):
    me, sib, xn, yn = partners()
    diag = xn + yn - me
    half = p_ref.shape[1] // 2
    copy = functools.partial(remote, send, recv)
    upper, lower = pl.ds(0, half), pl.ds(half, half)
    greet((sib, xn, yn))
    beside, loads = [], []
    for i, owner in enumerate((diag, xn, yn, me)):
        beside.append(copy(i, p_ref.at[owner + sib - me], got.at[i], sib))
        loads.append(pltpu.make_async_copy(p_ref.at[owner], held.at[i], own_sem.at[i]))
        beside[i].start()
        loads[i].start()

    def pair_sum(i):
        beside[i].wait_recv()
        loads[i].wait()
        held[i] = held[i] + got[i]

    pair_sum(0)
    x0 = copy(4, held.at[0, upper], one.at[0], xn)
    x0.start()
    y0 = copy(5, held.at[0, lower], one.at[1], yn)
    y0.start()
    pair_sum(1)
    x1 = copy(6, held.at[1, upper], one.at[2], xn)
    x1.start()
    pair_sum(2)
    y1 = copy(7, held.at[2, lower], one.at[3], yn)
    y1.start()
    pair_sum(3)
    x0.wait_recv()
    held[2, :half] = held[2, :half] + one[0]
    y2 = copy(8, held.at[2, upper], two.at[0], yn)
    y2.start()
    y0.wait_recv()
    held[1, half:] = held[1, half:] + one[1]
    x2 = copy(9, held.at[1, lower], two.at[1], xn)
    x2.start()
    x1.wait_recv()
    y1.wait_recv()
    y2.wait_recv()
    wide = jnp.float32
    o_ref[:half] = held[3, :half].astype(wide) + one[2].astype(wide) + two[0].astype(wide)
    x2.wait_recv()
    o_ref[half:] = held[3, half:].astype(wide) + one[3].astype(wide) + two[1].astype(wide)
    for c in (*beside, x0, y0, x1, y1, y2, x2):
        c.wait_send()


def scatter_plane(part, number):
    pieces, rows, columns = part.shape
    if pieces != 8:
        return lax.psum_scatter(part, "seq", scatter_dimension=0).astype(jnp.float32)
    return pl.pallas_call(
        scatter_kernel,
        out_shape=jax.ShapeDtypeStruct((rows, columns), jnp.float32),
        in_specs=[pl.BlockSpec(memory_space=pl.ANY)],
        out_specs=pl.BlockSpec(memory_space=pltpu.VMEM),
        scratch_shapes=[
            pltpu.VMEM((4, rows, columns), LOW),
            pltpu.VMEM((4, rows, columns), LOW),
            pltpu.VMEM((4, rows // 2, columns), LOW),
            pltpu.VMEM((2, rows // 2, columns), LOW),
            pltpu.SemaphoreType.DMA((10,)),
            pltpu.SemaphoreType.DMA((10,)),
            pltpu.SemaphoreType.DMA((4,)),
        ],
        compiler_params=pltpu.CompilerParams(
            collective_id=number, has_side_effects=True, vmem_limit_bytes=40 * MIB
        ),
        cost_estimate=moved(2 * part.size),
        name="scatter",
    )(part)


def exchange_kernel(x_ref, o_ref, send, recv, own_sem):
    me = lax.axis_index("seq")
    others = [lax.rem(me + i, 8) for i in range(1, 8)]
    greet(others)
    own = pltpu.make_async_copy(x_ref.at[me], o_ref.at[me], own_sem)
    own.start()
    copies = [
        remote(send, recv, i, x_ref.at[other], o_ref.at[me], other)
        for i, other in enumerate(others)
    ]
    for c in copies:
        c.start()
    own.wait()
    for c in copies:
        c.wait()


def exchange_plane(x, number):
    if lax.axis_size("seq") != 8:
        return lax.all_to_all(x, "seq", 0, 0)
    return pl.pallas_call(
        exchange_kernel,
        out_shape=jax.ShapeDtypeStruct(x.shape, x.dtype),
        in_specs=[pl.BlockSpec(memory_space=pl.ANY)],
        out_specs=pl.BlockSpec(memory_space=pl.ANY),
        scratch_shapes=[
            pltpu.SemaphoreType.DMA((7,)),
            pltpu.SemaphoreType.DMA((7,)),
            pltpu.SemaphoreType.DMA,
        ],
        compiler_params=pltpu.CompilerParams(collective_id=number, has_side_effects=True),
        cost_estimate=moved(4 * x.size),
        name="exchange",
    )(x)


CHUNKS = (64, 64, 48)


class PlaneGather:
    def __init__(self, source, target, send, recv):
        me, sib, xn, yn = partners()
        diag = xn + yn - me
        half = target.shape[1] // 2
        upper, lower = pl.ds(0, half), pl.ds(half, half)
        copy = functools.partial(remote, send, recv)

        def direct(k, part, to):
            return copy(k, source.at[part], target.at[me, part], to)

        def pass_on(k, origin, part, to):
            return copy(k, target.at[origin, part], target.at[origin, part], to)

        self.xa, self.yb = direct(0, upper, xn), direct(1, lower, yn)
        self.xb, self.ya = direct(2, lower, xn), direct(3, upper, yn)
        self.s0 = copy(4, source, target.at[me], sib)
        self.fy, self.fx = pass_on(5, xn, upper, yn), pass_on(6, yn, lower, xn)
        self.s1, self.s2 = pass_on(7, xn, upper, sib), pass_on(8, yn, lower, sib)
        self.s3, self.s4 = pass_on(9, xn, lower, sib), pass_on(10, yn, upper, sib)
        self.s5, self.s6 = pass_on(11, diag, upper, sib), pass_on(12, diag, lower, sib)

    def start(self):
        for c in (self.xa, self.yb, self.xb, self.ya, self.s0):
            c.start()

    def forward_first(self):
        self.xa.wait_recv()
        self.yb.wait_recv()
        for c in (self.fy, self.fx, self.s1, self.s2):
            c.start()

    def forward_second(self):
        self.xb.wait_recv()
        self.ya.wait_recv()
        self.s3.start()
        self.s4.start()

    def forward_third(self):
        self.fy.wait_recv()
        self.fx.wait_recv()
        self.s5.start()
        self.s6.start()

    def from_sibling(self, chip):
        for c in {"own": (self.s0,), "x": (self.s1, self.s3), "y": (self.s2, self.s4), "diag": (self.s5, self.s6)}[chip]:
            c.wait_recv()

    def sent(self):
        for c in (self.xa, self.yb, self.xb, self.ya, self.s0, self.fy, self.fx):
            c.wait_send()
        for c in (self.s1, self.s2, self.s3, self.s4, self.s5, self.s6):
            c.wait_send()

    def arrive(self, step):
        @pl.when(step == 1)
        def _():
            self.from_sibling("own")

        @pl.when(step == 2)
        def _():
            self.forward_first()
            self.forward_second()
            self.from_sibling("x")

        @pl.when(step == 4)
        def _():
            self.from_sibling("y")

        @pl.when(step == 6)
        def _():
            self.forward_third()
            self.from_sibling("diag")


class LineGather:
    def __init__(self, item, source, block, send, recv, local):
        z = lax.axis_index("dp")
        self.z = z

        def copy(k, src, owner, to):
            return pltpu.make_async_remote_copy(
                src_ref=src,
                dst_ref=block(owner),
                send_sem=send.at[item, k],
                recv_sem=recv.at[item, owner],
                device_id={"dp": to},
                device_id_type=MESH,
            )

        self.sends = []
        for k, d in enumerate((2, -2, 1, -1)):
            to = z + d
            valid = (to >= 0) & (to < 4)
            self.sends.append((valid, copy(k, source, z, jnp.clip(to, 0, 3))))
        inner = (z == 1) | (z == 2)
        far = jnp.where(z == 1, 3, 0)
        self.stop = (inner, copy(4, block(far), far, jnp.where(z == 1, 0, 3)))
        others = [lax.rem(z + o, 4) for o in (1, 2, 3)]
        self.blocks = [copy(0, source, other, other) for other in others]
        self.own = pltpu.make_async_copy(source, block(z), local.at[item])

    def start(self):
        self.own.start()
        for valid, c in self.sends:

            @pl.when(valid)
            def _(c=c):
                c.start()

    def forward(self):
        inner, c = self.stop

        @pl.when(inner)
        def _():
            self.blocks[1].wait_recv()
            c.start()

    def wait(self):
        inner, unused = self.stop
        self.blocks[0].wait_recv()
        self.blocks[2].wait_recv()

        @pl.when(jnp.logical_not(inner))
        def _():
            self.blocks[1].wait_recv()

        self.own.wait()

    def sent(self):
        for valid, c in (*self.sends, self.stop):

            @pl.when(valid)
            def _(c=c):
                c.wait_send()


def nearest_first(step):
    me, sib, xn, yn = partners()
    chip = jnp.where(step < 4, xn, jnp.where(step < 6, yn, xn + yn - me))
    later = chip + jnp.where(lax.rem(step, 2) == 0, sib - me, 0)
    return jnp.where(step == 0, me, jnp.where(step == 1, sib, later))


def farthest_first(step):
    me, sib, xn, yn = partners()
    chip = jnp.where(step < 4, xn, yn)
    chip = jnp.where(step < 2, xn + yn - me, jnp.where(step < 6, chip, me))
    return chip + jnp.where(lax.rem(step, 2) == 0, sib - me, 0)


def layer_kernel(
    x_ref,
    c_ref,
    wa_ref,
    wo_ref,
    wgu_ref,
    wd_ref,
    gain_ref,
    first_ref,
    x_all,
    c_all,
    h2_all,
    wo_all,
    h1_out,
    q_out,
    k_out,
    v_out,
    att_out,
    tok_out,
    mid_out,
    wa_out,
    gain_out,
    out_part,
    gh_ref,
    dgu_out,
    dd_out,
    wa,
    wgu,
    wd,
    gains,
    q_s,
    k_s,
    v_s,
    att_s,
    tok,
    mid,
    act_s,
    ggu_s,
    sum_gu,
    sum_d,
    x_buf,
    c_buf,
    o_buf,
    w_buf,
    beside,
    held,
    got,
    one,
    two,
    gsend,
    grecv,
    zsend,
    zrecv,
    zlocal,
    esend,
    erecv,
    rsend,
    rrecv,
    load_sem,
    out_sem,
    h1_sem,
    w_sem,
    done_sem,
    self_sem,
):
    me, sib, xn, yn = partners()
    z = lax.axis_index("dp")
    rows, width = x_ref.shape
    span = rows // 2
    wide, qk = v_s.shape[2], q_s.shape[2]
    share = CHUNKS[0] + CHUNKS[1] + CHUNKS[2]
    half = rows // 2
    upper, lower = pl.ds(0, half), pl.ds(half, half)

    barrier = pltpu.get_barrier_semaphore()
    for i in range(1, 8):
        pl.semaphore_signal(
            barrier, inc=1, device_id={"seq": lax.rem(me + i, 8)}, device_id_type=MESH
        )
    for i in range(1, 4):
        pl.semaphore_signal(
            barrier, inc=1, device_id={"dp": lax.rem(z + i, 4)}, device_id_type=MESH
        )
    pl.semaphore_wait(barrier, 10)

    tokens = PlaneGather(x_ref, x_all, gsend.at[0], grecv.at[0])
    out_w = PlaneGather(wo_all.at[me], wo_all, gsend.at[1], grecv.at[1])
    cots = PlaneGather(c_ref, c_all, gsend.at[2], grecv.at[2])
    hidden_in = PlaneGather(held.at[0], h2_all, gsend.at[3], grecv.at[3])

    def line(item, source, block):
        return LineGather(item, source, block, zsend, zrecv, zlocal)

    depth = wa_ref.shape[0]

    def rows_of(ref, count, columns=None):
        def block(owner):
            if columns is None:
                return ref.at[pl.ds(owner * count, count)]
            return ref.at[pl.ds(owner * count, count), columns]

        return block

    z_gain = line(
        0, gain_ref, lambda owner: gains.at[:, pl.ds(pl.multiple_of(owner * depth, 128), depth)]
    )
    z_attn = line(1, wa_ref, rows_of(wa, depth))
    z_out = line(
        2,
        wo_ref.at[:, pl.ds(pl.multiple_of(me * wide, 128), wide)],
        lambda owner: wo_all.at[me, pl.ds(owner * depth, depth)],
    )
    z_up, z_down = [], []
    column, before = 0, 0
    columns, hiddens = [], []
    for k, count in enumerate(CHUNKS):
        part = pl.ds(column, 8 * count)
        z_up.append(line(3 + k, wgu_ref.at[:, part], rows_of(wgu, depth, part)))
        z_down.append(
            line(
                6 + k,
                wd_ref.at[pl.ds(me * share + before, count)],
                lambda owner, base=4 * before, count=count: wd.at[
                    pl.ds(base + owner * count, count)
                ],
            )
        )
        columns.append(column)
        hiddens.append(4 * before)
        column += 8 * count
        before += count

    tokens.start()
    for g in (z_gain, z_attn, z_out):
        g.start()

    def loads(order, step, sources):
        slot = lax.rem(step, 2)
        owner = order(step)
        return [
            pltpu.make_async_copy(source.at[owner], buf.at[slot], load_sem.at[i, slot])
            for i, (source, buf) in enumerate(sources)
        ]

    first_load = pltpu.make_async_copy(x_ref, x_buf.at[0], load_sem.at[0, 0])
    first_load.start()
    tokens.forward_first()
    z_gain.forward()
    z_attn.forward()
    tokens.forward_second()
    z_gain.wait()
    z_attn.wait()
    for g in (z_up[0], z_down[0]):
        g.start()

    def h1_copies(step):
        slot = lax.rem(step, 2)
        owner = nearest_first(step)
        return [
            pltpu.make_async_copy(
                o_buf.at[slot, pl.ds(m * span, span)],
                h1_out.at[m, pl.ds(owner * span, span)],
                h1_sem.at[m, slot],
            )
            for m in range(2)
        ]

    def arrive_tokens(step):
        @pl.when(step == 1)
        def _():
            tokens.from_sibling("own")

        @pl.when(step == 2)
        def _():
            tokens.from_sibling("x")

        @pl.when(step == 4)
        def _():
            tokens.forward_third()
            tokens.from_sibling("y")

        @pl.when(step == 5)
        def _():
            z_out.forward()

        @pl.when(step == 6)
        def _():
            tokens.from_sibling("diag")

    token_source = [(x_all, x_buf)]

    def project(step, carry):
        slot = lax.rem(step, 2)
        owner = nearest_first(step)
        for c in loads(nearest_first, step, token_source):
            c.wait()

        @pl.when(step >= 2)
        def _():
            for c in h1_copies(step - 2):
                c.wait()

        x = x_buf[slot].astype(jnp.float32)
        gain = gains[0:1, :].astype(jnp.float32)
        h_one = (x * norm_scale(x) * gain).astype(LOW)
        o_buf[slot] = h_one
        for c in h1_copies(step):
            c.start()
        arrive_tokens(step + 1)

        @pl.when(step < 7)
        def _():
            for c in loads(nearest_first, step + 1, token_source):
                c.start()

        projected = dot(h_one, wa[...]).astype(LOW)
        for m in range(2):
            there = pl.ds(owner * span, span)
            mine = projected[m * span : (m + 1) * span]
            v_s[m, there, :] = mine[:, :wide]
            q_s[m, there, :] = mine[:, wide : wide + qk]
            k_s[m, there, :] = mine[:, wide + qk : wide + 2 * qk]
        return carry

    lax.fori_loop(0, 8, project, 0)
    for step in (6, 7):
        for c in h1_copies(step):
            c.wait()
    z_out.wait()
    out_w.start()
    for g in (z_up[1], z_down[1]):
        g.start()

    finals = [
        pltpu.make_async_copy(source, target, done_sem.at[i])
        for i, (source, target) in enumerate(
            (
                (q_s, q_out),
                (k_s, k_out),
                (v_s, v_out),
                (wa, wa_out),
                (gains, gain_out),
                (att_s, att_out),
                (tok, tok_out),
                (mid, mid_out),
            )
        )
    ]
    for c in finals[:5]:
        c.start()

    length = v_s.shape[1]
    block = 256

    def attend_stream(m, carry):
        for i in range(length // block):
            rows_i = slice(i * block, (i + 1) * block)
            seen = (i + 1) * block
            for head in range(wide // HEAD_V):
                lanes = slice(head * HEAD_V, (head + 1) * HEAD_V)
                unused, unused_mask, weight = weights_of(
                    q_s[m, rows_i, :], k_s[m, :seen, :], head, first_ref[m, rows_i, :], i * block
                )
                denom = jnp.sum(weight, axis=1, keepdims=True)
                numer = dot(weight.astype(LOW), v_s[m, :seen, lanes])
                att_s[m, rows_i, lanes] = (numer / denom).astype(LOW)
        return carry

    lax.fori_loop(0, 2, attend_stream, 0)
    out_w.forward_first()
    cots.start()
    finals[5].start()

    to_mine = pl.ds(pl.multiple_of(me * wide, 128), wide)
    swaps = []
    for i in range(1, 8):
        other = lax.rem(me + i, 8)
        for m in range(2):
            swaps.append(
                remote(
                    esend,
                    erecv,
                    2 * (i - 1) + m,
                    att_s.at[m, pl.ds(other * span, span)],
                    tok.at[pl.ds(m * span, span), to_mine],
                    other,
                )
            )
            swaps[-1].start()
    kept = [
        pltpu.make_async_copy(
            att_s.at[m, pl.ds(me * span, span)],
            tok.at[pl.ds(m * span, span), to_mine],
            self_sem.at[m],
        )
        for m in range(2)
    ]
    for c in kept:
        c.start()
    x_load = pltpu.make_async_copy(x_ref, x_buf.at[0], load_sem.at[0, 0])
    x_load.start()

    def w_load(step):
        slot = lax.rem(step, 2)
        return pltpu.make_async_copy(wo_all.at[nearest_first(step)], w_buf.at[slot], w_sem.at[slot])

    w_load(0).start()
    out_w.forward_second()
    z_up[0].forward()
    z_down[0].forward()
    for c in kept:
        c.wait()
    for c in swaps:
        c.wait_recv()
    finals[6].start()
    x_load.wait()

    def arrive_out(step):
        @pl.when(step == 1)
        def _():
            out_w.from_sibling("own")

        @pl.when(step == 2)
        def _():
            out_w.from_sibling("x")

        @pl.when(step == 4)
        def _():
            out_w.forward_third()
            out_w.from_sibling("y")

        @pl.when(step == 6)
        def _():
            out_w.from_sibling("diag")

    def project_out(step, carry):
        slot = lax.rem(step, 2)
        owner = nearest_first(step)
        w_load(step).wait()
        arrive_out(step + 1)

        @pl.when(step < 7)
        def _():
            w_load(step + 1).start()

        there = pl.ds(pl.multiple_of(owner * wide, 128), wide)
        mid[:, there] = dot(tok[...], w_buf[slot])
        return carry

    lax.fori_loop(0, 8, project_out, 0)
    mid_value = x_buf[0].astype(jnp.float32) + mid[...]
    mid[...] = mid_value
    held[0] = (mid_value * norm_scale(mid_value) * gains[1:2, :].astype(jnp.float32)).astype(LOW)
    finals[7].start()
    hidden_in.start()
    own_h2 = pltpu.make_async_copy(held.at[0], h2_all.at[me], self_sem.at[2])
    own_c = pltpu.make_async_copy(c_ref, c_all.at[me], self_sem.at[3])
    own_h2.start()
    own_c.start()
    cots.forward_first()
    cots.forward_second()
    for g in (z_up[2], z_down[2]):
        g.start()
    own_h2.wait()
    own_c.wait()
    z_up[0].wait()
    z_down[0].wait()

    sources = [(h2_all, x_buf), (c_all, c_buf)]

    def out_copy(order, step):
        slot = lax.rem(step, 2)
        return pltpu.make_async_copy(o_buf.at[slot], out_part.at[order(step)], out_sem.at[slot])

    def hidden_chunk(k, owner, h, c):
        count = 4 * CHUNKS[k]
        pair = pl.ds(columns[k], 2 * count)
        here = pl.ds(hiddens[k], count)
        both = dot(h, wgu[:, pair])
        gate, up = both[:, :count], both[:, count:]
        g_act = contract(c, wd[here, :], 1, 1)
        sigmoid = jax.nn.sigmoid(gate)
        silu = gate * sigmoid
        act = (silu * up).astype(LOW)
        g_gate = (g_act * up * sigmoid * (1.0 + gate * (1.0 - sigmoid))).astype(LOW)
        g_up = (g_act * silu).astype(LOW)
        there = pl.ds(owner * rows, rows)
        act_s[there, here] = act
        g_both = jnp.concatenate([g_gate, g_up], axis=1)
        ggu_s[there, pair] = g_both
        return act, g_both

    def add_grads(k, step, h, c, act, g_both):
        count = 4 * CHUNKS[k]

        @pl.when(step == 0)
        def _():
            sum_gu[...] = jnp.zeros_like(sum_gu)
            sum_d[...] = jnp.zeros_like(sum_d)

        sum_gu[:, : 2 * count] += contract(h, g_both, 0, 0)
        sum_d[:count, :] += contract(act, c, 0, 0)

    def emit(k):
        count = 4 * CHUNKS[k]
        pending = [None, None]
        for i in range(width // rows):
            slot = i % 2
            if pending[slot] is not None:
                pending[slot].wait()
            o_buf[slot, :, : 2 * count] = sum_gu[i * rows : (i + 1) * rows, : 2 * count].astype(LOW)
            pending[slot] = pltpu.make_async_copy(
                o_buf.at[slot, :, pl.ds(0, 2 * count)],
                dgu_out.at[pl.ds(i * rows, rows), pl.ds(columns[k], 2 * count)],
                out_sem.at[slot],
            )
            pending[slot].start()
        for c in pending:
            c.wait()
        o_buf[0, :count, :] = sum_d[:count, :].astype(LOW)
        downs = []
        for owner in range(4):
            downs.append(
                pltpu.make_async_copy(
                    o_buf.at[0, pl.ds(owner * CHUNKS[k], CHUNKS[k])],
                    dd_out.at[pl.ds(owner * share + hiddens[k] // 4, CHUNKS[k])],
                    h1_sem.at[owner // 2, owner % 2],
                )
            )
            downs[-1].start()
        for c in downs:
            c.wait()

    def forward_pass(k, arrive, step, carry):
        slot = lax.rem(step, 2)
        for c in loads(nearest_first, step, sources):
            c.wait()
        h, c = x_buf[slot], c_buf[slot]
        act, g_both = hidden_chunk(k, nearest_first(step), h, c)
        if arrive is not None:
            arrive(step + 1)

        @pl.when(step < 7)
        def _():
            for c in loads(nearest_first, step + 1, sources):
                c.start()

        add_grads(k, step, h, c, act, g_both)
        return carry

    def arrive_both(step):
        hidden_in.arrive(step)

        @pl.when(step == 1)
        def _():
            cots.from_sibling("own")

        @pl.when(step == 2)
        def _():
            cots.from_sibling("x")

        @pl.when(step == 4)
        def _():
            cots.forward_third()
            cots.from_sibling("y")

        @pl.when(step == 5)
        def _():
            z_up[1].forward()
            z_down[1].forward()

        @pl.when(step == 6)
        def _():
            cots.from_sibling("diag")

    for c in loads(nearest_first, 0, sources):
        c.start()
    lax.fori_loop(0, 8, functools.partial(forward_pass, 0, arrive_both), 0)
    hidden_in.sent()
    z_up[1].wait()
    z_down[1].wait()
    for c in loads(nearest_first, 0, sources):
        c.start()
    emit(0)

    def arrive_last(step):
        @pl.when(step == 4)
        def _():
            z_up[2].forward()
            z_down[2].forward()

    lax.fori_loop(0, 8, functools.partial(forward_pass, 1, arrive_last), 0)
    z_up[2].wait()
    z_down[2].wait()
    for c in loads(farthest_first, 0, sources):
        c.start()
    emit(1)

    copy = functools.partial(remote, rsend, rrecv)
    b_diag = copy(0, beside.at[0], got.at[2], sib)
    b_x = copy(1, beside.at[1], got.at[1], sib)
    b_y = copy(2, beside.at[0], got.at[3], sib)
    b_own = copy(3, beside.at[1], got.at[0], sib)
    x0 = copy(4, held.at[2, upper], one.at[0], xn)
    y0 = copy(5, held.at[2, lower], one.at[1], yn)
    x1 = copy(6, held.at[1, upper], one.at[2], xn)
    y1 = copy(7, held.at[3, lower], one.at[3], yn)
    y2 = copy(8, held.at[3, upper], two.at[0], yn)
    x2 = copy(9, held.at[1, lower], two.at[1], xn)

    def last_pass(step, carry):
        slot = lax.rem(step, 2)
        owner = farthest_first(step)
        there = pl.ds(owner * rows, rows)
        for c in loads(farthest_first, step, sources):
            c.wait()
        h, c = x_buf[slot], c_buf[slot]
        act, g_both = hidden_chunk(2, owner, h, c)
        part = contract(ggu_s[there, :], wgu[...], 1, 1).astype(LOW)

        for k, place, sent in ((0, 0, b_diag), (2, 1, b_x), (4, 0, b_y), (6, 1, b_own)):

            @pl.when(step == k)
            def _(k=k, place=place, sent=sent):
                if k == 4:
                    b_diag.wait_send()
                if k == 6:
                    b_x.wait_send()
                beside[place] = part
                sent.start()

        for k, place, arrived in ((1, 2, b_diag), (3, 1, b_x), (5, 3, b_y), (7, 0, b_own)):

            @pl.when(step == k)
            def _(k=k, place=place, arrived=arrived):
                arrived.wait_recv()
                held[place] = part + got[place]
                if k == 1:
                    x0.start()
                    y0.start()
                if k == 3:
                    x1.start()
                if k == 5:
                    y1.start()
                    y0.wait_recv()
                    held[1, half:] = held[1, half:] + one[1]
                    x2.start()
                    x0.wait_recv()
                    held[3, :half] = held[3, :half] + one[0]
                    y2.start()

        @pl.when(step >= 2)
        def _():
            out_copy(farthest_first, step - 2).wait()

        o_buf[slot] = dot(act_s[there, :], wd[...]).astype(LOW)
        out_copy(farthest_first, step).start()

        @pl.when(step < 7)
        def _():
            for c in loads(farthest_first, step + 1, sources):
                c.start()

        add_grads(2, step, h, c, act, g_both)
        return carry

    lax.fori_loop(0, 8, last_pass, 0)
    out_copy(farthest_first, 6).wait()
    out_copy(farthest_first, 7).wait()
    emit(2)
    f32 = jnp.float32
    x1.wait_recv()
    y2.wait_recv()
    gh_ref[:half] = held[0, :half].astype(f32) + one[2].astype(f32) + two[0].astype(f32)
    y1.wait_recv()
    x2.wait_recv()
    gh_ref[half:] = held[0, half:].astype(f32) + one[3].astype(f32) + two[1].astype(f32)
    for c in finals:
        c.wait()
    for c in (b_y, b_own, x0, y0, x1, y1, y2, x2, *swaps):
        c.wait_send()
    for g in (tokens, out_w, cots, z_gain, z_attn, z_out, *z_up, *z_down):
        g.sent()


def layer_front(tokens, cot, attn_slice, w_out, ffn_slice, w_down, gain_rows, first, wide, qk):
    rows, width = tokens.shape
    streams, length, unused = first.shape
    hidden = 4 * sum(CHUNKS)
    largest = 4 * max(CHUNKS)
    shape = jax.ShapeDtypeStruct
    f32 = jnp.float32
    anywhere = pl.BlockSpec(memory_space=pl.ANY)
    in_vmem = pl.BlockSpec(memory_space=pltpu.VMEM)
    plane = shape((8, rows, width), LOW)
    narrow = shape((streams, length, qk), LOW)
    broad = shape((streams, length, wide), LOW)
    attn_shape = (width, attn_slice.shape[1])
    out_shape = [
        plane,
        plane,
        plane,
        shape((8, width, width // 8), LOW),
        shape((streams, length, width), LOW),
        narrow,
        narrow,
        broad,
        broad,
        shape((rows, width), LOW),
        shape((rows, width), f32),
        shape(attn_shape, LOW),
        shape((gain_rows.shape[0], width), LOW),
        plane,
        shape((rows, width), f32),
        shape((width, 2 * hidden), LOW),
        shape((hidden, width), LOW),
    ]
    dma = pltpu.SemaphoreType.DMA
    vmem = pltpu.VMEM
    return pl.pallas_call(
        layer_kernel,
        out_shape=out_shape,
        in_specs=[anywhere] * 7 + [in_vmem],
        out_specs=[anywhere] * 14 + [in_vmem] + [anywhere] * 2,
        scratch_shapes=[
            vmem(attn_shape, LOW),
            vmem((width, 2 * hidden), LOW),
            vmem((hidden, width), LOW),
            vmem((gain_rows.shape[0], width), LOW),
            vmem(narrow.shape, LOW),
            vmem(narrow.shape, LOW),
            vmem(broad.shape, LOW),
            vmem(broad.shape, LOW),
            vmem((rows, width), LOW),
            vmem((rows, width), f32),
            vmem((8 * rows, hidden), LOW),
            vmem((8 * rows, 2 * hidden), LOW),
            vmem((width, 2 * largest), f32),
            vmem((largest, width), f32),
            vmem((2, rows, width), LOW),
            vmem((2, rows, width), LOW),
            vmem((2, rows, width), LOW),
            vmem((2, width, width // 8), LOW),
            vmem((2, rows, width), LOW),
            vmem((4, rows, width), LOW),
            vmem((4, rows, width), LOW),
            vmem((4, rows // 2, width), LOW),
            vmem((2, rows // 2, width), LOW),
            dma((4, 13)),
            dma((4, 13)),
            dma((9, 5)),
            dma((9, 4)),
            dma((9,)),
            dma((14,)),
            dma((14,)),
            dma((10,)),
            dma((10,)),
            dma((2, 2)),
            dma((2,)),
            dma((2, 2)),
            dma((2,)),
            dma((8,)),
            dma((4,)),
        ],
        compiler_params=pltpu.CompilerParams(
            collective_id=21, has_side_effects=True, vmem_limit_bytes=63 * MIB
        ),
        cost_estimate=pl.CostEstimate(
            flops=6 * 3 * 8 * rows * width * hidden,
            bytes_accessed=400 * rows * width,
            transcendentals=0,
        ),
        name="layer",
    )(tokens, cot, attn_slice, w_out, ffn_slice, w_down, gain_rows, first)


class PlaneScatter:
    def __init__(self, beside, held, got, one, two, send, recv):
        me, sib, xn, yn = partners()
        half = got.shape[1] // 2
        self.half = half
        upper, lower = pl.ds(0, half), pl.ds(half, half)
        copy = functools.partial(remote, send, recv)
        self.held, self.got, self.one, self.two = held, got, one, two
        self.pairs = [copy(i, beside(i), got.at[i], sib) for i in range(4)]
        self.x0 = copy(4, held(2).at[upper], one.at[0], xn)
        self.y0 = copy(5, held(2).at[lower], one.at[1], yn)
        self.x1 = copy(6, held(1).at[upper], one.at[2], xn)
        self.y1 = copy(7, held(3).at[lower], one.at[3], yn)
        self.y2 = copy(8, held(3).at[upper], two.at[0], yn)
        self.x2 = copy(9, held(1).at[lower], two.at[1], xn)

    def start_pair(self, i):
        self.pairs[i].start()

    def start_pairs(self):
        for i in (2, 1, 3, 0):
            self.start_pair(i)

    def add_pair(self, i):
        self.pairs[i].wait_recv()
        block = self.held(i)
        block[...] = block[...] + self.got[i]
        for c in {0: (), 1: (self.x1,), 2: (self.x0, self.y0), 3: (self.y1,)}[i]:
            c.start()

    def add_pairs(self):
        for i in (2, 1, 3, 0):
            self.add_pair(i)

    def second(self):
        half = self.half
        self.y0.wait_recv()
        block = self.held(1)
        block[half:, :] = block[half:, :] + self.one[1]
        self.x2.start()
        self.x0.wait_recv()
        block = self.held(3)
        block[:half, :] = block[:half, :] + self.one[0]
        self.y2.start()

    def upper_sum(self):
        f32 = jnp.float32
        self.x1.wait_recv()
        self.y2.wait_recv()
        own = self.held(0)[: self.half, :].astype(f32)
        return own + self.one[2].astype(f32) + self.two[0].astype(f32)

    def lower_sum(self):
        f32 = jnp.float32
        self.y1.wait_recv()
        self.x2.wait_recv()
        own = self.held(0)[self.half :, :].astype(f32)
        return own + self.one[3].astype(f32) + self.two[1].astype(f32)

    def sent(self):
        for c in (*self.pairs, self.x0, self.y0, self.x1, self.y1, self.y2, self.x2):
            c.wait_send()


def chips():
    me, unused, xn, yn = partners()
    return me, xn, xn + yn - me, yn


def turn_kernel(
    gh_ref,
    mid_ref,
    c_ref,
    gain_ref,
    wo_all,
    part_ref,
    tok_ref,
    q_ref,
    k_ref,
    v_ref,
    att_ref,
    first_ref,
    output_ref,
    g_mid_out,
    g_out,
    go_out,
    gain_out,
    g_mid,
    work,
    g_low,
    g_att,
    g_heads,
    g_s,
    w_buf,
    go_part,
    held_o,
    got_g,
    one_g,
    two_g,
    got_o,
    one_o,
    two_o,
    gk_sum,
    gv_sum,
    esend,
    erecv,
    ssend,
    srecv,
    load_sem,
    w_sem,
    self_sem,
    done_sem,
):
    me, sib, xn, yn = partners()
    flip = sib - me
    rows, width = g_low.shape
    span = rows // 2
    wide, qk = v_ref.shape[2], q_ref.shape[2]
    half = rows // 2
    greet([lax.rem(me + i, 8) for i in range(1, 8)])
    owners = chips()

    loads = [
        pltpu.make_async_copy(source, target, load_sem.at[i])
        for i, (source, target) in enumerate(
            ((gh_ref, g_mid), (mid_ref, work), (c_ref, g_low))
        )
    ]
    held_loads = [
        pltpu.make_async_copy(part_ref.at[owners[i]], held_o.at[i], load_sem.at[3 + i])
        for i in range(4)
    ]

    def w_load(step):
        slot = lax.rem(step, 2)
        return pltpu.make_async_copy(wo_all.at[step], w_buf.at[slot], w_sem.at[slot])

    for c in loads:
        c.start()
    w_load(0).start()
    outs = PlaneScatter(
        lambda i: part_ref.at[owners[i] + flip],
        lambda i: held_o.at[i],
        got_o,
        one_o,
        two_o,
        ssend.at[0],
        srecv.at[0],
    )
    weights = PlaneScatter(
        lambda i: go_part.at[owners[i] + flip],
        lambda i: go_part.at[owners[i]],
        got_g,
        one_g,
        two_g,
        ssend.at[1],
        srecv.at[1],
    )
    outs.start_pairs()
    for c in held_loads:
        c.start()
    for c in loads:
        c.wait()

    f32 = jnp.float32
    mid = work[...]
    inverse = norm_scale(mid)
    normed = mid * inverse
    grad = g_mid[...]
    gain_out[...] = jnp.broadcast_to(
        jnp.sum(grad * normed, axis=0, keepdims=True), gain_out.shape
    )
    gain = gain_ref[1:2, :].astype(f32)
    grad_mid = g_low[...].astype(f32) + norm_backward(grad, normed, inverse, gain)
    g_mid[...] = grad_mid
    g_low[...] = grad_mid.astype(LOW)
    done = [pltpu.make_async_copy(g_mid, g_mid_out, done_sem.at[0])]
    done[0].start()

    def back_out(step, carry):
        slot = lax.rem(step, 2)
        w_load(step).wait()

        @pl.when(step < 7)
        def _():
            w_load(step + 1).start()

        there = pl.ds(pl.multiple_of(step * wide, 128), wide)
        term = contract(g_low[:, there], w_buf[slot], 1, 1)

        @pl.when(step == 0)
        def _():
            work[...] = term

        @pl.when(step > 0)
        def _():
            work[...] += term

        return carry

    lax.fori_loop(0, 8, back_out, 0)
    g_att[...] = work[...].astype(LOW)
    mid_load = pltpu.make_async_copy(mid_ref, work, load_sem.at[1])
    mid_load.start()
    swaps = []
    here = pl.ds(me * span, span)
    for i in range(1, 8):
        other = lax.rem(me + i, 8)
        lanes = pl.ds(pl.multiple_of(other * wide, 128), wide)
        for m in range(2):
            swaps.append(
                remote(
                    esend,
                    erecv,
                    2 * (i - 1) + m,
                    g_att.at[pl.ds(m * span, span), lanes],
                    g_heads.at[m, here],
                    other,
                )
            )
            swaps[-1].start()
    kept = [
        pltpu.make_async_copy(
            g_att.at[pl.ds(m * span, span), pl.ds(pl.multiple_of(me * wide, 128), wide)],
            g_heads.at[m, here],
            self_sem.at[m],
        )
        for m in range(2)
    ]
    for c in kept:
        c.start()

    own = width // 32
    for z in range(4):
        lanes = slice(z * 8 * own, (z + 1) * 8 * own)
        block = contract(tok_ref[:, lanes], g_low[...], 0, 0).astype(LOW)
        for s in range(8):
            go_part[s, z * own : (z + 1) * own, :] = block[s * own : (s + 1) * own]
    weights.start_pairs()
    for c in kept:
        c.wait()
    for c in swaps:
        c.wait_recv()
    weights.add_pairs()

    length = v_ref.shape[1]
    block = 256

    def back_stream(m, carry):
        gk_sum[...] = jnp.zeros_like(gk_sum)
        gv_sum[...] = jnp.zeros_like(gv_sum)
        for i in range(length // block):
            rows_i = slice(i * block, (i + 1) * block)
            seen = (i + 1) * block
            query, key = q_ref[m, rows_i, :], k_ref[m, :seen, :]
            g_query = jnp.zeros(query.shape, f32)
            for head in range(wide // HEAD_V):
                lanes = slice(head * HEAD_V, (head + 1) * HEAD_V)
                scores, mask, weight = weights_of(
                    query, key, head, first_ref[m, rows_i, :], i * block
                )
                denom = jnp.sum(weight, axis=1, keepdims=True)
                a = (g_heads[m, rows_i, lanes].astype(f32) / denom).astype(LOW)
                b = -jnp.sum(
                    a.astype(f32) * att_ref[m, rows_i, lanes].astype(f32), axis=1, keepdims=True
                )
                g_weight = contract(a, v_ref[m, :seen, lanes], 1, 1) + b
                slope = 1.0 / math.sqrt(QK_DIM) + scores * (1.0 / QK_DIM)
                g_scores = jnp.where(mask, g_weight * slope, 0.0).astype(LOW)
                g_query += head_lanes(dot(g_scores, key), head)
                gk_sum[:seen, :] += contract(g_scores, head_lanes(query, head), 0, 0)
                gv_sum[:seen, lanes] += contract(weight.astype(LOW), a, 0, 0)
            g_s[m, rows_i, wide : wide + qk] = g_query.astype(LOW)
        g_s[m, :, :wide] = gv_sum[...].astype(LOW)
        g_s[m, :, wide + qk : wide + 2 * qk] = gk_sum[...].astype(LOW)
        g_s[m, :, wide + 2 * qk :] = jnp.zeros((length, g_s.shape[2] - wide - 2 * qk), LOW)

        @pl.when(m == 0)
        def _():
            for c in held_loads:
                c.wait()
            outs.add_pairs()

        return carry

    lax.fori_loop(0, 2, back_stream, 0)
    weights.second()
    done.append(pltpu.make_async_copy(g_s, g_out, done_sem.at[1]))
    done[1].start()
    mid_load.wait()
    outs.second()
    go_out[:half] = weights.upper_sum().astype(LOW)
    go_out[half:] = weights.lower_sum().astype(LOW)
    output_ref[:half] = (work[:half] + outs.upper_sum()).astype(LOW)
    output_ref[half:] = (work[half:] + outs.lower_sum()).astype(LOW)
    for c in done:
        c.wait()
    for c in swaps:
        c.wait_send()
    weights.sent()
    outs.sent()


def layer_turn(gh, mid, cot, gains, wo_all, part, tok, query, key, value, att, first, columns):
    rows, width = mid.shape
    streams, length, wide = value.shape
    qk = query.shape[2]
    shape = jax.ShapeDtypeStruct
    f32 = jnp.float32
    anywhere = pl.BlockSpec(memory_space=pl.ANY)
    in_vmem = pl.BlockSpec(memory_space=pltpu.VMEM)
    dma = pltpu.SemaphoreType.DMA
    vmem = pltpu.VMEM
    arriving = [
        vmem((4, rows, width), LOW),
        vmem((4, rows // 2, width), LOW),
        vmem((2, rows // 2, width), LOW),
    ]
    return pl.pallas_call(
        turn_kernel,
        out_shape=[
            shape((rows, width), LOW),
            shape((rows, width), f32),
            shape((streams, length, columns), LOW),
            shape((rows, width), LOW),
            shape((8, width), f32),
        ],
        in_specs=[anywhere] * 3 + [in_vmem] + [anywhere] * 2 + [in_vmem] * 6,
        out_specs=[in_vmem, anywhere, anywhere, in_vmem, in_vmem],
        scratch_shapes=[
            vmem((rows, width), f32),
            vmem((rows, width), f32),
            vmem((rows, width), LOW),
            vmem((rows, width), LOW),
            vmem((streams, length, wide), LOW),
            vmem((streams, length, columns), LOW),
            vmem((2, width, wide), LOW),
            vmem((8, rows, width), LOW),
            vmem((4, rows, width), LOW),
            *arriving,
            *arriving,
            vmem((length, qk), f32),
            vmem((length, wide), f32),
            dma((14,)),
            dma((14,)),
            dma((2, 10)),
            dma((2, 10)),
            dma((7,)),
            dma((2,)),
            dma((2,)),
            dma((2,)),
        ],
        compiler_params=pltpu.CompilerParams(
            collective_id=22, has_side_effects=True, vmem_limit_bytes=63 * MIB
        ),
        cost_estimate=moved(16 * rows * width),
        name="turn",
    )(gh, mid, cot, gains, wo_all, part, tok, query, key, value, att, first)


def close_kernel(
    g_ref,
    wa_ref,
    h1_ref,
    g_mid_ref,
    x_ref,
    gain_ref,
    sum_ref,
    grad_ref,
    attn_ref,
    beside,
    held,
    got,
    one,
    two,
    h_buf,
    sums,
    ssend,
    srecv,
    h_sem,
):
    me, sib, xn, yn = partners()
    rows, width = x_ref.shape
    span = rows // 2
    half = rows // 2
    f32 = jnp.float32
    greet((sib, xn, yn))
    scatter = PlaneScatter(
        lambda i: beside.at[i], lambda i: held.at[i], got, one, two, ssend, srecv
    )
    streams, length, columns = g_ref.shape
    pieces = length // rows

    def h_load(step):
        slot = lax.rem(step, 2)
        return pltpu.make_async_copy(
            h1_ref.at[step // pieces, pl.ds(lax.rem(step, pieces) * rows, rows)],
            h_buf.at[slot],
            h_sem.at[slot],
        )

    h_load(0).start()

    def part_of(owner):
        there = pl.ds(pl.multiple_of(owner * span, span), span)
        grads = jnp.concatenate([g_ref[0, there, :], g_ref[1, there, :]], axis=0)
        return contract(grads, wa_ref[...], 1, 1).astype(LOW)

    owners = chips()
    for i in (2, 1, 3, 0):
        beside[i] = part_of(owners[i] + sib - me)
        scatter.start_pair(i)
        held[i] = part_of(owners[i])
        scatter.add_pair(i)

    def add_grads(step, carry):
        slot = lax.rem(step, 2)
        h_load(step).wait()

        @pl.when(step < streams * pieces - 1)
        def _():
            h_load(step + 1).start()

        there = pl.ds(pl.multiple_of(lax.rem(step, pieces) * rows, rows), rows)
        term = contract(h_buf[slot], g_ref[step // pieces, there, :], 0, 0)

        @pl.when(step == 0)
        def _():
            sums[...] = term

        @pl.when(step > 0)
        def _():
            sums[...] += term

        return carry

    lax.fori_loop(0, streams * pieces, add_grads, 0)
    scatter.second()

    x = x_ref[...].astype(f32)
    inverse = norm_scale(x)
    normed = x * inverse
    gain = gain_ref[0:1, :].astype(f32)

    def finish(start, g_h):
        part = slice(start, start + half)
        grad_ref[part] = g_mid_ref[part] + norm_backward(g_h, normed[part], inverse[part], gain)
        return jnp.sum(g_h * normed[part], axis=0, keepdims=True)

    gain_sum = finish(0, scatter.upper_sum()) + finish(half, scatter.lower_sum())

    both = jnp.concatenate(
        [gain_sum, sum_ref[0:1, :], jnp.zeros((14, width), f32)], axis=0
    ).astype(LOW)
    at = columns - 64
    entry = lax.broadcasted_iota(jnp.int32, (16, 128), 0)
    lane = lax.broadcasted_iota(jnp.int32, (16, 128), 1)
    pick = jnp.where(lane == entry + (at - (columns - 128)), 1.0, 0.0).astype(LOW)
    attn_ref[:, : columns - 128] = sums[:, : columns - 128].astype(LOW)
    tail = sums[:, columns - 128 :] + contract(both, pick, 0, 0)
    attn_ref[:, columns - 128 :] = tail.astype(LOW)
    scatter.sent()


def layer_close(g_all, wa, h1_all, g_mid, tokens, gains, gain_sum):
    rows, width = tokens.shape
    shape = jax.ShapeDtypeStruct
    anywhere = pl.BlockSpec(memory_space=pl.ANY)
    in_vmem = pl.BlockSpec(memory_space=pltpu.VMEM)
    dma = pltpu.SemaphoreType.DMA
    vmem = pltpu.VMEM
    return pl.pallas_call(
        close_kernel,
        out_shape=[shape((rows, width), jnp.float32), shape(wa.shape, LOW)],
        in_specs=[in_vmem, in_vmem, anywhere] + [in_vmem] * 4,
        out_specs=[in_vmem, in_vmem],
        scratch_shapes=[
            vmem((4, rows, width), LOW),
            vmem((4, rows, width), LOW),
            vmem((4, rows, width), LOW),
            vmem((4, rows // 2, width), LOW),
            vmem((2, rows // 2, width), LOW),
            vmem((2, rows, width), LOW),
            vmem(wa.shape, jnp.float32),
            dma((10,)),
            dma((10,)),
            dma((2,)),
        ],
        compiler_params=pltpu.CompilerParams(
            collective_id=23, has_side_effects=True, vmem_limit_bytes=56 * MIB
        ),
        cost_estimate=moved(16 * rows * width),
        name="close",
    )(g_all, wa, h1_all, g_mid, tokens, gains, gain_sum)


def ffn_lax(h_two, cot_all, gate_full, up_full, down_full):
    pieces, rows, width = cot_all.shape
    h_two_all = gather_plane(h_two, 5).reshape(-1, width)
    cot_all = cot_all.reshape(-1, width)
    gate = dot(h_two_all, gate_full)
    up = dot(h_two_all, up_full)
    g_act = contract(cot_all, down_full, 1, 1)
    sigmoid = jax.nn.sigmoid(gate)
    silu = gate * sigmoid
    act = (silu * up).astype(LOW)
    g_gate = (g_act * up * sigmoid * (1.0 + gate * (1.0 - sigmoid))).astype(LOW)
    g_up = (g_act * silu).astype(LOW)
    part = (contract(g_gate, gate_full, 1, 1) + contract(g_up, up_full, 1, 1)).astype(LOW)
    return (
        dot(act, down_full).astype(LOW).reshape(pieces, rows, width),
        scatter_plane(part.reshape(pieces, rows, width), 7),
        contract(h_two_all, g_gate, 0, 0).astype(LOW),
        contract(h_two_all, g_up, 0, 0).astype(LOW),
        contract(act, cot_all, 0, 0).astype(LOW),
    )


def norm_scale(rows):
    return lax.rsqrt(jnp.mean(rows * rows, axis=-1, keepdims=True) + epsilon)


def norm_backward(grad, normed, inverse, gain):
    scaled = grad * gain
    return inverse * (scaled - normed * jnp.mean(scaled * normed, axis=-1, keepdims=True))


def local(
    tokens,
    doc_lengths,
    w_query,
    w_key,
    w_value,
    w_out,
    w_gate,
    w_up,
    w_down,
    gain_attn,
    gain_mlp,
    cotangent,
):
    micro, span = tokens.shape[1:3]
    pieces, groups = lax.axis_size("seq"), lax.axis_size("dp")
    place = lax.axis_index("seq")
    length = pieces * span
    heads = max(1, HEADS // pieces)
    sharers = max(1, pieces // HEADS)
    streams = micro // sharers
    first_head = place // sharers * heads
    first_stream = place % sharers * streams
    qk, wide = heads * QK_DIM, heads * HEAD_V
    hidden = FF // pieces

    out_width = D // pieces
    rows_dp = w_gate.shape[0]
    share = hidden // groups
    block = FF // groups
    mine = micro * span
    fused = pieces == 8 and groups == 4 and micro == 2 and span == 128
    chunks = CHUNKS if fused else (share,)

    def hidden_columns(w):
        parts = [
            lax.dynamic_slice_in_dim(w, z * block + place * share, share, 1) for z in range(groups)
        ]
        edges = [sum(chunks[:k]) for k in range(len(chunks) + 1)]
        return [
            [part[:, edges[k] : edges[k + 1]] for part in parts] for k in range(len(chunks))
        ]

    gate_parts, up_parts = hidden_columns(w_gate), hidden_columns(w_up)
    ffn_slice = jnp.concatenate(
        [part for k in range(len(chunks)) for part in gate_parts[k] + up_parts[k]], axis=1
    )
    attn_parts = [
        lax.dynamic_slice_in_dim(w_value, first_head * HEAD_V, wide, 1),
        lax.dynamic_slice_in_dim(w_query, first_head * QK_DIM, qk, 1),
        lax.dynamic_slice_in_dim(w_key, first_head * QK_DIM, qk, 1),
    ]

    lengths = lax.dynamic_slice_in_dim(doc_lengths[0], first_stream, streams, 0)
    starts = jnp.cumsum(lengths, axis=1) - lengths
    position = jnp.arange(length, dtype=jnp.int32)
    begun = starts[:, None, :] <= position[None, :, None]
    first = jnp.max(jnp.where(begun, starts[:, None, :], 0), axis=2)[..., None]

    x_own = tokens[0].reshape(mine, D)
    flat = x_own.astype(jnp.float32)
    cot = cotangent[0].reshape(mine, D)

    def to_tokens(by_head):
        sent = by_head.reshape(streams, pieces, span, wide).transpose(1, 0, 2, 3)
        got = exchange_plane(sent, 3).reshape(pieces // sharers, micro, span, wide)
        return got.transpose(1, 2, 0, 3).reshape(mine, HEADS * HEAD_V)

    def to_heads(by_token):
        sent = by_token.reshape(micro, span, pieces // sharers, wide).transpose(2, 0, 1, 3)
        got = exchange_plane(sent.reshape(pieces, streams, span, wide), 4)
        return got.transpose(1, 0, 2, 3).reshape(streams, length, wide)

    if fused:
        attn_slice = jnp.concatenate(
            attn_parts + [jnp.zeros((rows_dp, 128 - 2 * qk), LOW)], axis=1
        )
        gain_rows = jnp.concatenate(
            [gain_attn[None], gain_mlp[None], jnp.zeros((14, rows_dp), LOW)], axis=0
        )
        front = layer_front(
            x_own, cot, attn_slice, w_out, ffn_slice, w_down, gain_rows, first, wide, qk
        )
        out_full, h_all, query, key, value, att_heads, attended, mid = front[3:11]
        attn_full, gain_rows_all, out_part, g_h_two, d_ffn, d_down = front[11:]
    else:

        def gather_dp(w):
            return lax.all_gather(w, "dp", axis=0, tiled=True)

        attn_got = gather_dp(
            jnp.concatenate(
                attn_parts
                + [
                    lax.dynamic_slice_in_dim(w_out, place * out_width, out_width, 1),
                    gain_attn[:, None],
                    gain_mlp[:, None],
                ],
                axis=1,
            )
        )
        ffn_full = gather_dp(ffn_slice)
        down_full = gather_dp(lax.dynamic_slice_in_dim(w_down, place * share, share, 0))
        value_full = attn_got[:, :wide]
        query_full = attn_got[:, wide : wide + qk]
        key_full = attn_got[:, wide + qk : wide + 2 * qk]
        out_full = gather_plane(attn_got[:, wide + 2 * qk : wide + 2 * qk + out_width], 2)
        gains = attn_got[:, wide + 2 * qk + out_width :].astype(jnp.float32)
        gain_one, gain_two = gains[:, 0], gains[:, 1]
        x_all = gather_plane(x_own, 1).reshape(pieces, micro, span, D).transpose(1, 0, 2, 3)
        x_all = lax.dynamic_slice_in_dim(x_all, first_stream, streams, 0).astype(jnp.float32)
        h_flat = (x_all * norm_scale(x_all) * gain_one).astype(LOW).reshape(streams * length, D)
        value = dot(h_flat, value_full).astype(LOW).reshape(streams, length, wide)
        query = dot(h_flat, query_full).astype(LOW).reshape(streams, length, qk)
        key = dot(h_flat, key_full).astype(LOW).reshape(streams, length, qk)
        att_heads = attend(query, key, value, first, heads)
        attended = to_tokens(att_heads)
        mid = flat + jnp.einsum(
            "tk,skn->tsn", attended, out_full, preferred_element_type=jnp.float32
        ).reshape(mine, D)
        h_two = (mid * norm_scale(mid) * gain_two).astype(LOW)
        out_part, g_h_two, d_gate, d_up, d_down = ffn_lax(
            h_two, gather_plane(cot, 6), ffn_full[:, :hidden], ffn_full[:, hidden:], down_full
        )
        d_ffn = jnp.concatenate([d_gate, d_up], axis=1)

    def scatter_dp(part):
        return lax.psum_scatter(part, "dp", scatter_dimension=0, tiled=True)

    own = rows_dp // pieces
    sum_ffn, sum_down = scatter_dp(d_ffn), scatter_dp(d_down)

    if fused:
        output, g_mid, g_all, grad_out, gain_sum = layer_turn(
            g_h_two, mid, cot, gain_rows_all, out_full, out_part, attended, query, key, value,
            att_heads, first, attn_full.shape[1],
        )
        input_grad, grad_attn = layer_close(
            g_all, attn_full, h_all, g_mid, x_own, gain_rows_all, gain_sum
        )
    else:
        inverse_two = norm_scale(mid)
        plain_two = mid * inverse_two
        output = (mid + scatter_plane(out_part, 8)).astype(LOW)
        g_mid = cot.astype(jnp.float32) + norm_backward(g_h_two, plain_two, inverse_two, gain_two)
        g_mid_low = g_mid.astype(LOW)
        g_att = jnp.einsum(
            "tsn,skn->tk",
            g_mid_low.reshape(mine, pieces, out_width),
            out_full,
            preferred_element_type=jnp.float32,
        )
        g_att = to_heads(g_att.astype(LOW))
        g_query, g_key, g_value = attend_back(query, key, value, first, att_heads, g_att, heads)
        g_value = g_value.reshape(streams * length, wide)
        g_query = g_query.reshape(streams * length, qk)
        g_key = g_key.reshape(streams * length, qk)
        g_h_one_part = (
            contract(g_value, value_full, 1, 1)
            + contract(g_query, query_full, 1, 1)
            + contract(g_key, key_full, 1, 1)
        ).astype(LOW)
        g_h_one_part = g_h_one_part.reshape(streams, pieces, span, D).transpose(1, 0, 2, 3)
        if sharers > 1:
            padded = jnp.zeros((pieces, micro, span, D), LOW)
            g_h_one_part = lax.dynamic_update_slice_in_dim(padded, g_h_one_part, first_stream, 1)
        g_h_one = scatter_plane(g_h_one_part.reshape(pieces, mine, D), 9)
        inverse_one = norm_scale(flat)
        plain_one = flat * inverse_one
        input_grad = g_mid + norm_backward(g_h_one, plain_one, inverse_one, gain_one)
        grad_out = contract(attended, g_mid_low, 0, 0).astype(LOW)
        grad_out = grad_out.reshape(groups, pieces, own, D).transpose(1, 0, 2, 3)
        grad_out = scatter_plane(grad_out.reshape(pieces, groups * own, D), 10).astype(LOW)
        grad_attn = jnp.concatenate(
            [
                contract(h_flat, g_value, 0, 0).astype(LOW),
                contract(h_flat, g_query, 0, 0).astype(LOW),
                contract(h_flat, g_key, 0, 0).astype(LOW),
                jnp.sum(g_h_one * plain_one, axis=0).astype(LOW)[:, None],
                jnp.sum(g_h_two * plain_two, axis=0).astype(LOW)[:, None],
            ],
            axis=1,
        )

    grad_out, sum_ffn, sum_down = lax.optimization_barrier((grad_out, sum_ffn, sum_down))
    grad_out = scatter_dp(grad_out)
    grad_attn = scatter_dp(grad_attn)
    ffn_got = exchange_plane(sum_ffn.reshape(pieces, own, 2 * hidden), 11).astype(jnp.float32)
    attn_got = exchange_plane(grad_attn.reshape(pieces, own, -1), 12).astype(jnp.float32)
    grad_gains = jnp.sum(attn_got[:, :, wide + 2 * qk : wide + 2 * qk + 2], axis=0)
    attn_got = jnp.sum(attn_got.reshape(pieces // sharers, sharers, own, -1), axis=1)

    def by_rows(block):
        return block.transpose(1, 0, 2).reshape(own, -1)

    def by_hidden(second):
        parts, start = [], 0
        for count in chunks:
            begin = start + second * groups * count
            part = ffn_got[:, :, begin : begin + groups * count]
            parts.append(part.reshape(pieces, own, groups, count))
            start += 2 * groups * count
        whole = jnp.concatenate(parts, axis=3)
        return whole.transpose(1, 2, 0, 3).reshape(own, FF)

    return (
        output.reshape(tokens.shape),
        input_grad.reshape(tokens.shape),
        by_rows(attn_got[:, :, wide : wide + qk]),
        by_rows(attn_got[:, :, wide + qk : wide + 2 * qk]),
        by_rows(attn_got[:, :, :wide]),
        grad_out.astype(jnp.float32),
        by_hidden(0),
        by_hidden(1),
        sum_down.astype(jnp.float32),
        grad_gains[:, 0],
        grad_gains[:, 1],
    )


def solution(mesh):
    by_token, by_row = P("dp", None, "seq", None), P("dp", None)
    grad_rows, grad_entries = P(("dp", "seq"), None), P(("dp", "seq"))
    return jax.shard_map(
        local,
        mesh=mesh,
        in_specs=(by_token, P("dp", None, None)) + (by_row,) * 7 + (P("dp"), P("dp"), by_token),
        out_specs=(by_token, by_token) + (grad_rows,) * 7 + (grad_entries,) * 2,
        check_vma=False,
    )
```

```python
import functools
import math

import jax
import jax.numpy as jnp
from jax import lax
from jax.experimental import pallas as pl
from jax.experimental.pallas import tpu as pltpu
from jax.sharding import PartitionSpec as P

D = 2048
HEADS = 16
QK_DIM = 16
FF = 5632
HEAD_V = 128
epsilon = 1e-06
MIB = 1024 * 1024


def dot(left, right):
    return jnp.dot(left, right, preferred_element_type=jnp.float32)


def contract(left, right, left_dim, right_dim):
    return lax.dot_general(
        left, right, (((left_dim,), (right_dim,)), ((), ())), preferred_element_type=jnp.float32
    )


def head_lanes(rows, head):
    lane = lax.broadcasted_iota(jnp.int32, rows.shape, 1)
    inside = (lane >= head * QK_DIM) & (lane < (head + 1) * QK_DIM)
    return jnp.where(inside, rows, jnp.zeros_like(rows))


def weights_of(query, key, head, first, base):
    scores = contract(head_lanes(query, head), key, 1, 1)
    row = base + lax.broadcasted_iota(jnp.int32, scores.shape, 0)
    column = lax.broadcasted_iota(jnp.int32, scores.shape, 1)
    mask = (column <= row) & (column >= first)
    poly = 1.0 + scores * (1.0 / math.sqrt(QK_DIM)) + scores * scores * (0.5 / QK_DIM)
    return scores, mask, jnp.where(mask, poly, 0.0)


def attend_kernel(heads, q_ref, k_ref, v_ref, first_ref, out_ref):
    rows = q_ref.shape[1]
    base = pl.program_id(1) * rows
    for head in range(heads):
        columns = slice(head * HEAD_V, (head + 1) * HEAD_V)
        unused, unused_mask, weight = weights_of(
            q_ref[0], k_ref[0], head, first_ref[0], base
        )
        denom = jnp.sum(weight, axis=1, keepdims=True)
        numer = dot(weight.astype(jnp.bfloat16), v_ref[0, :, columns])
        out_ref[0, :, columns] = (numer / denom).astype(jnp.bfloat16)


def attend(query, key, value, first, heads):
    streams, length, width = query.shape
    rows = min(256, length)
    return pl.pallas_call(
        functools.partial(attend_kernel, heads),
        grid=(streams, length // rows),
        in_specs=[
            pl.BlockSpec((1, rows, width), lambda m, i: (m, i, 0)),
            pl.BlockSpec((1, length, width), lambda m, i: (m, 0, 0)),
            pl.BlockSpec((1, length, heads * HEAD_V), lambda m, i: (m, 0, 0)),
            pl.BlockSpec((1, rows, 1), lambda m, i: (m, i, 0)),
        ],
        out_specs=pl.BlockSpec((1, rows, heads * HEAD_V), lambda m, i: (m, i, 0)),
        out_shape=jax.ShapeDtypeStruct(value.shape, jnp.bfloat16),
        compiler_params=pltpu.CompilerParams(vmem_limit_bytes=48 * MIB),
        name="attend",
    )(query, key, value, first)


def attend_back_kernel(
    heads, q_ref, k_ref, v_ref, first_ref, att_ref, g_ref, gq_ref, gk_ref, gv_ref, gk_sum, gv_sum
):
    rows = q_ref.shape[1]
    step = pl.program_id(1)
    base = step * rows

    @pl.when(step == 0)
    def _():
        gk_sum[...] = jnp.zeros_like(gk_sum)
        gv_sum[...] = jnp.zeros_like(gv_sum)

    query, key = q_ref[0], k_ref[0]
    g_query = jnp.zeros(query.shape, jnp.float32)
    for head in range(heads):
        columns = slice(head * HEAD_V, (head + 1) * HEAD_V)
        scores, mask, weight = weights_of(query, key, head, first_ref[0], base)
        denom = jnp.sum(weight, axis=1, keepdims=True)
        a = (g_ref[0, :, columns].astype(jnp.float32) / denom).astype(jnp.bfloat16)
        b = -jnp.sum(
            a.astype(jnp.float32) * att_ref[0, :, columns].astype(jnp.float32),
            axis=1,
            keepdims=True,
        )
        g_weight = contract(a, v_ref[0, :, columns], 1, 1) + b
        slope = 1.0 / math.sqrt(QK_DIM) + scores * (1.0 / QK_DIM)
        g_scores = jnp.where(mask, g_weight * slope, 0.0).astype(jnp.bfloat16)
        g_query += head_lanes(dot(g_scores, key), head)
        gk_sum[...] += contract(g_scores, head_lanes(query, head), 0, 0)
        gv_sum[:, columns] += contract(weight.astype(jnp.bfloat16), a, 0, 0)
    gq_ref[0] = g_query.astype(jnp.bfloat16)

    @pl.when(step == pl.num_programs(1) - 1)
    def _():
        gk_ref[0] = gk_sum[...].astype(jnp.bfloat16)
        gv_ref[0] = gv_sum[...].astype(jnp.bfloat16)


def attend_back(query, key, value, first, attended, grad, heads):
    streams, length, width = query.shape
    rows = min(256, length)
    some = pl.BlockSpec((1, rows, width), lambda m, i: (m, i, 0))
    all_narrow = pl.BlockSpec((1, length, width), lambda m, i: (m, 0, 0))
    all_wide = pl.BlockSpec((1, length, heads * HEAD_V), lambda m, i: (m, 0, 0))
    some_wide = pl.BlockSpec((1, rows, heads * HEAD_V), lambda m, i: (m, i, 0))
    return pl.pallas_call(
        functools.partial(attend_back_kernel, heads),
        grid=(streams, length // rows),
        in_specs=[
            some,
            all_narrow,
            all_wide,
            pl.BlockSpec((1, rows, 1), lambda m, i: (m, i, 0)),
            some_wide,
            some_wide,
        ],
        out_specs=[some, all_narrow, all_wide],
        out_shape=[
            jax.ShapeDtypeStruct(query.shape, jnp.bfloat16),
            jax.ShapeDtypeStruct(key.shape, jnp.bfloat16),
            jax.ShapeDtypeStruct(value.shape, jnp.bfloat16),
        ],
        scratch_shapes=[
            pltpu.VMEM((length, width), jnp.float32),
            pltpu.VMEM((length, heads * HEAD_V), jnp.float32),
        ],
        compiler_params=pltpu.CompilerParams(vmem_limit_bytes=56 * MIB),
        name="attend_back",
    )(query, key, value, first, attended, grad)

MESH = pl.DeviceIdType.MESH
LOW = jnp.bfloat16


def partners():
    me = lax.axis_index("seq")
    core, x, y = me % 2, me // 2 % 2, me // 4
    return me, me + 1 - 2 * core, me + 2 - 4 * x, me + 4 - 8 * y


def greet(others):
    barrier = pltpu.get_barrier_semaphore()
    for other in others:
        pl.semaphore_signal(barrier, inc=1, device_id={"seq": other}, device_id_type=MESH)
    pl.semaphore_wait(barrier, len(others))


def remote(send, recv, k, src, dst, to):
    return pltpu.make_async_remote_copy(
        src_ref=src,
        dst_ref=dst,
        send_sem=send.at[k],
        recv_sem=recv.at[k],
        device_id={"seq": to},
        device_id_type=MESH,
    )


def gather_kernel(x_ref, o_ref, send, recv, own_sem):
    me, sib, xn, yn = partners()
    diag = xn + yn - me
    half = x_ref.shape[0] // 2
    copy = functools.partial(remote, send, recv)
    upper, lower = pl.ds(0, half), pl.ds(half, half)
    greet((sib, xn, yn))
    own = pltpu.make_async_copy(x_ref, o_ref.at[me], own_sem)
    own.start()
    xa = copy(0, x_ref.at[upper], o_ref.at[me, upper], xn)
    yb = copy(1, x_ref.at[lower], o_ref.at[me, lower], yn)
    xb = copy(2, x_ref.at[lower], o_ref.at[me, lower], xn)
    ya = copy(3, x_ref.at[upper], o_ref.at[me, upper], yn)
    beside = [copy(4, x_ref, o_ref.at[me], sib)]
    started = [xa, yb, xb, ya, beside[0]]
    for c in started:
        c.start()

    def pass_on(k, origin, part, to):
        block = o_ref.at[origin, part]
        c = copy(k, block, block, to)
        c.start()
        started.append(c)
        return c

    xa.wait_recv()
    fy = pass_on(5, xn, upper, yn)
    beside.append(pass_on(6, xn, upper, sib))
    yb.wait_recv()
    fx = pass_on(7, yn, lower, xn)
    beside.append(pass_on(8, yn, lower, sib))
    xb.wait_recv()
    beside.append(pass_on(9, xn, lower, sib))
    ya.wait_recv()
    beside.append(pass_on(10, yn, upper, sib))
    fy.wait_recv()
    beside.append(pass_on(11, diag, upper, sib))
    fx.wait_recv()
    beside.append(pass_on(12, diag, lower, sib))
    own.wait()
    for c in beside:
        c.wait_recv()
    for c in started:
        c.wait_send()


def moved(nbytes):
    return pl.CostEstimate(flops=0, bytes_accessed=nbytes * 10, transcendentals=0)


def gather_plane(x, number):
    pieces = lax.axis_size("seq")
    if pieces != 8:
        return lax.all_gather(x, "seq", axis=0)
    return pl.pallas_call(
        gather_kernel,
        out_shape=jax.ShapeDtypeStruct((8,) + x.shape, x.dtype),
        in_specs=[pl.BlockSpec(memory_space=pl.ANY)],
        out_specs=pl.BlockSpec(memory_space=pl.ANY),
        scratch_shapes=[
            pltpu.SemaphoreType.DMA((13,)),
            pltpu.SemaphoreType.DMA((13,)),
            pltpu.SemaphoreType.DMA,
        ],
        compiler_params=pltpu.CompilerParams(collective_id=number, has_side_effects=True),
        cost_estimate=moved(16 * x.size),
        name="gather",
    )(x)


def scatter_kernel(p_ref, o_ref, held, got, one, two, send, recv, own_sem):
    me, sib, xn, yn = partners()
    diag = xn + yn - me
    half = p_ref.shape[1] // 2
    copy = functools.partial(remote, send, recv)
    upper, lower = pl.ds(0, half), pl.ds(half, half)
    greet((sib, xn, yn))
    beside, loads = [], []
    for i, owner in enumerate((diag, xn, yn, me)):
        beside.append(copy(i, p_ref.at[owner + sib - me], got.at[i], sib))
        loads.append(pltpu.make_async_copy(p_ref.at[owner], held.at[i], own_sem.at[i]))
        beside[i].start()
        loads[i].start()

    def pair_sum(i):
        beside[i].wait_recv()
        loads[i].wait()
        held[i] = held[i] + got[i]

    pair_sum(0)
    x0 = copy(4, held.at[0, upper], one.at[0], xn)
    x0.start()
    y0 = copy(5, held.at[0, lower], one.at[1], yn)
    y0.start()
    pair_sum(1)
    x1 = copy(6, held.at[1, upper], one.at[2], xn)
    x1.start()
    pair_sum(2)
    y1 = copy(7, held.at[2, lower], one.at[3], yn)
    y1.start()
    pair_sum(3)
    x0.wait_recv()
    held[2, :half] = held[2, :half] + one[0]
    y2 = copy(8, held.at[2, upper], two.at[0], yn)
    y2.start()
    y0.wait_recv()
    held[1, half:] = held[1, half:] + one[1]
    x2 = copy(9, held.at[1, lower], two.at[1], xn)
    x2.start()
    x1.wait_recv()
    y1.wait_recv()
    y2.wait_recv()
    wide = jnp.float32
    o_ref[:half] = held[3, :half].astype(wide) + one[2].astype(wide) + two[0].astype(wide)
    x2.wait_recv()
    o_ref[half:] = held[3, half:].astype(wide) + one[3].astype(wide) + two[1].astype(wide)
    for c in (*beside, x0, y0, x1, y1, y2, x2):
        c.wait_send()


def scatter_plane(part, number):
    pieces, rows, columns = part.shape
    if pieces != 8:
        return lax.psum_scatter(part, "seq", scatter_dimension=0).astype(jnp.float32)
    return pl.pallas_call(
        scatter_kernel,
        out_shape=jax.ShapeDtypeStruct((rows, columns), jnp.float32),
        in_specs=[pl.BlockSpec(memory_space=pl.ANY)],
        out_specs=pl.BlockSpec(memory_space=pltpu.VMEM),
        scratch_shapes=[
            pltpu.VMEM((4, rows, columns), LOW),
            pltpu.VMEM((4, rows, columns), LOW),
            pltpu.VMEM((4, rows // 2, columns), LOW),
            pltpu.VMEM((2, rows // 2, columns), LOW),
            pltpu.SemaphoreType.DMA((10,)),
            pltpu.SemaphoreType.DMA((10,)),
            pltpu.SemaphoreType.DMA((4,)),
        ],
        compiler_params=pltpu.CompilerParams(
            collective_id=number, has_side_effects=True, vmem_limit_bytes=40 * MIB
        ),
        cost_estimate=moved(2 * part.size),
        name="scatter",
    )(part)


def exchange_kernel(x_ref, o_ref, send, recv, own_sem):
    me = lax.axis_index("seq")
    others = [lax.rem(me + i, 8) for i in range(1, 8)]
    greet(others)
    own = pltpu.make_async_copy(x_ref.at[me], o_ref.at[me], own_sem)
    own.start()
    copies = [
        remote(send, recv, i, x_ref.at[other], o_ref.at[me], other)
        for i, other in enumerate(others)
    ]
    for c in copies:
        c.start()
    own.wait()
    for c in copies:
        c.wait()


def exchange_plane(x, number):
    if lax.axis_size("seq") != 8:
        return lax.all_to_all(x, "seq", 0, 0)
    return pl.pallas_call(
        exchange_kernel,
        out_shape=jax.ShapeDtypeStruct(x.shape, x.dtype),
        in_specs=[pl.BlockSpec(memory_space=pl.ANY)],
        out_specs=pl.BlockSpec(memory_space=pl.ANY),
        scratch_shapes=[
            pltpu.SemaphoreType.DMA((7,)),
            pltpu.SemaphoreType.DMA((7,)),
            pltpu.SemaphoreType.DMA,
        ],
        compiler_params=pltpu.CompilerParams(collective_id=number, has_side_effects=True),
        cost_estimate=moved(4 * x.size),
        name="exchange",
    )(x)


CHUNKS = (64, 64, 48)


class PlaneGather:
    def __init__(self, source, target, send, recv):
        me, sib, xn, yn = partners()
        diag = xn + yn - me
        half = target.shape[1] // 2
        upper, lower = pl.ds(0, half), pl.ds(half, half)
        copy = functools.partial(remote, send, recv)

        def direct(k, part, to):
            return copy(k, source.at[part], target.at[me, part], to)

        def pass_on(k, origin, part, to):
            return copy(k, target.at[origin, part], target.at[origin, part], to)

        self.xa, self.yb = direct(0, upper, xn), direct(1, lower, yn)
        self.xb, self.ya = direct(2, lower, xn), direct(3, upper, yn)
        self.s0 = copy(4, source, target.at[me], sib)
        self.fy, self.fx = pass_on(5, xn, upper, yn), pass_on(6, yn, lower, xn)
        self.s1, self.s2 = pass_on(7, xn, upper, sib), pass_on(8, yn, lower, sib)
        self.s3, self.s4 = pass_on(9, xn, lower, sib), pass_on(10, yn, upper, sib)
        self.s5, self.s6 = pass_on(11, diag, upper, sib), pass_on(12, diag, lower, sib)

    def start(self):
        for c in (self.xa, self.yb, self.xb, self.ya, self.s0):
            c.start()

    def forward_first(self):
        self.xa.wait_recv()
        self.yb.wait_recv()
        for c in (self.fy, self.fx, self.s1, self.s2):
            c.start()

    def forward_second(self):
        self.xb.wait_recv()
        self.ya.wait_recv()
        self.s3.start()
        self.s4.start()

    def forward_third(self):
        self.fy.wait_recv()
        self.fx.wait_recv()
        self.s5.start()
        self.s6.start()

    def from_sibling(self, chip):
        for c in {"own": (self.s0,), "x": (self.s1, self.s3), "y": (self.s2, self.s4), "diag": (self.s5, self.s6)}[chip]:
            c.wait_recv()

    def sent(self):
        for c in (self.xa, self.yb, self.xb, self.ya, self.s0, self.fy, self.fx):
            c.wait_send()
        for c in (self.s1, self.s2, self.s3, self.s4, self.s5, self.s6):
            c.wait_send()

    def arrive(self, step):
        @pl.when(step == 1)
        def _():
            self.from_sibling("own")

        @pl.when(step == 2)
        def _():
            self.forward_first()
            self.forward_second()
            self.from_sibling("x")

        @pl.when(step == 4)
        def _():
            self.from_sibling("y")

        @pl.when(step == 6)
        def _():
            self.forward_third()
            self.from_sibling("diag")


class LineGather:
    def __init__(self, item, source, block, send, recv, local):
        z = lax.axis_index("dp")
        self.z = z

        def copy(k, src, owner, to):
            return pltpu.make_async_remote_copy(
                src_ref=src,
                dst_ref=block(owner),
                send_sem=send.at[item, k],
                recv_sem=recv.at[item, owner],
                device_id={"dp": to},
                device_id_type=MESH,
            )

        self.sends = []
        for k, d in enumerate((2, -2, 1, -1)):
            to = z + d
            valid = (to >= 0) & (to < 4)
            self.sends.append((valid, copy(k, source, z, jnp.clip(to, 0, 3))))
        inner = (z == 1) | (z == 2)
        far = jnp.where(z == 1, 3, 0)
        self.stop = (inner, copy(4, block(far), far, jnp.where(z == 1, 0, 3)))
        others = [lax.rem(z + o, 4) for o in (1, 2, 3)]
        self.blocks = [copy(0, source, other, other) for other in others]
        self.own = pltpu.make_async_copy(source, block(z), local.at[item])

    def start(self):
        self.own.start()
        for valid, c in self.sends:

            @pl.when(valid)
            def _(c=c):
                c.start()

    def forward(self):
        inner, c = self.stop

        @pl.when(inner)
        def _():
            self.blocks[1].wait_recv()
            c.start()

    def wait(self):
        inner, unused = self.stop
        self.blocks[0].wait_recv()
        self.blocks[2].wait_recv()

        @pl.when(jnp.logical_not(inner))
        def _():
            self.blocks[1].wait_recv()

        self.own.wait()

    def sent(self):
        for valid, c in (*self.sends, self.stop):

            @pl.when(valid)
            def _(c=c):
                c.wait_send()


def nearest_first(step):
    me, sib, xn, yn = partners()
    chip = jnp.where(step < 4, xn, jnp.where(step < 6, yn, xn + yn - me))
    later = chip + jnp.where(lax.rem(step, 2) == 0, sib - me, 0)
    return jnp.where(step == 0, me, jnp.where(step == 1, sib, later))


def farthest_first(step):
    me, sib, xn, yn = partners()
    chip = jnp.where(step < 4, xn, yn)
    chip = jnp.where(step < 2, xn + yn - me, jnp.where(step < 6, chip, me))
    return chip + jnp.where(lax.rem(step, 2) == 0, sib - me, 0)


def layer_kernel(
    x_ref,
    c_ref,
    wa_ref,
    wo_ref,
    wgu_ref,
    wd_ref,
    gain_ref,
    first_ref,
    x_all,
    c_all,
    h2_all,
    wo_all,
    h1_out,
    q_out,
    k_out,
    v_out,
    att_out,
    tok_out,
    mid_out,
    wa_out,
    gain_out,
    out_part,
    gh_ref,
    dgu_first,
    dd_first,
    dgu_out,
    dd_out,
    dgu_all,
    dd_all,
    wa,
    wgu,
    wd,
    gains,
    q_s,
    k_s,
    v_s,
    att_s,
    tok,
    mid,
    act_s,
    ggu_s,
    sum_gu,
    sum_d,
    x_buf,
    c_buf,
    o_buf,
    w_buf,
    beside,
    held,
    got,
    one,
    two,
    gsend,
    grecv,
    zsend,
    zrecv,
    zlocal,
    esend,
    erecv,
    rsend,
    rrecv,
    load_sem,
    out_sem,
    h1_sem,
    w_sem,
    done_sem,
    self_sem,
    fsend,
    frecv,
):
    me, sib, xn, yn = partners()
    z = lax.axis_index("dp")
    rows, width = x_ref.shape
    span = rows // 2
    wide, qk = v_s.shape[2], q_s.shape[2]
    share = CHUNKS[0] + CHUNKS[1] + CHUNKS[2]
    half = rows // 2
    upper, lower = pl.ds(0, half), pl.ds(half, half)

    barrier = pltpu.get_barrier_semaphore()
    for i in range(1, 8):
        pl.semaphore_signal(
            barrier, inc=1, device_id={"seq": lax.rem(me + i, 8)}, device_id_type=MESH
        )
    for i in range(1, 4):
        pl.semaphore_signal(
            barrier, inc=1, device_id={"dp": lax.rem(z + i, 4)}, device_id_type=MESH
        )
    pl.semaphore_wait(barrier, 10)

    tokens = PlaneGather(x_ref, x_all, gsend.at[0], grecv.at[0])
    out_w = PlaneGather(wo_all.at[me], wo_all, gsend.at[1], grecv.at[1])
    cots = PlaneGather(c_ref, c_all, gsend.at[2], grecv.at[2])
    hidden_in = PlaneGather(held.at[0], h2_all, gsend.at[3], grecv.at[3])

    def line(item, source, block):
        return LineGather(item, source, block, zsend, zrecv, zlocal)

    depth = wa_ref.shape[0]

    def rows_of(ref, count, columns=None):
        def block(owner):
            if columns is None:
                return ref.at[pl.ds(owner * count, count)]
            return ref.at[pl.ds(owner * count, count), columns]

        return block

    z_gain = line(
        0, gain_ref, lambda owner: gains.at[:, pl.ds(pl.multiple_of(owner * depth, 128), depth)]
    )
    z_attn = line(1, wa_ref, rows_of(wa, depth))
    z_out = line(
        2,
        wo_ref.at[:, pl.ds(pl.multiple_of(me * wide, 128), wide)],
        lambda owner: wo_all.at[me, pl.ds(owner * depth, depth)],
    )
    z_up, z_down = [], []
    column, before = 0, 0
    columns, hiddens = [], []
    for k, count in enumerate(CHUNKS):
        part = pl.ds(column, 8 * count)
        z_up.append(line(3 + k, wgu_ref.at[:, part], rows_of(wgu, depth, part)))
        z_down.append(
            line(
                6 + k,
                wd_ref.at[pl.ds(me * share + before, count)],
                lambda owner, base=4 * before, count=count: wd.at[
                    pl.ds(base + owner * count, count)
                ],
            )
        )
        columns.append(column)
        hiddens.append(4 * before)
        column += 8 * count
        before += count

    tokens.start()
    for g in (z_gain, z_attn, z_out):
        g.start()

    def loads(order, step, sources):
        slot = lax.rem(step, 2)
        owner = order(step)
        return [
            pltpu.make_async_copy(source.at[owner], buf.at[slot], load_sem.at[i, slot])
            for i, (source, buf) in enumerate(sources)
        ]

    first_load = pltpu.make_async_copy(x_ref, x_buf.at[0], load_sem.at[0, 0])
    first_load.start()
    tokens.forward_first()
    z_gain.forward()
    z_attn.forward()
    tokens.forward_second()
    z_gain.wait()
    z_attn.wait()
    for g in (z_up[0], z_down[0]):
        g.start()

    def h1_copies(step):
        slot = lax.rem(step, 2)
        owner = nearest_first(step)
        return [
            pltpu.make_async_copy(
                o_buf.at[slot, pl.ds(m * span, span)],
                h1_out.at[m, pl.ds(owner * span, span)],
                h1_sem.at[m, slot],
            )
            for m in range(2)
        ]

    def arrive_tokens(step):
        @pl.when(step == 1)
        def _():
            tokens.from_sibling("own")

        @pl.when(step == 2)
        def _():
            tokens.from_sibling("x")

        @pl.when(step == 4)
        def _():
            tokens.forward_third()
            tokens.from_sibling("y")

        @pl.when(step == 5)
        def _():
            z_out.forward()

        @pl.when(step == 6)
        def _():
            tokens.from_sibling("diag")

    token_source = [(x_all, x_buf)]

    def project(step, carry):
        slot = lax.rem(step, 2)
        owner = nearest_first(step)
        for c in loads(nearest_first, step, token_source):
            c.wait()

        @pl.when(step >= 2)
        def _():
            for c in h1_copies(step - 2):
                c.wait()

        x = x_buf[slot].astype(jnp.float32)
        gain = gains[0:1, :].astype(jnp.float32)
        h_one = (x * norm_scale(x) * gain).astype(LOW)
        o_buf[slot] = h_one
        for c in h1_copies(step):
            c.start()
        arrive_tokens(step + 1)

        @pl.when(step < 7)
        def _():
            for c in loads(nearest_first, step + 1, token_source):
                c.start()

        projected = dot(h_one, wa[...]).astype(LOW)
        for m in range(2):
            there = pl.ds(owner * span, span)
            mine = projected[m * span : (m + 1) * span]
            v_s[m, there, :] = mine[:, :wide]
            q_s[m, there, :] = mine[:, wide : wide + qk]
            k_s[m, there, :] = mine[:, wide + qk : wide + 2 * qk]
        return carry

    lax.fori_loop(0, 8, project, 0)
    for step in (6, 7):
        for c in h1_copies(step):
            c.wait()
    z_out.wait()
    out_w.start()
    for g in (z_up[1], z_down[1]):
        g.start()

    finals = [
        pltpu.make_async_copy(source, target, done_sem.at[i])
        for i, (source, target) in enumerate(
            (
                (q_s, q_out),
                (k_s, k_out),
                (v_s, v_out),
                (wa, wa_out),
                (gains, gain_out),
                (att_s, att_out),
                (tok, tok_out),
                (mid, mid_out),
            )
        )
    ]
    for c in finals[:5]:
        c.start()

    length = v_s.shape[1]
    block = 256

    def attend_stream(m, carry):
        for i in range(length // block):
            rows_i = slice(i * block, (i + 1) * block)
            seen = (i + 1) * block
            for head in range(wide // HEAD_V):
                lanes = slice(head * HEAD_V, (head + 1) * HEAD_V)
                unused, unused_mask, weight = weights_of(
                    q_s[m, rows_i, :], k_s[m, :seen, :], head, first_ref[m, rows_i, :], i * block
                )
                denom = jnp.sum(weight, axis=1, keepdims=True)
                numer = dot(weight.astype(LOW), v_s[m, :seen, lanes])
                att_s[m, rows_i, lanes] = (numer / denom).astype(LOW)
        return carry

    lax.fori_loop(0, 2, attend_stream, 0)
    out_w.forward_first()
    cots.start()
    finals[5].start()

    to_mine = pl.ds(pl.multiple_of(me * wide, 128), wide)
    swaps = []
    for i in range(1, 8):
        other = lax.rem(me + i, 8)
        for m in range(2):
            swaps.append(
                remote(
                    esend,
                    erecv,
                    2 * (i - 1) + m,
                    att_s.at[m, pl.ds(other * span, span)],
                    tok.at[pl.ds(m * span, span), to_mine],
                    other,
                )
            )
            swaps[-1].start()
    kept = [
        pltpu.make_async_copy(
            att_s.at[m, pl.ds(me * span, span)],
            tok.at[pl.ds(m * span, span), to_mine],
            self_sem.at[m],
        )
        for m in range(2)
    ]
    for c in kept:
        c.start()
    x_load = pltpu.make_async_copy(x_ref, x_buf.at[0], load_sem.at[0, 0])
    x_load.start()

    def w_load(step):
        slot = lax.rem(step, 2)
        return pltpu.make_async_copy(wo_all.at[nearest_first(step)], w_buf.at[slot], w_sem.at[slot])

    w_load(0).start()
    out_w.forward_second()
    z_up[0].forward()
    z_down[0].forward()
    for c in kept:
        c.wait()
    for c in swaps:
        c.wait_recv()
    finals[6].start()
    x_load.wait()

    def arrive_out(step):
        @pl.when(step == 1)
        def _():
            out_w.from_sibling("own")

        @pl.when(step == 2)
        def _():
            out_w.from_sibling("x")

        @pl.when(step == 4)
        def _():
            out_w.forward_third()
            out_w.from_sibling("y")

        @pl.when(step == 6)
        def _():
            out_w.from_sibling("diag")

    def project_out(step, carry):
        slot = lax.rem(step, 2)
        owner = nearest_first(step)
        w_load(step).wait()
        arrive_out(step + 1)

        @pl.when(step < 7)
        def _():
            w_load(step + 1).start()

        there = pl.ds(pl.multiple_of(owner * wide, 128), wide)
        mid[:, there] = dot(tok[...], w_buf[slot])
        return carry

    lax.fori_loop(0, 8, project_out, 0)
    mid_value = x_buf[0].astype(jnp.float32) + mid[...]
    mid[...] = mid_value
    held[0] = (mid_value * norm_scale(mid_value) * gains[1:2, :].astype(jnp.float32)).astype(LOW)
    finals[7].start()
    hidden_in.start()
    own_h2 = pltpu.make_async_copy(held.at[0], h2_all.at[me], self_sem.at[2])
    own_c = pltpu.make_async_copy(c_ref, c_all.at[me], self_sem.at[3])
    own_h2.start()
    own_c.start()
    cots.forward_first()
    cots.forward_second()
    for g in (z_up[2], z_down[2]):
        g.start()
    own_h2.wait()
    own_c.wait()
    z_up[0].wait()
    z_down[0].wait()

    sources = [(h2_all, x_buf), (c_all, c_buf)]

    def out_copy(order, step):
        slot = lax.rem(step, 2)
        return pltpu.make_async_copy(o_buf.at[slot], out_part.at[order(step)], out_sem.at[slot])

    def hidden_chunk(k, owner, h, c):
        count = 4 * CHUNKS[k]
        pair = pl.ds(columns[k], 2 * count)
        here = pl.ds(hiddens[k], count)
        both = dot(h, wgu[:, pair])
        gate, up = both[:, :count], both[:, count:]
        g_act = contract(c, wd[here, :], 1, 1)
        sigmoid = jax.nn.sigmoid(gate)
        silu = gate * sigmoid
        act = (silu * up).astype(LOW)
        g_gate = (g_act * up * sigmoid * (1.0 + gate * (1.0 - sigmoid))).astype(LOW)
        g_up = (g_act * silu).astype(LOW)
        there = pl.ds(owner * rows, rows)
        act_s[there, here] = act
        g_both = jnp.concatenate([g_gate, g_up], axis=1)
        ggu_s[there, pair] = g_both
        return act, g_both

    def add_grads(k, step, h, c, act, g_both):
        count = 4 * CHUNKS[k]

        @pl.when(step == 0)
        def _():
            sum_gu[...] = jnp.zeros_like(sum_gu)
            sum_d[...] = jnp.zeros_like(sum_d)

        sum_gu[:, : 2 * count] += contract(h, g_both, 0, 0)
        sum_d[:count, :] += contract(act, c, 0, 0)

    def emit(k):
        count = 4 * CHUNKS[k]
        rest = share - CHUNKS[0]

        def gu_target(i):
            there = pl.ds(i * rows, rows)
            if k == 0:
                return dgu_first.at[there]
            return dgu_out.at[there, pl.ds(columns[k] - columns[1], 2 * count)]

        def d_target(owner):
            if k == 0:
                return dd_first.at[pl.ds(owner * CHUNKS[0], CHUNKS[0])]
            start = owner * rest + (hiddens[k] - hiddens[1]) // 4
            return dd_out.at[pl.ds(start, CHUNKS[k])]

        pending = [None, None]
        for i in range(width // rows):
            slot = i % 2
            if pending[slot] is not None:
                pending[slot].wait()
            o_buf[slot, :, : 2 * count] = sum_gu[i * rows : (i + 1) * rows, : 2 * count].astype(LOW)
            pending[slot] = pltpu.make_async_copy(
                o_buf.at[slot, :, pl.ds(0, 2 * count)], gu_target(i), out_sem.at[slot]
            )
            pending[slot].start()
        for c in pending:
            c.wait()
        o_buf[0, :count, :] = sum_d[:count, :].astype(LOW)
        downs = []
        for owner in range(4):
            downs.append(
                pltpu.make_async_copy(
                    o_buf.at[0, pl.ds(owner * CHUNKS[k], CHUNKS[k])],
                    d_target(owner),
                    h1_sem.at[owner // 2, owner % 2],
                )
            )
            downs[-1].start()
        for c in downs:
            c.wait()

    def forward_pass(k, arrive, step, carry):
        slot = lax.rem(step, 2)
        for c in loads(nearest_first, step, sources):
            c.wait()
        h, c = x_buf[slot], c_buf[slot]
        act, g_both = hidden_chunk(k, nearest_first(step), h, c)
        if arrive is not None:
            arrive(step + 1)

        @pl.when(step < 7)
        def _():
            for c in loads(nearest_first, step + 1, sources):
                c.start()

        add_grads(k, step, h, c, act, g_both)
        return carry

    def arrive_both(step):
        hidden_in.arrive(step)

        @pl.when(step == 1)
        def _():
            cots.from_sibling("own")

        @pl.when(step == 2)
        def _():
            cots.from_sibling("x")

        @pl.when(step == 4)
        def _():
            cots.forward_third()
            cots.from_sibling("y")

        @pl.when(step == 5)
        def _():
            z_up[1].forward()
            z_down[1].forward()

        @pl.when(step == 6)
        def _():
            cots.from_sibling("diag")

    for c in loads(nearest_first, 0, sources):
        c.start()
    lax.fori_loop(0, 8, functools.partial(forward_pass, 0, arrive_both), 0)
    hidden_in.sent()
    z_up[1].wait()
    z_down[1].wait()
    for c in loads(nearest_first, 0, sources):
        c.start()
    emit(0)
    sum_lines = [
        LineScatter(dgu_first, depth, dgu_all, fsend.at[0], frecv.at[0], self_sem.at[0]),
        LineScatter(dd_first, CHUNKS[0], dd_all, fsend.at[1], frecv.at[1], self_sem.at[1]),
    ]
    for g in sum_lines:
        g.start()

    def arrive_last(step):
        @pl.when(step == 4)
        def _():
            z_up[2].forward()
            z_down[2].forward()

    lax.fori_loop(0, 8, functools.partial(forward_pass, 1, arrive_last), 0)
    z_up[2].wait()
    z_down[2].wait()
    for c in loads(farthest_first, 0, sources):
        c.start()
    emit(1)

    copy = functools.partial(remote, rsend, rrecv)
    b_diag = copy(0, beside.at[0], got.at[2], sib)
    b_x = copy(1, beside.at[1], got.at[1], sib)
    b_y = copy(2, beside.at[0], got.at[3], sib)
    b_own = copy(3, beside.at[1], got.at[0], sib)
    x0 = copy(4, held.at[2, upper], one.at[0], xn)
    y0 = copy(5, held.at[2, lower], one.at[1], yn)
    x1 = copy(6, held.at[1, upper], one.at[2], xn)
    y1 = copy(7, held.at[3, lower], one.at[3], yn)
    y2 = copy(8, held.at[3, upper], two.at[0], yn)
    x2 = copy(9, held.at[1, lower], two.at[1], xn)

    def last_pass(step, carry):
        slot = lax.rem(step, 2)
        owner = farthest_first(step)
        there = pl.ds(owner * rows, rows)
        for c in loads(farthest_first, step, sources):
            c.wait()
        h, c = x_buf[slot], c_buf[slot]
        act, g_both = hidden_chunk(2, owner, h, c)
        part = contract(ggu_s[there, :], wgu[...], 1, 1).astype(LOW)

        for k, place, sent in ((0, 0, b_diag), (2, 1, b_x), (4, 0, b_y), (6, 1, b_own)):

            @pl.when(step == k)
            def _(k=k, place=place, sent=sent):
                if k == 4:
                    b_diag.wait_send()
                if k == 6:
                    b_x.wait_send()
                beside[place] = part
                sent.start()

        for k, place, arrived in ((1, 2, b_diag), (3, 1, b_x), (5, 3, b_y), (7, 0, b_own)):

            @pl.when(step == k)
            def _(k=k, place=place, arrived=arrived):
                arrived.wait_recv()
                held[place] = part + got[place]
                if k == 1:
                    x0.start()
                    y0.start()
                if k == 3:
                    x1.start()
                if k == 5:
                    y1.start()
                    y0.wait_recv()
                    held[1, half:] = held[1, half:] + one[1]
                    x2.start()
                    x0.wait_recv()
                    held[3, :half] = held[3, :half] + one[0]
                    y2.start()

        @pl.when(step >= 2)
        def _():
            out_copy(farthest_first, step - 2).wait()

        o_buf[slot] = dot(act_s[there, :], wd[...]).astype(LOW)
        out_copy(farthest_first, step).start()

        @pl.when(step < 7)
        def _():
            for c in loads(farthest_first, step + 1, sources):
                c.start()

        add_grads(2, step, h, c, act, g_both)
        return carry

    lax.fori_loop(0, 8, last_pass, 0)
    out_copy(farthest_first, 6).wait()
    out_copy(farthest_first, 7).wait()
    emit(2)
    f32 = jnp.float32
    x1.wait_recv()
    y2.wait_recv()
    gh_ref[:half] = held[0, :half].astype(f32) + one[2].astype(f32) + two[0].astype(f32)
    y1.wait_recv()
    x2.wait_recv()
    gh_ref[half:] = held[0, half:].astype(f32) + one[3].astype(f32) + two[1].astype(f32)
    for c in finals:
        c.wait()
    for g in sum_lines:
        g.wait()
    for c in (b_y, b_own, x0, y0, x1, y1, y2, x2, *swaps):
        c.wait_send()
    for g in (tokens, out_w, cots, z_gain, z_attn, z_out, *z_up, *z_down):
        g.sent()


def layer_front(tokens, cot, attn_slice, w_out, ffn_slice, w_down, gain_rows, first, wide, qk):
    rows, width = tokens.shape
    streams, length, unused = first.shape
    hidden = 4 * sum(CHUNKS)
    largest = 4 * max(CHUNKS)
    shape = jax.ShapeDtypeStruct
    f32 = jnp.float32
    anywhere = pl.BlockSpec(memory_space=pl.ANY)
    in_vmem = pl.BlockSpec(memory_space=pltpu.VMEM)
    plane = shape((8, rows, width), LOW)
    narrow = shape((streams, length, qk), LOW)
    broad = shape((streams, length, wide), LOW)
    attn_shape = (width, attn_slice.shape[1])
    out_shape = [
        plane,
        plane,
        plane,
        shape((8, width, width // 8), LOW),
        shape((streams, length, width), LOW),
        narrow,
        narrow,
        broad,
        broad,
        shape((rows, width), LOW),
        shape((rows, width), f32),
        shape(attn_shape, LOW),
        shape((gain_rows.shape[0], width), LOW),
        plane,
        shape((rows, width), f32),
        shape((width, 8 * CHUNKS[0]), LOW),
        shape((4 * CHUNKS[0], width), LOW),
        shape((width, 2 * hidden - 8 * CHUNKS[0]), LOW),
        shape((hidden - 4 * CHUNKS[0], width), LOW),
        shape((4, width // 4, 8 * CHUNKS[0]), LOW),
        shape((4, CHUNKS[0], width), LOW),
    ]
    dma = pltpu.SemaphoreType.DMA
    vmem = pltpu.VMEM
    return pl.pallas_call(
        layer_kernel,
        out_shape=out_shape,
        in_specs=[anywhere] * 7 + [in_vmem],
        out_specs=[anywhere] * 14 + [in_vmem] + [anywhere] * 6,
        scratch_shapes=[
            vmem(attn_shape, LOW),
            vmem((width, 2 * hidden), LOW),
            vmem((hidden, width), LOW),
            vmem((gain_rows.shape[0], width), LOW),
            vmem(narrow.shape, LOW),
            vmem(narrow.shape, LOW),
            vmem(broad.shape, LOW),
            vmem(broad.shape, LOW),
            vmem((rows, width), LOW),
            vmem((rows, width), f32),
            vmem((8 * rows, hidden), LOW),
            vmem((8 * rows, 2 * hidden), LOW),
            vmem((width, 2 * largest), f32),
            vmem((largest, width), f32),
            vmem((2, rows, width), LOW),
            vmem((2, rows, width), LOW),
            vmem((2, rows, width), LOW),
            vmem((2, width, width // 8), LOW),
            vmem((2, rows, width), LOW),
            vmem((4, rows, width), LOW),
            vmem((4, rows, width), LOW),
            vmem((4, rows // 2, width), LOW),
            vmem((2, rows // 2, width), LOW),
            dma((4, 13)),
            dma((4, 13)),
            dma((9, 5)),
            dma((9, 4)),
            dma((9,)),
            dma((14,)),
            dma((14,)),
            dma((10,)),
            dma((10,)),
            dma((2, 2)),
            dma((2,)),
            dma((2, 2)),
            dma((2,)),
            dma((8,)),
            dma((4,)),
            dma((2, 3)),
            dma((2, 4)),
        ],
        compiler_params=pltpu.CompilerParams(
            collective_id=21, has_side_effects=True, vmem_limit_bytes=63 * MIB
        ),
        cost_estimate=pl.CostEstimate(
            flops=6 * 3 * 8 * rows * width * hidden,
            bytes_accessed=400 * rows * width,
            transcendentals=0,
        ),
        name="layer",
    )(tokens, cot, attn_slice, w_out, ffn_slice, w_down, gain_rows, first)


class LineScatter:
    def __init__(self, source, count, target, send, recv, local):
        z = lax.axis_index("dp")

        def copy(k, to, owner):
            return pltpu.make_async_remote_copy(
                src_ref=source.at[pl.ds(to * count, count)],
                dst_ref=target.at[owner],
                send_sem=send.at[k],
                recv_sem=recv.at[owner],
                device_id={"dp": to},
                device_id_type=MESH,
            )

        others = [lax.rem(z + o, 4) for o in (2, 1, 3)]
        self.sends = [copy(k, other, z) for k, other in enumerate(others)]
        self.arrivals = [copy(0, other, other) for other in others]
        self.own = pltpu.make_async_copy(source.at[pl.ds(z * count, count)], target.at[z], local)

    def start(self):
        self.own.start()
        for c in self.sends:
            c.start()

    def wait(self):
        for c in self.arrivals:
            c.wait_recv()
        self.own.wait()
        for c in self.sends:
            c.wait_send()


class PlaneScatter:
    def __init__(self, beside, held, got, one, two, send, recv):
        me, sib, xn, yn = partners()
        half = got.shape[1] // 2
        self.half = half
        upper, lower = pl.ds(0, half), pl.ds(half, half)
        copy = functools.partial(remote, send, recv)
        self.held, self.got, self.one, self.two = held, got, one, two
        self.pairs = [copy(i, beside(i), got.at[i], sib) for i in range(4)]
        self.x0 = copy(4, held(2).at[upper], one.at[0], xn)
        self.y0 = copy(5, held(2).at[lower], one.at[1], yn)
        self.x1 = copy(6, held(1).at[upper], one.at[2], xn)
        self.y1 = copy(7, held(3).at[lower], one.at[3], yn)
        self.y2 = copy(8, held(3).at[upper], two.at[0], yn)
        self.x2 = copy(9, held(1).at[lower], two.at[1], xn)

    def start_pair(self, i):
        self.pairs[i].start()

    def start_pairs(self):
        for i in (2, 1, 3, 0):
            self.start_pair(i)

    def add_pair(self, i):
        self.pairs[i].wait_recv()
        block = self.held(i)
        block[...] = block[...] + self.got[i]
        for c in {0: (), 1: (self.x1,), 2: (self.x0, self.y0), 3: (self.y1,)}[i]:
            c.start()

    def add_pairs(self):
        for i in (2, 1, 3, 0):
            self.add_pair(i)

    def second(self):
        half = self.half
        self.y0.wait_recv()
        block = self.held(1)
        block[half:, :] = block[half:, :] + self.one[1]
        self.x2.start()
        self.x0.wait_recv()
        block = self.held(3)
        block[:half, :] = block[:half, :] + self.one[0]
        self.y2.start()

    def upper_sum(self):
        f32 = jnp.float32
        self.x1.wait_recv()
        self.y2.wait_recv()
        own = self.held(0)[: self.half, :].astype(f32)
        return own + self.one[2].astype(f32) + self.two[0].astype(f32)

    def lower_sum(self):
        f32 = jnp.float32
        self.y1.wait_recv()
        self.x2.wait_recv()
        own = self.held(0)[self.half :, :].astype(f32)
        return own + self.one[3].astype(f32) + self.two[1].astype(f32)

    def sent(self):
        for c in (*self.pairs, self.x0, self.y0, self.x1, self.y1, self.y2, self.x2):
            c.wait_send()


def chips():
    me, unused, xn, yn = partners()
    return me, xn, xn + yn - me, yn


def turn_kernel(
    gh_ref,
    mid_ref,
    c_ref,
    gain_ref,
    wo_all,
    part_ref,
    tok_ref,
    q_ref,
    k_ref,
    v_ref,
    att_ref,
    first_ref,
    h1_ref,
    output_ref,
    g_mid_out,
    g_out,
    gain_out,
    attn_ref,
    g_mid,
    work,
    g_low,
    g_att,
    g_heads,
    g_s,
    w_buf,
    go_part,
    held_o,
    got_g,
    one_g,
    two_g,
    got_o,
    one_o,
    two_o,
    gk_sum,
    gv_sum,
    h_buf,
    sums,
    esend,
    erecv,
    ssend,
    srecv,
    load_sem,
    w_sem,
    self_sem,
    done_sem,
    h_sem,
):
    me, sib, xn, yn = partners()
    flip = sib - me
    rows, width = g_low.shape
    span = rows // 2
    wide, qk = v_ref.shape[2], q_ref.shape[2]
    half = rows // 2
    greet([lax.rem(me + i, 8) for i in range(1, 8)])
    owners = chips()

    loads = [
        pltpu.make_async_copy(source, target, load_sem.at[i])
        for i, (source, target) in enumerate(
            ((gh_ref, g_mid), (mid_ref, work), (c_ref, g_low))
        )
    ]
    held_loads = [
        pltpu.make_async_copy(part_ref.at[owners[i]], held_o.at[i], load_sem.at[3 + i])
        for i in range(4)
    ]

    def w_load(step):
        slot = lax.rem(step, 2)
        return pltpu.make_async_copy(wo_all.at[step], w_buf.at[slot], w_sem.at[slot])

    for c in loads:
        c.start()
    w_load(0).start()
    outs = PlaneScatter(
        lambda i: part_ref.at[owners[i] + flip],
        lambda i: held_o.at[i],
        got_o,
        one_o,
        two_o,
        ssend.at[0],
        srecv.at[0],
    )
    weights = PlaneScatter(
        lambda i: go_part.at[owners[i] + flip],
        lambda i: go_part.at[owners[i]],
        got_g,
        one_g,
        two_g,
        ssend.at[1],
        srecv.at[1],
    )
    outs.start_pairs()
    for c in held_loads:
        c.start()
    for c in loads:
        c.wait()

    f32 = jnp.float32
    mid = work[...]
    inverse = norm_scale(mid)
    normed = mid * inverse
    grad = g_mid[...]
    gain_out[...] = jnp.broadcast_to(
        jnp.sum(grad * normed, axis=0, keepdims=True), gain_out.shape
    )
    gain = gain_ref[1:2, :].astype(f32)
    grad_mid = g_low[...].astype(f32) + norm_backward(grad, normed, inverse, gain)
    g_mid[...] = grad_mid
    g_low[...] = grad_mid.astype(LOW)
    done = [pltpu.make_async_copy(g_mid, g_mid_out, done_sem.at[0])]
    done[0].start()

    def back_out(step, carry):
        slot = lax.rem(step, 2)
        w_load(step).wait()

        @pl.when(step < 7)
        def _():
            w_load(step + 1).start()

        there = pl.ds(pl.multiple_of(step * wide, 128), wide)
        term = contract(g_low[:, there], w_buf[slot], 1, 1)

        @pl.when(step == 0)
        def _():
            work[...] = term

        @pl.when(step > 0)
        def _():
            work[...] += term

        return carry

    lax.fori_loop(0, 8, back_out, 0)
    g_att[...] = work[...].astype(LOW)
    mid_load = pltpu.make_async_copy(mid_ref, work, load_sem.at[1])
    mid_load.start()
    swaps = []
    here = pl.ds(me * span, span)
    for i in range(1, 8):
        other = lax.rem(me + i, 8)
        lanes = pl.ds(pl.multiple_of(other * wide, 128), wide)
        for m in range(2):
            swaps.append(
                remote(
                    esend,
                    erecv,
                    2 * (i - 1) + m,
                    g_att.at[pl.ds(m * span, span), lanes],
                    g_heads.at[m, here],
                    other,
                )
            )
            swaps[-1].start()
    kept = [
        pltpu.make_async_copy(
            g_att.at[pl.ds(m * span, span), pl.ds(pl.multiple_of(me * wide, 128), wide)],
            g_heads.at[m, here],
            self_sem.at[m],
        )
        for m in range(2)
    ]
    for c in kept:
        c.start()

    own = width // 32
    for z in range(4):
        lanes = slice(z * 8 * own, (z + 1) * 8 * own)
        block = contract(tok_ref[:, lanes], g_low[...], 0, 0).astype(LOW)
        for s in range(8):
            go_part[s, z * own : (z + 1) * own, :] = block[s * own : (s + 1) * own]
    weights.start_pairs()
    for c in kept:
        c.wait()
    for c in swaps:
        c.wait_recv()
    weights.add_pairs()

    length = v_ref.shape[1]
    block = 256
    streams = v_ref.shape[0]
    pieces = length // rows

    def h_load(step):
        slot = lax.rem(step, 2)
        return pltpu.make_async_copy(
            h1_ref.at[step // pieces, pl.ds(lax.rem(step, pieces) * rows, rows)],
            h_buf.at[slot],
            h_sem.at[slot],
        )

    h_load(0).start()

    def back_stream(m, carry):
        gk_sum[...] = jnp.zeros_like(gk_sum)
        gv_sum[...] = jnp.zeros_like(gv_sum)
        for i in range(length // block):
            rows_i = slice(i * block, (i + 1) * block)
            seen = (i + 1) * block
            query, key = q_ref[m, rows_i, :], k_ref[m, :seen, :]
            g_query = jnp.zeros(query.shape, f32)
            for head in range(wide // HEAD_V):
                lanes = slice(head * HEAD_V, (head + 1) * HEAD_V)
                scores, mask, weight = weights_of(
                    query, key, head, first_ref[m, rows_i, :], i * block
                )
                denom = jnp.sum(weight, axis=1, keepdims=True)
                a = (g_heads[m, rows_i, lanes].astype(f32) / denom).astype(LOW)
                b = -jnp.sum(
                    a.astype(f32) * att_ref[m, rows_i, lanes].astype(f32), axis=1, keepdims=True
                )
                g_weight = contract(a, v_ref[m, :seen, lanes], 1, 1) + b
                slope = 1.0 / math.sqrt(QK_DIM) + scores * (1.0 / QK_DIM)
                g_scores = jnp.where(mask, g_weight * slope, 0.0).astype(LOW)
                g_query += head_lanes(dot(g_scores, key), head)
                gk_sum[:seen, :] += contract(g_scores, head_lanes(query, head), 0, 0)
                gv_sum[:seen, lanes] += contract(weight.astype(LOW), a, 0, 0)
            g_s[m, rows_i, wide : wide + qk] = g_query.astype(LOW)
        g_s[m, :, :wide] = gv_sum[...].astype(LOW)
        g_s[m, :, wide + qk : wide + 2 * qk] = gk_sum[...].astype(LOW)
        g_s[m, :, wide + 2 * qk :] = jnp.zeros((length, g_s.shape[2] - wide - 2 * qk), LOW)

        @pl.when(m == 0)
        def _():
            for c in held_loads:
                c.wait()
            outs.add_pairs()

        return carry

    lax.fori_loop(0, 2, back_stream, 0)
    weights.second()
    done.append(pltpu.make_async_copy(g_s, g_out, done_sem.at[1]))
    done[1].start()
    outs.second()

    def add_grads(step, carry):
        slot = lax.rem(step, 2)
        h_load(step).wait()

        @pl.when(step < streams * pieces - 1)
        def _():
            h_load(step + 1).start()

        there = pl.ds(pl.multiple_of(lax.rem(step, pieces) * rows, rows), rows)
        term = contract(h_buf[slot], g_s[step // pieces, there, :], 0, 0)

        @pl.when(step == 0)
        def _():
            sums[...] = term

        @pl.when(step > 0)
        def _():
            sums[...] += term

        return carry

    lax.fori_loop(0, streams * pieces, add_grads, 0)
    narrow = sums.shape[1]
    attn_ref[:, :narrow] = sums[...].astype(LOW)
    mid_load.wait()
    for part, total in enumerate((weights.upper_sum(), weights.lower_sum())):
        total = total.astype(LOW)
        for z in range(2):
            for i in range(8):
                start = ((2 * part + z) * 8 + i) * own
                attn_ref[start : start + own, narrow:] = total[
                    z * own : (z + 1) * own, i * wide : (i + 1) * wide
                ]
    output_ref[:half] = (work[:half] + outs.upper_sum()).astype(LOW)
    output_ref[half:] = (work[half:] + outs.lower_sum()).astype(LOW)
    for c in done:
        c.wait()
    for c in swaps:
        c.wait_send()
    weights.sent()
    outs.sent()


def layer_turn(gh, mid, cot, gains, wo_all, part, tok, query, key, value, att, first, h1, columns):
    rows, width = mid.shape
    streams, length, wide = value.shape
    qk = query.shape[2]
    shape = jax.ShapeDtypeStruct
    f32 = jnp.float32
    anywhere = pl.BlockSpec(memory_space=pl.ANY)
    in_vmem = pl.BlockSpec(memory_space=pltpu.VMEM)
    dma = pltpu.SemaphoreType.DMA
    vmem = pltpu.VMEM
    arriving = [
        vmem((4, rows, width), LOW),
        vmem((4, rows // 2, width), LOW),
        vmem((2, rows // 2, width), LOW),
    ]
    return pl.pallas_call(
        turn_kernel,
        out_shape=[
            shape((rows, width), LOW),
            shape((rows, width), f32),
            shape((streams, length, columns), LOW),
            shape((8, width), f32),
            shape((width, columns + wide), LOW),
        ],
        in_specs=[anywhere] * 3 + [in_vmem] + [anywhere] * 2 + [in_vmem] * 6 + [anywhere],
        out_specs=[in_vmem, anywhere, anywhere, in_vmem, in_vmem],
        scratch_shapes=[
            vmem((rows, width), f32),
            vmem((rows, width), f32),
            vmem((rows, width), LOW),
            vmem((rows, width), LOW),
            vmem((streams, length, wide), LOW),
            vmem((streams, length, columns), LOW),
            vmem((2, width, wide), LOW),
            vmem((8, rows, width), LOW),
            vmem((4, rows, width), LOW),
            *arriving,
            *arriving,
            vmem((length, qk), f32),
            vmem((length, wide), f32),
            vmem((2, rows, width), LOW),
            vmem((width, columns), f32),
            dma((14,)),
            dma((14,)),
            dma((2, 10)),
            dma((2, 10)),
            dma((7,)),
            dma((2,)),
            dma((2,)),
            dma((2,)),
            dma((2,)),
        ],
        compiler_params=pltpu.CompilerParams(
            collective_id=22, has_side_effects=True, vmem_limit_bytes=63 * MIB
        ),
        cost_estimate=moved(16 * rows * width),
        name="turn",
    )(gh, mid, cot, gains, wo_all, part, tok, query, key, value, att, first, h1)


def close_kernel(
    g_ref,
    wa_ref,
    g_mid_ref,
    x_ref,
    gain_ref,
    sum_ref,
    grad_ref,
    gains_ref,
    beside,
    held,
    got,
    one,
    two,
    gain_rows,
    gain_line,
    gain_columns,
    gain_plane,
    ssend,
    srecv,
    zsend,
    zrecv,
    esend,
    erecv,
    self_sem,
):
    me, sib, xn, yn = partners()
    z = lax.axis_index("dp")
    rows, width = x_ref.shape
    span = rows // 2
    half = rows // 2
    f32 = jnp.float32
    barrier = pltpu.get_barrier_semaphore()
    for i in range(1, 8):
        pl.semaphore_signal(
            barrier, inc=1, device_id={"seq": lax.rem(me + i, 8)}, device_id_type=MESH
        )
    for i in range(1, 4):
        pl.semaphore_signal(
            barrier, inc=1, device_id={"dp": lax.rem(z + i, 4)}, device_id_type=MESH
        )
    pl.semaphore_wait(barrier, 10)
    scatter = PlaneScatter(
        lambda i: beside.at[i], lambda i: held.at[i], got, one, two, ssend, srecv
    )
    def part_of(owner):
        there = pl.ds(pl.multiple_of(owner * span, span), span)
        grads = jnp.concatenate([g_ref[0, there, :], g_ref[1, there, :]], axis=0)
        return contract(grads, wa_ref[...], 1, 1).astype(LOW)

    owners = chips()
    for i in (2, 1, 3, 0):
        beside[i] = part_of(owners[i] + sib - me)
        scatter.start_pair(i)
        held[i] = part_of(owners[i])
        scatter.add_pair(i)

    scatter.second()

    x = x_ref[...].astype(f32)
    inverse = norm_scale(x)
    normed = x * inverse
    gain = gain_ref[0:1, :].astype(f32)

    def finish(start, g_h):
        part = slice(start, start + half)
        grad_ref[part] = g_mid_ref[part] + norm_backward(g_h, normed[part], inverse[part], gain)
        return jnp.sum(g_h * normed[part], axis=0, keepdims=True)

    gain_sum = finish(0, scatter.upper_sum()) + finish(half, scatter.lower_sum())

    both = jnp.concatenate([gain_sum, sum_ref[0:1, :], jnp.zeros((14, width), f32)], axis=0)
    gain_rows[...] = both.astype(LOW)
    depth = width // 4

    def lanes(owner):
        return pl.ds(pl.multiple_of(owner * depth, 128), depth)

    def over_line(k, to, owner):
        return pltpu.make_async_remote_copy(
            src_ref=gain_rows.at[:, lanes(to)],
            dst_ref=gain_line.at[owner],
            send_sem=zsend.at[k],
            recv_sem=zrecv.at[owner],
            device_id={"dp": to},
            device_id_type=MESH,
        )

    others = [lax.rem(z + o, 4) for o in (1, 2, 3)]
    sends = [over_line(k, other, z) for k, other in enumerate(others)]
    own = pltpu.make_async_copy(gain_rows.at[:, lanes(z)], gain_line.at[z], self_sem.at[0])
    own.start()
    for c in sends:
        c.start()
    own.wait()
    for other in others:
        over_line(0, other, other).wait_recv()
    total = gain_line[0].astype(f32)
    for k in range(1, 4):
        total = total + gain_line[k].astype(f32)
    entry = lax.broadcasted_iota(jnp.int32, (16, 128), 0)
    lane = lax.broadcasted_iota(jnp.int32, (16, 128), 1)
    pick = jnp.where(lane == entry, 1.0, 0.0).astype(LOW)
    gain_columns[...] = contract(total.astype(LOW), pick, 0, 0).astype(LOW)
    count = depth // 8
    own = pltpu.make_async_copy(
        gain_columns.at[pl.ds(me * count, count)], gain_plane.at[me], self_sem.at[1]
    )
    own.start()
    swaps = []
    for i in range(1, 8):
        other = lax.rem(me + i, 8)
        swaps.append(
            remote(
                esend,
                erecv,
                i - 1,
                gain_columns.at[pl.ds(other * count, count)],
                gain_plane.at[me],
                other,
            )
        )
        swaps[-1].start()
    own.wait()
    for c in swaps:
        c.wait_recv()
    total = gain_plane[0].astype(f32)
    for k in range(1, 8):
        total = total + gain_plane[k].astype(f32)
    gains_ref[...] = total
    scatter.sent()
    for c in (*sends, *swaps):
        c.wait_send()


def layer_close(g_all, wa, g_mid, tokens, gains, gain_sum):
    rows, width = tokens.shape
    shape = jax.ShapeDtypeStruct
    in_vmem = pl.BlockSpec(memory_space=pltpu.VMEM)
    dma = pltpu.SemaphoreType.DMA
    vmem = pltpu.VMEM
    return pl.pallas_call(
        close_kernel,
        out_shape=[
            shape((rows, width), jnp.float32),
            shape((width // 32, 128), jnp.float32),
        ],
        in_specs=[in_vmem] * 6,
        out_specs=[in_vmem, in_vmem],
        scratch_shapes=[
            vmem((4, rows, width), LOW),
            vmem((4, rows, width), LOW),
            vmem((4, rows, width), LOW),
            vmem((4, rows // 2, width), LOW),
            vmem((2, rows // 2, width), LOW),
            vmem((16, width), LOW),
            vmem((4, 16, width // 4), LOW),
            vmem((width // 4, 128), LOW),
            vmem((8, width // 32, 128), LOW),
            dma((10,)),
            dma((10,)),
            dma((3,)),
            dma((4,)),
            dma((7,)),
            dma((7,)),
            dma((2,)),
        ],
        compiler_params=pltpu.CompilerParams(
            collective_id=23, has_side_effects=True, vmem_limit_bytes=56 * MIB
        ),
        cost_estimate=moved(16 * rows * width),
        name="close",
    )(g_all, wa, g_mid, tokens, gains, gain_sum)


def ffn_lax(h_two, cot_all, gate_full, up_full, down_full):
    pieces, rows, width = cot_all.shape
    h_two_all = gather_plane(h_two, 5).reshape(-1, width)
    cot_all = cot_all.reshape(-1, width)
    gate = dot(h_two_all, gate_full)
    up = dot(h_two_all, up_full)
    g_act = contract(cot_all, down_full, 1, 1)
    sigmoid = jax.nn.sigmoid(gate)
    silu = gate * sigmoid
    act = (silu * up).astype(LOW)
    g_gate = (g_act * up * sigmoid * (1.0 + gate * (1.0 - sigmoid))).astype(LOW)
    g_up = (g_act * silu).astype(LOW)
    part = (contract(g_gate, gate_full, 1, 1) + contract(g_up, up_full, 1, 1)).astype(LOW)
    return (
        dot(act, down_full).astype(LOW).reshape(pieces, rows, width),
        scatter_plane(part.reshape(pieces, rows, width), 7),
        contract(h_two_all, g_gate, 0, 0).astype(LOW),
        contract(h_two_all, g_up, 0, 0).astype(LOW),
        contract(act, cot_all, 0, 0).astype(LOW),
    )


def norm_scale(rows):
    return lax.rsqrt(jnp.mean(rows * rows, axis=-1, keepdims=True) + epsilon)


def norm_backward(grad, normed, inverse, gain):
    scaled = grad * gain
    return inverse * (scaled - normed * jnp.mean(scaled * normed, axis=-1, keepdims=True))


def local(
    tokens,
    doc_lengths,
    w_query,
    w_key,
    w_value,
    w_out,
    w_gate,
    w_up,
    w_down,
    gain_attn,
    gain_mlp,
    cotangent,
):
    micro, span = tokens.shape[1:3]
    pieces, groups = lax.axis_size("seq"), lax.axis_size("dp")
    place = lax.axis_index("seq")
    length = pieces * span
    heads = max(1, HEADS // pieces)
    sharers = max(1, pieces // HEADS)
    streams = micro // sharers
    first_head = place // sharers * heads
    first_stream = place % sharers * streams
    qk, wide = heads * QK_DIM, heads * HEAD_V
    hidden = FF // pieces

    out_width = D // pieces
    rows_dp = w_gate.shape[0]
    share = hidden // groups
    block = FF // groups
    mine = micro * span
    fused = pieces == 8 and groups == 4 and micro == 2 and span == 128
    chunks = CHUNKS if fused else (share,)

    def hidden_columns(w):
        parts = [
            lax.dynamic_slice_in_dim(w, z * block + place * share, share, 1) for z in range(groups)
        ]
        edges = [sum(chunks[:k]) for k in range(len(chunks) + 1)]
        return [
            [part[:, edges[k] : edges[k + 1]] for part in parts] for k in range(len(chunks))
        ]

    gate_parts, up_parts = hidden_columns(w_gate), hidden_columns(w_up)
    ffn_slice = jnp.concatenate(
        [part for k in range(len(chunks)) for part in gate_parts[k] + up_parts[k]], axis=1
    )
    attn_parts = [
        lax.dynamic_slice_in_dim(w_value, first_head * HEAD_V, wide, 1),
        lax.dynamic_slice_in_dim(w_query, first_head * QK_DIM, qk, 1),
        lax.dynamic_slice_in_dim(w_key, first_head * QK_DIM, qk, 1),
    ]

    lengths = lax.dynamic_slice_in_dim(doc_lengths[0], first_stream, streams, 0)
    starts = jnp.cumsum(lengths, axis=1) - lengths
    position = jnp.arange(length, dtype=jnp.int32)
    begun = starts[:, None, :] <= position[None, :, None]
    first = jnp.max(jnp.where(begun, starts[:, None, :], 0), axis=2)[..., None]

    x_own = tokens[0].reshape(mine, D)
    flat = x_own.astype(jnp.float32)
    cot = cotangent[0].reshape(mine, D)

    def to_tokens(by_head):
        sent = by_head.reshape(streams, pieces, span, wide).transpose(1, 0, 2, 3)
        got = exchange_plane(sent, 3).reshape(pieces // sharers, micro, span, wide)
        return got.transpose(1, 2, 0, 3).reshape(mine, HEADS * HEAD_V)

    def to_heads(by_token):
        sent = by_token.reshape(micro, span, pieces // sharers, wide).transpose(2, 0, 1, 3)
        got = exchange_plane(sent.reshape(pieces, streams, span, wide), 4)
        return got.transpose(1, 0, 2, 3).reshape(streams, length, wide)

    if fused:
        attn_slice = jnp.concatenate(
            attn_parts + [jnp.zeros((rows_dp, 128 - 2 * qk), LOW)], axis=1
        )
        gain_rows = jnp.concatenate(
            [gain_attn[None], gain_mlp[None], jnp.zeros((14, rows_dp), LOW)], axis=0
        )
        front = layer_front(
            x_own, cot, attn_slice, w_out, ffn_slice, w_down, gain_rows, first, wide, qk
        )
        out_full, h_all, query, key, value, att_heads, attended, mid = front[3:11]
        attn_full, gain_rows_all, out_part, g_h_two = front[11:15]
        d_ffn, d_down, ffn_blocks, down_blocks = front[17:]
    else:

        def gather_dp(w):
            return lax.all_gather(w, "dp", axis=0, tiled=True)

        attn_got = gather_dp(
            jnp.concatenate(
                attn_parts
                + [
                    lax.dynamic_slice_in_dim(w_out, place * out_width, out_width, 1),
                    gain_attn[:, None],
                    gain_mlp[:, None],
                ],
                axis=1,
            )
        )
        ffn_full = gather_dp(ffn_slice)
        down_full = gather_dp(lax.dynamic_slice_in_dim(w_down, place * share, share, 0))
        value_full = attn_got[:, :wide]
        query_full = attn_got[:, wide : wide + qk]
        key_full = attn_got[:, wide + qk : wide + 2 * qk]
        out_full = gather_plane(attn_got[:, wide + 2 * qk : wide + 2 * qk + out_width], 2)
        gains = attn_got[:, wide + 2 * qk + out_width :].astype(jnp.float32)
        gain_one, gain_two = gains[:, 0], gains[:, 1]
        x_all = gather_plane(x_own, 1).reshape(pieces, micro, span, D).transpose(1, 0, 2, 3)
        x_all = lax.dynamic_slice_in_dim(x_all, first_stream, streams, 0).astype(jnp.float32)
        h_flat = (x_all * norm_scale(x_all) * gain_one).astype(LOW).reshape(streams * length, D)
        value = dot(h_flat, value_full).astype(LOW).reshape(streams, length, wide)
        query = dot(h_flat, query_full).astype(LOW).reshape(streams, length, qk)
        key = dot(h_flat, key_full).astype(LOW).reshape(streams, length, qk)
        att_heads = attend(query, key, value, first, heads)
        attended = to_tokens(att_heads)
        mid = flat + jnp.einsum(
            "tk,skn->tsn", attended, out_full, preferred_element_type=jnp.float32
        ).reshape(mine, D)
        h_two = (mid * norm_scale(mid) * gain_two).astype(LOW)
        out_part, g_h_two, d_gate, d_up, d_down = ffn_lax(
            h_two, gather_plane(cot, 6), ffn_full[:, :hidden], ffn_full[:, hidden:], down_full
        )
        d_ffn = jnp.concatenate([d_gate, d_up], axis=1)

    def scatter_dp(part):
        return lax.psum_scatter(part, "dp", scatter_dimension=0, tiled=True)

    own = rows_dp // pieces
    sum_ffn, sum_down = scatter_dp(d_ffn), scatter_dp(d_down)

    if fused:
        output, g_mid, g_all, gain_sum, grad_attn = layer_turn(
            g_h_two, mid, cot, gain_rows_all, out_full, out_part, attended, query, key, value,
            att_heads, first, h_all, attn_full.shape[1],
        )
        input_grad, gain_columns = layer_close(
            g_all, attn_full, g_mid, x_own, gain_rows_all, gain_sum
        )
    else:
        inverse_two = norm_scale(mid)
        plain_two = mid * inverse_two
        output = (mid + scatter_plane(out_part, 8)).astype(LOW)
        g_mid = cot.astype(jnp.float32) + norm_backward(g_h_two, plain_two, inverse_two, gain_two)
        g_mid_low = g_mid.astype(LOW)
        g_att = jnp.einsum(
            "tsn,skn->tk",
            g_mid_low.reshape(mine, pieces, out_width),
            out_full,
            preferred_element_type=jnp.float32,
        )
        g_att = to_heads(g_att.astype(LOW))
        g_query, g_key, g_value = attend_back(query, key, value, first, att_heads, g_att, heads)
        g_value = g_value.reshape(streams * length, wide)
        g_query = g_query.reshape(streams * length, qk)
        g_key = g_key.reshape(streams * length, qk)
        g_h_one_part = (
            contract(g_value, value_full, 1, 1)
            + contract(g_query, query_full, 1, 1)
            + contract(g_key, key_full, 1, 1)
        ).astype(LOW)
        g_h_one_part = g_h_one_part.reshape(streams, pieces, span, D).transpose(1, 0, 2, 3)
        if sharers > 1:
            padded = jnp.zeros((pieces, micro, span, D), LOW)
            g_h_one_part = lax.dynamic_update_slice_in_dim(padded, g_h_one_part, first_stream, 1)
        g_h_one = scatter_plane(g_h_one_part.reshape(pieces, mine, D), 9)
        inverse_one = norm_scale(flat)
        plain_one = flat * inverse_one
        input_grad = g_mid + norm_backward(g_h_one, plain_one, inverse_one, gain_one)
        grad_out = contract(attended, g_mid_low, 0, 0).astype(LOW)
        grad_out = grad_out.reshape(groups, pieces, own, D).transpose(1, 0, 2, 3)
        grad_out = scatter_plane(grad_out.reshape(pieces, groups * own, D), 10).astype(LOW)
        grad_out = scatter_dp(grad_out)
        grad_attn = jnp.concatenate(
            [
                contract(h_flat, g_value, 0, 0).astype(LOW),
                contract(h_flat, g_query, 0, 0).astype(LOW),
                contract(h_flat, g_key, 0, 0).astype(LOW),
                jnp.sum(g_h_one * plain_one, axis=0).astype(LOW)[:, None],
                jnp.sum(g_h_two * plain_two, axis=0).astype(LOW)[:, None],
            ],
            axis=1,
        )

    grad_attn, sum_ffn, sum_down = lax.optimization_barrier((grad_attn, sum_ffn, sum_down))
    grad_attn = scatter_dp(grad_attn)
    if fused:
        grad_out = grad_attn[:, -out_width:].reshape(pieces, own, out_width)
        grad_out = grad_out.transpose(1, 0, 2).reshape(own, D)
        grad_attn = grad_attn[:, :-out_width]
        first_ffn = jnp.sum(ffn_blocks.astype(jnp.float32), axis=0).astype(LOW)
        sum_ffn = jnp.concatenate([first_ffn, sum_ffn], axis=1)
        first_down = jnp.sum(down_blocks.astype(jnp.float32), axis=0)
        sum_down = jnp.concatenate([first_down, sum_down.astype(jnp.float32)], axis=0)
    ffn_got = exchange_plane(sum_ffn.reshape(pieces, own, 2 * hidden), 11).astype(jnp.float32)

    def by_hidden(second):
        parts, start = [], 0
        for count in chunks:
            begin = start + second * groups * count
            part = ffn_got[:, :, begin : begin + groups * count]
            parts.append(part.reshape(pieces, own, groups, count))
            start += 2 * groups * count
        whole = jnp.concatenate(parts, axis=3)
        return whole.transpose(1, 2, 0, 3).reshape(own, FF)

    grad_gate, grad_up = by_hidden(0), by_hidden(1)
    grad_attn, grad_gate, grad_up = lax.optimization_barrier((grad_attn, grad_gate, grad_up))
    attn_got = exchange_plane(grad_attn.reshape(pieces, own, -1), 12).astype(jnp.float32)
    if fused:
        grad_gains = gain_columns
    else:
        grad_gains = jnp.sum(attn_got[:, :, wide + 2 * qk : wide + 2 * qk + 2], axis=0)
    attn_got = jnp.sum(attn_got.reshape(pieces // sharers, sharers, own, -1), axis=1)

    def by_rows(block):
        return block.transpose(1, 0, 2).reshape(own, -1)

    return (
        output.reshape(tokens.shape),
        input_grad.reshape(tokens.shape),
        by_rows(attn_got[:, :, wide : wide + qk]),
        by_rows(attn_got[:, :, wide + qk : wide + 2 * qk]),
        by_rows(attn_got[:, :, :wide]),
        grad_out.astype(jnp.float32),
        grad_gate,
        grad_up,
        sum_down.astype(jnp.float32),
        grad_gains[:, 0],
        grad_gains[:, 1],
    )


def solution(mesh):
    by_token, by_row = P("dp", None, "seq", None), P("dp", None)
    grad_rows, grad_entries = P(("dp", "seq"), None), P(("dp", "seq"))
    return jax.shard_map(
        local,
        mesh=mesh,
        in_specs=(by_token, P("dp", None, None)) + (by_row,) * 7 + (P("dp"), P("dp"), by_token),
        out_specs=(by_token, by_token) + (grad_rows,) * 7 + (grad_entries,) * 2,
        check_vma=False,
    )
```

```python
import functools
import math

import jax
import jax.numpy as jnp
from jax import lax
from jax.experimental import pallas as pl
from jax.experimental.pallas import tpu as pltpu
from jax.sharding import PartitionSpec as P

D = 2048
HEADS = 16
QK_DIM = 16
FF = 5632
HEAD_V = 128
epsilon = 1e-06
MIB = 1024 * 1024


def dot(left, right):
    return jnp.dot(left, right, preferred_element_type=jnp.float32)


def contract(left, right, left_dim, right_dim):
    return lax.dot_general(
        left, right, (((left_dim,), (right_dim,)), ((), ())), preferred_element_type=jnp.float32
    )


def head_lanes(rows, head):
    lane = lax.broadcasted_iota(jnp.int32, rows.shape, 1)
    inside = (lane >= head * QK_DIM) & (lane < (head + 1) * QK_DIM)
    return jnp.where(inside, rows, jnp.zeros_like(rows))


def weights_of(query, key, head, first, base):
    scores = contract(head_lanes(query, head), key, 1, 1)
    row = base + lax.broadcasted_iota(jnp.int32, scores.shape, 0)
    column = lax.broadcasted_iota(jnp.int32, scores.shape, 1)
    mask = (column <= row) & (column >= first)
    poly = 1.0 + scores * (1.0 / math.sqrt(QK_DIM)) + scores * scores * (0.5 / QK_DIM)
    return scores, mask, jnp.where(mask, poly, 0.0)


def attend_kernel(heads, q_ref, k_ref, v_ref, first_ref, out_ref):
    rows = q_ref.shape[1]
    base = pl.program_id(1) * rows
    for head in range(heads):
        columns = slice(head * HEAD_V, (head + 1) * HEAD_V)
        unused, unused_mask, weight = weights_of(
            q_ref[0], k_ref[0], head, first_ref[0], base
        )
        denom = jnp.sum(weight, axis=1, keepdims=True)
        numer = dot(weight.astype(jnp.bfloat16), v_ref[0, :, columns])
        out_ref[0, :, columns] = (numer / denom).astype(jnp.bfloat16)


def attend(query, key, value, first, heads):
    streams, length, width = query.shape
    rows = min(256, length)
    return pl.pallas_call(
        functools.partial(attend_kernel, heads),
        grid=(streams, length // rows),
        in_specs=[
            pl.BlockSpec((1, rows, width), lambda m, i: (m, i, 0)),
            pl.BlockSpec((1, length, width), lambda m, i: (m, 0, 0)),
            pl.BlockSpec((1, length, heads * HEAD_V), lambda m, i: (m, 0, 0)),
            pl.BlockSpec((1, rows, 1), lambda m, i: (m, i, 0)),
        ],
        out_specs=pl.BlockSpec((1, rows, heads * HEAD_V), lambda m, i: (m, i, 0)),
        out_shape=jax.ShapeDtypeStruct(value.shape, jnp.bfloat16),
        compiler_params=pltpu.CompilerParams(vmem_limit_bytes=48 * MIB),
        name="attend",
    )(query, key, value, first)


def attend_back_kernel(
    heads, q_ref, k_ref, v_ref, first_ref, att_ref, g_ref, gq_ref, gk_ref, gv_ref, gk_sum, gv_sum
):
    rows = q_ref.shape[1]
    step = pl.program_id(1)
    base = step * rows

    @pl.when(step == 0)
    def _():
        gk_sum[...] = jnp.zeros_like(gk_sum)
        gv_sum[...] = jnp.zeros_like(gv_sum)

    query, key = q_ref[0], k_ref[0]
    g_query = jnp.zeros(query.shape, jnp.float32)
    for head in range(heads):
        columns = slice(head * HEAD_V, (head + 1) * HEAD_V)
        scores, mask, weight = weights_of(query, key, head, first_ref[0], base)
        denom = jnp.sum(weight, axis=1, keepdims=True)
        a = (g_ref[0, :, columns].astype(jnp.float32) / denom).astype(jnp.bfloat16)
        b = -jnp.sum(
            a.astype(jnp.float32) * att_ref[0, :, columns].astype(jnp.float32),
            axis=1,
            keepdims=True,
        )
        g_weight = contract(a, v_ref[0, :, columns], 1, 1) + b
        slope = 1.0 / math.sqrt(QK_DIM) + scores * (1.0 / QK_DIM)
        g_scores = jnp.where(mask, g_weight * slope, 0.0).astype(jnp.bfloat16)
        g_query += head_lanes(dot(g_scores, key), head)
        gk_sum[...] += contract(g_scores, head_lanes(query, head), 0, 0)
        gv_sum[:, columns] += contract(weight.astype(jnp.bfloat16), a, 0, 0)
    gq_ref[0] = g_query.astype(jnp.bfloat16)

    @pl.when(step == pl.num_programs(1) - 1)
    def _():
        gk_ref[0] = gk_sum[...].astype(jnp.bfloat16)
        gv_ref[0] = gv_sum[...].astype(jnp.bfloat16)


def attend_back(query, key, value, first, attended, grad, heads):
    streams, length, width = query.shape
    rows = min(256, length)
    some = pl.BlockSpec((1, rows, width), lambda m, i: (m, i, 0))
    all_narrow = pl.BlockSpec((1, length, width), lambda m, i: (m, 0, 0))
    all_wide = pl.BlockSpec((1, length, heads * HEAD_V), lambda m, i: (m, 0, 0))
    some_wide = pl.BlockSpec((1, rows, heads * HEAD_V), lambda m, i: (m, i, 0))
    return pl.pallas_call(
        functools.partial(attend_back_kernel, heads),
        grid=(streams, length // rows),
        in_specs=[
            some,
            all_narrow,
            all_wide,
            pl.BlockSpec((1, rows, 1), lambda m, i: (m, i, 0)),
            some_wide,
            some_wide,
        ],
        out_specs=[some, all_narrow, all_wide],
        out_shape=[
            jax.ShapeDtypeStruct(query.shape, jnp.bfloat16),
            jax.ShapeDtypeStruct(key.shape, jnp.bfloat16),
            jax.ShapeDtypeStruct(value.shape, jnp.bfloat16),
        ],
        scratch_shapes=[
            pltpu.VMEM((length, width), jnp.float32),
            pltpu.VMEM((length, heads * HEAD_V), jnp.float32),
        ],
        compiler_params=pltpu.CompilerParams(vmem_limit_bytes=56 * MIB),
        name="attend_back",
    )(query, key, value, first, attended, grad)

MESH = pl.DeviceIdType.MESH
LOW = jnp.bfloat16


def partners():
    me = lax.axis_index("seq")
    core, x, y = me % 2, me // 2 % 2, me // 4
    return me, me + 1 - 2 * core, me + 2 - 4 * x, me + 4 - 8 * y


def greet(others):
    barrier = pltpu.get_barrier_semaphore()
    for other in others:
        pl.semaphore_signal(barrier, inc=1, device_id={"seq": other}, device_id_type=MESH)
    pl.semaphore_wait(barrier, len(others))


def remote(send, recv, k, src, dst, to):
    return pltpu.make_async_remote_copy(
        src_ref=src,
        dst_ref=dst,
        send_sem=send.at[k],
        recv_sem=recv.at[k],
        device_id={"seq": to},
        device_id_type=MESH,
    )


def gather_kernel(x_ref, o_ref, send, recv, own_sem):
    me, sib, xn, yn = partners()
    diag = xn + yn - me
    half = x_ref.shape[0] // 2
    copy = functools.partial(remote, send, recv)
    upper, lower = pl.ds(0, half), pl.ds(half, half)
    greet((sib, xn, yn))
    own = pltpu.make_async_copy(x_ref, o_ref.at[me], own_sem)
    own.start()
    xa = copy(0, x_ref.at[upper], o_ref.at[me, upper], xn)
    yb = copy(1, x_ref.at[lower], o_ref.at[me, lower], yn)
    xb = copy(2, x_ref.at[lower], o_ref.at[me, lower], xn)
    ya = copy(3, x_ref.at[upper], o_ref.at[me, upper], yn)
    beside = [copy(4, x_ref, o_ref.at[me], sib)]
    started = [xa, yb, xb, ya, beside[0]]
    for c in started:
        c.start()

    def pass_on(k, origin, part, to):
        block = o_ref.at[origin, part]
        c = copy(k, block, block, to)
        c.start()
        started.append(c)
        return c

    xa.wait_recv()
    fy = pass_on(5, xn, upper, yn)
    beside.append(pass_on(6, xn, upper, sib))
    yb.wait_recv()
    fx = pass_on(7, yn, lower, xn)
    beside.append(pass_on(8, yn, lower, sib))
    xb.wait_recv()
    beside.append(pass_on(9, xn, lower, sib))
    ya.wait_recv()
    beside.append(pass_on(10, yn, upper, sib))
    fy.wait_recv()
    beside.append(pass_on(11, diag, upper, sib))
    fx.wait_recv()
    beside.append(pass_on(12, diag, lower, sib))
    own.wait()
    for c in beside:
        c.wait_recv()
    for c in started:
        c.wait_send()


def moved(nbytes):
    return pl.CostEstimate(flops=0, bytes_accessed=nbytes * 10, transcendentals=0)


def gather_plane(x, number):
    pieces = lax.axis_size("seq")
    if pieces != 8:
        return lax.all_gather(x, "seq", axis=0)
    return pl.pallas_call(
        gather_kernel,
        out_shape=jax.ShapeDtypeStruct((8,) + x.shape, x.dtype),
        in_specs=[pl.BlockSpec(memory_space=pl.ANY)],
        out_specs=pl.BlockSpec(memory_space=pl.ANY),
        scratch_shapes=[
            pltpu.SemaphoreType.DMA((13,)),
            pltpu.SemaphoreType.DMA((13,)),
            pltpu.SemaphoreType.DMA,
        ],
        compiler_params=pltpu.CompilerParams(collective_id=number, has_side_effects=True),
        cost_estimate=moved(16 * x.size),
        name="gather",
    )(x)


def scatter_kernel(p_ref, o_ref, held, got, one, two, send, recv, own_sem):
    me, sib, xn, yn = partners()
    diag = xn + yn - me
    half = p_ref.shape[1] // 2
    copy = functools.partial(remote, send, recv)
    upper, lower = pl.ds(0, half), pl.ds(half, half)
    greet((sib, xn, yn))
    beside, loads = [], []
    for i, owner in enumerate((diag, xn, yn, me)):
        beside.append(copy(i, p_ref.at[owner + sib - me], got.at[i], sib))
        loads.append(pltpu.make_async_copy(p_ref.at[owner], held.at[i], own_sem.at[i]))
        beside[i].start()
        loads[i].start()

    def pair_sum(i):
        beside[i].wait_recv()
        loads[i].wait()
        held[i] = held[i] + got[i]

    pair_sum(0)
    x0 = copy(4, held.at[0, upper], one.at[0], xn)
    x0.start()
    y0 = copy(5, held.at[0, lower], one.at[1], yn)
    y0.start()
    pair_sum(1)
    x1 = copy(6, held.at[1, upper], one.at[2], xn)
    x1.start()
    pair_sum(2)
    y1 = copy(7, held.at[2, lower], one.at[3], yn)
    y1.start()
    pair_sum(3)
    x0.wait_recv()
    held[2, :half] = held[2, :half] + one[0]
    y2 = copy(8, held.at[2, upper], two.at[0], yn)
    y2.start()
    y0.wait_recv()
    held[1, half:] = held[1, half:] + one[1]
    x2 = copy(9, held.at[1, lower], two.at[1], xn)
    x2.start()
    x1.wait_recv()
    y1.wait_recv()
    y2.wait_recv()
    wide = jnp.float32
    o_ref[:half] = held[3, :half].astype(wide) + one[2].astype(wide) + two[0].astype(wide)
    x2.wait_recv()
    o_ref[half:] = held[3, half:].astype(wide) + one[3].astype(wide) + two[1].astype(wide)
    for c in (*beside, x0, y0, x1, y1, y2, x2):
        c.wait_send()


def scatter_plane(part, number):
    pieces, rows, columns = part.shape
    if pieces != 8:
        return lax.psum_scatter(part, "seq", scatter_dimension=0).astype(jnp.float32)
    return pl.pallas_call(
        scatter_kernel,
        out_shape=jax.ShapeDtypeStruct((rows, columns), jnp.float32),
        in_specs=[pl.BlockSpec(memory_space=pl.ANY)],
        out_specs=pl.BlockSpec(memory_space=pltpu.VMEM),
        scratch_shapes=[
            pltpu.VMEM((4, rows, columns), LOW),
            pltpu.VMEM((4, rows, columns), LOW),
            pltpu.VMEM((4, rows // 2, columns), LOW),
            pltpu.VMEM((2, rows // 2, columns), LOW),
            pltpu.SemaphoreType.DMA((10,)),
            pltpu.SemaphoreType.DMA((10,)),
            pltpu.SemaphoreType.DMA((4,)),
        ],
        compiler_params=pltpu.CompilerParams(
            collective_id=number, has_side_effects=True, vmem_limit_bytes=40 * MIB
        ),
        cost_estimate=moved(2 * part.size),
        name="scatter",
    )(part)


def exchange_kernel(x_ref, o_ref, send, recv, own_sem):
    me = lax.axis_index("seq")
    others = [lax.rem(me + i, 8) for i in range(1, 8)]
    greet(others)
    own = pltpu.make_async_copy(x_ref.at[me], o_ref.at[me], own_sem)
    own.start()
    copies = [
        remote(send, recv, i, x_ref.at[other], o_ref.at[me], other)
        for i, other in enumerate(others)
    ]
    for c in copies:
        c.start()
    own.wait()
    for c in copies:
        c.wait()


def exchange_plane(x, number):
    if lax.axis_size("seq") != 8:
        return lax.all_to_all(x, "seq", 0, 0)
    return pl.pallas_call(
        exchange_kernel,
        out_shape=jax.ShapeDtypeStruct(x.shape, x.dtype),
        in_specs=[pl.BlockSpec(memory_space=pl.ANY)],
        out_specs=pl.BlockSpec(memory_space=pl.ANY),
        scratch_shapes=[
            pltpu.SemaphoreType.DMA((7,)),
            pltpu.SemaphoreType.DMA((7,)),
            pltpu.SemaphoreType.DMA,
        ],
        compiler_params=pltpu.CompilerParams(collective_id=number, has_side_effects=True),
        cost_estimate=moved(4 * x.size),
        name="exchange",
    )(x)


CHUNKS = (64, 64, 48)


class PlaneGather:
    def __init__(self, source, target, send, recv):
        me, sib, xn, yn = partners()
        diag = xn + yn - me
        half = target.shape[1] // 2
        upper, lower = pl.ds(0, half), pl.ds(half, half)
        copy = functools.partial(remote, send, recv)

        def direct(k, part, to):
            return copy(k, source.at[part], target.at[me, part], to)

        def pass_on(k, origin, part, to):
            return copy(k, target.at[origin, part], target.at[origin, part], to)

        self.xa, self.yb = direct(0, upper, xn), direct(1, lower, yn)
        self.xb, self.ya = direct(2, lower, xn), direct(3, upper, yn)
        self.s0 = copy(4, source, target.at[me], sib)
        self.fy, self.fx = pass_on(5, xn, upper, yn), pass_on(6, yn, lower, xn)
        self.s1, self.s2 = pass_on(7, xn, upper, sib), pass_on(8, yn, lower, sib)
        self.s3, self.s4 = pass_on(9, xn, lower, sib), pass_on(10, yn, upper, sib)
        self.s5, self.s6 = pass_on(11, diag, upper, sib), pass_on(12, diag, lower, sib)

    def start(self):
        for c in (self.xa, self.yb, self.xb, self.ya, self.s0):
            c.start()

    def forward_first(self):
        self.xa.wait_recv()
        self.yb.wait_recv()
        for c in (self.fy, self.fx, self.s1, self.s2):
            c.start()

    def forward_second(self):
        self.xb.wait_recv()
        self.ya.wait_recv()
        self.s3.start()
        self.s4.start()

    def forward_third(self):
        self.fy.wait_recv()
        self.fx.wait_recv()
        self.s5.start()
        self.s6.start()

    def from_sibling(self, chip):
        for c in {"own": (self.s0,), "x": (self.s1, self.s3), "y": (self.s2, self.s4), "diag": (self.s5, self.s6)}[chip]:
            c.wait_recv()

    def sent(self):
        for c in (self.xa, self.yb, self.xb, self.ya, self.s0, self.fy, self.fx):
            c.wait_send()
        for c in (self.s1, self.s2, self.s3, self.s4, self.s5, self.s6):
            c.wait_send()

    def arrive(self, step):
        @pl.when(step == 1)
        def _():
            self.from_sibling("own")

        @pl.when(step == 2)
        def _():
            self.forward_first()
            self.forward_second()
            self.from_sibling("x")

        @pl.when(step == 4)
        def _():
            self.from_sibling("y")

        @pl.when(step == 6)
        def _():
            self.forward_third()
            self.from_sibling("diag")


class LineGather:
    def __init__(self, item, source, block, send, recv, local):
        z = lax.axis_index("dp")
        self.z = z

        def copy(k, src, owner, to):
            return pltpu.make_async_remote_copy(
                src_ref=src,
                dst_ref=block(owner),
                send_sem=send.at[item, k],
                recv_sem=recv.at[item, owner],
                device_id={"dp": to},
                device_id_type=MESH,
            )

        self.sends = []
        for k, d in enumerate((2, -2, 1, -1)):
            to = z + d
            valid = (to >= 0) & (to < 4)
            self.sends.append((valid, copy(k, source, z, jnp.clip(to, 0, 3))))
        inner = (z == 1) | (z == 2)
        far = jnp.where(z == 1, 3, 0)
        self.stop = (inner, copy(4, block(far), far, jnp.where(z == 1, 0, 3)))
        others = [lax.rem(z + o, 4) for o in (1, 2, 3)]
        self.blocks = [copy(0, source, other, other) for other in others]
        self.own = pltpu.make_async_copy(source, block(z), local.at[item])

    def start(self):
        self.own.start()
        for valid, c in self.sends:

            @pl.when(valid)
            def _(c=c):
                c.start()

    def forward(self):
        inner, c = self.stop

        @pl.when(inner)
        def _():
            self.blocks[1].wait_recv()
            c.start()

    def wait(self):
        inner, unused = self.stop
        self.blocks[0].wait_recv()
        self.blocks[2].wait_recv()

        @pl.when(jnp.logical_not(inner))
        def _():
            self.blocks[1].wait_recv()

        self.own.wait()

    def sent(self):
        for valid, c in (*self.sends, self.stop):

            @pl.when(valid)
            def _(c=c):
                c.wait_send()


def nearest_first(step):
    me, sib, xn, yn = partners()
    chip = jnp.where(step < 4, xn, jnp.where(step < 6, yn, xn + yn - me))
    later = chip + jnp.where(lax.rem(step, 2) == 0, sib - me, 0)
    return jnp.where(step == 0, me, jnp.where(step == 1, sib, later))


def farthest_first(step):
    me, sib, xn, yn = partners()
    chip = jnp.where(step < 4, xn, yn)
    chip = jnp.where(step < 2, xn + yn - me, jnp.where(step < 6, chip, me))
    return chip + jnp.where(lax.rem(step, 2) == 0, sib - me, 0)


def layer_kernel(
    x_ref,
    c_ref,
    wa_ref,
    wo_ref,
    wgu_ref,
    wd_ref,
    gain_ref,
    first_ref,
    x_all,
    c_all,
    h2_all,
    wo_all,
    h1_out,
    q_out,
    k_out,
    v_out,
    att_out,
    tok_out,
    mid_out,
    wa_out,
    gain_out,
    out_part,
    gh_out,
    dgu_first,
    dd_first,
    dgu_out,
    dd_out,
    dgu_all,
    dd_all,
    wa,
    wgu,
    wd,
    gains,
    q_s,
    k_s,
    v_s,
    att_s,
    tok,
    mid,
    act_s,
    ggu_s,
    sum_gu,
    sum_d,
    x_buf,
    c_buf,
    o_buf,
    beside,
    held,
    got,
    one,
    two,
    gsend,
    grecv,
    zsend,
    zrecv,
    zlocal,
    esend,
    erecv,
    rsend,
    rrecv,
    load_sem,
    out_sem,
    h1_sem,
    w_sem,
    done_sem,
    self_sem,
    fsend,
    frecv,
    f_sem,
    gu_stop,
    d_stop,
):
    me, sib, xn, yn = partners()
    z = lax.axis_index("dp")
    rows, width = x_ref.shape
    span = rows // 2
    wide, qk = v_s.shape[2], q_s.shape[2]
    share = CHUNKS[0] + CHUNKS[1] + CHUNKS[2]
    half = rows // 2
    upper, lower = pl.ds(0, half), pl.ds(half, half)

    barrier = pltpu.get_barrier_semaphore()
    for i in range(1, 8):
        pl.semaphore_signal(
            barrier, inc=1, device_id={"seq": lax.rem(me + i, 8)}, device_id_type=MESH
        )
    for i in range(1, 4):
        pl.semaphore_signal(
            barrier, inc=1, device_id={"dp": lax.rem(z + i, 4)}, device_id_type=MESH
        )
    pl.semaphore_wait(barrier, 10)

    tokens = PlaneGather(x_ref, x_all, gsend.at[0], grecv.at[0])
    out_w = PlaneGather(wo_all.at[me], wo_all, gsend.at[1], grecv.at[1])
    cots = PlaneGather(c_ref, c_all, gsend.at[2], grecv.at[2])
    hidden_in = PlaneGather(held.at[0], h2_all, gsend.at[3], grecv.at[3])

    def line(item, source, block):
        return LineGather(item, source, block, zsend, zrecv, zlocal)

    depth = wa_ref.shape[0]

    def rows_of(ref, count, columns=None):
        def block(owner):
            if columns is None:
                return ref.at[pl.ds(owner * count, count)]
            return ref.at[pl.ds(owner * count, count), columns]

        return block

    z_gain = line(
        0, gain_ref, lambda owner: gains.at[:, pl.ds(pl.multiple_of(owner * depth, 128), depth)]
    )
    z_attn = line(1, wa_ref, rows_of(wa, depth))
    z_out = line(
        2,
        wo_ref.at[:, pl.ds(pl.multiple_of(me * wide, 128), wide)],
        lambda owner: wo_all.at[me, pl.ds(owner * depth, depth)],
    )
    z_up, z_down = [], []
    column, before = 0, 0
    columns, hiddens = [], []
    for k, count in enumerate(CHUNKS):
        part = pl.ds(column, 8 * count)
        z_up.append(line(3 + k, wgu_ref.at[:, part], rows_of(wgu, depth, part)))
        z_down.append(
            line(
                6 + k,
                wd_ref.at[pl.ds(me * share + before, count)],
                lambda owner, base=4 * before, count=count: wd.at[
                    pl.ds(base + owner * count, count)
                ],
            )
        )
        columns.append(column)
        hiddens.append(4 * before)
        column += 8 * count
        before += count

    tokens.start()
    z_gain.start()
    z_attn.start()

    def loads(order, step, sources):
        slot = lax.rem(step, 2)
        owner = order(step)
        return [
            pltpu.make_async_copy(source.at[owner], buf.at[slot], load_sem.at[i, slot])
            for i, (source, buf) in enumerate(sources)
        ]

    first_load = pltpu.make_async_copy(x_ref, x_buf.at[0], load_sem.at[0, 0])
    first_load.start()
    tokens.forward_first()
    z_gain.forward()
    z_attn.forward()
    tokens.forward_second()
    cots.start()
    z_gain.wait()
    z_attn.wait()
    z_out.start()

    def h1_copies(step):
        slot = lax.rem(step, 2)
        owner = nearest_first(step)
        return [
            pltpu.make_async_copy(
                o_buf.at[slot, pl.ds(m * span, span)],
                h1_out.at[m, pl.ds(owner * span, span)],
                h1_sem.at[m, slot],
            )
            for m in range(2)
        ]

    def arrive_tokens(step):
        @pl.when(step == 1)
        def _():
            tokens.from_sibling("own")

        @pl.when(step == 2)
        def _():
            tokens.from_sibling("x")

        @pl.when(step == 4)
        def _():
            tokens.forward_third()
            tokens.from_sibling("y")

        @pl.when(step == 3)
        def _():
            for g in (z_up[0], z_down[0]):
                g.start()

        @pl.when(step == 6)
        def _():
            tokens.from_sibling("diag")

        @pl.when(step == 7)
        def _():
            z_out.forward()

    token_source = [(x_all, x_buf)]

    def project(step, carry):
        slot = lax.rem(step, 2)
        owner = nearest_first(step)
        for c in loads(nearest_first, step, token_source):
            c.wait()

        @pl.when(step >= 2)
        def _():
            for c in h1_copies(step - 2):
                c.wait()

        x = x_buf[slot].astype(jnp.float32)
        gain = gains[0:1, :].astype(jnp.float32)
        h_one = (x * norm_scale(x) * gain).astype(LOW)
        o_buf[slot] = h_one
        for c in h1_copies(step):
            c.start()
        arrive_tokens(step + 1)

        @pl.when(step < 7)
        def _():
            for c in loads(nearest_first, step + 1, token_source):
                c.start()

        projected = dot(h_one, wa[...]).astype(LOW)
        for m in range(2):
            there = pl.ds(owner * span, span)
            mine = projected[m * span : (m + 1) * span]
            v_s[m, there, :] = mine[:, :wide]
            q_s[m, there, :] = mine[:, wide : wide + qk]
            k_s[m, there, :] = mine[:, wide + qk : wide + 2 * qk]
        return carry

    lax.fori_loop(0, 8, project, 0)
    for step in (6, 7):
        for c in h1_copies(step):
            c.wait()
    z_out.wait()
    out_w.start()
    for g in (z_up[1], z_down[1]):
        g.start()

    finals = [
        pltpu.make_async_copy(source, target, done_sem.at[i])
        for i, (source, target) in enumerate(
            (
                (q_s, q_out),
                (k_s, k_out),
                (v_s, v_out),
                (wa, wa_out),
                (gains, gain_out),
                (att_s, att_out),
                (tok, tok_out),
                (mid, mid_out),
            )
        )
    ]
    for c in finals[:5]:
        c.start()

    length = v_s.shape[1]
    block = 256

    def attend_stream(m, carry):
        for i in range(length // block):
            rows_i = slice(i * block, (i + 1) * block)
            seen = (i + 1) * block
            for head in range(wide // HEAD_V):
                lanes = slice(head * HEAD_V, (head + 1) * HEAD_V)
                unused, unused_mask, weight = weights_of(
                    q_s[m, rows_i, :], k_s[m, :seen, :], head, first_ref[m, rows_i, :], i * block
                )
                denom = jnp.sum(weight, axis=1, keepdims=True)
                numer = dot(weight.astype(LOW), v_s[m, :seen, lanes])
                att_s[m, rows_i, lanes] = (numer / denom).astype(LOW)
        return carry

    lax.fori_loop(0, 2, attend_stream, 0)
    out_w.forward_first()
    finals[5].start()

    to_mine = pl.ds(pl.multiple_of(me * wide, 128), wide)
    swaps = []
    for i in range(1, 8):
        other = lax.rem(me + i, 8)
        for m in range(2):
            swaps.append(
                remote(
                    esend,
                    erecv,
                    2 * (i - 1) + m,
                    att_s.at[m, pl.ds(other * span, span)],
                    tok.at[pl.ds(m * span, span), to_mine],
                    other,
                )
            )
            swaps[-1].start()
    kept = [
        pltpu.make_async_copy(
            att_s.at[m, pl.ds(me * span, span)],
            tok.at[pl.ds(m * span, span), to_mine],
            self_sem.at[m],
        )
        for m in range(2)
    ]
    for c in kept:
        c.start()
    x_load = pltpu.make_async_copy(x_ref, x_buf.at[0], load_sem.at[0, 0])
    x_load.start()

    def w_lanes(slot):
        return pl.ds(pl.multiple_of(slot * wide, 128), wide)

    def w_load(step):
        slot = lax.rem(step, 2)
        return pltpu.make_async_copy(
            wo_all.at[nearest_first(step)], act_s.at[:, w_lanes(slot)], w_sem.at[slot]
        )

    w_load(0).start()
    out_w.forward_second()
    cots.forward_first()
    cots.forward_second()
    z_up[0].forward()
    z_down[0].forward()
    for g in (z_up[2], z_down[2]):
        g.start()
    for c in kept:
        c.wait()
    for c in swaps:
        c.wait_recv()
    finals[6].start()
    x_load.wait()

    def arrive_out(step):
        @pl.when(step == 1)
        def _():
            out_w.from_sibling("own")

        @pl.when(step == 2)
        def _():
            out_w.from_sibling("x")

        @pl.when(step == 4)
        def _():
            out_w.forward_third()
            out_w.from_sibling("y")

        @pl.when(step == 6)
        def _():
            out_w.from_sibling("diag")

    def project_out(step, carry):
        slot = lax.rem(step, 2)
        owner = nearest_first(step)
        w_load(step).wait()
        arrive_out(step + 1)

        @pl.when(step < 7)
        def _():
            w_load(step + 1).start()

        there = pl.ds(pl.multiple_of(owner * wide, 128), wide)
        mid[:, there] = dot(tok[...], act_s[:, w_lanes(slot)])
        return carry

    lax.fori_loop(0, 8, project_out, 0)
    mid_value = x_buf[0].astype(jnp.float32) + mid[...]
    mid[...] = mid_value
    held[0] = (mid_value * norm_scale(mid_value) * gains[1:2, :].astype(jnp.float32)).astype(LOW)
    finals[7].start()
    hidden_in.start()
    own_h2 = pltpu.make_async_copy(held.at[0], h2_all.at[me], self_sem.at[2])
    own_c = pltpu.make_async_copy(c_ref, c_all.at[me], self_sem.at[3])
    own_h2.start()
    own_c.start()
    cots.forward_third()
    own_h2.wait()
    own_c.wait()
    z_up[0].wait()
    z_down[0].wait()

    largest = 4 * max(CHUNKS)
    sources = [(h2_all, x_buf), (c_all, c_buf)]

    def out_copy(order, step):
        slot = lax.rem(step, 2)
        return pltpu.make_async_copy(o_buf.at[slot], out_part.at[order(step)], out_sem.at[slot])

    def hidden_chunk(k, owner, h, c):
        count = 4 * CHUNKS[k]
        pair = pl.ds(columns[k], 2 * count)
        here = pl.ds(hiddens[k], count)
        both = dot(h, wgu[:, pair])
        gate, up = both[:, :count], both[:, count:]
        g_act = contract(c, wd[here, :], 1, 1)
        sigmoid = jax.nn.sigmoid(gate)
        silu = gate * sigmoid
        act = (silu * up).astype(LOW)
        g_gate = (g_act * up * sigmoid * (1.0 + gate * (1.0 - sigmoid))).astype(LOW)
        g_up = (g_act * silu).astype(LOW)
        there = pl.ds(owner * rows, rows)
        act_s[there, here] = act
        g_both = jnp.concatenate([g_gate, g_up], axis=1)
        ggu_s[there, pair] = g_both
        return act, g_both

    def add_grads(k, step, h, c, act, g_both):
        count = 4 * CHUNKS[k]

        to, low = (2 * largest, largest) if k == 1 else (0, 0)

        @pl.when(step == 0)
        def _():
            sum_gu[:, to : to + 2 * count] = jnp.zeros((width, 2 * count), jnp.float32)
            sum_d[low : low + count, :] = jnp.zeros((count, width), jnp.float32)

        sum_gu[:, to : to + 2 * count] += contract(h, g_both, 0, 0)
        sum_d[low : low + count, :] += contract(act, c, 0, 0)

    def emit(k):
        count = 4 * CHUNKS[k]
        rest = share - CHUNKS[0]
        to, low = (2 * largest, largest) if k == 1 else (0, 0)

        def gu_copies(i, slot):
            there = pl.ds(i * rows, rows)
            if k == 0:
                return [
                    pltpu.make_async_copy(
                        o_buf.at[slot, :, pl.ds(second * count, count)],
                        dgu_first.at[second, there],
                        h1_sem.at[second, slot],
                    )
                    for second in range(2)
                ]
            return [
                pltpu.make_async_copy(
                    o_buf.at[slot, :, pl.ds(0, 2 * count)],
                    dgu_out.at[there, pl.ds(columns[k] - columns[1], 2 * count)],
                    out_sem.at[slot],
                )
            ]

        def d_target(owner):
            if k == 0:
                return dd_first.at[pl.ds(owner * CHUNKS[0], CHUNKS[0])]
            start = owner * rest + (hiddens[k] - hiddens[1]) // 4
            return dd_out.at[pl.ds(start, CHUNKS[k])]

        pending = [[], []]
        for i in range(width // rows):
            slot = i % 2
            for c in pending[slot]:
                c.wait()
            total = sum_gu[i * rows : (i + 1) * rows, to : to + 2 * count]
            o_buf[slot, :, : 2 * count] = total.astype(LOW)
            pending[slot] = gu_copies(i, slot)
            for c in pending[slot]:
                c.start()
        for c in (*pending[0], *pending[1]):
            c.wait()
        o_buf[0, :count, :] = sum_d[low : low + count, :].astype(LOW)
        downs = []
        for owner in range(4):
            downs.append(
                pltpu.make_async_copy(
                    o_buf.at[0, pl.ds(owner * CHUNKS[k], CHUNKS[k])],
                    d_target(owner),
                    h1_sem.at[owner // 2, owner % 2],
                )
            )
            downs[-1].start()
        for c in downs:
            c.wait()

    def forward_pass(chunks, last, arrive, step, carry):
        slot = lax.rem(step, 2)
        for c in loads(nearest_first, step, sources):
            c.wait()
        h, c = x_buf[slot], c_buf[slot]
        made = [hidden_chunk(k, nearest_first(step), h, c) for k in chunks]
        if arrive is not None:
            arrive(step + 1)

        @pl.when(step < last)
        def _():
            for c in loads(nearest_first, step + 1, sources):
                c.start()

        for k, (act, g_both) in zip(chunks, made):
            add_grads(k, step, h, c, act, g_both)
        return carry

    def arrive_both(step):
        hidden_in.arrive(step)

        @pl.when(step == 1)
        def _():
            cots.from_sibling("own")

        @pl.when(step == 2)
        def _():
            cots.from_sibling("x")

        @pl.when(step == 4)
        def _():
            cots.from_sibling("y")

        @pl.when(step == 6)
        def _():
            cots.from_sibling("diag")

        @pl.when(step == 7)
        def _():
            z_up[2].forward()
            z_down[2].forward()

    for c in loads(nearest_first, 0, sources):
        c.start()

    def arrive_near(step):
        @pl.when(step < 4)
        def _():
            arrive_both(step)

    lax.fori_loop(0, 4, functools.partial(forward_pass, (0,), 3, arrive_near), 0)
    for c in loads(nearest_first, 0, sources):
        c.start()
    z_up[1].forward()
    z_down[1].forward()
    z_up[1].wait()
    z_down[1].wait()
    lax.fori_loop(0, 4, functools.partial(forward_pass, (1,), 3, None), 0)
    arrive_both(jnp.int32(4))
    for c in loads(nearest_first, 4, sources):
        c.start()
    lax.fori_loop(4, 8, functools.partial(forward_pass, (0, 1), 7, arrive_both), 0)
    hidden_in.sent()
    for c in loads(farthest_first, 0, sources):
        c.start()
    emit(0)
    sum_lines = [
        LineScatter(
            lambda owner: dgu_first.at[:, pl.ds(owner * depth, depth), :],
            dgu_all,
            gu_stop,
            att_s.at[:, pl.ds(0, depth), :],
            fsend.at[0],
            frecv.at[0],
            f_sem.at[0],
        ),
        LineScatter(
            lambda owner: dd_first.at[pl.ds(owner * CHUNKS[0], CHUNKS[0])],
            dd_all,
            d_stop,
            tok.at[pl.ds(0, CHUNKS[0])],
            fsend.at[1],
            frecv.at[1],
            f_sem.at[1],
        ),
    ]
    for c in swaps:
        c.wait_send()
    finals[5].wait()
    finals[6].wait()
    for g in sum_lines:
        g.start_first()

    z_up[2].wait()
    z_down[2].wait()

    copy = functools.partial(remote, rsend, rrecv)
    b_diag = copy(0, beside.at[0], got.at[2], sib)
    b_x = copy(1, beside.at[1], got.at[1], sib)
    b_y = copy(2, beside.at[0], got.at[3], sib)
    b_own = copy(3, beside.at[1], got.at[0], sib)
    x0 = copy(4, held.at[2, upper], one.at[0], xn)
    y0 = copy(5, held.at[2, lower], one.at[1], yn)
    x1 = copy(6, held.at[1, upper], one.at[2], xn)
    y1 = copy(7, held.at[3, lower], one.at[3], yn)
    y2 = copy(8, held.at[3, upper], two.at[0], yn)
    x2 = copy(9, held.at[1, lower], two.at[1], xn)

    def last_pass(step, carry):
        slot = lax.rem(step, 2)
        owner = farthest_first(step)
        there = pl.ds(owner * rows, rows)
        for c in loads(farthest_first, step, sources):
            c.wait()
        hidden_chunk(2, owner, x_buf[slot], c_buf[slot])

        @pl.when(step < 7)
        def _():
            for c in loads(farthest_first, step + 1, sources):
                c.start()

        part = contract(ggu_s[there, :], wgu[...], 1, 1).astype(LOW)

        @pl.when(step == 2)
        def _():
            for g in sum_lines:
                g.start()

        @pl.when(step == 6)
        def _():
            for g in sum_lines:
                g.join()

        for k, place, sent in ((0, 0, b_diag), (2, 1, b_x), (4, 0, b_y), (6, 1, b_own)):

            @pl.when(step == k)
            def _(k=k, place=place, sent=sent):
                if k == 4:
                    b_diag.wait_send()
                if k == 6:
                    b_x.wait_send()
                beside[place] = part
                sent.start()

        for k, place, arrived in ((1, 2, b_diag), (3, 1, b_x), (5, 3, b_y), (7, 0, b_own)):

            @pl.when(step == k)
            def _(k=k, place=place, arrived=arrived):
                arrived.wait_recv()
                held[place] = part + got[place]
                if k == 1:
                    x0.start()
                    y0.start()
                if k == 3:
                    x1.start()
                if k == 5:
                    y1.start()
                    y0.wait_recv()
                    held[1, half:] = held[1, half:] + one[1]
                    x2.start()
                    x0.wait_recv()
                    held[3, :half] = held[3, :half] + one[0]
                    y2.start()
        return carry

    lax.fori_loop(0, 8, last_pass, 0)
    for c in loads(farthest_first, 0, sources):
        c.start()

    def close_pass(step, carry):
        slot = lax.rem(step, 2)
        there = pl.ds(farthest_first(step) * rows, rows)
        for c in loads(farthest_first, step, sources):
            c.wait()

        @pl.when(step < 7)
        def _():
            for c in loads(farthest_first, step + 1, sources):
                c.start()

        @pl.when(step >= 2)
        def _():
            out_copy(farthest_first, step - 2).wait()

        o_buf[slot] = dot(act_s[there, :], wd[...]).astype(LOW)
        out_copy(farthest_first, step).start()
        act = act_s[there, pl.ds(hiddens[2], 4 * CHUNKS[2])]
        g_both = ggu_s[there, pl.ds(columns[2], 8 * CHUNKS[2])]
        add_grads(2, step, x_buf[slot], c_buf[slot], act, g_both)
        return carry

    lax.fori_loop(0, 8, close_pass, 0)
    out_copy(farthest_first, 6).wait()
    out_copy(farthest_first, 7).wait()
    emit(1)
    emit(2)
    f32 = jnp.float32
    x1.wait_recv()
    y2.wait_recv()
    for c in (*finals[:5], finals[7]):
        c.wait()
    mid[:half] = held[0, :half].astype(f32) + one[2].astype(f32) + two[0].astype(f32)
    y1.wait_recv()
    x2.wait_recv()
    mid[half:] = held[0, half:].astype(f32) + one[3].astype(f32) + two[1].astype(f32)
    gh_copy = pltpu.make_async_copy(mid, gh_out, done_sem.at[7])
    gh_copy.start()
    for g in sum_lines:
        g.wait()
    gh_copy.wait()
    for c in (b_y, b_own, x0, y0, x1, y1, y2, x2):
        c.wait_send()
    for g in (tokens, out_w, cots, z_gain, z_attn, z_out, *z_up, *z_down):
        g.sent()


def layer_front(tokens, cot, attn_slice, w_out, ffn_slice, w_down, gain_rows, first, wide, qk):
    rows, width = tokens.shape
    streams, length, unused = first.shape
    hidden = 4 * sum(CHUNKS)
    largest = 4 * max(CHUNKS)
    shape = jax.ShapeDtypeStruct
    f32 = jnp.float32
    anywhere = pl.BlockSpec(memory_space=pl.ANY)
    in_vmem = pl.BlockSpec(memory_space=pltpu.VMEM)
    plane = shape((8, rows, width), LOW)
    narrow = shape((streams, length, qk), LOW)
    broad = shape((streams, length, wide), LOW)
    attn_shape = (width, attn_slice.shape[1])
    out_shape = [
        plane,
        plane,
        plane,
        shape((8, width, width // 8), LOW),
        shape((streams, length, width), LOW),
        narrow,
        narrow,
        broad,
        broad,
        shape((rows, width), LOW),
        shape((rows, width), f32),
        shape(attn_shape, LOW),
        shape((gain_rows.shape[0], width), LOW),
        plane,
        shape((rows, width), f32),
        shape((2, width, 4 * CHUNKS[0]), LOW),
        shape((4 * CHUNKS[0], width), LOW),
        shape((width, 2 * hidden - 8 * CHUNKS[0]), LOW),
        shape((hidden - 4 * CHUNKS[0], width), LOW),
        shape((4, 2, width // 4, 4 * CHUNKS[0]), LOW),
        shape((4, CHUNKS[0], width), LOW),
    ]
    dma = pltpu.SemaphoreType.DMA
    vmem = pltpu.VMEM
    return pl.pallas_call(
        layer_kernel,
        out_shape=out_shape,
        in_specs=[anywhere] * 7 + [in_vmem],
        out_specs=[anywhere] * 21,
        scratch_shapes=[
            vmem(attn_shape, LOW),
            vmem((width, 2 * hidden), LOW),
            vmem((hidden, width), LOW),
            vmem((gain_rows.shape[0], width), LOW),
            vmem(narrow.shape, LOW),
            vmem(narrow.shape, LOW),
            vmem(broad.shape, LOW),
            vmem(broad.shape, LOW),
            vmem((rows, width), LOW),
            vmem((rows, width), f32),
            vmem((8 * rows, hidden), LOW),
            vmem((8 * rows, 2 * hidden), LOW),
            vmem((width, 4 * largest), f32),
            vmem((2 * largest, width), f32),
            vmem((2, rows, width), LOW),
            vmem((2, rows, width), LOW),
            vmem((2, rows, width), LOW),
            vmem((2, rows, width), LOW),
            vmem((4, rows, width), LOW),
            vmem((4, rows, width), LOW),
            vmem((4, rows // 2, width), LOW),
            vmem((2, rows // 2, width), LOW),
            dma((4, 13)),
            dma((4, 13)),
            dma((9, 5)),
            dma((9, 4)),
            dma((9,)),
            dma((14,)),
            dma((14,)),
            dma((10,)),
            dma((10,)),
            dma((2, 2)),
            dma((2,)),
            dma((2, 2)),
            dma((2,)),
            dma((8,)),
            dma((4,)),
            dma((2, 5)),
            dma((2, 5)),
            dma((2, 2)),
            vmem((2, width // 4, 4 * CHUNKS[0]), LOW),
            vmem((CHUNKS[0], width), LOW),
        ],
        compiler_params=pltpu.CompilerParams(
            collective_id=21, has_side_effects=True, vmem_limit_bytes=63 * MIB
        ),
        cost_estimate=pl.CostEstimate(
            flops=6 * 3 * 8 * rows * width * hidden,
            bytes_accessed=400 * rows * width,
            transcendentals=0,
        ),
        name="layer",
    )(tokens, cot, attn_slice, w_out, ffn_slice, w_down, gain_rows, first)


class LineScatter:
    def __init__(self, block, target, stop, mine, send, recv, local):
        z = lax.axis_index("dp")
        self.z, self.stop, self.mine = z, stop, mine
        self.inner = (z == 1) | (z == 2)
        self.outer = jnp.logical_not(self.inner)

        def copy(k, src, dst, at, to):
            return pltpu.make_async_remote_copy(
                src_ref=src,
                dst_ref=dst,
                send_sem=send.at[k],
                recv_sem=recv.at[at],
                device_id={"dp": to},
                device_id_type=MESH,
            )

        far = jnp.where(z < 2, 3, 0)
        near = jnp.where(z < 2, 1, 2)
        self.first = copy(0, block(far), stop, 4, jnp.where(self.inner, 3 - near, near))
        self.sends = []
        for k, d in enumerate((1, -1)):
            to = z + d
            valid = (to >= 0) & (to < 4)
            there = jnp.clip(to, 0, 3)
            self.sends.append((valid, copy(1 + k, block(there), target.at[z], z, there)))
        other = 3 - near
        self.sends.append((self.outer, copy(3, block(other), target.at[z], z, other)))
        self.own_far = pltpu.make_async_copy(block(far), mine, local.at[0])
        self.joined = copy(4, mine, target.at[z], z, far)
        self.own = pltpu.make_async_copy(block(z), target.at[z], local.at[1])
        self.arrivals = []
        for d in (1, -1, 2, -2):
            owner = z + d
            valid = (owner >= 0) & (owner < 4)
            there = jnp.clip(owner, 0, 3)
            self.arrivals.append((valid, copy(1, block(there), target.at[there], there, there)))

    def start_first(self):
        self.own.start()

        @pl.when(self.outer)
        def _():
            self.first.start()

        @pl.when(self.inner)
        def _():
            self.own_far.start()

    def start(self):
        for valid, c in self.sends:

            @pl.when(valid)
            def _(c=c):
                c.start()

    def join(self):
        @pl.when(self.inner)
        def _():
            self.first.wait_recv()
            self.own_far.wait()
            self.mine[...] = self.mine[...] + self.stop[...]
            self.joined.start()

    def wait(self):
        for valid, c in self.arrivals:

            @pl.when(valid)
            def _(c=c):
                c.wait_recv()

        self.own.wait()
        for valid, c in (*self.sends, (self.outer, self.first), (self.inner, self.joined)):

            @pl.when(valid)
            def _(c=c):
                c.wait_send()


class PlaneScatter:
    def __init__(self, beside, held, got, one, two, send, recv):
        me, sib, xn, yn = partners()
        half = got.shape[1] // 2
        self.half = half
        upper, lower = pl.ds(0, half), pl.ds(half, half)
        copy = functools.partial(remote, send, recv)
        self.held, self.got, self.one, self.two = held, got, one, two
        self.pairs = [copy(i, beside(i), got.at[i], sib) for i in range(4)]
        self.x0 = copy(4, held(2).at[upper], one.at[0], xn)
        self.y0 = copy(5, held(2).at[lower], one.at[1], yn)
        self.x1 = copy(6, held(1).at[upper], one.at[2], xn)
        self.y1 = copy(7, held(3).at[lower], one.at[3], yn)
        self.y2 = copy(8, held(3).at[upper], two.at[0], yn)
        self.x2 = copy(9, held(1).at[lower], two.at[1], xn)

    def start_pair(self, i):
        self.pairs[i].start()

    def start_pairs(self):
        for i in (2, 1, 3, 0):
            self.start_pair(i)

    def add_pair(self, i):
        self.pairs[i].wait_recv()
        block = self.held(i)
        block[...] = block[...] + self.got[i]
        for c in {0: (), 1: (self.x1,), 2: (self.x0, self.y0), 3: (self.y1,)}[i]:
            c.start()

    def add_pairs(self):
        for i in (2, 1, 3, 0):
            self.add_pair(i)

    def second(self):
        half = self.half
        self.y0.wait_recv()
        block = self.held(1)
        block[half:, :] = block[half:, :] + self.one[1]
        self.x2.start()
        self.x0.wait_recv()
        block = self.held(3)
        block[:half, :] = block[:half, :] + self.one[0]
        self.y2.start()

    def upper_sum(self):
        f32 = jnp.float32
        self.x1.wait_recv()
        self.y2.wait_recv()
        own = self.held(0)[: self.half, :].astype(f32)
        return own + self.one[2].astype(f32) + self.two[0].astype(f32)

    def lower_sum(self):
        f32 = jnp.float32
        self.y1.wait_recv()
        self.x2.wait_recv()
        own = self.held(0)[self.half :, :].astype(f32)
        return own + self.one[3].astype(f32) + self.two[1].astype(f32)

    def sent(self):
        for c in (*self.pairs, self.x0, self.y0, self.x1, self.y1, self.y2, self.x2):
            c.wait_send()


def chips():
    me, unused, xn, yn = partners()
    return me, xn, xn + yn - me, yn


def turn_kernel(
    gh_ref,
    mid_ref,
    c_ref,
    gain_ref,
    wo_all,
    part_ref,
    tok_ref,
    q_ref,
    k_ref,
    v_ref,
    att_ref,
    first_ref,
    h1_ref,
    output_ref,
    g_mid_out,
    g_out,
    gain_out,
    attn_ref,
    g_mid,
    work,
    g_low,
    g_att,
    g_heads,
    g_s,
    w_buf,
    go_part,
    held_o,
    got_g,
    one_g,
    two_g,
    got_o,
    one_o,
    two_o,
    gk_sum,
    gv_sum,
    h_buf,
    sums,
    esend,
    erecv,
    ssend,
    srecv,
    load_sem,
    w_sem,
    self_sem,
    done_sem,
    h_sem,
):
    me, sib, xn, yn = partners()
    flip = sib - me
    rows, width = g_low.shape
    span = rows // 2
    wide, qk = v_ref.shape[2], q_ref.shape[2]
    half = rows // 2
    greet([lax.rem(me + i, 8) for i in range(1, 8)])
    owners = chips()

    loads = [
        pltpu.make_async_copy(source, target, load_sem.at[i])
        for i, (source, target) in enumerate(
            ((gh_ref, g_mid), (mid_ref, work), (c_ref, g_low))
        )
    ]
    held_loads = [
        pltpu.make_async_copy(part_ref.at[owners[i]], held_o.at[i], load_sem.at[3 + i])
        for i in range(4)
    ]

    def w_load(step):
        slot = lax.rem(step, 2)
        return pltpu.make_async_copy(wo_all.at[step], w_buf.at[slot], w_sem.at[slot])

    for c in loads:
        c.start()
    w_load(0).start()
    outs = PlaneScatter(
        lambda i: part_ref.at[owners[i] + flip],
        lambda i: held_o.at[i],
        got_o,
        one_o,
        two_o,
        ssend.at[0],
        srecv.at[0],
    )
    weights = PlaneScatter(
        lambda i: go_part.at[owners[i] + flip],
        lambda i: go_part.at[owners[i]],
        got_g,
        one_g,
        two_g,
        ssend.at[1],
        srecv.at[1],
    )
    outs.start_pairs()
    for c in held_loads:
        c.start()
    for c in loads:
        c.wait()

    f32 = jnp.float32
    mid = work[...]
    inverse = norm_scale(mid)
    normed = mid * inverse
    grad = g_mid[...]
    gain_out[...] = jnp.broadcast_to(
        jnp.sum(grad * normed, axis=0, keepdims=True), gain_out.shape
    )
    gain = gain_ref[1:2, :].astype(f32)
    grad_mid = g_low[...].astype(f32) + norm_backward(grad, normed, inverse, gain)
    g_mid[...] = grad_mid
    g_low[...] = grad_mid.astype(LOW)
    done = [pltpu.make_async_copy(g_mid, g_mid_out, done_sem.at[0])]
    done[0].start()

    def back_out(step, carry):
        slot = lax.rem(step, 2)
        w_load(step).wait()

        @pl.when(step < 7)
        def _():
            w_load(step + 1).start()

        there = pl.ds(pl.multiple_of(step * wide, 128), wide)
        term = contract(g_low[:, there], w_buf[slot], 1, 1)

        @pl.when(step == 0)
        def _():
            work[...] = term

        @pl.when(step > 0)
        def _():
            work[...] += term

        return carry

    lax.fori_loop(0, 8, back_out, 0)
    g_att[...] = work[...].astype(LOW)
    mid_load = pltpu.make_async_copy(mid_ref, work, load_sem.at[1])
    mid_load.start()
    swaps = []
    here = pl.ds(me * span, span)
    for i in range(1, 8):
        other = lax.rem(me + i, 8)
        lanes = pl.ds(pl.multiple_of(other * wide, 128), wide)
        for m in range(2):
            swaps.append(
                remote(
                    esend,
                    erecv,
                    2 * (i - 1) + m,
                    g_att.at[pl.ds(m * span, span), lanes],
                    g_heads.at[m, here],
                    other,
                )
            )
            swaps[-1].start()
    kept = [
        pltpu.make_async_copy(
            g_att.at[pl.ds(m * span, span), pl.ds(pl.multiple_of(me * wide, 128), wide)],
            g_heads.at[m, here],
            self_sem.at[m],
        )
        for m in range(2)
    ]
    for c in kept:
        c.start()

    own = width // 32
    for z in range(4):
        lanes = slice(z * 8 * own, (z + 1) * 8 * own)
        block = contract(tok_ref[:, lanes], g_low[...], 0, 0).astype(LOW)
        for s in range(8):
            go_part[s, z * own : (z + 1) * own, :] = block[s * own : (s + 1) * own]
    weights.start_pairs()
    for c in kept:
        c.wait()
    for c in swaps:
        c.wait_recv()
    weights.add_pairs()

    length = v_ref.shape[1]
    block = 256
    streams = v_ref.shape[0]
    pieces = length // rows

    def h_load(step):
        slot = lax.rem(step, 2)
        return pltpu.make_async_copy(
            h1_ref.at[step // pieces, pl.ds(lax.rem(step, pieces) * rows, rows)],
            h_buf.at[slot],
            h_sem.at[slot],
        )

    h_load(0).start()

    def back_stream(m, carry):
        gk_sum[...] = jnp.zeros_like(gk_sum)
        gv_sum[...] = jnp.zeros_like(gv_sum)
        for i in range(length // block):
            rows_i = slice(i * block, (i + 1) * block)
            seen = (i + 1) * block
            query, key = q_ref[m, rows_i, :], k_ref[m, :seen, :]
            g_query = jnp.zeros(query.shape, f32)
            for head in range(wide // HEAD_V):
                lanes = slice(head * HEAD_V, (head + 1) * HEAD_V)
                scores, mask, weight = weights_of(
                    query, key, head, first_ref[m, rows_i, :], i * block
                )
                denom = jnp.sum(weight, axis=1, keepdims=True)
                a = (g_heads[m, rows_i, lanes].astype(f32) / denom).astype(LOW)
                b = -jnp.sum(
                    a.astype(f32) * att_ref[m, rows_i, lanes].astype(f32), axis=1, keepdims=True
                )
                g_weight = contract(a, v_ref[m, :seen, lanes], 1, 1) + b
                slope = 1.0 / math.sqrt(QK_DIM) + scores * (1.0 / QK_DIM)
                g_scores = jnp.where(mask, g_weight * slope, 0.0).astype(LOW)
                g_query += head_lanes(dot(g_scores, key), head)
                gk_sum[:seen, :] += contract(g_scores, head_lanes(query, head), 0, 0)
                gv_sum[:seen, lanes] += contract(weight.astype(LOW), a, 0, 0)
            g_s[m, rows_i, wide : wide + qk] = g_query.astype(LOW)
        g_s[m, :, :wide] = gv_sum[...].astype(LOW)
        g_s[m, :, wide + qk : wide + 2 * qk] = gk_sum[...].astype(LOW)
        g_s[m, :, wide + 2 * qk :] = jnp.zeros((length, g_s.shape[2] - wide - 2 * qk), LOW)

        @pl.when(m == 0)
        def _():
            for c in held_loads:
                c.wait()
            outs.add_pairs()

        return carry

    lax.fori_loop(0, 2, back_stream, 0)
    weights.second()
    done.append(pltpu.make_async_copy(g_s, g_out, done_sem.at[1]))
    done[1].start()
    outs.second()

    def add_grads(step, carry):
        slot = lax.rem(step, 2)
        h_load(step).wait()

        @pl.when(step < streams * pieces - 1)
        def _():
            h_load(step + 1).start()

        there = pl.ds(pl.multiple_of(lax.rem(step, pieces) * rows, rows), rows)
        term = contract(h_buf[slot], g_s[step // pieces, there, :], 0, 0)

        @pl.when(step == 0)
        def _():
            sums[...] = term

        @pl.when(step > 0)
        def _():
            sums[...] += term

        return carry

    lax.fori_loop(0, streams * pieces, add_grads, 0)
    narrow = sums.shape[1]
    attn_ref[:, :narrow] = sums[...].astype(LOW)
    mid_load.wait()
    for part, total in enumerate((weights.upper_sum(), weights.lower_sum())):
        total = total.astype(LOW)
        for z in range(2):
            for i in range(8):
                start = ((2 * part + z) * 8 + i) * own
                attn_ref[start : start + own, narrow:] = total[
                    z * own : (z + 1) * own, i * wide : (i + 1) * wide
                ]
    output_ref[:half] = (work[:half] + outs.upper_sum()).astype(LOW)
    output_ref[half:] = (work[half:] + outs.lower_sum()).astype(LOW)
    for c in done:
        c.wait()
    for c in swaps:
        c.wait_send()
    weights.sent()
    outs.sent()


def layer_turn(gh, mid, cot, gains, wo_all, part, tok, query, key, value, att, first, h1, columns):
    rows, width = mid.shape
    streams, length, wide = value.shape
    qk = query.shape[2]
    shape = jax.ShapeDtypeStruct
    f32 = jnp.float32
    anywhere = pl.BlockSpec(memory_space=pl.ANY)
    in_vmem = pl.BlockSpec(memory_space=pltpu.VMEM)
    dma = pltpu.SemaphoreType.DMA
    vmem = pltpu.VMEM
    arriving = [
        vmem((4, rows, width), LOW),
        vmem((4, rows // 2, width), LOW),
        vmem((2, rows // 2, width), LOW),
    ]
    return pl.pallas_call(
        turn_kernel,
        out_shape=[
            shape((rows, width), LOW),
            shape((rows, width), f32),
            shape((streams, length, columns), LOW),
            shape((8, width), f32),
            shape((width, columns + wide), LOW),
        ],
        in_specs=[anywhere] * 3 + [in_vmem] + [anywhere] * 2 + [in_vmem] * 6 + [anywhere],
        out_specs=[in_vmem, anywhere, anywhere, in_vmem, in_vmem],
        scratch_shapes=[
            vmem((rows, width), f32),
            vmem((rows, width), f32),
            vmem((rows, width), LOW),
            vmem((rows, width), LOW),
            vmem((streams, length, wide), LOW),
            vmem((streams, length, columns), LOW),
            vmem((2, width, wide), LOW),
            vmem((8, rows, width), LOW),
            vmem((4, rows, width), LOW),
            *arriving,
            *arriving,
            vmem((length, qk), f32),
            vmem((length, wide), f32),
            vmem((2, rows, width), LOW),
            vmem((width, columns), f32),
            dma((14,)),
            dma((14,)),
            dma((2, 10)),
            dma((2, 10)),
            dma((7,)),
            dma((2,)),
            dma((2,)),
            dma((2,)),
            dma((2,)),
        ],
        compiler_params=pltpu.CompilerParams(
            collective_id=22, has_side_effects=True, vmem_limit_bytes=63 * MIB
        ),
        cost_estimate=moved(16 * rows * width),
        name="turn",
    )(gh, mid, cot, gains, wo_all, part, tok, query, key, value, att, first, h1)


def close_kernel(
    g_ref,
    wa_ref,
    g_mid_ref,
    x_ref,
    gain_ref,
    sum_ref,
    grad_ref,
    gains_ref,
    beside,
    held,
    got,
    one,
    two,
    gain_rows,
    gain_line,
    gain_columns,
    gain_plane,
    ssend,
    srecv,
    zsend,
    zrecv,
    esend,
    erecv,
    self_sem,
):
    me, sib, xn, yn = partners()
    z = lax.axis_index("dp")
    rows, width = x_ref.shape
    span = rows // 2
    half = rows // 2
    f32 = jnp.float32
    barrier = pltpu.get_barrier_semaphore()
    for i in range(1, 8):
        pl.semaphore_signal(
            barrier, inc=1, device_id={"seq": lax.rem(me + i, 8)}, device_id_type=MESH
        )
    for i in range(1, 4):
        pl.semaphore_signal(
            barrier, inc=1, device_id={"dp": lax.rem(z + i, 4)}, device_id_type=MESH
        )
    pl.semaphore_wait(barrier, 10)
    scatter = PlaneScatter(
        lambda i: beside.at[i], lambda i: held.at[i], got, one, two, ssend, srecv
    )
    def part_of(owner):
        there = pl.ds(pl.multiple_of(owner * span, span), span)
        grads = jnp.concatenate([g_ref[0, there, :], g_ref[1, there, :]], axis=0)
        return contract(grads, wa_ref[...], 1, 1).astype(LOW)

    owners = chips()
    for i in (2, 1, 3, 0):
        beside[i] = part_of(owners[i] + sib - me)
        scatter.start_pair(i)
        held[i] = part_of(owners[i])
        scatter.add_pair(i)

    scatter.second()

    x = x_ref[...].astype(f32)
    inverse = norm_scale(x)
    normed = x * inverse
    gain = gain_ref[0:1, :].astype(f32)

    def finish(start, g_h):
        part = slice(start, start + half)
        grad_ref[part] = g_mid_ref[part] + norm_backward(g_h, normed[part], inverse[part], gain)
        return jnp.sum(g_h * normed[part], axis=0, keepdims=True)

    gain_sum = finish(0, scatter.upper_sum()) + finish(half, scatter.lower_sum())

    both = jnp.concatenate([gain_sum, sum_ref[0:1, :], jnp.zeros((14, width), f32)], axis=0)
    gain_rows[...] = both.astype(LOW)
    depth = width // 4

    def lanes(owner):
        return pl.ds(pl.multiple_of(owner * depth, 128), depth)

    def over_line(k, to, owner):
        return pltpu.make_async_remote_copy(
            src_ref=gain_rows.at[:, lanes(to)],
            dst_ref=gain_line.at[owner],
            send_sem=zsend.at[k],
            recv_sem=zrecv.at[owner],
            device_id={"dp": to},
            device_id_type=MESH,
        )

    others = [lax.rem(z + o, 4) for o in (1, 2, 3)]
    sends = [over_line(k, other, z) for k, other in enumerate(others)]
    own = pltpu.make_async_copy(gain_rows.at[:, lanes(z)], gain_line.at[z], self_sem.at[0])
    own.start()
    for c in sends:
        c.start()
    own.wait()
    for other in others:
        over_line(0, other, other).wait_recv()
    total = gain_line[0].astype(f32)
    for k in range(1, 4):
        total = total + gain_line[k].astype(f32)
    entry = lax.broadcasted_iota(jnp.int32, (16, 128), 0)
    lane = lax.broadcasted_iota(jnp.int32, (16, 128), 1)
    pick = jnp.where(lane == entry, 1.0, 0.0).astype(LOW)
    gain_columns[...] = contract(total.astype(LOW), pick, 0, 0).astype(LOW)
    count = depth // 8
    own = pltpu.make_async_copy(
        gain_columns.at[pl.ds(me * count, count)], gain_plane.at[me], self_sem.at[1]
    )
    own.start()
    swaps = []
    for i in range(1, 8):
        other = lax.rem(me + i, 8)
        swaps.append(
            remote(
                esend,
                erecv,
                i - 1,
                gain_columns.at[pl.ds(other * count, count)],
                gain_plane.at[me],
                other,
            )
        )
        swaps[-1].start()
    own.wait()
    for c in swaps:
        c.wait_recv()
    total = gain_plane[0].astype(f32)
    for k in range(1, 8):
        total = total + gain_plane[k].astype(f32)
    gains_ref[...] = total
    scatter.sent()
    for c in (*sends, *swaps):
        c.wait_send()


def layer_close(g_all, wa, g_mid, tokens, gains, gain_sum):
    rows, width = tokens.shape
    shape = jax.ShapeDtypeStruct
    in_vmem = pl.BlockSpec(memory_space=pltpu.VMEM)
    dma = pltpu.SemaphoreType.DMA
    vmem = pltpu.VMEM
    return pl.pallas_call(
        close_kernel,
        out_shape=[
            shape((rows, width), jnp.float32),
            shape((width // 32, 128), jnp.float32),
        ],
        in_specs=[in_vmem] * 6,
        out_specs=[in_vmem, in_vmem],
        scratch_shapes=[
            vmem((4, rows, width), LOW),
            vmem((4, rows, width), LOW),
            vmem((4, rows, width), LOW),
            vmem((4, rows // 2, width), LOW),
            vmem((2, rows // 2, width), LOW),
            vmem((16, width), LOW),
            vmem((4, 16, width // 4), LOW),
            vmem((width // 4, 128), LOW),
            vmem((8, width // 32, 128), LOW),
            dma((10,)),
            dma((10,)),
            dma((3,)),
            dma((4,)),
            dma((7,)),
            dma((7,)),
            dma((2,)),
        ],
        compiler_params=pltpu.CompilerParams(
            collective_id=23, has_side_effects=True, vmem_limit_bytes=56 * MIB
        ),
        cost_estimate=moved(16 * rows * width),
        name="close",
    )(g_all, wa, g_mid, tokens, gains, gain_sum)


def ffn_lax(h_two, cot_all, gate_full, up_full, down_full):
    pieces, rows, width = cot_all.shape
    h_two_all = gather_plane(h_two, 5).reshape(-1, width)
    cot_all = cot_all.reshape(-1, width)
    gate = dot(h_two_all, gate_full)
    up = dot(h_two_all, up_full)
    g_act = contract(cot_all, down_full, 1, 1)
    sigmoid = jax.nn.sigmoid(gate)
    silu = gate * sigmoid
    act = (silu * up).astype(LOW)
    g_gate = (g_act * up * sigmoid * (1.0 + gate * (1.0 - sigmoid))).astype(LOW)
    g_up = (g_act * silu).astype(LOW)
    part = (contract(g_gate, gate_full, 1, 1) + contract(g_up, up_full, 1, 1)).astype(LOW)
    return (
        dot(act, down_full).astype(LOW).reshape(pieces, rows, width),
        scatter_plane(part.reshape(pieces, rows, width), 7),
        contract(h_two_all, g_gate, 0, 0).astype(LOW),
        contract(h_two_all, g_up, 0, 0).astype(LOW),
        contract(act, cot_all, 0, 0).astype(LOW),
    )


def norm_scale(rows):
    return lax.rsqrt(jnp.mean(rows * rows, axis=-1, keepdims=True) + epsilon)


def norm_backward(grad, normed, inverse, gain):
    scaled = grad * gain
    return inverse * (scaled - normed * jnp.mean(scaled * normed, axis=-1, keepdims=True))


def local(
    tokens,
    doc_lengths,
    w_query,
    w_key,
    w_value,
    w_out,
    w_gate,
    w_up,
    w_down,
    gain_attn,
    gain_mlp,
    cotangent,
):
    micro, span = tokens.shape[1:3]
    pieces, groups = lax.axis_size("seq"), lax.axis_size("dp")
    place = lax.axis_index("seq")
    length = pieces * span
    heads = max(1, HEADS // pieces)
    sharers = max(1, pieces // HEADS)
    streams = micro // sharers
    first_head = place // sharers * heads
    first_stream = place % sharers * streams
    qk, wide = heads * QK_DIM, heads * HEAD_V
    hidden = FF // pieces

    out_width = D // pieces
    rows_dp = w_gate.shape[0]
    share = hidden // groups
    block = FF // groups
    mine = micro * span
    fused = pieces == 8 and groups == 4 and micro == 2 and span == 128
    chunks = CHUNKS if fused else (share,)

    def hidden_columns(w):
        parts = [
            lax.dynamic_slice_in_dim(w, z * block + place * share, share, 1) for z in range(groups)
        ]
        edges = [sum(chunks[:k]) for k in range(len(chunks) + 1)]
        return [
            [part[:, edges[k] : edges[k + 1]] for part in parts] for k in range(len(chunks))
        ]

    gate_parts, up_parts = hidden_columns(w_gate), hidden_columns(w_up)
    ffn_slice = jnp.concatenate(
        [part for k in range(len(chunks)) for part in gate_parts[k] + up_parts[k]], axis=1
    )
    attn_parts = [
        lax.dynamic_slice_in_dim(w_value, first_head * HEAD_V, wide, 1),
        lax.dynamic_slice_in_dim(w_query, first_head * QK_DIM, qk, 1),
        lax.dynamic_slice_in_dim(w_key, first_head * QK_DIM, qk, 1),
    ]

    lengths = lax.dynamic_slice_in_dim(doc_lengths[0], first_stream, streams, 0)
    starts = jnp.cumsum(lengths, axis=1) - lengths
    position = jnp.arange(length, dtype=jnp.int32)
    begun = starts[:, None, :] <= position[None, :, None]
    first = jnp.max(jnp.where(begun, starts[:, None, :], 0), axis=2)[..., None]

    x_own = tokens[0].reshape(mine, D)
    flat = x_own.astype(jnp.float32)
    cot = cotangent[0].reshape(mine, D)

    def to_tokens(by_head):
        sent = by_head.reshape(streams, pieces, span, wide).transpose(1, 0, 2, 3)
        got = exchange_plane(sent, 3).reshape(pieces // sharers, micro, span, wide)
        return got.transpose(1, 2, 0, 3).reshape(mine, HEADS * HEAD_V)

    def to_heads(by_token):
        sent = by_token.reshape(micro, span, pieces // sharers, wide).transpose(2, 0, 1, 3)
        got = exchange_plane(sent.reshape(pieces, streams, span, wide), 4)
        return got.transpose(1, 0, 2, 3).reshape(streams, length, wide)

    if fused:
        attn_slice = jnp.concatenate(
            attn_parts + [jnp.zeros((rows_dp, 128 - 2 * qk), LOW)], axis=1
        )
        gain_rows = jnp.concatenate(
            [gain_attn[None], gain_mlp[None], jnp.zeros((14, rows_dp), LOW)], axis=0
        )
        front = layer_front(
            x_own, cot, attn_slice, w_out, ffn_slice, w_down, gain_rows, first, wide, qk
        )
        out_full, h_all, query, key, value, att_heads, attended, mid = front[3:11]
        attn_full, gain_rows_all, out_part, g_h_two = front[11:15]
        d_ffn, d_down, ffn_blocks, down_blocks = front[17:]
    else:

        def gather_dp(w):
            return lax.all_gather(w, "dp", axis=0, tiled=True)

        attn_got = gather_dp(
            jnp.concatenate(
                attn_parts
                + [
                    lax.dynamic_slice_in_dim(w_out, place * out_width, out_width, 1),
                    gain_attn[:, None],
                    gain_mlp[:, None],
                ],
                axis=1,
            )
        )
        ffn_full = gather_dp(ffn_slice)
        down_full = gather_dp(lax.dynamic_slice_in_dim(w_down, place * share, share, 0))
        value_full = attn_got[:, :wide]
        query_full = attn_got[:, wide : wide + qk]
        key_full = attn_got[:, wide + qk : wide + 2 * qk]
        out_full = gather_plane(attn_got[:, wide + 2 * qk : wide + 2 * qk + out_width], 2)
        gains = attn_got[:, wide + 2 * qk + out_width :].astype(jnp.float32)
        gain_one, gain_two = gains[:, 0], gains[:, 1]
        x_all = gather_plane(x_own, 1).reshape(pieces, micro, span, D).transpose(1, 0, 2, 3)
        x_all = lax.dynamic_slice_in_dim(x_all, first_stream, streams, 0).astype(jnp.float32)
        h_flat = (x_all * norm_scale(x_all) * gain_one).astype(LOW).reshape(streams * length, D)
        value = dot(h_flat, value_full).astype(LOW).reshape(streams, length, wide)
        query = dot(h_flat, query_full).astype(LOW).reshape(streams, length, qk)
        key = dot(h_flat, key_full).astype(LOW).reshape(streams, length, qk)
        att_heads = attend(query, key, value, first, heads)
        attended = to_tokens(att_heads)
        mid = flat + jnp.einsum(
            "tk,skn->tsn", attended, out_full, preferred_element_type=jnp.float32
        ).reshape(mine, D)
        h_two = (mid * norm_scale(mid) * gain_two).astype(LOW)
        out_part, g_h_two, d_gate, d_up, d_down = ffn_lax(
            h_two, gather_plane(cot, 6), ffn_full[:, :hidden], ffn_full[:, hidden:], down_full
        )
        d_ffn = jnp.concatenate([d_gate, d_up], axis=1)

    def scatter_dp(part):
        return lax.psum_scatter(part, "dp", scatter_dimension=0, tiled=True)

    own = rows_dp // pieces
    sum_ffn, sum_down = scatter_dp(d_ffn), scatter_dp(d_down)

    if fused:
        output, g_mid, g_all, gain_sum, grad_attn = layer_turn(
            g_h_two, mid, cot, gain_rows_all, out_full, out_part, attended, query, key, value,
            att_heads, first, h_all, attn_full.shape[1],
        )
        input_grad, gain_columns = layer_close(
            g_all, attn_full, g_mid, x_own, gain_rows_all, gain_sum
        )
    else:
        inverse_two = norm_scale(mid)
        plain_two = mid * inverse_two
        output = (mid + scatter_plane(out_part, 8)).astype(LOW)
        g_mid = cot.astype(jnp.float32) + norm_backward(g_h_two, plain_two, inverse_two, gain_two)
        g_mid_low = g_mid.astype(LOW)
        g_att = jnp.einsum(
            "tsn,skn->tk",
            g_mid_low.reshape(mine, pieces, out_width),
            out_full,
            preferred_element_type=jnp.float32,
        )
        g_att = to_heads(g_att.astype(LOW))
        g_query, g_key, g_value = attend_back(query, key, value, first, att_heads, g_att, heads)
        g_value = g_value.reshape(streams * length, wide)
        g_query = g_query.reshape(streams * length, qk)
        g_key = g_key.reshape(streams * length, qk)
        g_h_one_part = (
            contract(g_value, value_full, 1, 1)
            + contract(g_query, query_full, 1, 1)
            + contract(g_key, key_full, 1, 1)
        ).astype(LOW)
        g_h_one_part = g_h_one_part.reshape(streams, pieces, span, D).transpose(1, 0, 2, 3)
        if sharers > 1:
            padded = jnp.zeros((pieces, micro, span, D), LOW)
            g_h_one_part = lax.dynamic_update_slice_in_dim(padded, g_h_one_part, first_stream, 1)
        g_h_one = scatter_plane(g_h_one_part.reshape(pieces, mine, D), 9)
        inverse_one = norm_scale(flat)
        plain_one = flat * inverse_one
        input_grad = g_mid + norm_backward(g_h_one, plain_one, inverse_one, gain_one)
        grad_out = contract(attended, g_mid_low, 0, 0).astype(LOW)
        grad_out = grad_out.reshape(groups, pieces, own, D).transpose(1, 0, 2, 3)
        grad_out = scatter_plane(grad_out.reshape(pieces, groups * own, D), 10).astype(LOW)
        grad_out = scatter_dp(grad_out)
        grad_attn = jnp.concatenate(
            [
                contract(h_flat, g_value, 0, 0).astype(LOW),
                contract(h_flat, g_query, 0, 0).astype(LOW),
                contract(h_flat, g_key, 0, 0).astype(LOW),
                jnp.sum(g_h_one * plain_one, axis=0).astype(LOW)[:, None],
                jnp.sum(g_h_two * plain_two, axis=0).astype(LOW)[:, None],
            ],
            axis=1,
        )

    grad_attn, sum_ffn, sum_down = lax.optimization_barrier((grad_attn, sum_ffn, sum_down))
    grad_attn = scatter_dp(grad_attn)
    if fused:
        grad_out = grad_attn[:, -out_width:].reshape(pieces, own, out_width)
        grad_out = grad_out.transpose(1, 0, 2).reshape(own, D)
        grad_attn = grad_attn[:, :-out_width]
        far = jnp.abs(jnp.arange(4) - lax.axis_index("dp")) == 3
        ffn_blocks = jnp.where(far[:, None, None, None], 0.0, ffn_blocks.astype(jnp.float32))
        first_ffn = jnp.sum(ffn_blocks, axis=0).astype(LOW)
        first_ffn = jnp.concatenate([first_ffn[0], first_ffn[1]], axis=1)
        sum_ffn = jnp.concatenate([first_ffn, sum_ffn], axis=1)
        first_down = jnp.sum(jnp.where(far[:, None, None], 0.0, down_blocks.astype(jnp.float32)), axis=0)
        sum_down = jnp.concatenate([first_down, sum_down.astype(jnp.float32)], axis=0)
    ffn_got = exchange_plane(sum_ffn.reshape(pieces, own, 2 * hidden), 11).astype(jnp.float32)

    def by_hidden(second):
        parts, start = [], 0
        for count in chunks:
            begin = start + second * groups * count
            part = ffn_got[:, :, begin : begin + groups * count]
            parts.append(part.reshape(pieces, own, groups, count))
            start += 2 * groups * count
        whole = jnp.concatenate(parts, axis=3)
        return whole.transpose(1, 2, 0, 3).reshape(own, FF)

    grad_gate, grad_up = by_hidden(0), by_hidden(1)
    grad_attn, grad_gate, grad_up = lax.optimization_barrier((grad_attn, grad_gate, grad_up))
    attn_got = exchange_plane(grad_attn.reshape(pieces, own, -1), 12).astype(jnp.float32)
    if fused:
        grad_gains = gain_columns
    else:
        grad_gains = jnp.sum(attn_got[:, :, wide + 2 * qk : wide + 2 * qk + 2], axis=0)
    attn_got = jnp.sum(attn_got.reshape(pieces // sharers, sharers, own, -1), axis=1)

    def by_rows(block):
        return block.transpose(1, 0, 2).reshape(own, -1)

    return (
        output.reshape(tokens.shape),
        input_grad.reshape(tokens.shape),
        by_rows(attn_got[:, :, wide : wide + qk]),
        by_rows(attn_got[:, :, wide + qk : wide + 2 * qk]),
        by_rows(attn_got[:, :, :wide]),
        grad_out.astype(jnp.float32),
        grad_gate,
        grad_up,
        sum_down.astype(jnp.float32),
        grad_gains[:, 0],
        grad_gains[:, 1],
    )


def solution(mesh):
    by_token, by_row = P("dp", None, "seq", None), P("dp", None)
    grad_rows, grad_entries = P(("dp", "seq"), None), P(("dp", "seq"))
    return jax.shard_map(
        local,
        mesh=mesh,
        in_specs=(by_token, P("dp", None, None)) + (by_row,) * 7 + (P("dp"), P("dp"), by_token),
        out_specs=(by_token, by_token) + (grad_rows,) * 7 + (grad_entries,) * 2,
        check_vma=False,
    )
```

```python
import functools
import math

import jax
import jax.numpy as jnp
from jax import lax
from jax.experimental import pallas as pl
from jax.experimental.pallas import tpu as pltpu
from jax.sharding import PartitionSpec as P

D = 2048
HEADS = 16
QK_DIM = 16
FF = 5632
HEAD_V = 128
epsilon = 1e-06
MIB = 1024 * 1024


def dot(left, right):
    return jnp.dot(left, right, preferred_element_type=jnp.float32)


def contract(left, right, left_dim, right_dim):
    return lax.dot_general(
        left, right, (((left_dim,), (right_dim,)), ((), ())), preferred_element_type=jnp.float32
    )


def head_lanes(rows, head):
    lane = lax.broadcasted_iota(jnp.int32, rows.shape, 1)
    inside = (lane >= head * QK_DIM) & (lane < (head + 1) * QK_DIM)
    return jnp.where(inside, rows, jnp.zeros_like(rows))


def weights_of(query, key, head, first, base):
    scores = contract(head_lanes(query, head), key, 1, 1)
    row = base + lax.broadcasted_iota(jnp.int32, scores.shape, 0)
    column = lax.broadcasted_iota(jnp.int32, scores.shape, 1)
    mask = (column <= row) & (column >= first)
    poly = 1.0 + scores * (1.0 / math.sqrt(QK_DIM)) + scores * scores * (0.5 / QK_DIM)
    return scores, mask, jnp.where(mask, poly, 0.0)


def attend_kernel(heads, q_ref, k_ref, v_ref, first_ref, out_ref):
    rows = q_ref.shape[1]
    base = pl.program_id(1) * rows
    for head in range(heads):
        columns = slice(head * HEAD_V, (head + 1) * HEAD_V)
        unused, unused_mask, weight = weights_of(
            q_ref[0], k_ref[0], head, first_ref[0], base
        )
        denom = jnp.sum(weight, axis=1, keepdims=True)
        numer = dot(weight.astype(jnp.bfloat16), v_ref[0, :, columns])
        out_ref[0, :, columns] = (numer / denom).astype(jnp.bfloat16)


def attend(query, key, value, first, heads):
    streams, length, width = query.shape
    rows = min(256, length)
    return pl.pallas_call(
        functools.partial(attend_kernel, heads),
        grid=(streams, length // rows),
        in_specs=[
            pl.BlockSpec((1, rows, width), lambda m, i: (m, i, 0)),
            pl.BlockSpec((1, length, width), lambda m, i: (m, 0, 0)),
            pl.BlockSpec((1, length, heads * HEAD_V), lambda m, i: (m, 0, 0)),
            pl.BlockSpec((1, rows, 1), lambda m, i: (m, i, 0)),
        ],
        out_specs=pl.BlockSpec((1, rows, heads * HEAD_V), lambda m, i: (m, i, 0)),
        out_shape=jax.ShapeDtypeStruct(value.shape, jnp.bfloat16),
        compiler_params=pltpu.CompilerParams(vmem_limit_bytes=48 * MIB),
        name="attend",
    )(query, key, value, first)


def attend_back_kernel(
    heads, q_ref, k_ref, v_ref, first_ref, att_ref, g_ref, gq_ref, gk_ref, gv_ref, gk_sum, gv_sum
):
    rows = q_ref.shape[1]
    step = pl.program_id(1)
    base = step * rows

    @pl.when(step == 0)
    def _():
        gk_sum[...] = jnp.zeros_like(gk_sum)
        gv_sum[...] = jnp.zeros_like(gv_sum)

    query, key = q_ref[0], k_ref[0]
    g_query = jnp.zeros(query.shape, jnp.float32)
    for head in range(heads):
        columns = slice(head * HEAD_V, (head + 1) * HEAD_V)
        scores, mask, weight = weights_of(query, key, head, first_ref[0], base)
        denom = jnp.sum(weight, axis=1, keepdims=True)
        a = (g_ref[0, :, columns].astype(jnp.float32) / denom).astype(jnp.bfloat16)
        b = -jnp.sum(
            a.astype(jnp.float32) * att_ref[0, :, columns].astype(jnp.float32),
            axis=1,
            keepdims=True,
        )
        g_weight = contract(a, v_ref[0, :, columns], 1, 1) + b
        slope = 1.0 / math.sqrt(QK_DIM) + scores * (1.0 / QK_DIM)
        g_scores = jnp.where(mask, g_weight * slope, 0.0).astype(jnp.bfloat16)
        g_query += head_lanes(dot(g_scores, key), head)
        gk_sum[...] += contract(g_scores, head_lanes(query, head), 0, 0)
        gv_sum[:, columns] += contract(weight.astype(jnp.bfloat16), a, 0, 0)
    gq_ref[0] = g_query.astype(jnp.bfloat16)

    @pl.when(step == pl.num_programs(1) - 1)
    def _():
        gk_ref[0] = gk_sum[...].astype(jnp.bfloat16)
        gv_ref[0] = gv_sum[...].astype(jnp.bfloat16)


def attend_back(query, key, value, first, attended, grad, heads):
    streams, length, width = query.shape
    rows = min(256, length)
    some = pl.BlockSpec((1, rows, width), lambda m, i: (m, i, 0))
    all_narrow = pl.BlockSpec((1, length, width), lambda m, i: (m, 0, 0))
    all_wide = pl.BlockSpec((1, length, heads * HEAD_V), lambda m, i: (m, 0, 0))
    some_wide = pl.BlockSpec((1, rows, heads * HEAD_V), lambda m, i: (m, i, 0))
    return pl.pallas_call(
        functools.partial(attend_back_kernel, heads),
        grid=(streams, length // rows),
        in_specs=[
            some,
            all_narrow,
            all_wide,
            pl.BlockSpec((1, rows, 1), lambda m, i: (m, i, 0)),
            some_wide,
            some_wide,
        ],
        out_specs=[some, all_narrow, all_wide],
        out_shape=[
            jax.ShapeDtypeStruct(query.shape, jnp.bfloat16),
            jax.ShapeDtypeStruct(key.shape, jnp.bfloat16),
            jax.ShapeDtypeStruct(value.shape, jnp.bfloat16),
        ],
        scratch_shapes=[
            pltpu.VMEM((length, width), jnp.float32),
            pltpu.VMEM((length, heads * HEAD_V), jnp.float32),
        ],
        compiler_params=pltpu.CompilerParams(vmem_limit_bytes=56 * MIB),
        name="attend_back",
    )(query, key, value, first, attended, grad)

MESH = pl.DeviceIdType.MESH
LOW = jnp.bfloat16


def partners():
    me = lax.axis_index("seq")
    core, x, y = me % 2, me // 2 % 2, me // 4
    return me, me + 1 - 2 * core, me + 2 - 4 * x, me + 4 - 8 * y


def greet(others):
    barrier = pltpu.get_barrier_semaphore()
    for other in others:
        pl.semaphore_signal(barrier, inc=1, device_id={"seq": other}, device_id_type=MESH)
    pl.semaphore_wait(barrier, len(others))


def remote(send, recv, k, src, dst, to):
    return pltpu.make_async_remote_copy(
        src_ref=src,
        dst_ref=dst,
        send_sem=send.at[k],
        recv_sem=recv.at[k],
        device_id={"seq": to},
        device_id_type=MESH,
    )


def gather_kernel(x_ref, o_ref, send, recv, own_sem):
    me, sib, xn, yn = partners()
    diag = xn + yn - me
    half = x_ref.shape[0] // 2
    copy = functools.partial(remote, send, recv)
    upper, lower = pl.ds(0, half), pl.ds(half, half)
    greet((sib, xn, yn))
    own = pltpu.make_async_copy(x_ref, o_ref.at[me], own_sem)
    own.start()
    xa = copy(0, x_ref.at[upper], o_ref.at[me, upper], xn)
    yb = copy(1, x_ref.at[lower], o_ref.at[me, lower], yn)
    xb = copy(2, x_ref.at[lower], o_ref.at[me, lower], xn)
    ya = copy(3, x_ref.at[upper], o_ref.at[me, upper], yn)
    beside = [copy(4, x_ref, o_ref.at[me], sib)]
    started = [xa, yb, xb, ya, beside[0]]
    for c in started:
        c.start()

    def pass_on(k, origin, part, to):
        block = o_ref.at[origin, part]
        c = copy(k, block, block, to)
        c.start()
        started.append(c)
        return c

    xa.wait_recv()
    fy = pass_on(5, xn, upper, yn)
    beside.append(pass_on(6, xn, upper, sib))
    yb.wait_recv()
    fx = pass_on(7, yn, lower, xn)
    beside.append(pass_on(8, yn, lower, sib))
    xb.wait_recv()
    beside.append(pass_on(9, xn, lower, sib))
    ya.wait_recv()
    beside.append(pass_on(10, yn, upper, sib))
    fy.wait_recv()
    beside.append(pass_on(11, diag, upper, sib))
    fx.wait_recv()
    beside.append(pass_on(12, diag, lower, sib))
    own.wait()
    for c in beside:
        c.wait_recv()
    for c in started:
        c.wait_send()


def moved(nbytes):
    return pl.CostEstimate(flops=0, bytes_accessed=nbytes * 10, transcendentals=0)


def gather_plane(x, number):
    pieces = lax.axis_size("seq")
    if pieces != 8:
        return lax.all_gather(x, "seq", axis=0)
    return pl.pallas_call(
        gather_kernel,
        out_shape=jax.ShapeDtypeStruct((8,) + x.shape, x.dtype),
        in_specs=[pl.BlockSpec(memory_space=pl.ANY)],
        out_specs=pl.BlockSpec(memory_space=pl.ANY),
        scratch_shapes=[
            pltpu.SemaphoreType.DMA((13,)),
            pltpu.SemaphoreType.DMA((13,)),
            pltpu.SemaphoreType.DMA,
        ],
        compiler_params=pltpu.CompilerParams(collective_id=number, has_side_effects=True),
        cost_estimate=moved(16 * x.size),
        name="gather",
    )(x)


def scatter_kernel(p_ref, o_ref, held, got, one, two, send, recv, own_sem):
    me, sib, xn, yn = partners()
    diag = xn + yn - me
    half = p_ref.shape[1] // 2
    copy = functools.partial(remote, send, recv)
    upper, lower = pl.ds(0, half), pl.ds(half, half)
    greet((sib, xn, yn))
    beside, loads = [], []
    for i, owner in enumerate((diag, xn, yn, me)):
        beside.append(copy(i, p_ref.at[owner + sib - me], got.at[i], sib))
        loads.append(pltpu.make_async_copy(p_ref.at[owner], held.at[i], own_sem.at[i]))
        beside[i].start()
        loads[i].start()

    def pair_sum(i):
        beside[i].wait_recv()
        loads[i].wait()
        held[i] = held[i] + got[i]

    pair_sum(0)
    x0 = copy(4, held.at[0, upper], one.at[0], xn)
    x0.start()
    y0 = copy(5, held.at[0, lower], one.at[1], yn)
    y0.start()
    pair_sum(1)
    x1 = copy(6, held.at[1, upper], one.at[2], xn)
    x1.start()
    pair_sum(2)
    y1 = copy(7, held.at[2, lower], one.at[3], yn)
    y1.start()
    pair_sum(3)
    x0.wait_recv()
    held[2, :half] = held[2, :half] + one[0]
    y2 = copy(8, held.at[2, upper], two.at[0], yn)
    y2.start()
    y0.wait_recv()
    held[1, half:] = held[1, half:] + one[1]
    x2 = copy(9, held.at[1, lower], two.at[1], xn)
    x2.start()
    x1.wait_recv()
    y1.wait_recv()
    y2.wait_recv()
    wide = jnp.float32
    o_ref[:half] = held[3, :half].astype(wide) + one[2].astype(wide) + two[0].astype(wide)
    x2.wait_recv()
    o_ref[half:] = held[3, half:].astype(wide) + one[3].astype(wide) + two[1].astype(wide)
    for c in (*beside, x0, y0, x1, y1, y2, x2):
        c.wait_send()


def scatter_plane(part, number):
    pieces, rows, columns = part.shape
    if pieces != 8:
        return lax.psum_scatter(part, "seq", scatter_dimension=0).astype(jnp.float32)
    return pl.pallas_call(
        scatter_kernel,
        out_shape=jax.ShapeDtypeStruct((rows, columns), jnp.float32),
        in_specs=[pl.BlockSpec(memory_space=pl.ANY)],
        out_specs=pl.BlockSpec(memory_space=pltpu.VMEM),
        scratch_shapes=[
            pltpu.VMEM((4, rows, columns), LOW),
            pltpu.VMEM((4, rows, columns), LOW),
            pltpu.VMEM((4, rows // 2, columns), LOW),
            pltpu.VMEM((2, rows // 2, columns), LOW),
            pltpu.SemaphoreType.DMA((10,)),
            pltpu.SemaphoreType.DMA((10,)),
            pltpu.SemaphoreType.DMA((4,)),
        ],
        compiler_params=pltpu.CompilerParams(
            collective_id=number, has_side_effects=True, vmem_limit_bytes=40 * MIB
        ),
        cost_estimate=moved(2 * part.size),
        name="scatter",
    )(part)


def exchange_kernel(x_ref, o_ref, send, recv, own_sem):
    me = lax.axis_index("seq")
    others = [lax.rem(me + i, 8) for i in range(1, 8)]
    greet(others)
    own = pltpu.make_async_copy(x_ref.at[me], o_ref.at[me], own_sem)
    own.start()
    copies = [
        remote(send, recv, i, x_ref.at[other], o_ref.at[me], other)
        for i, other in enumerate(others)
    ]
    for c in copies:
        c.start()
    own.wait()
    for c in copies:
        c.wait()


def exchange_plane(x, number):
    if lax.axis_size("seq") != 8:
        return lax.all_to_all(x, "seq", 0, 0)
    return pl.pallas_call(
        exchange_kernel,
        out_shape=jax.ShapeDtypeStruct(x.shape, x.dtype),
        in_specs=[pl.BlockSpec(memory_space=pl.ANY)],
        out_specs=pl.BlockSpec(memory_space=pl.ANY),
        scratch_shapes=[
            pltpu.SemaphoreType.DMA((7,)),
            pltpu.SemaphoreType.DMA((7,)),
            pltpu.SemaphoreType.DMA,
        ],
        compiler_params=pltpu.CompilerParams(collective_id=number, has_side_effects=True),
        cost_estimate=moved(4 * x.size),
        name="exchange",
    )(x)


CHUNKS = (64, 64, 48)


class PlaneGather:
    def __init__(self, source, target, send, recv):
        me, sib, xn, yn = partners()
        diag = xn + yn - me
        half = target.shape[1] // 2
        upper, lower = pl.ds(0, half), pl.ds(half, half)
        copy = functools.partial(remote, send, recv)

        def direct(k, part, to):
            return copy(k, source.at[part], target.at[me, part], to)

        def pass_on(k, origin, part, to):
            return copy(k, target.at[origin, part], target.at[origin, part], to)

        self.xa, self.yb = direct(0, upper, xn), direct(1, lower, yn)
        self.xb, self.ya = direct(2, lower, xn), direct(3, upper, yn)
        self.s0 = copy(4, source, target.at[me], sib)
        self.fy, self.fx = pass_on(5, xn, upper, yn), pass_on(6, yn, lower, xn)
        self.s1, self.s2 = pass_on(7, xn, upper, sib), pass_on(8, yn, lower, sib)
        self.s3, self.s4 = pass_on(9, xn, lower, sib), pass_on(10, yn, upper, sib)
        self.s5, self.s6 = pass_on(11, diag, upper, sib), pass_on(12, diag, lower, sib)

    def start(self):
        for c in (self.xa, self.yb, self.xb, self.ya, self.s0):
            c.start()

    def forward_first(self):
        self.xa.wait_recv()
        self.yb.wait_recv()
        for c in (self.fy, self.fx, self.s1, self.s2):
            c.start()

    def forward_second(self):
        self.xb.wait_recv()
        self.ya.wait_recv()
        self.s3.start()
        self.s4.start()

    def forward_third(self):
        self.fy.wait_recv()
        self.fx.wait_recv()
        self.s5.start()
        self.s6.start()

    def from_sibling(self, chip):
        for c in {"own": (self.s0,), "x": (self.s1, self.s3), "y": (self.s2, self.s4), "diag": (self.s5, self.s6)}[chip]:
            c.wait_recv()

    def sent(self):
        for c in (self.xa, self.yb, self.xb, self.ya, self.s0, self.fy, self.fx):
            c.wait_send()
        for c in (self.s1, self.s2, self.s3, self.s4, self.s5, self.s6):
            c.wait_send()

    def arrive(self, step):
        @pl.when(step == 1)
        def _():
            self.from_sibling("own")

        @pl.when(step == 2)
        def _():
            self.forward_first()
            self.forward_second()
            self.from_sibling("x")

        @pl.when(step == 4)
        def _():
            self.from_sibling("y")

        @pl.when(step == 6)
        def _():
            self.forward_third()
            self.from_sibling("diag")


class LineGather:
    def __init__(self, item, source, block, send, recv, local):
        z = lax.axis_index("dp")
        self.z = z

        def copy(k, src, owner, to):
            return pltpu.make_async_remote_copy(
                src_ref=src,
                dst_ref=block(owner),
                send_sem=send.at[item, k],
                recv_sem=recv.at[item, owner],
                device_id={"dp": to},
                device_id_type=MESH,
            )

        self.sends = []
        for k, d in enumerate((2, -2, 1, -1)):
            to = z + d
            valid = (to >= 0) & (to < 4)
            self.sends.append((valid, copy(k, source, z, jnp.clip(to, 0, 3))))
        inner = (z == 1) | (z == 2)
        far = jnp.where(z == 1, 3, 0)
        self.stop = (inner, copy(4, block(far), far, jnp.where(z == 1, 0, 3)))
        others = [lax.rem(z + o, 4) for o in (1, 2, 3)]
        self.blocks = [copy(0, source, other, other) for other in others]
        self.own = pltpu.make_async_copy(source, block(z), local.at[item])

    def start(self):
        self.own.start()
        for valid, c in self.sends:

            @pl.when(valid)
            def _(c=c):
                c.start()

    def forward(self):
        inner, c = self.stop

        @pl.when(inner)
        def _():
            self.blocks[1].wait_recv()
            c.start()

    def wait(self):
        inner, unused = self.stop
        self.blocks[0].wait_recv()
        self.blocks[2].wait_recv()

        @pl.when(jnp.logical_not(inner))
        def _():
            self.blocks[1].wait_recv()

        self.own.wait()

    def sent(self):
        for valid, c in (*self.sends, self.stop):

            @pl.when(valid)
            def _(c=c):
                c.wait_send()


def nearest_first(step):
    me, sib, xn, yn = partners()
    chip = jnp.where(step < 4, xn, jnp.where(step < 6, yn, xn + yn - me))
    later = chip + jnp.where(lax.rem(step, 2) == 0, sib - me, 0)
    return jnp.where(step == 0, me, jnp.where(step == 1, sib, later))


def farthest_first(step):
    me, sib, xn, yn = partners()
    chip = jnp.where(step < 4, xn, yn)
    chip = jnp.where(step < 2, xn + yn - me, jnp.where(step < 6, chip, me))
    return chip + jnp.where(lax.rem(step, 2) == 0, sib - me, 0)


def layer_kernel(
    x_ref,
    c_ref,
    wa_ref,
    wo_ref,
    wgu_ref,
    wd_ref,
    gain_ref,
    first_ref,
    x_all,
    c_all,
    h2_all,
    wo_all,
    h1_out,
    q_out,
    k_out,
    v_out,
    att_out,
    tok_out,
    mid_out,
    wa_out,
    gain_out,
    out_part,
    gh_out,
    dgu_first,
    dd_first,
    dgu_out,
    dd_out,
    dgu_all,
    dd_all,
    wa,
    wgu,
    wd,
    gains,
    q_s,
    k_s,
    v_s,
    att_s,
    tok,
    mid,
    act_s,
    ggu_s,
    sum_gu,
    sum_d,
    x_buf,
    c_buf,
    o_buf,
    beside,
    held,
    got,
    one,
    two,
    gsend,
    grecv,
    zsend,
    zrecv,
    zlocal,
    esend,
    erecv,
    rsend,
    rrecv,
    load_sem,
    out_sem,
    h1_sem,
    w_sem,
    done_sem,
    self_sem,
    fsend,
    frecv,
    f_sem,
    gu_stop,
    d_stop,
):
    me, sib, xn, yn = partners()
    z = lax.axis_index("dp")
    rows, width = x_ref.shape
    span = rows // 2
    wide, qk = v_s.shape[2], q_s.shape[2]
    share = CHUNKS[0] + CHUNKS[1] + CHUNKS[2]
    half = rows // 2
    upper, lower = pl.ds(0, half), pl.ds(half, half)

    barrier = pltpu.get_barrier_semaphore()
    for i in range(1, 8):
        pl.semaphore_signal(
            barrier, inc=1, device_id={"seq": lax.rem(me + i, 8)}, device_id_type=MESH
        )
    for i in range(1, 4):
        pl.semaphore_signal(
            barrier, inc=1, device_id={"dp": lax.rem(z + i, 4)}, device_id_type=MESH
        )
    pl.semaphore_wait(barrier, 10)

    tokens = PlaneGather(x_ref, x_all, gsend.at[0], grecv.at[0])
    out_w = PlaneGather(wo_all.at[me], wo_all, gsend.at[1], grecv.at[1])
    cots = PlaneGather(c_ref, c_all, gsend.at[2], grecv.at[2])
    hidden_in = PlaneGather(held.at[0], h2_all, gsend.at[3], grecv.at[3])

    def line(item, source, block):
        return LineGather(item, source, block, zsend, zrecv, zlocal)

    depth = wa_ref.shape[0]

    def rows_of(ref, count, columns=None):
        def block(owner):
            if columns is None:
                return ref.at[pl.ds(owner * count, count)]
            return ref.at[pl.ds(owner * count, count), columns]

        return block

    z_gain = line(
        0, gain_ref, lambda owner: gains.at[:, pl.ds(pl.multiple_of(owner * depth, 128), depth)]
    )
    z_attn = line(1, wa_ref, rows_of(wa, depth))
    z_out = line(
        2,
        wo_ref.at[:, pl.ds(pl.multiple_of(me * wide, 128), wide)],
        lambda owner: wo_all.at[me, pl.ds(owner * depth, depth)],
    )
    z_up, z_down = [], []
    column, before = 0, 0
    columns, hiddens = [], []
    for k, count in enumerate(CHUNKS):
        part = pl.ds(column, 8 * count)
        z_up.append(line(3 + k, wgu_ref.at[:, part], rows_of(wgu, depth, part)))
        z_down.append(
            line(
                6 + k,
                wd_ref.at[pl.ds(me * share + before, count)],
                lambda owner, base=4 * before, count=count: wd.at[
                    pl.ds(base + owner * count, count)
                ],
            )
        )
        columns.append(column)
        hiddens.append(4 * before)
        column += 8 * count
        before += count

    tokens.start()
    z_gain.start()
    z_attn.start()

    def loads(order, step, sources):
        slot = lax.rem(step, 2)
        owner = order(step)
        return [
            pltpu.make_async_copy(source.at[owner], buf.at[slot], load_sem.at[i, slot])
            for i, (source, buf) in enumerate(sources)
        ]

    first_load = pltpu.make_async_copy(x_ref, x_buf.at[0], load_sem.at[0, 0])
    first_load.start()
    tokens.forward_first()
    z_gain.forward()
    z_attn.forward()
    tokens.forward_second()
    cots.start()
    z_gain.wait()
    z_attn.wait()
    z_out.start()

    def h1_copies(step):
        slot = lax.rem(step, 2)
        owner = nearest_first(step)
        return [
            pltpu.make_async_copy(
                o_buf.at[slot, pl.ds(m * span, span)],
                h1_out.at[m, pl.ds(owner * span, span)],
                h1_sem.at[m, slot],
            )
            for m in range(2)
        ]

    def arrive_tokens(step):
        @pl.when(step == 1)
        def _():
            tokens.from_sibling("own")

        @pl.when(step == 2)
        def _():
            tokens.from_sibling("x")

        @pl.when(step == 4)
        def _():
            tokens.forward_third()
            tokens.from_sibling("y")

        @pl.when(step == 3)
        def _():
            for g in (z_up[0], z_down[0]):
                g.start()

        @pl.when(step == 6)
        def _():
            tokens.from_sibling("diag")

        @pl.when(step == 7)
        def _():
            z_out.forward()

    token_source = [(x_all, x_buf)]

    def project(step, carry):
        slot = lax.rem(step, 2)
        owner = nearest_first(step)
        for c in loads(nearest_first, step, token_source):
            c.wait()

        @pl.when(step >= 2)
        def _():
            for c in h1_copies(step - 2):
                c.wait()

        x = x_buf[slot].astype(jnp.float32)
        gain = gains[0:1, :].astype(jnp.float32)
        h_one = (x * norm_scale(x) * gain).astype(LOW)
        o_buf[slot] = h_one
        for c in h1_copies(step):
            c.start()
        arrive_tokens(step + 1)

        @pl.when(step < 7)
        def _():
            for c in loads(nearest_first, step + 1, token_source):
                c.start()

        projected = dot(h_one, wa[...]).astype(LOW)
        for m in range(2):
            there = pl.ds(owner * span, span)
            mine = projected[m * span : (m + 1) * span]
            v_s[m, there, :] = mine[:, :wide]
            q_s[m, there, :] = mine[:, wide : wide + qk]
            k_s[m, there, :] = mine[:, wide + qk : wide + 2 * qk]
        return carry

    lax.fori_loop(0, 8, project, 0)
    for step in (6, 7):
        for c in h1_copies(step):
            c.wait()
    z_out.wait()
    out_w.start()
    for g in (z_up[1], z_down[1]):
        g.start()

    finals = [
        pltpu.make_async_copy(source, target, done_sem.at[i])
        for i, (source, target) in enumerate(
            (
                (q_s, q_out),
                (k_s, k_out),
                (v_s, v_out),
                (wa, wa_out),
                (gains, gain_out),
                (att_s, att_out),
                (tok, tok_out),
                (mid, mid_out),
            )
        )
    ]
    for c in finals[:5]:
        c.start()

    length = v_s.shape[1]
    block = 256

    def attend_stream(m, carry):
        for i in range(length // block):
            rows_i = slice(i * block, (i + 1) * block)
            seen = (i + 1) * block
            for head in range(wide // HEAD_V):
                lanes = slice(head * HEAD_V, (head + 1) * HEAD_V)
                unused, unused_mask, weight = weights_of(
                    q_s[m, rows_i, :], k_s[m, :seen, :], head, first_ref[m, rows_i, :], i * block
                )
                denom = jnp.sum(weight, axis=1, keepdims=True)
                numer = dot(weight.astype(LOW), v_s[m, :seen, lanes])
                att_s[m, rows_i, lanes] = (numer / denom).astype(LOW)
        return carry

    lax.fori_loop(0, 2, attend_stream, 0)
    out_w.forward_first()
    finals[5].start()

    to_mine = pl.ds(pl.multiple_of(me * wide, 128), wide)
    swaps = []
    for i in range(1, 8):
        other = lax.rem(me + i, 8)
        for m in range(2):
            swaps.append(
                remote(
                    esend,
                    erecv,
                    2 * (i - 1) + m,
                    att_s.at[m, pl.ds(other * span, span)],
                    tok.at[pl.ds(m * span, span), to_mine],
                    other,
                )
            )
            swaps[-1].start()
    kept = [
        pltpu.make_async_copy(
            att_s.at[m, pl.ds(me * span, span)],
            tok.at[pl.ds(m * span, span), to_mine],
            self_sem.at[m],
        )
        for m in range(2)
    ]
    for c in kept:
        c.start()
    x_load = pltpu.make_async_copy(x_ref, x_buf.at[0], load_sem.at[0, 0])
    x_load.start()

    def w_lanes(slot):
        return pl.ds(pl.multiple_of(slot * wide, 128), wide)

    def w_load(step):
        slot = lax.rem(step, 2)
        return pltpu.make_async_copy(
            wo_all.at[nearest_first(step)], act_s.at[:, w_lanes(slot)], w_sem.at[slot]
        )

    w_load(0).start()
    out_w.forward_second()
    cots.forward_first()
    cots.forward_second()
    z_up[0].forward()
    z_down[0].forward()
    for g in (z_up[2], z_down[2]):
        g.start()
    for c in kept:
        c.wait()
    for c in swaps:
        c.wait_recv()
    finals[6].start()
    x_load.wait()

    def arrive_out(step):
        @pl.when(step == 1)
        def _():
            out_w.from_sibling("own")

        @pl.when(step == 2)
        def _():
            out_w.from_sibling("x")

        @pl.when(step == 4)
        def _():
            out_w.forward_third()
            out_w.from_sibling("y")

        @pl.when(step == 6)
        def _():
            out_w.from_sibling("diag")

    def project_out(step, carry):
        slot = lax.rem(step, 2)
        owner = nearest_first(step)
        w_load(step).wait()
        arrive_out(step + 1)

        @pl.when(step < 7)
        def _():
            w_load(step + 1).start()

        there = pl.ds(pl.multiple_of(owner * wide, 128), wide)
        mid[:, there] = dot(tok[...], act_s[:, w_lanes(slot)])
        return carry

    lax.fori_loop(0, 8, project_out, 0)
    mid_value = x_buf[0].astype(jnp.float32) + mid[...]
    mid[...] = mid_value
    held[0] = (mid_value * norm_scale(mid_value) * gains[1:2, :].astype(jnp.float32)).astype(LOW)
    finals[7].start()
    hidden_in.start()
    own_h2 = pltpu.make_async_copy(held.at[0], h2_all.at[me], self_sem.at[2])
    own_c = pltpu.make_async_copy(c_ref, c_all.at[me], self_sem.at[3])
    own_h2.start()
    own_c.start()
    cots.forward_third()
    own_h2.wait()
    own_c.wait()
    z_up[0].wait()
    z_down[0].wait()

    largest = 4 * max(CHUNKS)
    sources = [(h2_all, x_buf), (c_all, c_buf)]

    def out_copy(order, step):
        slot = lax.rem(step, 2)
        return pltpu.make_async_copy(o_buf.at[slot], out_part.at[order(step)], out_sem.at[slot])

    def hidden_chunk(k, owner, h, c):
        count = 4 * CHUNKS[k]
        pair = pl.ds(columns[k], 2 * count)
        here = pl.ds(hiddens[k], count)
        both = dot(h, wgu[:, pair])
        gate, up = both[:, :count], both[:, count:]
        g_act = contract(c, wd[here, :], 1, 1)
        sigmoid = jax.nn.sigmoid(gate)
        silu = gate * sigmoid
        act = (silu * up).astype(LOW)
        g_gate = (g_act * up * sigmoid * (1.0 + gate * (1.0 - sigmoid))).astype(LOW)
        g_up = (g_act * silu).astype(LOW)
        there = pl.ds(owner * rows, rows)
        act_s[there, here] = act
        g_both = jnp.concatenate([g_gate, g_up], axis=1)
        ggu_s[there, pair] = g_both
        return act, g_both

    def add_grads(k, step, h, c, act, g_both):
        count = 4 * CHUNKS[k]

        to, low = (2 * largest, largest) if k == 1 else (0, 0)

        @pl.when(step == 0)
        def _():
            sum_gu[:, to : to + 2 * count] = jnp.zeros((width, 2 * count), jnp.float32)
            sum_d[low : low + count, :] = jnp.zeros((count, width), jnp.float32)

        sum_gu[:, to : to + 2 * count] += contract(h, g_both, 0, 0)
        sum_d[low : low + count, :] += contract(act, c, 0, 0)

    def emit(k):
        count = 4 * CHUNKS[k]
        rest = share - CHUNKS[0]
        to, low = (2 * largest, largest) if k == 1 else (0, 0)

        def gu_copies(i, slot):
            there = pl.ds(i * rows, rows)
            if k == 0:
                return [
                    pltpu.make_async_copy(
                        o_buf.at[slot, :, pl.ds(second * count, count)],
                        dgu_first.at[second, there],
                        h1_sem.at[second, slot],
                    )
                    for second in range(2)
                ]
            return [
                pltpu.make_async_copy(
                    o_buf.at[slot, :, pl.ds(0, 2 * count)],
                    dgu_out.at[there, pl.ds(columns[k] - columns[1], 2 * count)],
                    out_sem.at[slot],
                )
            ]

        def d_target(owner):
            if k == 0:
                return dd_first.at[pl.ds(owner * CHUNKS[0], CHUNKS[0])]
            start = owner * rest + (hiddens[k] - hiddens[1]) // 4
            return dd_out.at[pl.ds(start, CHUNKS[k])]

        pending = [[], []]
        for i in range(width // rows):
            slot = i % 2
            for c in pending[slot]:
                c.wait()
            total = sum_gu[i * rows : (i + 1) * rows, to : to + 2 * count]
            o_buf[slot, :, : 2 * count] = total.astype(LOW)
            pending[slot] = gu_copies(i, slot)
            for c in pending[slot]:
                c.start()
        for c in (*pending[0], *pending[1]):
            c.wait()
        o_buf[0, :count, :] = sum_d[low : low + count, :].astype(LOW)
        downs = []
        for owner in range(4):
            downs.append(
                pltpu.make_async_copy(
                    o_buf.at[0, pl.ds(owner * CHUNKS[k], CHUNKS[k])],
                    d_target(owner),
                    h1_sem.at[owner // 2, owner % 2],
                )
            )
            downs[-1].start()
        for c in downs:
            c.wait()

    def forward_pass(chunks, last, arrive, step, carry):
        slot = lax.rem(step, 2)
        for c in loads(nearest_first, step, sources):
            c.wait()
        h, c = x_buf[slot], c_buf[slot]
        made = [hidden_chunk(k, nearest_first(step), h, c) for k in chunks]
        if arrive is not None:
            arrive(step + 1)

        @pl.when(step < last)
        def _():
            for c in loads(nearest_first, step + 1, sources):
                c.start()

        for k, (act, g_both) in zip(chunks, made):
            add_grads(k, step, h, c, act, g_both)
        return carry

    def arrive_both(step):
        hidden_in.arrive(step)

        @pl.when(step == 1)
        def _():
            cots.from_sibling("own")

        @pl.when(step == 2)
        def _():
            cots.from_sibling("x")

        @pl.when(step == 4)
        def _():
            cots.from_sibling("y")

        @pl.when(step == 6)
        def _():
            cots.from_sibling("diag")

        @pl.when(step == 7)
        def _():
            z_up[2].forward()
            z_down[2].forward()

    for c in loads(nearest_first, 0, sources):
        c.start()

    def arrive_near(step):
        @pl.when(step < 4)
        def _():
            arrive_both(step)

    lax.fori_loop(0, 4, functools.partial(forward_pass, (0,), 3, arrive_near), 0)
    for c in loads(nearest_first, 0, sources):
        c.start()
    z_up[1].forward()
    z_down[1].forward()
    z_up[1].wait()
    z_down[1].wait()
    lax.fori_loop(0, 4, functools.partial(forward_pass, (1,), 3, None), 0)
    arrive_both(jnp.int32(4))
    for c in loads(nearest_first, 4, sources):
        c.start()
    lax.fori_loop(4, 8, functools.partial(forward_pass, (0, 1), 7, arrive_both), 0)
    hidden_in.sent()
    for c in loads(farthest_first, 0, sources):
        c.start()
    emit(0)
    sum_lines = [
        LineScatter(
            lambda owner: dgu_first.at[:, pl.ds(owner * depth, depth), :],
            dgu_all,
            gu_stop,
            att_s.at[:, pl.ds(0, depth), :],
            fsend.at[0],
            frecv.at[0],
            f_sem.at[0],
        ),
        LineScatter(
            lambda owner: dd_first.at[pl.ds(owner * CHUNKS[0], CHUNKS[0])],
            dd_all,
            d_stop,
            tok.at[pl.ds(0, CHUNKS[0])],
            fsend.at[1],
            frecv.at[1],
            f_sem.at[1],
        ),
    ]
    for c in swaps:
        c.wait_send()
    finals[5].wait()
    finals[6].wait()
    for g in sum_lines:
        g.start_first()

    z_up[2].wait()
    z_down[2].wait()

    copy = functools.partial(remote, rsend, rrecv)
    b_diag = copy(0, beside.at[0], got.at[2], sib)
    b_x = copy(1, beside.at[1], got.at[1], sib)
    b_y = copy(2, beside.at[0], got.at[3], sib)
    b_own = copy(3, beside.at[1], got.at[0], sib)
    x0 = copy(4, held.at[2, upper], one.at[0], xn)
    y0 = copy(5, held.at[2, lower], one.at[1], yn)
    x1 = copy(6, held.at[1, upper], one.at[2], xn)
    y1 = copy(7, held.at[3, lower], one.at[3], yn)
    y2 = copy(8, held.at[3, upper], two.at[0], yn)
    x2 = copy(9, held.at[1, lower], two.at[1], xn)

    def last_pass(step, carry):
        slot = lax.rem(step, 2)
        owner = farthest_first(step)
        there = pl.ds(owner * rows, rows)
        for c in loads(farthest_first, step, sources):
            c.wait()
        hidden_chunk(2, owner, x_buf[slot], c_buf[slot])

        @pl.when(step < 7)
        def _():
            for c in loads(farthest_first, step + 1, sources):
                c.start()

        part = contract(ggu_s[there, :], wgu[...], 1, 1).astype(LOW)

        @pl.when(step == 2)
        def _():
            for g in sum_lines:
                g.start()

        @pl.when(step == 6)
        def _():
            for g in sum_lines:
                g.join()

        for k, place, sent in ((0, 0, b_diag), (2, 1, b_x), (4, 0, b_y), (6, 1, b_own)):

            @pl.when(step == k)
            def _(k=k, place=place, sent=sent):
                if k == 4:
                    b_diag.wait_send()
                if k == 6:
                    b_x.wait_send()
                beside[place] = part
                sent.start()

        for k, place, arrived in ((1, 2, b_diag), (3, 1, b_x), (5, 3, b_y), (7, 0, b_own)):

            @pl.when(step == k)
            def _(k=k, place=place, arrived=arrived):
                arrived.wait_recv()
                held[place] = part + got[place]
                if k == 1:
                    x0.start()
                    y0.start()
                if k == 3:
                    x1.start()
                if k == 5:
                    y1.start()
                    y0.wait_recv()
                    held[1, half:] = held[1, half:] + one[1]
                    x2.start()
                    x0.wait_recv()
                    held[3, :half] = held[3, :half] + one[0]
                    y2.start()
        return carry

    lax.fori_loop(0, 8, last_pass, 0)
    for c in loads(farthest_first, 0, sources):
        c.start()

    def close_pass(step, carry):
        slot = lax.rem(step, 2)
        there = pl.ds(farthest_first(step) * rows, rows)
        for c in loads(farthest_first, step, sources):
            c.wait()

        @pl.when(step < 7)
        def _():
            for c in loads(farthest_first, step + 1, sources):
                c.start()

        @pl.when(step >= 2)
        def _():
            out_copy(farthest_first, step - 2).wait()

        o_buf[slot] = dot(act_s[there, :], wd[...]).astype(LOW)
        out_copy(farthest_first, step).start()
        act = act_s[there, pl.ds(hiddens[2], 4 * CHUNKS[2])]
        g_both = ggu_s[there, pl.ds(columns[2], 8 * CHUNKS[2])]
        add_grads(2, step, x_buf[slot], c_buf[slot], act, g_both)
        return carry

    lax.fori_loop(0, 8, close_pass, 0)
    out_copy(farthest_first, 6).wait()
    out_copy(farthest_first, 7).wait()
    emit(1)
    emit(2)
    f32 = jnp.float32
    x1.wait_recv()
    y2.wait_recv()
    for c in (*finals[:5], finals[7]):
        c.wait()
    mid[:half] = held[0, :half].astype(f32) + one[2].astype(f32) + two[0].astype(f32)
    y1.wait_recv()
    x2.wait_recv()
    mid[half:] = held[0, half:].astype(f32) + one[3].astype(f32) + two[1].astype(f32)
    gh_copy = pltpu.make_async_copy(mid, gh_out, done_sem.at[7])
    gh_copy.start()
    for g in sum_lines:
        g.wait()
    gh_copy.wait()
    for c in (b_y, b_own, x0, y0, x1, y1, y2, x2):
        c.wait_send()
    for g in (tokens, out_w, cots, z_gain, z_attn, z_out, *z_up, *z_down):
        g.sent()


def layer_front(tokens, cot, attn_slice, w_out, ffn_slice, w_down, gain_rows, first, wide, qk):
    rows, width = tokens.shape
    streams, length, unused = first.shape
    hidden = 4 * sum(CHUNKS)
    largest = 4 * max(CHUNKS)
    shape = jax.ShapeDtypeStruct
    f32 = jnp.float32
    anywhere = pl.BlockSpec(memory_space=pl.ANY)
    in_vmem = pl.BlockSpec(memory_space=pltpu.VMEM)
    plane = shape((8, rows, width), LOW)
    narrow = shape((streams, length, qk), LOW)
    broad = shape((streams, length, wide), LOW)
    attn_shape = (width, attn_slice.shape[1])
    out_shape = [
        plane,
        plane,
        plane,
        shape((8, width, width // 8), LOW),
        shape((streams, length, width), LOW),
        narrow,
        narrow,
        broad,
        broad,
        shape((rows, width), LOW),
        shape((rows, width), f32),
        shape(attn_shape, LOW),
        shape((gain_rows.shape[0], width), LOW),
        plane,
        shape((rows, width), f32),
        shape((2, width, 4 * CHUNKS[0]), LOW),
        shape((4 * CHUNKS[0], width), LOW),
        shape((width, 2 * hidden - 8 * CHUNKS[0]), LOW),
        shape((hidden - 4 * CHUNKS[0], width), LOW),
        shape((4, 2, width // 4, 4 * CHUNKS[0]), LOW),
        shape((4, CHUNKS[0], width), LOW),
    ]
    dma = pltpu.SemaphoreType.DMA
    vmem = pltpu.VMEM
    return pl.pallas_call(
        layer_kernel,
        out_shape=out_shape,
        in_specs=[anywhere] * 7 + [in_vmem],
        out_specs=[anywhere] * 21,
        scratch_shapes=[
            vmem(attn_shape, LOW),
            vmem((width, 2 * hidden), LOW),
            vmem((hidden, width), LOW),
            vmem((gain_rows.shape[0], width), LOW),
            vmem(narrow.shape, LOW),
            vmem(narrow.shape, LOW),
            vmem(broad.shape, LOW),
            vmem(broad.shape, LOW),
            vmem((rows, width), LOW),
            vmem((rows, width), f32),
            vmem((8 * rows, hidden), LOW),
            vmem((8 * rows, 2 * hidden), LOW),
            vmem((width, 4 * largest), f32),
            vmem((2 * largest, width), f32),
            vmem((2, rows, width), LOW),
            vmem((2, rows, width), LOW),
            vmem((2, rows, width), LOW),
            vmem((2, rows, width), LOW),
            vmem((4, rows, width), LOW),
            vmem((4, rows, width), LOW),
            vmem((4, rows // 2, width), LOW),
            vmem((2, rows // 2, width), LOW),
            dma((4, 13)),
            dma((4, 13)),
            dma((9, 5)),
            dma((9, 4)),
            dma((9,)),
            dma((14,)),
            dma((14,)),
            dma((10,)),
            dma((10,)),
            dma((2, 2)),
            dma((2,)),
            dma((2, 2)),
            dma((2,)),
            dma((8,)),
            dma((4,)),
            dma((2, 5)),
            dma((2, 5)),
            dma((2, 2)),
            vmem((2, width // 4, 4 * CHUNKS[0]), LOW),
            vmem((CHUNKS[0], width), LOW),
        ],
        compiler_params=pltpu.CompilerParams(
            collective_id=21, has_side_effects=True, vmem_limit_bytes=63 * MIB
        ),
        cost_estimate=pl.CostEstimate(
            flops=6 * 3 * 8 * rows * width * hidden,
            bytes_accessed=400 * rows * width,
            transcendentals=0,
        ),
        name="layer",
    )(tokens, cot, attn_slice, w_out, ffn_slice, w_down, gain_rows, first)


class LineScatter:
    def __init__(self, block, target, stop, mine, send, recv, local):
        z = lax.axis_index("dp")
        self.z, self.stop, self.mine = z, stop, mine
        self.inner = (z == 1) | (z == 2)
        self.outer = jnp.logical_not(self.inner)

        def copy(k, src, dst, at, to):
            return pltpu.make_async_remote_copy(
                src_ref=src,
                dst_ref=dst,
                send_sem=send.at[k],
                recv_sem=recv.at[at],
                device_id={"dp": to},
                device_id_type=MESH,
            )

        far = jnp.where(z < 2, 3, 0)
        near = jnp.where(z < 2, 1, 2)
        self.first = copy(0, block(far), stop, 4, jnp.where(self.inner, 3 - near, near))
        self.sends = []
        for k, d in enumerate((1, -1)):
            to = z + d
            valid = (to >= 0) & (to < 4)
            there = jnp.clip(to, 0, 3)
            self.sends.append((valid, copy(1 + k, block(there), target.at[z], z, there)))
        other = 3 - near
        self.sends.append((self.outer, copy(3, block(other), target.at[z], z, other)))
        self.own_far = pltpu.make_async_copy(block(far), mine, local.at[0])
        self.joined = copy(4, mine, target.at[z], z, far)
        self.own = pltpu.make_async_copy(block(z), target.at[z], local.at[1])
        self.arrivals = []
        for d in (1, -1, 2, -2):
            owner = z + d
            valid = (owner >= 0) & (owner < 4)
            there = jnp.clip(owner, 0, 3)
            self.arrivals.append((valid, copy(1, block(there), target.at[there], there, there)))

    def start_first(self):
        self.own.start()

        @pl.when(self.outer)
        def _():
            self.first.start()

        @pl.when(self.inner)
        def _():
            self.own_far.start()

    def start(self):
        for valid, c in self.sends:

            @pl.when(valid)
            def _(c=c):
                c.start()

    def join(self):
        @pl.when(self.inner)
        def _():
            self.first.wait_recv()
            self.own_far.wait()
            self.mine[...] = self.mine[...] + self.stop[...]
            self.joined.start()

    def wait(self):
        for valid, c in self.arrivals:

            @pl.when(valid)
            def _(c=c):
                c.wait_recv()

        self.own.wait()
        for valid, c in (*self.sends, (self.outer, self.first), (self.inner, self.joined)):

            @pl.when(valid)
            def _(c=c):
                c.wait_send()


class PlaneScatter:
    def __init__(self, beside, held, got, one, two, send, recv):
        me, sib, xn, yn = partners()
        half = got.shape[1] // 2
        self.half = half
        upper, lower = pl.ds(0, half), pl.ds(half, half)
        copy = functools.partial(remote, send, recv)
        self.held, self.got, self.one, self.two = held, got, one, two
        self.pairs = [copy(i, beside(i), got.at[i], sib) for i in range(4)]
        self.x0 = copy(4, held(2).at[upper], one.at[0], xn)
        self.y0 = copy(5, held(2).at[lower], one.at[1], yn)
        self.x1 = copy(6, held(1).at[upper], one.at[2], xn)
        self.y1 = copy(7, held(3).at[lower], one.at[3], yn)
        self.y2 = copy(8, held(3).at[upper], two.at[0], yn)
        self.x2 = copy(9, held(1).at[lower], two.at[1], xn)

    def start_pair(self, i):
        self.pairs[i].start()

    def start_pairs(self):
        for i in (2, 1, 3, 0):
            self.start_pair(i)

    def add_pair(self, i):
        self.pairs[i].wait_recv()
        block = self.held(i)
        block[...] = block[...] + self.got[i]
        for c in {0: (), 1: (self.x1,), 2: (self.x0, self.y0), 3: (self.y1,)}[i]:
            c.start()

    def add_pairs(self):
        for i in (2, 1, 3, 0):
            self.add_pair(i)

    def second(self):
        half = self.half
        self.y0.wait_recv()
        block = self.held(1)
        block[half:, :] = block[half:, :] + self.one[1]
        self.x2.start()
        self.x0.wait_recv()
        block = self.held(3)
        block[:half, :] = block[:half, :] + self.one[0]
        self.y2.start()

    def upper_sum(self):
        f32 = jnp.float32
        self.x1.wait_recv()
        self.y2.wait_recv()
        own = self.held(0)[: self.half, :].astype(f32)
        return own + self.one[2].astype(f32) + self.two[0].astype(f32)

    def lower_sum(self):
        f32 = jnp.float32
        self.y1.wait_recv()
        self.x2.wait_recv()
        own = self.held(0)[self.half :, :].astype(f32)
        return own + self.one[3].astype(f32) + self.two[1].astype(f32)

    def sent(self):
        for c in (*self.pairs, self.x0, self.y0, self.x1, self.y1, self.y2, self.x2):
            c.wait_send()


def chips():
    me, unused, xn, yn = partners()
    return me, xn, xn + yn - me, yn


def turn_kernel(
    gh_ref,
    mid_ref,
    c_ref,
    gain_ref,
    wo_all,
    part_ref,
    tok_ref,
    q_ref,
    k_ref,
    v_ref,
    att_ref,
    first_ref,
    h1_ref,
    output_ref,
    g_mid_out,
    g_out,
    gain_out,
    attn_ref,
    g_mid,
    work,
    g_low,
    g_att,
    g_heads,
    g_s,
    w_buf,
    go_part,
    held_o,
    got_g,
    one_g,
    two_g,
    got_o,
    one_o,
    two_o,
    gk_sum,
    gv_sum,
    h_buf,
    sums,
    esend,
    erecv,
    ssend,
    srecv,
    load_sem,
    w_sem,
    self_sem,
    done_sem,
    h_sem,
):
    me, sib, xn, yn = partners()
    flip = sib - me
    rows, width = g_low.shape
    span = rows // 2
    wide, qk = v_ref.shape[2], q_ref.shape[2]
    half = rows // 2
    greet([lax.rem(me + i, 8) for i in range(1, 8)])
    owners = chips()

    loads = [
        pltpu.make_async_copy(source, target, load_sem.at[i])
        for i, (source, target) in enumerate(
            ((gh_ref, g_mid), (mid_ref, work), (c_ref, g_low))
        )
    ]
    held_loads = [
        pltpu.make_async_copy(part_ref.at[owners[i]], held_o.at[i], load_sem.at[3 + i])
        for i in range(4)
    ]

    def w_load(step):
        slot = lax.rem(step, 2)
        return pltpu.make_async_copy(wo_all.at[step], w_buf.at[slot], w_sem.at[slot])

    for c in loads:
        c.start()
    w_load(0).start()
    outs = PlaneScatter(
        lambda i: part_ref.at[owners[i] + flip],
        lambda i: held_o.at[i],
        got_o,
        one_o,
        two_o,
        ssend.at[0],
        srecv.at[0],
    )
    weights = PlaneScatter(
        lambda i: go_part.at[owners[i] + flip],
        lambda i: go_part.at[owners[i]],
        got_g,
        one_g,
        two_g,
        ssend.at[1],
        srecv.at[1],
    )
    outs.start_pairs()
    for c in held_loads:
        c.start()
    for c in loads:
        c.wait()

    f32 = jnp.float32
    mid = work[...]
    inverse = norm_scale(mid)
    normed = mid * inverse
    grad = g_mid[...]
    gain_out[...] = jnp.broadcast_to(
        jnp.sum(grad * normed, axis=0, keepdims=True), gain_out.shape
    )
    gain = gain_ref[1:2, :].astype(f32)
    grad_mid = g_low[...].astype(f32) + norm_backward(grad, normed, inverse, gain)
    g_mid[...] = grad_mid
    g_low[...] = grad_mid.astype(LOW)
    done = [pltpu.make_async_copy(g_mid, g_mid_out, done_sem.at[0])]
    done[0].start()

    def back_out(step, carry):
        slot = lax.rem(step, 2)
        w_load(step).wait()

        @pl.when(step < 7)
        def _():
            w_load(step + 1).start()

        there = pl.ds(pl.multiple_of(step * wide, 128), wide)
        term = contract(g_low[:, there], w_buf[slot], 1, 1)

        @pl.when(step == 0)
        def _():
            work[...] = term

        @pl.when(step > 0)
        def _():
            work[...] += term

        return carry

    lax.fori_loop(0, 8, back_out, 0)
    g_att[...] = work[...].astype(LOW)
    mid_load = pltpu.make_async_copy(mid_ref, work, load_sem.at[1])
    mid_load.start()
    swaps = []
    here = pl.ds(me * span, span)
    for i in range(1, 8):
        other = lax.rem(me + i, 8)
        lanes = pl.ds(pl.multiple_of(other * wide, 128), wide)
        for m in range(2):
            swaps.append(
                remote(
                    esend,
                    erecv,
                    2 * (i - 1) + m,
                    g_att.at[pl.ds(m * span, span), lanes],
                    g_heads.at[m, here],
                    other,
                )
            )
            swaps[-1].start()
    kept = [
        pltpu.make_async_copy(
            g_att.at[pl.ds(m * span, span), pl.ds(pl.multiple_of(me * wide, 128), wide)],
            g_heads.at[m, here],
            self_sem.at[m],
        )
        for m in range(2)
    ]
    for c in kept:
        c.start()

    own = width // 32
    for z in range(4):
        lanes = slice(z * 8 * own, (z + 1) * 8 * own)
        block = contract(tok_ref[:, lanes], g_low[...], 0, 0).astype(LOW)
        for s in range(8):
            go_part[s, z * own : (z + 1) * own, :] = block[s * own : (s + 1) * own]
    weights.start_pairs()
    for c in kept:
        c.wait()
    for c in swaps:
        c.wait_recv()
    weights.add_pairs()

    length = v_ref.shape[1]
    block = 256
    streams = v_ref.shape[0]
    pieces = length // rows

    def h_load(step):
        slot = lax.rem(step, 2)
        return pltpu.make_async_copy(
            h1_ref.at[step // pieces, pl.ds(lax.rem(step, pieces) * rows, rows)],
            h_buf.at[slot],
            h_sem.at[slot],
        )

    h_load(0).start()

    def back_stream(m, carry):
        gk_sum[...] = jnp.zeros_like(gk_sum)
        gv_sum[...] = jnp.zeros_like(gv_sum)
        for i in range(length // block):
            rows_i = slice(i * block, (i + 1) * block)
            seen = (i + 1) * block
            query, key = q_ref[m, rows_i, :], k_ref[m, :seen, :]
            g_query = jnp.zeros(query.shape, f32)
            for head in range(wide // HEAD_V):
                lanes = slice(head * HEAD_V, (head + 1) * HEAD_V)
                scores, mask, weight = weights_of(
                    query, key, head, first_ref[m, rows_i, :], i * block
                )
                denom = jnp.sum(weight, axis=1, keepdims=True)
                a = (g_heads[m, rows_i, lanes].astype(f32) / denom).astype(LOW)
                b = -jnp.sum(
                    a.astype(f32) * att_ref[m, rows_i, lanes].astype(f32), axis=1, keepdims=True
                )
                g_weight = contract(a, v_ref[m, :seen, lanes], 1, 1) + b
                slope = 1.0 / math.sqrt(QK_DIM) + scores * (1.0 / QK_DIM)
                g_scores = jnp.where(mask, g_weight * slope, 0.0).astype(LOW)
                g_query += head_lanes(dot(g_scores, key), head)
                gk_sum[:seen, :] += contract(g_scores, head_lanes(query, head), 0, 0)
                gv_sum[:seen, lanes] += contract(weight.astype(LOW), a, 0, 0)
            g_s[m, rows_i, wide : wide + qk] = g_query.astype(LOW)
        g_s[m, :, :wide] = gv_sum[...].astype(LOW)
        g_s[m, :, wide + qk : wide + 2 * qk] = gk_sum[...].astype(LOW)
        g_s[m, :, wide + 2 * qk :] = jnp.zeros((length, g_s.shape[2] - wide - 2 * qk), LOW)

        @pl.when(m == 0)
        def _():
            for c in held_loads:
                c.wait()
            outs.add_pairs()

        return carry

    lax.fori_loop(0, 2, back_stream, 0)
    weights.second()
    done.append(pltpu.make_async_copy(g_s, g_out, done_sem.at[1]))
    done[1].start()
    outs.second()

    def add_grads(step, carry):
        slot = lax.rem(step, 2)
        h_load(step).wait()

        @pl.when(step < streams * pieces - 1)
        def _():
            h_load(step + 1).start()

        there = pl.ds(pl.multiple_of(lax.rem(step, pieces) * rows, rows), rows)
        term = contract(h_buf[slot], g_s[step // pieces, there, :], 0, 0)

        @pl.when(step == 0)
        def _():
            sums[...] = term

        @pl.when(step > 0)
        def _():
            sums[...] += term

        return carry

    lax.fori_loop(0, streams * pieces, add_grads, 0)
    narrow = sums.shape[1]
    attn_ref[:, :narrow] = sums[...].astype(LOW)
    mid_load.wait()
    for part, total in enumerate((weights.upper_sum(), weights.lower_sum())):
        total = total.astype(LOW)
        for z in range(2):
            for i in range(8):
                start = ((2 * part + z) * 8 + i) * own
                attn_ref[start : start + own, narrow:] = total[
                    z * own : (z + 1) * own, i * wide : (i + 1) * wide
                ]
    output_ref[:half] = (work[:half] + outs.upper_sum()).astype(LOW)
    output_ref[half:] = (work[half:] + outs.lower_sum()).astype(LOW)
    for c in done:
        c.wait()
    for c in swaps:
        c.wait_send()
    weights.sent()
    outs.sent()


def layer_turn(gh, mid, cot, gains, wo_all, part, tok, query, key, value, att, first, h1, columns):
    rows, width = mid.shape
    streams, length, wide = value.shape
    qk = query.shape[2]
    shape = jax.ShapeDtypeStruct
    f32 = jnp.float32
    anywhere = pl.BlockSpec(memory_space=pl.ANY)
    in_vmem = pl.BlockSpec(memory_space=pltpu.VMEM)
    dma = pltpu.SemaphoreType.DMA
    vmem = pltpu.VMEM
    arriving = [
        vmem((4, rows, width), LOW),
        vmem((4, rows // 2, width), LOW),
        vmem((2, rows // 2, width), LOW),
    ]
    return pl.pallas_call(
        turn_kernel,
        out_shape=[
            shape((rows, width), LOW),
            shape((rows, width), f32),
            shape((streams, length, columns), LOW),
            shape((8, width), f32),
            shape((width, columns + wide), LOW),
        ],
        in_specs=[anywhere] * 3 + [in_vmem] + [anywhere] * 2 + [in_vmem] * 6 + [anywhere],
        out_specs=[in_vmem, anywhere, anywhere, in_vmem, in_vmem],
        scratch_shapes=[
            vmem((rows, width), f32),
            vmem((rows, width), f32),
            vmem((rows, width), LOW),
            vmem((rows, width), LOW),
            vmem((streams, length, wide), LOW),
            vmem((streams, length, columns), LOW),
            vmem((2, width, wide), LOW),
            vmem((8, rows, width), LOW),
            vmem((4, rows, width), LOW),
            *arriving,
            *arriving,
            vmem((length, qk), f32),
            vmem((length, wide), f32),
            vmem((2, rows, width), LOW),
            vmem((width, columns), f32),
            dma((14,)),
            dma((14,)),
            dma((2, 10)),
            dma((2, 10)),
            dma((7,)),
            dma((2,)),
            dma((2,)),
            dma((2,)),
            dma((2,)),
        ],
        compiler_params=pltpu.CompilerParams(
            collective_id=22, has_side_effects=True, vmem_limit_bytes=63 * MIB
        ),
        cost_estimate=moved(16 * rows * width),
        name="turn",
    )(gh, mid, cot, gains, wo_all, part, tok, query, key, value, att, first, h1)


def close_kernel(
    g_ref,
    wa_ref,
    g_mid_ref,
    x_ref,
    gain_ref,
    sum_ref,
    blocks_ref,
    rest_ref,
    grad_ref,
    gains_ref,
    first_got,
    rest_got,
    beside,
    held,
    got,
    one,
    two,
    gain_rows,
    gain_line,
    gain_columns,
    gain_plane,
    blocks,
    first_sum,
    ssend,
    srecv,
    zsend,
    zrecv,
    esend,
    erecv,
    self_sem,
    fsend,
    frecv,
    f_sem,
):
    me, sib, xn, yn = partners()
    z = lax.axis_index("dp")
    rows, width = x_ref.shape
    span = rows // 2
    half = rows // 2
    f32 = jnp.float32
    barrier = pltpu.get_barrier_semaphore()
    for i in range(1, 8):
        pl.semaphore_signal(
            barrier, inc=1, device_id={"seq": lax.rem(me + i, 8)}, device_id_type=MESH
        )
    for i in range(1, 4):
        pl.semaphore_signal(
            barrier, inc=1, device_id={"dp": lax.rem(z + i, 4)}, device_id_type=MESH
        )
    pl.semaphore_wait(barrier, 10)
    load = pltpu.make_async_copy(blocks_ref, blocks, f_sem.at[0])
    load.start()
    keep = first_got.shape[1]

    def exchange(item, source, target):
        mine = pltpu.make_async_copy(
            source.at[pl.ds(me * keep, keep)], target.at[me], f_sem.at[1 + item]
        )
        mine.start()
        copies = []
        for i in range(1, 8):
            other = lax.rem(me + i, 8)
            copies.append(
                remote(
                    fsend,
                    frecv,
                    7 * item + i - 1,
                    source.at[pl.ds(other * keep, keep)],
                    target.at[me],
                    other,
                )
            )
            copies[-1].start()
        return mine, copies

    moves = [exchange(1, rest_ref, rest_got)]
    scatter = PlaneScatter(
        lambda i: beside.at[i], lambda i: held.at[i], got, one, two, ssend, srecv
    )
    def part_of(owner):
        there = pl.ds(pl.multiple_of(owner * span, span), span)
        grads = jnp.concatenate([g_ref[0, there, :], g_ref[1, there, :]], axis=0)
        return contract(grads, wa_ref[...], 1, 1).astype(LOW)

    owners = chips()
    for i in (2, 1, 3, 0):
        beside[i] = part_of(owners[i] + sib - me)
        scatter.start_pair(i)
        held[i] = part_of(owners[i])
        scatter.add_pair(i)

    load.wait()
    for second in range(2):
        total = jnp.zeros(blocks.shape[2:], f32)
        for owner in range(4):
            came = jnp.abs(z - owner) < 3
            total = total + jnp.where(came, blocks[owner, second].astype(f32), 0.0)
        lanes_here = total.shape[1]
        first_sum[:, second * lanes_here : (second + 1) * lanes_here] = total.astype(LOW)
    moves.append(exchange(0, first_sum, first_got))

    scatter.second()

    x = x_ref[...].astype(f32)
    inverse = norm_scale(x)
    normed = x * inverse
    gain = gain_ref[0:1, :].astype(f32)

    def finish(start, g_h):
        part = slice(start, start + half)
        grad_ref[part] = g_mid_ref[part] + norm_backward(g_h, normed[part], inverse[part], gain)
        return jnp.sum(g_h * normed[part], axis=0, keepdims=True)

    gain_sum = finish(0, scatter.upper_sum()) + finish(half, scatter.lower_sum())

    both = jnp.concatenate([gain_sum, sum_ref[0:1, :], jnp.zeros((14, width), f32)], axis=0)
    gain_rows[...] = both.astype(LOW)
    depth = width // 4

    def lanes(owner):
        return pl.ds(pl.multiple_of(owner * depth, 128), depth)

    def over_line(k, to, owner):
        return pltpu.make_async_remote_copy(
            src_ref=gain_rows.at[:, lanes(to)],
            dst_ref=gain_line.at[owner],
            send_sem=zsend.at[k],
            recv_sem=zrecv.at[owner],
            device_id={"dp": to},
            device_id_type=MESH,
        )

    others = [lax.rem(z + o, 4) for o in (1, 2, 3)]
    sends = [over_line(k, other, z) for k, other in enumerate(others)]
    own = pltpu.make_async_copy(gain_rows.at[:, lanes(z)], gain_line.at[z], self_sem.at[0])
    own.start()
    for c in sends:
        c.start()
    own.wait()
    for other in others:
        over_line(0, other, other).wait_recv()
    total = gain_line[0].astype(f32)
    for k in range(1, 4):
        total = total + gain_line[k].astype(f32)
    entry = lax.broadcasted_iota(jnp.int32, (16, 128), 0)
    lane = lax.broadcasted_iota(jnp.int32, (16, 128), 1)
    pick = jnp.where(lane == entry, 1.0, 0.0).astype(LOW)
    gain_columns[...] = contract(total.astype(LOW), pick, 0, 0).astype(LOW)
    count = depth // 8
    own = pltpu.make_async_copy(
        gain_columns.at[pl.ds(me * count, count)], gain_plane.at[me], self_sem.at[1]
    )
    own.start()
    swaps = []
    for i in range(1, 8):
        other = lax.rem(me + i, 8)
        swaps.append(
            remote(
                esend,
                erecv,
                i - 1,
                gain_columns.at[pl.ds(other * count, count)],
                gain_plane.at[me],
                other,
            )
        )
        swaps[-1].start()
    own.wait()
    for c in swaps:
        c.wait_recv()
    total = gain_plane[0].astype(f32)
    for k in range(1, 8):
        total = total + gain_plane[k].astype(f32)
    gains_ref[...] = total
    scatter.sent()
    for c in (*sends, *swaps):
        c.wait_send()
    for mine, copies in moves:
        mine.wait()
        for c in copies:
            c.wait()


def layer_close(g_all, wa, g_mid, tokens, gains, gain_sum, blocks, rest):
    rows, width = tokens.shape
    shape = jax.ShapeDtypeStruct
    in_vmem = pl.BlockSpec(memory_space=pltpu.VMEM)
    anywhere = pl.BlockSpec(memory_space=pl.ANY)
    dma = pltpu.SemaphoreType.DMA
    vmem = pltpu.VMEM
    return pl.pallas_call(
        close_kernel,
        out_shape=[
            shape((rows, width), jnp.float32),
            shape((width // 32, 128), jnp.float32),
            shape((8, width // 32, 8 * CHUNKS[0]), LOW),
            shape((8, width // 32, rest.shape[1]), LOW),
        ],
        in_specs=[in_vmem] * 6 + [anywhere] * 2,
        out_specs=[in_vmem, in_vmem, anywhere, anywhere],
        scratch_shapes=[
            vmem((4, rows, width), LOW),
            vmem((4, rows, width), LOW),
            vmem((4, rows, width), LOW),
            vmem((4, rows // 2, width), LOW),
            vmem((2, rows // 2, width), LOW),
            vmem((16, width), LOW),
            vmem((4, 16, width // 4), LOW),
            vmem((width // 4, 128), LOW),
            vmem((8, width // 32, 128), LOW),
            vmem(blocks.shape, LOW),
            vmem((width // 4, 8 * CHUNKS[0]), LOW),
            dma((10,)),
            dma((10,)),
            dma((3,)),
            dma((4,)),
            dma((7,)),
            dma((7,)),
            dma((2,)),
            dma((14,)),
            dma((14,)),
            dma((3,)),
        ],
        compiler_params=pltpu.CompilerParams(
            collective_id=23, has_side_effects=True, vmem_limit_bytes=56 * MIB
        ),
        cost_estimate=moved(16 * rows * width),
        name="close",
    )(g_all, wa, g_mid, tokens, gains, gain_sum, blocks, rest)


def place_kernel(
    first_ref,
    rest_ref,
    blocks_ref,
    down_ref,
    out_ref,
    grad_ref,
    gate_out,
    up_out,
    down_out,
    out_copy,
    grad_copy,
    sems,
):
    copies = [
        pltpu.make_async_copy(out_ref, out_copy, sems.at[0]),
        pltpu.make_async_copy(grad_ref, grad_copy, sems.at[1]),
    ]
    for c in copies:
        c.start()
    f32 = jnp.float32
    z = lax.axis_index("dp")
    share = sum(CHUNKS)
    for second, target in enumerate((gate_out, up_out)):
        for owner in range(8):
            for group in range(4):
                at = group * 8 * share + owner * share
                start = 0
                for k, count in enumerate(CHUNKS):
                    source = first_ref if k == 0 else rest_ref
                    begin = start + (4 * second + group) * count
                    target[:, at : at + count] = source[owner, :, begin : begin + count].astype(f32)
                    at += count
                    start += 8 * count if k else 0
    total = jnp.zeros(blocks_ref.shape[1:], f32)
    for owner in range(4):
        came = jnp.abs(z - owner) < 3
        total = total + jnp.where(came, blocks_ref[owner].astype(f32), 0.0)
    down_out[: CHUNKS[0], :] = total
    down_out[CHUNKS[0] :, :] = down_ref[...].astype(f32)
    for c in copies:
        c.wait()


def place_rows(first, rest, blocks, down, output, input_grad):
    own, width = first.shape[1], blocks.shape[2]
    shape = jax.ShapeDtypeStruct
    anywhere = pl.BlockSpec(memory_space=pl.ANY)
    in_vmem = pl.BlockSpec(memory_space=pltpu.VMEM)
    wide = 32 * sum(CHUNKS)
    return pl.pallas_call(
        place_kernel,
        out_shape=[
            shape((own, wide), jnp.float32),
            shape((own, wide), jnp.float32),
            shape((sum(CHUNKS), width), jnp.float32),
            shape(output.shape, output.dtype),
            shape(input_grad.shape, input_grad.dtype),
        ],
        in_specs=[in_vmem] * 4 + [anywhere] * 2,
        out_specs=[in_vmem] * 3 + [anywhere] * 2,
        scratch_shapes=[pltpu.SemaphoreType.DMA((2,))],
        compiler_params=pltpu.CompilerParams(vmem_limit_bytes=40 * MIB),
        name="place",
    )(first, rest, blocks, down, output, input_grad)


def place_attn_kernel(got_ref, out_ref, query_out, key_out, value_out, grad_out):
    f32 = jnp.float32
    wide = value_out.shape[1] // 8
    qk = query_out.shape[1] // 8
    own = out_ref.shape[0] // 8
    for owner in range(8):
        value_out[:, owner * wide : (owner + 1) * wide] = got_ref[owner, :, :wide].astype(f32)
        here = slice(owner * qk, (owner + 1) * qk)
        query_out[:, here] = got_ref[owner, :, wide : wide + qk].astype(f32)
        key_out[:, here] = got_ref[owner, :, wide + qk : wide + 2 * qk].astype(f32)
        block = out_ref[owner * own : (owner + 1) * own, out_ref.shape[1] - wide :]
        grad_out[:, owner * wide : (owner + 1) * wide] = block.astype(f32)


def place_attn(got, summed, wide, qk):
    own = got.shape[1]
    shape = jax.ShapeDtypeStruct
    in_vmem = pl.BlockSpec(memory_space=pltpu.VMEM)
    return pl.pallas_call(
        place_attn_kernel,
        out_shape=[
            shape((own, 8 * qk), jnp.float32),
            shape((own, 8 * qk), jnp.float32),
            shape((own, 8 * wide), jnp.float32),
            shape((own, 8 * wide), jnp.float32),
        ],
        in_specs=[in_vmem] * 2,
        out_specs=[in_vmem] * 4,
        name="place_attn",
    )(got, summed)


def ffn_lax(h_two, cot_all, gate_full, up_full, down_full):
    pieces, rows, width = cot_all.shape
    h_two_all = gather_plane(h_two, 5).reshape(-1, width)
    cot_all = cot_all.reshape(-1, width)
    gate = dot(h_two_all, gate_full)
    up = dot(h_two_all, up_full)
    g_act = contract(cot_all, down_full, 1, 1)
    sigmoid = jax.nn.sigmoid(gate)
    silu = gate * sigmoid
    act = (silu * up).astype(LOW)
    g_gate = (g_act * up * sigmoid * (1.0 + gate * (1.0 - sigmoid))).astype(LOW)
    g_up = (g_act * silu).astype(LOW)
    part = (contract(g_gate, gate_full, 1, 1) + contract(g_up, up_full, 1, 1)).astype(LOW)
    return (
        dot(act, down_full).astype(LOW).reshape(pieces, rows, width),
        scatter_plane(part.reshape(pieces, rows, width), 7),
        contract(h_two_all, g_gate, 0, 0).astype(LOW),
        contract(h_two_all, g_up, 0, 0).astype(LOW),
        contract(act, cot_all, 0, 0).astype(LOW),
    )


def norm_scale(rows):
    return lax.rsqrt(jnp.mean(rows * rows, axis=-1, keepdims=True) + epsilon)


def norm_backward(grad, normed, inverse, gain):
    scaled = grad * gain
    return inverse * (scaled - normed * jnp.mean(scaled * normed, axis=-1, keepdims=True))


def local(
    tokens,
    doc_lengths,
    w_query,
    w_key,
    w_value,
    w_out,
    w_gate,
    w_up,
    w_down,
    gain_attn,
    gain_mlp,
    cotangent,
):
    micro, span = tokens.shape[1:3]
    pieces, groups = lax.axis_size("seq"), lax.axis_size("dp")
    place = lax.axis_index("seq")
    length = pieces * span
    heads = max(1, HEADS // pieces)
    sharers = max(1, pieces // HEADS)
    streams = micro // sharers
    first_head = place // sharers * heads
    first_stream = place % sharers * streams
    qk, wide = heads * QK_DIM, heads * HEAD_V
    hidden = FF // pieces

    out_width = D // pieces
    rows_dp = w_gate.shape[0]
    share = hidden // groups
    block = FF // groups
    mine = micro * span
    fused = pieces == 8 and groups == 4 and micro == 2 and span == 128
    chunks = CHUNKS if fused else (share,)

    def hidden_columns(w):
        parts = [
            lax.dynamic_slice_in_dim(w, z * block + place * share, share, 1) for z in range(groups)
        ]
        edges = [sum(chunks[:k]) for k in range(len(chunks) + 1)]
        return [
            [part[:, edges[k] : edges[k + 1]] for part in parts] for k in range(len(chunks))
        ]

    gate_parts, up_parts = hidden_columns(w_gate), hidden_columns(w_up)
    ffn_slice = jnp.concatenate(
        [part for k in range(len(chunks)) for part in gate_parts[k] + up_parts[k]], axis=1
    )
    attn_parts = [
        lax.dynamic_slice_in_dim(w_value, first_head * HEAD_V, wide, 1),
        lax.dynamic_slice_in_dim(w_query, first_head * QK_DIM, qk, 1),
        lax.dynamic_slice_in_dim(w_key, first_head * QK_DIM, qk, 1),
    ]

    lengths = lax.dynamic_slice_in_dim(doc_lengths[0], first_stream, streams, 0)
    starts = jnp.cumsum(lengths, axis=1) - lengths
    position = jnp.arange(length, dtype=jnp.int32)
    begun = starts[:, None, :] <= position[None, :, None]
    first = jnp.max(jnp.where(begun, starts[:, None, :], 0), axis=2)[..., None]

    x_own = tokens[0].reshape(mine, D)
    flat = x_own.astype(jnp.float32)
    cot = cotangent[0].reshape(mine, D)

    def to_tokens(by_head):
        sent = by_head.reshape(streams, pieces, span, wide).transpose(1, 0, 2, 3)
        got = exchange_plane(sent, 3).reshape(pieces // sharers, micro, span, wide)
        return got.transpose(1, 2, 0, 3).reshape(mine, HEADS * HEAD_V)

    def to_heads(by_token):
        sent = by_token.reshape(micro, span, pieces // sharers, wide).transpose(2, 0, 1, 3)
        got = exchange_plane(sent.reshape(pieces, streams, span, wide), 4)
        return got.transpose(1, 0, 2, 3).reshape(streams, length, wide)

    if fused:
        attn_slice = jnp.concatenate(
            attn_parts + [jnp.zeros((rows_dp, 128 - 2 * qk), LOW)], axis=1
        )
        gain_rows = jnp.concatenate(
            [gain_attn[None], gain_mlp[None], jnp.zeros((14, rows_dp), LOW)], axis=0
        )
        front = layer_front(
            x_own, cot, attn_slice, w_out, ffn_slice, w_down, gain_rows, first, wide, qk
        )
        out_full, h_all, query, key, value, att_heads, attended, mid = front[3:11]
        attn_full, gain_rows_all, out_part, g_h_two = front[11:15]
        d_ffn, d_down, ffn_blocks, down_blocks = front[17:]
    else:

        def gather_dp(w):
            return lax.all_gather(w, "dp", axis=0, tiled=True)

        attn_got = gather_dp(
            jnp.concatenate(
                attn_parts
                + [
                    lax.dynamic_slice_in_dim(w_out, place * out_width, out_width, 1),
                    gain_attn[:, None],
                    gain_mlp[:, None],
                ],
                axis=1,
            )
        )
        ffn_full = gather_dp(ffn_slice)
        down_full = gather_dp(lax.dynamic_slice_in_dim(w_down, place * share, share, 0))
        value_full = attn_got[:, :wide]
        query_full = attn_got[:, wide : wide + qk]
        key_full = attn_got[:, wide + qk : wide + 2 * qk]
        out_full = gather_plane(attn_got[:, wide + 2 * qk : wide + 2 * qk + out_width], 2)
        gains = attn_got[:, wide + 2 * qk + out_width :].astype(jnp.float32)
        gain_one, gain_two = gains[:, 0], gains[:, 1]
        x_all = gather_plane(x_own, 1).reshape(pieces, micro, span, D).transpose(1, 0, 2, 3)
        x_all = lax.dynamic_slice_in_dim(x_all, first_stream, streams, 0).astype(jnp.float32)
        h_flat = (x_all * norm_scale(x_all) * gain_one).astype(LOW).reshape(streams * length, D)
        value = dot(h_flat, value_full).astype(LOW).reshape(streams, length, wide)
        query = dot(h_flat, query_full).astype(LOW).reshape(streams, length, qk)
        key = dot(h_flat, key_full).astype(LOW).reshape(streams, length, qk)
        att_heads = attend(query, key, value, first, heads)
        attended = to_tokens(att_heads)
        mid = flat + jnp.einsum(
            "tk,skn->tsn", attended, out_full, preferred_element_type=jnp.float32
        ).reshape(mine, D)
        h_two = (mid * norm_scale(mid) * gain_two).astype(LOW)
        out_part, g_h_two, d_gate, d_up, d_down = ffn_lax(
            h_two, gather_plane(cot, 6), ffn_full[:, :hidden], ffn_full[:, hidden:], down_full
        )
        d_ffn = jnp.concatenate([d_gate, d_up], axis=1)

    def scatter_dp(part):
        return lax.psum_scatter(part, "dp", scatter_dimension=0, tiled=True)

    own = rows_dp // pieces
    sum_ffn, sum_down = scatter_dp(d_ffn), scatter_dp(d_down)

    if fused:
        output, g_mid, g_all, gain_sum, grad_attn = layer_turn(
            g_h_two, mid, cot, gain_rows_all, out_full, out_part, attended, query, key, value,
            att_heads, first, h_all, attn_full.shape[1],
        )
        grad_attn, sum_ffn, sum_down = lax.optimization_barrier((grad_attn, sum_ffn, sum_down))
        grad_attn = scatter_dp(grad_attn)
        input_grad, gain_columns, first_got, rest_got = layer_close(
            g_all, attn_full, g_mid, x_own, gain_rows_all, gain_sum, ffn_blocks, sum_ffn
        )
        grad_gate, grad_up, grad_down, output, input_grad = place_rows(
            first_got, rest_got, down_blocks, sum_down, output, input_grad
        )
        grad_attn, grad_gate = lax.optimization_barrier((grad_attn, grad_gate))
        attn_got = exchange_plane(grad_attn[:, : attn_full.shape[1]].reshape(pieces, own, -1), 12)
        grad_query, grad_key, grad_value, grad_out = place_attn(attn_got, grad_attn, wide, qk)
        return (
            output.reshape(tokens.shape),
            input_grad.reshape(tokens.shape),
            grad_query,
            grad_key,
            grad_value,
            grad_out,
            grad_gate,
            grad_up,
            grad_down,
            gain_columns[:, 0],
            gain_columns[:, 1],
        )

    inverse_two = norm_scale(mid)
    plain_two = mid * inverse_two
    output = (mid + scatter_plane(out_part, 8)).astype(LOW)
    g_mid = cot.astype(jnp.float32) + norm_backward(g_h_two, plain_two, inverse_two, gain_two)
    g_mid_low = g_mid.astype(LOW)
    g_att = jnp.einsum(
        "tsn,skn->tk",
        g_mid_low.reshape(mine, pieces, out_width),
        out_full,
        preferred_element_type=jnp.float32,
    )
    g_att = to_heads(g_att.astype(LOW))
    g_query, g_key, g_value = attend_back(query, key, value, first, att_heads, g_att, heads)
    g_value = g_value.reshape(streams * length, wide)
    g_query = g_query.reshape(streams * length, qk)
    g_key = g_key.reshape(streams * length, qk)
    g_h_one_part = (
        contract(g_value, value_full, 1, 1)
        + contract(g_query, query_full, 1, 1)
        + contract(g_key, key_full, 1, 1)
    ).astype(LOW)
    g_h_one_part = g_h_one_part.reshape(streams, pieces, span, D).transpose(1, 0, 2, 3)
    if sharers > 1:
        padded = jnp.zeros((pieces, micro, span, D), LOW)
        g_h_one_part = lax.dynamic_update_slice_in_dim(padded, g_h_one_part, first_stream, 1)
    g_h_one = scatter_plane(g_h_one_part.reshape(pieces, mine, D), 9)
    inverse_one = norm_scale(flat)
    plain_one = flat * inverse_one
    input_grad = g_mid + norm_backward(g_h_one, plain_one, inverse_one, gain_one)
    grad_out = contract(attended, g_mid_low, 0, 0).astype(LOW)
    grad_out = grad_out.reshape(groups, pieces, own, D).transpose(1, 0, 2, 3)
    grad_out = scatter_plane(grad_out.reshape(pieces, groups * own, D), 10).astype(LOW)
    grad_out = scatter_dp(grad_out)
    grad_attn = jnp.concatenate(
        [
            contract(h_flat, g_value, 0, 0).astype(LOW),
            contract(h_flat, g_query, 0, 0).astype(LOW),
            contract(h_flat, g_key, 0, 0).astype(LOW),
            jnp.sum(g_h_one * plain_one, axis=0).astype(LOW)[:, None],
            jnp.sum(g_h_two * plain_two, axis=0).astype(LOW)[:, None],
        ],
        axis=1,
    )

    grad_attn = scatter_dp(grad_attn)
    ffn_got = exchange_plane(sum_ffn.reshape(pieces, own, 2 * hidden), 11).astype(jnp.float32)
    attn_got = exchange_plane(grad_attn.reshape(pieces, own, -1), 12).astype(jnp.float32)
    grad_gains = jnp.sum(attn_got[:, :, wide + 2 * qk :], axis=0)
    attn_got = jnp.sum(attn_got.reshape(pieces // sharers, sharers, own, -1), axis=1)

    def by_hidden(block):
        return block.reshape(pieces, own, groups, share).transpose(1, 2, 0, 3).reshape(own, FF)

    def by_rows(block):
        return block.transpose(1, 0, 2).reshape(own, -1)

    return (
        output.reshape(tokens.shape),
        input_grad.reshape(tokens.shape),
        by_rows(attn_got[:, :, wide : wide + qk]),
        by_rows(attn_got[:, :, wide + qk : wide + 2 * qk]),
        by_rows(attn_got[:, :, :wide]),
        grad_out.astype(jnp.float32),
        by_hidden(ffn_got[:, :, :hidden]),
        by_hidden(ffn_got[:, :, hidden:]),
        sum_down.astype(jnp.float32),
        grad_gains[:, 0],
        grad_gains[:, 1],
    )


def solution(mesh):
    by_token, by_row = P("dp", None, "seq", None), P("dp", None)
    grad_rows, grad_entries = P(("dp", "seq"), None), P(("dp", "seq"))
    return jax.shard_map(
        local,
        mesh=mesh,
        in_specs=(by_token, P("dp", None, None)) + (by_row,) * 7 + (P("dp"), P("dp"), by_token),
        out_specs=(by_token, by_token) + (grad_rows,) * 7 + (grad_entries,) * 2,
        check_vma=False,
    )
```

```python
import functools
import math

import jax
import jax.numpy as jnp
from jax import lax
from jax.experimental import pallas as pl
from jax.experimental.pallas import tpu as pltpu
from jax.sharding import PartitionSpec as P

D = 2048
HEADS = 16
QK_DIM = 16
FF = 5632
HEAD_V = 128
epsilon = 1e-06
MIB = 1024 * 1024


def dot(left, right):
    return jnp.dot(left, right, preferred_element_type=jnp.float32)


def contract(left, right, left_dim, right_dim):
    return lax.dot_general(
        left, right, (((left_dim,), (right_dim,)), ((), ())), preferred_element_type=jnp.float32
    )


def head_lanes(rows, head):
    lane = lax.broadcasted_iota(jnp.int32, rows.shape, 1)
    inside = (lane >= head * QK_DIM) & (lane < (head + 1) * QK_DIM)
    return jnp.where(inside, rows, jnp.zeros_like(rows))


def weights_of(query, key, head, first, base):
    scores = contract(head_lanes(query, head), key, 1, 1)
    row = base + lax.broadcasted_iota(jnp.int32, scores.shape, 0)
    column = lax.broadcasted_iota(jnp.int32, scores.shape, 1)
    mask = (column <= row) & (column >= first)
    poly = 1.0 + scores * (1.0 / math.sqrt(QK_DIM)) + scores * scores * (0.5 / QK_DIM)
    return scores, mask, jnp.where(mask, poly, 0.0)


def attend_kernel(heads, q_ref, k_ref, v_ref, first_ref, out_ref):
    rows = q_ref.shape[1]
    base = pl.program_id(1) * rows
    for head in range(heads):
        columns = slice(head * HEAD_V, (head + 1) * HEAD_V)
        unused, unused_mask, weight = weights_of(
            q_ref[0], k_ref[0], head, first_ref[0], base
        )
        denom = jnp.sum(weight, axis=1, keepdims=True)
        numer = dot(weight.astype(jnp.bfloat16), v_ref[0, :, columns])
        out_ref[0, :, columns] = (numer / denom).astype(jnp.bfloat16)


def attend(query, key, value, first, heads):
    streams, length, width = query.shape
    rows = min(256, length)
    return pl.pallas_call(
        functools.partial(attend_kernel, heads),
        grid=(streams, length // rows),
        in_specs=[
            pl.BlockSpec((1, rows, width), lambda m, i: (m, i, 0)),
            pl.BlockSpec((1, length, width), lambda m, i: (m, 0, 0)),
            pl.BlockSpec((1, length, heads * HEAD_V), lambda m, i: (m, 0, 0)),
            pl.BlockSpec((1, rows, 1), lambda m, i: (m, i, 0)),
        ],
        out_specs=pl.BlockSpec((1, rows, heads * HEAD_V), lambda m, i: (m, i, 0)),
        out_shape=jax.ShapeDtypeStruct(value.shape, jnp.bfloat16),
        compiler_params=pltpu.CompilerParams(vmem_limit_bytes=48 * MIB),
        name="attend",
    )(query, key, value, first)


def attend_back_kernel(
    heads, q_ref, k_ref, v_ref, first_ref, att_ref, g_ref, gq_ref, gk_ref, gv_ref, gk_sum, gv_sum
):
    rows = q_ref.shape[1]
    step = pl.program_id(1)
    base = step * rows

    @pl.when(step == 0)
    def _():
        gk_sum[...] = jnp.zeros_like(gk_sum)
        gv_sum[...] = jnp.zeros_like(gv_sum)

    query, key = q_ref[0], k_ref[0]
    g_query = jnp.zeros(query.shape, jnp.float32)
    for head in range(heads):
        columns = slice(head * HEAD_V, (head + 1) * HEAD_V)
        scores, mask, weight = weights_of(query, key, head, first_ref[0], base)
        denom = jnp.sum(weight, axis=1, keepdims=True)
        a = (g_ref[0, :, columns].astype(jnp.float32) / denom).astype(jnp.bfloat16)
        b = -jnp.sum(
            a.astype(jnp.float32) * att_ref[0, :, columns].astype(jnp.float32),
            axis=1,
            keepdims=True,
        )
        g_weight = contract(a, v_ref[0, :, columns], 1, 1) + b
        slope = 1.0 / math.sqrt(QK_DIM) + scores * (1.0 / QK_DIM)
        g_scores = jnp.where(mask, g_weight * slope, 0.0).astype(jnp.bfloat16)
        g_query += head_lanes(dot(g_scores, key), head)
        gk_sum[...] += contract(g_scores, head_lanes(query, head), 0, 0)
        gv_sum[:, columns] += contract(weight.astype(jnp.bfloat16), a, 0, 0)
    gq_ref[0] = g_query.astype(jnp.bfloat16)

    @pl.when(step == pl.num_programs(1) - 1)
    def _():
        gk_ref[0] = gk_sum[...].astype(jnp.bfloat16)
        gv_ref[0] = gv_sum[...].astype(jnp.bfloat16)


def attend_back(query, key, value, first, attended, grad, heads):
    streams, length, width = query.shape
    rows = min(256, length)
    some = pl.BlockSpec((1, rows, width), lambda m, i: (m, i, 0))
    all_narrow = pl.BlockSpec((1, length, width), lambda m, i: (m, 0, 0))
    all_wide = pl.BlockSpec((1, length, heads * HEAD_V), lambda m, i: (m, 0, 0))
    some_wide = pl.BlockSpec((1, rows, heads * HEAD_V), lambda m, i: (m, i, 0))
    return pl.pallas_call(
        functools.partial(attend_back_kernel, heads),
        grid=(streams, length // rows),
        in_specs=[
            some,
            all_narrow,
            all_wide,
            pl.BlockSpec((1, rows, 1), lambda m, i: (m, i, 0)),
            some_wide,
            some_wide,
        ],
        out_specs=[some, all_narrow, all_wide],
        out_shape=[
            jax.ShapeDtypeStruct(query.shape, jnp.bfloat16),
            jax.ShapeDtypeStruct(key.shape, jnp.bfloat16),
            jax.ShapeDtypeStruct(value.shape, jnp.bfloat16),
        ],
        scratch_shapes=[
            pltpu.VMEM((length, width), jnp.float32),
            pltpu.VMEM((length, heads * HEAD_V), jnp.float32),
        ],
        compiler_params=pltpu.CompilerParams(vmem_limit_bytes=56 * MIB),
        name="attend_back",
    )(query, key, value, first, attended, grad)

MESH = pl.DeviceIdType.MESH
LOW = jnp.bfloat16


def partners():
    me = lax.axis_index("seq")
    core, x, y = me % 2, me // 2 % 2, me // 4
    return me, me + 1 - 2 * core, me + 2 - 4 * x, me + 4 - 8 * y


def greet(others):
    barrier = pltpu.get_barrier_semaphore()
    for other in others:
        pl.semaphore_signal(barrier, inc=1, device_id={"seq": other}, device_id_type=MESH)
    pl.semaphore_wait(barrier, len(others))


def remote(send, recv, k, src, dst, to):
    return pltpu.make_async_remote_copy(
        src_ref=src,
        dst_ref=dst,
        send_sem=send.at[k],
        recv_sem=recv.at[k],
        device_id={"seq": to},
        device_id_type=MESH,
    )


def gather_kernel(x_ref, o_ref, send, recv, own_sem):
    me, sib, xn, yn = partners()
    diag = xn + yn - me
    half = x_ref.shape[0] // 2
    copy = functools.partial(remote, send, recv)
    upper, lower = pl.ds(0, half), pl.ds(half, half)
    greet((sib, xn, yn))
    own = pltpu.make_async_copy(x_ref, o_ref.at[me], own_sem)
    own.start()
    xa = copy(0, x_ref.at[upper], o_ref.at[me, upper], xn)
    yb = copy(1, x_ref.at[lower], o_ref.at[me, lower], yn)
    xb = copy(2, x_ref.at[lower], o_ref.at[me, lower], xn)
    ya = copy(3, x_ref.at[upper], o_ref.at[me, upper], yn)
    beside = [copy(4, x_ref, o_ref.at[me], sib)]
    started = [xa, yb, xb, ya, beside[0]]
    for c in started:
        c.start()

    def pass_on(k, origin, part, to):
        block = o_ref.at[origin, part]
        c = copy(k, block, block, to)
        c.start()
        started.append(c)
        return c

    xa.wait_recv()
    fy = pass_on(5, xn, upper, yn)
    beside.append(pass_on(6, xn, upper, sib))
    yb.wait_recv()
    fx = pass_on(7, yn, lower, xn)
    beside.append(pass_on(8, yn, lower, sib))
    xb.wait_recv()
    beside.append(pass_on(9, xn, lower, sib))
    ya.wait_recv()
    beside.append(pass_on(10, yn, upper, sib))
    fy.wait_recv()
    beside.append(pass_on(11, diag, upper, sib))
    fx.wait_recv()
    beside.append(pass_on(12, diag, lower, sib))
    own.wait()
    for c in beside:
        c.wait_recv()
    for c in started:
        c.wait_send()


def moved(nbytes):
    return pl.CostEstimate(flops=0, bytes_accessed=nbytes * 10, transcendentals=0)


def gather_plane(x, number):
    pieces = lax.axis_size("seq")
    if pieces != 8:
        return lax.all_gather(x, "seq", axis=0)
    return pl.pallas_call(
        gather_kernel,
        out_shape=jax.ShapeDtypeStruct((8,) + x.shape, x.dtype),
        in_specs=[pl.BlockSpec(memory_space=pl.ANY)],
        out_specs=pl.BlockSpec(memory_space=pl.ANY),
        scratch_shapes=[
            pltpu.SemaphoreType.DMA((13,)),
            pltpu.SemaphoreType.DMA((13,)),
            pltpu.SemaphoreType.DMA,
        ],
        compiler_params=pltpu.CompilerParams(collective_id=number, has_side_effects=True),
        cost_estimate=moved(16 * x.size),
        name="gather",
    )(x)


def scatter_kernel(p_ref, o_ref, held, got, one, two, send, recv, own_sem):
    me, sib, xn, yn = partners()
    diag = xn + yn - me
    half = p_ref.shape[1] // 2
    copy = functools.partial(remote, send, recv)
    upper, lower = pl.ds(0, half), pl.ds(half, half)
    greet((sib, xn, yn))
    beside, loads = [], []
    for i, owner in enumerate((diag, xn, yn, me)):
        beside.append(copy(i, p_ref.at[owner + sib - me], got.at[i], sib))
        loads.append(pltpu.make_async_copy(p_ref.at[owner], held.at[i], own_sem.at[i]))
        beside[i].start()
        loads[i].start()

    def pair_sum(i):
        beside[i].wait_recv()
        loads[i].wait()
        held[i] = held[i] + got[i]

    pair_sum(0)
    x0 = copy(4, held.at[0, upper], one.at[0], xn)
    x0.start()
    y0 = copy(5, held.at[0, lower], one.at[1], yn)
    y0.start()
    pair_sum(1)
    x1 = copy(6, held.at[1, upper], one.at[2], xn)
    x1.start()
    pair_sum(2)
    y1 = copy(7, held.at[2, lower], one.at[3], yn)
    y1.start()
    pair_sum(3)
    x0.wait_recv()
    held[2, :half] = held[2, :half] + one[0]
    y2 = copy(8, held.at[2, upper], two.at[0], yn)
    y2.start()
    y0.wait_recv()
    held[1, half:] = held[1, half:] + one[1]
    x2 = copy(9, held.at[1, lower], two.at[1], xn)
    x2.start()
    x1.wait_recv()
    y1.wait_recv()
    y2.wait_recv()
    wide = jnp.float32
    o_ref[:half] = held[3, :half].astype(wide) + one[2].astype(wide) + two[0].astype(wide)
    x2.wait_recv()
    o_ref[half:] = held[3, half:].astype(wide) + one[3].astype(wide) + two[1].astype(wide)
    for c in (*beside, x0, y0, x1, y1, y2, x2):
        c.wait_send()


def scatter_plane(part, number):
    pieces, rows, columns = part.shape
    if pieces != 8:
        return lax.psum_scatter(part, "seq", scatter_dimension=0).astype(jnp.float32)
    return pl.pallas_call(
        scatter_kernel,
        out_shape=jax.ShapeDtypeStruct((rows, columns), jnp.float32),
        in_specs=[pl.BlockSpec(memory_space=pl.ANY)],
        out_specs=pl.BlockSpec(memory_space=pltpu.VMEM),
        scratch_shapes=[
            pltpu.VMEM((4, rows, columns), LOW),
            pltpu.VMEM((4, rows, columns), LOW),
            pltpu.VMEM((4, rows // 2, columns), LOW),
            pltpu.VMEM((2, rows // 2, columns), LOW),
            pltpu.SemaphoreType.DMA((10,)),
            pltpu.SemaphoreType.DMA((10,)),
            pltpu.SemaphoreType.DMA((4,)),
        ],
        compiler_params=pltpu.CompilerParams(
            collective_id=number, has_side_effects=True, vmem_limit_bytes=40 * MIB
        ),
        cost_estimate=moved(2 * part.size),
        name="scatter",
    )(part)


def exchange_kernel(x_ref, o_ref, send, recv, own_sem):
    me = lax.axis_index("seq")
    others = [lax.rem(me + i, 8) for i in range(1, 8)]
    greet(others)
    own = pltpu.make_async_copy(x_ref.at[me], o_ref.at[me], own_sem)
    own.start()
    copies = [
        remote(send, recv, i, x_ref.at[other], o_ref.at[me], other)
        for i, other in enumerate(others)
    ]
    for c in copies:
        c.start()
    own.wait()
    for c in copies:
        c.wait()


def exchange_plane(x, number):
    if lax.axis_size("seq") != 8:
        return lax.all_to_all(x, "seq", 0, 0)
    return pl.pallas_call(
        exchange_kernel,
        out_shape=jax.ShapeDtypeStruct(x.shape, x.dtype),
        in_specs=[pl.BlockSpec(memory_space=pl.ANY)],
        out_specs=pl.BlockSpec(memory_space=pl.ANY),
        scratch_shapes=[
            pltpu.SemaphoreType.DMA((7,)),
            pltpu.SemaphoreType.DMA((7,)),
            pltpu.SemaphoreType.DMA,
        ],
        compiler_params=pltpu.CompilerParams(collective_id=number, has_side_effects=True),
        cost_estimate=moved(4 * x.size),
        name="exchange",
    )(x)


CHUNKS = (64, 64, 48)


class PlaneGather:
    def __init__(self, source, target, send, recv):
        me, sib, xn, yn = partners()
        diag = xn + yn - me
        half = target.shape[1] // 2
        upper, lower = pl.ds(0, half), pl.ds(half, half)
        copy = functools.partial(remote, send, recv)

        def direct(k, part, to):
            return copy(k, source.at[part], target.at[me, part], to)

        def pass_on(k, origin, part, to):
            return copy(k, target.at[origin, part], target.at[origin, part], to)

        self.xa, self.yb = direct(0, upper, xn), direct(1, lower, yn)
        self.xb, self.ya = direct(2, lower, xn), direct(3, upper, yn)
        self.s0 = copy(4, source, target.at[me], sib)
        self.fy, self.fx = pass_on(5, xn, upper, yn), pass_on(6, yn, lower, xn)
        self.s1, self.s2 = pass_on(7, xn, upper, sib), pass_on(8, yn, lower, sib)
        self.s3, self.s4 = pass_on(9, xn, lower, sib), pass_on(10, yn, upper, sib)
        self.s5, self.s6 = pass_on(11, diag, upper, sib), pass_on(12, diag, lower, sib)

    def start(self):
        for c in (self.xa, self.yb, self.xb, self.ya, self.s0):
            c.start()

    def forward_first(self):
        self.xa.wait_recv()
        self.yb.wait_recv()
        for c in (self.fy, self.fx, self.s1, self.s2):
            c.start()

    def forward_second(self):
        self.xb.wait_recv()
        self.ya.wait_recv()
        self.s3.start()
        self.s4.start()

    def forward_third(self):
        self.fy.wait_recv()
        self.fx.wait_recv()
        self.s5.start()
        self.s6.start()

    def from_sibling(self, chip):
        for c in {"own": (self.s0,), "x": (self.s1, self.s3), "y": (self.s2, self.s4), "diag": (self.s5, self.s6)}[chip]:
            c.wait_recv()

    def sent(self):
        for c in (self.xa, self.yb, self.xb, self.ya, self.s0, self.fy, self.fx):
            c.wait_send()
        for c in (self.s1, self.s2, self.s3, self.s4, self.s5, self.s6):
            c.wait_send()

    def arrive(self, step):
        @pl.when(step == 1)
        def _():
            self.from_sibling("own")

        @pl.when(step == 2)
        def _():
            self.forward_first()
            self.forward_second()
            self.from_sibling("x")

        @pl.when(step == 4)
        def _():
            self.from_sibling("y")

        @pl.when(step == 6)
        def _():
            self.forward_third()
            self.from_sibling("diag")


class LineGather:
    def __init__(self, item, source, block, send, recv, local=None):
        z = lax.axis_index("dp")
        self.z = z

        def copy(k, src, owner, to):
            return pltpu.make_async_remote_copy(
                src_ref=src,
                dst_ref=block(owner),
                send_sem=send.at[item, k],
                recv_sem=recv.at[item, owner],
                device_id={"dp": to},
                device_id_type=MESH,
            )

        self.sends = []
        for k, d in enumerate((2, -2, 1, -1)):
            to = z + d
            valid = (to >= 0) & (to < 4)
            self.sends.append((valid, copy(k, source, z, jnp.clip(to, 0, 3))))
        inner = (z == 1) | (z == 2)
        far = jnp.where(z == 1, 3, 0)
        self.stop = (inner, copy(4, block(far), far, jnp.where(z == 1, 0, 3)))
        others = [lax.rem(z + o, 4) for o in (1, 2, 3)]
        self.blocks = [copy(0, source, other, other) for other in others]
        self.own = None
        if local is not None:
            self.own = pltpu.make_async_copy(source, block(z), local.at[item])

    def start_far(self):
        if self.own is not None:
            self.own.start()
        self.begin(self.sends[:2])

    def start_near(self):
        self.begin(self.sends[2:])

    def start(self):
        self.start_far()
        self.start_near()

    def begin(self, sends):
        for valid, c in sends:

            @pl.when(valid)
            def _(c=c):
                c.start()

    def forward(self):
        inner, c = self.stop

        @pl.when(inner)
        def _():
            self.blocks[1].wait_recv()
            c.start()

    def wait(self):
        inner, unused = self.stop
        self.blocks[0].wait_recv()
        self.blocks[2].wait_recv()

        @pl.when(jnp.logical_not(inner))
        def _():
            self.blocks[1].wait_recv()

        if self.own is not None:
            self.own.wait()

    def sent(self):
        for valid, c in (*self.sends, self.stop):

            @pl.when(valid)
            def _(c=c):
                c.wait_send()


def nearest_first(step):
    me, sib, xn, yn = partners()
    chip = jnp.where(step < 4, xn, jnp.where(step < 6, yn, xn + yn - me))
    later = chip + jnp.where(lax.rem(step, 2) == 0, sib - me, 0)
    return jnp.where(step == 0, me, jnp.where(step == 1, sib, later))


def farthest_first(step):
    me, sib, xn, yn = partners()
    chip = jnp.where(step < 4, xn, yn)
    chip = jnp.where(step < 2, xn + yn - me, jnp.where(step < 6, chip, me))
    return chip + jnp.where(lax.rem(step, 2) == 0, sib - me, 0)


def first_of(lengths, stream, base, count):
    row = base + lax.broadcasted_iota(jnp.int32, (count, 1), 0)
    start, first = jnp.int32(0), jnp.zeros((count, 1), jnp.int32)
    for j in range(lengths.shape[1]):
        first = jnp.where(row >= start, start, first)
        start = start + lengths[stream, j]
    return first


def layer_kernel(
    x_ref,
    c_ref,
    wq_ref,
    wk_ref,
    wv_ref,
    wo_ref,
    wg_ref,
    wu_ref,
    wd_ref,
    gain_ref,
    lengths_ref,
    x_all,
    c_all,
    h2_all,
    wo_all,
    h1_out,
    q_out,
    k_out,
    v_out,
    att_out,
    tok_out,
    mid_out,
    wa_out,
    gain_out,
    out_part,
    gh_out,
    dgu_first,
    dd_first,
    dgu_out,
    dd_out,
    dgu_all,
    dd_all,
    wa,
    wgu,
    wd,
    gains,
    q_s,
    k_s,
    v_s,
    att_s,
    tok,
    mid,
    act_s,
    ggu_s,
    sum_gu,
    sum_d,
    x_buf,
    c_buf,
    o_buf,
    beside,
    held,
    got,
    one,
    two,
    gsend,
    grecv,
    zsend,
    zrecv,
    zlocal,
    esend,
    erecv,
    rsend,
    rrecv,
    load_sem,
    out_sem,
    h1_sem,
    w_sem,
    done_sem,
    self_sem,
    fsend,
    frecv,
    f_sem,
    cut_sem,
    gu_stop,
    d_stop,
):
    me, sib, xn, yn = partners()
    z = lax.axis_index("dp")
    rows, width = x_ref.shape
    span = rows // 2
    wide, qk = v_s.shape[2], q_s.shape[2]
    share = CHUNKS[0] + CHUNKS[1] + CHUNKS[2]
    half = rows // 2
    upper, lower = pl.ds(0, half), pl.ds(half, half)

    barrier = pltpu.get_barrier_semaphore()
    for i in range(1, 8):
        pl.semaphore_signal(
            barrier, inc=1, device_id={"seq": lax.rem(me + i, 8)}, device_id_type=MESH
        )
    for i in range(1, 4):
        pl.semaphore_signal(
            barrier, inc=1, device_id={"dp": lax.rem(z + i, 4)}, device_id_type=MESH
        )
    pl.semaphore_wait(barrier, 10)

    tokens = PlaneGather(x_ref, x_all, gsend.at[0], grecv.at[0])
    out_w = PlaneGather(wo_all.at[me], wo_all, gsend.at[1], grecv.at[1])
    cots = PlaneGather(c_ref, c_all, gsend.at[2], grecv.at[2])
    hidden_in = PlaneGather(held.at[0], h2_all, gsend.at[3], grecv.at[3])

    def line(item, source, block):
        return LineGather(item, source, block, zsend, zrecv, zlocal)

    def line_in_place(item, block):
        return LineGather(item, block(z), block, zsend, zrecv)

    depth = wq_ref.shape[0]

    def rows_of(ref, count, columns=None):
        def block(owner):
            if columns is None:
                return ref.at[pl.ds(owner * count, count)]
            return ref.at[pl.ds(owner * count, count), columns]

        return block

    z_gain = line(
        0, gain_ref, lambda owner: gains.at[:, pl.ds(pl.multiple_of(owner * depth, 128), depth)]
    )
    z_attn = line_in_place(1, rows_of(wa, depth))
    z_out = line(
        2,
        wo_ref.at[:, pl.ds(pl.multiple_of(me * wide, 128), wide)],
        lambda owner: wo_all.at[me, pl.ds(owner * depth, depth)],
    )
    z_up, z_down = [], []
    column, before = 0, 0
    columns, hiddens = [], []
    for k, count in enumerate(CHUNKS):
        part = pl.ds(column, 8 * count)
        z_up.append(line_in_place(3 + k, rows_of(wgu, depth, part)))
        z_down.append(
            line(
                6 + k,
                wd_ref.at[pl.ds(me * share + before, count)],
                lambda owner, base=4 * before, count=count: wd.at[
                    pl.ds(base + owner * count, count)
                ],
            )
        )
        columns.append(column)
        hiddens.append(4 * before)
        column += 8 * count
        before += count

    tokens.start()
    z_gain.start()

    window = 384
    tall = depth // 2

    def cut_window(i, source, start, size, r, slot, lane):
        return pltpu.make_async_copy(
            source.at[pl.ds(r * tall, tall), pl.ds(pl.multiple_of(start, 128), size)],
            got.at[slot, :, pl.ds(lane, size)],
            cut_sem.at[i],
        )

    per_tile = 128 // qk
    narrow = me // per_tile * 128
    shift = lax.rem(me, per_tile) * qk
    own_rows = pl.ds(pl.multiple_of(z * depth, depth), depth)
    v_cut = pltpu.make_async_copy(
        wv_ref.at[:, pl.ds(pl.multiple_of(me * wide, 128), wide)],
        wa.at[own_rows, pl.ds(0, wide)],
        cut_sem.at[20],
    )
    v_cut.start()
    qk_cuts = [
        cut_window(2 * r + i, source, narrow, 128, r, r, 128 * i)
        for r in range(2)
        for i, source in enumerate((wq_ref, wk_ref))
    ]
    for c in qk_cuts:
        c.start()
    ff_cuts = []
    ff_width = wg_ref.shape[1]
    for second, source in enumerate((wg_ref, wu_ref)):
        for group in range(4):
            start = group * (ff_width // 4) + me * share
            aligned = jnp.minimum(start // 128 * 128, ff_width - window)
            lane = 256 * (1 - second) + window * group
            for r in range(2):
                c = cut_window(
                    4 + len(ff_cuts), source, aligned, window, r, 2 * second + r, lane
                )
                c.start()
                ff_cuts.append((c, second, group, r, lane, start - aligned))
    for c in qk_cuts:
        c.wait()
    for r in range(2):
        lane = lax.broadcasted_iota(jnp.int32, (tall, 128), 1)
        q_rows = pltpu.roll(got[r, :, 0:128].astype(jnp.float32), lax.rem(128 - shift, 128), 1)
        k_rows = pltpu.roll(
            got[r, :, 128:256].astype(jnp.float32), lax.rem(128 + qk - shift, 128), 1
        )
        both = jnp.where(lane < qk, q_rows, jnp.where(lane < 2 * qk, k_rows, 0.0))
        there = pl.ds(pl.multiple_of(z * depth + r * tall, tall), tall)
        wa[there, wide : wide + 128] = both.astype(LOW)
    v_cut.wait()
    z_attn.start()
    for c, second, group, r, lane, shift_by in ff_cuts:
        c.wait()
        rolled = pltpu.roll(
            got[2 * second + r, :, lane : lane + window].astype(jnp.float32),
            lax.rem(window - shift_by, window),
            1,
        )
        there = pl.ds(pl.multiple_of(z * depth + r * tall, tall), tall)
        begin = 0
        for k, count in enumerate(CHUNKS):
            at = columns[k] + (4 * second + group) * count
            wgu[there, at : at + count] = rolled[:, begin : begin + count].astype(LOW)
            begin += count

    def loads(order, step, sources):
        slot = lax.rem(step, 2)
        owner = order(step)
        return [
            pltpu.make_async_copy(source.at[owner], buf.at[slot], load_sem.at[i, slot])
            for i, (source, buf) in enumerate(sources)
        ]

    first_load = pltpu.make_async_copy(x_ref, x_buf.at[0], load_sem.at[0, 0])
    first_load.start()
    own_c = pltpu.make_async_copy(c_ref, c_all.at[me], self_sem.at[3])
    own_c.start()
    tokens.forward_first()
    z_gain.forward()
    z_attn.forward()
    tokens.forward_second()
    cots.start()
    z_gain.wait()
    z_attn.wait()
    z_out.start()

    def h1_copies(step):
        slot = lax.rem(step, 2)
        owner = nearest_first(step)
        return [
            pltpu.make_async_copy(
                o_buf.at[slot, pl.ds(m * span, span)],
                h1_out.at[m, pl.ds(owner * span, span)],
                h1_sem.at[m, slot],
            )
            for m in range(2)
        ]

    def arrive_tokens(step):
        @pl.when(step == 1)
        def _():
            tokens.from_sibling("own")

        @pl.when(step == 2)
        def _():
            tokens.from_sibling("x")

        @pl.when(step == 4)
        def _():
            tokens.forward_third()
            tokens.from_sibling("y")

        @pl.when(step == 3)
        def _():
            for g in (z_up[0], z_down[0]):
                g.start()

        @pl.when(step == 6)
        def _():
            tokens.from_sibling("diag")

        @pl.when(step == 7)
        def _():
            z_out.forward()

    token_source = [(x_all, x_buf)]

    def project(step, carry):
        slot = lax.rem(step, 2)
        owner = nearest_first(step)
        for c in loads(nearest_first, step, token_source):
            c.wait()

        @pl.when(step >= 2)
        def _():
            for c in h1_copies(step - 2):
                c.wait()

        x = x_buf[slot].astype(jnp.float32)
        gain = gains[0:1, :].astype(jnp.float32)
        h_one = (x * norm_scale(x) * gain).astype(LOW)
        o_buf[slot] = h_one
        for c in h1_copies(step):
            c.start()
        arrive_tokens(step + 1)

        @pl.when(step < 7)
        def _():
            for c in loads(nearest_first, step + 1, token_source):
                c.start()

        projected = dot(h_one, wa[...]).astype(LOW)
        for m in range(2):
            there = pl.ds(owner * span, span)
            mine = projected[m * span : (m + 1) * span]
            v_s[m, there, :] = mine[:, :wide]
            q_s[m, there, :] = mine[:, wide : wide + qk]
            k_s[m, there, :] = mine[:, wide + qk : wide + 2 * qk]
        return carry

    lax.fori_loop(0, 8, project, 0)
    for step in (6, 7):
        for c in h1_copies(step):
            c.wait()
    z_out.wait()
    out_w.start()
    for g in (z_up[1], z_down[1]):
        g.start()

    finals = [
        pltpu.make_async_copy(source, target, done_sem.at[i])
        for i, (source, target) in enumerate(
            (
                (q_s, q_out),
                (k_s, k_out),
                (v_s, v_out),
                (wa, wa_out),
                (gains, gain_out),
                (att_s, att_out),
                (tok, tok_out),
                (mid, mid_out),
            )
        )
    ]
    for c in finals[:5]:
        c.start()

    length = v_s.shape[1]
    block = 256

    def attend_stream(m, carry):
        for i in range(length // block):
            rows_i = slice(i * block, (i + 1) * block)
            seen = (i + 1) * block
            first = first_of(lengths_ref, m, i * block, block)
            for head in range(wide // HEAD_V):
                lanes = slice(head * HEAD_V, (head + 1) * HEAD_V)
                unused, unused_mask, weight = weights_of(
                    q_s[m, rows_i, :], k_s[m, :seen, :], head, first, i * block
                )
                denom = jnp.sum(weight, axis=1, keepdims=True)
                numer = dot(weight.astype(LOW), v_s[m, :seen, lanes])
                att_s[m, rows_i, lanes] = (numer / denom).astype(LOW)
        return carry

    lax.fori_loop(0, 2, attend_stream, 0)
    out_w.forward_first()
    finals[5].start()

    to_mine = pl.ds(pl.multiple_of(me * wide, 128), wide)
    swaps = []
    for i in range(1, 8):
        other = lax.rem(me + i, 8)
        for m in range(2):
            swaps.append(
                remote(
                    esend,
                    erecv,
                    2 * (i - 1) + m,
                    att_s.at[m, pl.ds(other * span, span)],
                    tok.at[pl.ds(m * span, span), to_mine],
                    other,
                )
            )
            swaps[-1].start()
    kept = [
        pltpu.make_async_copy(
            att_s.at[m, pl.ds(me * span, span)],
            tok.at[pl.ds(m * span, span), to_mine],
            self_sem.at[m],
        )
        for m in range(2)
    ]
    for c in kept:
        c.start()
    x_load = pltpu.make_async_copy(x_ref, x_buf.at[0], load_sem.at[0, 0])
    x_load.start()

    def w_lanes(slot):
        return pl.ds(pl.multiple_of(slot * wide, 128), wide)

    def w_load(step):
        slot = lax.rem(step, 2)
        return pltpu.make_async_copy(
            wo_all.at[nearest_first(step)], act_s.at[:, w_lanes(slot)], w_sem.at[slot]
        )

    w_load(0).start()
    out_w.forward_second()
    cots.forward_first()
    cots.forward_second()
    z_up[0].forward()
    z_down[0].forward()
    for g in (z_up[2], z_down[2]):
        g.start_far()
    for c in kept:
        c.wait()
    for c in swaps:
        c.wait_recv()
    finals[6].start()
    x_load.wait()

    def arrive_out(step):
        @pl.when(step == 1)
        def _():
            out_w.from_sibling("own")

        @pl.when(step == 2)
        def _():
            out_w.from_sibling("x")

        @pl.when(step == 4)
        def _():
            out_w.forward_third()
            out_w.from_sibling("y")

        @pl.when(step == 6)
        def _():
            out_w.from_sibling("diag")

    def project_out(step, carry):
        slot = lax.rem(step, 2)
        owner = nearest_first(step)
        w_load(step).wait()
        arrive_out(step + 1)

        @pl.when(step < 7)
        def _():
            w_load(step + 1).start()

        there = pl.ds(pl.multiple_of(owner * wide, 128), wide)
        mid[:, there] = dot(tok[...], act_s[:, w_lanes(slot)])
        return carry

    lax.fori_loop(0, 8, project_out, 0)
    mid_value = x_buf[0].astype(jnp.float32) + mid[...]
    mid[...] = mid_value
    held[0] = (mid_value * norm_scale(mid_value) * gains[1:2, :].astype(jnp.float32)).astype(LOW)
    hidden_in.start()
    own_h2 = pltpu.make_async_copy(held.at[0], h2_all.at[me], self_sem.at[2])
    own_h2.start()
    for g in (z_up[2], z_down[2]):
        g.start_near()
    cots.forward_third()
    own_h2.wait()
    own_c.wait()
    z_up[0].wait()
    z_down[0].wait()

    largest = 4 * max(CHUNKS)
    sources = [(h2_all, x_buf), (c_all, c_buf)]

    def out_copy(order, step):
        slot = lax.rem(step, 2)
        return pltpu.make_async_copy(o_buf.at[slot], out_part.at[order(step)], out_sem.at[slot])

    def hidden_chunk(k, owner, h, c):
        count = 4 * CHUNKS[k]
        pair = pl.ds(columns[k], 2 * count)
        here = pl.ds(hiddens[k], count)
        both = dot(h, wgu[:, pair])
        gate, up = both[:, :count], both[:, count:]
        g_act = contract(c, wd[here, :], 1, 1)
        sigmoid = jax.nn.sigmoid(gate)
        silu = gate * sigmoid
        act = (silu * up).astype(LOW)
        g_gate = (g_act * up * sigmoid * (1.0 + gate * (1.0 - sigmoid))).astype(LOW)
        g_up = (g_act * silu).astype(LOW)
        there = pl.ds(owner * rows, rows)
        act_s[there, here] = act
        g_both = jnp.concatenate([g_gate, g_up], axis=1)
        ggu_s[there, pair] = g_both
        return act, g_both

    def add_grads(k, step, h, c, act, g_both):
        count = 4 * CHUNKS[k]

        to, low = (2 * largest, largest) if k == 1 else (0, 0)

        @pl.when(step == 0)
        def _():
            sum_gu[:, to : to + 2 * count] = jnp.zeros((width, 2 * count), jnp.float32)
            sum_d[low : low + count, :] = jnp.zeros((count, width), jnp.float32)

        sum_gu[:, to : to + 2 * count] += contract(h, g_both, 0, 0)
        sum_d[low : low + count, :] += contract(act, c, 0, 0)

    def emit(k):
        count = 4 * CHUNKS[k]
        rest = share - CHUNKS[0]
        to, low = (2 * largest, largest) if k == 1 else (0, 0)

        def gu_copies(i, slot):
            there = pl.ds(i * rows, rows)
            if k == 0:
                return [
                    pltpu.make_async_copy(
                        o_buf.at[slot, :, pl.ds(second * count, count)],
                        dgu_first.at[second, there],
                        h1_sem.at[second, slot],
                    )
                    for second in range(2)
                ]
            return [
                pltpu.make_async_copy(
                    o_buf.at[slot, :, pl.ds(0, 2 * count)],
                    dgu_out.at[there, pl.ds(columns[k] - columns[1], 2 * count)],
                    out_sem.at[slot],
                )
            ]

        def d_target(owner):
            if k == 0:
                return dd_first.at[pl.ds(owner * CHUNKS[0], CHUNKS[0])]
            start = owner * rest + (hiddens[k] - hiddens[1]) // 4
            return dd_out.at[pl.ds(start, CHUNKS[k])]

        pending = [[], []]
        for i in range(width // rows):
            slot = i % 2
            for c in pending[slot]:
                c.wait()
            total = sum_gu[i * rows : (i + 1) * rows, to : to + 2 * count]
            o_buf[slot, :, : 2 * count] = total.astype(LOW)
            pending[slot] = gu_copies(i, slot)
            for c in pending[slot]:
                c.start()
        for c in (*pending[0], *pending[1]):
            c.wait()
        o_buf[0, :count, :] = sum_d[low : low + count, :].astype(LOW)
        downs = []
        for owner in range(4):
            downs.append(
                pltpu.make_async_copy(
                    o_buf.at[0, pl.ds(owner * CHUNKS[k], CHUNKS[k])],
                    d_target(owner),
                    h1_sem.at[owner // 2, owner % 2],
                )
            )
            downs[-1].start()
        for c in downs:
            c.wait()

    def forward_pass(chunks, last, arrive, step, carry):
        slot = lax.rem(step, 2)
        for c in loads(nearest_first, step, sources):
            c.wait()
        h, c = x_buf[slot], c_buf[slot]
        made = [hidden_chunk(k, nearest_first(step), h, c) for k in chunks]
        if arrive is not None:
            arrive(step + 1)

        @pl.when(step < last)
        def _():
            for c in loads(nearest_first, step + 1, sources):
                c.start()

        for k, (act, g_both) in zip(chunks, made):
            add_grads(k, step, h, c, act, g_both)
        return carry

    def arrive_both(step):
        hidden_in.arrive(step)

        @pl.when(step == 1)
        def _():
            cots.from_sibling("own")

        @pl.when(step == 2)
        def _():
            cots.from_sibling("x")

        @pl.when(step == 4)
        def _():
            cots.from_sibling("y")

        @pl.when(step == 6)
        def _():
            cots.from_sibling("diag")

        @pl.when(step == 7)
        def _():
            z_up[2].forward()
            z_down[2].forward()

    for c in loads(nearest_first, 0, sources):
        c.start()

    def arrive_near(step):
        @pl.when(step < 4)
        def _():
            arrive_both(step)

    lax.fori_loop(0, 4, functools.partial(forward_pass, (0,), 3, arrive_near), 0)
    for c in loads(nearest_first, 0, sources):
        c.start()
    z_up[1].forward()
    z_down[1].forward()
    z_up[1].wait()
    z_down[1].wait()
    lax.fori_loop(0, 4, functools.partial(forward_pass, (1,), 3, None), 0)
    arrive_both(jnp.int32(4))
    for c in loads(nearest_first, 4, sources):
        c.start()
    lax.fori_loop(4, 8, functools.partial(forward_pass, (0, 1), 7, arrive_both), 0)
    hidden_in.sent()
    finals[7].start()
    for c in loads(farthest_first, 0, sources):
        c.start()
    emit(0)
    sum_lines = [
        LineScatter(
            lambda owner: dgu_first.at[:, pl.ds(owner * depth, depth), :],
            dgu_all,
            gu_stop,
            att_s.at[:, pl.ds(0, depth), :],
            fsend.at[0],
            frecv.at[0],
            f_sem.at[0],
        ),
        LineScatter(
            lambda owner: dd_first.at[pl.ds(owner * CHUNKS[0], CHUNKS[0])],
            dd_all,
            d_stop,
            tok.at[pl.ds(0, CHUNKS[0])],
            fsend.at[1],
            frecv.at[1],
            f_sem.at[1],
        ),
    ]
    for c in swaps:
        c.wait_send()
    finals[5].wait()
    finals[6].wait()
    for g in sum_lines:
        g.start_first()

    z_up[2].wait()
    z_down[2].wait()

    copy = functools.partial(remote, rsend, rrecv)
    b_diag = copy(0, beside.at[0], got.at[2], sib)
    b_x = copy(1, beside.at[1], got.at[1], sib)
    b_y = copy(2, beside.at[0], got.at[3], sib)
    b_own = copy(3, beside.at[1], got.at[0], sib)
    x0 = copy(4, held.at[2, upper], one.at[0], xn)
    y0 = copy(5, held.at[2, lower], one.at[1], yn)
    x1 = copy(6, held.at[1, upper], one.at[2], xn)
    y1 = copy(7, held.at[3, lower], one.at[3], yn)
    y2 = copy(8, held.at[3, upper], two.at[0], yn)
    x2 = copy(9, held.at[1, lower], two.at[1], xn)

    def last_pass(step, carry):
        slot = lax.rem(step, 2)
        owner = farthest_first(step)
        there = pl.ds(owner * rows, rows)
        for c in loads(farthest_first, step, sources):
            c.wait()
        hidden_chunk(2, owner, x_buf[slot], c_buf[slot])

        @pl.when(step < 7)
        def _():
            for c in loads(farthest_first, step + 1, sources):
                c.start()

        part = contract(ggu_s[there, :], wgu[...], 1, 1).astype(LOW)

        @pl.when(step == 2)
        def _():
            for g in sum_lines:
                g.start()

        @pl.when(step == 6)
        def _():
            for g in sum_lines:
                g.join()

        for k, place, sent in ((0, 0, b_diag), (2, 1, b_x), (4, 0, b_y), (6, 1, b_own)):

            @pl.when(step == k)
            def _(k=k, place=place, sent=sent):
                if k == 4:
                    b_diag.wait_send()
                if k == 6:
                    b_x.wait_send()
                beside[place] = part
                sent.start()

        for k, place, arrived in ((1, 2, b_diag), (3, 1, b_x), (5, 3, b_y), (7, 0, b_own)):

            @pl.when(step == k)
            def _(k=k, place=place, arrived=arrived):
                arrived.wait_recv()
                held[place] = part + got[place]
                if k == 1:
                    x0.start()
                    y0.start()
                if k == 3:
                    x1.start()
                if k == 5:
                    y1.start()
                    y0.wait_recv()
                    held[1, half:] = held[1, half:] + one[1]
                    x2.start()
                    x0.wait_recv()
                    held[3, :half] = held[3, :half] + one[0]
                    y2.start()
        return carry

    lax.fori_loop(0, 8, last_pass, 0)
    for c in loads(farthest_first, 0, sources):
        c.start()

    def close_pass(step, carry):
        slot = lax.rem(step, 2)
        there = pl.ds(farthest_first(step) * rows, rows)
        for c in loads(farthest_first, step, sources):
            c.wait()

        @pl.when(step < 7)
        def _():
            for c in loads(farthest_first, step + 1, sources):
                c.start()

        @pl.when(step >= 2)
        def _():
            out_copy(farthest_first, step - 2).wait()

        o_buf[slot] = dot(act_s[there, :], wd[...]).astype(LOW)
        out_copy(farthest_first, step).start()
        act = act_s[there, pl.ds(hiddens[2], 4 * CHUNKS[2])]
        g_both = ggu_s[there, pl.ds(columns[2], 8 * CHUNKS[2])]
        add_grads(2, step, x_buf[slot], c_buf[slot], act, g_both)
        return carry

    lax.fori_loop(0, 8, close_pass, 0)
    out_copy(farthest_first, 6).wait()
    out_copy(farthest_first, 7).wait()
    emit(1)
    emit(2)
    f32 = jnp.float32
    x1.wait_recv()
    y2.wait_recv()
    for c in (*finals[:5], finals[7]):
        c.wait()
    mid[:half] = held[0, :half].astype(f32) + one[2].astype(f32) + two[0].astype(f32)
    y1.wait_recv()
    x2.wait_recv()
    mid[half:] = held[0, half:].astype(f32) + one[3].astype(f32) + two[1].astype(f32)
    gh_copy = pltpu.make_async_copy(mid, gh_out, done_sem.at[7])
    gh_copy.start()
    for g in sum_lines:
        g.wait()
    gh_copy.wait()
    for c in (b_y, b_own, x0, y0, x1, y1, y2, x2):
        c.wait_send()
    for g in (tokens, out_w, cots, z_gain, z_attn, z_out, *z_up, *z_down):
        g.sent()


def layer_front(tokens, cot, weights, gain_rows, lengths, length, wide, qk):
    rows, width = tokens.shape
    streams = lengths.shape[0]
    hidden = 4 * sum(CHUNKS)
    largest = 4 * max(CHUNKS)
    shape = jax.ShapeDtypeStruct
    f32 = jnp.float32
    anywhere = pl.BlockSpec(memory_space=pl.ANY)
    plane = shape((8, rows, width), LOW)
    narrow = shape((streams, length, qk), LOW)
    broad = shape((streams, length, wide), LOW)
    attn_shape = (width, wide + 128)
    out_shape = [
        plane,
        plane,
        plane,
        shape((8, width, width // 8), LOW),
        shape((streams, length, width), LOW),
        narrow,
        narrow,
        broad,
        broad,
        shape((rows, width), LOW),
        shape((rows, width), f32),
        shape(attn_shape, LOW),
        shape((gain_rows.shape[0], width), LOW),
        plane,
        shape((rows, width), f32),
        shape((2, width, 4 * CHUNKS[0]), LOW),
        shape((4 * CHUNKS[0], width), LOW),
        shape((width, 2 * hidden - 8 * CHUNKS[0]), LOW),
        shape((hidden - 4 * CHUNKS[0], width), LOW),
        shape((4, 2, width // 4, 4 * CHUNKS[0]), LOW),
        shape((4, CHUNKS[0], width), LOW),
    ]
    dma = pltpu.SemaphoreType.DMA
    vmem = pltpu.VMEM
    return pl.pallas_call(
        layer_kernel,
        out_shape=out_shape,
        in_specs=[anywhere] * 10 + [pl.BlockSpec(memory_space=pltpu.SMEM)],
        out_specs=[anywhere] * 21,
        scratch_shapes=[
            vmem(attn_shape, LOW),
            vmem((width, 2 * hidden), LOW),
            vmem((hidden, width), LOW),
            vmem((gain_rows.shape[0], width), LOW),
            vmem(narrow.shape, LOW),
            vmem(narrow.shape, LOW),
            vmem(broad.shape, LOW),
            vmem(broad.shape, LOW),
            vmem((rows, width), LOW),
            vmem((rows, width), f32),
            vmem((8 * rows, hidden), LOW),
            vmem((8 * rows, 2 * hidden), LOW),
            vmem((width, 4 * largest), f32),
            vmem((2 * largest, width), f32),
            vmem((2, rows, width), LOW),
            vmem((2, rows, width), LOW),
            vmem((2, rows, width), LOW),
            vmem((2, rows, width), LOW),
            vmem((4, rows, width), LOW),
            vmem((4, rows, width), LOW),
            vmem((4, rows // 2, width), LOW),
            vmem((2, rows // 2, width), LOW),
            dma((4, 13)),
            dma((4, 13)),
            dma((9, 5)),
            dma((9, 4)),
            dma((9,)),
            dma((14,)),
            dma((14,)),
            dma((10,)),
            dma((10,)),
            dma((2, 2)),
            dma((2,)),
            dma((2, 2)),
            dma((2,)),
            dma((8,)),
            dma((4,)),
            dma((2, 5)),
            dma((2, 5)),
            dma((2, 2)),
            dma((21,)),
            vmem((2, width // 4, 4 * CHUNKS[0]), LOW),
            vmem((CHUNKS[0], width), LOW),
        ],
        compiler_params=pltpu.CompilerParams(
            collective_id=21, has_side_effects=True, vmem_limit_bytes=63 * MIB
        ),
        cost_estimate=pl.CostEstimate(
            flops=6 * 3 * 8 * rows * width * hidden,
            bytes_accessed=400 * rows * width,
            transcendentals=0,
        ),
        name="layer",
    )(tokens, cot, *weights, gain_rows, lengths)


class LineScatter:
    def __init__(self, block, target, stop, mine, send, recv, local):
        z = lax.axis_index("dp")
        self.z, self.stop, self.mine = z, stop, mine
        self.inner = (z == 1) | (z == 2)
        self.outer = jnp.logical_not(self.inner)

        def copy(k, src, dst, at, to):
            return pltpu.make_async_remote_copy(
                src_ref=src,
                dst_ref=dst,
                send_sem=send.at[k],
                recv_sem=recv.at[at],
                device_id={"dp": to},
                device_id_type=MESH,
            )

        far = jnp.where(z < 2, 3, 0)
        near = jnp.where(z < 2, 1, 2)
        self.first = copy(0, block(far), stop, 4, jnp.where(self.inner, 3 - near, near))
        self.sends = []
        for k, d in enumerate((1, -1)):
            to = z + d
            valid = (to >= 0) & (to < 4)
            there = jnp.clip(to, 0, 3)
            self.sends.append((valid, copy(1 + k, block(there), target.at[z], z, there)))
        other = 3 - near
        self.sends.append((self.outer, copy(3, block(other), target.at[z], z, other)))
        self.own_far = pltpu.make_async_copy(block(far), mine, local.at[0])
        self.joined = copy(4, mine, target.at[z], z, far)
        self.own = pltpu.make_async_copy(block(z), target.at[z], local.at[1])
        self.arrivals = []
        for d in (1, -1, 2, -2):
            owner = z + d
            valid = (owner >= 0) & (owner < 4)
            there = jnp.clip(owner, 0, 3)
            self.arrivals.append((valid, copy(1, block(there), target.at[there], there, there)))

    def start_first(self):
        self.own.start()

        @pl.when(self.outer)
        def _():
            self.first.start()

        @pl.when(self.inner)
        def _():
            self.own_far.start()

    def start(self):
        for valid, c in self.sends:

            @pl.when(valid)
            def _(c=c):
                c.start()

    def join(self):
        @pl.when(self.inner)
        def _():
            self.first.wait_recv()
            self.own_far.wait()
            self.mine[...] = self.mine[...] + self.stop[...]
            self.joined.start()

    def wait(self):
        for valid, c in self.arrivals:

            @pl.when(valid)
            def _(c=c):
                c.wait_recv()

        self.own.wait()
        for valid, c in (*self.sends, (self.outer, self.first), (self.inner, self.joined)):

            @pl.when(valid)
            def _(c=c):
                c.wait_send()


class PlaneScatter:
    def __init__(self, beside, held, got, one, two, send, recv):
        me, sib, xn, yn = partners()
        half = got.shape[1] // 2
        self.half = half
        upper, lower = pl.ds(0, half), pl.ds(half, half)
        copy = functools.partial(remote, send, recv)
        self.held, self.got, self.one, self.two = held, got, one, two
        self.pairs = [copy(i, beside(i), got.at[i], sib) for i in range(4)]
        self.x0 = copy(4, held(2).at[upper], one.at[0], xn)
        self.y0 = copy(5, held(2).at[lower], one.at[1], yn)
        self.x1 = copy(6, held(1).at[upper], one.at[2], xn)
        self.y1 = copy(7, held(3).at[lower], one.at[3], yn)
        self.y2 = copy(8, held(3).at[upper], two.at[0], yn)
        self.x2 = copy(9, held(1).at[lower], two.at[1], xn)

    def start_pair(self, i):
        self.pairs[i].start()

    def start_pairs(self):
        for i in (2, 1, 3, 0):
            self.start_pair(i)

    def add_pair(self, i):
        self.pairs[i].wait_recv()
        block = self.held(i)
        block[...] = block[...] + self.got[i]
        for c in {0: (), 1: (self.x1,), 2: (self.x0, self.y0), 3: (self.y1,)}[i]:
            c.start()

    def add_pairs(self):
        for i in (2, 1, 3, 0):
            self.add_pair(i)

    def second(self):
        half = self.half
        self.y0.wait_recv()
        block = self.held(1)
        block[half:, :] = block[half:, :] + self.one[1]
        self.x2.start()
        self.x0.wait_recv()
        block = self.held(3)
        block[:half, :] = block[:half, :] + self.one[0]
        self.y2.start()

    def upper_sum(self):
        f32 = jnp.float32
        self.x1.wait_recv()
        self.y2.wait_recv()
        own = self.held(0)[: self.half, :].astype(f32)
        return own + self.one[2].astype(f32) + self.two[0].astype(f32)

    def lower_sum(self):
        f32 = jnp.float32
        self.y1.wait_recv()
        self.x2.wait_recv()
        own = self.held(0)[self.half :, :].astype(f32)
        return own + self.one[3].astype(f32) + self.two[1].astype(f32)

    def sent(self):
        for c in (*self.pairs, self.x0, self.y0, self.x1, self.y1, self.y2, self.x2):
            c.wait_send()


def chips():
    me, unused, xn, yn = partners()
    return me, xn, xn + yn - me, yn


def turn_kernel(
    gh_ref,
    mid_ref,
    c_ref,
    gain_ref,
    wo_all,
    part_ref,
    tok_ref,
    q_ref,
    k_ref,
    v_ref,
    att_ref,
    lengths_ref,
    h1_ref,
    output_ref,
    g_mid_out,
    g_out,
    gain_out,
    attn_ref,
    g_mid,
    work,
    g_low,
    g_att,
    g_heads,
    g_s,
    w_buf,
    go_part,
    held_o,
    got_g,
    one_g,
    two_g,
    got_o,
    one_o,
    two_o,
    gk_sum,
    gv_sum,
    h_buf,
    sums,
    esend,
    erecv,
    ssend,
    srecv,
    load_sem,
    w_sem,
    self_sem,
    done_sem,
    h_sem,
):
    me, sib, xn, yn = partners()
    flip = sib - me
    rows, width = g_low.shape
    span = rows // 2
    wide, qk = v_ref.shape[2], q_ref.shape[2]
    half = rows // 2
    greet([lax.rem(me + i, 8) for i in range(1, 8)])
    owners = chips()

    loads = [
        pltpu.make_async_copy(source, target, load_sem.at[i])
        for i, (source, target) in enumerate(
            ((gh_ref, g_mid), (mid_ref, work), (c_ref, g_low))
        )
    ]
    held_loads = [
        pltpu.make_async_copy(part_ref.at[owners[i]], held_o.at[i], load_sem.at[3 + i])
        for i in range(4)
    ]

    def w_load(step):
        slot = lax.rem(step, 2)
        return pltpu.make_async_copy(wo_all.at[step], w_buf.at[slot], w_sem.at[slot])

    for c in loads:
        c.start()
    w_load(0).start()
    outs = PlaneScatter(
        lambda i: part_ref.at[owners[i] + flip],
        lambda i: held_o.at[i],
        got_o,
        one_o,
        two_o,
        ssend.at[0],
        srecv.at[0],
    )
    weights = PlaneScatter(
        lambda i: go_part.at[owners[i] + flip],
        lambda i: go_part.at[owners[i]],
        got_g,
        one_g,
        two_g,
        ssend.at[1],
        srecv.at[1],
    )
    outs.start_pairs()
    for c in held_loads:
        c.start()
    for c in loads:
        c.wait()

    f32 = jnp.float32
    mid = work[...]
    inverse = norm_scale(mid)
    normed = mid * inverse
    grad = g_mid[...]
    gain_out[...] = jnp.broadcast_to(
        jnp.sum(grad * normed, axis=0, keepdims=True), gain_out.shape
    )
    gain = gain_ref[1:2, :].astype(f32)
    grad_mid = g_low[...].astype(f32) + norm_backward(grad, normed, inverse, gain)
    g_mid[...] = grad_mid
    g_low[...] = grad_mid.astype(LOW)
    done = [pltpu.make_async_copy(g_mid, g_mid_out, done_sem.at[0])]
    done[0].start()

    def back_out(step, carry):
        slot = lax.rem(step, 2)
        w_load(step).wait()

        @pl.when(step < 7)
        def _():
            w_load(step + 1).start()

        there = pl.ds(pl.multiple_of(step * wide, 128), wide)
        term = contract(g_low[:, there], w_buf[slot], 1, 1)

        @pl.when(step == 0)
        def _():
            work[...] = term

        @pl.when(step > 0)
        def _():
            work[...] += term

        return carry

    lax.fori_loop(0, 8, back_out, 0)
    g_att[...] = work[...].astype(LOW)
    mid_load = pltpu.make_async_copy(mid_ref, work, load_sem.at[1])
    mid_load.start()
    swaps = []
    here = pl.ds(me * span, span)
    for i in range(1, 8):
        other = lax.rem(me + i, 8)
        lanes = pl.ds(pl.multiple_of(other * wide, 128), wide)
        for m in range(2):
            swaps.append(
                remote(
                    esend,
                    erecv,
                    2 * (i - 1) + m,
                    g_att.at[pl.ds(m * span, span), lanes],
                    g_heads.at[m, here],
                    other,
                )
            )
            swaps[-1].start()
    kept = [
        pltpu.make_async_copy(
            g_att.at[pl.ds(m * span, span), pl.ds(pl.multiple_of(me * wide, 128), wide)],
            g_heads.at[m, here],
            self_sem.at[m],
        )
        for m in range(2)
    ]
    for c in kept:
        c.start()

    own = width // 32
    for z in range(4):
        lanes = slice(z * 8 * own, (z + 1) * 8 * own)
        block = contract(tok_ref[:, lanes], g_low[...], 0, 0).astype(LOW)
        for s in range(8):
            go_part[s, z * own : (z + 1) * own, :] = block[s * own : (s + 1) * own]
    weights.start_pairs()
    for c in kept:
        c.wait()
    for c in swaps:
        c.wait_recv()
    weights.add_pairs()

    length = v_ref.shape[1]
    block = 256
    streams = v_ref.shape[0]
    pieces = length // rows

    def h_load(step):
        slot = lax.rem(step, 2)
        return pltpu.make_async_copy(
            h1_ref.at[step // pieces, pl.ds(lax.rem(step, pieces) * rows, rows)],
            h_buf.at[slot],
            h_sem.at[slot],
        )

    h_load(0).start()

    def back_stream(m, carry):
        gk_sum[...] = jnp.zeros_like(gk_sum)
        gv_sum[...] = jnp.zeros_like(gv_sum)
        for i in range(length // block):
            rows_i = slice(i * block, (i + 1) * block)
            seen = (i + 1) * block
            query, key = q_ref[m, rows_i, :], k_ref[m, :seen, :]
            g_query = jnp.zeros(query.shape, f32)
            first = first_of(lengths_ref, m, i * block, block)
            for head in range(wide // HEAD_V):
                lanes = slice(head * HEAD_V, (head + 1) * HEAD_V)
                scores, mask, weight = weights_of(query, key, head, first, i * block)
                denom = jnp.sum(weight, axis=1, keepdims=True)
                a = (g_heads[m, rows_i, lanes].astype(f32) / denom).astype(LOW)
                b = -jnp.sum(
                    a.astype(f32) * att_ref[m, rows_i, lanes].astype(f32), axis=1, keepdims=True
                )
                g_weight = contract(a, v_ref[m, :seen, lanes], 1, 1) + b
                slope = 1.0 / math.sqrt(QK_DIM) + scores * (1.0 / QK_DIM)
                g_scores = jnp.where(mask, g_weight * slope, 0.0).astype(LOW)
                g_query += head_lanes(dot(g_scores, key), head)
                gk_sum[:seen, :] += contract(g_scores, head_lanes(query, head), 0, 0)
                gv_sum[:seen, lanes] += contract(weight.astype(LOW), a, 0, 0)
            g_s[m, rows_i, wide : wide + qk] = g_query.astype(LOW)
        g_s[m, :, :wide] = gv_sum[...].astype(LOW)
        g_s[m, :, wide + qk : wide + 2 * qk] = gk_sum[...].astype(LOW)
        g_s[m, :, wide + 2 * qk :] = jnp.zeros((length, g_s.shape[2] - wide - 2 * qk), LOW)

        @pl.when(m == 0)
        def _():
            for c in held_loads:
                c.wait()
            outs.add_pairs()

        return carry

    lax.fori_loop(0, 2, back_stream, 0)
    weights.second()
    done.append(pltpu.make_async_copy(g_s, g_out, done_sem.at[1]))
    done[1].start()
    outs.second()

    def add_grads(step, carry):
        slot = lax.rem(step, 2)
        h_load(step).wait()

        @pl.when(step < streams * pieces - 1)
        def _():
            h_load(step + 1).start()

        there = pl.ds(pl.multiple_of(lax.rem(step, pieces) * rows, rows), rows)
        term = contract(h_buf[slot], g_s[step // pieces, there, :], 0, 0)

        @pl.when(step == 0)
        def _():
            sums[...] = term

        @pl.when(step > 0)
        def _():
            sums[...] += term

        return carry

    lax.fori_loop(0, streams * pieces, add_grads, 0)
    narrow = sums.shape[1]
    attn_ref[:, :narrow] = sums[...].astype(LOW)
    mid_load.wait()
    for part, total in enumerate((weights.upper_sum(), weights.lower_sum())):
        total = total.astype(LOW)
        for z in range(2):
            for i in range(8):
                start = ((2 * part + z) * 8 + i) * own
                attn_ref[start : start + own, narrow:] = total[
                    z * own : (z + 1) * own, i * wide : (i + 1) * wide
                ]
    output_ref[:half] = (work[:half] + outs.upper_sum()).astype(LOW)
    output_ref[half:] = (work[half:] + outs.lower_sum()).astype(LOW)
    for c in done:
        c.wait()
    for c in swaps:
        c.wait_send()
    weights.sent()
    outs.sent()


def layer_turn(gh, mid, cot, gains, wo_all, part, tok, query, key, value, att, lengths, h1, columns):
    rows, width = mid.shape
    streams, length, wide = value.shape
    qk = query.shape[2]
    shape = jax.ShapeDtypeStruct
    f32 = jnp.float32
    anywhere = pl.BlockSpec(memory_space=pl.ANY)
    in_vmem = pl.BlockSpec(memory_space=pltpu.VMEM)
    dma = pltpu.SemaphoreType.DMA
    vmem = pltpu.VMEM
    arriving = [
        vmem((4, rows, width), LOW),
        vmem((4, rows // 2, width), LOW),
        vmem((2, rows // 2, width), LOW),
    ]
    return pl.pallas_call(
        turn_kernel,
        out_shape=[
            shape((rows, width), LOW),
            shape((rows, width), f32),
            shape((streams, length, columns), LOW),
            shape((8, width), f32),
            shape((width, columns + wide), LOW),
        ],
        in_specs=[anywhere] * 3
        + [in_vmem]
        + [anywhere] * 2
        + [in_vmem] * 5
        + [pl.BlockSpec(memory_space=pltpu.SMEM), anywhere],
        out_specs=[in_vmem, anywhere, anywhere, in_vmem, in_vmem],
        scratch_shapes=[
            vmem((rows, width), f32),
            vmem((rows, width), f32),
            vmem((rows, width), LOW),
            vmem((rows, width), LOW),
            vmem((streams, length, wide), LOW),
            vmem((streams, length, columns), LOW),
            vmem((2, width, wide), LOW),
            vmem((8, rows, width), LOW),
            vmem((4, rows, width), LOW),
            *arriving,
            *arriving,
            vmem((length, qk), f32),
            vmem((length, wide), f32),
            vmem((2, rows, width), LOW),
            vmem((width, columns), f32),
            dma((14,)),
            dma((14,)),
            dma((2, 10)),
            dma((2, 10)),
            dma((7,)),
            dma((2,)),
            dma((2,)),
            dma((2,)),
            dma((2,)),
        ],
        compiler_params=pltpu.CompilerParams(
            collective_id=22, has_side_effects=True, vmem_limit_bytes=63 * MIB
        ),
        cost_estimate=moved(16 * rows * width),
        name="turn",
    )(gh, mid, cot, gains, wo_all, part, tok, query, key, value, att, lengths, h1)


def close_kernel(
    g_ref,
    wa_ref,
    g_mid_ref,
    x_ref,
    gain_ref,
    sum_ref,
    blocks_ref,
    rest_ref,
    grad_ref,
    gains_ref,
    first_got,
    rest_got,
    beside,
    held,
    got,
    one,
    two,
    gain_rows,
    gain_line,
    gain_columns,
    gain_plane,
    blocks,
    first_sum,
    ssend,
    srecv,
    zsend,
    zrecv,
    esend,
    erecv,
    self_sem,
    fsend,
    frecv,
    f_sem,
):
    me, sib, xn, yn = partners()
    z = lax.axis_index("dp")
    rows, width = x_ref.shape
    span = rows // 2
    half = rows // 2
    f32 = jnp.float32
    barrier = pltpu.get_barrier_semaphore()
    for i in range(1, 8):
        pl.semaphore_signal(
            barrier, inc=1, device_id={"seq": lax.rem(me + i, 8)}, device_id_type=MESH
        )
    for i in range(1, 4):
        pl.semaphore_signal(
            barrier, inc=1, device_id={"dp": lax.rem(z + i, 4)}, device_id_type=MESH
        )
    pl.semaphore_wait(barrier, 10)
    load = pltpu.make_async_copy(blocks_ref, blocks, f_sem.at[0])
    load.start()
    keep = first_got.shape[1]

    def exchange(item, source, target):
        mine = pltpu.make_async_copy(
            source.at[pl.ds(me * keep, keep)], target.at[me], f_sem.at[1 + item]
        )
        mine.start()
        copies = []
        for i in range(1, 8):
            other = lax.rem(me + i, 8)
            copies.append(
                remote(
                    fsend,
                    frecv,
                    7 * item + i - 1,
                    source.at[pl.ds(other * keep, keep)],
                    target.at[me],
                    other,
                )
            )
            copies[-1].start()
        return mine, copies

    moves = [exchange(1, rest_ref, rest_got)]
    scatter = PlaneScatter(
        lambda i: beside.at[i], lambda i: held.at[i], got, one, two, ssend, srecv
    )
    def part_of(owner):
        there = pl.ds(pl.multiple_of(owner * span, span), span)
        grads = jnp.concatenate([g_ref[0, there, :], g_ref[1, there, :]], axis=0)
        return contract(grads, wa_ref[...], 1, 1).astype(LOW)

    owners = chips()
    for i in (2, 1, 3, 0):
        beside[i] = part_of(owners[i] + sib - me)
        scatter.start_pair(i)
        held[i] = part_of(owners[i])
        scatter.add_pair(i)

    load.wait()
    for second in range(2):
        total = jnp.zeros(blocks.shape[2:], f32)
        for owner in range(4):
            came = jnp.abs(z - owner) < 3
            total = total + jnp.where(came, blocks[owner, second].astype(f32), 0.0)
        lanes_here = total.shape[1]
        first_sum[:, second * lanes_here : (second + 1) * lanes_here] = total.astype(LOW)
    moves.append(exchange(0, first_sum, first_got))

    scatter.second()

    x = x_ref[...].astype(f32)
    inverse = norm_scale(x)
    normed = x * inverse
    gain = gain_ref[0:1, :].astype(f32)

    def finish(start, g_h):
        part = slice(start, start + half)
        grad_ref[part] = g_mid_ref[part] + norm_backward(g_h, normed[part], inverse[part], gain)
        return jnp.sum(g_h * normed[part], axis=0, keepdims=True)

    gain_sum = finish(0, scatter.upper_sum()) + finish(half, scatter.lower_sum())

    both = jnp.concatenate([gain_sum, sum_ref[0:1, :], jnp.zeros((14, width), f32)], axis=0)
    gain_rows[...] = both.astype(LOW)
    depth = width // 4

    def lanes(owner):
        return pl.ds(pl.multiple_of(owner * depth, 128), depth)

    def over_line(k, to, owner):
        return pltpu.make_async_remote_copy(
            src_ref=gain_rows.at[:, lanes(to)],
            dst_ref=gain_line.at[owner],
            send_sem=zsend.at[k],
            recv_sem=zrecv.at[owner],
            device_id={"dp": to},
            device_id_type=MESH,
        )

    others = [lax.rem(z + o, 4) for o in (1, 2, 3)]
    sends = [over_line(k, other, z) for k, other in enumerate(others)]
    own = pltpu.make_async_copy(gain_rows.at[:, lanes(z)], gain_line.at[z], self_sem.at[0])
    own.start()
    for c in sends:
        c.start()
    own.wait()
    for other in others:
        over_line(0, other, other).wait_recv()
    total = gain_line[0].astype(f32)
    for k in range(1, 4):
        total = total + gain_line[k].astype(f32)
    entry = lax.broadcasted_iota(jnp.int32, (16, 128), 0)
    lane = lax.broadcasted_iota(jnp.int32, (16, 128), 1)
    pick = jnp.where(lane == entry, 1.0, 0.0).astype(LOW)
    gain_columns[...] = contract(total.astype(LOW), pick, 0, 0).astype(LOW)
    count = depth // 8
    own = pltpu.make_async_copy(
        gain_columns.at[pl.ds(me * count, count)], gain_plane.at[me], self_sem.at[1]
    )
    own.start()
    swaps = []
    for i in range(1, 8):
        other = lax.rem(me + i, 8)
        swaps.append(
            remote(
                esend,
                erecv,
                i - 1,
                gain_columns.at[pl.ds(other * count, count)],
                gain_plane.at[me],
                other,
            )
        )
        swaps[-1].start()
    own.wait()
    for c in swaps:
        c.wait_recv()
    total = gain_plane[0].astype(f32)
    for k in range(1, 8):
        total = total + gain_plane[k].astype(f32)
    gains_ref[...] = total
    scatter.sent()
    for c in (*sends, *swaps):
        c.wait_send()
    for mine, copies in moves:
        mine.wait()
        for c in copies:
            c.wait()


def layer_close(g_all, wa, g_mid, tokens, gains, gain_sum, blocks, rest):
    rows, width = tokens.shape
    shape = jax.ShapeDtypeStruct
    in_vmem = pl.BlockSpec(memory_space=pltpu.VMEM)
    anywhere = pl.BlockSpec(memory_space=pl.ANY)
    dma = pltpu.SemaphoreType.DMA
    vmem = pltpu.VMEM
    return pl.pallas_call(
        close_kernel,
        out_shape=[
            shape((rows, width), jnp.float32),
            shape((width // 32, 128), jnp.float32),
            shape((8, width // 32, 8 * CHUNKS[0]), LOW),
            shape((8, width // 32, rest.shape[1]), LOW),
        ],
        in_specs=[in_vmem] * 6 + [anywhere] * 2,
        out_specs=[in_vmem, in_vmem, anywhere, anywhere],
        scratch_shapes=[
            vmem((4, rows, width), LOW),
            vmem((4, rows, width), LOW),
            vmem((4, rows, width), LOW),
            vmem((4, rows // 2, width), LOW),
            vmem((2, rows // 2, width), LOW),
            vmem((16, width), LOW),
            vmem((4, 16, width // 4), LOW),
            vmem((width // 4, 128), LOW),
            vmem((8, width // 32, 128), LOW),
            vmem(blocks.shape, LOW),
            vmem((width // 4, 8 * CHUNKS[0]), LOW),
            dma((10,)),
            dma((10,)),
            dma((3,)),
            dma((4,)),
            dma((7,)),
            dma((7,)),
            dma((2,)),
            dma((14,)),
            dma((14,)),
            dma((3,)),
        ],
        compiler_params=pltpu.CompilerParams(
            collective_id=23, has_side_effects=True, vmem_limit_bytes=56 * MIB
        ),
        cost_estimate=moved(16 * rows * width),
        name="close",
    )(g_all, wa, g_mid, tokens, gains, gain_sum, blocks, rest)


def place_kernel(
    first_ref,
    rest_ref,
    blocks_ref,
    down_ref,
    out_ref,
    grad_ref,
    gate_out,
    up_out,
    down_out,
    out_copy,
    grad_copy,
    sems,
):
    copies = [
        pltpu.make_async_copy(out_ref, out_copy, sems.at[0]),
        pltpu.make_async_copy(grad_ref, grad_copy, sems.at[1]),
    ]
    for c in copies:
        c.start()
    f32 = jnp.float32
    z = lax.axis_index("dp")
    share = sum(CHUNKS)
    for second, target in enumerate((gate_out, up_out)):
        for owner in range(8):
            for group in range(4):
                at = group * 8 * share + owner * share
                start = 0
                for k, count in enumerate(CHUNKS):
                    source = first_ref if k == 0 else rest_ref
                    begin = start + (4 * second + group) * count
                    target[:, at : at + count] = source[owner, :, begin : begin + count].astype(f32)
                    at += count
                    start += 8 * count if k else 0
    total = jnp.zeros(blocks_ref.shape[1:], f32)
    for owner in range(4):
        came = jnp.abs(z - owner) < 3
        total = total + jnp.where(came, blocks_ref[owner].astype(f32), 0.0)
    down_out[: CHUNKS[0], :] = total
    down_out[CHUNKS[0] :, :] = down_ref[...].astype(f32)
    for c in copies:
        c.wait()


def place_rows(first, rest, blocks, down, output, input_grad):
    own, width = first.shape[1], blocks.shape[2]
    shape = jax.ShapeDtypeStruct
    anywhere = pl.BlockSpec(memory_space=pl.ANY)
    in_vmem = pl.BlockSpec(memory_space=pltpu.VMEM)
    wide = 32 * sum(CHUNKS)
    return pl.pallas_call(
        place_kernel,
        out_shape=[
            shape((own, wide), jnp.float32),
            shape((own, wide), jnp.float32),
            shape((sum(CHUNKS), width), jnp.float32),
            shape(output.shape, output.dtype),
            shape(input_grad.shape, input_grad.dtype),
        ],
        in_specs=[in_vmem] * 4 + [anywhere] * 2,
        out_specs=[in_vmem] * 3 + [anywhere] * 2,
        scratch_shapes=[pltpu.SemaphoreType.DMA((2,))],
        compiler_params=pltpu.CompilerParams(vmem_limit_bytes=40 * MIB),
        name="place",
    )(first, rest, blocks, down, output, input_grad)


def place_attn_kernel(got_ref, out_ref, query_out, key_out, value_out, grad_out):
    f32 = jnp.float32
    wide = value_out.shape[1] // 8
    qk = query_out.shape[1] // 8
    own = out_ref.shape[0] // 8
    for owner in range(8):
        value_out[:, owner * wide : (owner + 1) * wide] = got_ref[owner, :, :wide].astype(f32)
        here = slice(owner * qk, (owner + 1) * qk)
        query_out[:, here] = got_ref[owner, :, wide : wide + qk].astype(f32)
        key_out[:, here] = got_ref[owner, :, wide + qk : wide + 2 * qk].astype(f32)
        block = out_ref[owner * own : (owner + 1) * own, out_ref.shape[1] - wide :]
        grad_out[:, owner * wide : (owner + 1) * wide] = block.astype(f32)


def place_attn(got, summed, wide, qk):
    own = got.shape[1]
    shape = jax.ShapeDtypeStruct
    in_vmem = pl.BlockSpec(memory_space=pltpu.VMEM)
    return pl.pallas_call(
        place_attn_kernel,
        out_shape=[
            shape((own, 8 * qk), jnp.float32),
            shape((own, 8 * qk), jnp.float32),
            shape((own, 8 * wide), jnp.float32),
            shape((own, 8 * wide), jnp.float32),
        ],
        in_specs=[in_vmem] * 2,
        out_specs=[in_vmem] * 4,
        name="place_attn",
    )(got, summed)


def ffn_lax(h_two, cot_all, gate_full, up_full, down_full):
    pieces, rows, width = cot_all.shape
    h_two_all = gather_plane(h_two, 5).reshape(-1, width)
    cot_all = cot_all.reshape(-1, width)
    gate = dot(h_two_all, gate_full)
    up = dot(h_two_all, up_full)
    g_act = contract(cot_all, down_full, 1, 1)
    sigmoid = jax.nn.sigmoid(gate)
    silu = gate * sigmoid
    act = (silu * up).astype(LOW)
    g_gate = (g_act * up * sigmoid * (1.0 + gate * (1.0 - sigmoid))).astype(LOW)
    g_up = (g_act * silu).astype(LOW)
    part = (contract(g_gate, gate_full, 1, 1) + contract(g_up, up_full, 1, 1)).astype(LOW)
    return (
        dot(act, down_full).astype(LOW).reshape(pieces, rows, width),
        scatter_plane(part.reshape(pieces, rows, width), 7),
        contract(h_two_all, g_gate, 0, 0).astype(LOW),
        contract(h_two_all, g_up, 0, 0).astype(LOW),
        contract(act, cot_all, 0, 0).astype(LOW),
    )


def norm_scale(rows):
    return lax.rsqrt(jnp.mean(rows * rows, axis=-1, keepdims=True) + epsilon)


def norm_backward(grad, normed, inverse, gain):
    scaled = grad * gain
    return inverse * (scaled - normed * jnp.mean(scaled * normed, axis=-1, keepdims=True))


def local(
    tokens,
    doc_lengths,
    w_query,
    w_key,
    w_value,
    w_out,
    w_gate,
    w_up,
    w_down,
    gain_attn,
    gain_mlp,
    cotangent,
):
    micro, span = tokens.shape[1:3]
    pieces, groups = lax.axis_size("seq"), lax.axis_size("dp")
    place = lax.axis_index("seq")
    length = pieces * span
    heads = max(1, HEADS // pieces)
    sharers = max(1, pieces // HEADS)
    streams = micro // sharers
    first_head = place // sharers * heads
    first_stream = place % sharers * streams
    qk, wide = heads * QK_DIM, heads * HEAD_V
    hidden = FF // pieces

    out_width = D // pieces
    rows_dp = w_gate.shape[0]
    share = hidden // groups
    block = FF // groups
    mine = micro * span
    fused = pieces == 8 and groups == 4 and micro == 2 and span == 128
    chunks = CHUNKS if fused else (share,)

    def hidden_columns(w):
        parts = [
            lax.dynamic_slice_in_dim(w, z * block + place * share, share, 1) for z in range(groups)
        ]
        edges = [sum(chunks[:k]) for k in range(len(chunks) + 1)]
        return [
            [part[:, edges[k] : edges[k + 1]] for part in parts] for k in range(len(chunks))
        ]

    x_own = tokens[0].reshape(mine, D)
    flat = x_own.astype(jnp.float32)
    cot = cotangent[0].reshape(mine, D)

    def to_tokens(by_head):
        sent = by_head.reshape(streams, pieces, span, wide).transpose(1, 0, 2, 3)
        got = exchange_plane(sent, 3).reshape(pieces // sharers, micro, span, wide)
        return got.transpose(1, 2, 0, 3).reshape(mine, HEADS * HEAD_V)

    def to_heads(by_token):
        sent = by_token.reshape(micro, span, pieces // sharers, wide).transpose(2, 0, 1, 3)
        got = exchange_plane(sent.reshape(pieces, streams, span, wide), 4)
        return got.transpose(1, 0, 2, 3).reshape(streams, length, wide)

    if fused:
        gain_rows = jnp.concatenate(
            [gain_attn[None], gain_mlp[None], jnp.zeros((14, rows_dp), LOW)], axis=0
        )
        weights = (w_query, w_key, w_value, w_out, w_gate, w_up, w_down)
        front = layer_front(x_own, cot, weights, gain_rows, doc_lengths[0], length, wide, qk)
        out_full, h_all, query, key, value, att_heads, attended, mid = front[3:11]
        attn_full, gain_rows_all, out_part, g_h_two = front[11:15]
        d_ffn, d_down, ffn_blocks, down_blocks = front[17:]
    else:
        gate_parts, up_parts = hidden_columns(w_gate), hidden_columns(w_up)
        ffn_slice = jnp.concatenate(
            [part for k in range(len(chunks)) for part in gate_parts[k] + up_parts[k]], axis=1
        )
        attn_parts = [
            lax.dynamic_slice_in_dim(w_value, first_head * HEAD_V, wide, 1),
            lax.dynamic_slice_in_dim(w_query, first_head * QK_DIM, qk, 1),
            lax.dynamic_slice_in_dim(w_key, first_head * QK_DIM, qk, 1),
        ]

        lengths = lax.dynamic_slice_in_dim(doc_lengths[0], first_stream, streams, 0)
        starts = jnp.cumsum(lengths, axis=1) - lengths
        position = jnp.arange(length, dtype=jnp.int32)
        begun = starts[:, None, :] <= position[None, :, None]
        first = jnp.max(jnp.where(begun, starts[:, None, :], 0), axis=2)[..., None]

        def gather_dp(w):
            return lax.all_gather(w, "dp", axis=0, tiled=True)

        attn_got = gather_dp(
            jnp.concatenate(
                attn_parts
                + [
                    lax.dynamic_slice_in_dim(w_out, place * out_width, out_width, 1),
                    gain_attn[:, None],
                    gain_mlp[:, None],
                ],
                axis=1,
            )
        )
        ffn_full = gather_dp(ffn_slice)
        down_full = gather_dp(lax.dynamic_slice_in_dim(w_down, place * share, share, 0))
        value_full = attn_got[:, :wide]
        query_full = attn_got[:, wide : wide + qk]
        key_full = attn_got[:, wide + qk : wide + 2 * qk]
        out_full = gather_plane(attn_got[:, wide + 2 * qk : wide + 2 * qk + out_width], 2)
        gains = attn_got[:, wide + 2 * qk + out_width :].astype(jnp.float32)
        gain_one, gain_two = gains[:, 0], gains[:, 1]
        x_all = gather_plane(x_own, 1).reshape(pieces, micro, span, D).transpose(1, 0, 2, 3)
        x_all = lax.dynamic_slice_in_dim(x_all, first_stream, streams, 0).astype(jnp.float32)
        h_flat = (x_all * norm_scale(x_all) * gain_one).astype(LOW).reshape(streams * length, D)
        value = dot(h_flat, value_full).astype(LOW).reshape(streams, length, wide)
        query = dot(h_flat, query_full).astype(LOW).reshape(streams, length, qk)
        key = dot(h_flat, key_full).astype(LOW).reshape(streams, length, qk)
        att_heads = attend(query, key, value, first, heads)
        attended = to_tokens(att_heads)
        mid = flat + jnp.einsum(
            "tk,skn->tsn", attended, out_full, preferred_element_type=jnp.float32
        ).reshape(mine, D)
        h_two = (mid * norm_scale(mid) * gain_two).astype(LOW)
        out_part, g_h_two, d_gate, d_up, d_down = ffn_lax(
            h_two, gather_plane(cot, 6), ffn_full[:, :hidden], ffn_full[:, hidden:], down_full
        )
        d_ffn = jnp.concatenate([d_gate, d_up], axis=1)

    def scatter_dp(part):
        return lax.psum_scatter(part, "dp", scatter_dimension=0, tiled=True)

    own = rows_dp // pieces
    sum_ffn, sum_down = scatter_dp(d_ffn), scatter_dp(d_down)

    if fused:
        output, g_mid, g_all, gain_sum, grad_attn = layer_turn(
            g_h_two, mid, cot, gain_rows_all, out_full, out_part, attended, query, key, value,
            att_heads, doc_lengths[0], h_all, attn_full.shape[1],
        )
        grad_attn, sum_ffn, sum_down = lax.optimization_barrier((grad_attn, sum_ffn, sum_down))
        grad_attn = scatter_dp(grad_attn)
        input_grad, gain_columns, first_got, rest_got = layer_close(
            g_all, attn_full, g_mid, x_own, gain_rows_all, gain_sum, ffn_blocks, sum_ffn
        )
        grad_gate, grad_up, grad_down, output, input_grad = place_rows(
            first_got, rest_got, down_blocks, sum_down, output, input_grad
        )
        grad_attn, grad_gate = lax.optimization_barrier((grad_attn, grad_gate))
        attn_got = exchange_plane(grad_attn[:, : attn_full.shape[1]].reshape(pieces, own, -1), 12)
        grad_query, grad_key, grad_value, grad_out = place_attn(attn_got, grad_attn, wide, qk)
        return (
            output.reshape(tokens.shape),
            input_grad.reshape(tokens.shape),
            grad_query,
            grad_key,
            grad_value,
            grad_out,
            grad_gate,
            grad_up,
            grad_down,
            gain_columns[:, 0],
            gain_columns[:, 1],
        )

    inverse_two = norm_scale(mid)
    plain_two = mid * inverse_two
    output = (mid + scatter_plane(out_part, 8)).astype(LOW)
    g_mid = cot.astype(jnp.float32) + norm_backward(g_h_two, plain_two, inverse_two, gain_two)
    g_mid_low = g_mid.astype(LOW)
    g_att = jnp.einsum(
        "tsn,skn->tk",
        g_mid_low.reshape(mine, pieces, out_width),
        out_full,
        preferred_element_type=jnp.float32,
    )
    g_att = to_heads(g_att.astype(LOW))
    g_query, g_key, g_value = attend_back(query, key, value, first, att_heads, g_att, heads)
    g_value = g_value.reshape(streams * length, wide)
    g_query = g_query.reshape(streams * length, qk)
    g_key = g_key.reshape(streams * length, qk)
    g_h_one_part = (
        contract(g_value, value_full, 1, 1)
        + contract(g_query, query_full, 1, 1)
        + contract(g_key, key_full, 1, 1)
    ).astype(LOW)
    g_h_one_part = g_h_one_part.reshape(streams, pieces, span, D).transpose(1, 0, 2, 3)
    if sharers > 1:
        padded = jnp.zeros((pieces, micro, span, D), LOW)
        g_h_one_part = lax.dynamic_update_slice_in_dim(padded, g_h_one_part, first_stream, 1)
    g_h_one = scatter_plane(g_h_one_part.reshape(pieces, mine, D), 9)
    inverse_one = norm_scale(flat)
    plain_one = flat * inverse_one
    input_grad = g_mid + norm_backward(g_h_one, plain_one, inverse_one, gain_one)
    grad_out = contract(attended, g_mid_low, 0, 0).astype(LOW)
    grad_out = grad_out.reshape(groups, pieces, own, D).transpose(1, 0, 2, 3)
    grad_out = scatter_plane(grad_out.reshape(pieces, groups * own, D), 10).astype(LOW)
    grad_out = scatter_dp(grad_out)
    grad_attn = jnp.concatenate(
        [
            contract(h_flat, g_value, 0, 0).astype(LOW),
            contract(h_flat, g_query, 0, 0).astype(LOW),
            contract(h_flat, g_key, 0, 0).astype(LOW),
            jnp.sum(g_h_one * plain_one, axis=0).astype(LOW)[:, None],
            jnp.sum(g_h_two * plain_two, axis=0).astype(LOW)[:, None],
        ],
        axis=1,
    )

    grad_attn = scatter_dp(grad_attn)
    ffn_got = exchange_plane(sum_ffn.reshape(pieces, own, 2 * hidden), 11).astype(jnp.float32)
    attn_got = exchange_plane(grad_attn.reshape(pieces, own, -1), 12).astype(jnp.float32)
    grad_gains = jnp.sum(attn_got[:, :, wide + 2 * qk :], axis=0)
    attn_got = jnp.sum(attn_got.reshape(pieces // sharers, sharers, own, -1), axis=1)

    def by_hidden(block):
        return block.reshape(pieces, own, groups, share).transpose(1, 2, 0, 3).reshape(own, FF)

    def by_rows(block):
        return block.transpose(1, 0, 2).reshape(own, -1)

    return (
        output.reshape(tokens.shape),
        input_grad.reshape(tokens.shape),
        by_rows(attn_got[:, :, wide : wide + qk]),
        by_rows(attn_got[:, :, wide + qk : wide + 2 * qk]),
        by_rows(attn_got[:, :, :wide]),
        grad_out.astype(jnp.float32),
        by_hidden(ffn_got[:, :, :hidden]),
        by_hidden(ffn_got[:, :, hidden:]),
        sum_down.astype(jnp.float32),
        grad_gains[:, 0],
        grad_gains[:, 1],
    )


def solution(mesh):
    by_token, by_row = P("dp", None, "seq", None), P("dp", None)
    grad_rows, grad_entries = P(("dp", "seq"), None), P(("dp", "seq"))
    return jax.shard_map(
        local,
        mesh=mesh,
        in_specs=(by_token, P("dp", None, None)) + (by_row,) * 7 + (P("dp"), P("dp"), by_token),
        out_specs=(by_token, by_token) + (grad_rows,) * 7 + (grad_entries,) * 2,
        check_vma=False,
    )
```

```python
import functools
import math

import jax
import jax.numpy as jnp
from jax import lax
from jax.experimental import pallas as pl
from jax.experimental.pallas import tpu as pltpu
from jax.sharding import PartitionSpec as P

D = 2048
HEADS = 16
QK_DIM = 16
FF = 5632
HEAD_V = 128
epsilon = 1e-06
MIB = 1024 * 1024


def dot(left, right):
    return jnp.dot(left, right, preferred_element_type=jnp.float32)


def contract(left, right, left_dim, right_dim):
    return lax.dot_general(
        left, right, (((left_dim,), (right_dim,)), ((), ())), preferred_element_type=jnp.float32
    )


def head_lanes(rows, head):
    lane = lax.broadcasted_iota(jnp.int32, rows.shape, 1)
    inside = (lane >= head * QK_DIM) & (lane < (head + 1) * QK_DIM)
    return jnp.where(inside, rows, jnp.zeros_like(rows))


def weights_of(query, key, head, first, base):
    scores = contract(head_lanes(query, head), key, 1, 1)
    row = base + lax.broadcasted_iota(jnp.int32, scores.shape, 0)
    column = lax.broadcasted_iota(jnp.int32, scores.shape, 1)
    mask = (column <= row) & (column >= first)
    poly = 1.0 + scores * (1.0 / math.sqrt(QK_DIM)) + scores * scores * (0.5 / QK_DIM)
    return scores, mask, jnp.where(mask, poly, 0.0)


def attend_kernel(heads, q_ref, k_ref, v_ref, first_ref, out_ref):
    rows = q_ref.shape[1]
    base = pl.program_id(1) * rows
    for head in range(heads):
        columns = slice(head * HEAD_V, (head + 1) * HEAD_V)
        unused, unused_mask, weight = weights_of(
            q_ref[0], k_ref[0], head, first_ref[0], base
        )
        denom = jnp.sum(weight, axis=1, keepdims=True)
        numer = dot(weight.astype(jnp.bfloat16), v_ref[0, :, columns])
        out_ref[0, :, columns] = (numer / denom).astype(jnp.bfloat16)


def attend(query, key, value, first, heads):
    streams, length, width = query.shape
    rows = min(256, length)
    return pl.pallas_call(
        functools.partial(attend_kernel, heads),
        grid=(streams, length // rows),
        in_specs=[
            pl.BlockSpec((1, rows, width), lambda m, i: (m, i, 0)),
            pl.BlockSpec((1, length, width), lambda m, i: (m, 0, 0)),
            pl.BlockSpec((1, length, heads * HEAD_V), lambda m, i: (m, 0, 0)),
            pl.BlockSpec((1, rows, 1), lambda m, i: (m, i, 0)),
        ],
        out_specs=pl.BlockSpec((1, rows, heads * HEAD_V), lambda m, i: (m, i, 0)),
        out_shape=jax.ShapeDtypeStruct(value.shape, jnp.bfloat16),
        compiler_params=pltpu.CompilerParams(vmem_limit_bytes=48 * MIB),
        name="attend",
    )(query, key, value, first)


def attend_back_kernel(
    heads, q_ref, k_ref, v_ref, first_ref, att_ref, g_ref, gq_ref, gk_ref, gv_ref, gk_sum, gv_sum
):
    rows = q_ref.shape[1]
    step = pl.program_id(1)
    base = step * rows

    @pl.when(step == 0)
    def _():
        gk_sum[...] = jnp.zeros_like(gk_sum)
        gv_sum[...] = jnp.zeros_like(gv_sum)

    query, key = q_ref[0], k_ref[0]
    g_query = jnp.zeros(query.shape, jnp.float32)
    for head in range(heads):
        columns = slice(head * HEAD_V, (head + 1) * HEAD_V)
        scores, mask, weight = weights_of(query, key, head, first_ref[0], base)
        denom = jnp.sum(weight, axis=1, keepdims=True)
        a = (g_ref[0, :, columns].astype(jnp.float32) / denom).astype(jnp.bfloat16)
        b = -jnp.sum(
            a.astype(jnp.float32) * att_ref[0, :, columns].astype(jnp.float32),
            axis=1,
            keepdims=True,
        )
        g_weight = contract(a, v_ref[0, :, columns], 1, 1) + b
        slope = 1.0 / math.sqrt(QK_DIM) + scores * (1.0 / QK_DIM)
        g_scores = jnp.where(mask, g_weight * slope, 0.0).astype(jnp.bfloat16)
        g_query += head_lanes(dot(g_scores, key), head)
        gk_sum[...] += contract(g_scores, head_lanes(query, head), 0, 0)
        gv_sum[:, columns] += contract(weight.astype(jnp.bfloat16), a, 0, 0)
    gq_ref[0] = g_query.astype(jnp.bfloat16)

    @pl.when(step == pl.num_programs(1) - 1)
    def _():
        gk_ref[0] = gk_sum[...].astype(jnp.bfloat16)
        gv_ref[0] = gv_sum[...].astype(jnp.bfloat16)


def attend_back(query, key, value, first, attended, grad, heads):
    streams, length, width = query.shape
    rows = min(256, length)
    some = pl.BlockSpec((1, rows, width), lambda m, i: (m, i, 0))
    all_narrow = pl.BlockSpec((1, length, width), lambda m, i: (m, 0, 0))
    all_wide = pl.BlockSpec((1, length, heads * HEAD_V), lambda m, i: (m, 0, 0))
    some_wide = pl.BlockSpec((1, rows, heads * HEAD_V), lambda m, i: (m, i, 0))
    return pl.pallas_call(
        functools.partial(attend_back_kernel, heads),
        grid=(streams, length // rows),
        in_specs=[
            some,
            all_narrow,
            all_wide,
            pl.BlockSpec((1, rows, 1), lambda m, i: (m, i, 0)),
            some_wide,
            some_wide,
        ],
        out_specs=[some, all_narrow, all_wide],
        out_shape=[
            jax.ShapeDtypeStruct(query.shape, jnp.bfloat16),
            jax.ShapeDtypeStruct(key.shape, jnp.bfloat16),
            jax.ShapeDtypeStruct(value.shape, jnp.bfloat16),
        ],
        scratch_shapes=[
            pltpu.VMEM((length, width), jnp.float32),
            pltpu.VMEM((length, heads * HEAD_V), jnp.float32),
        ],
        compiler_params=pltpu.CompilerParams(vmem_limit_bytes=56 * MIB),
        name="attend_back",
    )(query, key, value, first, attended, grad)

MESH = pl.DeviceIdType.MESH
LOW = jnp.bfloat16


def partners():
    me = lax.axis_index("seq")
    core, x, y = me % 2, me // 2 % 2, me // 4
    return me, me + 1 - 2 * core, me + 2 - 4 * x, me + 4 - 8 * y


def greet(others):
    barrier = pltpu.get_barrier_semaphore()
    for other in others:
        pl.semaphore_signal(barrier, inc=1, device_id={"seq": other}, device_id_type=MESH)
    pl.semaphore_wait(barrier, len(others))


def remote(send, recv, k, src, dst, to):
    return pltpu.make_async_remote_copy(
        src_ref=src,
        dst_ref=dst,
        send_sem=send.at[k],
        recv_sem=recv.at[k],
        device_id={"seq": to},
        device_id_type=MESH,
    )


def gather_kernel(x_ref, o_ref, send, recv, own_sem):
    me, sib, xn, yn = partners()
    diag = xn + yn - me
    half = x_ref.shape[0] // 2
    copy = functools.partial(remote, send, recv)
    upper, lower = pl.ds(0, half), pl.ds(half, half)
    greet((sib, xn, yn))
    own = pltpu.make_async_copy(x_ref, o_ref.at[me], own_sem)
    own.start()
    xa = copy(0, x_ref.at[upper], o_ref.at[me, upper], xn)
    yb = copy(1, x_ref.at[lower], o_ref.at[me, lower], yn)
    xb = copy(2, x_ref.at[lower], o_ref.at[me, lower], xn)
    ya = copy(3, x_ref.at[upper], o_ref.at[me, upper], yn)
    beside = [copy(4, x_ref, o_ref.at[me], sib)]
    started = [xa, yb, xb, ya, beside[0]]
    for c in started:
        c.start()

    def pass_on(k, origin, part, to):
        block = o_ref.at[origin, part]
        c = copy(k, block, block, to)
        c.start()
        started.append(c)
        return c

    xa.wait_recv()
    fy = pass_on(5, xn, upper, yn)
    beside.append(pass_on(6, xn, upper, sib))
    yb.wait_recv()
    fx = pass_on(7, yn, lower, xn)
    beside.append(pass_on(8, yn, lower, sib))
    xb.wait_recv()
    beside.append(pass_on(9, xn, lower, sib))
    ya.wait_recv()
    beside.append(pass_on(10, yn, upper, sib))
    fy.wait_recv()
    beside.append(pass_on(11, diag, upper, sib))
    fx.wait_recv()
    beside.append(pass_on(12, diag, lower, sib))
    own.wait()
    for c in beside:
        c.wait_recv()
    for c in started:
        c.wait_send()


def moved(nbytes):
    return pl.CostEstimate(flops=0, bytes_accessed=nbytes * 10, transcendentals=0)


def gather_plane(x, number):
    pieces = lax.axis_size("seq")
    if pieces != 8:
        return lax.all_gather(x, "seq", axis=0)
    return pl.pallas_call(
        gather_kernel,
        out_shape=jax.ShapeDtypeStruct((8,) + x.shape, x.dtype),
        in_specs=[pl.BlockSpec(memory_space=pl.ANY)],
        out_specs=pl.BlockSpec(memory_space=pl.ANY),
        scratch_shapes=[
            pltpu.SemaphoreType.DMA((13,)),
            pltpu.SemaphoreType.DMA((13,)),
            pltpu.SemaphoreType.DMA,
        ],
        compiler_params=pltpu.CompilerParams(collective_id=number, has_side_effects=True),
        cost_estimate=moved(16 * x.size),
        name="gather",
    )(x)


def scatter_kernel(p_ref, o_ref, held, got, one, two, send, recv, own_sem):
    me, sib, xn, yn = partners()
    diag = xn + yn - me
    half = p_ref.shape[1] // 2
    copy = functools.partial(remote, send, recv)
    upper, lower = pl.ds(0, half), pl.ds(half, half)
    greet((sib, xn, yn))
    beside, loads = [], []
    for i, owner in enumerate((diag, xn, yn, me)):
        beside.append(copy(i, p_ref.at[owner + sib - me], got.at[i], sib))
        loads.append(pltpu.make_async_copy(p_ref.at[owner], held.at[i], own_sem.at[i]))
        beside[i].start()
        loads[i].start()

    def pair_sum(i):
        beside[i].wait_recv()
        loads[i].wait()
        held[i] = held[i] + got[i]

    pair_sum(0)
    x0 = copy(4, held.at[0, upper], one.at[0], xn)
    x0.start()
    y0 = copy(5, held.at[0, lower], one.at[1], yn)
    y0.start()
    pair_sum(1)
    x1 = copy(6, held.at[1, upper], one.at[2], xn)
    x1.start()
    pair_sum(2)
    y1 = copy(7, held.at[2, lower], one.at[3], yn)
    y1.start()
    pair_sum(3)
    x0.wait_recv()
    held[2, :half] = held[2, :half] + one[0]
    y2 = copy(8, held.at[2, upper], two.at[0], yn)
    y2.start()
    y0.wait_recv()
    held[1, half:] = held[1, half:] + one[1]
    x2 = copy(9, held.at[1, lower], two.at[1], xn)
    x2.start()
    x1.wait_recv()
    y1.wait_recv()
    y2.wait_recv()
    wide = jnp.float32
    o_ref[:half] = held[3, :half].astype(wide) + one[2].astype(wide) + two[0].astype(wide)
    x2.wait_recv()
    o_ref[half:] = held[3, half:].astype(wide) + one[3].astype(wide) + two[1].astype(wide)
    for c in (*beside, x0, y0, x1, y1, y2, x2):
        c.wait_send()


def scatter_plane(part, number):
    pieces, rows, columns = part.shape
    if pieces != 8:
        return lax.psum_scatter(part, "seq", scatter_dimension=0).astype(jnp.float32)
    return pl.pallas_call(
        scatter_kernel,
        out_shape=jax.ShapeDtypeStruct((rows, columns), jnp.float32),
        in_specs=[pl.BlockSpec(memory_space=pl.ANY)],
        out_specs=pl.BlockSpec(memory_space=pltpu.VMEM),
        scratch_shapes=[
            pltpu.VMEM((4, rows, columns), LOW),
            pltpu.VMEM((4, rows, columns), LOW),
            pltpu.VMEM((4, rows // 2, columns), LOW),
            pltpu.VMEM((2, rows // 2, columns), LOW),
            pltpu.SemaphoreType.DMA((10,)),
            pltpu.SemaphoreType.DMA((10,)),
            pltpu.SemaphoreType.DMA((4,)),
        ],
        compiler_params=pltpu.CompilerParams(
            collective_id=number, has_side_effects=True, vmem_limit_bytes=40 * MIB
        ),
        cost_estimate=moved(2 * part.size),
        name="scatter",
    )(part)


def exchange_kernel(x_ref, o_ref, send, recv, own_sem):
    me = lax.axis_index("seq")
    columns = pl.ds(0, o_ref.shape[2])
    others = [lax.rem(me + i, 8) for i in range(1, 8)]
    greet(others)
    own = pltpu.make_async_copy(x_ref.at[me, :, columns], o_ref.at[me], own_sem)
    own.start()
    copies = [
        remote(send, recv, i, x_ref.at[other, :, columns], o_ref.at[me], other)
        for i, other in enumerate(others)
    ]
    for c in copies:
        c.start()
    own.wait()
    for c in copies:
        c.wait()


def exchange_plane(x, number, columns=None):
    if lax.axis_size("seq") != 8:
        return lax.all_to_all(x, "seq", 0, 0)
    return pl.pallas_call(
        exchange_kernel,
        out_shape=jax.ShapeDtypeStruct(x.shape[:-1] + (columns or x.shape[-1],), x.dtype),
        in_specs=[pl.BlockSpec(memory_space=pl.ANY)],
        out_specs=pl.BlockSpec(memory_space=pl.ANY),
        scratch_shapes=[
            pltpu.SemaphoreType.DMA((7,)),
            pltpu.SemaphoreType.DMA((7,)),
            pltpu.SemaphoreType.DMA,
        ],
        compiler_params=pltpu.CompilerParams(collective_id=number, has_side_effects=True),
        cost_estimate=moved(4 * x.size),
        name="exchange",
    )(x)


CHUNKS = (64, 64, 48)


class PlaneGather:
    def __init__(self, source, target, send, recv):
        me, sib, xn, yn = partners()
        diag = xn + yn - me
        half = target.shape[1] // 2
        upper, lower = pl.ds(0, half), pl.ds(half, half)
        copy = functools.partial(remote, send, recv)

        def direct(k, part, to):
            return copy(k, source.at[part], target.at[me, part], to)

        def pass_on(k, origin, part, to):
            return copy(k, target.at[origin, part], target.at[origin, part], to)

        self.xa, self.yb = direct(0, upper, xn), direct(1, lower, yn)
        self.xb, self.ya = direct(2, lower, xn), direct(3, upper, yn)
        self.s0 = copy(4, source, target.at[me], sib)
        self.fy, self.fx = pass_on(5, xn, upper, yn), pass_on(6, yn, lower, xn)
        self.s1, self.s2 = pass_on(7, xn, upper, sib), pass_on(8, yn, lower, sib)
        self.s3, self.s4 = pass_on(9, xn, lower, sib), pass_on(10, yn, upper, sib)
        self.s5, self.s6 = pass_on(11, diag, upper, sib), pass_on(12, diag, lower, sib)

    def start(self):
        for c in (self.xa, self.yb, self.xb, self.ya, self.s0):
            c.start()

    def forward_first(self):
        self.xa.wait_recv()
        self.yb.wait_recv()
        for c in (self.fy, self.fx, self.s1, self.s2):
            c.start()

    def forward_second(self):
        self.xb.wait_recv()
        self.ya.wait_recv()
        self.s3.start()
        self.s4.start()

    def forward_third(self):
        self.fy.wait_recv()
        self.fx.wait_recv()
        self.s5.start()
        self.s6.start()

    def from_sibling(self, chip):
        for c in {"own": (self.s0,), "x": (self.s1, self.s3), "y": (self.s2, self.s4), "diag": (self.s5, self.s6)}[chip]:
            c.wait_recv()

    def sent(self):
        for c in (self.xa, self.yb, self.xb, self.ya, self.s0, self.fy, self.fx):
            c.wait_send()
        for c in (self.s1, self.s2, self.s3, self.s4, self.s5, self.s6):
            c.wait_send()

    def arrive(self, step):
        @pl.when(step == 1)
        def _():
            self.from_sibling("own")

        @pl.when(step == 2)
        def _():
            self.forward_first()
            self.forward_second()
            self.from_sibling("x")

        @pl.when(step == 4)
        def _():
            self.from_sibling("y")

        @pl.when(step == 6)
        def _():
            self.forward_third()
            self.from_sibling("diag")


class LineGather:
    def __init__(self, item, source, block, send, recv, local=None):
        z = lax.axis_index("dp")
        self.z = z

        def copy(k, src, owner, to):
            return pltpu.make_async_remote_copy(
                src_ref=src,
                dst_ref=block(owner),
                send_sem=send.at[item, k],
                recv_sem=recv.at[item, owner],
                device_id={"dp": to},
                device_id_type=MESH,
            )

        self.sends = []
        for k, d in enumerate((2, -2, 1, -1)):
            to = z + d
            valid = (to >= 0) & (to < 4)
            self.sends.append((valid, copy(k, source, z, jnp.clip(to, 0, 3))))
        inner = (z == 1) | (z == 2)
        far = jnp.where(z == 1, 3, 0)
        self.stop = (inner, copy(4, block(far), far, jnp.where(z == 1, 0, 3)))
        others = [lax.rem(z + o, 4) for o in (1, 2, 3)]
        self.blocks = [copy(0, source, other, other) for other in others]
        self.own = None
        if local is not None:
            self.own = pltpu.make_async_copy(source, block(z), local.at[item])

    def start_far(self):
        if self.own is not None:
            self.own.start()
        self.begin(self.sends[:2])

    def start_near(self):
        self.begin(self.sends[2:])

    def start(self):
        self.start_far()
        self.start_near()

    def begin(self, sends):
        for valid, c in sends:

            @pl.when(valid)
            def _(c=c):
                c.start()

    def forward(self):
        inner, c = self.stop

        @pl.when(inner)
        def _():
            self.blocks[1].wait_recv()
            c.start()

    def wait(self):
        inner, unused = self.stop
        self.blocks[0].wait_recv()
        self.blocks[2].wait_recv()

        @pl.when(jnp.logical_not(inner))
        def _():
            self.blocks[1].wait_recv()

        if self.own is not None:
            self.own.wait()

    def sent(self):
        for valid, c in (*self.sends, self.stop):

            @pl.when(valid)
            def _(c=c):
                c.wait_send()


def nearest_first(step):
    me, sib, xn, yn = partners()
    chip = jnp.where(step < 4, xn, jnp.where(step < 6, yn, xn + yn - me))
    later = chip + jnp.where(lax.rem(step, 2) == 0, sib - me, 0)
    return jnp.where(step == 0, me, jnp.where(step == 1, sib, later))


def farthest_first(step):
    me, sib, xn, yn = partners()
    chip = jnp.where(step < 4, xn, yn)
    chip = jnp.where(step < 2, xn + yn - me, jnp.where(step < 6, chip, me))
    return chip + jnp.where(lax.rem(step, 2) == 0, sib - me, 0)


def first_of(lengths, stream, base, count):
    row = base + lax.broadcasted_iota(jnp.int32, (count, 1), 0)
    start, first = jnp.int32(0), jnp.zeros((count, 1), jnp.int32)
    for j in range(lengths.shape[1]):
        first = jnp.where(row >= start, start, first)
        start = start + lengths[stream, j]
    return first


def layer_kernel(
    x_ref,
    c_ref,
    wq_ref,
    wk_ref,
    wv_ref,
    wo_ref,
    wg_ref,
    wu_ref,
    wd_ref,
    gain_ref,
    lengths_ref,
    x_all,
    c_all,
    h2_all,
    wo_all,
    h1_out,
    q_out,
    k_out,
    v_out,
    att_out,
    tok_out,
    mid_out,
    wa_out,
    gain_out,
    out_part,
    gh_out,
    dgu_first,
    dd_first,
    dgu_out,
    dd_out,
    dgu_all,
    dd_all,
    wa,
    wgu,
    wd,
    gains,
    q_s,
    k_s,
    v_s,
    att_s,
    tok,
    mid,
    act_s,
    ggu_s,
    sum_gu,
    sum_d,
    x_buf,
    c_buf,
    o_buf,
    beside,
    held,
    got,
    one,
    two,
    gsend,
    grecv,
    zsend,
    zrecv,
    zlocal,
    esend,
    erecv,
    rsend,
    rrecv,
    load_sem,
    out_sem,
    h1_sem,
    w_sem,
    done_sem,
    self_sem,
    fsend,
    frecv,
    f_sem,
    cut_sem,
    gu_stop,
    d_stop,
):
    me, sib, xn, yn = partners()
    z = lax.axis_index("dp")
    rows, width = x_ref.shape
    span = rows // 2
    wide, qk = v_s.shape[2], q_s.shape[2]
    share = CHUNKS[0] + CHUNKS[1] + CHUNKS[2]
    half = rows // 2
    upper, lower = pl.ds(0, half), pl.ds(half, half)

    barrier = pltpu.get_barrier_semaphore()
    for i in range(1, 8):
        pl.semaphore_signal(
            barrier, inc=1, device_id={"seq": lax.rem(me + i, 8)}, device_id_type=MESH
        )
    for i in range(1, 4):
        pl.semaphore_signal(
            barrier, inc=1, device_id={"dp": lax.rem(z + i, 4)}, device_id_type=MESH
        )
    pl.semaphore_wait(barrier, 10)

    tokens = PlaneGather(x_ref, x_all, gsend.at[0], grecv.at[0])
    out_w = PlaneGather(wo_all.at[me], wo_all, gsend.at[1], grecv.at[1])
    cots = PlaneGather(c_ref, c_all, gsend.at[2], grecv.at[2])
    hidden_in = PlaneGather(held.at[0], h2_all, gsend.at[3], grecv.at[3])

    def line(item, source, block):
        return LineGather(item, source, block, zsend, zrecv, zlocal)

    def line_in_place(item, block):
        return LineGather(item, block(z), block, zsend, zrecv)

    depth = wq_ref.shape[0]

    def rows_of(ref, count, columns=None):
        def block(owner):
            if columns is None:
                return ref.at[pl.ds(owner * count, count)]
            return ref.at[pl.ds(owner * count, count), columns]

        return block

    z_gain = line(
        0, gain_ref, lambda owner: gains.at[:, pl.ds(pl.multiple_of(owner * depth, 128), depth)]
    )
    z_attn = line_in_place(1, rows_of(wa, depth))
    z_out = line(
        2,
        wo_ref.at[:, pl.ds(pl.multiple_of(me * wide, 128), wide)],
        lambda owner: wo_all.at[me, pl.ds(owner * depth, depth)],
    )
    z_up, z_down = [], []
    column, before = 0, 0
    columns, hiddens = [], []
    for k, count in enumerate(CHUNKS):
        part = pl.ds(column, 8 * count)
        z_up.append(line_in_place(3 + k, rows_of(wgu, depth, part)))
        z_down.append(
            line(
                6 + k,
                wd_ref.at[pl.ds(me * share + before, count)],
                lambda owner, base=4 * before, count=count: wd.at[
                    pl.ds(base + owner * count, count)
                ],
            )
        )
        columns.append(column)
        hiddens.append(4 * before)
        column += 8 * count
        before += count

    tokens.start()
    z_gain.start()

    window = 384
    tall = depth // 2

    def cut_window(i, source, start, size, r, slot, lane):
        return pltpu.make_async_copy(
            source.at[pl.ds(r * tall, tall), pl.ds(pl.multiple_of(start, 128), size)],
            got.at[slot, :, pl.ds(lane, size)],
            cut_sem.at[i],
        )

    per_tile = 128 // qk
    narrow = me // per_tile * 128
    shift = lax.rem(me, per_tile) * qk
    own_rows = pl.ds(pl.multiple_of(z * depth, depth), depth)
    v_cut = pltpu.make_async_copy(
        wv_ref.at[:, pl.ds(pl.multiple_of(me * wide, 128), wide)],
        wa.at[own_rows, pl.ds(0, wide)],
        cut_sem.at[20],
    )
    v_cut.start()
    qk_cuts = [
        cut_window(2 * r + i, source, narrow, 128, r, r, 128 * i)
        for r in range(2)
        for i, source in enumerate((wq_ref, wk_ref))
    ]
    for c in qk_cuts:
        c.start()
    ff_cuts = []
    ff_width = wg_ref.shape[1]
    for second, source in enumerate((wg_ref, wu_ref)):
        for group in range(4):
            start = group * (ff_width // 4) + me * share
            aligned = jnp.minimum(start // 128 * 128, ff_width - window)
            lane = 256 * (1 - second) + window * group
            for r in range(2):
                c = cut_window(
                    4 + len(ff_cuts), source, aligned, window, r, 2 * second + r, lane
                )
                c.start()
                ff_cuts.append((c, second, group, r, lane, start - aligned))
    for c in qk_cuts:
        c.wait()
    for r in range(2):
        lane = lax.broadcasted_iota(jnp.int32, (tall, 128), 1)
        q_rows = pltpu.roll(got[r, :, 0:128].astype(jnp.float32), lax.rem(128 - shift, 128), 1)
        k_rows = pltpu.roll(
            got[r, :, 128:256].astype(jnp.float32), lax.rem(128 + qk - shift, 128), 1
        )
        both = jnp.where(lane < qk, q_rows, jnp.where(lane < 2 * qk, k_rows, 0.0))
        there = pl.ds(pl.multiple_of(z * depth + r * tall, tall), tall)
        wa[there, wide : wide + 128] = both.astype(LOW)
    v_cut.wait()
    z_attn.start()
    for c, second, group, r, lane, shift_by in ff_cuts:
        c.wait()
        rolled = pltpu.roll(
            got[2 * second + r, :, lane : lane + window].astype(jnp.float32),
            lax.rem(window - shift_by, window),
            1,
        )
        there = pl.ds(pl.multiple_of(z * depth + r * tall, tall), tall)
        begin = 0
        for k, count in enumerate(CHUNKS):
            at = columns[k] + (4 * second + group) * count
            wgu[there, at : at + count] = rolled[:, begin : begin + count].astype(LOW)
            begin += count
    z_out.start()
    for g in (z_up[0], z_down[0]):
        g.start()

    def loads(order, step, sources):
        slot = lax.rem(step, 2)
        owner = order(step)
        return [
            pltpu.make_async_copy(source.at[owner], buf.at[slot], load_sem.at[i, slot])
            for i, (source, buf) in enumerate(sources)
        ]

    first_load = pltpu.make_async_copy(x_ref, x_buf.at[0], load_sem.at[0, 0])
    first_load.start()
    c_load = pltpu.make_async_copy(c_ref, c_buf.at[0], load_sem.at[1, 0])
    c_load.start()
    tokens.forward_first()
    z_gain.forward()
    z_attn.forward()
    tokens.forward_second()
    cots.start()
    c_load.wait()
    own_c = pltpu.make_async_copy(c_buf.at[0], c_all.at[me], self_sem.at[3])
    own_c.start()
    z_gain.wait()
    z_attn.wait()
    for g in (z_up[1], z_down[1]):
        g.start()

    def h1_copies(step):
        slot = lax.rem(step, 2)
        owner = nearest_first(step)
        return [
            pltpu.make_async_copy(
                o_buf.at[slot, pl.ds(m * span, span)],
                h1_out.at[m, pl.ds(owner * span, span)],
                h1_sem.at[m, slot],
            )
            for m in range(2)
        ]

    def arrive_tokens(step):
        @pl.when(step == 1)
        def _():
            tokens.from_sibling("own")

        @pl.when(step == 2)
        def _():
            tokens.from_sibling("x")

        @pl.when(step == 4)
        def _():
            tokens.forward_third()
            tokens.from_sibling("y")

        @pl.when(step == 6)
        def _():
            tokens.from_sibling("diag")

        @pl.when(step == 7)
        def _():
            z_out.forward()

    token_source = [(x_all, x_buf)]

    def project(step, carry):
        slot = lax.rem(step, 2)
        owner = nearest_first(step)
        for c in loads(nearest_first, step, token_source):
            c.wait()

        @pl.when(step >= 2)
        def _():
            for c in h1_copies(step - 2):
                c.wait()

        x = x_buf[slot].astype(jnp.float32)
        gain = gains[0:1, :].astype(jnp.float32)
        h_one = (x * norm_scale(x) * gain).astype(LOW)
        o_buf[slot] = h_one
        for c in h1_copies(step):
            c.start()
        arrive_tokens(step + 1)

        @pl.when(step < 7)
        def _():
            for c in loads(nearest_first, step + 1, token_source):
                c.start()

        projected = dot(h_one, wa[...]).astype(LOW)
        for m in range(2):
            there = pl.ds(owner * span, span)
            mine = projected[m * span : (m + 1) * span]
            v_s[m, there, :] = mine[:, :wide]
            q_s[m, there, :] = mine[:, wide : wide + qk]
            k_s[m, there, :] = mine[:, wide + qk : wide + 2 * qk]
        return carry

    lax.fori_loop(0, 8, project, 0)
    for step in (6, 7):
        for c in h1_copies(step):
            c.wait()
    z_out.wait()
    out_w.start()
    for g in (z_up[2], z_down[2]):
        g.start()

    finals = [
        pltpu.make_async_copy(source, target, done_sem.at[i])
        for i, (source, target) in enumerate(
            (
                (q_s, q_out),
                (k_s, k_out),
                (v_s, v_out),
                (wa, wa_out),
                (gains, gain_out),
                (att_s, att_out),
                (tok, tok_out),
                (mid, mid_out),
            )
        )
    ]
    for c in finals[:5]:
        c.start()

    length = v_s.shape[1]
    block = 256

    def attend_stream(m, carry):
        for i in range(length // block):
            rows_i = slice(i * block, (i + 1) * block)
            seen = (i + 1) * block
            first = first_of(lengths_ref, m, i * block, block)
            for head in range(wide // HEAD_V):
                lanes = slice(head * HEAD_V, (head + 1) * HEAD_V)
                unused, unused_mask, weight = weights_of(
                    q_s[m, rows_i, :], k_s[m, :seen, :], head, first, i * block
                )
                denom = jnp.sum(weight, axis=1, keepdims=True)
                numer = dot(weight.astype(LOW), v_s[m, :seen, lanes])
                att_s[m, rows_i, lanes] = (numer / denom).astype(LOW)
        return carry

    lax.fori_loop(0, 2, attend_stream, 0)
    out_w.forward_first()
    finals[5].start()

    to_mine = pl.ds(pl.multiple_of(me * wide, 128), wide)
    swaps = []
    for i in range(1, 8):
        other = lax.rem(me + i, 8)
        for m in range(2):
            swaps.append(
                remote(
                    esend,
                    erecv,
                    2 * (i - 1) + m,
                    att_s.at[m, pl.ds(other * span, span)],
                    tok.at[pl.ds(m * span, span), to_mine],
                    other,
                )
            )
            swaps[-1].start()
    kept = [
        pltpu.make_async_copy(
            att_s.at[m, pl.ds(me * span, span)],
            tok.at[pl.ds(m * span, span), to_mine],
            self_sem.at[m],
        )
        for m in range(2)
    ]
    for c in kept:
        c.start()
    x_load = pltpu.make_async_copy(x_ref, x_buf.at[0], load_sem.at[0, 0])
    x_load.start()

    def w_lanes(slot):
        return pl.ds(pl.multiple_of(slot * wide, 128), wide)

    def w_load(step):
        slot = lax.rem(step, 2)
        return pltpu.make_async_copy(
            wo_all.at[nearest_first(step)], act_s.at[:, w_lanes(slot)], w_sem.at[slot]
        )

    w_load(0).start()
    out_w.forward_second()
    cots.forward_first()
    cots.forward_second()
    z_up[0].forward()
    z_down[0].forward()
    for c in kept:
        c.wait()
    for c in swaps:
        c.wait_recv()
    finals[6].start()
    x_load.wait()

    def arrive_out(step):
        @pl.when(step == 1)
        def _():
            out_w.from_sibling("own")

        @pl.when(step == 2)
        def _():
            out_w.from_sibling("x")

        @pl.when(step == 4)
        def _():
            out_w.forward_third()
            out_w.from_sibling("y")

        @pl.when(step == 6)
        def _():
            out_w.from_sibling("diag")

    def project_out(step, carry):
        slot = lax.rem(step, 2)
        owner = nearest_first(step)
        w_load(step).wait()
        arrive_out(step + 1)

        @pl.when(step < 7)
        def _():
            w_load(step + 1).start()

        there = pl.ds(pl.multiple_of(owner * wide, 128), wide)
        mid[:, there] = dot(tok[...], act_s[:, w_lanes(slot)])
        return carry

    lax.fori_loop(0, 8, project_out, 0)
    mid_value = x_buf[0].astype(jnp.float32) + mid[...]
    mid[...] = mid_value
    held[0] = (mid_value * norm_scale(mid_value) * gains[1:2, :].astype(jnp.float32)).astype(LOW)
    hidden_in.start()
    own_h2 = pltpu.make_async_copy(held.at[0], h2_all.at[me], self_sem.at[2])
    own_h2.start()
    cots.forward_third()
    z_up[1].forward()
    z_down[1].forward()
    own_h2.wait()
    own_c.wait()
    z_up[0].wait()
    z_down[0].wait()

    largest = 4 * max(CHUNKS)
    sources = [(h2_all, x_buf), (c_all, c_buf)]

    def out_copy(order, step):
        slot = lax.rem(step, 2)
        return pltpu.make_async_copy(o_buf.at[slot], out_part.at[order(step)], out_sem.at[slot])

    def hidden_chunk(k, owner, h, c):
        count = 4 * CHUNKS[k]
        pair = pl.ds(columns[k], 2 * count)
        here = pl.ds(hiddens[k], count)
        both = dot(h, wgu[:, pair])
        gate, up = both[:, :count], both[:, count:]
        g_act = contract(c, wd[here, :], 1, 1)
        sigmoid = jax.nn.sigmoid(gate)
        silu = gate * sigmoid
        act = (silu * up).astype(LOW)
        g_gate = (g_act * up * sigmoid * (1.0 + gate * (1.0 - sigmoid))).astype(LOW)
        g_up = (g_act * silu).astype(LOW)
        there = pl.ds(owner * rows, rows)
        act_s[there, here] = act
        g_both = jnp.concatenate([g_gate, g_up], axis=1)
        ggu_s[there, pair] = g_both
        return act, g_both

    def add_grads(k, step, h, c, act, g_both):
        count = 4 * CHUNKS[k]

        to, low = (2 * largest, largest) if k == 1 else (0, 0)

        @pl.when(step == 0)
        def _():
            sum_gu[:, to : to + 2 * count] = jnp.zeros((width, 2 * count), jnp.float32)
            sum_d[low : low + count, :] = jnp.zeros((count, width), jnp.float32)

        sum_gu[:, to : to + 2 * count] += contract(h, g_both, 0, 0)
        sum_d[low : low + count, :] += contract(act, c, 0, 0)

    def emit(k):
        count = 4 * CHUNKS[k]
        rest = share - CHUNKS[0]
        to, low = (2 * largest, largest) if k == 1 else (0, 0)

        def gu_copies(i, slot):
            there = pl.ds(i * rows, rows)
            if k == 0:
                return [
                    pltpu.make_async_copy(
                        o_buf.at[slot, :, pl.ds(second * count, count)],
                        dgu_first.at[second, there],
                        h1_sem.at[second, slot],
                    )
                    for second in range(2)
                ]
            return [
                pltpu.make_async_copy(
                    o_buf.at[slot, :, pl.ds(0, 2 * count)],
                    dgu_out.at[there, pl.ds(columns[k] - columns[1], 2 * count)],
                    out_sem.at[slot],
                )
            ]

        def d_target(owner):
            if k == 0:
                return dd_first.at[pl.ds(owner * CHUNKS[0], CHUNKS[0])]
            start = owner * rest + (hiddens[k] - hiddens[1]) // 4
            return dd_out.at[pl.ds(start, CHUNKS[k])]

        pending = [[], []]
        for i in range(width // rows):
            slot = i % 2
            for c in pending[slot]:
                c.wait()
            total = sum_gu[i * rows : (i + 1) * rows, to : to + 2 * count]
            o_buf[slot, :, : 2 * count] = total.astype(LOW)
            pending[slot] = gu_copies(i, slot)
            for c in pending[slot]:
                c.start()
        for c in (*pending[0], *pending[1]):
            c.wait()
        o_buf[0, :count, :] = sum_d[low : low + count, :].astype(LOW)
        downs = []
        for owner in range(4):
            downs.append(
                pltpu.make_async_copy(
                    o_buf.at[0, pl.ds(owner * CHUNKS[k], CHUNKS[k])],
                    d_target(owner),
                    h1_sem.at[owner // 2, owner % 2],
                )
            )
            downs[-1].start()
        for c in downs:
            c.wait()

    def forward_pass(chunks, last, arrive, step, carry):
        slot = lax.rem(step, 2)
        for c in loads(nearest_first, step, sources):
            c.wait()
        h, c = x_buf[slot], c_buf[slot]
        made = [hidden_chunk(k, nearest_first(step), h, c) for k in chunks]
        if arrive is not None:
            arrive(step + 1)

        @pl.when(step < last)
        def _():
            for c in loads(nearest_first, step + 1, sources):
                c.start()

        for k, (act, g_both) in zip(chunks, made):
            add_grads(k, step, h, c, act, g_both)
        return carry

    def arrive_both(step):
        hidden_in.arrive(step)

        @pl.when(step == 1)
        def _():
            cots.from_sibling("own")

        @pl.when(step == 2)
        def _():
            cots.from_sibling("x")

        @pl.when(step == 4)
        def _():
            cots.from_sibling("y")

        @pl.when(step == 6)
        def _():
            cots.from_sibling("diag")

    for c in loads(nearest_first, 0, sources):
        c.start()

    def arrive_near(step):
        @pl.when(step < 4)
        def _():
            arrive_both(step)

    lax.fori_loop(0, 4, functools.partial(forward_pass, (0,), 3, arrive_near), 0)
    for c in loads(nearest_first, 0, sources):
        c.start()
    z_up[1].wait()
    z_down[1].wait()
    lax.fori_loop(0, 4, functools.partial(forward_pass, (1,), 3, None), 0)
    z_up[2].forward()
    z_down[2].forward()
    arrive_both(jnp.int32(4))
    for c in loads(nearest_first, 4, sources):
        c.start()
    lax.fori_loop(4, 8, functools.partial(forward_pass, (0, 1), 7, arrive_both), 0)
    hidden_in.sent()
    finals[7].start()
    for c in loads(farthest_first, 0, sources):
        c.start()
    emit(0)
    sum_lines = [
        LineScatter(
            lambda owner: dgu_first.at[:, pl.ds(owner * depth, depth), :],
            dgu_all,
            gu_stop,
            att_s.at[:, pl.ds(0, depth), :],
            fsend.at[0],
            frecv.at[0],
            f_sem.at[0],
        ),
        LineScatter(
            lambda owner: dd_first.at[pl.ds(owner * CHUNKS[0], CHUNKS[0])],
            dd_all,
            d_stop,
            tok.at[pl.ds(0, CHUNKS[0])],
            fsend.at[1],
            frecv.at[1],
            f_sem.at[1],
        ),
    ]
    for c in swaps:
        c.wait_send()
    finals[5].wait()
    finals[6].wait()
    for g in sum_lines:
        g.start_first()

    z_up[2].wait()
    z_down[2].wait()

    copy = functools.partial(remote, rsend, rrecv)
    b_diag = copy(0, beside.at[0], got.at[2], sib)
    b_x = copy(1, beside.at[1], got.at[1], sib)
    b_y = copy(2, beside.at[0], got.at[3], sib)
    b_own = copy(3, beside.at[1], got.at[0], sib)
    x0 = copy(4, held.at[2, upper], one.at[0], xn)
    y0 = copy(5, held.at[2, lower], one.at[1], yn)
    x1 = copy(6, held.at[1, upper], one.at[2], xn)
    y1 = copy(7, held.at[3, lower], one.at[3], yn)
    y2 = copy(8, held.at[3, upper], two.at[0], yn)
    x2 = copy(9, held.at[1, lower], two.at[1], xn)

    def last_pass(step, carry):
        slot = lax.rem(step, 2)
        owner = farthest_first(step)
        there = pl.ds(owner * rows, rows)
        for c in loads(farthest_first, step, sources):
            c.wait()
        hidden_chunk(2, owner, x_buf[slot], c_buf[slot])

        @pl.when(step < 7)
        def _():
            for c in loads(farthest_first, step + 1, sources):
                c.start()

        part = contract(ggu_s[there, :], wgu[...], 1, 1).astype(LOW)

        @pl.when(step == 2)
        def _():
            for g in sum_lines:
                g.start()

        @pl.when(step == 6)
        def _():
            for g in sum_lines:
                g.join()

        for k, place, sent in ((0, 0, b_diag), (2, 1, b_x), (4, 0, b_y), (6, 1, b_own)):

            @pl.when(step == k)
            def _(k=k, place=place, sent=sent):
                if k == 4:
                    b_diag.wait_send()
                if k == 6:
                    b_x.wait_send()
                beside[place] = part
                sent.start()

        for k, place, arrived in ((1, 2, b_diag), (3, 1, b_x), (5, 3, b_y), (7, 0, b_own)):

            @pl.when(step == k)
            def _(k=k, place=place, arrived=arrived):
                arrived.wait_recv()
                held[place] = part + got[place]
                if k == 1:
                    x0.start()
                    y0.start()
                if k == 3:
                    x1.start()
                if k == 5:
                    y1.start()
                    y0.wait_recv()
                    held[1, half:] = held[1, half:] + one[1]
                    x2.start()
                    x0.wait_recv()
                    held[3, :half] = held[3, :half] + one[0]
                    y2.start()
        return carry

    lax.fori_loop(0, 8, last_pass, 0)
    for c in loads(farthest_first, 0, sources):
        c.start()

    def close_pass(step, carry):
        slot = lax.rem(step, 2)
        there = pl.ds(farthest_first(step) * rows, rows)
        for c in loads(farthest_first, step, sources):
            c.wait()

        @pl.when(step < 7)
        def _():
            for c in loads(farthest_first, step + 1, sources):
                c.start()

        @pl.when(step >= 2)
        def _():
            out_copy(farthest_first, step - 2).wait()

        o_buf[slot] = dot(act_s[there, :], wd[...]).astype(LOW)
        out_copy(farthest_first, step).start()
        act = act_s[there, pl.ds(hiddens[2], 4 * CHUNKS[2])]
        g_both = ggu_s[there, pl.ds(columns[2], 8 * CHUNKS[2])]
        add_grads(2, step, x_buf[slot], c_buf[slot], act, g_both)
        return carry

    lax.fori_loop(0, 8, close_pass, 0)
    out_copy(farthest_first, 6).wait()
    out_copy(farthest_first, 7).wait()
    emit(1)
    emit(2)
    f32 = jnp.float32
    x1.wait_recv()
    y2.wait_recv()
    for c in (*finals[:5], finals[7]):
        c.wait()
    mid[:half] = held[0, :half].astype(f32) + one[2].astype(f32) + two[0].astype(f32)
    y1.wait_recv()
    x2.wait_recv()
    mid[half:] = held[0, half:].astype(f32) + one[3].astype(f32) + two[1].astype(f32)
    gh_copy = pltpu.make_async_copy(mid, gh_out, done_sem.at[7])
    gh_copy.start()
    for g in sum_lines:
        g.wait()
    gh_copy.wait()
    for c in (b_y, b_own, x0, y0, x1, y1, y2, x2):
        c.wait_send()
    for g in (tokens, out_w, cots, z_gain, z_attn, z_out, *z_up, *z_down):
        g.sent()


def layer_front(tokens, cot, weights, gain_rows, lengths, length, wide, qk):
    rows, width = tokens.shape
    streams = lengths.shape[0]
    hidden = 4 * sum(CHUNKS)
    largest = 4 * max(CHUNKS)
    shape = jax.ShapeDtypeStruct
    f32 = jnp.float32
    anywhere = pl.BlockSpec(memory_space=pl.ANY)
    plane = shape((8, rows, width), LOW)
    narrow = shape((streams, length, qk), LOW)
    broad = shape((streams, length, wide), LOW)
    attn_shape = (width, wide + 128)
    out_shape = [
        plane,
        plane,
        plane,
        shape((8, width, width // 8), LOW),
        shape((streams, length, width), LOW),
        narrow,
        narrow,
        broad,
        broad,
        shape((rows, width), LOW),
        shape((rows, width), f32),
        shape(attn_shape, LOW),
        shape((gain_rows.shape[0], width), LOW),
        plane,
        shape((rows, width), f32),
        shape((2, width, 4 * CHUNKS[0]), LOW),
        shape((4 * CHUNKS[0], width), LOW),
        shape((width, 2 * hidden - 8 * CHUNKS[0]), LOW),
        shape((hidden - 4 * CHUNKS[0], width), LOW),
        shape((4, 2, width // 4, 4 * CHUNKS[0]), LOW),
        shape((4, CHUNKS[0], width), LOW),
    ]
    dma = pltpu.SemaphoreType.DMA
    vmem = pltpu.VMEM
    return pl.pallas_call(
        layer_kernel,
        out_shape=out_shape,
        in_specs=[anywhere] * 10 + [pl.BlockSpec(memory_space=pltpu.SMEM)],
        out_specs=[anywhere] * 21,
        scratch_shapes=[
            vmem(attn_shape, LOW),
            vmem((width, 2 * hidden), LOW),
            vmem((hidden, width), LOW),
            vmem((gain_rows.shape[0], width), LOW),
            vmem(narrow.shape, LOW),
            vmem(narrow.shape, LOW),
            vmem(broad.shape, LOW),
            vmem(broad.shape, LOW),
            vmem((rows, width), LOW),
            vmem((rows, width), f32),
            vmem((8 * rows, hidden), LOW),
            vmem((8 * rows, 2 * hidden), LOW),
            vmem((width, 4 * largest), f32),
            vmem((2 * largest, width), f32),
            vmem((2, rows, width), LOW),
            vmem((2, rows, width), LOW),
            vmem((2, rows, width), LOW),
            vmem((2, rows, width), LOW),
            vmem((4, rows, width), LOW),
            vmem((4, rows, width), LOW),
            vmem((4, rows // 2, width), LOW),
            vmem((2, rows // 2, width), LOW),
            dma((4, 13)),
            dma((4, 13)),
            dma((9, 5)),
            dma((9, 4)),
            dma((9,)),
            dma((14,)),
            dma((14,)),
            dma((10,)),
            dma((10,)),
            dma((2, 2)),
            dma((2,)),
            dma((2, 2)),
            dma((2,)),
            dma((8,)),
            dma((4,)),
            dma((2, 5)),
            dma((2, 5)),
            dma((2, 2)),
            dma((21,)),
            vmem((2, width // 4, 4 * CHUNKS[0]), LOW),
            vmem((CHUNKS[0], width), LOW),
        ],
        compiler_params=pltpu.CompilerParams(
            collective_id=21, has_side_effects=True, vmem_limit_bytes=63 * MIB
        ),
        cost_estimate=pl.CostEstimate(
            flops=6 * 3 * 8 * rows * width * hidden,
            bytes_accessed=400 * rows * width,
            transcendentals=0,
        ),
        name="layer",
    )(tokens, cot, *weights, gain_rows, lengths)


class LineScatter:
    def __init__(self, block, target, stop, mine, send, recv, local):
        z = lax.axis_index("dp")
        self.z, self.stop, self.mine = z, stop, mine
        self.inner = (z == 1) | (z == 2)
        self.outer = jnp.logical_not(self.inner)

        def copy(k, src, dst, at, to):
            return pltpu.make_async_remote_copy(
                src_ref=src,
                dst_ref=dst,
                send_sem=send.at[k],
                recv_sem=recv.at[at],
                device_id={"dp": to},
                device_id_type=MESH,
            )

        far = jnp.where(z < 2, 3, 0)
        near = jnp.where(z < 2, 1, 2)
        self.first = copy(0, block(far), stop, 4, jnp.where(self.inner, 3 - near, near))
        self.sends = []
        for k, d in enumerate((1, -1)):
            to = z + d
            valid = (to >= 0) & (to < 4)
            there = jnp.clip(to, 0, 3)
            self.sends.append((valid, copy(1 + k, block(there), target.at[z], z, there)))
        other = 3 - near
        self.sends.append((self.outer, copy(3, block(other), target.at[z], z, other)))
        self.own_far = pltpu.make_async_copy(block(far), mine, local.at[0])
        self.joined = copy(4, mine, target.at[z], z, far)
        self.own = pltpu.make_async_copy(block(z), target.at[z], local.at[1])
        self.arrivals = []
        for d in (1, -1, 2, -2):
            owner = z + d
            valid = (owner >= 0) & (owner < 4)
            there = jnp.clip(owner, 0, 3)
            self.arrivals.append((valid, copy(1, block(there), target.at[there], there, there)))

    def start_first(self):
        self.own.start()

        @pl.when(self.outer)
        def _():
            self.first.start()

        @pl.when(self.inner)
        def _():
            self.own_far.start()

    def start(self):
        for valid, c in self.sends:

            @pl.when(valid)
            def _(c=c):
                c.start()

    def join(self):
        @pl.when(self.inner)
        def _():
            self.first.wait_recv()
            self.own_far.wait()
            self.mine[...] = self.mine[...] + self.stop[...]
            self.joined.start()

    def wait(self):
        for valid, c in self.arrivals:

            @pl.when(valid)
            def _(c=c):
                c.wait_recv()

        self.own.wait()
        for valid, c in (*self.sends, (self.outer, self.first), (self.inner, self.joined)):

            @pl.when(valid)
            def _(c=c):
                c.wait_send()


class PlaneScatter:
    def __init__(self, beside, held, got, one, two, send, recv):
        me, sib, xn, yn = partners()
        half = got.shape[1] // 2
        self.half = half
        upper, lower = pl.ds(0, half), pl.ds(half, half)
        copy = functools.partial(remote, send, recv)
        self.held, self.got, self.one, self.two = held, got, one, two
        self.pairs = [copy(i, beside(i), got.at[i], sib) for i in range(4)]
        self.x0 = copy(4, held(2).at[upper], one.at[0], xn)
        self.y0 = copy(5, held(2).at[lower], one.at[1], yn)
        self.x1 = copy(6, held(1).at[upper], one.at[2], xn)
        self.y1 = copy(7, held(3).at[lower], one.at[3], yn)
        self.y2 = copy(8, held(3).at[upper], two.at[0], yn)
        self.x2 = copy(9, held(1).at[lower], two.at[1], xn)

    def start_pair(self, i):
        self.pairs[i].start()

    def start_pairs(self):
        for i in (2, 1, 3, 0):
            self.start_pair(i)

    def add_pair(self, i):
        self.pairs[i].wait_recv()
        block = self.held(i)
        block[...] = block[...] + self.got[i]
        for c in {0: (), 1: (self.x1,), 2: (self.x0, self.y0), 3: (self.y1,)}[i]:
            c.start()

    def add_pairs(self):
        for i in (2, 1, 3, 0):
            self.add_pair(i)

    def second(self):
        half = self.half
        self.y0.wait_recv()
        block = self.held(1)
        block[half:, :] = block[half:, :] + self.one[1]
        self.x2.start()
        self.x0.wait_recv()
        block = self.held(3)
        block[:half, :] = block[:half, :] + self.one[0]
        self.y2.start()

    def upper_sum(self):
        f32 = jnp.float32
        self.x1.wait_recv()
        self.y2.wait_recv()
        own = self.held(0)[: self.half, :].astype(f32)
        return own + self.one[2].astype(f32) + self.two[0].astype(f32)

    def lower_sum(self):
        f32 = jnp.float32
        self.y1.wait_recv()
        self.x2.wait_recv()
        own = self.held(0)[self.half :, :].astype(f32)
        return own + self.one[3].astype(f32) + self.two[1].astype(f32)

    def sent(self):
        for c in (*self.pairs, self.x0, self.y0, self.x1, self.y1, self.y2, self.x2):
            c.wait_send()


def chips():
    me, unused, xn, yn = partners()
    return me, xn, xn + yn - me, yn


def turn_kernel(
    gh_ref,
    mid_ref,
    c_ref,
    gain_ref,
    wo_all,
    part_ref,
    tok_ref,
    q_ref,
    k_ref,
    v_ref,
    att_ref,
    lengths_ref,
    h1_ref,
    output_ref,
    g_mid_out,
    g_out,
    gain_out,
    attn_ref,
    g_mid,
    work,
    g_low,
    g_att,
    g_heads,
    g_s,
    w_buf,
    go_part,
    held_o,
    got_g,
    one_g,
    two_g,
    got_o,
    one_o,
    two_o,
    gk_sum,
    gv_sum,
    h_buf,
    sums,
    esend,
    erecv,
    ssend,
    srecv,
    load_sem,
    w_sem,
    self_sem,
    done_sem,
    h_sem,
):
    me, sib, xn, yn = partners()
    flip = sib - me
    rows, width = g_low.shape
    span = rows // 2
    wide, qk = v_ref.shape[2], q_ref.shape[2]
    half = rows // 2
    greet([lax.rem(me + i, 8) for i in range(1, 8)])
    owners = chips()

    loads = [
        pltpu.make_async_copy(source, target, load_sem.at[i])
        for i, (source, target) in enumerate(
            ((gh_ref, g_mid), (mid_ref, work), (c_ref, g_low))
        )
    ]
    held_loads = [
        pltpu.make_async_copy(part_ref.at[owners[i]], held_o.at[i], load_sem.at[3 + i])
        for i in range(4)
    ]

    def w_load(step):
        slot = lax.rem(step, 2)
        return pltpu.make_async_copy(wo_all.at[step], w_buf.at[slot], w_sem.at[slot])

    for c in loads:
        c.start()
    w_load(0).start()
    outs = PlaneScatter(
        lambda i: part_ref.at[owners[i] + flip],
        lambda i: held_o.at[i],
        got_o,
        one_o,
        two_o,
        ssend.at[0],
        srecv.at[0],
    )
    weights = PlaneScatter(
        lambda i: go_part.at[owners[i] + flip],
        lambda i: go_part.at[owners[i]],
        got_g,
        one_g,
        two_g,
        ssend.at[1],
        srecv.at[1],
    )
    outs.start_pairs()
    for c in held_loads:
        c.start()
    for c in loads:
        c.wait()

    f32 = jnp.float32
    mid = work[...]
    inverse = norm_scale(mid)
    normed = mid * inverse
    grad = g_mid[...]
    gain_out[...] = jnp.broadcast_to(
        jnp.sum(grad * normed, axis=0, keepdims=True), gain_out.shape
    )
    gain = gain_ref[1:2, :].astype(f32)
    grad_mid = g_low[...].astype(f32) + norm_backward(grad, normed, inverse, gain)
    g_mid[...] = grad_mid
    g_low[...] = grad_mid.astype(LOW)
    done = [pltpu.make_async_copy(g_mid, g_mid_out, done_sem.at[0])]
    done[0].start()

    def back_out(step, carry):
        slot = lax.rem(step, 2)
        w_load(step).wait()

        @pl.when(step < 7)
        def _():
            w_load(step + 1).start()

        there = pl.ds(pl.multiple_of(step * wide, 128), wide)
        term = contract(g_low[:, there], w_buf[slot], 1, 1)

        @pl.when(step == 0)
        def _():
            work[...] = term

        @pl.when(step > 0)
        def _():
            work[...] += term

        return carry

    lax.fori_loop(0, 8, back_out, 0)
    g_att[...] = work[...].astype(LOW)
    mid_load = pltpu.make_async_copy(mid_ref, work, load_sem.at[1])
    mid_load.start()
    swaps = []
    here = pl.ds(me * span, span)
    for i in range(1, 8):
        other = lax.rem(me + i, 8)
        lanes = pl.ds(pl.multiple_of(other * wide, 128), wide)
        for m in range(2):
            swaps.append(
                remote(
                    esend,
                    erecv,
                    2 * (i - 1) + m,
                    g_att.at[pl.ds(m * span, span), lanes],
                    g_heads.at[m, here],
                    other,
                )
            )
            swaps[-1].start()
    kept = [
        pltpu.make_async_copy(
            g_att.at[pl.ds(m * span, span), pl.ds(pl.multiple_of(me * wide, 128), wide)],
            g_heads.at[m, here],
            self_sem.at[m],
        )
        for m in range(2)
    ]
    for c in kept:
        c.start()

    own = width // 32
    for z in range(4):
        lanes = slice(z * 8 * own, (z + 1) * 8 * own)
        block = contract(tok_ref[:, lanes], g_low[...], 0, 0).astype(LOW)
        for s in range(8):
            go_part[s, z * own : (z + 1) * own, :] = block[s * own : (s + 1) * own]
    weights.start_pairs()
    for c in kept:
        c.wait()
    for c in swaps:
        c.wait_recv()
    weights.add_pairs()

    length = v_ref.shape[1]
    block = 256
    streams = v_ref.shape[0]
    pieces = length // rows

    def h_load(step):
        slot = lax.rem(step, 2)
        return pltpu.make_async_copy(
            h1_ref.at[step // pieces, pl.ds(lax.rem(step, pieces) * rows, rows)],
            h_buf.at[slot],
            h_sem.at[slot],
        )

    h_load(0).start()

    def back_stream(m, carry):
        gk_sum[...] = jnp.zeros_like(gk_sum)
        gv_sum[...] = jnp.zeros_like(gv_sum)
        for i in range(length // block):
            rows_i = slice(i * block, (i + 1) * block)
            seen = (i + 1) * block
            query, key = q_ref[m, rows_i, :], k_ref[m, :seen, :]
            g_query = jnp.zeros(query.shape, f32)
            first = first_of(lengths_ref, m, i * block, block)
            for head in range(wide // HEAD_V):
                lanes = slice(head * HEAD_V, (head + 1) * HEAD_V)
                scores, mask, weight = weights_of(query, key, head, first, i * block)
                denom = jnp.sum(weight, axis=1, keepdims=True)
                a = (g_heads[m, rows_i, lanes].astype(f32) / denom).astype(LOW)
                b = -jnp.sum(
                    a.astype(f32) * att_ref[m, rows_i, lanes].astype(f32), axis=1, keepdims=True
                )
                g_weight = contract(a, v_ref[m, :seen, lanes], 1, 1) + b
                slope = 1.0 / math.sqrt(QK_DIM) + scores * (1.0 / QK_DIM)
                g_scores = jnp.where(mask, g_weight * slope, 0.0).astype(LOW)
                g_query += head_lanes(dot(g_scores, key), head)
                gk_sum[:seen, :] += contract(g_scores, head_lanes(query, head), 0, 0)
                gv_sum[:seen, lanes] += contract(weight.astype(LOW), a, 0, 0)
            g_s[m, rows_i, wide : wide + qk] = g_query.astype(LOW)
        g_s[m, :, :wide] = gv_sum[...].astype(LOW)
        g_s[m, :, wide + qk : wide + 2 * qk] = gk_sum[...].astype(LOW)
        g_s[m, :, wide + 2 * qk :] = jnp.zeros((length, g_s.shape[2] - wide - 2 * qk), LOW)

        @pl.when(m == 0)
        def _():
            for c in held_loads:
                c.wait()
            outs.add_pairs()

        return carry

    lax.fori_loop(0, 2, back_stream, 0)
    weights.second()
    done.append(pltpu.make_async_copy(g_s, g_out, done_sem.at[1]))
    done[1].start()
    outs.second()

    def add_grads(step, carry):
        slot = lax.rem(step, 2)
        h_load(step).wait()

        @pl.when(step < streams * pieces - 1)
        def _():
            h_load(step + 1).start()

        there = pl.ds(pl.multiple_of(lax.rem(step, pieces) * rows, rows), rows)
        term = contract(h_buf[slot], g_s[step // pieces, there, :], 0, 0)

        @pl.when(step == 0)
        def _():
            sums[...] = term

        @pl.when(step > 0)
        def _():
            sums[...] += term

        return carry

    lax.fori_loop(0, streams * pieces, add_grads, 0)
    narrow = sums.shape[1]
    attn_ref[:, :narrow] = sums[...].astype(LOW)
    mid_load.wait()
    for part, total in enumerate((weights.upper_sum(), weights.lower_sum())):
        total = total.astype(LOW)
        for z in range(2):
            for i in range(8):
                start = ((2 * part + z) * 8 + i) * own
                attn_ref[start : start + own, narrow:] = total[
                    z * own : (z + 1) * own, i * wide : (i + 1) * wide
                ]
    output_ref[:half] = (work[:half] + outs.upper_sum()).astype(LOW)
    output_ref[half:] = (work[half:] + outs.lower_sum()).astype(LOW)
    for c in done:
        c.wait()
    for c in swaps:
        c.wait_send()
    weights.sent()
    outs.sent()


def layer_turn(gh, mid, cot, gains, wo_all, part, tok, query, key, value, att, lengths, h1, columns):
    rows, width = mid.shape
    streams, length, wide = value.shape
    qk = query.shape[2]
    shape = jax.ShapeDtypeStruct
    f32 = jnp.float32
    anywhere = pl.BlockSpec(memory_space=pl.ANY)
    in_vmem = pl.BlockSpec(memory_space=pltpu.VMEM)
    dma = pltpu.SemaphoreType.DMA
    vmem = pltpu.VMEM
    arriving = [
        vmem((4, rows, width), LOW),
        vmem((4, rows // 2, width), LOW),
        vmem((2, rows // 2, width), LOW),
    ]
    return pl.pallas_call(
        turn_kernel,
        out_shape=[
            shape((rows, width), LOW),
            shape((rows, width), f32),
            shape((streams, length, columns), LOW),
            shape((8, width), f32),
            shape((width, columns + wide), LOW),
        ],
        in_specs=[anywhere] * 3
        + [in_vmem]
        + [anywhere] * 2
        + [in_vmem] * 5
        + [pl.BlockSpec(memory_space=pltpu.SMEM), anywhere],
        out_specs=[in_vmem, anywhere, anywhere, in_vmem, in_vmem],
        scratch_shapes=[
            vmem((rows, width), f32),
            vmem((rows, width), f32),
            vmem((rows, width), LOW),
            vmem((rows, width), LOW),
            vmem((streams, length, wide), LOW),
            vmem((streams, length, columns), LOW),
            vmem((2, width, wide), LOW),
            vmem((8, rows, width), LOW),
            vmem((4, rows, width), LOW),
            *arriving,
            *arriving,
            vmem((length, qk), f32),
            vmem((length, wide), f32),
            vmem((2, rows, width), LOW),
            vmem((width, columns), f32),
            dma((14,)),
            dma((14,)),
            dma((2, 10)),
            dma((2, 10)),
            dma((7,)),
            dma((2,)),
            dma((2,)),
            dma((2,)),
            dma((2,)),
        ],
        compiler_params=pltpu.CompilerParams(
            collective_id=22, has_side_effects=True, vmem_limit_bytes=63 * MIB
        ),
        cost_estimate=moved(16 * rows * width),
        name="turn",
    )(gh, mid, cot, gains, wo_all, part, tok, query, key, value, att, lengths, h1)


def close_kernel(
    g_ref,
    wa_ref,
    g_mid_ref,
    x_ref,
    gain_ref,
    sum_ref,
    blocks_ref,
    rest_ref,
    grad_ref,
    gains_ref,
    first_got,
    rest_got,
    beside,
    held,
    got,
    one,
    two,
    gain_rows,
    gain_line,
    gain_columns,
    gain_plane,
    blocks,
    first_sum,
    ssend,
    srecv,
    zsend,
    zrecv,
    esend,
    erecv,
    self_sem,
    fsend,
    frecv,
    f_sem,
):
    me, sib, xn, yn = partners()
    z = lax.axis_index("dp")
    rows, width = x_ref.shape
    span = rows // 2
    half = rows // 2
    f32 = jnp.float32
    barrier = pltpu.get_barrier_semaphore()
    for i in range(1, 8):
        pl.semaphore_signal(
            barrier, inc=1, device_id={"seq": lax.rem(me + i, 8)}, device_id_type=MESH
        )
    for i in range(1, 4):
        pl.semaphore_signal(
            barrier, inc=1, device_id={"dp": lax.rem(z + i, 4)}, device_id_type=MESH
        )
    pl.semaphore_wait(barrier, 10)
    load = pltpu.make_async_copy(blocks_ref, blocks, f_sem.at[0])
    load.start()
    keep = first_got.shape[1]

    def exchange(item, source, target):
        mine = pltpu.make_async_copy(
            source.at[pl.ds(me * keep, keep)], target.at[me], f_sem.at[1 + item]
        )
        mine.start()
        copies = []
        for i in range(1, 8):
            other = lax.rem(me + i, 8)
            copies.append(
                remote(
                    fsend,
                    frecv,
                    7 * item + i - 1,
                    source.at[pl.ds(other * keep, keep)],
                    target.at[me],
                    other,
                )
            )
            copies[-1].start()
        return mine, copies

    moves = [exchange(1, rest_ref, rest_got)]
    scatter = PlaneScatter(
        lambda i: beside.at[i], lambda i: held.at[i], got, one, two, ssend, srecv
    )
    def part_of(owner):
        there = pl.ds(pl.multiple_of(owner * span, span), span)
        grads = jnp.concatenate([g_ref[0, there, :], g_ref[1, there, :]], axis=0)
        return contract(grads, wa_ref[...], 1, 1).astype(LOW)

    owners = chips()
    for i in (2, 1, 3, 0):
        beside[i] = part_of(owners[i] + sib - me)
        scatter.start_pair(i)
        held[i] = part_of(owners[i])
        scatter.add_pair(i)

    load.wait()
    for second in range(2):
        total = jnp.zeros(blocks.shape[2:], f32)
        for owner in range(4):
            came = jnp.abs(z - owner) < 3
            total = total + jnp.where(came, blocks[owner, second].astype(f32), 0.0)
        lanes_here = total.shape[1]
        first_sum[:, second * lanes_here : (second + 1) * lanes_here] = total.astype(LOW)
    moves.append(exchange(0, first_sum, first_got))

    scatter.second()

    x = x_ref[...].astype(f32)
    inverse = norm_scale(x)
    normed = x * inverse
    gain = gain_ref[0:1, :].astype(f32)

    def finish(start, g_h):
        part = slice(start, start + half)
        grad_ref[part] = g_mid_ref[part] + norm_backward(g_h, normed[part], inverse[part], gain)
        return jnp.sum(g_h * normed[part], axis=0, keepdims=True)

    gain_sum = finish(0, scatter.upper_sum()) + finish(half, scatter.lower_sum())

    both = jnp.concatenate([gain_sum, sum_ref[0:1, :], jnp.zeros((14, width), f32)], axis=0)
    gain_rows[...] = both.astype(LOW)
    depth = width // 4

    def lanes(owner):
        return pl.ds(pl.multiple_of(owner * depth, 128), depth)

    def over_line(k, to, owner):
        return pltpu.make_async_remote_copy(
            src_ref=gain_rows.at[:, lanes(to)],
            dst_ref=gain_line.at[owner],
            send_sem=zsend.at[k],
            recv_sem=zrecv.at[owner],
            device_id={"dp": to},
            device_id_type=MESH,
        )

    others = [lax.rem(z + o, 4) for o in (1, 2, 3)]
    sends = [over_line(k, other, z) for k, other in enumerate(others)]
    own = pltpu.make_async_copy(gain_rows.at[:, lanes(z)], gain_line.at[z], self_sem.at[0])
    own.start()
    for c in sends:
        c.start()
    own.wait()
    for other in others:
        over_line(0, other, other).wait_recv()
    total = gain_line[0].astype(f32)
    for k in range(1, 4):
        total = total + gain_line[k].astype(f32)
    entry = lax.broadcasted_iota(jnp.int32, (16, 128), 0)
    lane = lax.broadcasted_iota(jnp.int32, (16, 128), 1)
    pick = jnp.where(lane == entry, 1.0, 0.0).astype(LOW)
    gain_columns[...] = contract(total.astype(LOW), pick, 0, 0).astype(LOW)
    count = depth // 8
    own = pltpu.make_async_copy(
        gain_columns.at[pl.ds(me * count, count)], gain_plane.at[me], self_sem.at[1]
    )
    own.start()
    swaps = []
    for i in range(1, 8):
        other = lax.rem(me + i, 8)
        swaps.append(
            remote(
                esend,
                erecv,
                i - 1,
                gain_columns.at[pl.ds(other * count, count)],
                gain_plane.at[me],
                other,
            )
        )
        swaps[-1].start()
    own.wait()
    for c in swaps:
        c.wait_recv()
    total = gain_plane[0].astype(f32)
    for k in range(1, 8):
        total = total + gain_plane[k].astype(f32)
    gains_ref[...] = total
    scatter.sent()
    for c in (*sends, *swaps):
        c.wait_send()
    for mine, copies in moves:
        mine.wait()
        for c in copies:
            c.wait()


def layer_close(g_all, wa, g_mid, tokens, gains, gain_sum, blocks, rest):
    rows, width = tokens.shape
    shape = jax.ShapeDtypeStruct
    in_vmem = pl.BlockSpec(memory_space=pltpu.VMEM)
    anywhere = pl.BlockSpec(memory_space=pl.ANY)
    dma = pltpu.SemaphoreType.DMA
    vmem = pltpu.VMEM
    return pl.pallas_call(
        close_kernel,
        out_shape=[
            shape((rows, width), jnp.float32),
            shape((width // 32, 128), jnp.float32),
            shape((8, width // 32, 8 * CHUNKS[0]), LOW),
            shape((8, width // 32, rest.shape[1]), LOW),
        ],
        in_specs=[in_vmem] * 6 + [anywhere] * 2,
        out_specs=[in_vmem, in_vmem, anywhere, anywhere],
        scratch_shapes=[
            vmem((4, rows, width), LOW),
            vmem((4, rows, width), LOW),
            vmem((4, rows, width), LOW),
            vmem((4, rows // 2, width), LOW),
            vmem((2, rows // 2, width), LOW),
            vmem((16, width), LOW),
            vmem((4, 16, width // 4), LOW),
            vmem((width // 4, 128), LOW),
            vmem((8, width // 32, 128), LOW),
            vmem(blocks.shape, LOW),
            vmem((width // 4, 8 * CHUNKS[0]), LOW),
            dma((10,)),
            dma((10,)),
            dma((3,)),
            dma((4,)),
            dma((7,)),
            dma((7,)),
            dma((2,)),
            dma((14,)),
            dma((14,)),
            dma((3,)),
        ],
        compiler_params=pltpu.CompilerParams(
            collective_id=23, has_side_effects=True, vmem_limit_bytes=56 * MIB
        ),
        cost_estimate=moved(16 * rows * width),
        name="close",
    )(g_all, wa, g_mid, tokens, gains, gain_sum, blocks, rest)


def place_kernel(
    first_in,
    rest_in,
    blocks_in,
    down_in,
    out_ref,
    grad_ref,
    gate_out,
    up_out,
    down_out,
    out_copy,
    grad_copy,
    first_ref,
    rest_ref,
    blocks_ref,
    down_ref,
    sems,
):
    copies = [
        pltpu.make_async_copy(source, target, sems.at[i])
        for i, (source, target) in enumerate(
            (
                (first_in, first_ref),
                (rest_in, rest_ref),
                (blocks_in, blocks_ref),
                (down_in, down_ref),
                (out_ref, out_copy),
                (grad_ref, grad_copy),
            )
        )
    ]
    for c in copies:
        c.start()
    for c in copies[:2]:
        c.wait()
    f32 = jnp.float32
    z = lax.axis_index("dp")
    share = sum(CHUNKS)
    for second, target in enumerate((gate_out, up_out)):
        for owner in range(8):
            for group in range(4):
                at = group * 8 * share + owner * share
                start = 0
                for k, count in enumerate(CHUNKS):
                    source = first_ref if k == 0 else rest_ref
                    begin = start + (4 * second + group) * count
                    target[:, at : at + count] = source[owner, :, begin : begin + count].astype(f32)
                    at += count
                    start += 8 * count if k else 0
    for c in copies[2:4]:
        c.wait()
    total = jnp.zeros(blocks_ref.shape[1:], f32)
    for owner in range(4):
        came = jnp.abs(z - owner) < 3
        total = total + jnp.where(came, blocks_ref[owner].astype(f32), 0.0)
    down_out[: CHUNKS[0], :] = total
    down_out[CHUNKS[0] :, :] = down_ref[...].astype(f32)
    for c in copies[4:]:
        c.wait()


def place_rows(first, rest, blocks, down, output, input_grad):
    own, width = first.shape[1], blocks.shape[2]
    shape = jax.ShapeDtypeStruct
    anywhere = pl.BlockSpec(memory_space=pl.ANY)
    in_vmem = pl.BlockSpec(memory_space=pltpu.VMEM)
    wide = 32 * sum(CHUNKS)
    return pl.pallas_call(
        place_kernel,
        out_shape=[
            shape((own, wide), jnp.float32),
            shape((own, wide), jnp.float32),
            shape((sum(CHUNKS), width), jnp.float32),
            shape(output.shape, output.dtype),
            shape(input_grad.shape, input_grad.dtype),
        ],
        in_specs=[anywhere] * 6,
        out_specs=[in_vmem] * 5,
        scratch_shapes=[
            pltpu.VMEM(first.shape, LOW),
            pltpu.VMEM(rest.shape, LOW),
            pltpu.VMEM(blocks.shape, LOW),
            pltpu.VMEM(down.shape, LOW),
            pltpu.SemaphoreType.DMA((6,)),
        ],
        compiler_params=pltpu.CompilerParams(vmem_limit_bytes=63 * MIB),
        name="place",
    )(first, rest, blocks, down, output, input_grad)


def place_attn_kernel(got_ref, out_ref, query_out, key_out, value_out, grad_out):
    f32 = jnp.float32
    wide = value_out.shape[1] // 8
    qk = query_out.shape[1] // 8
    own = out_ref.shape[0] // 8
    for owner in range(8):
        value_out[:, owner * wide : (owner + 1) * wide] = got_ref[owner, :, :wide].astype(f32)
        here = slice(owner * qk, (owner + 1) * qk)
        query_out[:, here] = got_ref[owner, :, wide : wide + qk].astype(f32)
        key_out[:, here] = got_ref[owner, :, wide + qk : wide + 2 * qk].astype(f32)
        block = out_ref[owner * own : (owner + 1) * own, out_ref.shape[1] - wide :]
        grad_out[:, owner * wide : (owner + 1) * wide] = block.astype(f32)


def place_attn(got, summed, wide, qk):
    own = got.shape[1]
    shape = jax.ShapeDtypeStruct
    in_vmem = pl.BlockSpec(memory_space=pltpu.VMEM)
    return pl.pallas_call(
        place_attn_kernel,
        out_shape=[
            shape((own, 8 * qk), jnp.float32),
            shape((own, 8 * qk), jnp.float32),
            shape((own, 8 * wide), jnp.float32),
            shape((own, 8 * wide), jnp.float32),
        ],
        in_specs=[in_vmem] * 2,
        out_specs=[in_vmem] * 4,
        name="place_attn",
    )(got, summed)


def ffn_lax(h_two, cot_all, gate_full, up_full, down_full):
    pieces, rows, width = cot_all.shape
    h_two_all = gather_plane(h_two, 5).reshape(-1, width)
    cot_all = cot_all.reshape(-1, width)
    gate = dot(h_two_all, gate_full)
    up = dot(h_two_all, up_full)
    g_act = contract(cot_all, down_full, 1, 1)
    sigmoid = jax.nn.sigmoid(gate)
    silu = gate * sigmoid
    act = (silu * up).astype(LOW)
    g_gate = (g_act * up * sigmoid * (1.0 + gate * (1.0 - sigmoid))).astype(LOW)
    g_up = (g_act * silu).astype(LOW)
    part = (contract(g_gate, gate_full, 1, 1) + contract(g_up, up_full, 1, 1)).astype(LOW)
    return (
        dot(act, down_full).astype(LOW).reshape(pieces, rows, width),
        scatter_plane(part.reshape(pieces, rows, width), 7),
        contract(h_two_all, g_gate, 0, 0).astype(LOW),
        contract(h_two_all, g_up, 0, 0).astype(LOW),
        contract(act, cot_all, 0, 0).astype(LOW),
    )


def norm_scale(rows):
    return lax.rsqrt(jnp.mean(rows * rows, axis=-1, keepdims=True) + epsilon)


def norm_backward(grad, normed, inverse, gain):
    scaled = grad * gain
    return inverse * (scaled - normed * jnp.mean(scaled * normed, axis=-1, keepdims=True))


def local(
    tokens,
    doc_lengths,
    w_query,
    w_key,
    w_value,
    w_out,
    w_gate,
    w_up,
    w_down,
    gain_attn,
    gain_mlp,
    cotangent,
):
    micro, span = tokens.shape[1:3]
    pieces, groups = lax.axis_size("seq"), lax.axis_size("dp")
    place = lax.axis_index("seq")
    length = pieces * span
    heads = max(1, HEADS // pieces)
    sharers = max(1, pieces // HEADS)
    streams = micro // sharers
    first_head = place // sharers * heads
    first_stream = place % sharers * streams
    qk, wide = heads * QK_DIM, heads * HEAD_V
    hidden = FF // pieces

    out_width = D // pieces
    rows_dp = w_gate.shape[0]
    share = hidden // groups
    block = FF // groups
    mine = micro * span
    fused = pieces == 8 and groups == 4 and micro == 2 and span == 128
    chunks = CHUNKS if fused else (share,)

    def hidden_columns(w):
        parts = [
            lax.dynamic_slice_in_dim(w, z * block + place * share, share, 1) for z in range(groups)
        ]
        edges = [sum(chunks[:k]) for k in range(len(chunks) + 1)]
        return [
            [part[:, edges[k] : edges[k + 1]] for part in parts] for k in range(len(chunks))
        ]

    x_own = tokens[0].reshape(mine, D)
    flat = x_own.astype(jnp.float32)
    cot = cotangent[0].reshape(mine, D)

    def to_tokens(by_head):
        sent = by_head.reshape(streams, pieces, span, wide).transpose(1, 0, 2, 3)
        got = exchange_plane(sent, 3).reshape(pieces // sharers, micro, span, wide)
        return got.transpose(1, 2, 0, 3).reshape(mine, HEADS * HEAD_V)

    def to_heads(by_token):
        sent = by_token.reshape(micro, span, pieces // sharers, wide).transpose(2, 0, 1, 3)
        got = exchange_plane(sent.reshape(pieces, streams, span, wide), 4)
        return got.transpose(1, 0, 2, 3).reshape(streams, length, wide)

    if fused:
        gain_rows = jnp.concatenate(
            [gain_attn[None], gain_mlp[None], jnp.zeros((14, rows_dp), LOW)], axis=0
        )
        weights = (w_query, w_key, w_value, w_out, w_gate, w_up, w_down)
        front = layer_front(x_own, cot, weights, gain_rows, doc_lengths[0], length, wide, qk)
        out_full, h_all, query, key, value, att_heads, attended, mid = front[3:11]
        attn_full, gain_rows_all, out_part, g_h_two = front[11:15]
        d_ffn, d_down, ffn_blocks, down_blocks = front[17:]
    else:
        gate_parts, up_parts = hidden_columns(w_gate), hidden_columns(w_up)
        ffn_slice = jnp.concatenate(
            [part for k in range(len(chunks)) for part in gate_parts[k] + up_parts[k]], axis=1
        )
        attn_parts = [
            lax.dynamic_slice_in_dim(w_value, first_head * HEAD_V, wide, 1),
            lax.dynamic_slice_in_dim(w_query, first_head * QK_DIM, qk, 1),
            lax.dynamic_slice_in_dim(w_key, first_head * QK_DIM, qk, 1),
        ]

        lengths = lax.dynamic_slice_in_dim(doc_lengths[0], first_stream, streams, 0)
        starts = jnp.cumsum(lengths, axis=1) - lengths
        position = jnp.arange(length, dtype=jnp.int32)
        begun = starts[:, None, :] <= position[None, :, None]
        first = jnp.max(jnp.where(begun, starts[:, None, :], 0), axis=2)[..., None]

        def gather_dp(w):
            return lax.all_gather(w, "dp", axis=0, tiled=True)

        attn_got = gather_dp(
            jnp.concatenate(
                attn_parts
                + [
                    lax.dynamic_slice_in_dim(w_out, place * out_width, out_width, 1),
                    gain_attn[:, None],
                    gain_mlp[:, None],
                ],
                axis=1,
            )
        )
        ffn_full = gather_dp(ffn_slice)
        down_full = gather_dp(lax.dynamic_slice_in_dim(w_down, place * share, share, 0))
        value_full = attn_got[:, :wide]
        query_full = attn_got[:, wide : wide + qk]
        key_full = attn_got[:, wide + qk : wide + 2 * qk]
        out_full = gather_plane(attn_got[:, wide + 2 * qk : wide + 2 * qk + out_width], 2)
        gains = attn_got[:, wide + 2 * qk + out_width :].astype(jnp.float32)
        gain_one, gain_two = gains[:, 0], gains[:, 1]
        x_all = gather_plane(x_own, 1).reshape(pieces, micro, span, D).transpose(1, 0, 2, 3)
        x_all = lax.dynamic_slice_in_dim(x_all, first_stream, streams, 0).astype(jnp.float32)
        h_flat = (x_all * norm_scale(x_all) * gain_one).astype(LOW).reshape(streams * length, D)
        value = dot(h_flat, value_full).astype(LOW).reshape(streams, length, wide)
        query = dot(h_flat, query_full).astype(LOW).reshape(streams, length, qk)
        key = dot(h_flat, key_full).astype(LOW).reshape(streams, length, qk)
        att_heads = attend(query, key, value, first, heads)
        attended = to_tokens(att_heads)
        mid = flat + jnp.einsum(
            "tk,skn->tsn", attended, out_full, preferred_element_type=jnp.float32
        ).reshape(mine, D)
        h_two = (mid * norm_scale(mid) * gain_two).astype(LOW)
        out_part, g_h_two, d_gate, d_up, d_down = ffn_lax(
            h_two, gather_plane(cot, 6), ffn_full[:, :hidden], ffn_full[:, hidden:], down_full
        )
        d_ffn = jnp.concatenate([d_gate, d_up], axis=1)

    def scatter_dp(part):
        return lax.psum_scatter(part, "dp", scatter_dimension=0, tiled=True)

    own = rows_dp // pieces
    sum_ffn, sum_down = scatter_dp(d_ffn), scatter_dp(d_down)

    if fused:
        output, g_mid, g_all, gain_sum, grad_attn = layer_turn(
            g_h_two, mid, cot, gain_rows_all, out_full, out_part, attended, query, key, value,
            att_heads, doc_lengths[0], h_all, attn_full.shape[1],
        )
        grad_attn, sum_ffn, sum_down = lax.optimization_barrier((grad_attn, sum_ffn, sum_down))
        grad_attn = scatter_dp(grad_attn)
        input_grad, gain_columns, first_got, rest_got = layer_close(
            g_all, attn_full, g_mid, x_own, gain_rows_all, gain_sum, ffn_blocks, sum_ffn
        )
        grad_attn, gain_columns = lax.optimization_barrier((grad_attn, gain_columns))
        kept = attn_full.shape[1]
        attn_got = exchange_plane(grad_attn.reshape(pieces, own, -1), 12, kept)
        attn_got, first_got = lax.optimization_barrier((attn_got, first_got))
        grad_gate, grad_up, grad_down, output, input_grad = place_rows(
            first_got, rest_got, down_blocks, sum_down, output, input_grad
        )
        grad_query, grad_key, grad_value, grad_out = place_attn(attn_got, grad_attn, wide, qk)
        return (
            output.reshape(tokens.shape),
            input_grad.reshape(tokens.shape),
            grad_query,
            grad_key,
            grad_value,
            grad_out,
            grad_gate,
            grad_up,
            grad_down,
            gain_columns[:, 0],
            gain_columns[:, 1],
        )

    inverse_two = norm_scale(mid)
    plain_two = mid * inverse_two
    output = (mid + scatter_plane(out_part, 8)).astype(LOW)
    g_mid = cot.astype(jnp.float32) + norm_backward(g_h_two, plain_two, inverse_two, gain_two)
    g_mid_low = g_mid.astype(LOW)
    g_att = jnp.einsum(
        "tsn,skn->tk",
        g_mid_low.reshape(mine, pieces, out_width),
        out_full,
        preferred_element_type=jnp.float32,
    )
    g_att = to_heads(g_att.astype(LOW))
    g_query, g_key, g_value = attend_back(query, key, value, first, att_heads, g_att, heads)
    g_value = g_value.reshape(streams * length, wide)
    g_query = g_query.reshape(streams * length, qk)
    g_key = g_key.reshape(streams * length, qk)
    g_h_one_part = (
        contract(g_value, value_full, 1, 1)
        + contract(g_query, query_full, 1, 1)
        + contract(g_key, key_full, 1, 1)
    ).astype(LOW)
    g_h_one_part = g_h_one_part.reshape(streams, pieces, span, D).transpose(1, 0, 2, 3)
    if sharers > 1:
        padded = jnp.zeros((pieces, micro, span, D), LOW)
        g_h_one_part = lax.dynamic_update_slice_in_dim(padded, g_h_one_part, first_stream, 1)
    g_h_one = scatter_plane(g_h_one_part.reshape(pieces, mine, D), 9)
    inverse_one = norm_scale(flat)
    plain_one = flat * inverse_one
    input_grad = g_mid + norm_backward(g_h_one, plain_one, inverse_one, gain_one)
    grad_out = contract(attended, g_mid_low, 0, 0).astype(LOW)
    grad_out = grad_out.reshape(groups, pieces, own, D).transpose(1, 0, 2, 3)
    grad_out = scatter_plane(grad_out.reshape(pieces, groups * own, D), 10).astype(LOW)
    grad_out = scatter_dp(grad_out)
    grad_attn = jnp.concatenate(
        [
            contract(h_flat, g_value, 0, 0).astype(LOW),
            contract(h_flat, g_query, 0, 0).astype(LOW),
            contract(h_flat, g_key, 0, 0).astype(LOW),
            jnp.sum(g_h_one * plain_one, axis=0).astype(LOW)[:, None],
            jnp.sum(g_h_two * plain_two, axis=0).astype(LOW)[:, None],
        ],
        axis=1,
    )

    grad_attn = scatter_dp(grad_attn)
    ffn_got = exchange_plane(sum_ffn.reshape(pieces, own, 2 * hidden), 11).astype(jnp.float32)
    attn_got = exchange_plane(grad_attn.reshape(pieces, own, -1), 12).astype(jnp.float32)
    grad_gains = jnp.sum(attn_got[:, :, wide + 2 * qk :], axis=0)
    attn_got = jnp.sum(attn_got.reshape(pieces // sharers, sharers, own, -1), axis=1)

    def by_hidden(block):
        return block.reshape(pieces, own, groups, share).transpose(1, 2, 0, 3).reshape(own, FF)

    def by_rows(block):
        return block.transpose(1, 0, 2).reshape(own, -1)

    return (
        output.reshape(tokens.shape),
        input_grad.reshape(tokens.shape),
        by_rows(attn_got[:, :, wide : wide + qk]),
        by_rows(attn_got[:, :, wide + qk : wide + 2 * qk]),
        by_rows(attn_got[:, :, :wide]),
        grad_out.astype(jnp.float32),
        by_hidden(ffn_got[:, :, :hidden]),
        by_hidden(ffn_got[:, :, hidden:]),
        sum_down.astype(jnp.float32),
        grad_gains[:, 0],
        grad_gains[:, 1],
    )


def solution(mesh):
    by_token, by_row = P("dp", None, "seq", None), P("dp", None)
    grad_rows, grad_entries = P(("dp", "seq"), None), P(("dp", "seq"))
    return jax.shard_map(
        local,
        mesh=mesh,
        in_specs=(by_token, P("dp", None, None)) + (by_row,) * 7 + (P("dp"), P("dp"), by_token),
        out_specs=(by_token, by_token) + (grad_rows,) * 7 + (grad_entries,) * 2,
        check_vma=False,
    )
```

```python
import functools
import math

import jax
import jax.numpy as jnp
from jax import lax
from jax.experimental import pallas as pl
from jax.experimental.pallas import tpu as pltpu
from jax.sharding import PartitionSpec as P

D = 2048
HEADS = 16
QK_DIM = 16
FF = 5632
HEAD_V = 128
epsilon = 1e-06
MIB = 1024 * 1024


def dot(left, right):
    return jnp.dot(left, right, preferred_element_type=jnp.float32)


def contract(left, right, left_dim, right_dim):
    return lax.dot_general(
        left, right, (((left_dim,), (right_dim,)), ((), ())), preferred_element_type=jnp.float32
    )


def head_lanes(rows, head):
    lane = lax.broadcasted_iota(jnp.int32, rows.shape, 1)
    inside = (lane >= head * QK_DIM) & (lane < (head + 1) * QK_DIM)
    return jnp.where(inside, rows, jnp.zeros_like(rows))


def weights_of(query, key, head, first, base):
    scores = contract(head_lanes(query, head), key, 1, 1)
    row = base + lax.broadcasted_iota(jnp.int32, scores.shape, 0)
    column = lax.broadcasted_iota(jnp.int32, scores.shape, 1)
    mask = (column <= row) & (column >= first)
    poly = 1.0 + scores * (1.0 / math.sqrt(QK_DIM)) + scores * scores * (0.5 / QK_DIM)
    return scores, mask, jnp.where(mask, poly, 0.0)


def attend_kernel(heads, q_ref, k_ref, v_ref, first_ref, out_ref):
    rows = q_ref.shape[1]
    base = pl.program_id(1) * rows
    for head in range(heads):
        columns = slice(head * HEAD_V, (head + 1) * HEAD_V)
        unused, unused_mask, weight = weights_of(
            q_ref[0], k_ref[0], head, first_ref[0], base
        )
        denom = jnp.sum(weight, axis=1, keepdims=True)
        numer = dot(weight.astype(jnp.bfloat16), v_ref[0, :, columns])
        out_ref[0, :, columns] = (numer / denom).astype(jnp.bfloat16)


def attend(query, key, value, first, heads):
    streams, length, width = query.shape
    rows = min(256, length)
    return pl.pallas_call(
        functools.partial(attend_kernel, heads),
        grid=(streams, length // rows),
        in_specs=[
            pl.BlockSpec((1, rows, width), lambda m, i: (m, i, 0)),
            pl.BlockSpec((1, length, width), lambda m, i: (m, 0, 0)),
            pl.BlockSpec((1, length, heads * HEAD_V), lambda m, i: (m, 0, 0)),
            pl.BlockSpec((1, rows, 1), lambda m, i: (m, i, 0)),
        ],
        out_specs=pl.BlockSpec((1, rows, heads * HEAD_V), lambda m, i: (m, i, 0)),
        out_shape=jax.ShapeDtypeStruct(value.shape, jnp.bfloat16),
        compiler_params=pltpu.CompilerParams(vmem_limit_bytes=48 * MIB),
        name="attend",
    )(query, key, value, first)


def attend_back_kernel(
    heads, q_ref, k_ref, v_ref, first_ref, att_ref, g_ref, gq_ref, gk_ref, gv_ref, gk_sum, gv_sum
):
    rows = q_ref.shape[1]
    step = pl.program_id(1)
    base = step * rows

    @pl.when(step == 0)
    def _():
        gk_sum[...] = jnp.zeros_like(gk_sum)
        gv_sum[...] = jnp.zeros_like(gv_sum)

    query, key = q_ref[0], k_ref[0]
    g_query = jnp.zeros(query.shape, jnp.float32)
    for head in range(heads):
        columns = slice(head * HEAD_V, (head + 1) * HEAD_V)
        scores, mask, weight = weights_of(query, key, head, first_ref[0], base)
        denom = jnp.sum(weight, axis=1, keepdims=True)
        a = (g_ref[0, :, columns].astype(jnp.float32) / denom).astype(jnp.bfloat16)
        b = -jnp.sum(
            a.astype(jnp.float32) * att_ref[0, :, columns].astype(jnp.float32),
            axis=1,
            keepdims=True,
        )
        g_weight = contract(a, v_ref[0, :, columns], 1, 1) + b
        slope = 1.0 / math.sqrt(QK_DIM) + scores * (1.0 / QK_DIM)
        g_scores = jnp.where(mask, g_weight * slope, 0.0).astype(jnp.bfloat16)
        g_query += head_lanes(dot(g_scores, key), head)
        gk_sum[...] += contract(g_scores, head_lanes(query, head), 0, 0)
        gv_sum[:, columns] += contract(weight.astype(jnp.bfloat16), a, 0, 0)
    gq_ref[0] = g_query.astype(jnp.bfloat16)

    @pl.when(step == pl.num_programs(1) - 1)
    def _():
        gk_ref[0] = gk_sum[...].astype(jnp.bfloat16)
        gv_ref[0] = gv_sum[...].astype(jnp.bfloat16)


def attend_back(query, key, value, first, attended, grad, heads):
    streams, length, width = query.shape
    rows = min(256, length)
    some = pl.BlockSpec((1, rows, width), lambda m, i: (m, i, 0))
    all_narrow = pl.BlockSpec((1, length, width), lambda m, i: (m, 0, 0))
    all_wide = pl.BlockSpec((1, length, heads * HEAD_V), lambda m, i: (m, 0, 0))
    some_wide = pl.BlockSpec((1, rows, heads * HEAD_V), lambda m, i: (m, i, 0))
    return pl.pallas_call(
        functools.partial(attend_back_kernel, heads),
        grid=(streams, length // rows),
        in_specs=[
            some,
            all_narrow,
            all_wide,
            pl.BlockSpec((1, rows, 1), lambda m, i: (m, i, 0)),
            some_wide,
            some_wide,
        ],
        out_specs=[some, all_narrow, all_wide],
        out_shape=[
            jax.ShapeDtypeStruct(query.shape, jnp.bfloat16),
            jax.ShapeDtypeStruct(key.shape, jnp.bfloat16),
            jax.ShapeDtypeStruct(value.shape, jnp.bfloat16),
        ],
        scratch_shapes=[
            pltpu.VMEM((length, width), jnp.float32),
            pltpu.VMEM((length, heads * HEAD_V), jnp.float32),
        ],
        compiler_params=pltpu.CompilerParams(vmem_limit_bytes=56 * MIB),
        name="attend_back",
    )(query, key, value, first, attended, grad)

MESH = pl.DeviceIdType.MESH
LOW = jnp.bfloat16


def partners():
    me = lax.axis_index("seq")
    core, x, y = me % 2, me // 2 % 2, me // 4
    return me, me + 1 - 2 * core, me + 2 - 4 * x, me + 4 - 8 * y


def greet(others):
    barrier = pltpu.get_barrier_semaphore()
    for other in others:
        pl.semaphore_signal(barrier, inc=1, device_id={"seq": other}, device_id_type=MESH)
    pl.semaphore_wait(barrier, len(others))


def remote(send, recv, k, src, dst, to):
    return pltpu.make_async_remote_copy(
        src_ref=src,
        dst_ref=dst,
        send_sem=send.at[k],
        recv_sem=recv.at[k],
        device_id={"seq": to},
        device_id_type=MESH,
    )


def gather_kernel(x_ref, o_ref, send, recv, own_sem):
    me, sib, xn, yn = partners()
    diag = xn + yn - me
    half = x_ref.shape[0] // 2
    copy = functools.partial(remote, send, recv)
    upper, lower = pl.ds(0, half), pl.ds(half, half)
    greet((sib, xn, yn))
    own = pltpu.make_async_copy(x_ref, o_ref.at[me], own_sem)
    own.start()
    xa = copy(0, x_ref.at[upper], o_ref.at[me, upper], xn)
    yb = copy(1, x_ref.at[lower], o_ref.at[me, lower], yn)
    xb = copy(2, x_ref.at[lower], o_ref.at[me, lower], xn)
    ya = copy(3, x_ref.at[upper], o_ref.at[me, upper], yn)
    beside = [copy(4, x_ref, o_ref.at[me], sib)]
    started = [xa, yb, xb, ya, beside[0]]
    for c in started:
        c.start()

    def pass_on(k, origin, part, to):
        block = o_ref.at[origin, part]
        c = copy(k, block, block, to)
        c.start()
        started.append(c)
        return c

    xa.wait_recv()
    fy = pass_on(5, xn, upper, yn)
    beside.append(pass_on(6, xn, upper, sib))
    yb.wait_recv()
    fx = pass_on(7, yn, lower, xn)
    beside.append(pass_on(8, yn, lower, sib))
    xb.wait_recv()
    beside.append(pass_on(9, xn, lower, sib))
    ya.wait_recv()
    beside.append(pass_on(10, yn, upper, sib))
    fy.wait_recv()
    beside.append(pass_on(11, diag, upper, sib))
    fx.wait_recv()
    beside.append(pass_on(12, diag, lower, sib))
    own.wait()
    for c in beside:
        c.wait_recv()
    for c in started:
        c.wait_send()


def moved(nbytes):
    return pl.CostEstimate(flops=0, bytes_accessed=nbytes * 10, transcendentals=0)


def gather_plane(x, number):
    pieces = lax.axis_size("seq")
    if pieces != 8:
        return lax.all_gather(x, "seq", axis=0)
    return pl.pallas_call(
        gather_kernel,
        out_shape=jax.ShapeDtypeStruct((8,) + x.shape, x.dtype),
        in_specs=[pl.BlockSpec(memory_space=pl.ANY)],
        out_specs=pl.BlockSpec(memory_space=pl.ANY),
        scratch_shapes=[
            pltpu.SemaphoreType.DMA((13,)),
            pltpu.SemaphoreType.DMA((13,)),
            pltpu.SemaphoreType.DMA,
        ],
        compiler_params=pltpu.CompilerParams(collective_id=number, has_side_effects=True),
        cost_estimate=moved(16 * x.size),
        name="gather",
    )(x)


def scatter_kernel(p_ref, o_ref, held, got, one, two, send, recv, own_sem):
    me, sib, xn, yn = partners()
    diag = xn + yn - me
    half = p_ref.shape[1] // 2
    copy = functools.partial(remote, send, recv)
    upper, lower = pl.ds(0, half), pl.ds(half, half)
    greet((sib, xn, yn))
    beside, loads = [], []
    for i, owner in enumerate((diag, xn, yn, me)):
        beside.append(copy(i, p_ref.at[owner + sib - me], got.at[i], sib))
        loads.append(pltpu.make_async_copy(p_ref.at[owner], held.at[i], own_sem.at[i]))
        beside[i].start()
        loads[i].start()

    def pair_sum(i):
        beside[i].wait_recv()
        loads[i].wait()
        held[i] = held[i] + got[i]

    pair_sum(0)
    x0 = copy(4, held.at[0, upper], one.at[0], xn)
    x0.start()
    y0 = copy(5, held.at[0, lower], one.at[1], yn)
    y0.start()
    pair_sum(1)
    x1 = copy(6, held.at[1, upper], one.at[2], xn)
    x1.start()
    pair_sum(2)
    y1 = copy(7, held.at[2, lower], one.at[3], yn)
    y1.start()
    pair_sum(3)
    x0.wait_recv()
    held[2, :half] = held[2, :half] + one[0]
    y2 = copy(8, held.at[2, upper], two.at[0], yn)
    y2.start()
    y0.wait_recv()
    held[1, half:] = held[1, half:] + one[1]
    x2 = copy(9, held.at[1, lower], two.at[1], xn)
    x2.start()
    x1.wait_recv()
    y1.wait_recv()
    y2.wait_recv()
    wide = jnp.float32
    o_ref[:half] = held[3, :half].astype(wide) + one[2].astype(wide) + two[0].astype(wide)
    x2.wait_recv()
    o_ref[half:] = held[3, half:].astype(wide) + one[3].astype(wide) + two[1].astype(wide)
    for c in (*beside, x0, y0, x1, y1, y2, x2):
        c.wait_send()


def scatter_plane(part, number):
    pieces, rows, columns = part.shape
    if pieces != 8:
        return lax.psum_scatter(part, "seq", scatter_dimension=0).astype(jnp.float32)
    return pl.pallas_call(
        scatter_kernel,
        out_shape=jax.ShapeDtypeStruct((rows, columns), jnp.float32),
        in_specs=[pl.BlockSpec(memory_space=pl.ANY)],
        out_specs=pl.BlockSpec(memory_space=pltpu.VMEM),
        scratch_shapes=[
            pltpu.VMEM((4, rows, columns), LOW),
            pltpu.VMEM((4, rows, columns), LOW),
            pltpu.VMEM((4, rows // 2, columns), LOW),
            pltpu.VMEM((2, rows // 2, columns), LOW),
            pltpu.SemaphoreType.DMA((10,)),
            pltpu.SemaphoreType.DMA((10,)),
            pltpu.SemaphoreType.DMA((4,)),
        ],
        compiler_params=pltpu.CompilerParams(
            collective_id=number, has_side_effects=True, vmem_limit_bytes=40 * MIB
        ),
        cost_estimate=moved(2 * part.size),
        name="scatter",
    )(part)


def exchange_kernel(x_ref, o_ref, send, recv, own_sem):
    me = lax.axis_index("seq")
    columns = pl.ds(0, o_ref.shape[2])
    others = [lax.rem(me + i, 8) for i in range(1, 8)]
    greet(others)
    own = pltpu.make_async_copy(x_ref.at[me, :, columns], o_ref.at[me], own_sem)
    own.start()
    copies = [
        remote(send, recv, i, x_ref.at[other, :, columns], o_ref.at[me], other)
        for i, other in enumerate(others)
    ]
    for c in copies:
        c.start()
    own.wait()
    for c in copies:
        c.wait()


def exchange_plane(x, number, columns=None):
    if lax.axis_size("seq") != 8:
        return lax.all_to_all(x, "seq", 0, 0)
    return pl.pallas_call(
        exchange_kernel,
        out_shape=jax.ShapeDtypeStruct(x.shape[:-1] + (columns or x.shape[-1],), x.dtype),
        in_specs=[pl.BlockSpec(memory_space=pl.ANY)],
        out_specs=pl.BlockSpec(memory_space=pl.ANY),
        scratch_shapes=[
            pltpu.SemaphoreType.DMA((7,)),
            pltpu.SemaphoreType.DMA((7,)),
            pltpu.SemaphoreType.DMA,
        ],
        compiler_params=pltpu.CompilerParams(collective_id=number, has_side_effects=True),
        cost_estimate=moved(4 * x.size),
        name="exchange",
    )(x)


CHUNKS = (64, 64, 48)


class PlaneGather:
    def __init__(self, source, target, send, recv):
        me, sib, xn, yn = partners()
        diag = xn + yn - me
        half = target.shape[1] // 2
        upper, lower = pl.ds(0, half), pl.ds(half, half)
        copy = functools.partial(remote, send, recv)

        def direct(k, part, to):
            return copy(k, source.at[part], target.at[me, part], to)

        def pass_on(k, origin, part, to):
            return copy(k, target.at[origin, part], target.at[origin, part], to)

        self.xa, self.yb = direct(0, upper, xn), direct(1, lower, yn)
        self.xb, self.ya = direct(2, lower, xn), direct(3, upper, yn)
        self.s0 = copy(4, source, target.at[me], sib)
        self.fy, self.fx = pass_on(5, xn, upper, yn), pass_on(6, yn, lower, xn)
        self.s1, self.s2 = pass_on(7, xn, upper, sib), pass_on(8, yn, lower, sib)
        self.s3, self.s4 = pass_on(9, xn, lower, sib), pass_on(10, yn, upper, sib)
        self.s5, self.s6 = pass_on(11, diag, upper, sib), pass_on(12, diag, lower, sib)

    def start(self):
        for c in (self.xa, self.yb, self.xb, self.ya, self.s0):
            c.start()

    def forward_first(self):
        self.xa.wait_recv()
        self.yb.wait_recv()
        for c in (self.fy, self.fx, self.s1, self.s2):
            c.start()

    def forward_second(self):
        self.xb.wait_recv()
        self.ya.wait_recv()
        self.s3.start()
        self.s4.start()

    def forward_third(self):
        self.fy.wait_recv()
        self.fx.wait_recv()
        self.s5.start()
        self.s6.start()

    def from_sibling(self, chip):
        for c in {"own": (self.s0,), "x": (self.s1, self.s3), "y": (self.s2, self.s4), "diag": (self.s5, self.s6)}[chip]:
            c.wait_recv()

    def sent(self):
        for c in (self.xa, self.yb, self.xb, self.ya, self.s0, self.fy, self.fx):
            c.wait_send()
        for c in (self.s1, self.s2, self.s3, self.s4, self.s5, self.s6):
            c.wait_send()

    def arrive(self, step):
        @pl.when(step == 1)
        def _():
            self.from_sibling("own")

        @pl.when(step == 2)
        def _():
            self.forward_first()
            self.forward_second()
            self.from_sibling("x")

        @pl.when(step == 4)
        def _():
            self.from_sibling("y")

        @pl.when(step == 6)
        def _():
            self.forward_third()
            self.from_sibling("diag")


class LineGather:
    def __init__(self, item, source, block, send, recv, local=None):
        z = lax.axis_index("dp")
        self.z = z

        def copy(k, src, owner, to):
            return pltpu.make_async_remote_copy(
                src_ref=src,
                dst_ref=block(owner),
                send_sem=send.at[item, k],
                recv_sem=recv.at[item, owner],
                device_id={"dp": to},
                device_id_type=MESH,
            )

        self.sends = []
        for k, d in enumerate((2, -2, 1, -1)):
            to = z + d
            valid = (to >= 0) & (to < 4)
            self.sends.append((valid, copy(k, source, z, jnp.clip(to, 0, 3))))
        inner = (z == 1) | (z == 2)
        far = jnp.where(z == 1, 3, 0)
        self.stop = (inner, copy(4, block(far), far, jnp.where(z == 1, 0, 3)))
        others = [lax.rem(z + o, 4) for o in (1, 2, 3)]
        self.blocks = [copy(0, source, other, other) for other in others]
        self.own = None
        if local is not None:
            self.own = pltpu.make_async_copy(source, block(z), local.at[item])

    def start_far(self):
        if self.own is not None:
            self.own.start()
        self.begin(self.sends[:2])

    def start_near(self):
        self.begin(self.sends[2:])

    def start(self):
        self.start_far()
        self.start_near()

    def begin(self, sends):
        for valid, c in sends:

            @pl.when(valid)
            def _(c=c):
                c.start()

    def forward(self):
        inner, c = self.stop

        @pl.when(inner)
        def _():
            self.blocks[1].wait_recv()
            c.start()

    def wait(self):
        inner, unused = self.stop
        self.blocks[0].wait_recv()
        self.blocks[2].wait_recv()

        @pl.when(jnp.logical_not(inner))
        def _():
            self.blocks[1].wait_recv()

        if self.own is not None:
            self.own.wait()

    def sent(self):
        for valid, c in (*self.sends, self.stop):

            @pl.when(valid)
            def _(c=c):
                c.wait_send()


def nearest_first(step):
    me, sib, xn, yn = partners()
    chip = jnp.where(step < 4, xn, jnp.where(step < 6, yn, xn + yn - me))
    later = chip + jnp.where(lax.rem(step, 2) == 0, sib - me, 0)
    return jnp.where(step == 0, me, jnp.where(step == 1, sib, later))


def farthest_first(step):
    me, sib, xn, yn = partners()
    chip = jnp.where(step < 4, xn, yn)
    chip = jnp.where(step < 2, xn + yn - me, jnp.where(step < 6, chip, me))
    return chip + jnp.where(lax.rem(step, 2) == 0, sib - me, 0)


def first_of(lengths, stream, base, count):
    row = base + lax.broadcasted_iota(jnp.int32, (count, 1), 0)
    start, first = jnp.int32(0), jnp.zeros((count, 1), jnp.int32)
    for j in range(lengths.shape[1]):
        first = jnp.where(row >= start, start, first)
        start = start + lengths[stream, j]
    return first


def layer_kernel(
    x_ref,
    c_ref,
    wq_ref,
    wk_ref,
    wv_ref,
    wo_ref,
    wg_ref,
    wu_ref,
    wd_ref,
    gain_ref,
    lengths_ref,
    x_all,
    c_all,
    h2_all,
    wo_all,
    h1_out,
    q_out,
    k_out,
    v_out,
    att_out,
    tok_out,
    mid_out,
    wa_out,
    gain_out,
    out_part,
    gh_out,
    dgu_first,
    dd_first,
    dgu_out,
    dd_out,
    dgu_all,
    dd_all,
    wa,
    wgu,
    wd,
    gains,
    q_s,
    k_s,
    v_s,
    att_s,
    tok,
    mid,
    act_s,
    ggu_s,
    sum_gu,
    sum_d,
    x_buf,
    c_buf,
    o_buf,
    beside,
    held,
    got,
    one,
    two,
    gsend,
    grecv,
    zsend,
    zrecv,
    zlocal,
    esend,
    erecv,
    rsend,
    rrecv,
    load_sem,
    out_sem,
    h1_sem,
    w_sem,
    done_sem,
    self_sem,
    fsend,
    frecv,
    f_sem,
    cut_sem,
    gu_stop,
    d_stop,
):
    me, sib, xn, yn = partners()
    z = lax.axis_index("dp")
    rows, width = x_ref.shape
    span = rows // 2
    wide, qk = v_s.shape[2], q_s.shape[2]
    share = CHUNKS[0] + CHUNKS[1] + CHUNKS[2]
    half = rows // 2
    upper, lower = pl.ds(0, half), pl.ds(half, half)

    barrier = pltpu.get_barrier_semaphore()
    for i in range(1, 8):
        pl.semaphore_signal(
            barrier, inc=1, device_id={"seq": lax.rem(me + i, 8)}, device_id_type=MESH
        )
    for i in range(1, 4):
        pl.semaphore_signal(
            barrier, inc=1, device_id={"dp": lax.rem(z + i, 4)}, device_id_type=MESH
        )
    pl.semaphore_wait(barrier, 10)

    tokens = PlaneGather(x_ref, x_all, gsend.at[0], grecv.at[0])
    out_w = PlaneGather(wo_all.at[me], wo_all, gsend.at[1], grecv.at[1])
    cots = PlaneGather(c_ref, c_all, gsend.at[2], grecv.at[2])
    hidden_in = PlaneGather(held.at[0], h2_all, gsend.at[3], grecv.at[3])

    def line(item, source, block):
        return LineGather(item, source, block, zsend, zrecv, zlocal)

    def line_in_place(item, block):
        return LineGather(item, block(z), block, zsend, zrecv)

    depth = wq_ref.shape[0]

    def rows_of(ref, count, columns=None):
        def block(owner):
            if columns is None:
                return ref.at[pl.ds(owner * count, count)]
            return ref.at[pl.ds(owner * count, count), columns]

        return block

    z_gain = line(
        0, gain_ref, lambda owner: gains.at[:, pl.ds(pl.multiple_of(owner * depth, 128), depth)]
    )
    z_attn = line_in_place(1, rows_of(wa, depth))
    z_out = line(
        2,
        wo_ref.at[:, pl.ds(pl.multiple_of(me * wide, 128), wide)],
        lambda owner: wo_all.at[me, pl.ds(owner * depth, depth)],
    )
    z_up, z_down = [], []
    column, before = 0, 0
    columns, hiddens = [], []
    for k, count in enumerate(CHUNKS):
        part = pl.ds(column, 8 * count)
        z_up.append(line_in_place(3 + k, rows_of(wgu, depth, part)))
        z_down.append(
            line(
                6 + k,
                wd_ref.at[pl.ds(me * share + before, count)],
                lambda owner, base=4 * before, count=count: wd.at[
                    pl.ds(base + owner * count, count)
                ],
            )
        )
        columns.append(column)
        hiddens.append(4 * before)
        column += 8 * count
        before += count

    tokens.start()
    z_gain.start()

    window = 384
    tall = depth // 2

    def cut_window(i, source, start, size, r, slot, lane):
        return pltpu.make_async_copy(
            source.at[pl.ds(r * tall, tall), pl.ds(pl.multiple_of(start, 128), size)],
            got.at[slot, :, pl.ds(lane, size)],
            cut_sem.at[i],
        )

    per_tile = 128 // qk
    narrow = me // per_tile * 128
    shift = lax.rem(me, per_tile) * qk
    own_rows = pl.ds(pl.multiple_of(z * depth, depth), depth)
    v_cut = pltpu.make_async_copy(
        wv_ref.at[:, pl.ds(pl.multiple_of(me * wide, 128), wide)],
        wa.at[own_rows, pl.ds(0, wide)],
        cut_sem.at[20],
    )
    v_cut.start()
    qk_cuts = [
        cut_window(2 * r + i, source, narrow, 128, r, r, 128 * i)
        for r in range(2)
        for i, source in enumerate((wq_ref, wk_ref))
    ]
    for c in qk_cuts:
        c.start()
    ff_cuts = []
    ff_width = wg_ref.shape[1]
    for second, source in enumerate((wg_ref, wu_ref)):
        for group in range(4):
            start = group * (ff_width // 4) + me * share
            aligned = jnp.minimum(start // 128 * 128, ff_width - window)
            lane = 256 * (1 - second) + window * group
            for r in range(2):
                c = cut_window(
                    4 + len(ff_cuts), source, aligned, window, r, 2 * second + r, lane
                )
                c.start()
                ff_cuts.append((c, second, group, r, lane, start - aligned))
    for c in qk_cuts:
        c.wait()
    for r in range(2):
        lane = lax.broadcasted_iota(jnp.int32, (tall, 128), 1)
        q_rows = pltpu.roll(got[r, :, 0:128].astype(jnp.float32), lax.rem(128 - shift, 128), 1)
        k_rows = pltpu.roll(
            got[r, :, 128:256].astype(jnp.float32), lax.rem(128 + qk - shift, 128), 1
        )
        both = jnp.where(lane < qk, q_rows, jnp.where(lane < 2 * qk, k_rows, 0.0))
        there = pl.ds(pl.multiple_of(z * depth + r * tall, tall), tall)
        wa[there, wide : wide + 128] = both.astype(LOW)
    v_cut.wait()
    z_attn.start()
    for c, second, group, r, lane, shift_by in ff_cuts:
        c.wait()
        rolled = pltpu.roll(
            got[2 * second + r, :, lane : lane + window].astype(jnp.float32),
            lax.rem(window - shift_by, window),
            1,
        )
        there = pl.ds(pl.multiple_of(z * depth + r * tall, tall), tall)
        begin = 0
        for k, count in enumerate(CHUNKS):
            at = columns[k] + (4 * second + group) * count
            wgu[there, at : at + count] = rolled[:, begin : begin + count].astype(LOW)
            begin += count
    z_out.start()
    for g in (z_up[0], z_down[0]):
        g.start()

    def loads(order, step, sources):
        slot = lax.rem(step, 2)
        owner = order(step)
        return [
            pltpu.make_async_copy(source.at[owner], buf.at[slot], load_sem.at[i, slot])
            for i, (source, buf) in enumerate(sources)
        ]

    first_load = pltpu.make_async_copy(x_ref, x_buf.at[0], load_sem.at[0, 0])
    first_load.start()
    c_load = pltpu.make_async_copy(c_ref, c_buf.at[0], load_sem.at[1, 0])
    c_load.start()
    tokens.forward_first()
    z_gain.forward()
    z_attn.forward()
    tokens.forward_second()
    cots.start()
    c_load.wait()
    own_c = pltpu.make_async_copy(c_buf.at[0], c_all.at[me], self_sem.at[3])
    own_c.start()
    z_gain.wait()
    z_attn.wait()
    for g in (z_up[1], z_down[1]):
        g.start()

    def h1_copies(step):
        slot = lax.rem(step, 2)
        owner = nearest_first(step)
        return [
            pltpu.make_async_copy(
                o_buf.at[slot, pl.ds(m * span, span)],
                h1_out.at[m, pl.ds(owner * span, span)],
                h1_sem.at[m, slot],
            )
            for m in range(2)
        ]

    def arrive_tokens(step):
        @pl.when(step == 1)
        def _():
            tokens.from_sibling("own")

        @pl.when(step == 2)
        def _():
            tokens.from_sibling("x")

        @pl.when(step == 4)
        def _():
            tokens.forward_third()
            tokens.from_sibling("y")

        @pl.when(step == 6)
        def _():
            tokens.from_sibling("diag")

        @pl.when(step == 7)
        def _():
            z_out.forward()

    token_source = [(x_all, x_buf)]

    def project(step, carry):
        slot = lax.rem(step, 2)
        owner = nearest_first(step)
        for c in loads(nearest_first, step, token_source):
            c.wait()

        @pl.when(step >= 2)
        def _():
            for c in h1_copies(step - 2):
                c.wait()

        x = x_buf[slot].astype(jnp.float32)
        gain = gains[0:1, :].astype(jnp.float32)
        h_one = (x * norm_scale(x) * gain).astype(LOW)
        o_buf[slot] = h_one
        for c in h1_copies(step):
            c.start()
        arrive_tokens(step + 1)

        @pl.when(step < 7)
        def _():
            for c in loads(nearest_first, step + 1, token_source):
                c.start()

        projected = dot(h_one, wa[...]).astype(LOW)
        for m in range(2):
            there = pl.ds(owner * span, span)
            mine = projected[m * span : (m + 1) * span]
            v_s[m, there, :] = mine[:, :wide]
            q_s[m, there, :] = mine[:, wide : wide + qk]
            k_s[m, there, :] = mine[:, wide + qk : wide + 2 * qk]
        return carry

    lax.fori_loop(0, 8, project, 0)
    for step in (6, 7):
        for c in h1_copies(step):
            c.wait()
    z_out.wait()
    out_w.start()
    for g in (z_up[2], z_down[2]):
        g.start()

    finals = [
        pltpu.make_async_copy(source, target, done_sem.at[i])
        for i, (source, target) in enumerate(
            (
                (q_s, q_out),
                (k_s, k_out),
                (v_s, v_out),
                (wa, wa_out),
                (gains, gain_out),
                (att_s, att_out),
                (tok, tok_out),
                (mid, mid_out),
            )
        )
    ]
    for c in finals[:5]:
        c.start()

    length = v_s.shape[1]
    block = 256

    def attend_stream(m, carry):
        for i in range(length // block):
            rows_i = slice(i * block, (i + 1) * block)
            seen = (i + 1) * block
            first = first_of(lengths_ref, m, i * block, block)
            for head in range(wide // HEAD_V):
                lanes = slice(head * HEAD_V, (head + 1) * HEAD_V)
                unused, unused_mask, weight = weights_of(
                    q_s[m, rows_i, :], k_s[m, :seen, :], head, first, i * block
                )
                denom = jnp.sum(weight, axis=1, keepdims=True)
                numer = dot(weight.astype(LOW), v_s[m, :seen, lanes])
                att_s[m, rows_i, lanes] = (numer / denom).astype(LOW)
        return carry

    lax.fori_loop(0, 2, attend_stream, 0)
    out_w.forward_first()
    finals[5].start()

    to_mine = pl.ds(pl.multiple_of(me * wide, 128), wide)
    swaps = []
    for i in range(1, 8):
        other = lax.rem(me + i, 8)
        for m in range(2):
            swaps.append(
                remote(
                    esend,
                    erecv,
                    2 * (i - 1) + m,
                    att_s.at[m, pl.ds(other * span, span)],
                    tok.at[pl.ds(m * span, span), to_mine],
                    other,
                )
            )
            swaps[-1].start()
    kept = [
        pltpu.make_async_copy(
            att_s.at[m, pl.ds(me * span, span)],
            tok.at[pl.ds(m * span, span), to_mine],
            self_sem.at[m],
        )
        for m in range(2)
    ]
    for c in kept:
        c.start()
    x_load = pltpu.make_async_copy(x_ref, x_buf.at[0], load_sem.at[0, 0])
    x_load.start()

    def w_lanes(slot):
        return pl.ds(pl.multiple_of(slot * wide, 128), wide)

    def w_load(step):
        slot = lax.rem(step, 2)
        return pltpu.make_async_copy(
            wo_all.at[nearest_first(step)], act_s.at[:, w_lanes(slot)], w_sem.at[slot]
        )

    w_load(0).start()
    out_w.forward_second()
    cots.forward_first()
    cots.forward_second()
    z_up[0].forward()
    z_down[0].forward()
    for c in kept:
        c.wait()
    for c in swaps:
        c.wait_recv()
    finals[6].start()
    x_load.wait()

    def arrive_out(step):
        @pl.when(step == 1)
        def _():
            out_w.from_sibling("own")

        @pl.when(step == 2)
        def _():
            out_w.from_sibling("x")

        @pl.when(step == 4)
        def _():
            out_w.forward_third()
            out_w.from_sibling("y")

        @pl.when(step == 6)
        def _():
            out_w.from_sibling("diag")

    def project_out(step, carry):
        slot = lax.rem(step, 2)
        owner = nearest_first(step)
        w_load(step).wait()
        arrive_out(step + 1)

        @pl.when(step < 7)
        def _():
            w_load(step + 1).start()

        there = pl.ds(pl.multiple_of(owner * wide, 128), wide)
        mid[:, there] = dot(tok[...], act_s[:, w_lanes(slot)])
        return carry

    lax.fori_loop(0, 8, project_out, 0)
    mid_value = x_buf[0].astype(jnp.float32) + mid[...]
    mid[...] = mid_value
    held[0] = (mid_value * norm_scale(mid_value) * gains[1:2, :].astype(jnp.float32)).astype(LOW)
    hidden_in.start()
    own_h2 = pltpu.make_async_copy(held.at[0], h2_all.at[me], self_sem.at[2])
    own_h2.start()
    cots.forward_third()
    z_up[1].forward()
    z_down[1].forward()
    own_h2.wait()
    own_c.wait()
    z_up[0].wait()
    z_down[0].wait()

    largest = 4 * max(CHUNKS)
    sources = [(h2_all, x_buf), (c_all, c_buf)]

    def out_copy(order, step):
        slot = lax.rem(step, 2)
        return pltpu.make_async_copy(o_buf.at[slot], out_part.at[order(step)], out_sem.at[slot])

    def hidden_chunk(k, owner, h, c):
        count = 4 * CHUNKS[k]
        pair = pl.ds(columns[k], 2 * count)
        here = pl.ds(hiddens[k], count)
        both = dot(h, wgu[:, pair])
        gate, up = both[:, :count], both[:, count:]
        g_act = contract(c, wd[here, :], 1, 1)
        sigmoid = jax.nn.sigmoid(gate)
        silu = gate * sigmoid
        act = (silu * up).astype(LOW)
        g_gate = (g_act * up * sigmoid * (1.0 + gate * (1.0 - sigmoid))).astype(LOW)
        g_up = (g_act * silu).astype(LOW)
        there = pl.ds(owner * rows, rows)
        act_s[there, here] = act
        g_both = jnp.concatenate([g_gate, g_up], axis=1)
        ggu_s[there, pair] = g_both
        return act, g_both

    def add_grads(k, step, h, c, act, g_both):
        count = 4 * CHUNKS[k]

        to, low = (2 * largest, largest) if k == 1 else (0, 0)

        @pl.when(step == 0)
        def _():
            sum_gu[:, to : to + 2 * count] = jnp.zeros((width, 2 * count), jnp.float32)
            sum_d[low : low + count, :] = jnp.zeros((count, width), jnp.float32)

        sum_gu[:, to : to + 2 * count] += contract(h, g_both, 0, 0)
        sum_d[low : low + count, :] += contract(act, c, 0, 0)

    def emit(k):
        count = 4 * CHUNKS[k]
        rest = share - CHUNKS[0]
        to, low = (2 * largest, largest) if k == 1 else (0, 0)

        def gu_copies(i, slot):
            there = pl.ds(i * rows, rows)
            if k == 0:
                return [
                    pltpu.make_async_copy(
                        o_buf.at[slot, :, pl.ds(second * count, count)],
                        dgu_first.at[second, there],
                        h1_sem.at[second, slot],
                    )
                    for second in range(2)
                ]
            return [
                pltpu.make_async_copy(
                    o_buf.at[slot, :, pl.ds(0, 2 * count)],
                    dgu_out.at[there, pl.ds(columns[k] - columns[1], 2 * count)],
                    out_sem.at[slot],
                )
            ]

        def d_target(owner):
            if k == 0:
                return dd_first.at[pl.ds(owner * CHUNKS[0], CHUNKS[0])]
            start = owner * rest + (hiddens[k] - hiddens[1]) // 4
            return dd_out.at[pl.ds(start, CHUNKS[k])]

        pending = [[], []]
        for i in range(width // rows):
            slot = i % 2
            for c in pending[slot]:
                c.wait()
            total = sum_gu[i * rows : (i + 1) * rows, to : to + 2 * count]
            o_buf[slot, :, : 2 * count] = total.astype(LOW)
            pending[slot] = gu_copies(i, slot)
            for c in pending[slot]:
                c.start()
        for c in (*pending[0], *pending[1]):
            c.wait()
        o_buf[0, :count, :] = sum_d[low : low + count, :].astype(LOW)
        downs = []
        for owner in range(4):
            downs.append(
                pltpu.make_async_copy(
                    o_buf.at[0, pl.ds(owner * CHUNKS[k], CHUNKS[k])],
                    d_target(owner),
                    h1_sem.at[owner // 2, owner % 2],
                )
            )
            downs[-1].start()
        for c in downs:
            c.wait()

    def forward_pass(chunks, last, arrive, step, carry):
        slot = lax.rem(step, 2)
        for c in loads(nearest_first, step, sources):
            c.wait()
        h, c = x_buf[slot], c_buf[slot]
        made = [hidden_chunk(k, nearest_first(step), h, c) for k in chunks]
        if arrive is not None:
            arrive(step + 1)

        @pl.when(step < last)
        def _():
            for c in loads(nearest_first, step + 1, sources):
                c.start()

        for k, (act, g_both) in zip(chunks, made):
            add_grads(k, step, h, c, act, g_both)
        return carry

    def arrive_both(step):
        hidden_in.arrive(step)

        @pl.when(step == 1)
        def _():
            cots.from_sibling("own")

        @pl.when(step == 2)
        def _():
            cots.from_sibling("x")

        @pl.when(step == 4)
        def _():
            cots.from_sibling("y")

        @pl.when(step == 6)
        def _():
            cots.from_sibling("diag")

    for c in loads(nearest_first, 0, sources):
        c.start()

    def arrive_near(step):
        @pl.when(step < 4)
        def _():
            arrive_both(step)

    lax.fori_loop(0, 4, functools.partial(forward_pass, (0,), 3, arrive_near), 0)
    for c in loads(nearest_first, 0, sources):
        c.start()
    z_up[1].wait()
    z_down[1].wait()
    lax.fori_loop(0, 4, functools.partial(forward_pass, (1,), 3, None), 0)
    z_up[2].forward()
    z_down[2].forward()
    arrive_both(jnp.int32(4))
    for c in loads(nearest_first, 4, sources):
        c.start()
    lax.fori_loop(4, 8, functools.partial(forward_pass, (0, 1), 7, arrive_both), 0)
    hidden_in.sent()
    finals[7].start()
    for c in loads(farthest_first, 0, sources):
        c.start()
    emit(0)
    sum_lines = [
        LineScatter(
            lambda owner: dgu_first.at[:, pl.ds(owner * depth, depth), :],
            dgu_all,
            gu_stop,
            att_s.at[:, pl.ds(0, depth), :],
            fsend.at[0],
            frecv.at[0],
            f_sem.at[0],
        ),
        LineScatter(
            lambda owner: dd_first.at[pl.ds(owner * CHUNKS[0], CHUNKS[0])],
            dd_all,
            d_stop,
            tok.at[pl.ds(0, CHUNKS[0])],
            fsend.at[1],
            frecv.at[1],
            f_sem.at[1],
        ),
    ]
    for c in swaps:
        c.wait_send()
    finals[5].wait()
    finals[6].wait()
    for g in sum_lines:
        g.start_first()

    z_up[2].wait()
    z_down[2].wait()

    copy = functools.partial(remote, rsend, rrecv)
    b_diag = copy(0, beside.at[0], got.at[2], sib)
    b_x = copy(1, beside.at[1], got.at[1], sib)
    b_y = copy(2, beside.at[0], got.at[3], sib)
    b_own = copy(3, beside.at[1], got.at[0], sib)
    x0 = copy(4, held.at[2, upper], one.at[0], xn)
    y0 = copy(5, held.at[2, lower], one.at[1], yn)
    x1 = copy(6, held.at[1, upper], one.at[2], xn)
    y1 = copy(7, held.at[3, lower], one.at[3], yn)
    y2 = copy(8, held.at[3, upper], two.at[0], yn)
    x2 = copy(9, held.at[1, lower], two.at[1], xn)

    def last_pass(step, carry):
        slot = lax.rem(step, 2)
        owner = farthest_first(step)
        there = pl.ds(owner * rows, rows)
        for c in loads(farthest_first, step, sources):
            c.wait()
        hidden_chunk(2, owner, x_buf[slot], c_buf[slot])

        @pl.when(step < 7)
        def _():
            for c in loads(farthest_first, step + 1, sources):
                c.start()

        part = contract(ggu_s[there, :], wgu[...], 1, 1).astype(LOW)

        @pl.when(step == 2)
        def _():
            for g in sum_lines:
                g.start()

        @pl.when(step == 6)
        def _():
            for g in sum_lines:
                g.join()

        for k, place, sent in ((0, 0, b_diag), (2, 1, b_x), (4, 0, b_y), (6, 1, b_own)):

            @pl.when(step == k)
            def _(k=k, place=place, sent=sent):
                if k == 4:
                    b_diag.wait_send()
                if k == 6:
                    b_x.wait_send()
                beside[place] = part
                sent.start()

        for k, place, arrived in ((1, 2, b_diag), (3, 1, b_x), (5, 3, b_y), (7, 0, b_own)):

            @pl.when(step == k)
            def _(k=k, place=place, arrived=arrived):
                arrived.wait_recv()
                held[place] = part + got[place]
                if k == 1:
                    x0.start()
                    y0.start()
                if k == 3:
                    x1.start()
                if k == 5:
                    y1.start()
                    y0.wait_recv()
                    held[1, half:] = held[1, half:] + one[1]
                    x2.start()
                    x0.wait_recv()
                    held[3, :half] = held[3, :half] + one[0]
                    y2.start()
        return carry

    lax.fori_loop(0, 8, last_pass, 0)
    for c in loads(farthest_first, 0, sources):
        c.start()

    def close_pass(step, carry):
        slot = lax.rem(step, 2)
        there = pl.ds(farthest_first(step) * rows, rows)
        for c in loads(farthest_first, step, sources):
            c.wait()

        @pl.when(step < 7)
        def _():
            for c in loads(farthest_first, step + 1, sources):
                c.start()

        @pl.when(step >= 2)
        def _():
            out_copy(farthest_first, step - 2).wait()

        o_buf[slot] = dot(act_s[there, :], wd[...]).astype(LOW)
        out_copy(farthest_first, step).start()
        act = act_s[there, pl.ds(hiddens[2], 4 * CHUNKS[2])]
        g_both = ggu_s[there, pl.ds(columns[2], 8 * CHUNKS[2])]
        add_grads(2, step, x_buf[slot], c_buf[slot], act, g_both)
        return carry

    lax.fori_loop(0, 8, close_pass, 0)
    out_copy(farthest_first, 6).wait()
    out_copy(farthest_first, 7).wait()
    emit(1)
    emit(2)
    f32 = jnp.float32
    x1.wait_recv()
    y2.wait_recv()
    for c in (*finals[:5], finals[7]):
        c.wait()
    mid[:half] = held[0, :half].astype(f32) + one[2].astype(f32) + two[0].astype(f32)
    y1.wait_recv()
    x2.wait_recv()
    mid[half:] = held[0, half:].astype(f32) + one[3].astype(f32) + two[1].astype(f32)
    gh_copy = pltpu.make_async_copy(mid, gh_out, done_sem.at[7])
    gh_copy.start()
    for g in sum_lines:
        g.wait()
    gh_copy.wait()
    for c in (b_y, b_own, x0, y0, x1, y1, y2, x2):
        c.wait_send()
    for g in (tokens, out_w, cots, z_gain, z_attn, z_out, *z_up, *z_down):
        g.sent()


def layer_front(tokens, cot, weights, gain_rows, lengths, length, wide, qk):
    rows, width = tokens.shape
    streams = lengths.shape[0]
    hidden = 4 * sum(CHUNKS)
    largest = 4 * max(CHUNKS)
    shape = jax.ShapeDtypeStruct
    f32 = jnp.float32
    anywhere = pl.BlockSpec(memory_space=pl.ANY)
    plane = shape((8, rows, width), LOW)
    narrow = shape((streams, length, qk), LOW)
    broad = shape((streams, length, wide), LOW)
    attn_shape = (width, wide + 128)
    out_shape = [
        plane,
        plane,
        plane,
        shape((8, width, width // 8), LOW),
        shape((streams, length, width), LOW),
        narrow,
        narrow,
        broad,
        broad,
        shape((rows, width), LOW),
        shape((rows, width), f32),
        shape(attn_shape, LOW),
        shape((gain_rows.shape[0], width), LOW),
        plane,
        shape((rows, width), f32),
        shape((2, width, 4 * CHUNKS[0]), LOW),
        shape((4 * CHUNKS[0], width), LOW),
        shape((width, 2 * hidden - 8 * CHUNKS[0]), LOW),
        shape((hidden - 4 * CHUNKS[0], width), LOW),
        shape((4, 2, width // 4, 4 * CHUNKS[0]), LOW),
        shape((4, CHUNKS[0], width), LOW),
    ]
    dma = pltpu.SemaphoreType.DMA
    vmem = pltpu.VMEM
    return pl.pallas_call(
        layer_kernel,
        out_shape=out_shape,
        in_specs=[anywhere] * 10 + [pl.BlockSpec(memory_space=pltpu.SMEM)],
        out_specs=[anywhere] * 21,
        scratch_shapes=[
            vmem(attn_shape, LOW),
            vmem((width, 2 * hidden), LOW),
            vmem((hidden, width), LOW),
            vmem((gain_rows.shape[0], width), LOW),
            vmem(narrow.shape, LOW),
            vmem(narrow.shape, LOW),
            vmem(broad.shape, LOW),
            vmem(broad.shape, LOW),
            vmem((rows, width), LOW),
            vmem((rows, width), f32),
            vmem((8 * rows, hidden), LOW),
            vmem((8 * rows, 2 * hidden), LOW),
            vmem((width, 4 * largest), f32),
            vmem((2 * largest, width), f32),
            vmem((2, rows, width), LOW),
            vmem((2, rows, width), LOW),
            vmem((2, rows, width), LOW),
            vmem((2, rows, width), LOW),
            vmem((4, rows, width), LOW),
            vmem((4, rows, width), LOW),
            vmem((4, rows // 2, width), LOW),
            vmem((2, rows // 2, width), LOW),
            dma((4, 13)),
            dma((4, 13)),
            dma((9, 5)),
            dma((9, 4)),
            dma((9,)),
            dma((14,)),
            dma((14,)),
            dma((10,)),
            dma((10,)),
            dma((2, 2)),
            dma((2,)),
            dma((2, 2)),
            dma((2,)),
            dma((8,)),
            dma((4,)),
            dma((2, 5)),
            dma((2, 5)),
            dma((2, 2)),
            dma((21,)),
            vmem((2, width // 4, 4 * CHUNKS[0]), LOW),
            vmem((CHUNKS[0], width), LOW),
        ],
        compiler_params=pltpu.CompilerParams(
            collective_id=21, has_side_effects=True, vmem_limit_bytes=63 * MIB
        ),
        cost_estimate=pl.CostEstimate(
            flops=6 * 3 * 8 * rows * width * hidden,
            bytes_accessed=400 * rows * width,
            transcendentals=0,
        ),
        name="layer",
    )(tokens, cot, *weights, gain_rows, lengths)


class LineScatter:
    def __init__(self, block, target, stop, mine, send, recv, local):
        z = lax.axis_index("dp")
        self.z, self.stop, self.mine = z, stop, mine
        self.inner = (z == 1) | (z == 2)
        self.outer = jnp.logical_not(self.inner)

        def copy(k, src, dst, at, to):
            return pltpu.make_async_remote_copy(
                src_ref=src,
                dst_ref=dst,
                send_sem=send.at[k],
                recv_sem=recv.at[at],
                device_id={"dp": to},
                device_id_type=MESH,
            )

        far = jnp.where(z < 2, 3, 0)
        near = jnp.where(z < 2, 1, 2)
        self.first = copy(0, block(far), stop, 4, jnp.where(self.inner, 3 - near, near))
        self.sends = []
        for k, d in enumerate((1, -1)):
            to = z + d
            valid = (to >= 0) & (to < 4)
            there = jnp.clip(to, 0, 3)
            self.sends.append((valid, copy(1 + k, block(there), target.at[z], z, there)))
        other = 3 - near
        self.sends.append((self.outer, copy(3, block(other), target.at[z], z, other)))
        self.own_far = pltpu.make_async_copy(block(far), mine, local.at[0])
        self.joined = copy(4, mine, target.at[z], z, far)
        self.own = pltpu.make_async_copy(block(z), target.at[z], local.at[1])
        self.arrivals = []
        for d in (1, -1, 2, -2):
            owner = z + d
            valid = (owner >= 0) & (owner < 4)
            there = jnp.clip(owner, 0, 3)
            self.arrivals.append((valid, copy(1, block(there), target.at[there], there, there)))

    def start_first(self):
        self.own.start()

        @pl.when(self.outer)
        def _():
            self.first.start()

        @pl.when(self.inner)
        def _():
            self.own_far.start()

    def start(self):
        for valid, c in self.sends:

            @pl.when(valid)
            def _(c=c):
                c.start()

    def join(self):
        @pl.when(self.inner)
        def _():
            self.first.wait_recv()
            self.own_far.wait()
            self.mine[...] = self.mine[...] + self.stop[...]
            self.joined.start()

    def wait(self):
        for valid, c in self.arrivals:

            @pl.when(valid)
            def _(c=c):
                c.wait_recv()

        self.own.wait()
        for valid, c in (*self.sends, (self.outer, self.first), (self.inner, self.joined)):

            @pl.when(valid)
            def _(c=c):
                c.wait_send()


class PlaneScatter:
    def __init__(self, beside, held, got, one, two, send, recv):
        me, sib, xn, yn = partners()
        half = got.shape[1] // 2
        self.half = half
        upper, lower = pl.ds(0, half), pl.ds(half, half)
        copy = functools.partial(remote, send, recv)
        self.held, self.got, self.one, self.two = held, got, one, two
        self.pairs = [copy(i, beside(i), got.at[i], sib) for i in range(4)]
        self.x0 = copy(4, held(2).at[upper], one.at[0], xn)
        self.y0 = copy(5, held(2).at[lower], one.at[1], yn)
        self.x1 = copy(6, held(1).at[upper], one.at[2], xn)
        self.y1 = copy(7, held(3).at[lower], one.at[3], yn)
        self.y2 = copy(8, held(3).at[upper], two.at[0], yn)
        self.x2 = copy(9, held(1).at[lower], two.at[1], xn)

    def start_pair(self, i):
        self.pairs[i].start()

    def start_pairs(self):
        for i in (2, 1, 3, 0):
            self.start_pair(i)

    def add_pair(self, i):
        self.pairs[i].wait_recv()
        block = self.held(i)
        block[...] = block[...] + self.got[i]
        for c in {0: (), 1: (self.x1,), 2: (self.x0, self.y0), 3: (self.y1,)}[i]:
            c.start()

    def add_pairs(self):
        for i in (2, 1, 3, 0):
            self.add_pair(i)

    def second(self):
        half = self.half
        self.y0.wait_recv()
        block = self.held(1)
        block[half:, :] = block[half:, :] + self.one[1]
        self.x2.start()
        self.x0.wait_recv()
        block = self.held(3)
        block[:half, :] = block[:half, :] + self.one[0]
        self.y2.start()

    def upper_sum(self):
        f32 = jnp.float32
        self.x1.wait_recv()
        self.y2.wait_recv()
        own = self.held(0)[: self.half, :].astype(f32)
        return own + self.one[2].astype(f32) + self.two[0].astype(f32)

    def lower_sum(self):
        f32 = jnp.float32
        self.y1.wait_recv()
        self.x2.wait_recv()
        own = self.held(0)[self.half :, :].astype(f32)
        return own + self.one[3].astype(f32) + self.two[1].astype(f32)

    def sent(self):
        for c in (*self.pairs, self.x0, self.y0, self.x1, self.y1, self.y2, self.x2):
            c.wait_send()


def chips():
    me, unused, xn, yn = partners()
    return me, xn, xn + yn - me, yn


def turn_kernel(
    gh_ref,
    mid_ref,
    c_ref,
    gain_ref,
    wo_all,
    part_ref,
    tok_ref,
    q_ref,
    k_ref,
    v_ref,
    att_ref,
    lengths_ref,
    h1_ref,
    output_ref,
    g_mid_out,
    g_out,
    gain_out,
    attn_ref,
    g_mid,
    work,
    g_low,
    g_att,
    g_heads,
    g_s,
    w_buf,
    go_part,
    held_o,
    got_g,
    one_g,
    two_g,
    got_o,
    one_o,
    two_o,
    gk_sum,
    gv_sum,
    h_buf,
    sums,
    esend,
    erecv,
    ssend,
    srecv,
    load_sem,
    w_sem,
    self_sem,
    done_sem,
    h_sem,
):
    me, sib, xn, yn = partners()
    flip = sib - me
    rows, width = g_low.shape
    span = rows // 2
    wide, qk = v_ref.shape[2], q_ref.shape[2]
    half = rows // 2
    greet([lax.rem(me + i, 8) for i in range(1, 8)])
    owners = chips()

    loads = [
        pltpu.make_async_copy(source, target, load_sem.at[i])
        for i, (source, target) in enumerate(
            ((gh_ref, g_mid), (mid_ref, work), (c_ref, g_low))
        )
    ]
    held_loads = [
        pltpu.make_async_copy(part_ref.at[owners[i]], held_o.at[i], load_sem.at[3 + i])
        for i in range(4)
    ]

    def w_load(step):
        slot = lax.rem(step, 2)
        return pltpu.make_async_copy(wo_all.at[step], w_buf.at[slot], w_sem.at[slot])

    for c in loads:
        c.start()
    w_load(0).start()
    outs = PlaneScatter(
        lambda i: part_ref.at[owners[i] + flip],
        lambda i: held_o.at[i],
        got_o,
        one_o,
        two_o,
        ssend.at[0],
        srecv.at[0],
    )
    weights = PlaneScatter(
        lambda i: go_part.at[owners[i] + flip],
        lambda i: go_part.at[owners[i]],
        got_g,
        one_g,
        two_g,
        ssend.at[1],
        srecv.at[1],
    )
    outs.start_pairs()
    for c in held_loads:
        c.start()
    for c in loads:
        c.wait()

    f32 = jnp.float32
    mid = work[...]
    inverse = norm_scale(mid)
    normed = mid * inverse
    grad = g_mid[...]
    gain_out[...] = jnp.broadcast_to(
        jnp.sum(grad * normed, axis=0, keepdims=True), gain_out.shape
    )
    gain = gain_ref[1:2, :].astype(f32)
    grad_mid = g_low[...].astype(f32) + norm_backward(grad, normed, inverse, gain)
    g_mid[...] = grad_mid
    g_low[...] = grad_mid.astype(LOW)
    done = [pltpu.make_async_copy(g_mid, g_mid_out, done_sem.at[0])]
    done[0].start()

    def back_out(step, carry):
        slot = lax.rem(step, 2)
        w_load(step).wait()

        @pl.when(step < 7)
        def _():
            w_load(step + 1).start()

        there = pl.ds(pl.multiple_of(step * wide, 128), wide)
        term = contract(g_low[:, there], w_buf[slot], 1, 1)

        @pl.when(step == 0)
        def _():
            work[...] = term

        @pl.when(step > 0)
        def _():
            work[...] += term

        return carry

    lax.fori_loop(0, 8, back_out, 0)
    g_att[...] = work[...].astype(LOW)
    mid_load = pltpu.make_async_copy(mid_ref, work, load_sem.at[1])
    mid_load.start()
    swaps = []
    here = pl.ds(me * span, span)
    for i in range(1, 8):
        other = lax.rem(me + i, 8)
        lanes = pl.ds(pl.multiple_of(other * wide, 128), wide)
        for m in range(2):
            swaps.append(
                remote(
                    esend,
                    erecv,
                    2 * (i - 1) + m,
                    g_att.at[pl.ds(m * span, span), lanes],
                    g_heads.at[m, here],
                    other,
                )
            )
            swaps[-1].start()
    kept = [
        pltpu.make_async_copy(
            g_att.at[pl.ds(m * span, span), pl.ds(pl.multiple_of(me * wide, 128), wide)],
            g_heads.at[m, here],
            self_sem.at[m],
        )
        for m in range(2)
    ]
    for c in kept:
        c.start()

    own = width // 32
    for z in range(4):
        lanes = slice(z * 8 * own, (z + 1) * 8 * own)
        block = contract(tok_ref[:, lanes], g_low[...], 0, 0).astype(LOW)
        for s in range(8):
            go_part[s, z * own : (z + 1) * own, :] = block[s * own : (s + 1) * own]
    weights.start_pairs()
    for c in kept:
        c.wait()
    for c in swaps:
        c.wait_recv()
    weights.add_pairs()

    length = v_ref.shape[1]
    block = 256
    streams = v_ref.shape[0]
    pieces = length // rows

    def h_load(step):
        slot = lax.rem(step, 2)
        return pltpu.make_async_copy(
            h1_ref.at[step // pieces, pl.ds(lax.rem(step, pieces) * rows, rows)],
            h_buf.at[slot],
            h_sem.at[slot],
        )

    h_load(0).start()

    def back_stream(m, carry):
        gk_sum[...] = jnp.zeros_like(gk_sum)
        gv_sum[...] = jnp.zeros_like(gv_sum)
        for i in range(length // block):
            rows_i = slice(i * block, (i + 1) * block)
            seen = (i + 1) * block
            query, key = q_ref[m, rows_i, :], k_ref[m, :seen, :]
            g_query = jnp.zeros(query.shape, f32)
            first = first_of(lengths_ref, m, i * block, block)
            for head in range(wide // HEAD_V):
                lanes = slice(head * HEAD_V, (head + 1) * HEAD_V)
                scores, mask, weight = weights_of(query, key, head, first, i * block)
                denom = jnp.sum(weight, axis=1, keepdims=True)
                a = (g_heads[m, rows_i, lanes].astype(f32) / denom).astype(LOW)
                b = -jnp.sum(
                    a.astype(f32) * att_ref[m, rows_i, lanes].astype(f32), axis=1, keepdims=True
                )
                g_weight = contract(a, v_ref[m, :seen, lanes], 1, 1) + b
                slope = 1.0 / math.sqrt(QK_DIM) + scores * (1.0 / QK_DIM)
                g_scores = jnp.where(mask, g_weight * slope, 0.0).astype(LOW)
                g_query += head_lanes(dot(g_scores, key), head)
                gk_sum[:seen, :] += contract(g_scores, head_lanes(query, head), 0, 0)
                gv_sum[:seen, lanes] += contract(weight.astype(LOW), a, 0, 0)
            g_s[m, rows_i, wide : wide + qk] = g_query.astype(LOW)
        g_s[m, :, :wide] = gv_sum[...].astype(LOW)
        g_s[m, :, wide + qk : wide + 2 * qk] = gk_sum[...].astype(LOW)
        g_s[m, :, wide + 2 * qk :] = jnp.zeros((length, g_s.shape[2] - wide - 2 * qk), LOW)

        @pl.when(m == 0)
        def _():
            for c in held_loads:
                c.wait()
            outs.add_pairs()

        return carry

    lax.fori_loop(0, 2, back_stream, 0)
    weights.second()
    done.append(pltpu.make_async_copy(g_s, g_out, done_sem.at[1]))
    done[1].start()
    outs.second()

    def add_grads(step, carry):
        slot = lax.rem(step, 2)
        h_load(step).wait()

        @pl.when(step < streams * pieces - 1)
        def _():
            h_load(step + 1).start()

        there = pl.ds(pl.multiple_of(lax.rem(step, pieces) * rows, rows), rows)
        term = contract(h_buf[slot], g_s[step // pieces, there, :], 0, 0)

        @pl.when(step == 0)
        def _():
            sums[...] = term

        @pl.when(step > 0)
        def _():
            sums[...] += term

        return carry

    lax.fori_loop(0, streams * pieces, add_grads, 0)
    narrow = sums.shape[1]
    attn_ref[:, :narrow] = sums[...].astype(LOW)
    mid_load.wait()
    for part, total in enumerate((weights.upper_sum(), weights.lower_sum())):
        total = total.astype(LOW)
        for z in range(2):
            for i in range(8):
                start = ((2 * part + z) * 8 + i) * own
                attn_ref[start : start + own, narrow:] = total[
                    z * own : (z + 1) * own, i * wide : (i + 1) * wide
                ]
    output_ref[:half] = (work[:half] + outs.upper_sum()).astype(LOW)
    output_ref[half:] = (work[half:] + outs.lower_sum()).astype(LOW)
    for c in done:
        c.wait()
    for c in swaps:
        c.wait_send()
    weights.sent()
    outs.sent()


def layer_turn(gh, mid, cot, gains, wo_all, part, tok, query, key, value, att, lengths, h1, columns):
    rows, width = mid.shape
    streams, length, wide = value.shape
    qk = query.shape[2]
    shape = jax.ShapeDtypeStruct
    f32 = jnp.float32
    anywhere = pl.BlockSpec(memory_space=pl.ANY)
    in_vmem = pl.BlockSpec(memory_space=pltpu.VMEM)
    dma = pltpu.SemaphoreType.DMA
    vmem = pltpu.VMEM
    arriving = [
        vmem((4, rows, width), LOW),
        vmem((4, rows // 2, width), LOW),
        vmem((2, rows // 2, width), LOW),
    ]
    return pl.pallas_call(
        turn_kernel,
        out_shape=[
            shape((rows, width), LOW),
            shape((rows, width), f32),
            shape((streams, length, columns), LOW),
            shape((8, width), f32),
            shape((width, columns + wide), LOW),
        ],
        in_specs=[anywhere] * 3
        + [in_vmem]
        + [anywhere] * 2
        + [in_vmem] * 5
        + [pl.BlockSpec(memory_space=pltpu.SMEM), anywhere],
        out_specs=[in_vmem, anywhere, anywhere, in_vmem, in_vmem],
        scratch_shapes=[
            vmem((rows, width), f32),
            vmem((rows, width), f32),
            vmem((rows, width), LOW),
            vmem((rows, width), LOW),
            vmem((streams, length, wide), LOW),
            vmem((streams, length, columns), LOW),
            vmem((2, width, wide), LOW),
            vmem((8, rows, width), LOW),
            vmem((4, rows, width), LOW),
            *arriving,
            *arriving,
            vmem((length, qk), f32),
            vmem((length, wide), f32),
            vmem((2, rows, width), LOW),
            vmem((width, columns), f32),
            dma((14,)),
            dma((14,)),
            dma((2, 10)),
            dma((2, 10)),
            dma((7,)),
            dma((2,)),
            dma((2,)),
            dma((2,)),
            dma((2,)),
        ],
        compiler_params=pltpu.CompilerParams(
            collective_id=22, has_side_effects=True, vmem_limit_bytes=63 * MIB
        ),
        cost_estimate=moved(16 * rows * width),
        name="turn",
    )(gh, mid, cot, gains, wo_all, part, tok, query, key, value, att, lengths, h1)


def close_kernel(
    g_ref,
    wa_ref,
    g_mid_ref,
    x_ref,
    gain_ref,
    sum_ref,
    blocks_ref,
    rest_ref,
    grad_ref,
    gains_ref,
    first_got,
    rest_got,
    beside,
    held,
    got,
    one,
    two,
    gain_rows,
    gain_line,
    gain_columns,
    gain_plane,
    blocks,
    first_sum,
    ssend,
    srecv,
    zsend,
    zrecv,
    esend,
    erecv,
    self_sem,
    fsend,
    frecv,
    f_sem,
):
    me, sib, xn, yn = partners()
    z = lax.axis_index("dp")
    rows, width = x_ref.shape
    span = rows // 2
    half = rows // 2
    f32 = jnp.float32
    barrier = pltpu.get_barrier_semaphore()
    for i in range(1, 8):
        pl.semaphore_signal(
            barrier, inc=1, device_id={"seq": lax.rem(me + i, 8)}, device_id_type=MESH
        )
    for i in range(1, 4):
        pl.semaphore_signal(
            barrier, inc=1, device_id={"dp": lax.rem(z + i, 4)}, device_id_type=MESH
        )
    pl.semaphore_wait(barrier, 10)
    load = pltpu.make_async_copy(blocks_ref, blocks, f_sem.at[0])
    load.start()
    keep = first_got.shape[1]

    def exchange(item, source, target):
        mine = pltpu.make_async_copy(
            source.at[pl.ds(me * keep, keep)], target.at[me], f_sem.at[1 + item]
        )
        mine.start()
        copies = []
        for i in range(1, 8):
            other = lax.rem(me + i, 8)
            copies.append(
                remote(
                    fsend,
                    frecv,
                    7 * item + i - 1,
                    source.at[pl.ds(other * keep, keep)],
                    target.at[me],
                    other,
                )
            )
            copies[-1].start()
        return mine, copies

    scatter = PlaneScatter(
        lambda i: beside.at[i], lambda i: held.at[i], got, one, two, ssend, srecv
    )
    def part_of(owner):
        there = pl.ds(pl.multiple_of(owner * span, span), span)
        grads = jnp.concatenate([g_ref[0, there, :], g_ref[1, there, :]], axis=0)
        return contract(grads, wa_ref[...], 1, 1).astype(LOW)

    owners = chips()
    for i in (2, 1, 3, 0):
        beside[i] = part_of(owners[i] + sib - me)
        scatter.start_pair(i)
        held[i] = part_of(owners[i])
        scatter.add_pair(i)

    load.wait()
    for second in range(2):
        total = jnp.zeros(blocks.shape[2:], f32)
        for owner in range(4):
            came = jnp.abs(z - owner) < 3
            total = total + jnp.where(came, blocks[owner, second].astype(f32), 0.0)
        lanes_here = total.shape[1]
        first_sum[:, second * lanes_here : (second + 1) * lanes_here] = total.astype(LOW)
    scatter.second()
    moves = [exchange(1, rest_ref, rest_got), exchange(0, first_sum, first_got)]

    x = x_ref[...].astype(f32)
    inverse = norm_scale(x)
    normed = x * inverse
    gain = gain_ref[0:1, :].astype(f32)

    def finish(start, g_h):
        part = slice(start, start + half)
        grad_ref[part] = g_mid_ref[part] + norm_backward(g_h, normed[part], inverse[part], gain)
        return jnp.sum(g_h * normed[part], axis=0, keepdims=True)

    gain_sum = finish(0, scatter.upper_sum()) + finish(half, scatter.lower_sum())

    both = jnp.concatenate([gain_sum, sum_ref[0:1, :], jnp.zeros((14, width), f32)], axis=0)
    gain_rows[...] = both.astype(LOW)
    depth = width // 4

    def lanes(owner):
        return pl.ds(pl.multiple_of(owner * depth, 128), depth)

    def over_line(k, to, owner):
        return pltpu.make_async_remote_copy(
            src_ref=gain_rows.at[:, lanes(to)],
            dst_ref=gain_line.at[owner],
            send_sem=zsend.at[k],
            recv_sem=zrecv.at[owner],
            device_id={"dp": to},
            device_id_type=MESH,
        )

    others = [lax.rem(z + o, 4) for o in (1, 2, 3)]
    sends = [over_line(k, other, z) for k, other in enumerate(others)]
    own = pltpu.make_async_copy(gain_rows.at[:, lanes(z)], gain_line.at[z], self_sem.at[0])
    own.start()
    for c in sends:
        c.start()
    own.wait()
    for other in others:
        over_line(0, other, other).wait_recv()
    total = gain_line[0].astype(f32)
    for k in range(1, 4):
        total = total + gain_line[k].astype(f32)
    entry = lax.broadcasted_iota(jnp.int32, (16, 128), 0)
    lane = lax.broadcasted_iota(jnp.int32, (16, 128), 1)
    pick = jnp.where(lane == entry, 1.0, 0.0).astype(LOW)
    gain_columns[...] = contract(total.astype(LOW), pick, 0, 0).astype(LOW)
    count = depth // 8
    own = pltpu.make_async_copy(
        gain_columns.at[pl.ds(me * count, count)], gain_plane.at[me], self_sem.at[1]
    )
    own.start()
    swaps = []
    for i in range(1, 8):
        other = lax.rem(me + i, 8)
        swaps.append(
            remote(
                esend,
                erecv,
                i - 1,
                gain_columns.at[pl.ds(other * count, count)],
                gain_plane.at[me],
                other,
            )
        )
        swaps[-1].start()
    own.wait()
    for c in swaps:
        c.wait_recv()
    total = gain_plane[0].astype(f32)
    for k in range(1, 8):
        total = total + gain_plane[k].astype(f32)
    gains_ref[...] = total
    scatter.sent()
    for c in (*sends, *swaps):
        c.wait_send()
    for mine, copies in moves:
        mine.wait()
        for c in copies:
            c.wait()


def layer_close(g_all, wa, g_mid, tokens, gains, gain_sum, blocks, rest):
    rows, width = tokens.shape
    shape = jax.ShapeDtypeStruct
    in_vmem = pl.BlockSpec(memory_space=pltpu.VMEM)
    anywhere = pl.BlockSpec(memory_space=pl.ANY)
    dma = pltpu.SemaphoreType.DMA
    vmem = pltpu.VMEM
    return pl.pallas_call(
        close_kernel,
        out_shape=[
            shape((rows, width), jnp.float32),
            shape((width // 32, 128), jnp.float32),
            shape((8, width // 32, 8 * CHUNKS[0]), LOW),
            shape((8, width // 32, rest.shape[1]), LOW),
        ],
        in_specs=[in_vmem] * 6 + [anywhere] * 2,
        out_specs=[in_vmem, in_vmem, anywhere, anywhere],
        scratch_shapes=[
            vmem((4, rows, width), LOW),
            vmem((4, rows, width), LOW),
            vmem((4, rows, width), LOW),
            vmem((4, rows // 2, width), LOW),
            vmem((2, rows // 2, width), LOW),
            vmem((16, width), LOW),
            vmem((4, 16, width // 4), LOW),
            vmem((width // 4, 128), LOW),
            vmem((8, width // 32, 128), LOW),
            vmem(blocks.shape, LOW),
            vmem((width // 4, 8 * CHUNKS[0]), LOW),
            dma((10,)),
            dma((10,)),
            dma((3,)),
            dma((4,)),
            dma((7,)),
            dma((7,)),
            dma((2,)),
            dma((14,)),
            dma((14,)),
            dma((3,)),
        ],
        compiler_params=pltpu.CompilerParams(
            collective_id=23, has_side_effects=True, vmem_limit_bytes=56 * MIB
        ),
        cost_estimate=moved(16 * rows * width),
        name="close",
    )(g_all, wa, g_mid, tokens, gains, gain_sum, blocks, rest)


def place_kernel(
    first_in,
    rest_in,
    blocks_in,
    down_in,
    out_ref,
    grad_ref,
    gate_out,
    up_out,
    down_out,
    out_copy,
    grad_copy,
    first_ref,
    rest_ref,
    blocks_ref,
    down_ref,
    sems,
):
    copies = [
        pltpu.make_async_copy(source, target, sems.at[i])
        for i, (source, target) in enumerate(
            (
                (first_in, first_ref),
                (rest_in, rest_ref),
                (blocks_in, blocks_ref),
                (down_in, down_ref),
                (out_ref, out_copy),
                (grad_ref, grad_copy),
            )
        )
    ]
    for c in copies:
        c.start()
    for c in copies[:2]:
        c.wait()
    f32 = jnp.float32
    z = lax.axis_index("dp")
    share = sum(CHUNKS)
    for second, target in enumerate((gate_out, up_out)):
        for owner in range(8):
            for group in range(4):
                at = group * 8 * share + owner * share
                start = 0
                for k, count in enumerate(CHUNKS):
                    source = first_ref if k == 0 else rest_ref
                    begin = start + (4 * second + group) * count
                    target[:, at : at + count] = source[owner, :, begin : begin + count].astype(f32)
                    at += count
                    start += 8 * count if k else 0
    for c in copies[2:4]:
        c.wait()
    total = jnp.zeros(blocks_ref.shape[1:], f32)
    for owner in range(4):
        came = jnp.abs(z - owner) < 3
        total = total + jnp.where(came, blocks_ref[owner].astype(f32), 0.0)
    down_out[: CHUNKS[0], :] = total
    down_out[CHUNKS[0] :, :] = down_ref[...].astype(f32)
    for c in copies[4:]:
        c.wait()


def place_rows(first, rest, blocks, down, output, input_grad):
    own, width = first.shape[1], blocks.shape[2]
    shape = jax.ShapeDtypeStruct
    anywhere = pl.BlockSpec(memory_space=pl.ANY)
    in_vmem = pl.BlockSpec(memory_space=pltpu.VMEM)
    wide = 32 * sum(CHUNKS)
    return pl.pallas_call(
        place_kernel,
        out_shape=[
            shape((own, wide), jnp.float32),
            shape((own, wide), jnp.float32),
            shape((sum(CHUNKS), width), jnp.float32),
            shape(output.shape, output.dtype),
            shape(input_grad.shape, input_grad.dtype),
        ],
        in_specs=[anywhere] * 6,
        out_specs=[in_vmem] * 5,
        scratch_shapes=[
            pltpu.VMEM(first.shape, LOW),
            pltpu.VMEM(rest.shape, LOW),
            pltpu.VMEM(blocks.shape, LOW),
            pltpu.VMEM(down.shape, LOW),
            pltpu.SemaphoreType.DMA((6,)),
        ],
        compiler_params=pltpu.CompilerParams(vmem_limit_bytes=63 * MIB),
        name="place",
    )(first, rest, blocks, down, output, input_grad)


def place_attn_kernel(got_ref, out_ref, query_out, key_out, value_out, grad_out):
    f32 = jnp.float32
    wide = value_out.shape[1] // 8
    qk = query_out.shape[1] // 8
    own = out_ref.shape[0] // 8
    for owner in range(8):
        value_out[:, owner * wide : (owner + 1) * wide] = got_ref[owner, :, :wide].astype(f32)
        here = slice(owner * qk, (owner + 1) * qk)
        query_out[:, here] = got_ref[owner, :, wide : wide + qk].astype(f32)
        key_out[:, here] = got_ref[owner, :, wide + qk : wide + 2 * qk].astype(f32)
        block = out_ref[owner * own : (owner + 1) * own, out_ref.shape[1] - wide :]
        grad_out[:, owner * wide : (owner + 1) * wide] = block.astype(f32)


def place_attn(got, summed, wide, qk):
    own = got.shape[1]
    shape = jax.ShapeDtypeStruct
    in_vmem = pl.BlockSpec(memory_space=pltpu.VMEM)
    return pl.pallas_call(
        place_attn_kernel,
        out_shape=[
            shape((own, 8 * qk), jnp.float32),
            shape((own, 8 * qk), jnp.float32),
            shape((own, 8 * wide), jnp.float32),
            shape((own, 8 * wide), jnp.float32),
        ],
        in_specs=[in_vmem] * 2,
        out_specs=[in_vmem] * 4,
        name="place_attn",
    )(got, summed)


def ffn_lax(h_two, cot_all, gate_full, up_full, down_full):
    pieces, rows, width = cot_all.shape
    h_two_all = gather_plane(h_two, 5).reshape(-1, width)
    cot_all = cot_all.reshape(-1, width)
    gate = dot(h_two_all, gate_full)
    up = dot(h_two_all, up_full)
    g_act = contract(cot_all, down_full, 1, 1)
    sigmoid = jax.nn.sigmoid(gate)
    silu = gate * sigmoid
    act = (silu * up).astype(LOW)
    g_gate = (g_act * up * sigmoid * (1.0 + gate * (1.0 - sigmoid))).astype(LOW)
    g_up = (g_act * silu).astype(LOW)
    part = (contract(g_gate, gate_full, 1, 1) + contract(g_up, up_full, 1, 1)).astype(LOW)
    return (
        dot(act, down_full).astype(LOW).reshape(pieces, rows, width),
        scatter_plane(part.reshape(pieces, rows, width), 7),
        contract(h_two_all, g_gate, 0, 0).astype(LOW),
        contract(h_two_all, g_up, 0, 0).astype(LOW),
        contract(act, cot_all, 0, 0).astype(LOW),
    )


def norm_scale(rows):
    return lax.rsqrt(jnp.mean(rows * rows, axis=-1, keepdims=True) + epsilon)


def norm_backward(grad, normed, inverse, gain):
    scaled = grad * gain
    return inverse * (scaled - normed * jnp.mean(scaled * normed, axis=-1, keepdims=True))


def local(
    tokens,
    doc_lengths,
    w_query,
    w_key,
    w_value,
    w_out,
    w_gate,
    w_up,
    w_down,
    gain_attn,
    gain_mlp,
    cotangent,
):
    micro, span = tokens.shape[1:3]
    pieces, groups = lax.axis_size("seq"), lax.axis_size("dp")
    place = lax.axis_index("seq")
    length = pieces * span
    heads = max(1, HEADS // pieces)
    sharers = max(1, pieces // HEADS)
    streams = micro // sharers
    first_head = place // sharers * heads
    first_stream = place % sharers * streams
    qk, wide = heads * QK_DIM, heads * HEAD_V
    hidden = FF // pieces

    out_width = D // pieces
    rows_dp = w_gate.shape[0]
    share = hidden // groups
    block = FF // groups
    mine = micro * span
    fused = pieces == 8 and groups == 4 and micro == 2 and span == 128
    chunks = CHUNKS if fused else (share,)

    def hidden_columns(w):
        parts = [
            lax.dynamic_slice_in_dim(w, z * block + place * share, share, 1) for z in range(groups)
        ]
        edges = [sum(chunks[:k]) for k in range(len(chunks) + 1)]
        return [
            [part[:, edges[k] : edges[k + 1]] for part in parts] for k in range(len(chunks))
        ]

    x_own = tokens[0].reshape(mine, D)
    flat = x_own.astype(jnp.float32)
    cot = cotangent[0].reshape(mine, D)

    def to_tokens(by_head):
        sent = by_head.reshape(streams, pieces, span, wide).transpose(1, 0, 2, 3)
        got = exchange_plane(sent, 3).reshape(pieces // sharers, micro, span, wide)
        return got.transpose(1, 2, 0, 3).reshape(mine, HEADS * HEAD_V)

    def to_heads(by_token):
        sent = by_token.reshape(micro, span, pieces // sharers, wide).transpose(2, 0, 1, 3)
        got = exchange_plane(sent.reshape(pieces, streams, span, wide), 4)
        return got.transpose(1, 0, 2, 3).reshape(streams, length, wide)

    if fused:
        gain_rows = jnp.concatenate(
            [gain_attn[None], gain_mlp[None], jnp.zeros((14, rows_dp), LOW)], axis=0
        )
        weights = (w_query, w_key, w_value, w_out, w_gate, w_up, w_down)
        front = layer_front(x_own, cot, weights, gain_rows, doc_lengths[0], length, wide, qk)
        out_full, h_all, query, key, value, att_heads, attended, mid = front[3:11]
        attn_full, gain_rows_all, out_part, g_h_two = front[11:15]
        d_ffn, d_down, ffn_blocks, down_blocks = front[17:]
    else:
        gate_parts, up_parts = hidden_columns(w_gate), hidden_columns(w_up)
        ffn_slice = jnp.concatenate(
            [part for k in range(len(chunks)) for part in gate_parts[k] + up_parts[k]], axis=1
        )
        attn_parts = [
            lax.dynamic_slice_in_dim(w_value, first_head * HEAD_V, wide, 1),
            lax.dynamic_slice_in_dim(w_query, first_head * QK_DIM, qk, 1),
            lax.dynamic_slice_in_dim(w_key, first_head * QK_DIM, qk, 1),
        ]

        lengths = lax.dynamic_slice_in_dim(doc_lengths[0], first_stream, streams, 0)
        starts = jnp.cumsum(lengths, axis=1) - lengths
        position = jnp.arange(length, dtype=jnp.int32)
        begun = starts[:, None, :] <= position[None, :, None]
        first = jnp.max(jnp.where(begun, starts[:, None, :], 0), axis=2)[..., None]

        def gather_dp(w):
            return lax.all_gather(w, "dp", axis=0, tiled=True)

        attn_got = gather_dp(
            jnp.concatenate(
                attn_parts
                + [
                    lax.dynamic_slice_in_dim(w_out, place * out_width, out_width, 1),
                    gain_attn[:, None],
                    gain_mlp[:, None],
                ],
                axis=1,
            )
        )
        ffn_full = gather_dp(ffn_slice)
        down_full = gather_dp(lax.dynamic_slice_in_dim(w_down, place * share, share, 0))
        value_full = attn_got[:, :wide]
        query_full = attn_got[:, wide : wide + qk]
        key_full = attn_got[:, wide + qk : wide + 2 * qk]
        out_full = gather_plane(attn_got[:, wide + 2 * qk : wide + 2 * qk + out_width], 2)
        gains = attn_got[:, wide + 2 * qk + out_width :].astype(jnp.float32)
        gain_one, gain_two = gains[:, 0], gains[:, 1]
        x_all = gather_plane(x_own, 1).reshape(pieces, micro, span, D).transpose(1, 0, 2, 3)
        x_all = lax.dynamic_slice_in_dim(x_all, first_stream, streams, 0).astype(jnp.float32)
        h_flat = (x_all * norm_scale(x_all) * gain_one).astype(LOW).reshape(streams * length, D)
        value = dot(h_flat, value_full).astype(LOW).reshape(streams, length, wide)
        query = dot(h_flat, query_full).astype(LOW).reshape(streams, length, qk)
        key = dot(h_flat, key_full).astype(LOW).reshape(streams, length, qk)
        att_heads = attend(query, key, value, first, heads)
        attended = to_tokens(att_heads)
        mid = flat + jnp.einsum(
            "tk,skn->tsn", attended, out_full, preferred_element_type=jnp.float32
        ).reshape(mine, D)
        h_two = (mid * norm_scale(mid) * gain_two).astype(LOW)
        out_part, g_h_two, d_gate, d_up, d_down = ffn_lax(
            h_two, gather_plane(cot, 6), ffn_full[:, :hidden], ffn_full[:, hidden:], down_full
        )
        d_ffn = jnp.concatenate([d_gate, d_up], axis=1)

    def scatter_dp(part):
        return lax.psum_scatter(part, "dp", scatter_dimension=0, tiled=True)

    own = rows_dp // pieces
    sum_ffn, sum_down = scatter_dp(d_ffn), scatter_dp(d_down)

    if fused:
        output, g_mid, g_all, gain_sum, grad_attn = layer_turn(
            g_h_two, mid, cot, gain_rows_all, out_full, out_part, attended, query, key, value,
            att_heads, doc_lengths[0], h_all, attn_full.shape[1],
        )
        grad_attn, sum_ffn, sum_down = lax.optimization_barrier((grad_attn, sum_ffn, sum_down))
        grad_attn = scatter_dp(grad_attn)
        input_grad, gain_columns, first_got, rest_got = layer_close(
            g_all, attn_full, g_mid, x_own, gain_rows_all, gain_sum, ffn_blocks, sum_ffn
        )
        grad_attn, gain_columns = lax.optimization_barrier((grad_attn, gain_columns))
        kept = attn_full.shape[1]
        attn_got = exchange_plane(grad_attn.reshape(pieces, own, -1), 12, kept)
        attn_got, first_got = lax.optimization_barrier((attn_got, first_got))
        grad_gate, grad_up, grad_down, output, input_grad = place_rows(
            first_got, rest_got, down_blocks, sum_down, output, input_grad
        )
        grad_query, grad_key, grad_value, grad_out = place_attn(attn_got, grad_attn, wide, qk)
        return (
            output.reshape(tokens.shape),
            input_grad.reshape(tokens.shape),
            grad_query,
            grad_key,
            grad_value,
            grad_out,
            grad_gate,
            grad_up,
            grad_down,
            gain_columns[:, 0],
            gain_columns[:, 1],
        )

    inverse_two = norm_scale(mid)
    plain_two = mid * inverse_two
    output = (mid + scatter_plane(out_part, 8)).astype(LOW)
    g_mid = cot.astype(jnp.float32) + norm_backward(g_h_two, plain_two, inverse_two, gain_two)
    g_mid_low = g_mid.astype(LOW)
    g_att = jnp.einsum(
        "tsn,skn->tk",
        g_mid_low.reshape(mine, pieces, out_width),
        out_full,
        preferred_element_type=jnp.float32,
    )
    g_att = to_heads(g_att.astype(LOW))
    g_query, g_key, g_value = attend_back(query, key, value, first, att_heads, g_att, heads)
    g_value = g_value.reshape(streams * length, wide)
    g_query = g_query.reshape(streams * length, qk)
    g_key = g_key.reshape(streams * length, qk)
    g_h_one_part = (
        contract(g_value, value_full, 1, 1)
        + contract(g_query, query_full, 1, 1)
        + contract(g_key, key_full, 1, 1)
    ).astype(LOW)
    g_h_one_part = g_h_one_part.reshape(streams, pieces, span, D).transpose(1, 0, 2, 3)
    if sharers > 1:
        padded = jnp.zeros((pieces, micro, span, D), LOW)
        g_h_one_part = lax.dynamic_update_slice_in_dim(padded, g_h_one_part, first_stream, 1)
    g_h_one = scatter_plane(g_h_one_part.reshape(pieces, mine, D), 9)
    inverse_one = norm_scale(flat)
    plain_one = flat * inverse_one
    input_grad = g_mid + norm_backward(g_h_one, plain_one, inverse_one, gain_one)
    grad_out = contract(attended, g_mid_low, 0, 0).astype(LOW)
    grad_out = grad_out.reshape(groups, pieces, own, D).transpose(1, 0, 2, 3)
    grad_out = scatter_plane(grad_out.reshape(pieces, groups * own, D), 10).astype(LOW)
    grad_out = scatter_dp(grad_out)
    grad_attn = jnp.concatenate(
        [
            contract(h_flat, g_value, 0, 0).astype(LOW),
            contract(h_flat, g_query, 0, 0).astype(LOW),
            contract(h_flat, g_key, 0, 0).astype(LOW),
            jnp.sum(g_h_one * plain_one, axis=0).astype(LOW)[:, None],
            jnp.sum(g_h_two * plain_two, axis=0).astype(LOW)[:, None],
        ],
        axis=1,
    )

    grad_attn = scatter_dp(grad_attn)
    ffn_got = exchange_plane(sum_ffn.reshape(pieces, own, 2 * hidden), 11).astype(jnp.float32)
    attn_got = exchange_plane(grad_attn.reshape(pieces, own, -1), 12).astype(jnp.float32)
    grad_gains = jnp.sum(attn_got[:, :, wide + 2 * qk :], axis=0)
    attn_got = jnp.sum(attn_got.reshape(pieces // sharers, sharers, own, -1), axis=1)

    def by_hidden(block):
        return block.reshape(pieces, own, groups, share).transpose(1, 2, 0, 3).reshape(own, FF)

    def by_rows(block):
        return block.transpose(1, 0, 2).reshape(own, -1)

    return (
        output.reshape(tokens.shape),
        input_grad.reshape(tokens.shape),
        by_rows(attn_got[:, :, wide : wide + qk]),
        by_rows(attn_got[:, :, wide + qk : wide + 2 * qk]),
        by_rows(attn_got[:, :, :wide]),
        grad_out.astype(jnp.float32),
        by_hidden(ffn_got[:, :, :hidden]),
        by_hidden(ffn_got[:, :, hidden:]),
        sum_down.astype(jnp.float32),
        grad_gains[:, 0],
        grad_gains[:, 1],
    )


def solution(mesh):
    by_token, by_row = P("dp", None, "seq", None), P("dp", None)
    grad_rows, grad_entries = P(("dp", "seq"), None), P(("dp", "seq"))
    return jax.shard_map(
        local,
        mesh=mesh,
        in_specs=(by_token, P("dp", None, None)) + (by_row,) * 7 + (P("dp"), P("dp"), by_token),
        out_specs=(by_token, by_token) + (grad_rows,) * 7 + (grad_entries,) * 2,
        check_vma=False,
    )
```

```python
import functools
import math

import jax
import jax.numpy as jnp
from jax import lax
from jax.experimental import pallas as pl
from jax.experimental.pallas import tpu as pltpu
from jax.sharding import PartitionSpec as P

D = 2048
HEADS = 16
QK_DIM = 16
FF = 5632
HEAD_V = 128
epsilon = 1e-06
MIB = 1024 * 1024


def dot(left, right):
    return jnp.dot(left, right, preferred_element_type=jnp.float32)


def contract(left, right, left_dim, right_dim):
    return lax.dot_general(
        left, right, (((left_dim,), (right_dim,)), ((), ())), preferred_element_type=jnp.float32
    )


def head_lanes(rows, head):
    lane = lax.broadcasted_iota(jnp.int32, rows.shape, 1)
    inside = (lane >= head * QK_DIM) & (lane < (head + 1) * QK_DIM)
    return jnp.where(inside, rows, jnp.zeros_like(rows))


def weights_of(query, key, head, first, base):
    scores = contract(head_lanes(query, head), key, 1, 1)
    row = base + lax.broadcasted_iota(jnp.int32, scores.shape, 0)
    column = lax.broadcasted_iota(jnp.int32, scores.shape, 1)
    mask = (column <= row) & (column >= first)
    poly = 1.0 + scores * (1.0 / math.sqrt(QK_DIM)) + scores * scores * (0.5 / QK_DIM)
    return scores, mask, jnp.where(mask, poly, 0.0)


def attend_kernel(heads, q_ref, k_ref, v_ref, first_ref, out_ref):
    rows = q_ref.shape[1]
    base = pl.program_id(1) * rows
    for head in range(heads):
        columns = slice(head * HEAD_V, (head + 1) * HEAD_V)
        unused, unused_mask, weight = weights_of(
            q_ref[0], k_ref[0], head, first_ref[0], base
        )
        denom = jnp.sum(weight, axis=1, keepdims=True)
        numer = dot(weight.astype(jnp.bfloat16), v_ref[0, :, columns])
        out_ref[0, :, columns] = (numer / denom).astype(jnp.bfloat16)


def attend(query, key, value, first, heads):
    streams, length, width = query.shape
    rows = min(256, length)
    return pl.pallas_call(
        functools.partial(attend_kernel, heads),
        grid=(streams, length // rows),
        in_specs=[
            pl.BlockSpec((1, rows, width), lambda m, i: (m, i, 0)),
            pl.BlockSpec((1, length, width), lambda m, i: (m, 0, 0)),
            pl.BlockSpec((1, length, heads * HEAD_V), lambda m, i: (m, 0, 0)),
            pl.BlockSpec((1, rows, 1), lambda m, i: (m, i, 0)),
        ],
        out_specs=pl.BlockSpec((1, rows, heads * HEAD_V), lambda m, i: (m, i, 0)),
        out_shape=jax.ShapeDtypeStruct(value.shape, jnp.bfloat16),
        compiler_params=pltpu.CompilerParams(vmem_limit_bytes=48 * MIB),
        name="attend",
    )(query, key, value, first)


def attend_back_kernel(
    heads, q_ref, k_ref, v_ref, first_ref, att_ref, g_ref, gq_ref, gk_ref, gv_ref, gk_sum, gv_sum
):
    rows = q_ref.shape[1]
    step = pl.program_id(1)
    base = step * rows

    @pl.when(step == 0)
    def _():
        gk_sum[...] = jnp.zeros_like(gk_sum)
        gv_sum[...] = jnp.zeros_like(gv_sum)

    query, key = q_ref[0], k_ref[0]
    g_query = jnp.zeros(query.shape, jnp.float32)
    for head in range(heads):
        columns = slice(head * HEAD_V, (head + 1) * HEAD_V)
        scores, mask, weight = weights_of(query, key, head, first_ref[0], base)
        denom = jnp.sum(weight, axis=1, keepdims=True)
        a = (g_ref[0, :, columns].astype(jnp.float32) / denom).astype(jnp.bfloat16)
        b = -jnp.sum(
            a.astype(jnp.float32) * att_ref[0, :, columns].astype(jnp.float32),
            axis=1,
            keepdims=True,
        )
        g_weight = contract(a, v_ref[0, :, columns], 1, 1) + b
        slope = 1.0 / math.sqrt(QK_DIM) + scores * (1.0 / QK_DIM)
        g_scores = jnp.where(mask, g_weight * slope, 0.0).astype(jnp.bfloat16)
        g_query += head_lanes(dot(g_scores, key), head)
        gk_sum[...] += contract(g_scores, head_lanes(query, head), 0, 0)
        gv_sum[:, columns] += contract(weight.astype(jnp.bfloat16), a, 0, 0)
    gq_ref[0] = g_query.astype(jnp.bfloat16)

    @pl.when(step == pl.num_programs(1) - 1)
    def _():
        gk_ref[0] = gk_sum[...].astype(jnp.bfloat16)
        gv_ref[0] = gv_sum[...].astype(jnp.bfloat16)


def attend_back(query, key, value, first, attended, grad, heads):
    streams, length, width = query.shape
    rows = min(256, length)
    some = pl.BlockSpec((1, rows, width), lambda m, i: (m, i, 0))
    all_narrow = pl.BlockSpec((1, length, width), lambda m, i: (m, 0, 0))
    all_wide = pl.BlockSpec((1, length, heads * HEAD_V), lambda m, i: (m, 0, 0))
    some_wide = pl.BlockSpec((1, rows, heads * HEAD_V), lambda m, i: (m, i, 0))
    return pl.pallas_call(
        functools.partial(attend_back_kernel, heads),
        grid=(streams, length // rows),
        in_specs=[
            some,
            all_narrow,
            all_wide,
            pl.BlockSpec((1, rows, 1), lambda m, i: (m, i, 0)),
            some_wide,
            some_wide,
        ],
        out_specs=[some, all_narrow, all_wide],
        out_shape=[
            jax.ShapeDtypeStruct(query.shape, jnp.bfloat16),
            jax.ShapeDtypeStruct(key.shape, jnp.bfloat16),
            jax.ShapeDtypeStruct(value.shape, jnp.bfloat16),
        ],
        scratch_shapes=[
            pltpu.VMEM((length, width), jnp.float32),
            pltpu.VMEM((length, heads * HEAD_V), jnp.float32),
        ],
        compiler_params=pltpu.CompilerParams(vmem_limit_bytes=56 * MIB),
        name="attend_back",
    )(query, key, value, first, attended, grad)

MESH = pl.DeviceIdType.MESH
LOW = jnp.bfloat16


def partners():
    me = lax.axis_index("seq")
    core, x, y = me % 2, me // 2 % 2, me // 4
    return me, me + 1 - 2 * core, me + 2 - 4 * x, me + 4 - 8 * y


def greet(others):
    barrier = pltpu.get_barrier_semaphore()
    for other in others:
        pl.semaphore_signal(barrier, inc=1, device_id={"seq": other}, device_id_type=MESH)
    pl.semaphore_wait(barrier, len(others))


def remote(send, recv, k, src, dst, to):
    return pltpu.make_async_remote_copy(
        src_ref=src,
        dst_ref=dst,
        send_sem=send.at[k],
        recv_sem=recv.at[k],
        device_id={"seq": to},
        device_id_type=MESH,
    )


def gather_kernel(x_ref, o_ref, send, recv, own_sem):
    me, sib, xn, yn = partners()
    diag = xn + yn - me
    half = x_ref.shape[0] // 2
    copy = functools.partial(remote, send, recv)
    upper, lower = pl.ds(0, half), pl.ds(half, half)
    greet((sib, xn, yn))
    own = pltpu.make_async_copy(x_ref, o_ref.at[me], own_sem)
    own.start()
    xa = copy(0, x_ref.at[upper], o_ref.at[me, upper], xn)
    yb = copy(1, x_ref.at[lower], o_ref.at[me, lower], yn)
    xb = copy(2, x_ref.at[lower], o_ref.at[me, lower], xn)
    ya = copy(3, x_ref.at[upper], o_ref.at[me, upper], yn)
    beside = [copy(4, x_ref, o_ref.at[me], sib)]
    started = [xa, yb, xb, ya, beside[0]]
    for c in started:
        c.start()

    def pass_on(k, origin, part, to):
        block = o_ref.at[origin, part]
        c = copy(k, block, block, to)
        c.start()
        started.append(c)
        return c

    xa.wait_recv()
    fy = pass_on(5, xn, upper, yn)
    beside.append(pass_on(6, xn, upper, sib))
    yb.wait_recv()
    fx = pass_on(7, yn, lower, xn)
    beside.append(pass_on(8, yn, lower, sib))
    xb.wait_recv()
    beside.append(pass_on(9, xn, lower, sib))
    ya.wait_recv()
    beside.append(pass_on(10, yn, upper, sib))
    fy.wait_recv()
    beside.append(pass_on(11, diag, upper, sib))
    fx.wait_recv()
    beside.append(pass_on(12, diag, lower, sib))
    own.wait()
    for c in beside:
        c.wait_recv()
    for c in started:
        c.wait_send()


def moved(nbytes):
    return pl.CostEstimate(flops=0, bytes_accessed=nbytes * 10, transcendentals=0)


def gather_plane(x, number):
    pieces = lax.axis_size("seq")
    if pieces != 8:
        return lax.all_gather(x, "seq", axis=0)
    return pl.pallas_call(
        gather_kernel,
        out_shape=jax.ShapeDtypeStruct((8,) + x.shape, x.dtype),
        in_specs=[pl.BlockSpec(memory_space=pl.ANY)],
        out_specs=pl.BlockSpec(memory_space=pl.ANY),
        scratch_shapes=[
            pltpu.SemaphoreType.DMA((13,)),
            pltpu.SemaphoreType.DMA((13,)),
            pltpu.SemaphoreType.DMA,
        ],
        compiler_params=pltpu.CompilerParams(collective_id=number, has_side_effects=True),
        cost_estimate=moved(16 * x.size),
        name="gather",
    )(x)


def scatter_kernel(p_ref, o_ref, held, got, one, two, send, recv, own_sem):
    me, sib, xn, yn = partners()
    diag = xn + yn - me
    half = p_ref.shape[1] // 2
    copy = functools.partial(remote, send, recv)
    upper, lower = pl.ds(0, half), pl.ds(half, half)
    greet((sib, xn, yn))
    beside, loads = [], []
    for i, owner in enumerate((diag, xn, yn, me)):
        beside.append(copy(i, p_ref.at[owner + sib - me], got.at[i], sib))
        loads.append(pltpu.make_async_copy(p_ref.at[owner], held.at[i], own_sem.at[i]))
        beside[i].start()
        loads[i].start()

    def pair_sum(i):
        beside[i].wait_recv()
        loads[i].wait()
        held[i] = held[i] + got[i]

    pair_sum(0)
    x0 = copy(4, held.at[0, upper], one.at[0], xn)
    x0.start()
    y0 = copy(5, held.at[0, lower], one.at[1], yn)
    y0.start()
    pair_sum(1)
    x1 = copy(6, held.at[1, upper], one.at[2], xn)
    x1.start()
    pair_sum(2)
    y1 = copy(7, held.at[2, lower], one.at[3], yn)
    y1.start()
    pair_sum(3)
    x0.wait_recv()
    held[2, :half] = held[2, :half] + one[0]
    y2 = copy(8, held.at[2, upper], two.at[0], yn)
    y2.start()
    y0.wait_recv()
    held[1, half:] = held[1, half:] + one[1]
    x2 = copy(9, held.at[1, lower], two.at[1], xn)
    x2.start()
    x1.wait_recv()
    y1.wait_recv()
    y2.wait_recv()
    wide = jnp.float32
    o_ref[:half] = held[3, :half].astype(wide) + one[2].astype(wide) + two[0].astype(wide)
    x2.wait_recv()
    o_ref[half:] = held[3, half:].astype(wide) + one[3].astype(wide) + two[1].astype(wide)
    for c in (*beside, x0, y0, x1, y1, y2, x2):
        c.wait_send()


def scatter_plane(part, number):
    pieces, rows, columns = part.shape
    if pieces != 8:
        return lax.psum_scatter(part, "seq", scatter_dimension=0).astype(jnp.float32)
    return pl.pallas_call(
        scatter_kernel,
        out_shape=jax.ShapeDtypeStruct((rows, columns), jnp.float32),
        in_specs=[pl.BlockSpec(memory_space=pl.ANY)],
        out_specs=pl.BlockSpec(memory_space=pltpu.VMEM),
        scratch_shapes=[
            pltpu.VMEM((4, rows, columns), LOW),
            pltpu.VMEM((4, rows, columns), LOW),
            pltpu.VMEM((4, rows // 2, columns), LOW),
            pltpu.VMEM((2, rows // 2, columns), LOW),
            pltpu.SemaphoreType.DMA((10,)),
            pltpu.SemaphoreType.DMA((10,)),
            pltpu.SemaphoreType.DMA((4,)),
        ],
        compiler_params=pltpu.CompilerParams(
            collective_id=number, has_side_effects=True, vmem_limit_bytes=40 * MIB
        ),
        cost_estimate=moved(2 * part.size),
        name="scatter",
    )(part)


def exchange_kernel(x_ref, o_ref, send, recv, own_sem):
    me = lax.axis_index("seq")
    columns = pl.ds(0, o_ref.shape[2])
    others = [lax.rem(me + i, 8) for i in range(1, 8)]
    greet(others)
    own = pltpu.make_async_copy(x_ref.at[me, :, columns], o_ref.at[me], own_sem)
    own.start()
    copies = [
        remote(send, recv, i, x_ref.at[other, :, columns], o_ref.at[me], other)
        for i, other in enumerate(others)
    ]
    for c in copies:
        c.start()
    own.wait()
    for c in copies:
        c.wait()


def exchange_plane(x, number, columns=None):
    if lax.axis_size("seq") != 8:
        return lax.all_to_all(x, "seq", 0, 0)
    return pl.pallas_call(
        exchange_kernel,
        out_shape=jax.ShapeDtypeStruct(x.shape[:-1] + (columns or x.shape[-1],), x.dtype),
        in_specs=[pl.BlockSpec(memory_space=pl.ANY)],
        out_specs=pl.BlockSpec(memory_space=pl.ANY),
        scratch_shapes=[
            pltpu.SemaphoreType.DMA((7,)),
            pltpu.SemaphoreType.DMA((7,)),
            pltpu.SemaphoreType.DMA,
        ],
        compiler_params=pltpu.CompilerParams(collective_id=number, has_side_effects=True),
        cost_estimate=moved(4 * x.size),
        name="exchange",
    )(x)


CHUNKS = (64, 64, 48)


class PlaneGather:
    def __init__(self, source, target, send, recv):
        me, sib, xn, yn = partners()
        diag = xn + yn - me
        half = target.shape[1] // 2
        upper, lower = pl.ds(0, half), pl.ds(half, half)
        copy = functools.partial(remote, send, recv)

        def direct(k, part, to):
            return copy(k, source.at[part], target.at[me, part], to)

        def pass_on(k, origin, part, to):
            return copy(k, target.at[origin, part], target.at[origin, part], to)

        self.xa, self.yb = direct(0, upper, xn), direct(1, lower, yn)
        self.xb, self.ya = direct(2, lower, xn), direct(3, upper, yn)
        self.s0 = copy(4, source, target.at[me], sib)
        self.fy, self.fx = pass_on(5, xn, upper, yn), pass_on(6, yn, lower, xn)
        self.s1, self.s2 = pass_on(7, xn, upper, sib), pass_on(8, yn, lower, sib)
        self.s3, self.s4 = pass_on(9, xn, lower, sib), pass_on(10, yn, upper, sib)
        self.s5, self.s6 = pass_on(11, diag, upper, sib), pass_on(12, diag, lower, sib)

    def start(self):
        for c in (self.xa, self.yb, self.xb, self.ya, self.s0):
            c.start()

    def forward_first(self):
        self.xa.wait_recv()
        self.yb.wait_recv()
        for c in (self.fy, self.fx, self.s1, self.s2):
            c.start()

    def forward_second(self):
        self.xb.wait_recv()
        self.ya.wait_recv()
        self.s3.start()
        self.s4.start()

    def forward_third(self):
        self.fy.wait_recv()
        self.fx.wait_recv()
        self.s5.start()
        self.s6.start()

    def from_sibling(self, chip):
        for c in {"own": (self.s0,), "x": (self.s1, self.s3), "y": (self.s2, self.s4), "diag": (self.s5, self.s6)}[chip]:
            c.wait_recv()

    def sent(self):
        for c in (self.xa, self.yb, self.xb, self.ya, self.s0, self.fy, self.fx):
            c.wait_send()
        for c in (self.s1, self.s2, self.s3, self.s4, self.s5, self.s6):
            c.wait_send()

    def arrive(self, step):
        @pl.when(step == 1)
        def _():
            self.from_sibling("own")

        @pl.when(step == 2)
        def _():
            self.forward_first()
            self.forward_second()
            self.from_sibling("x")

        @pl.when(step == 4)
        def _():
            self.from_sibling("y")

        @pl.when(step == 6)
        def _():
            self.forward_third()
            self.from_sibling("diag")


class LineGather:
    def __init__(self, item, source, block, send, recv, local=None):
        z = lax.axis_index("dp")
        self.z = z

        def copy(k, src, owner, to):
            return pltpu.make_async_remote_copy(
                src_ref=src,
                dst_ref=block(owner),
                send_sem=send.at[item, k],
                recv_sem=recv.at[item, owner],
                device_id={"dp": to},
                device_id_type=MESH,
            )

        self.sends = []
        for k, d in enumerate((2, -2, 1, -1)):
            to = z + d
            valid = (to >= 0) & (to < 4)
            self.sends.append((valid, copy(k, source, z, jnp.clip(to, 0, 3))))
        inner = (z == 1) | (z == 2)
        far = jnp.where(z == 1, 3, 0)
        self.stop = (inner, copy(4, block(far), far, jnp.where(z == 1, 0, 3)))
        others = [lax.rem(z + o, 4) for o in (1, 2, 3)]
        self.blocks = [copy(0, source, other, other) for other in others]
        self.own = None
        if local is not None:
            self.own = pltpu.make_async_copy(source, block(z), local.at[item])

    def start_far(self):
        if self.own is not None:
            self.own.start()
        self.begin(self.sends[:2])

    def start_near(self):
        self.begin(self.sends[2:])

    def start(self):
        self.start_far()
        self.start_near()

    def begin(self, sends):
        for valid, c in sends:

            @pl.when(valid)
            def _(c=c):
                c.start()

    def forward(self):
        inner, c = self.stop

        @pl.when(inner)
        def _():
            self.blocks[1].wait_recv()
            c.start()

    def wait(self):
        inner, unused = self.stop
        self.blocks[0].wait_recv()
        self.blocks[2].wait_recv()

        @pl.when(jnp.logical_not(inner))
        def _():
            self.blocks[1].wait_recv()

        if self.own is not None:
            self.own.wait()

    def sent(self):
        for valid, c in (*self.sends, self.stop):

            @pl.when(valid)
            def _(c=c):
                c.wait_send()


def nearest_first(step):
    me, sib, xn, yn = partners()
    chip = jnp.where(step < 4, xn, jnp.where(step < 6, yn, xn + yn - me))
    later = chip + jnp.where(lax.rem(step, 2) == 0, sib - me, 0)
    return jnp.where(step == 0, me, jnp.where(step == 1, sib, later))


def farthest_first(step):
    me, sib, xn, yn = partners()
    chip = jnp.where(step < 4, xn, yn)
    chip = jnp.where(step < 2, xn + yn - me, jnp.where(step < 6, chip, me))
    return chip + jnp.where(lax.rem(step, 2) == 0, sib - me, 0)


def first_of(lengths, stream, base, count):
    row = base + lax.broadcasted_iota(jnp.int32, (count, 1), 0)
    start, first = jnp.int32(0), jnp.zeros((count, 1), jnp.int32)
    for j in range(lengths.shape[1]):
        first = jnp.where(row >= start, start, first)
        start = start + lengths[stream, j]
    return first


def layer_kernel(
    x_ref,
    c_ref,
    wq_ref,
    wk_ref,
    wv_ref,
    wo_ref,
    wg_ref,
    wu_ref,
    wd_ref,
    gain_ref,
    lengths_ref,
    x_all,
    c_all,
    h2_all,
    wo_all,
    h1_out,
    q_out,
    k_out,
    v_out,
    att_out,
    tok_out,
    mid_out,
    wa_out,
    gain_out,
    out_part,
    gh_out,
    dgu_first,
    dd_first,
    dgu_out,
    dd_out,
    dgu_all,
    dd_all,
    wa,
    wgu,
    wd,
    gains,
    q_s,
    k_s,
    v_s,
    att_s,
    tok,
    mid,
    act_s,
    ggu_s,
    sum_gu,
    sum_d,
    x_buf,
    c_buf,
    o_buf,
    beside,
    held,
    got,
    one,
    two,
    gsend,
    grecv,
    zsend,
    zrecv,
    zlocal,
    esend,
    erecv,
    rsend,
    rrecv,
    load_sem,
    out_sem,
    h1_sem,
    w_sem,
    done_sem,
    self_sem,
    fsend,
    frecv,
    f_sem,
    cut_sem,
    gu_stop,
    d_stop,
):
    me, sib, xn, yn = partners()
    z = lax.axis_index("dp")
    rows, width = x_ref.shape
    span = rows // 2
    wide, qk = v_s.shape[2], q_s.shape[2]
    share = CHUNKS[0] + CHUNKS[1] + CHUNKS[2]
    half = rows // 2
    upper, lower = pl.ds(0, half), pl.ds(half, half)

    barrier = pltpu.get_barrier_semaphore()
    for i in range(1, 8):
        pl.semaphore_signal(
            barrier, inc=1, device_id={"seq": lax.rem(me + i, 8)}, device_id_type=MESH
        )
    for i in range(1, 4):
        pl.semaphore_signal(
            barrier, inc=1, device_id={"dp": lax.rem(z + i, 4)}, device_id_type=MESH
        )
    pl.semaphore_wait(barrier, 10)

    tokens = PlaneGather(x_ref, x_all, gsend.at[0], grecv.at[0])
    out_w = PlaneGather(wo_all.at[me], wo_all, gsend.at[1], grecv.at[1])
    cots = PlaneGather(c_ref, c_all, gsend.at[2], grecv.at[2])
    hidden_in = PlaneGather(held.at[0], h2_all, gsend.at[3], grecv.at[3])

    def line(item, source, block):
        return LineGather(item, source, block, zsend, zrecv, zlocal)

    def line_in_place(item, block):
        return LineGather(item, block(z), block, zsend, zrecv)

    depth = wq_ref.shape[0]

    def rows_of(ref, count, columns=None):
        def block(owner):
            if columns is None:
                return ref.at[pl.ds(owner * count, count)]
            return ref.at[pl.ds(owner * count, count), columns]

        return block

    z_gain = line(
        0, gain_ref, lambda owner: gains.at[:, pl.ds(pl.multiple_of(owner * depth, 128), depth)]
    )
    z_attn = line_in_place(1, rows_of(wa, depth))
    z_out = line(
        2,
        wo_ref.at[:, pl.ds(pl.multiple_of(me * wide, 128), wide)],
        lambda owner: wo_all.at[me, pl.ds(owner * depth, depth)],
    )
    z_up, z_down = [], []
    column, before = 0, 0
    columns, hiddens = [], []
    for k, count in enumerate(CHUNKS):
        part = pl.ds(column, 8 * count)
        z_up.append(line_in_place(3 + k, rows_of(wgu, depth, part)))
        z_down.append(
            line(
                6 + k,
                wd_ref.at[pl.ds(me * share + before, count)],
                lambda owner, base=4 * before, count=count: wd.at[
                    pl.ds(base + owner * count, count)
                ],
            )
        )
        columns.append(column)
        hiddens.append(4 * before)
        column += 8 * count
        before += count

    tokens.start()
    z_gain.start()

    window = 384
    tall = depth // 2

    def cut_window(i, source, start, size, r, slot, lane):
        return pltpu.make_async_copy(
            source.at[pl.ds(r * tall, tall), pl.ds(pl.multiple_of(start, 128), size)],
            got.at[slot, :, pl.ds(lane, size)],
            cut_sem.at[i],
        )

    per_tile = 128 // qk
    narrow = me // per_tile * 128
    shift = lax.rem(me, per_tile) * qk
    own_rows = pl.ds(pl.multiple_of(z * depth, depth), depth)
    v_cut = pltpu.make_async_copy(
        wv_ref.at[:, pl.ds(pl.multiple_of(me * wide, 128), wide)],
        wa.at[own_rows, pl.ds(0, wide)],
        cut_sem.at[20],
    )
    v_cut.start()
    qk_cuts = [
        cut_window(2 * r + i, source, narrow, 128, r, r, 128 * i)
        for r in range(2)
        for i, source in enumerate((wq_ref, wk_ref))
    ]
    for c in qk_cuts:
        c.start()
    ff_cuts = []
    ff_width = wg_ref.shape[1]
    for second, source in enumerate((wg_ref, wu_ref)):
        for group in range(4):
            start = group * (ff_width // 4) + me * share
            aligned = jnp.minimum(start // 128 * 128, ff_width - window)
            lane = 256 * (1 - second) + window * group
            for r in range(2):
                c = cut_window(
                    4 + len(ff_cuts), source, aligned, window, r, 2 * second + r, lane
                )
                c.start()
                ff_cuts.append((c, second, group, r, lane, start - aligned))
    for c in qk_cuts:
        c.wait()
    for r in range(2):
        lane = lax.broadcasted_iota(jnp.int32, (tall, 128), 1)
        q_rows = pltpu.roll(got[r, :, 0:128].astype(jnp.float32), lax.rem(128 - shift, 128), 1)
        k_rows = pltpu.roll(
            got[r, :, 128:256].astype(jnp.float32), lax.rem(128 + qk - shift, 128), 1
        )
        both = jnp.where(lane < qk, q_rows, jnp.where(lane < 2 * qk, k_rows, 0.0))
        there = pl.ds(pl.multiple_of(z * depth + r * tall, tall), tall)
        wa[there, wide : wide + 128] = both.astype(LOW)
    v_cut.wait()
    z_attn.start()
    for c, second, group, r, lane, shift_by in ff_cuts:
        c.wait()
        rolled = pltpu.roll(
            got[2 * second + r, :, lane : lane + window].astype(jnp.float32),
            lax.rem(window - shift_by, window),
            1,
        )
        there = pl.ds(pl.multiple_of(z * depth + r * tall, tall), tall)
        begin = 0
        for k, count in enumerate(CHUNKS):
            at = columns[k] + (4 * second + group) * count
            wgu[there, at : at + count] = rolled[:, begin : begin + count].astype(LOW)
            begin += count
    z_out.start()
    for g in (z_up[0], z_down[0]):
        g.start()

    def loads(order, step, sources):
        slot = lax.rem(step, 2)
        owner = order(step)
        return [
            pltpu.make_async_copy(source.at[owner], buf.at[slot], load_sem.at[i, slot])
            for i, (source, buf) in enumerate(sources)
        ]

    first_load = pltpu.make_async_copy(x_ref, x_buf.at[0], load_sem.at[0, 0])
    first_load.start()
    c_load = pltpu.make_async_copy(c_ref, c_buf.at[0], load_sem.at[1, 0])
    c_load.start()
    tokens.forward_first()
    z_gain.forward()
    z_attn.forward()
    tokens.forward_second()
    cots.start()
    c_load.wait()
    own_c = pltpu.make_async_copy(c_buf.at[0], c_all.at[me], self_sem.at[3])
    own_c.start()
    z_gain.wait()
    z_attn.wait()
    for g in (z_up[1], z_down[1]):
        g.start()

    def h1_copies(step):
        slot = lax.rem(step, 2)
        owner = nearest_first(step)
        return [
            pltpu.make_async_copy(
                o_buf.at[slot, pl.ds(m * span, span)],
                h1_out.at[m, pl.ds(owner * span, span)],
                h1_sem.at[m, slot],
            )
            for m in range(2)
        ]

    def arrive_tokens(step):
        @pl.when(step == 1)
        def _():
            tokens.from_sibling("own")

        @pl.when(step == 2)
        def _():
            tokens.from_sibling("x")

        @pl.when(step == 4)
        def _():
            tokens.forward_third()
            tokens.from_sibling("y")

        @pl.when(step == 6)
        def _():
            tokens.from_sibling("diag")

        @pl.when(step == 7)
        def _():
            z_out.forward()

    token_source = [(x_all, x_buf)]

    def project(step, carry):
        slot = lax.rem(step, 2)
        owner = nearest_first(step)
        for c in loads(nearest_first, step, token_source):
            c.wait()

        @pl.when(step >= 2)
        def _():
            for c in h1_copies(step - 2):
                c.wait()

        x = x_buf[slot].astype(jnp.float32)
        gain = gains[0:1, :].astype(jnp.float32)
        h_one = (x * norm_scale(x) * gain).astype(LOW)
        o_buf[slot] = h_one
        for c in h1_copies(step):
            c.start()
        arrive_tokens(step + 1)

        @pl.when(step < 7)
        def _():
            for c in loads(nearest_first, step + 1, token_source):
                c.start()

        projected = dot(h_one, wa[...]).astype(LOW)
        for m in range(2):
            there = pl.ds(owner * span, span)
            mine = projected[m * span : (m + 1) * span]
            v_s[m, there, :] = mine[:, :wide]
            q_s[m, there, :] = mine[:, wide : wide + qk]
            k_s[m, there, :] = mine[:, wide + qk : wide + 2 * qk]
        return carry

    lax.fori_loop(0, 8, project, 0)
    for step in (6, 7):
        for c in h1_copies(step):
            c.wait()
    z_out.wait()
    out_w.start()
    for g in (z_up[2], z_down[2]):
        g.start()

    finals = [
        pltpu.make_async_copy(source, target, done_sem.at[i])
        for i, (source, target) in enumerate(
            (
                (q_s, q_out),
                (k_s, k_out),
                (v_s, v_out),
                (wa, wa_out),
                (gains, gain_out),
                (att_s, att_out),
                (tok, tok_out),
                (mid, mid_out),
            )
        )
    ]
    for c in finals[:5]:
        c.start()

    length = v_s.shape[1]
    block = 256

    def attend_stream(m, carry):
        for i in range(length // block):
            rows_i = slice(i * block, (i + 1) * block)
            seen = (i + 1) * block
            first = first_of(lengths_ref, m, i * block, block)
            for head in range(wide // HEAD_V):
                lanes = slice(head * HEAD_V, (head + 1) * HEAD_V)
                unused, unused_mask, weight = weights_of(
                    q_s[m, rows_i, :], k_s[m, :seen, :], head, first, i * block
                )
                denom = jnp.sum(weight, axis=1, keepdims=True)
                numer = dot(weight.astype(LOW), v_s[m, :seen, lanes])
                att_s[m, rows_i, lanes] = (numer / denom).astype(LOW)
        return carry

    lax.fori_loop(0, 2, attend_stream, 0)
    out_w.forward_first()
    finals[5].start()

    to_mine = pl.ds(pl.multiple_of(me * wide, 128), wide)
    swaps = []
    for i in range(1, 8):
        other = lax.rem(me + i, 8)
        for m in range(2):
            swaps.append(
                remote(
                    esend,
                    erecv,
                    2 * (i - 1) + m,
                    att_s.at[m, pl.ds(other * span, span)],
                    tok.at[pl.ds(m * span, span), to_mine],
                    other,
                )
            )
            swaps[-1].start()
    kept = [
        pltpu.make_async_copy(
            att_s.at[m, pl.ds(me * span, span)],
            tok.at[pl.ds(m * span, span), to_mine],
            self_sem.at[m],
        )
        for m in range(2)
    ]
    for c in kept:
        c.start()
    x_load = pltpu.make_async_copy(x_ref, x_buf.at[0], load_sem.at[0, 0])
    x_load.start()

    def w_lanes(slot):
        return pl.ds(pl.multiple_of(slot * wide, 128), wide)

    def w_load(step):
        slot = lax.rem(step, 2)
        return pltpu.make_async_copy(
            wo_all.at[nearest_first(step)], act_s.at[:, w_lanes(slot)], w_sem.at[slot]
        )

    w_load(0).start()
    out_w.forward_second()
    cots.forward_first()
    cots.forward_second()
    z_up[0].forward()
    z_down[0].forward()
    for c in kept:
        c.wait()
    for c in swaps:
        c.wait_recv()
    finals[6].start()
    x_load.wait()

    def arrive_out(step):
        @pl.when(step == 1)
        def _():
            out_w.from_sibling("own")

        @pl.when(step == 2)
        def _():
            out_w.from_sibling("x")

        @pl.when(step == 4)
        def _():
            out_w.forward_third()
            out_w.from_sibling("y")

        @pl.when(step == 6)
        def _():
            out_w.from_sibling("diag")

    def project_out(step, carry):
        slot = lax.rem(step, 2)
        owner = nearest_first(step)
        w_load(step).wait()
        arrive_out(step + 1)

        @pl.when(step < 7)
        def _():
            w_load(step + 1).start()

        there = pl.ds(pl.multiple_of(owner * wide, 128), wide)
        mid[:, there] = dot(tok[...], act_s[:, w_lanes(slot)])
        return carry

    lax.fori_loop(0, 8, project_out, 0)
    mid_value = x_buf[0].astype(jnp.float32) + mid[...]
    mid[...] = mid_value
    held[0] = (mid_value * norm_scale(mid_value) * gains[1:2, :].astype(jnp.float32)).astype(LOW)
    hidden_in.start()
    own_h2 = pltpu.make_async_copy(held.at[0], h2_all.at[me], self_sem.at[2])
    own_h2.start()
    cots.forward_third()
    z_up[1].forward()
    z_down[1].forward()
    own_h2.wait()
    own_c.wait()
    z_up[0].wait()
    z_down[0].wait()

    largest = 4 * max(CHUNKS)
    sources = [(h2_all, x_buf), (c_all, c_buf)]

    def out_copy(order, step):
        slot = lax.rem(step, 2)
        return pltpu.make_async_copy(o_buf.at[slot], out_part.at[order(step)], out_sem.at[slot])

    def hidden_chunk(k, owner, h, c):
        count = 4 * CHUNKS[k]
        pair = pl.ds(columns[k], 2 * count)
        here = pl.ds(hiddens[k], count)
        both = dot(h, wgu[:, pair])
        gate, up = both[:, :count], both[:, count:]
        g_act = contract(c, wd[here, :], 1, 1)
        sigmoid = jax.nn.sigmoid(gate)
        silu = gate * sigmoid
        act = (silu * up).astype(LOW)
        g_gate = (g_act * up * sigmoid * (1.0 + gate * (1.0 - sigmoid))).astype(LOW)
        g_up = (g_act * silu).astype(LOW)
        there = pl.ds(owner * rows, rows)
        act_s[there, here] = act
        g_both = jnp.concatenate([g_gate, g_up], axis=1)
        ggu_s[there, pair] = g_both
        return act, g_both

    def add_grads(k, step, h, c, act, g_both):
        count = 4 * CHUNKS[k]

        to, low = (2 * largest, largest) if k == 1 else (0, 0)

        @pl.when(step == 0)
        def _():
            sum_gu[:, to : to + 2 * count] = jnp.zeros((width, 2 * count), jnp.float32)
            sum_d[low : low + count, :] = jnp.zeros((count, width), jnp.float32)

        sum_gu[:, to : to + 2 * count] += contract(h, g_both, 0, 0)
        sum_d[low : low + count, :] += contract(act, c, 0, 0)

    def emit(k):
        count = 4 * CHUNKS[k]
        rest = share - CHUNKS[0]
        to, low = (2 * largest, largest) if k == 1 else (0, 0)

        def gu_copies(i, slot):
            there = pl.ds(i * rows, rows)
            if k == 0:
                return [
                    pltpu.make_async_copy(
                        o_buf.at[slot, :, pl.ds(second * count, count)],
                        dgu_first.at[second, there],
                        h1_sem.at[second, slot],
                    )
                    for second in range(2)
                ]
            return [
                pltpu.make_async_copy(
                    o_buf.at[slot, :, pl.ds(0, 2 * count)],
                    dgu_out.at[there, pl.ds(columns[k] - columns[1], 2 * count)],
                    out_sem.at[slot],
                )
            ]

        def d_target(owner):
            if k == 0:
                return dd_first.at[pl.ds(owner * CHUNKS[0], CHUNKS[0])]
            start = owner * rest + (hiddens[k] - hiddens[1]) // 4
            return dd_out.at[pl.ds(start, CHUNKS[k])]

        pending = [[], []]
        for i in range(width // rows):
            slot = i % 2
            for c in pending[slot]:
                c.wait()
            total = sum_gu[i * rows : (i + 1) * rows, to : to + 2 * count]
            o_buf[slot, :, : 2 * count] = total.astype(LOW)
            pending[slot] = gu_copies(i, slot)
            for c in pending[slot]:
                c.start()
        for c in (*pending[0], *pending[1]):
            c.wait()
        o_buf[0, :count, :] = sum_d[low : low + count, :].astype(LOW)
        downs = []
        for owner in range(4):
            downs.append(
                pltpu.make_async_copy(
                    o_buf.at[0, pl.ds(owner * CHUNKS[k], CHUNKS[k])],
                    d_target(owner),
                    h1_sem.at[owner // 2, owner % 2],
                )
            )
            downs[-1].start()
        for c in downs:
            c.wait()

    def forward_pass(chunks, last, arrive, step, carry):
        slot = lax.rem(step, 2)
        for c in loads(nearest_first, step, sources):
            c.wait()
        h, c = x_buf[slot], c_buf[slot]
        made = [hidden_chunk(k, nearest_first(step), h, c) for k in chunks]
        if arrive is not None:
            arrive(step + 1)

        @pl.when(step < last)
        def _():
            for c in loads(nearest_first, step + 1, sources):
                c.start()

        for k, (act, g_both) in zip(chunks, made):
            add_grads(k, step, h, c, act, g_both)
        return carry

    def arrive_both(step):
        hidden_in.arrive(step)

        @pl.when(step == 1)
        def _():
            cots.from_sibling("own")

        @pl.when(step == 2)
        def _():
            cots.from_sibling("x")

        @pl.when(step == 4)
        def _():
            cots.from_sibling("y")

        @pl.when(step == 6)
        def _():
            cots.from_sibling("diag")

    for c in loads(nearest_first, 0, sources):
        c.start()

    def arrive_near(step):
        @pl.when(step < 4)
        def _():
            arrive_both(step)

    lax.fori_loop(0, 4, functools.partial(forward_pass, (0,), 3, arrive_near), 0)
    for c in loads(nearest_first, 0, sources):
        c.start()
    z_up[1].wait()
    z_down[1].wait()
    z_up[2].forward()
    z_down[2].forward()
    lax.fori_loop(0, 4, functools.partial(forward_pass, (1,), 3, None), 0)
    arrive_both(jnp.int32(4))
    for c in loads(nearest_first, 4, sources):
        c.start()
    lax.fori_loop(4, 8, functools.partial(forward_pass, (0, 1), 7, arrive_both), 0)
    hidden_in.sent()
    finals[7].start()
    for c in loads(farthest_first, 0, sources):
        c.start()
    emit(0)
    sum_lines = [
        LineScatter(
            lambda owner: dgu_first.at[:, pl.ds(owner * depth, depth), :],
            dgu_all,
            gu_stop,
            att_s.at[:, pl.ds(0, depth), :],
            fsend.at[0],
            frecv.at[0],
            f_sem.at[0],
        ),
        LineScatter(
            lambda owner: dd_first.at[pl.ds(owner * CHUNKS[0], CHUNKS[0])],
            dd_all,
            d_stop,
            tok.at[pl.ds(0, CHUNKS[0])],
            fsend.at[1],
            frecv.at[1],
            f_sem.at[1],
        ),
    ]
    for c in swaps:
        c.wait_send()
    finals[5].wait()
    finals[6].wait()
    for g in sum_lines:
        g.start_first()

    z_up[2].wait()
    z_down[2].wait()

    copy = functools.partial(remote, rsend, rrecv)
    b_diag = copy(0, beside.at[0], got.at[2], sib)
    b_x = copy(1, beside.at[1], got.at[1], sib)
    b_y = copy(2, beside.at[0], got.at[3], sib)
    b_own = copy(3, beside.at[1], got.at[0], sib)
    x0 = copy(4, held.at[2, upper], one.at[0], xn)
    y0 = copy(5, held.at[2, lower], one.at[1], yn)
    x1 = copy(6, held.at[1, upper], one.at[2], xn)
    y1 = copy(7, held.at[3, lower], one.at[3], yn)
    y2 = copy(8, held.at[3, upper], two.at[0], yn)
    x2 = copy(9, held.at[1, lower], two.at[1], xn)

    def last_pass(step, carry):
        slot = lax.rem(step, 2)
        owner = farthest_first(step)
        there = pl.ds(owner * rows, rows)
        for c in loads(farthest_first, step, sources):
            c.wait()
        hidden_chunk(2, owner, x_buf[slot], c_buf[slot])

        @pl.when(step < 7)
        def _():
            for c in loads(farthest_first, step + 1, sources):
                c.start()

        part = contract(ggu_s[there, :], wgu[...], 1, 1).astype(LOW)

        @pl.when(step == 2)
        def _():
            for g in sum_lines:
                g.start()

        @pl.when(step == 6)
        def _():
            for g in sum_lines:
                g.join()

        for k, place, sent in ((0, 0, b_diag), (2, 1, b_x), (4, 0, b_y), (6, 1, b_own)):

            @pl.when(step == k)
            def _(k=k, place=place, sent=sent):
                if k == 4:
                    b_diag.wait_send()
                if k == 6:
                    b_x.wait_send()
                beside[place] = part
                sent.start()

        for k, place, arrived in ((1, 2, b_diag), (3, 1, b_x), (5, 3, b_y), (7, 0, b_own)):

            @pl.when(step == k)
            def _(k=k, place=place, arrived=arrived):
                arrived.wait_recv()
                held[place] = part + got[place]
                if k == 1:
                    x0.start()
                    y0.start()
                if k == 3:
                    x1.start()
                if k == 5:
                    y1.start()
                    y0.wait_recv()
                    held[1, half:] = held[1, half:] + one[1]
                    x2.start()
                    x0.wait_recv()
                    held[3, :half] = held[3, :half] + one[0]
                    y2.start()
        return carry

    lax.fori_loop(0, 8, last_pass, 0)
    for c in loads(farthest_first, 0, sources):
        c.start()

    def close_pass(step, carry):
        slot = lax.rem(step, 2)
        there = pl.ds(farthest_first(step) * rows, rows)
        for c in loads(farthest_first, step, sources):
            c.wait()

        @pl.when(step < 7)
        def _():
            for c in loads(farthest_first, step + 1, sources):
                c.start()

        @pl.when(step >= 2)
        def _():
            out_copy(farthest_first, step - 2).wait()

        o_buf[slot] = dot(act_s[there, :], wd[...]).astype(LOW)
        out_copy(farthest_first, step).start()
        act = act_s[there, pl.ds(hiddens[2], 4 * CHUNKS[2])]
        g_both = ggu_s[there, pl.ds(columns[2], 8 * CHUNKS[2])]
        add_grads(2, step, x_buf[slot], c_buf[slot], act, g_both)
        return carry

    lax.fori_loop(0, 8, close_pass, 0)
    out_copy(farthest_first, 6).wait()
    out_copy(farthest_first, 7).wait()
    emit(1)
    emit(2)
    f32 = jnp.float32
    x1.wait_recv()
    y2.wait_recv()
    for c in (*finals[:5], finals[7]):
        c.wait()
    mid[:half] = held[0, :half].astype(f32) + one[2].astype(f32) + two[0].astype(f32)
    y1.wait_recv()
    x2.wait_recv()
    mid[half:] = held[0, half:].astype(f32) + one[3].astype(f32) + two[1].astype(f32)
    gh_copy = pltpu.make_async_copy(mid, gh_out, done_sem.at[7])
    gh_copy.start()
    for g in sum_lines:
        g.wait()
    gh_copy.wait()
    for c in (b_y, b_own, x0, y0, x1, y1, y2, x2):
        c.wait_send()
    for g in (tokens, out_w, cots, z_gain, z_attn, z_out, *z_up, *z_down):
        g.sent()


def layer_front(tokens, cot, weights, gain_rows, lengths, length, wide, qk):
    rows, width = tokens.shape
    streams = lengths.shape[0]
    hidden = 4 * sum(CHUNKS)
    largest = 4 * max(CHUNKS)
    shape = jax.ShapeDtypeStruct
    f32 = jnp.float32
    anywhere = pl.BlockSpec(memory_space=pl.ANY)
    plane = shape((8, rows, width), LOW)
    narrow = shape((streams, length, qk), LOW)
    broad = shape((streams, length, wide), LOW)
    attn_shape = (width, wide + 128)
    out_shape = [
        plane,
        plane,
        plane,
        shape((8, width, width // 8), LOW),
        shape((streams, length, width), LOW),
        narrow,
        narrow,
        broad,
        broad,
        shape((rows, width), LOW),
        shape((rows, width), f32),
        shape(attn_shape, LOW),
        shape((gain_rows.shape[0], width), LOW),
        plane,
        shape((rows, width), f32),
        shape((2, width, 4 * CHUNKS[0]), LOW),
        shape((4 * CHUNKS[0], width), LOW),
        shape((width, 2 * hidden - 8 * CHUNKS[0]), LOW),
        shape((hidden - 4 * CHUNKS[0], width), LOW),
        shape((4, 2, width // 4, 4 * CHUNKS[0]), LOW),
        shape((4, CHUNKS[0], width), LOW),
    ]
    dma = pltpu.SemaphoreType.DMA
    vmem = pltpu.VMEM
    return pl.pallas_call(
        layer_kernel,
        out_shape=out_shape,
        in_specs=[anywhere] * 10 + [pl.BlockSpec(memory_space=pltpu.SMEM)],
        out_specs=[anywhere] * 21,
        scratch_shapes=[
            vmem(attn_shape, LOW),
            vmem((width, 2 * hidden), LOW),
            vmem((hidden, width), LOW),
            vmem((gain_rows.shape[0], width), LOW),
            vmem(narrow.shape, LOW),
            vmem(narrow.shape, LOW),
            vmem(broad.shape, LOW),
            vmem(broad.shape, LOW),
            vmem((rows, width), LOW),
            vmem((rows, width), f32),
            vmem((8 * rows, hidden), LOW),
            vmem((8 * rows, 2 * hidden), LOW),
            vmem((width, 4 * largest), f32),
            vmem((2 * largest, width), f32),
            vmem((2, rows, width), LOW),
            vmem((2, rows, width), LOW),
            vmem((2, rows, width), LOW),
            vmem((2, rows, width), LOW),
            vmem((4, rows, width), LOW),
            vmem((4, rows, width), LOW),
            vmem((4, rows // 2, width), LOW),
            vmem((2, rows // 2, width), LOW),
            dma((4, 13)),
            dma((4, 13)),
            dma((9, 5)),
            dma((9, 4)),
            dma((9,)),
            dma((14,)),
            dma((14,)),
            dma((10,)),
            dma((10,)),
            dma((2, 2)),
            dma((2,)),
            dma((2, 2)),
            dma((2,)),
            dma((8,)),
            dma((4,)),
            dma((2, 5)),
            dma((2, 5)),
            dma((2, 2)),
            dma((21,)),
            vmem((2, width // 4, 4 * CHUNKS[0]), LOW),
            vmem((CHUNKS[0], width), LOW),
        ],
        compiler_params=pltpu.CompilerParams(
            collective_id=21, has_side_effects=True, vmem_limit_bytes=63 * MIB
        ),
        cost_estimate=pl.CostEstimate(
            flops=6 * 3 * 8 * rows * width * hidden,
            bytes_accessed=400 * rows * width,
            transcendentals=0,
        ),
        name="layer",
    )(tokens, cot, *weights, gain_rows, lengths)


class LineScatter:
    def __init__(self, block, target, stop, mine, send, recv, local):
        z = lax.axis_index("dp")
        self.z, self.stop, self.mine = z, stop, mine
        self.inner = (z == 1) | (z == 2)
        self.outer = jnp.logical_not(self.inner)

        def copy(k, src, dst, at, to):
            return pltpu.make_async_remote_copy(
                src_ref=src,
                dst_ref=dst,
                send_sem=send.at[k],
                recv_sem=recv.at[at],
                device_id={"dp": to},
                device_id_type=MESH,
            )

        far = jnp.where(z < 2, 3, 0)
        near = jnp.where(z < 2, 1, 2)
        self.first = copy(0, block(far), stop, 4, jnp.where(self.inner, 3 - near, near))
        self.sends = []
        for k, d in enumerate((1, -1)):
            to = z + d
            valid = (to >= 0) & (to < 4)
            there = jnp.clip(to, 0, 3)
            self.sends.append((valid, copy(1 + k, block(there), target.at[z], z, there)))
        other = 3 - near
        self.sends.append((self.outer, copy(3, block(other), target.at[z], z, other)))
        self.own_far = pltpu.make_async_copy(block(far), mine, local.at[0])
        self.joined = copy(4, mine, target.at[z], z, far)
        self.own = pltpu.make_async_copy(block(z), target.at[z], local.at[1])
        self.arrivals = []
        for d in (1, -1, 2, -2):
            owner = z + d
            valid = (owner >= 0) & (owner < 4)
            there = jnp.clip(owner, 0, 3)
            self.arrivals.append((valid, copy(1, block(there), target.at[there], there, there)))

    def start_first(self):
        self.own.start()

        @pl.when(self.outer)
        def _():
            self.first.start()

        @pl.when(self.inner)
        def _():
            self.own_far.start()

    def start(self):
        for valid, c in self.sends:

            @pl.when(valid)
            def _(c=c):
                c.start()

    def join(self):
        @pl.when(self.inner)
        def _():
            self.first.wait_recv()
            self.own_far.wait()
            self.mine[...] = self.mine[...] + self.stop[...]
            self.joined.start()

    def wait(self):
        for valid, c in self.arrivals:

            @pl.when(valid)
            def _(c=c):
                c.wait_recv()

        self.own.wait()
        for valid, c in (*self.sends, (self.outer, self.first), (self.inner, self.joined)):

            @pl.when(valid)
            def _(c=c):
                c.wait_send()


class PlaneScatter:
    def __init__(self, beside, held, got, one, two, send, recv):
        me, sib, xn, yn = partners()
        half = got.shape[1] // 2
        self.half = half
        upper, lower = pl.ds(0, half), pl.ds(half, half)
        copy = functools.partial(remote, send, recv)
        self.held, self.got, self.one, self.two = held, got, one, two
        self.pairs = [copy(i, beside(i), got.at[i], sib) for i in range(4)]
        self.x0 = copy(4, held(2).at[upper], one.at[0], xn)
        self.y0 = copy(5, held(2).at[lower], one.at[1], yn)
        self.x1 = copy(6, held(1).at[upper], one.at[2], xn)
        self.y1 = copy(7, held(3).at[lower], one.at[3], yn)
        self.y2 = copy(8, held(3).at[upper], two.at[0], yn)
        self.x2 = copy(9, held(1).at[lower], two.at[1], xn)

    def start_pair(self, i):
        self.pairs[i].start()

    def start_pairs(self):
        for i in (2, 1, 3, 0):
            self.start_pair(i)

    def add_pair(self, i):
        self.pairs[i].wait_recv()
        block = self.held(i)
        block[...] = block[...] + self.got[i]
        for c in {0: (), 1: (self.x1,), 2: (self.x0, self.y0), 3: (self.y1,)}[i]:
            c.start()

    def add_pairs(self):
        for i in (2, 1, 3, 0):
            self.add_pair(i)

    def second(self):
        half = self.half
        self.y0.wait_recv()
        block = self.held(1)
        block[half:, :] = block[half:, :] + self.one[1]
        self.x2.start()
        self.x0.wait_recv()
        block = self.held(3)
        block[:half, :] = block[:half, :] + self.one[0]
        self.y2.start()

    def upper_sum(self):
        f32 = jnp.float32
        self.x1.wait_recv()
        self.y2.wait_recv()
        own = self.held(0)[: self.half, :].astype(f32)
        return own + self.one[2].astype(f32) + self.two[0].astype(f32)

    def lower_sum(self):
        f32 = jnp.float32
        self.y1.wait_recv()
        self.x2.wait_recv()
        own = self.held(0)[self.half :, :].astype(f32)
        return own + self.one[3].astype(f32) + self.two[1].astype(f32)

    def sent(self):
        for c in (*self.pairs, self.x0, self.y0, self.x1, self.y1, self.y2, self.x2):
            c.wait_send()


def chips():
    me, unused, xn, yn = partners()
    return me, xn, xn + yn - me, yn


def turn_kernel(
    gh_ref,
    mid_ref,
    c_ref,
    gain_ref,
    wo_all,
    part_ref,
    tok_ref,
    q_ref,
    k_ref,
    v_ref,
    att_ref,
    lengths_ref,
    h1_ref,
    output_ref,
    g_mid_out,
    g_out,
    gain_out,
    attn_ref,
    g_mid,
    work,
    g_low,
    g_att,
    g_heads,
    g_s,
    w_buf,
    go_part,
    held_o,
    got_g,
    one_g,
    two_g,
    got_o,
    one_o,
    two_o,
    gk_sum,
    gv_sum,
    h_buf,
    sums,
    esend,
    erecv,
    ssend,
    srecv,
    load_sem,
    w_sem,
    self_sem,
    done_sem,
    h_sem,
):
    me, sib, xn, yn = partners()
    flip = sib - me
    rows, width = g_low.shape
    span = rows // 2
    wide, qk = v_ref.shape[2], q_ref.shape[2]
    half = rows // 2
    greet([lax.rem(me + i, 8) for i in range(1, 8)])
    owners = chips()

    loads = [
        pltpu.make_async_copy(source, target, load_sem.at[i])
        for i, (source, target) in enumerate(
            ((gh_ref, g_mid), (mid_ref, work), (c_ref, g_low))
        )
    ]
    held_loads = [
        pltpu.make_async_copy(part_ref.at[owners[i]], held_o.at[i], load_sem.at[3 + i])
        for i in range(4)
    ]

    def w_load(step):
        slot = lax.rem(step, 2)
        return pltpu.make_async_copy(wo_all.at[step], w_buf.at[slot], w_sem.at[slot])

    for c in loads:
        c.start()
    w_load(0).start()
    outs = PlaneScatter(
        lambda i: part_ref.at[owners[i] + flip],
        lambda i: held_o.at[i],
        got_o,
        one_o,
        two_o,
        ssend.at[0],
        srecv.at[0],
    )
    weights = PlaneScatter(
        lambda i: go_part.at[owners[i] + flip],
        lambda i: go_part.at[owners[i]],
        got_g,
        one_g,
        two_g,
        ssend.at[1],
        srecv.at[1],
    )
    outs.start_pairs()
    for c in held_loads:
        c.start()
    for c in loads:
        c.wait()

    f32 = jnp.float32
    mid = work[...]
    inverse = norm_scale(mid)
    normed = mid * inverse
    grad = g_mid[...]
    gain_out[...] = jnp.broadcast_to(
        jnp.sum(grad * normed, axis=0, keepdims=True), gain_out.shape
    )
    gain = gain_ref[1:2, :].astype(f32)
    grad_mid = g_low[...].astype(f32) + norm_backward(grad, normed, inverse, gain)
    g_mid[...] = grad_mid
    g_low[...] = grad_mid.astype(LOW)
    done = [pltpu.make_async_copy(g_mid, g_mid_out, done_sem.at[0])]
    done[0].start()

    def back_out(step, carry):
        slot = lax.rem(step, 2)
        w_load(step).wait()

        @pl.when(step < 7)
        def _():
            w_load(step + 1).start()

        there = pl.ds(pl.multiple_of(step * wide, 128), wide)
        term = contract(g_low[:, there], w_buf[slot], 1, 1)

        @pl.when(step == 0)
        def _():
            work[...] = term

        @pl.when(step > 0)
        def _():
            work[...] += term

        return carry

    lax.fori_loop(0, 8, back_out, 0)
    g_att[...] = work[...].astype(LOW)
    mid_load = pltpu.make_async_copy(mid_ref, work, load_sem.at[1])
    mid_load.start()
    swaps = []
    here = pl.ds(me * span, span)
    for i in range(1, 8):
        other = lax.rem(me + i, 8)
        lanes = pl.ds(pl.multiple_of(other * wide, 128), wide)
        for m in range(2):
            swaps.append(
                remote(
                    esend,
                    erecv,
                    2 * (i - 1) + m,
                    g_att.at[pl.ds(m * span, span), lanes],
                    g_heads.at[m, here],
                    other,
                )
            )
            swaps[-1].start()
    kept = [
        pltpu.make_async_copy(
            g_att.at[pl.ds(m * span, span), pl.ds(pl.multiple_of(me * wide, 128), wide)],
            g_heads.at[m, here],
            self_sem.at[m],
        )
        for m in range(2)
    ]
    for c in kept:
        c.start()

    own = width // 32
    for z in range(4):
        lanes = slice(z * 8 * own, (z + 1) * 8 * own)
        block = contract(tok_ref[:, lanes], g_low[...], 0, 0).astype(LOW)
        for s in range(8):
            go_part[s, z * own : (z + 1) * own, :] = block[s * own : (s + 1) * own]
    weights.start_pairs()
    for c in kept:
        c.wait()
    for c in swaps:
        c.wait_recv()
    weights.add_pairs()

    length = v_ref.shape[1]
    block = 256
    streams = v_ref.shape[0]
    pieces = length // rows

    def h_load(step):
        slot = lax.rem(step, 2)
        return pltpu.make_async_copy(
            h1_ref.at[step // pieces, pl.ds(lax.rem(step, pieces) * rows, rows)],
            h_buf.at[slot],
            h_sem.at[slot],
        )

    h_load(0).start()

    def back_stream(m, carry):
        gk_sum[...] = jnp.zeros_like(gk_sum)
        gv_sum[...] = jnp.zeros_like(gv_sum)
        for i in range(length // block):
            rows_i = slice(i * block, (i + 1) * block)
            seen = (i + 1) * block
            query, key = q_ref[m, rows_i, :], k_ref[m, :seen, :]
            g_query = jnp.zeros(query.shape, f32)
            first = first_of(lengths_ref, m, i * block, block)
            for head in range(wide // HEAD_V):
                lanes = slice(head * HEAD_V, (head + 1) * HEAD_V)
                scores, mask, weight = weights_of(query, key, head, first, i * block)
                denom = jnp.sum(weight, axis=1, keepdims=True)
                a = (g_heads[m, rows_i, lanes].astype(f32) / denom).astype(LOW)
                b = -jnp.sum(
                    a.astype(f32) * att_ref[m, rows_i, lanes].astype(f32), axis=1, keepdims=True
                )
                g_weight = contract(a, v_ref[m, :seen, lanes], 1, 1) + b
                slope = 1.0 / math.sqrt(QK_DIM) + scores * (1.0 / QK_DIM)
                g_scores = jnp.where(mask, g_weight * slope, 0.0).astype(LOW)
                g_query += head_lanes(dot(g_scores, key), head)
                gk_sum[:seen, :] += contract(g_scores, head_lanes(query, head), 0, 0)
                gv_sum[:seen, lanes] += contract(weight.astype(LOW), a, 0, 0)
            g_s[m, rows_i, wide : wide + qk] = g_query.astype(LOW)
        g_s[m, :, :wide] = gv_sum[...].astype(LOW)
        g_s[m, :, wide + qk : wide + 2 * qk] = gk_sum[...].astype(LOW)
        g_s[m, :, wide + 2 * qk :] = jnp.zeros((length, g_s.shape[2] - wide - 2 * qk), LOW)

        @pl.when(m == 0)
        def _():
            for c in held_loads:
                c.wait()
            outs.add_pairs()

        return carry

    lax.fori_loop(0, 2, back_stream, 0)
    weights.second()
    done.append(pltpu.make_async_copy(g_s, g_out, done_sem.at[1]))
    done[1].start()
    outs.second()

    def add_grads(step, carry):
        slot = lax.rem(step, 2)
        h_load(step).wait()

        @pl.when(step < streams * pieces - 1)
        def _():
            h_load(step + 1).start()

        there = pl.ds(pl.multiple_of(lax.rem(step, pieces) * rows, rows), rows)
        term = contract(h_buf[slot], g_s[step // pieces, there, :], 0, 0)

        @pl.when(step == 0)
        def _():
            sums[...] = term

        @pl.when(step > 0)
        def _():
            sums[...] += term

        return carry

    lax.fori_loop(0, streams * pieces, add_grads, 0)
    narrow = sums.shape[1]
    attn_ref[:, :narrow] = sums[...].astype(LOW)
    mid_load.wait()
    for part, total in enumerate((weights.upper_sum(), weights.lower_sum())):
        total = total.astype(LOW)
        for z in range(2):
            for i in range(8):
                start = ((2 * part + z) * 8 + i) * own
                attn_ref[start : start + own, narrow:] = total[
                    z * own : (z + 1) * own, i * wide : (i + 1) * wide
                ]
    output_ref[:half] = (work[:half] + outs.upper_sum()).astype(LOW)
    output_ref[half:] = (work[half:] + outs.lower_sum()).astype(LOW)
    for c in done:
        c.wait()
    for c in swaps:
        c.wait_send()
    weights.sent()
    outs.sent()


def layer_turn(gh, mid, cot, gains, wo_all, part, tok, query, key, value, att, lengths, h1, columns):
    rows, width = mid.shape
    streams, length, wide = value.shape
    qk = query.shape[2]
    shape = jax.ShapeDtypeStruct
    f32 = jnp.float32
    anywhere = pl.BlockSpec(memory_space=pl.ANY)
    in_vmem = pl.BlockSpec(memory_space=pltpu.VMEM)
    dma = pltpu.SemaphoreType.DMA
    vmem = pltpu.VMEM
    arriving = [
        vmem((4, rows, width), LOW),
        vmem((4, rows // 2, width), LOW),
        vmem((2, rows // 2, width), LOW),
    ]
    return pl.pallas_call(
        turn_kernel,
        out_shape=[
            shape((rows, width), LOW),
            shape((rows, width), f32),
            shape((streams, length, columns), LOW),
            shape((8, width), f32),
            shape((width, columns + wide), LOW),
        ],
        in_specs=[anywhere] * 3
        + [in_vmem]
        + [anywhere] * 2
        + [in_vmem] * 5
        + [pl.BlockSpec(memory_space=pltpu.SMEM), anywhere],
        out_specs=[in_vmem, anywhere, anywhere, in_vmem, in_vmem],
        scratch_shapes=[
            vmem((rows, width), f32),
            vmem((rows, width), f32),
            vmem((rows, width), LOW),
            vmem((rows, width), LOW),
            vmem((streams, length, wide), LOW),
            vmem((streams, length, columns), LOW),
            vmem((2, width, wide), LOW),
            vmem((8, rows, width), LOW),
            vmem((4, rows, width), LOW),
            *arriving,
            *arriving,
            vmem((length, qk), f32),
            vmem((length, wide), f32),
            vmem((2, rows, width), LOW),
            vmem((width, columns), f32),
            dma((14,)),
            dma((14,)),
            dma((2, 10)),
            dma((2, 10)),
            dma((7,)),
            dma((2,)),
            dma((2,)),
            dma((2,)),
            dma((2,)),
        ],
        compiler_params=pltpu.CompilerParams(
            collective_id=22, has_side_effects=True, vmem_limit_bytes=63 * MIB
        ),
        cost_estimate=moved(16 * rows * width),
        name="turn",
    )(gh, mid, cot, gains, wo_all, part, tok, query, key, value, att, lengths, h1)


def close_kernel(
    g_ref,
    wa_ref,
    g_mid_ref,
    x_ref,
    gain_ref,
    sum_ref,
    blocks_ref,
    rest_ref,
    grad_ref,
    gains_ref,
    first_got,
    rest_got,
    beside,
    held,
    got,
    one,
    two,
    gain_rows,
    gain_line,
    gain_columns,
    gain_plane,
    blocks,
    first_sum,
    ssend,
    srecv,
    zsend,
    zrecv,
    esend,
    erecv,
    self_sem,
    fsend,
    frecv,
    f_sem,
):
    me, sib, xn, yn = partners()
    z = lax.axis_index("dp")
    rows, width = x_ref.shape
    span = rows // 2
    half = rows // 2
    f32 = jnp.float32
    barrier = pltpu.get_barrier_semaphore()
    for i in range(1, 8):
        pl.semaphore_signal(
            barrier, inc=1, device_id={"seq": lax.rem(me + i, 8)}, device_id_type=MESH
        )
    for i in range(1, 4):
        pl.semaphore_signal(
            barrier, inc=1, device_id={"dp": lax.rem(z + i, 4)}, device_id_type=MESH
        )
    pl.semaphore_wait(barrier, 10)
    load = pltpu.make_async_copy(blocks_ref, blocks, f_sem.at[0])
    load.start()
    keep = first_got.shape[1]

    def exchange(item, source, target):
        mine = pltpu.make_async_copy(
            source.at[pl.ds(me * keep, keep)], target.at[me], f_sem.at[1 + item]
        )
        mine.start()
        copies = []
        for i in range(1, 8):
            other = lax.rem(me + i, 8)
            copies.append(
                remote(
                    fsend,
                    frecv,
                    7 * item + i - 1,
                    source.at[pl.ds(other * keep, keep)],
                    target.at[me],
                    other,
                )
            )
            copies[-1].start()
        return mine, copies

    scatter = PlaneScatter(
        lambda i: beside.at[i], lambda i: held.at[i], got, one, two, ssend, srecv
    )
    def part_of(owner):
        there = pl.ds(pl.multiple_of(owner * span, span), span)
        grads = jnp.concatenate([g_ref[0, there, :], g_ref[1, there, :]], axis=0)
        return contract(grads, wa_ref[...], 1, 1).astype(LOW)

    owners = chips()
    for i in (2, 1, 3, 0):
        beside[i] = part_of(owners[i] + sib - me)
        scatter.start_pair(i)
        held[i] = part_of(owners[i])
        scatter.add_pair(i)

    load.wait()
    for second in range(2):
        total = jnp.zeros(blocks.shape[2:], f32)
        for owner in range(4):
            came = jnp.abs(z - owner) < 3
            total = total + jnp.where(came, blocks[owner, second].astype(f32), 0.0)
        lanes_here = total.shape[1]
        first_sum[:, second * lanes_here : (second + 1) * lanes_here] = total.astype(LOW)
    scatter.second()
    moves = [exchange(1, rest_ref, rest_got), exchange(0, first_sum, first_got)]

    x = x_ref[...].astype(f32)
    inverse = norm_scale(x)
    normed = x * inverse
    gain = gain_ref[0:1, :].astype(f32)

    def finish(start, g_h):
        part = slice(start, start + half)
        grad_ref[part] = g_mid_ref[part] + norm_backward(g_h, normed[part], inverse[part], gain)
        return jnp.sum(g_h * normed[part], axis=0, keepdims=True)

    gain_sum = finish(0, scatter.upper_sum()) + finish(half, scatter.lower_sum())

    both = jnp.concatenate([gain_sum, sum_ref[0:1, :], jnp.zeros((14, width), f32)], axis=0)
    gain_rows[...] = both.astype(LOW)
    depth = width // 4

    def lanes(owner):
        return pl.ds(pl.multiple_of(owner * depth, 128), depth)

    def over_line(k, to, owner):
        return pltpu.make_async_remote_copy(
            src_ref=gain_rows.at[:, lanes(to)],
            dst_ref=gain_line.at[owner],
            send_sem=zsend.at[k],
            recv_sem=zrecv.at[owner],
            device_id={"dp": to},
            device_id_type=MESH,
        )

    others = [lax.rem(z + o, 4) for o in (1, 2, 3)]
    sends = [over_line(k, other, z) for k, other in enumerate(others)]
    own = pltpu.make_async_copy(gain_rows.at[:, lanes(z)], gain_line.at[z], self_sem.at[0])
    own.start()
    for c in sends:
        c.start()
    own.wait()
    for other in others:
        over_line(0, other, other).wait_recv()
    total = gain_line[0].astype(f32)
    for k in range(1, 4):
        total = total + gain_line[k].astype(f32)
    entry = lax.broadcasted_iota(jnp.int32, (16, 128), 0)
    lane = lax.broadcasted_iota(jnp.int32, (16, 128), 1)
    pick = jnp.where(lane == entry, 1.0, 0.0).astype(LOW)
    gain_columns[...] = contract(total.astype(LOW), pick, 0, 0).astype(LOW)
    count = depth // 8
    own = pltpu.make_async_copy(
        gain_columns.at[pl.ds(me * count, count)], gain_plane.at[me], self_sem.at[1]
    )
    own.start()
    swaps = []
    for i in range(1, 8):
        other = lax.rem(me + i, 8)
        swaps.append(
            remote(
                esend,
                erecv,
                i - 1,
                gain_columns.at[pl.ds(other * count, count)],
                gain_plane.at[me],
                other,
            )
        )
        swaps[-1].start()
    own.wait()
    for c in swaps:
        c.wait_recv()
    total = gain_plane[0].astype(f32)
    for k in range(1, 8):
        total = total + gain_plane[k].astype(f32)
    gains_ref[...] = total
    scatter.sent()
    for c in (*sends, *swaps):
        c.wait_send()
    for mine, copies in moves:
        mine.wait()
        for c in copies:
            c.wait()


def layer_close(g_all, wa, g_mid, tokens, gains, gain_sum, blocks, rest):
    rows, width = tokens.shape
    shape = jax.ShapeDtypeStruct
    in_vmem = pl.BlockSpec(memory_space=pltpu.VMEM)
    anywhere = pl.BlockSpec(memory_space=pl.ANY)
    dma = pltpu.SemaphoreType.DMA
    vmem = pltpu.VMEM
    return pl.pallas_call(
        close_kernel,
        out_shape=[
            shape((rows, width), jnp.float32),
            shape((width // 32, 128), jnp.float32),
            shape((8, width // 32, 8 * CHUNKS[0]), LOW),
            shape((8, width // 32, rest.shape[1]), LOW),
        ],
        in_specs=[in_vmem] * 6 + [anywhere] * 2,
        out_specs=[in_vmem, in_vmem, anywhere, anywhere],
        scratch_shapes=[
            vmem((4, rows, width), LOW),
            vmem((4, rows, width), LOW),
            vmem((4, rows, width), LOW),
            vmem((4, rows // 2, width), LOW),
            vmem((2, rows // 2, width), LOW),
            vmem((16, width), LOW),
            vmem((4, 16, width // 4), LOW),
            vmem((width // 4, 128), LOW),
            vmem((8, width // 32, 128), LOW),
            vmem(blocks.shape, LOW),
            vmem((width // 4, 8 * CHUNKS[0]), LOW),
            dma((10,)),
            dma((10,)),
            dma((3,)),
            dma((4,)),
            dma((7,)),
            dma((7,)),
            dma((2,)),
            dma((14,)),
            dma((14,)),
            dma((3,)),
        ],
        compiler_params=pltpu.CompilerParams(
            collective_id=23, has_side_effects=True, vmem_limit_bytes=56 * MIB
        ),
        cost_estimate=moved(16 * rows * width),
        name="close",
    )(g_all, wa, g_mid, tokens, gains, gain_sum, blocks, rest)


def place_kernel(
    first_in,
    rest_in,
    blocks_in,
    down_in,
    out_ref,
    grad_ref,
    gate_out,
    up_out,
    down_out,
    out_copy,
    grad_copy,
    first_ref,
    rest_ref,
    blocks_ref,
    down_ref,
    sems,
):
    copies = [
        pltpu.make_async_copy(source, target, sems.at[i])
        for i, (source, target) in enumerate(
            (
                (first_in, first_ref),
                (rest_in, rest_ref),
                (blocks_in, blocks_ref),
                (down_in, down_ref),
                (out_ref, out_copy),
                (grad_ref, grad_copy),
            )
        )
    ]
    for c in copies:
        c.start()
    for c in copies[:2]:
        c.wait()
    f32 = jnp.float32
    z = lax.axis_index("dp")
    share = sum(CHUNKS)
    for second, target in enumerate((gate_out, up_out)):
        for owner in range(8):
            for group in range(4):
                at = group * 8 * share + owner * share
                start = 0
                for k, count in enumerate(CHUNKS):
                    source = first_ref if k == 0 else rest_ref
                    begin = start + (4 * second + group) * count
                    target[:, at : at + count] = source[owner, :, begin : begin + count].astype(f32)
                    at += count
                    start += 8 * count if k else 0
    for c in copies[2:4]:
        c.wait()
    total = jnp.zeros(blocks_ref.shape[1:], f32)
    for owner in range(4):
        came = jnp.abs(z - owner) < 3
        total = total + jnp.where(came, blocks_ref[owner].astype(f32), 0.0)
    down_out[: CHUNKS[0], :] = total
    down_out[CHUNKS[0] :, :] = down_ref[...].astype(f32)
    for c in copies[4:]:
        c.wait()


def place_rows(first, rest, blocks, down, output, input_grad):
    own, width = first.shape[1], blocks.shape[2]
    shape = jax.ShapeDtypeStruct
    anywhere = pl.BlockSpec(memory_space=pl.ANY)
    in_vmem = pl.BlockSpec(memory_space=pltpu.VMEM)
    wide = 32 * sum(CHUNKS)
    return pl.pallas_call(
        place_kernel,
        out_shape=[
            shape((own, wide), jnp.float32),
            shape((own, wide), jnp.float32),
            shape((sum(CHUNKS), width), jnp.float32),
            shape(output.shape, output.dtype),
            shape(input_grad.shape, input_grad.dtype),
        ],
        in_specs=[anywhere] * 6,
        out_specs=[in_vmem] * 5,
        scratch_shapes=[
            pltpu.VMEM(first.shape, LOW),
            pltpu.VMEM(rest.shape, LOW),
            pltpu.VMEM(blocks.shape, LOW),
            pltpu.VMEM(down.shape, LOW),
            pltpu.SemaphoreType.DMA((6,)),
        ],
        compiler_params=pltpu.CompilerParams(vmem_limit_bytes=63 * MIB),
        name="place",
    )(first, rest, blocks, down, output, input_grad)


def place_attn_kernel(got_ref, out_ref, query_out, key_out, value_out, grad_out):
    f32 = jnp.float32
    wide = value_out.shape[1] // 8
    qk = query_out.shape[1] // 8
    own = out_ref.shape[0] // 8
    for owner in range(8):
        value_out[:, owner * wide : (owner + 1) * wide] = got_ref[owner, :, :wide].astype(f32)
        here = slice(owner * qk, (owner + 1) * qk)
        query_out[:, here] = got_ref[owner, :, wide : wide + qk].astype(f32)
        key_out[:, here] = got_ref[owner, :, wide + qk : wide + 2 * qk].astype(f32)
        block = out_ref[owner * own : (owner + 1) * own, out_ref.shape[1] - wide :]
        grad_out[:, owner * wide : (owner + 1) * wide] = block.astype(f32)


def place_attn(got, summed, wide, qk):
    own = got.shape[1]
    shape = jax.ShapeDtypeStruct
    in_vmem = pl.BlockSpec(memory_space=pltpu.VMEM)
    return pl.pallas_call(
        place_attn_kernel,
        out_shape=[
            shape((own, 8 * qk), jnp.float32),
            shape((own, 8 * qk), jnp.float32),
            shape((own, 8 * wide), jnp.float32),
            shape((own, 8 * wide), jnp.float32),
        ],
        in_specs=[in_vmem] * 2,
        out_specs=[in_vmem] * 4,
        name="place_attn",
    )(got, summed)


def ffn_lax(h_two, cot_all, gate_full, up_full, down_full):
    pieces, rows, width = cot_all.shape
    h_two_all = gather_plane(h_two, 5).reshape(-1, width)
    cot_all = cot_all.reshape(-1, width)
    gate = dot(h_two_all, gate_full)
    up = dot(h_two_all, up_full)
    g_act = contract(cot_all, down_full, 1, 1)
    sigmoid = jax.nn.sigmoid(gate)
    silu = gate * sigmoid
    act = (silu * up).astype(LOW)
    g_gate = (g_act * up * sigmoid * (1.0 + gate * (1.0 - sigmoid))).astype(LOW)
    g_up = (g_act * silu).astype(LOW)
    part = (contract(g_gate, gate_full, 1, 1) + contract(g_up, up_full, 1, 1)).astype(LOW)
    return (
        dot(act, down_full).astype(LOW).reshape(pieces, rows, width),
        scatter_plane(part.reshape(pieces, rows, width), 7),
        contract(h_two_all, g_gate, 0, 0).astype(LOW),
        contract(h_two_all, g_up, 0, 0).astype(LOW),
        contract(act, cot_all, 0, 0).astype(LOW),
    )


def norm_scale(rows):
    return lax.rsqrt(jnp.mean(rows * rows, axis=-1, keepdims=True) + epsilon)


def norm_backward(grad, normed, inverse, gain):
    scaled = grad * gain
    return inverse * (scaled - normed * jnp.mean(scaled * normed, axis=-1, keepdims=True))


def local(
    tokens,
    doc_lengths,
    w_query,
    w_key,
    w_value,
    w_out,
    w_gate,
    w_up,
    w_down,
    gain_attn,
    gain_mlp,
    cotangent,
):
    micro, span = tokens.shape[1:3]
    pieces, groups = lax.axis_size("seq"), lax.axis_size("dp")
    place = lax.axis_index("seq")
    length = pieces * span
    heads = max(1, HEADS // pieces)
    sharers = max(1, pieces // HEADS)
    streams = micro // sharers
    first_head = place // sharers * heads
    first_stream = place % sharers * streams
    qk, wide = heads * QK_DIM, heads * HEAD_V
    hidden = FF // pieces

    out_width = D // pieces
    rows_dp = w_gate.shape[0]
    share = hidden // groups
    block = FF // groups
    mine = micro * span
    fused = pieces == 8 and groups == 4 and micro == 2 and span == 128
    chunks = CHUNKS if fused else (share,)

    def hidden_columns(w):
        parts = [
            lax.dynamic_slice_in_dim(w, z * block + place * share, share, 1) for z in range(groups)
        ]
        edges = [sum(chunks[:k]) for k in range(len(chunks) + 1)]
        return [
            [part[:, edges[k] : edges[k + 1]] for part in parts] for k in range(len(chunks))
        ]

    x_own = tokens[0].reshape(mine, D)
    flat = x_own.astype(jnp.float32)
    cot = cotangent[0].reshape(mine, D)

    def to_tokens(by_head):
        sent = by_head.reshape(streams, pieces, span, wide).transpose(1, 0, 2, 3)
        got = exchange_plane(sent, 3).reshape(pieces // sharers, micro, span, wide)
        return got.transpose(1, 2, 0, 3).reshape(mine, HEADS * HEAD_V)

    def to_heads(by_token):
        sent = by_token.reshape(micro, span, pieces // sharers, wide).transpose(2, 0, 1, 3)
        got = exchange_plane(sent.reshape(pieces, streams, span, wide), 4)
        return got.transpose(1, 0, 2, 3).reshape(streams, length, wide)

    if fused:
        gain_rows = jnp.concatenate(
            [gain_attn[None], gain_mlp[None], jnp.zeros((14, rows_dp), LOW)], axis=0
        )
        weights = (w_query, w_key, w_value, w_out, w_gate, w_up, w_down)
        front = layer_front(x_own, cot, weights, gain_rows, doc_lengths[0], length, wide, qk)
        out_full, h_all, query, key, value, att_heads, attended, mid = front[3:11]
        attn_full, gain_rows_all, out_part, g_h_two = front[11:15]
        d_ffn, d_down, ffn_blocks, down_blocks = front[17:]
    else:
        gate_parts, up_parts = hidden_columns(w_gate), hidden_columns(w_up)
        ffn_slice = jnp.concatenate(
            [part for k in range(len(chunks)) for part in gate_parts[k] + up_parts[k]], axis=1
        )
        attn_parts = [
            lax.dynamic_slice_in_dim(w_value, first_head * HEAD_V, wide, 1),
            lax.dynamic_slice_in_dim(w_query, first_head * QK_DIM, qk, 1),
            lax.dynamic_slice_in_dim(w_key, first_head * QK_DIM, qk, 1),
        ]

        lengths = lax.dynamic_slice_in_dim(doc_lengths[0], first_stream, streams, 0)
        starts = jnp.cumsum(lengths, axis=1) - lengths
        position = jnp.arange(length, dtype=jnp.int32)
        begun = starts[:, None, :] <= position[None, :, None]
        first = jnp.max(jnp.where(begun, starts[:, None, :], 0), axis=2)[..., None]

        def gather_dp(w):
            return lax.all_gather(w, "dp", axis=0, tiled=True)

        attn_got = gather_dp(
            jnp.concatenate(
                attn_parts
                + [
                    lax.dynamic_slice_in_dim(w_out, place * out_width, out_width, 1),
                    gain_attn[:, None],
                    gain_mlp[:, None],
                ],
                axis=1,
            )
        )
        ffn_full = gather_dp(ffn_slice)
        down_full = gather_dp(lax.dynamic_slice_in_dim(w_down, place * share, share, 0))
        value_full = attn_got[:, :wide]
        query_full = attn_got[:, wide : wide + qk]
        key_full = attn_got[:, wide + qk : wide + 2 * qk]
        out_full = gather_plane(attn_got[:, wide + 2 * qk : wide + 2 * qk + out_width], 2)
        gains = attn_got[:, wide + 2 * qk + out_width :].astype(jnp.float32)
        gain_one, gain_two = gains[:, 0], gains[:, 1]
        x_all = gather_plane(x_own, 1).reshape(pieces, micro, span, D).transpose(1, 0, 2, 3)
        x_all = lax.dynamic_slice_in_dim(x_all, first_stream, streams, 0).astype(jnp.float32)
        h_flat = (x_all * norm_scale(x_all) * gain_one).astype(LOW).reshape(streams * length, D)
        value = dot(h_flat, value_full).astype(LOW).reshape(streams, length, wide)
        query = dot(h_flat, query_full).astype(LOW).reshape(streams, length, qk)
        key = dot(h_flat, key_full).astype(LOW).reshape(streams, length, qk)
        att_heads = attend(query, key, value, first, heads)
        attended = to_tokens(att_heads)
        mid = flat + jnp.einsum(
            "tk,skn->tsn", attended, out_full, preferred_element_type=jnp.float32
        ).reshape(mine, D)
        h_two = (mid * norm_scale(mid) * gain_two).astype(LOW)
        out_part, g_h_two, d_gate, d_up, d_down = ffn_lax(
            h_two, gather_plane(cot, 6), ffn_full[:, :hidden], ffn_full[:, hidden:], down_full
        )
        d_ffn = jnp.concatenate([d_gate, d_up], axis=1)

    def scatter_dp(part):
        return lax.psum_scatter(part, "dp", scatter_dimension=0, tiled=True)

    own = rows_dp // pieces
    sum_ffn, sum_down = scatter_dp(d_ffn), scatter_dp(d_down)

    if fused:
        output, g_mid, g_all, gain_sum, grad_attn = layer_turn(
            g_h_two, mid, cot, gain_rows_all, out_full, out_part, attended, query, key, value,
            att_heads, doc_lengths[0], h_all, attn_full.shape[1],
        )
        grad_attn, sum_ffn, sum_down = lax.optimization_barrier((grad_attn, sum_ffn, sum_down))
        grad_attn = scatter_dp(grad_attn)
        input_grad, gain_columns, first_got, rest_got = layer_close(
            g_all, attn_full, g_mid, x_own, gain_rows_all, gain_sum, ffn_blocks, sum_ffn
        )
        grad_attn, gain_columns = lax.optimization_barrier((grad_attn, gain_columns))
        kept = attn_full.shape[1]
        attn_got = exchange_plane(grad_attn.reshape(pieces, own, -1), 12, kept)
        attn_got, first_got = lax.optimization_barrier((attn_got, first_got))
        grad_gate, grad_up, grad_down, output, input_grad = place_rows(
            first_got, rest_got, down_blocks, sum_down, output, input_grad
        )
        grad_query, grad_key, grad_value, grad_out = place_attn(attn_got, grad_attn, wide, qk)
        return (
            output.reshape(tokens.shape),
            input_grad.reshape(tokens.shape),
            grad_query,
            grad_key,
            grad_value,
            grad_out,
            grad_gate,
            grad_up,
            grad_down,
            gain_columns[:, 0],
            gain_columns[:, 1],
        )

    inverse_two = norm_scale(mid)
    plain_two = mid * inverse_two
    output = (mid + scatter_plane(out_part, 8)).astype(LOW)
    g_mid = cot.astype(jnp.float32) + norm_backward(g_h_two, plain_two, inverse_two, gain_two)
    g_mid_low = g_mid.astype(LOW)
    g_att = jnp.einsum(
        "tsn,skn->tk",
        g_mid_low.reshape(mine, pieces, out_width),
        out_full,
        preferred_element_type=jnp.float32,
    )
    g_att = to_heads(g_att.astype(LOW))
    g_query, g_key, g_value = attend_back(query, key, value, first, att_heads, g_att, heads)
    g_value = g_value.reshape(streams * length, wide)
    g_query = g_query.reshape(streams * length, qk)
    g_key = g_key.reshape(streams * length, qk)
    g_h_one_part = (
        contract(g_value, value_full, 1, 1)
        + contract(g_query, query_full, 1, 1)
        + contract(g_key, key_full, 1, 1)
    ).astype(LOW)
    g_h_one_part = g_h_one_part.reshape(streams, pieces, span, D).transpose(1, 0, 2, 3)
    if sharers > 1:
        padded = jnp.zeros((pieces, micro, span, D), LOW)
        g_h_one_part = lax.dynamic_update_slice_in_dim(padded, g_h_one_part, first_stream, 1)
    g_h_one = scatter_plane(g_h_one_part.reshape(pieces, mine, D), 9)
    inverse_one = norm_scale(flat)
    plain_one = flat * inverse_one
    input_grad = g_mid + norm_backward(g_h_one, plain_one, inverse_one, gain_one)
    grad_out = contract(attended, g_mid_low, 0, 0).astype(LOW)
    grad_out = grad_out.reshape(groups, pieces, own, D).transpose(1, 0, 2, 3)
    grad_out = scatter_plane(grad_out.reshape(pieces, groups * own, D), 10).astype(LOW)
    grad_out = scatter_dp(grad_out)
    grad_attn = jnp.concatenate(
        [
            contract(h_flat, g_value, 0, 0).astype(LOW),
            contract(h_flat, g_query, 0, 0).astype(LOW),
            contract(h_flat, g_key, 0, 0).astype(LOW),
            jnp.sum(g_h_one * plain_one, axis=0).astype(LOW)[:, None],
            jnp.sum(g_h_two * plain_two, axis=0).astype(LOW)[:, None],
        ],
        axis=1,
    )

    grad_attn = scatter_dp(grad_attn)
    ffn_got = exchange_plane(sum_ffn.reshape(pieces, own, 2 * hidden), 11).astype(jnp.float32)
    attn_got = exchange_plane(grad_attn.reshape(pieces, own, -1), 12).astype(jnp.float32)
    grad_gains = jnp.sum(attn_got[:, :, wide + 2 * qk :], axis=0)
    attn_got = jnp.sum(attn_got.reshape(pieces // sharers, sharers, own, -1), axis=1)

    def by_hidden(block):
        return block.reshape(pieces, own, groups, share).transpose(1, 2, 0, 3).reshape(own, FF)

    def by_rows(block):
        return block.transpose(1, 0, 2).reshape(own, -1)

    return (
        output.reshape(tokens.shape),
        input_grad.reshape(tokens.shape),
        by_rows(attn_got[:, :, wide : wide + qk]),
        by_rows(attn_got[:, :, wide + qk : wide + 2 * qk]),
        by_rows(attn_got[:, :, :wide]),
        grad_out.astype(jnp.float32),
        by_hidden(ffn_got[:, :, :hidden]),
        by_hidden(ffn_got[:, :, hidden:]),
        sum_down.astype(jnp.float32),
        grad_gains[:, 0],
        grad_gains[:, 1],
    )


def solution(mesh):
    by_token, by_row = P("dp", None, "seq", None), P("dp", None)
    grad_rows, grad_entries = P(("dp", "seq"), None), P(("dp", "seq"))
    return jax.shard_map(
        local,
        mesh=mesh,
        in_specs=(by_token, P("dp", None, None)) + (by_row,) * 7 + (P("dp"), P("dp"), by_token),
        out_specs=(by_token, by_token) + (grad_rows,) * 7 + (grad_entries,) * 2,
        check_vma=False,
    )
```
